32 devices in a mesh: dom: 16 (over z, y, core), depth: 2 (over x).
Axes of the slice: x: 2, y: 2, z: 4, core: 2. Of those that a mesh axis runs over, the one named last changes fastest.
Arguments:
- adjoint_now: float32 [3, 64, 34, 128], P(None, 'dom', 'depth'), may hold values from -6 to 6
- adjoint_next: float32 [3, 64, 34, 128], P(None, 'dom', 'depth'), may hold values from -6 to 6
- lame_first: float32 [16, 8, 32], P('dom', 'depth'), may hold values from 1 to 3
- shear_modulus: float32 [16, 8, 32], P('dom', 'depth'), may hold values from 1 to 3
- density: float32 [64, 34, 128], P('dom', 'depth'), may hold values from 1 to 3
- branch_flags: int32 [4, 2, 64, 128], P(None, 'depth', 'dom'), may hold values from 0 to 2
- weak_slope: float32 [2, 64, 128], P('depth', 'dom'), may hold values from 0.1 to 0.5
- normal_stress: float32 [2, 64, 128], P('depth', 'dom'), may hold values from 1 to 10
- patch_owner: int32 [2, 64], P('depth', 'dom'), may hold values from 0 to 31, as said below
Outputs:
- earlier_state: float32 [3, 64, 34, 128], P(None, 'dom', 'depth')
- later_state: float32 [3, 64, 34, 128], P(None, 'dom', 'depth')
- patch_gradient: float32 [2, 32, 128], P('depth', 'dom')
The draws below stay inside these ranges and needn't reach their ends.
Inputs may be any that keep to these rules, and one draw needn't show every extreme that they name: `patch_owner`: patch p is owned by dom index p // 2; a column held by dom index d belongs to a patch whose owner is at most 2 indices of dom from d.
All inputs are finite; a program needn't handle non-finite values.
Results may differ from the reference program's by a relative error of at most 0.0001.
Values sent between devices are 32-bit elements; how exact they have to be, the bound alone decides.
No kernel may reach another device: no remote copies, remote signals or barrier semaphores. Data moves between devices by JAX's collectives and lax.ppermute only.
A program may use at most 64 MiB of HBM per device.

```python
import math
import jax
import jax.numpy as jnp
import numpy as np
from jax import lax

EX = 1
EY = 4
EZ = 32
STEPS = 4
PATCH_DEV = 2
REACH = 2
XE = 16
XG = 64
YE = 8
YG = 34
NZN = 128
N_DOM = 16
N_DEPTH = 2


def draw_patch_owner(key, part):
    columns = jnp.arange(4 * EX * N_DOM, dtype=jnp.int32)
    holder = columns // (4 * EX)
    first_key, second_key = jax.random.split(jax.random.fold_in(key, 11))
    offset = jax.random.randint(first_key, (N_DEPTH, 4 * EX * N_DOM), -REACH, REACH + 1)
    within = jax.random.randint(second_key, (N_DEPTH, 4 * EX * N_DOM), 0, PATCH_DEV)
    owner_index = jnp.clip(holder[None, :] + offset, 0, N_DOM - 1)
    numbers = owner_index * PATCH_DEV + within
    numbers = jnp.where(columns[None, :] == 4 * EX * N_DOM - 1, PATCH_DEV * N_DOM - 1, numbers)
    numbers = jnp.where(columns[None, :] == 0, 0, numbers)
    return numbers.astype(jnp.int32)


def plant(values, stream_key, smallest, high):
    longest = values.shape.index(max(values.shape))
    spots = []
    for shift in (0, 1):
        where = [jax.random.randint(jax.random.fold_in(stream_key, axis), (), 0, length) for axis, length in enumerate(values.shape)]
        where[longest] = (where[longest] + shift) % values.shape[longest]
        spots.append(tuple(where))
    return values.at[spots[0]].set(smallest).at[spots[1]].set(high)


def shard_levels(key, shape, shards, smallest, high):
    factor_of = 1.0
    for axis_at, blocks in shards:
        heights = jax.random.uniform(jax.random.fold_in(jax.random.fold_in(key, 6), axis_at), (blocks,), jnp.float32, smallest / len(shards), high / len(shards))
        factor_of = factor_of * jnp.repeat(jnp.exp(heights), shape[axis_at] // blocks).reshape((-1,) + (1,) * (len(shape) - 1 - axis_at))
    return factor_of


def noise(rng, extent, deviation, bound, cuts=(), kind=jnp.bfloat16):
    result = deviation * jax.random.normal(rng, extent, jnp.float32)
    if cuts:
        result = result * shard_levels(rng, extent, cuts, -0.22, 0.18)
    return jnp.clip(result, -bound, bound).astype(kind)


def setup_inputs(seed: int = 0) -> dict:
    splits = jax.random.split(jax.random.key(seed), 10)
    return {
        "adjoint_now": noise(splits[0], (3, XG, YG, NZN), 1.0, 6.0, ((1, 16), (2, 2)), jnp.float32),
        "adjoint_next": noise(splits[1], (3, XG, YG, NZN), 1.0, 6.0, ((1, 16), (2, 2)), jnp.float32),
        "lame_first": jnp.clip(jnp.exp(math.log(3.0) - 1.0986123 * jax.random.uniform(splits[2], (XE, YE, EZ), jnp.float32) ** shard_levels(splits[2], (XE, YE, EZ), ((0, 16), (1, 2)), -0.2, 0.2)), 1.0, 3.0),
        "shear_modulus": jnp.clip(jnp.exp(math.log(3.0) - 1.0986123 * jax.random.uniform(splits[3], (XE, YE, EZ), jnp.float32) ** shard_levels(splits[3], (XE, YE, EZ), ((0, 16), (1, 2)), -0.2, 0.2)), 1.0, 3.0),
        "density": jnp.clip(jnp.exp(math.log(3.0) - 1.0986123 * jax.random.uniform(splits[4], (XG, YG, NZN), jnp.float32) ** shard_levels(splits[4], (XG, YG, NZN), ((0, 16), (1, 2)), -0.2, 0.2)), 1.0, 3.0),
        "branch_flags": plant(jax.random.randint(splits[5], (STEPS, N_DEPTH, XG, NZN), 0, 3), jax.random.fold_in(splits[5], 1), 0, 2).astype(jnp.int32),
        "weak_slope": jnp.clip(jnp.exp(math.log(0.5) - 1.609438 * jax.random.uniform(splits[6], (N_DEPTH, XG, NZN), jnp.float32) ** shard_levels(splits[6], (N_DEPTH, XG, NZN), ((0, 2), (1, 16)), -0.2, 0.2)), 0.1, 0.5),
        "normal_stress": jnp.clip(jnp.exp(math.log(10.0) - 2.3025851 * jax.random.uniform(splits[7], (N_DEPTH, XG, NZN), jnp.float32) ** shard_levels(splits[7], (N_DEPTH, XG, NZN), ((0, 2), (1, 16)), -0.2, 0.2)), 1.0, 10.0),
        "patch_owner": draw_patch_owner(jax.random.fold_in(splits[9], 71), 0),
    }


time_step = 0.01
lock_stiffness = 0.5
highest = lax.Precision.HIGHEST

def basis_tables():
    points = [-1.0, -math.sqrt(3.0 / 7.0), 0.0, math.sqrt(3.0 / 7.0), 1.0]
    quad_weights = np.array([0.1, 49.0 / 90.0, 32.0 / 45.0, 49.0 / 90.0, 0.1])
    products = []
    for first in range(5):
        value = 1.0
        for other in range(5):
            if other != first:
                value = value * (points[first] - points[other])
        products.append(value)
    derivative = np.zeros((5, 5))
    for row in range(5):
        for column in range(5):
            if row == column:
                total = 0.0
                for other in range(5):
                    if other != row:
                        total = total + 1.0 / (points[row] - points[other])
                derivative[row, column] = total
            else:
                derivative[row, column] = products[row] / products[column] / (points[row] - points[column])
    return (quad_weights, derivative)

def element_maps(elements):
    quad_weights, derivative = basis_tables()
    expand = np.zeros((5 * elements, 4 * elements + 1))
    slopes = np.zeros((5 * elements, 4 * elements + 1))
    for element in range(elements):
        for corner in range(5):
            expand[5 * element + corner, 4 * element + corner] = 1.0
            slopes[5 * element + corner, 4 * element:4 * element + 5] = 2.0 * derivative[corner]
    return (expand, slopes, np.tile(quad_weights, elements))

def stiffness(displaced, lame_block, shear_block):
    x_elems, y_elems, z_elems = lame_block.shape
    maps_x = element_maps(x_elems)
    maps_y = element_maps(y_elems)
    maps_z = element_maps(z_elems)
    x_expand = jnp.asarray(maps_x[0], dtype=jnp.float32)
    x_slopes = jnp.asarray(maps_x[1], dtype=jnp.float32)
    y_expand = jnp.asarray(maps_y[0], dtype=jnp.float32)
    y_slopes = jnp.asarray(maps_y[1], dtype=jnp.float32)
    z_expand = jnp.asarray(maps_z[0], dtype=jnp.float32)
    z_slopes = jnp.asarray(maps_z[1], dtype=jnp.float32)
    weight_x = jnp.asarray(maps_x[2], dtype=jnp.float32)
    weight_y = jnp.asarray(maps_y[2], dtype=jnp.float32)
    weight_z = jnp.asarray(maps_z[2], dtype=jnp.float32)
    along_z = jnp.einsum('cxyz,qz->cxyq', displaced, z_expand, precision=highest)
    slope_z = jnp.einsum('cxyz,qz->cxyq', displaced, z_slopes, precision=highest)
    plain_yz = jnp.einsum('cxyq,py->cxpq', along_z, y_expand, precision=highest)
    slope_y = jnp.einsum('cxyq,py->cxpq', along_z, y_slopes, precision=highest)
    slope_zy = jnp.einsum('cxyq,py->cxpq', slope_z, y_expand, precision=highest)
    grad_x = jnp.einsum('cxpq,rx->crpq', plain_yz, x_slopes, precision=highest)
    grad_y = jnp.einsum('cxpq,rx->crpq', slope_y, x_expand, precision=highest)
    grad_z = jnp.einsum('cxpq,rx->crpq', slope_zy, x_expand, precision=highest)
    weight_q = weight_x[:, None, None] * weight_y[None, :, None] * weight_z[None, None, :] / 8.0
    lame_q = jnp.repeat(jnp.repeat(jnp.repeat(lame_block, 5, axis=0), 5, axis=1), 5, axis=2)
    shear_q = jnp.repeat(jnp.repeat(jnp.repeat(shear_block, 5, axis=0), 5, axis=1), 5, axis=2)
    divergence = grad_x[0] + grad_y[1] + grad_z[2]
    normal_part = lame_q * divergence
    stress_xx = normal_part + 2.0 * shear_q * grad_x[0]
    stress_yy = normal_part + 2.0 * shear_q * grad_y[1]
    stress_zz = normal_part + 2.0 * shear_q * grad_z[2]
    stress_xy = shear_q * (grad_x[1] + grad_y[0])
    stress_xz = shear_q * (grad_x[2] + grad_z[0])
    stress_yz = shear_q * (grad_y[2] + grad_z[1])
    flux_x = weight_q * jnp.stack([stress_xx, stress_xy, stress_xz])
    flux_y = weight_q * jnp.stack([stress_xy, stress_yy, stress_yz])
    flux_z = weight_q * jnp.stack([stress_xz, stress_yz, stress_zz])
    back_x = jnp.einsum('crpq,rx->cxpq', flux_x, x_slopes, precision=highest)
    back_y = jnp.einsum('crpq,rx->cxpq', flux_y, x_expand, precision=highest)
    back_z = jnp.einsum('crpq,rx->cxpq', flux_z, x_expand, precision=highest)
    partial_a = jnp.einsum('cxpq,py->cxyq', back_x, y_expand, precision=highest) + jnp.einsum('cxpq,py->cxyq', back_y, y_slopes, precision=highest)
    partial_b = jnp.einsum('cxpq,py->cxyq', back_z, y_expand, precision=highest)
    return jnp.einsum('cxyq,qz->cxyz', partial_a, z_expand, precision=highest) + jnp.einsum('cxyq,qz->cxyz', partial_b, z_slopes, precision=highest)

def clamped_stiffness(displaced, lame_block, shear_block):
    padded = jnp.concatenate([displaced, jnp.zeros_like(displaced[..., :1])], axis=-1)
    return stiffness(padded, lame_block, shear_block)[..., :displaced.shape[-1]]

def fault_force(tangent, slip_vector):
    return jnp.stack([tangent * slip_vector[0], lock_stiffness * slip_vector[1], tangent * slip_vector[2]])

def volume_forces(field_now, lame_first, shear_modulus):
    owned_nodes = 4 * EX
    slab_nodes = 4 * EY + 1
    blocked = field_now.reshape(3, N_DOM, owned_nodes, N_DEPTH, slab_nodes, 4 * EZ)
    next_planes = jnp.concatenate([blocked[:, 1:, :1], jnp.zeros_like(blocked[:, :1, :1])], axis=1)
    extended = jnp.concatenate([blocked, next_planes], axis=2)
    extended = jnp.transpose(extended, (1, 3, 0, 2, 4, 5))
    lame_blocks = jnp.transpose(lame_first.reshape(N_DOM, EX, N_DEPTH, EY, EZ), (0, 2, 1, 3, 4))
    shear_blocks = jnp.transpose(shear_modulus.reshape(N_DOM, EX, N_DEPTH, EY, EZ), (0, 2, 1, 3, 4))

    def per_block(entries):
        return jax.vmap(clamped_stiffness)(entries[0], entries[1], entries[2])
    element_forces = lax.map(per_block, (extended, lame_blocks, shear_blocks))
    end_planes = element_forces[:, :, :, owned_nodes]
    carried = jnp.concatenate([jnp.zeros_like(end_planes[:1]), end_planes[:-1]], axis=0)
    owned_part = element_forces[:, :, :, :owned_nodes].at[:, :, :, 0].add(carried)
    return jnp.transpose(owned_part, (2, 0, 3, 1, 4, 5)).reshape(field_now.shape)

def reference(adjoint_now, adjoint_next, lame_first, shear_modulus, density, branch_flags, weak_slope, normal_stress, patch_owner):
    slab_nodes = 4 * EY + 1
    depth_nodes = 4 * EZ
    strike_nodes = 4 * EX * N_DOM
    maps_x = element_maps(EX * N_DOM)
    maps_y = element_maps(EY)
    maps_z = element_maps(EZ)
    mass_x = jnp.asarray((maps_x[0].T @ maps_x[2])[:strike_nodes], dtype=jnp.float32)
    mass_y = jnp.asarray(np.tile(maps_y[0].T @ maps_y[2], N_DEPTH), dtype=jnp.float32)
    mass_z = jnp.asarray((maps_z[0].T @ maps_z[2])[:depth_nodes], dtype=jnp.float32)
    nodal_mass = density * mass_x[:, None, None] * mass_y[None, :, None] * mass_z[None, None, :] / 8.0
    tangent = jnp.where(branch_flags == 0, lock_stiffness, jnp.where(branch_flags == 1, -weak_slope[None], 0.0))
    response = jnp.where(branch_flags == 1, 0.5, jnp.where(branch_flags == 2, 1.0, 0.0))
    current, following = (adjoint_now, adjoint_next)
    gradient = jnp.zeros((N_DEPTH, strike_nodes, depth_nodes), jnp.float32)
    for section_index in range(STEPS):
        forces = volume_forces(current, lame_first, shear_modulus)
        slab_view = current.reshape(3, strike_nodes, N_DEPTH, slab_nodes, depth_nodes)
        minus_plane = jnp.transpose(slab_view[:, :, :, -1], (0, 2, 1, 3))
        lower_plane = jnp.transpose(slab_view[:, :, :, 0], (0, 2, 1, 3))
        plus_plane = jnp.roll(lower_plane, -1, axis=1)
        slip_vector = plus_plane - minus_plane
        pulled = fault_force(tangent[section_index], slip_vector)
        gradient = gradient + normal_stress * response[section_index] * slip_vector[0]
        from_below = jnp.roll(pulled, 1, axis=1)
        net_force = (-forces).reshape(3, strike_nodes, N_DEPTH, slab_nodes, depth_nodes)
        net_force = net_force.at[:, :, :, -1].add(jnp.transpose(pulled, (0, 2, 1, 3)))
        net_force = net_force.at[:, :, :, 0].add(-jnp.transpose(from_below, (0, 2, 1, 3)))
        net_force = net_force.reshape(current.shape)
        updated = 2.0 * current - following + time_step * time_step * (net_force / nodal_mass)
        following, current = (current, updated)

    def strand_sums(strand_gradient, strand_owner):
        return jax.ops.segment_sum(strand_gradient, strand_owner, num_segments=PATCH_DEV * N_DOM)
    patch_sums = jax.vmap(strand_sums)(gradient, patch_owner)
    return (current, following, patch_sums)
```

```python
import functools
import math

import jax
import jax.numpy as jnp
import ml_dtypes
import numpy as np
from jax import lax
from jax.experimental import pallas as pl
from jax.experimental.pallas import tpu as pltpu
from jax.sharding import PartitionSpec as P

PATCH_DEV = 2
REACH = 2

time_step = 0.01
lock_stiffness = 0.5

BLOCK = 16
PLANE = 5 * BLOCK


def basis_tables():
    points = [-1.0, -math.sqrt(3.0 / 7.0), 0.0, math.sqrt(3.0 / 7.0), 1.0]
    quad_weights = np.array([0.1, 49.0 / 90.0, 32.0 / 45.0, 49.0 / 90.0, 0.1])
    products = []
    for first in range(5):
        value = 1.0
        for other in range(5):
            if other != first:
                value = value * (points[first] - points[other])
        products.append(value)
    derivative = np.zeros((5, 5))
    for row in range(5):
        for column in range(5):
            if row == column:
                total = 0.0
                for other in range(5):
                    if other != row:
                        total = total + 1.0 / (points[row] - points[other])
                derivative[row, column] = total
            else:
                derivative[row, column] = (
                    products[row] / products[column] / (points[row] - points[column])
                )
    return (quad_weights, derivative)


def two_parts(table):
    high = table.astype(ml_dtypes.bfloat16)
    low = (table - high.astype(np.float64)).astype(ml_dtypes.bfloat16)
    return np.stack([high, low])


def element_stiffness():
    weights, derivative = basis_tables()
    eye = np.eye(5)
    slope = 2.0 * derivative
    grads = [
        np.kron(slope, np.kron(eye, eye)),
        np.kron(eye, np.kron(eye, slope)),
        np.kron(eye, np.kron(slope, eye)),
    ]
    quad = np.kron(weights, np.kron(weights, weights)) / 8.0
    first = np.zeros((125, 3, 125, 3))
    second = np.zeros((125, 3, 125, 3))
    lap = sum(g.T @ (quad[:, None] * g) for g in grads)
    for c in range(3):
        second[:, c, :, c] += lap
        for d in range(3):
            first[:, c, :, d] += grads[c].T @ (quad[:, None] * grads[d])
            second[:, c, :, d] += grads[d].T @ (quad[:, None] * grads[c])
    where = [
        node // 5 * BLOCK + node % 5 * 3 + c for node in range(125) for c in range(3)
    ]
    wide = []
    for small in (first, second):
        big = np.zeros((5 * PLANE, 5 * PLANE))
        big[np.ix_(where, where)] = small.reshape(375, 375)
        wide.append(big)
    return wide


OWN_COLS = 384
FAR_COLS = 128


@functools.cache
def stiffness_tables():
    wide = element_stiffness()
    own = 4 * PLANE
    parts = []
    for rows in (slice(0, own), slice(own, own + PLANE)):
        both = np.concatenate([w[rows] for w in wide])
        table = np.zeros((both.shape[0], OWN_COLS + FAR_COLS))
        table[:, :own] = both[:, :own]
        table[:, OWN_COLS : OWN_COLS + PLANE] = both[:, own:]
        parts.append(two_parts(table))
    return parts


@functools.cache
def layout_tables(y_elems, z_elems):
    lanes = y_elems * z_elems
    depth = 4 * z_elems
    gather = np.zeros((y_elems * depth, 5 * lanes), ml_dtypes.bfloat16)
    back = np.zeros((4 * lanes, y_elems * depth), ml_dtypes.bfloat16)
    fault = np.zeros((depth, depth), ml_dtypes.bfloat16)
    for k in range(z_elems):
        for zl in range(5):
            z = 4 * k + zl
            if z >= depth:
                continue
            for yel in range(y_elems):
                gather[yel * depth + z, zl * lanes + yel * z_elems + k] = 1
                if zl < 4:
                    back[zl * lanes + yel * z_elems + k, yel * depth + z] = 1
            if zl < 4:
                fault[z, zl * z_elems + k] = 1
    return gather, back, fault


@functools.cache
def mass_table(y_elems, z_elems):
    weights, _ = basis_tables()
    table = np.zeros((4, 5, BLOCK, y_elems, z_elems))
    for x in range(4):
        mx = 0.2 if x == 0 else weights[x]
        for zl in range(5):
            for yl in range(5):
                for yel in range(y_elems):
                    my = weights[yl]
                    if (yl == 0 and yel > 0) or (yl == 4 and yel < y_elems - 1):
                        my = 0.2
                    mz = np.full(z_elems, weights[zl])
                    if zl == 0:
                        mz[1:] = 0.2
                    if zl == 4:
                        mz[:] = 0.2
                    value = time_step * time_step * 8.0 / (mx * my * mz)
                    if zl == 4:
                        value[-1] = 0.0
                    table[x, zl, 3 * yl : 3 * yl + 3, yel] = value
    return table.reshape(4 * PLANE, y_elems * z_elems).astype(np.float32)


def pieces(value, count):
    out = []
    for _ in range(count):
        piece = value.astype(jnp.bfloat16)
        out.append(piece)
        value = value - piece.astype(jnp.float32)
    return out


def dot(a, b):
    return jnp.dot(a, b, preferred_element_type=jnp.float32)


def exact_dot(value, table, count=3):
    rows = value.shape[0]
    result = dot(jnp.concatenate(pieces(value, count), axis=0), table)
    total = result[:rows]
    for i in range(1, count):
        total = total + result[i * rows : (i + 1) * rows]
    return total


def split_dot(table_high, table_low, value):
    lanes = value.shape[1]
    high, low = pieces(value, 2)
    wide = dot(table_high, jnp.concatenate([high, low], axis=1))
    return wide[:, :lanes] + (wide[:, lanes:] + dot(table_low, high))


def to_elements(native, scratch, gather_ref, y_elems, count=3):
    scratch[...] = jnp.zeros_like(scratch)
    for c in range(3):
        for y in range(4 * y_elems + 1):
            rows = native(c, y)
            if y < 4 * y_elems:
                scratch[y // 4, pl.ds(y % 4 * 3 + c, 4, stride=BLOCK), :] = rows
            if y % 4 == 0 and y > 0:
                scratch[y // 4 - 1, pl.ds(12 + c, 4, stride=BLOCK), :] = rows
    wide = jnp.concatenate([scratch[i] for i in range(y_elems)], axis=1)
    result = exact_dot(wide, gather_ref[...], count)
    lanes = result.shape[1] // 5
    blocks = []
    for x in range(4):
        for zl in range(5):
            blocks.append(result[x * BLOCK : (x + 1) * BLOCK, zl * lanes : (zl + 1) * lanes])
    return jnp.concatenate(blocks, axis=0)


def from_elements(field, scratch, back_ref, out_ref, y_elems):
    rows = []
    for x in range(4):
        rows.append(
            jnp.concatenate(
                [field[x * PLANE + zl * BLOCK : x * PLANE + (zl + 1) * BLOCK] for zl in range(4)],
                axis=1,
            )
        )
    result = exact_dot(jnp.concatenate(rows, axis=0), back_ref[...])
    depth = result.shape[1] // y_elems
    for yel in range(y_elems):
        scratch[yel] = result[:, yel * depth : (yel + 1) * depth]
    for c in range(3):
        for y in range(4 * y_elems + 1):
            yel, yl = (y // 4, y % 4) if y < 4 * y_elems else (y_elems - 1, 4)
            out_ref[c, y] = scratch[yel, pl.ds(yl * 3 + c, 4, stride=BLOCK), :]


def block_iotas(lanes):
    return (
        lax.broadcasted_iota(jnp.int32, (8, lanes), 0),
        lax.broadcasted_iota(jnp.int32, (8, lanes), 1),
    )


def fault_message(field, z_elems):
    lanes = field.shape[1]
    row, lane = block_iotas(lanes)
    out = []
    for x in range(4):
        total = jnp.zeros((8, lanes), jnp.float32)
        for zl in range(4):
            at = x * PLANE + zl * BLOCK
            first = pltpu.roll(pltpu.roll(field[at : at + 8], 4, 0), zl * z_elems, 1)
            last = pltpu.roll(
                pltpu.roll(field[at + 8 : at + 16], 4, 0), (zl + 1) * z_elems % lanes, 1
            )
            here = lane // z_elems == zl
            total = jnp.where(here, jnp.where(row < 4, last, first), total)
        out.append(total)
    return jnp.concatenate(out, axis=0)


def swap_rows(message):
    parts = [pltpu.roll(message[i : i + 8], 4, 0) for i in range(0, message.shape[0], 8)]
    return jnp.concatenate(parts, axis=0)


def select_messages(parity, left, right):
    even = parity == 0
    return jnp.where(even, right, left), jnp.where(even, left, right)


def material_rows(lame_ref, shear_ref, spread_ref, lanes):
    y_elems, z_elems = lame_ref.shape
    both = jnp.concatenate(
        [lame_ref[...], shear_ref[...]], axis=0
    )
    tiled = exact_dot(both, spread_ref[...])
    row = lax.broadcasted_iota(jnp.int32, tiled.shape, 0)
    lane = lax.broadcasted_iota(jnp.int32, tiled.shape, 1)
    kept = jnp.where(row % y_elems == lane // z_elems, tiled, 0.0)
    return (
        jnp.sum(kept[:y_elems], axis=0, keepdims=True),
        jnp.sum(kept[y_elems:], axis=0, keepdims=True),
    )


def edge_force(edge_ref, own, lame_row, shear_row):
    lanes = own.shape[1]
    padded = jnp.concatenate(
        [own, jnp.zeros((OWN_COLS - own.shape[0], lanes), jnp.float32)], axis=0
    )
    result = split_dot(edge_ref[0, :, :OWN_COLS], edge_ref[1, :, :OWN_COLS], padded)
    force = lame_row * result[:PLANE] + shear_row * result[PLANE:]
    row = lax.broadcasted_iota(jnp.int32, force.shape, 0)
    force = jnp.where(row == BLOCK - 1, lame_row, force)
    return jnp.where(row == 2 * BLOCK - 1, shear_row, force)


def first_kernel(
    where_ref,
    now_ref,
    flags_ref,
    weak_ref,
    lame_ref,
    shear_ref,
    gather_ref,
    fault_ref,
    spread_ref,
    edge_ref,
    cur_ref,
    even_ref,
    odd_ref,
    fault_out_ref,
    material_ref,
    scratch,
):
    y_elems, z_elems = lame_ref.shape
    lanes = y_elems * z_elems
    parity = where_ref[0] % 2
    cur = to_elements(lambda c, y: now_ref[c, y], scratch, gather_ref, y_elems)
    cur_ref[...] = cur
    steps = flags_ref.shape[0]
    weak = weak_ref[...]
    tangent = []
    for i in range(steps):
        flag = flags_ref[i]
        tangent.append(
            jnp.where(flag == 0, lock_stiffness, jnp.where(flag == 1, -weak, 0.0))
        )
    tangent = exact_dot(jnp.concatenate(tangent, axis=0), fault_ref[...])
    fault_out_ref[...] = jnp.concatenate([fault_message(cur, z_elems), tangent], axis=0)
    lame_row, shear_row = material_rows(lame_ref, shear_ref, spread_ref, lanes)
    material_ref[...] = jnp.concatenate(
        [lame_row, shear_row, jnp.zeros((6, lanes), jnp.float32)], axis=0
    )
    right = edge_force(edge_ref, cur, lame_row, shear_row)
    even_ref[...], odd_ref[...] = select_messages(parity, cur[:PLANE], right)


def setup_kernel(
    where_ref,
    next_ref,
    density_ref,
    flags_ref,
    stress_ref,
    gather_ref,
    fault_ref,
    mass_ref,
    fol_ref,
    minv_ref,
    weight_ref,
    scratch,
    *,
    y_elems,
):
    fol_ref[...] = to_elements(lambda c, y: next_ref[c, y], scratch, gather_ref, y_elems)
    density = to_elements(lambda c, y: density_ref[y], scratch, gather_ref, y_elems)
    table = mass_ref[...]
    first = where_ref[0] == 0
    plane = lax.broadcasted_iota(jnp.int32, table.shape, 0) < PLANE
    table = jnp.where(jnp.logical_and(first, plane), 2.0 * table, table)
    minv_ref[...] = jnp.where(table > 0.0, table / jnp.where(table > 0.0, density, 1.0), 0.0)
    stress = stress_ref[...]
    weights = []
    for i in range(flags_ref.shape[0]):
        flag = flags_ref[i]
        weights.append(
            stress * jnp.where(flag == 1, 0.5, jnp.where(flag == 2, 1.0, 0.0))
        )
    weight_ref[...] = exact_dot(jnp.concatenate(weights, axis=0), fault_ref[...])


def advance(
    step, parity, cur, fol, minv, material, even_in, odd_in, fault_in, tangents, main_ref, edge_ref,
    own_fault, y_elems, z_elems,
):
    lanes = cur.shape[1]
    even = parity == 0
    far = jnp.where(even, even_in, odd_in)
    left = jnp.where(even, odd_in, even_in)
    lame_row, shear_row = material[0:1], material[1:2]
    zeros = jnp.zeros((FAR_COLS - PLANE, lanes), jnp.float32)
    gap = jnp.zeros((OWN_COLS - 4 * PLANE, lanes), jnp.float32)
    result = split_dot(
        main_ref[0], main_ref[1], jnp.concatenate([cur, gap, far, zeros], axis=0)
    )
    force = lame_row * result[: 4 * PLANE] + shear_row * result[4 * PLANE :]
    touch = split_dot(
        edge_ref[0, :, OWN_COLS:],
        edge_ref[1, :, OWN_COLS:],
        jnp.concatenate([cur[:PLANE], zeros], axis=0),
    )
    left_lame = left[BLOCK - 1 : BLOCK]
    left_shear = left[2 * BLOCK - 1 : 2 * BLOCK]
    from_left = left_lame * touch[:PLANE] + left_shear * touch[PLANE:] + left
    row, lane = block_iotas(lanes)
    across = lane // z_elems
    rows_first = row < 3
    rows_last = jnp.logical_and(row >= 4, row < 7)
    add_first = jnp.logical_and(rows_first, across > 0)
    take_last = jnp.logical_and(rows_last, across < y_elems - 1)
    pull_first = jnp.logical_and(rows_first, across == 0)
    pull_last = jnp.logical_and(rows_last, across == y_elems - 1)
    lane_wide = lax.broadcasted_iota(jnp.int32, (BLOCK, lanes), 1)
    above = lane_wide % z_elems != 0
    below_t, own_t = tangents
    planes = []
    for x in range(4):
        blocks = []
        for zl in range(5):
            at = x * PLANE + zl * BLOCK
            block = force[at : at + BLOCK]
            if x == 0:
                block = block + from_left[zl * BLOCK : (zl + 1) * BLOCK]
            blocks.append(block)
        blocks[0] = blocks[0] + jnp.where(above, pltpu.roll(blocks[4], 1, 1), 0.0)
        stiff = jnp.where(
            jnp.logical_or(row == 1, row == 5),
            lock_stiffness,
            jnp.where(row < 4, below_t[4 * step + x : 4 * step + x + 1], own_t[4 * step + x : 4 * step + x + 1]),
        )
        pulled = stiff * (fault_in[8 * x : 8 * x + 8] - own_fault[8 * x : 8 * x + 8])
        for zl in range(4):
            low, high = blocks[zl][:8], blocks[zl][8:]
            low = low + jnp.where(
                add_first, pltpu.roll(pltpu.roll(high, 4, 0), z_elems, 1), 0.0
            )
            high = jnp.where(
                take_last, pltpu.roll(pltpu.roll(low, 4, 0), lanes - z_elems, 1), high
            )
            low = low - jnp.where(
                pull_first, pltpu.roll(pulled, (lanes - zl * z_elems) % lanes, 1), 0.0
            )
            high = high - jnp.where(
                pull_last,
                pltpu.roll(pulled, (lanes - (zl + 1) * z_elems) % lanes, 1),
                0.0,
            )
            blocks[zl] = jnp.concatenate([low, high], axis=0)
        blocks[4] = pltpu.roll(blocks[0], lanes - 1, 1)
        planes.extend(blocks)
    return (2.0 * cur - fol) - minv * jnp.concatenate(planes, axis=0)


def fault_input(up_ref, down_ref, count):
    if down_ref is None:
        return up_ref[:count]
    up, down = up_ref[:count], down_ref[:count]
    row = lax.broadcasted_iota(jnp.int32, up.shape, 0)
    return jnp.where(row % 8 < 4, up, down)


def step_kernel(*refs, step, last, pair, y_elems, z_elems):
    refs = list(refs)
    where_ref, cur_ref, fol_ref, minv_ref, material_ref, even_ref, odd_ref = refs[:7]
    refs = refs[7:]
    up_ref = refs.pop(0)
    down_ref = None if pair else refs.pop(0)
    first_up_ref, own_ref, first_own_ref, main_ref, edge_ref = refs[:5]
    refs = refs[5:]
    parity = where_ref[0] % 2
    cur = cur_ref[...]
    tangents = (first_up_ref[32:], first_own_ref[32:])
    new = advance(
        step, parity, cur, fol_ref[...], minv_ref[...], material_ref[...], even_ref[...], odd_ref[...],
        fault_input(up_ref, down_ref, 32), tangents, main_ref, edge_ref, swap_rows(own_ref[:32]),
        y_elems, z_elems,
    )
    if last:
        back_ref, out_ref, scratch = refs
        from_elements(new, scratch, back_ref, out_ref, y_elems)
    else:
        new_ref, even_out, odd_out, fault_out = refs
        new_ref[...] = new
        fault_out[...] = fault_message(new, z_elems)
        right = edge_force(edge_ref, new, material_ref[0:1], material_ref[1:2])
        even_out[...], odd_out[...] = select_messages(parity, new[:PLANE], right)


def output_kernel(field_ref, back_ref, out_ref, scratch, *, y_elems):
    from_elements(field_ref[...], scratch, back_ref, out_ref, y_elems)


def patch_kernel(*refs, pair, steps):
    where_ref, owner_ref, weight_ref, fault_ref = refs[:4]
    messages = refs[4 : -5]
    home_out, out_a, out_b, out_c, out_d = refs[-5:]
    place = where_ref[0]
    lanes = weight_ref.shape[1]
    count = 2 if pair else 3
    grads = [jnp.zeros((8, lanes), jnp.float32) for _ in range(4)]
    for i in range(steps):
        group = messages[count * i : count * (i + 1)]
        slip = fault_input(group[1], None if pair else group[2], 32) - swap_rows(group[0][:32])
        for x in range(4):
            grads[x] = grads[x] + slip[8 * x : 8 * x + 8] * weight_ref[4 * i + x : 4 * i + x + 1]
    wide = 16
    number = lax.broadcasted_iota(jnp.int32, (wide, lanes), 0) + (place - REACH) * PATCH_DEV
    total = jnp.zeros((wide, lanes), jnp.float32)
    for x in range(4):
        total = total + jnp.where(number == owner_ref[0, x], grads[x][4:5], 0.0)
    total = exact_dot(total, fault_ref[...])
    rows = [total[2 * i : 2 * i + 2] for i in range(5)]
    home_out[...] = rows[2]
    even = place % 2 == 0
    out_a[...] = jnp.where(even, rows[3], rows[1])
    out_b[...] = jnp.where(even, rows[1], rows[3])
    low = place % 4 < 2
    out_c[...] = jnp.where(low, rows[4], rows[0])
    out_d[...] = jnp.where(low, rows[0], rows[4])


VMEM = pl.BlockSpec(memory_space=pltpu.VMEM)
SMEM = pl.BlockSpec(memory_space=pltpu.SMEM)


def kernel_call(body, outs, args, in_smem, scratch=(), **static):
    shapes = [jax.ShapeDtypeStruct(s, jnp.float32) for s in outs]
    return pl.pallas_call(
        functools.partial(body, **static) if static else body,
        out_shape=shapes,
        in_specs=[SMEM if i in in_smem else VMEM for i in range(len(args))],
        out_specs=[VMEM] * len(shapes),
        scratch_shapes=list(scratch),
        compiler_params=pltpu.CompilerParams(vmem_limit_bytes=24 * 2**20),
    )(*args)


def swapped(block, axis, distance, group):
    size = lax.axis_size(axis)
    route = []
    for left in range(size - distance):
        if left // distance % 2 == group:
            route += [(left, left + distance), (left + distance, left)]
    return lax.ppermute(block, axis, route)


def from_behind(block, axis, distance):
    size = lax.axis_size(axis)
    return lax.ppermute(block, axis, [((i - distance) % size, i) for i in range(size)])


def on_device(
    adjoint_now,
    adjoint_next,
    lame_first,
    shear_modulus,
    density,
    branch_flags,
    weak_slope,
    normal_stress,
    patch_owner,
):
    x_elems, y_elems, z_elems = lame_first.shape
    lanes = y_elems * z_elems
    assert x_elems == 1 and lanes == adjoint_now.shape[3]
    steps = branch_flags.shape[0]
    pair = lax.axis_size("depth") == 2
    place = lax.axis_index("dom").astype(jnp.int32).reshape(1)
    main_table, edge_table = (jnp.asarray(t) for t in stiffness_tables())
    gather, back, fault = (jnp.asarray(t) for t in layout_tables(y_elems, z_elems))
    spread = jnp.asarray(np.tile(np.eye(z_elems), (1, y_elems)).astype(ml_dtypes.bfloat16))
    mass = jnp.asarray(mass_table(y_elems, z_elems))
    now = jnp.transpose(adjoint_now, (0, 2, 1, 3))
    following = jnp.transpose(adjoint_next, (0, 2, 1, 3))
    rho = jnp.transpose(density, (1, 0, 2))
    flags = branch_flags[:, 0]
    native = pltpu.VMEM((y_elems, 4 * BLOCK, lanes), jnp.float32)
    field = (4 * PLANE, lanes)
    plane = (PLANE, lanes)

    def exchange(even, odd, fault_rows):
        if pair:
            faults = [from_behind(fault_rows, "depth", 1)]
        else:
            faults = [from_behind(fault_rows, "depth", 1), from_behind(fault_rows, "depth", -1)]
        return swapped(even, "dom", 1, 0), swapped(odd, "dom", 1, 1), faults

    cur, even, odd, fault_rows, material = kernel_call(
        first_kernel,
        [field, plane, plane, (32 + 4 * steps, lanes), (8, lanes)],
        (
            place, now, flags, weak_slope[0], lame_first[0], shear_modulus[0], gather, fault,
            spread, edge_table,
        ),
        (0,),
        [native],
    )
    first_fault = fault_rows
    even_in, odd_in, fault_in = exchange(even, odd, fault_rows)
    first_in = fault_in
    fol, minv, weight = kernel_call(
        setup_kernel,
        [field, field, (4 * steps, lanes)],
        (place, following, rho, flags, normal_stress[0], gather, fault, mass),
        (0,),
        [native],
        y_elems=y_elems,
    )
    seen = []
    for step in range(steps):
        last = step == steps - 1
        seen += [fault_rows] + fault_in
        args = [place, cur, fol, minv, material, even_in, odd_in] + fault_in
        args += [first_in[0], fault_rows, first_fault, main_table, edge_table]
        static = dict(step=step, last=last, pair=pair, y_elems=y_elems, z_elems=z_elems)
        if not last:
            new, even, odd, new_fault = kernel_call(
                step_kernel, [field, plane, plane, (32, lanes)], args, (0,), **static
            )
            fol, cur, fault_rows = cur, new, new_fault
            even_in, odd_in, fault_in = exchange(even, odd, fault_rows)
        else:
            sums = kernel_call(
                patch_kernel,
                [(PATCH_DEV, lanes)] * 5,
                [place, patch_owner, weight, jnp.asarray(fault.T)] + seen,
                (0, 1),
                pair=pair,
                steps=steps,
            )
            patch_sums = sums[0]
            for out, distance, group in zip(sums[1:], (1, 1, 2, 2), (0, 1, 0, 1)):
                patch_sums = patch_sums + swapped(out, "dom", distance, group)
            whole = (3, 4 * y_elems + 1, 4, lanes)
            later = kernel_call(
                output_kernel, [whole], [cur, back], (), [native], y_elems=y_elems
            )[0]
            earlier = kernel_call(
                step_kernel, [whole], args + [back], (0,), [native], **static
            )[0]
    return (
        jnp.transpose(earlier, (0, 2, 1, 3)),
        jnp.transpose(later, (0, 2, 1, 3)),
        patch_sums[None],
    )


def solution(mesh):
    return jax.shard_map(
        on_device,
        mesh=mesh,
        in_specs=(
            P(None, "dom", "depth", None),
            P(None, "dom", "depth", None),
            P("dom", "depth", None),
            P("dom", "depth", None),
            P("dom", "depth", None),
            P(None, "depth", "dom", None),
            P("depth", "dom", None),
            P("depth", "dom", None),
            P("depth", "dom"),
        ),
        out_specs=(
            P(None, "dom", "depth", None),
            P(None, "dom", "depth", None),
            P("depth", "dom", None),
        ),
        check_vma=False,
    )
```

```python
import functools
import math

import jax
import jax.numpy as jnp
import ml_dtypes
import numpy as np
from jax import lax
from jax.experimental import pallas as pl
from jax.experimental.pallas import tpu as pltpu
from jax.sharding import PartitionSpec as P

PATCH_DEV = 2
REACH = 2

time_step = 0.01
lock_stiffness = 0.5

BLOCK = 16
PLANE = 5 * BLOCK


def basis_tables():
    points = [-1.0, -math.sqrt(3.0 / 7.0), 0.0, math.sqrt(3.0 / 7.0), 1.0]
    quad_weights = np.array([0.1, 49.0 / 90.0, 32.0 / 45.0, 49.0 / 90.0, 0.1])
    products = []
    for first in range(5):
        value = 1.0
        for other in range(5):
            if other != first:
                value = value * (points[first] - points[other])
        products.append(value)
    derivative = np.zeros((5, 5))
    for row in range(5):
        for column in range(5):
            if row == column:
                total = 0.0
                for other in range(5):
                    if other != row:
                        total = total + 1.0 / (points[row] - points[other])
                derivative[row, column] = total
            else:
                derivative[row, column] = (
                    products[row] / products[column] / (points[row] - points[column])
                )
    return (quad_weights, derivative)


def two_parts(table):
    high = table.astype(ml_dtypes.bfloat16)
    low = (table - high.astype(np.float64)).astype(ml_dtypes.bfloat16)
    return np.stack([high, low])


def element_stiffness():
    weights, derivative = basis_tables()
    eye = np.eye(5)
    slope = 2.0 * derivative
    grads = [
        np.kron(slope, np.kron(eye, eye)),
        np.kron(eye, np.kron(eye, slope)),
        np.kron(eye, np.kron(slope, eye)),
    ]
    quad = np.kron(weights, np.kron(weights, weights)) / 8.0
    first = np.zeros((125, 3, 125, 3))
    second = np.zeros((125, 3, 125, 3))
    lap = sum(g.T @ (quad[:, None] * g) for g in grads)
    for c in range(3):
        second[:, c, :, c] += lap
        for d in range(3):
            first[:, c, :, d] += grads[c].T @ (quad[:, None] * grads[d])
            second[:, c, :, d] += grads[d].T @ (quad[:, None] * grads[c])
    where = [
        node // 5 * BLOCK + node % 5 * 3 + c for node in range(125) for c in range(3)
    ]
    wide = []
    for small in (first, second):
        big = np.zeros((5 * PLANE, 5 * PLANE))
        big[np.ix_(where, where)] = small.reshape(375, 375)
        wide.append(big)
    return wide


OWN_COLS = 384
FAR_COLS = 128


@functools.cache
def stiffness_tables():
    wide = element_stiffness()
    own = 4 * PLANE
    parts = []
    for rows in (slice(0, own), slice(own, own + PLANE)):
        both = np.concatenate([w[rows] for w in wide])
        table = np.zeros((both.shape[0], OWN_COLS + FAR_COLS))
        table[:, :own] = both[:, :own]
        table[:, OWN_COLS : OWN_COLS + PLANE] = both[:, own:]
        parts.append(two_parts(table))
    return parts


@functools.cache
def back_table(y_elems, z_elems):
    lanes = y_elems * z_elems
    depth = 4 * z_elems
    back = np.zeros((4 * lanes, y_elems * depth), ml_dtypes.bfloat16)
    for yel in range(y_elems):
        for k in range(z_elems):
            for zl in range(4):
                back[zl * lanes + yel * z_elems + k, yel * depth + 4 * k + zl] = 1
    return back


@functools.cache
def mass_table(y_elems, z_elems):
    weights, _ = basis_tables()
    table = np.zeros((4, 5, BLOCK, y_elems, z_elems))
    for x in range(4):
        mx = 0.2 if x == 0 else weights[x]
        for zl in range(5):
            for yl in range(5):
                for yel in range(y_elems):
                    my = weights[yl]
                    if (yl == 0 and yel > 0) or (yl == 4 and yel < y_elems - 1):
                        my = 0.2
                    mz = np.full(z_elems, weights[zl])
                    if zl == 0:
                        mz[1:] = 0.2
                    if zl == 4:
                        mz[:] = 0.2
                    value = time_step * time_step * 8.0 / (mx * my * mz)
                    if zl == 4:
                        value[-1] = 0.0
                    table[x, zl, 3 * yl : 3 * yl + 3, yel] = value
    return table.reshape(4 * PLANE, y_elems * z_elems).astype(np.float32)


def pieces(value, count):
    out = []
    for _ in range(count):
        piece = value.astype(jnp.bfloat16)
        out.append(piece)
        value = value - piece.astype(jnp.float32)
    return out


def dot(a, b):
    return jnp.dot(a, b, preferred_element_type=jnp.float32)


def exact_dot(value, table, count=3):
    rows = value.shape[0]
    result = dot(jnp.concatenate(pieces(value, count), axis=0), table)
    total = result[:rows]
    for i in range(1, count):
        total = total + result[i * rows : (i + 1) * rows]
    return total


def split_dot(table_high, table_low, value):
    lanes = value.shape[1]
    high, low = pieces(value, 2)
    wide = dot(table_high, jnp.concatenate([high, low], axis=1))
    return wide[:, :lanes] + (wide[:, lanes:] + dot(table_low, high))


def ones_where(rule, shape):
    row = lax.broadcasted_iota(jnp.int32, shape, 0)
    column = lax.broadcasted_iota(jnp.int32, shape, 1)
    return jnp.where(rule(row, column), 1.0, 0.0).astype(jnp.bfloat16)


def gather_table(lanes, z_elems):
    return ones_where(lambda z, c: z == 4 * (c % z_elems) + c // lanes, (lanes, 5 * lanes))


def fault_table(lanes, z_elems):
    return ones_where(lambda z, c: z == 4 * (c % z_elems) + c // z_elems, (lanes, lanes))


def fault_table_back(lanes, z_elems):
    return ones_where(lambda c, z: z == 4 * (c % z_elems) + c // z_elems, (lanes, lanes))


def to_elements(native, scratch, table, y_elems):
    group = 4 * BLOCK
    scratch[...] = jnp.zeros_like(scratch)
    for c in range(3):
        for y in range(4 * y_elems + 1):
            rows = native(c, y)
            if y < 4 * y_elems:
                scratch[y // 4, pl.ds(y % 4 * 3 + c, 4, stride=BLOCK), :] = rows
            if y % 4 == 0 and y > 0:
                scratch[y // 4 - 1, pl.ds(12 + c, 4, stride=BLOCK), :] = rows
    high, middle, low = pieces(
        jnp.concatenate([scratch[i] for i in range(y_elems)], axis=0), 3
    )
    result = dot(
        jnp.concatenate([high, middle], axis=1), jnp.concatenate([table, table], axis=0)
    ) + dot(low, table)
    lanes = result.shape[1] // 5
    across = lax.broadcasted_iota(jnp.int32, (group, result.shape[1]), 1) % lanes // (
        lanes // y_elems
    )
    total = result[:group]
    for yel in range(1, y_elems):
        total = jnp.where(across == yel, result[yel * group : (yel + 1) * group], total)
    blocks = []
    for x in range(4):
        for zl in range(5):
            blocks.append(total[x * BLOCK : (x + 1) * BLOCK, zl * lanes : (zl + 1) * lanes])
    return jnp.concatenate(blocks, axis=0)


def from_elements(field, scratch, back_ref, out_ref, y_elems):
    rows = []
    for x in range(4):
        rows.append(
            jnp.concatenate(
                [field[x * PLANE + zl * BLOCK : x * PLANE + (zl + 1) * BLOCK] for zl in range(4)],
                axis=1,
            )
        )
    result = exact_dot(jnp.concatenate(rows, axis=0), back_ref[...])
    depth = result.shape[1] // y_elems
    for yel in range(y_elems):
        scratch[yel] = result[:, yel * depth : (yel + 1) * depth]
    for c in range(3):
        for y in range(4 * y_elems + 1):
            yel, yl = (y // 4, y % 4) if y < 4 * y_elems else (y_elems - 1, 4)
            out_ref[c, y] = scratch[yel, pl.ds(yl * 3 + c, 4, stride=BLOCK), :]


def block_iotas(lanes):
    return (
        lax.broadcasted_iota(jnp.int32, (8, lanes), 0),
        lax.broadcasted_iota(jnp.int32, (8, lanes), 1),
    )


def fault_message(field, z_elems):
    lanes = field.shape[1]
    row, lane = block_iotas(lanes)
    out = []
    for x in range(4):
        total = jnp.zeros((8, lanes), jnp.float32)
        for zl in range(4):
            at = x * PLANE + zl * BLOCK
            first = pltpu.roll(pltpu.roll(field[at : at + 8], 4, 0), zl * z_elems, 1)
            last = pltpu.roll(
                pltpu.roll(field[at + 8 : at + 16], 4, 0), (zl + 1) * z_elems % lanes, 1
            )
            here = lane // z_elems == zl
            total = jnp.where(here, jnp.where(row < 4, last, first), total)
        out.append(total)
    return jnp.concatenate(out, axis=0)


def swap_rows(message):
    parts = [pltpu.roll(message[i : i + 8], 4, 0) for i in range(0, message.shape[0], 8)]
    return jnp.concatenate(parts, axis=0)


def select_messages(parity, left, right):
    even = parity == 0
    return jnp.where(even, right, left), jnp.where(even, left, right)


def material_rows(lame_ref, shear_ref):
    y_elems, z_elems = lame_ref.shape
    both = jnp.concatenate([lame_ref[...], shear_ref[...]], axis=0)
    spread = ones_where(lambda k, c: c % z_elems == k, (z_elems, y_elems * z_elems))
    tiled = exact_dot(both, spread)
    row = lax.broadcasted_iota(jnp.int32, tiled.shape, 0)
    lane = lax.broadcasted_iota(jnp.int32, tiled.shape, 1)
    kept = jnp.where(row % y_elems == lane // z_elems, tiled, 0.0)
    return (
        jnp.sum(kept[:y_elems], axis=0, keepdims=True),
        jnp.sum(kept[y_elems:], axis=0, keepdims=True),
    )


def above_lanes(lanes, z_elems):
    return lax.broadcasted_iota(jnp.int32, (BLOCK, lanes), 1) % z_elems != 0


def edge_force(edge_ref, own, lame_row, shear_row, z_elems):
    lanes = own.shape[1]
    padded = jnp.concatenate(
        [own, jnp.zeros((OWN_COLS - own.shape[0], lanes), jnp.float32)], axis=0
    )
    result = split_dot(edge_ref[0, :, :OWN_COLS], edge_ref[1, :, :OWN_COLS], padded)
    force = lame_row * result[:PLANE] + shear_row * result[PLANE:]
    top = force[:BLOCK] + jnp.where(
        above_lanes(lanes, z_elems), pltpu.roll(force[4 * BLOCK :], 1, 1), 0.0
    )
    row = lax.broadcasted_iota(jnp.int32, top.shape, 0)
    top = jnp.where(row == BLOCK - 1, lame_row, top)
    second = jnp.where(row == BLOCK - 1, shear_row, force[BLOCK : 2 * BLOCK])
    return jnp.concatenate([top, second, force[2 * BLOCK : 4 * BLOCK]], axis=0)


def start_copies(pairs, sems):
    copies = [
        pltpu.make_async_copy(source, target, sems.at[i])
        for i, (source, target) in enumerate(pairs)
    ]
    for copy in copies:
        copy.start()
    return copies


def first_kernel(
    where_ref,
    now_hbm,
    flags_hbm,
    weak_hbm,
    lame_hbm,
    shear_hbm,
    edge_hbm,
    cur_ref,
    even_ref,
    odd_ref,
    fault_out_ref,
    material_ref,
    scratch,
    now_ref,
    flags_ref,
    weak_ref,
    lame_ref,
    shear_ref,
    edge_ref,
    sems,
):
    copies = start_copies(
        [
            (now_hbm, now_ref),
            (flags_hbm, flags_ref),
            (weak_hbm, weak_ref),
            (lame_hbm, lame_ref),
            (shear_hbm, shear_ref),
            (edge_hbm, edge_ref),
        ],
        sems,
    )
    y_elems, z_elems = lame_ref.shape
    lanes = y_elems * z_elems
    parity = where_ref[0] % 2
    gather = gather_table(lanes, z_elems)
    fault = fault_table(lanes, z_elems)
    copies[0].wait()
    cur = to_elements(lambda c, y: now_ref[c, y], scratch, gather, y_elems)
    cur_ref[...] = cur
    steps = flags_ref.shape[0]
    copies[1].wait()
    copies[2].wait()
    weak = weak_ref[...]
    tangent = []
    for i in range(steps):
        flag = flags_ref[i]
        tangent.append(
            jnp.where(flag == 0, lock_stiffness, jnp.where(flag == 1, -weak, 0.0))
        )
    tangent = exact_dot(jnp.concatenate(tangent, axis=0), fault)
    fault_out_ref[...] = jnp.concatenate([fault_message(cur, z_elems), tangent], axis=0)
    copies[3].wait()
    copies[4].wait()
    lame_row, shear_row = material_rows(lame_ref, shear_ref)
    material_ref[...] = jnp.concatenate(
        [lame_row, shear_row, jnp.zeros((6, lanes), jnp.float32)], axis=0
    )
    copies[5].wait()
    right = edge_force(edge_ref, cur, lame_row, shear_row, z_elems)
    even_ref[...], odd_ref[...] = select_messages(parity, cur[: 4 * BLOCK], right)


def setup_kernel(
    where_ref,
    next_hbm,
    density_hbm,
    flags_hbm,
    stress_hbm,
    mass_hbm,
    fol_ref,
    minv_ref,
    weight_ref,
    scratch,
    next_ref,
    density_ref,
    flags_ref,
    stress_ref,
    mass_ref,
    sems,
    *,
    y_elems,
    z_elems,
):
    copies = start_copies(
        [
            (next_hbm, next_ref),
            (density_hbm, density_ref),
            (flags_hbm, flags_ref),
            (stress_hbm, stress_ref),
            (mass_hbm, mass_ref),
        ],
        sems,
    )
    gather = gather_table(y_elems * z_elems, z_elems)
    fault = fault_table(y_elems * z_elems, z_elems)
    for copy in copies:
        copy.wait()
    fol_ref[...] = to_elements(lambda c, y: next_ref[c, y], scratch, gather, y_elems)
    density = to_elements(lambda c, y: density_ref[y], scratch, gather, y_elems)
    table = mass_ref[...]
    first = where_ref[0] == 0
    plane = lax.broadcasted_iota(jnp.int32, table.shape, 0) < PLANE
    table = jnp.where(jnp.logical_and(first, plane), 2.0 * table, table)
    minv_ref[...] = jnp.where(table > 0.0, table / jnp.where(table > 0.0, density, 1.0), 0.0)
    stress = stress_ref[...]
    weights = []
    for i in range(flags_ref.shape[0]):
        flag = flags_ref[i]
        weights.append(
            stress * jnp.where(flag == 1, 0.5, jnp.where(flag == 2, 1.0, 0.0))
        )
    weight_ref[...] = exact_dot(jnp.concatenate(weights, axis=0), fault)


def advance(
    step, place, last_place, cur, fol, minv, material, even_in, odd_in, fault_in, tangents, main_ref, edge_ref,
    own_fault, y_elems, z_elems,
):
    lanes = cur.shape[1]
    even = place % 2 == 0
    far = jnp.where(place == last_place, 0.0, jnp.where(even, even_in, odd_in))
    left = jnp.where(place == 0, 0.0, jnp.where(even, odd_in, even_in))
    lane_wide = lax.broadcasted_iota(jnp.int32, (BLOCK, lanes), 1)
    below = jnp.where(
        lane_wide % z_elems != z_elems - 1, pltpu.roll(far[:BLOCK], lanes - 1, 1), 0.0
    )
    far = jnp.concatenate([far, below], axis=0)
    lame_row, shear_row = material[0:1], material[1:2]
    zeros = jnp.zeros((FAR_COLS - PLANE, lanes), jnp.float32)
    gap = jnp.zeros((OWN_COLS - 4 * PLANE, lanes), jnp.float32)
    result = split_dot(
        main_ref[0], main_ref[1], jnp.concatenate([cur, gap, far, zeros], axis=0)
    )
    force = lame_row * result[: 4 * PLANE] + shear_row * result[4 * PLANE :]
    touch = split_dot(
        edge_ref[0, :, OWN_COLS:],
        edge_ref[1, :, OWN_COLS:],
        jnp.concatenate([cur[:PLANE], zeros], axis=0),
    )
    left_lame = left[BLOCK - 1 : BLOCK]
    left_shear = left[2 * BLOCK - 1 : 2 * BLOCK]
    from_left = left_lame * touch[:PLANE] + left_shear * touch[PLANE:]
    from_left = jnp.concatenate([from_left[: 4 * BLOCK] + left, from_left[4 * BLOCK :]], axis=0)
    row, lane = block_iotas(lanes)
    across = lane // z_elems
    rows_first = row < 3
    rows_last = jnp.logical_and(row >= 4, row < 7)
    add_first = jnp.logical_and(rows_first, across > 0)
    take_last = jnp.logical_and(rows_last, across < y_elems - 1)
    pull_first = jnp.logical_and(rows_first, across == 0)
    pull_last = jnp.logical_and(rows_last, across == y_elems - 1)
    above = above_lanes(lanes, z_elems)
    below_t, own_t = tangents
    planes = []
    for x in range(4):
        blocks = []
        for zl in range(5):
            at = x * PLANE + zl * BLOCK
            block = force[at : at + BLOCK]
            if x == 0:
                block = block + from_left[zl * BLOCK : (zl + 1) * BLOCK]
            blocks.append(block)
        blocks[0] = blocks[0] + jnp.where(above, pltpu.roll(blocks[4], 1, 1), 0.0)
        stiff = jnp.where(
            jnp.logical_or(row == 1, row == 5),
            lock_stiffness,
            jnp.where(row < 4, below_t[4 * step + x : 4 * step + x + 1], own_t[4 * step + x : 4 * step + x + 1]),
        )
        pulled = stiff * (fault_in[8 * x : 8 * x + 8] - own_fault[8 * x : 8 * x + 8])
        for zl in range(4):
            low, high = blocks[zl][:8], blocks[zl][8:]
            low = low + jnp.where(
                add_first, pltpu.roll(pltpu.roll(high, 4, 0), z_elems, 1), 0.0
            )
            high = jnp.where(
                take_last, pltpu.roll(pltpu.roll(low, 4, 0), lanes - z_elems, 1), high
            )
            low = low - jnp.where(
                pull_first, pltpu.roll(pulled, (lanes - zl * z_elems) % lanes, 1), 0.0
            )
            high = high - jnp.where(
                pull_last,
                pltpu.roll(pulled, (lanes - (zl + 1) * z_elems) % lanes, 1),
                0.0,
            )
            blocks[zl] = jnp.concatenate([low, high], axis=0)
        blocks[4] = pltpu.roll(blocks[0], lanes - 1, 1)
        planes.extend(blocks)
    return (2.0 * cur - fol) - minv * jnp.concatenate(planes, axis=0)


def fault_input(up_ref, down_ref, count):
    if down_ref is None:
        return up_ref[:count]
    up, down = up_ref[:count], down_ref[:count]
    row = lax.broadcasted_iota(jnp.int32, up.shape, 0)
    return jnp.where(row % 8 < 4, up, down)


def step_kernel(*refs, step, last, last_place, pair, y_elems, z_elems):
    refs = list(refs)
    where_ref, cur_ref, fol_ref, minv_ref, material_ref, even_ref, odd_ref = refs[:7]
    refs = refs[7:]
    up_ref = refs.pop(0)
    down_ref = None if pair else refs.pop(0)
    first_up_ref, own_ref, first_own_ref, main_ref, edge_ref = refs[:5]
    refs = refs[5:]
    place = where_ref[0]
    cur = cur_ref[...]
    tangents = (first_up_ref[32:], first_own_ref[32:])
    new = advance(
        step, place, last_place, cur, fol_ref[...], minv_ref[...], material_ref[...], even_ref[...], odd_ref[...],
        fault_input(up_ref, down_ref, 32), tangents, main_ref, edge_ref, swap_rows(own_ref[:32]),
        y_elems, z_elems,
    )
    if last:
        _, back_ref, out_ref, scratch = refs
        from_elements(new, scratch, back_ref, out_ref, y_elems)
    else:
        new_ref, even_out, odd_out, fault_out = refs
        new_ref[...] = new
        fault_out[...] = fault_message(new, z_elems)
        right = edge_force(edge_ref, new, material_ref[0:1], material_ref[1:2], z_elems)
        even_out[...], odd_out[...] = select_messages(place % 2, new[: 4 * BLOCK], right)


def output_kernel(field_ref, back_ref, out_ref, scratch, *, y_elems):
    from_elements(field_ref[...], scratch, back_ref, out_ref, y_elems)


def patch_kernel(*refs, pair, steps, z_elems):
    where_ref, owner_ref, weight_ref = refs[:3]
    messages = refs[5:-5]
    home_out, out_a, out_b, out_c, out_d = refs[-5:]
    place = where_ref[0]
    lanes = weight_ref.shape[1]
    count = 2 if pair else 3
    grads = [jnp.zeros((8, lanes), jnp.float32) for _ in range(4)]
    for i in range(steps):
        group = messages[count * i : count * (i + 1)]
        slip = fault_input(group[1], None if pair else group[2], 32) - swap_rows(group[0][:32])
        for x in range(4):
            grads[x] = grads[x] + slip[8 * x : 8 * x + 8] * weight_ref[4 * i + x : 4 * i + x + 1]
    wide = 16
    number = lax.broadcasted_iota(jnp.int32, (wide, lanes), 0) + (place - REACH) * PATCH_DEV
    total = jnp.zeros((wide, lanes), jnp.float32)
    for x in range(4):
        total = total + jnp.where(number == owner_ref[0, x], grads[x][4:5], 0.0)
    total = exact_dot(total, fault_table_back(lanes, z_elems))
    rows = [total[2 * i : 2 * i + 2] for i in range(5)]
    home_out[...] = rows[2]
    even = place % 2 == 0
    out_a[...] = jnp.where(even, rows[3], rows[1])
    out_b[...] = jnp.where(even, rows[1], rows[3])
    low = place % 4 < 2
    out_c[...] = jnp.where(low, rows[4], rows[0])
    out_d[...] = jnp.where(low, rows[0], rows[4])


VMEM = pl.BlockSpec(memory_space=pltpu.VMEM)
HBM = pl.BlockSpec(memory_space=pltpu.HBM)
SMEM = pl.BlockSpec(memory_space=pltpu.SMEM)


def kernel_call(body, outs, args, in_smem, scratch=(), in_hbm=(), **static):
    shapes = [jax.ShapeDtypeStruct(s, jnp.float32) for s in outs]
    specs = [SMEM if i in in_smem else HBM if i in in_hbm else VMEM for i in range(len(args))]
    copied = [pltpu.VMEM(args[i].shape, args[i].dtype) for i in in_hbm]
    if in_hbm:
        copied.append(pltpu.SemaphoreType.DMA((len(in_hbm),)))
    return pl.pallas_call(
        functools.partial(body, **static) if static else body,
        out_shape=shapes,
        in_specs=specs,
        out_specs=[VMEM] * len(shapes),
        scratch_shapes=list(scratch) + copied,
        compiler_params=pltpu.CompilerParams(vmem_limit_bytes=24 * 2**20),
    )(*args)


def swapped(block, axis, distance, group):
    size = lax.axis_size(axis)
    route = {i: i for i in range(size)}
    for left in range(size - distance):
        if left // distance % 2 == group:
            route[left], route[left + distance] = left + distance, left
    return lax.ppermute(block, axis, list(route.items()))


def from_behind(block, axis, distance):
    size = lax.axis_size(axis)
    return lax.ppermute(block, axis, [((i - distance) % size, i) for i in range(size)])


def on_device(
    adjoint_now,
    adjoint_next,
    lame_first,
    shear_modulus,
    density,
    branch_flags,
    weak_slope,
    normal_stress,
    patch_owner,
):
    x_elems, y_elems, z_elems = lame_first.shape
    lanes = y_elems * z_elems
    assert x_elems == 1 and lanes == adjoint_now.shape[3]
    steps = branch_flags.shape[0]
    pair = lax.axis_size("depth") == 2
    place = lax.axis_index("dom").astype(jnp.int32).reshape(1)
    main_table, edge_table = (jnp.asarray(t) for t in stiffness_tables())
    back = jnp.asarray(back_table(y_elems, z_elems))
    mass = jnp.asarray(mass_table(y_elems, z_elems))
    now = jnp.transpose(adjoint_now, (0, 2, 1, 3))
    following = jnp.transpose(adjoint_next, (0, 2, 1, 3))
    rho = jnp.transpose(density, (1, 0, 2))
    flags = branch_flags[:, 0]
    native = pltpu.VMEM((y_elems, 4 * BLOCK, lanes), jnp.float32)
    field = (4 * PLANE, lanes)
    plane = (4 * BLOCK, lanes)

    def exchange(even, odd, fault_rows):
        if pair:
            faults = [from_behind(fault_rows, "depth", 1)]
        else:
            faults = [from_behind(fault_rows, "depth", 1), from_behind(fault_rows, "depth", -1)]
        return swapped(even, "dom", 1, 0), swapped(odd, "dom", 1, 1), faults

    cur, even, odd, fault_rows, material = kernel_call(
        first_kernel,
        [field, plane, plane, (32 + 4 * steps, lanes), (8, lanes)],
        (
            place, now, flags, weak_slope[0], lame_first[0], shear_modulus[0], edge_table,
        ),
        (0,),
        [native],
        range(1, 7),
    )
    first_fault = fault_rows
    even_in, odd_in, fault_in = exchange(even, odd, fault_rows)
    first_in = fault_in
    fol, minv, weight = kernel_call(
        setup_kernel,
        [field, field, (4 * steps, lanes)],
        (place, following, rho, flags, normal_stress[0], mass),
        (0,),
        [native],
        range(1, 6),
        y_elems=y_elems,
        z_elems=z_elems,
    )
    seen = []
    for step in range(steps):
        last = step == steps - 1
        seen += [fault_rows] + fault_in
        args = [place, cur, fol, minv, material, even_in, odd_in] + fault_in
        args += [first_in[0], fault_rows, first_fault, main_table, edge_table]
        static = dict(
            step=step, last=last, last_place=lax.axis_size("dom") - 1, pair=pair, y_elems=y_elems,
            z_elems=z_elems,
        )
        if not last:
            new, even, odd, new_fault = kernel_call(
                step_kernel, [field, plane, plane, (32, lanes)], args, (0,), **static
            )
            fol, cur, fault_rows = cur, new, new_fault
            even_in, odd_in, fault_in = exchange(even, odd, fault_rows)
        else:
            sums = kernel_call(
                patch_kernel,
                [(PATCH_DEV, lanes)] * 5,
                [place, patch_owner, weight, even_in, odd_in] + seen,
                (0, 1),
                pair=pair,
                steps=steps,
                z_elems=z_elems,
            )
            patch_sums = sums[0]
            for out, distance, group in zip(sums[1:], (1, 1, 2, 2), (0, 1, 0, 1)):
                patch_sums = patch_sums + swapped(out, "dom", distance, group)
            whole = (3, 4 * y_elems + 1, 4, lanes)
            later = kernel_call(
                output_kernel, [whole], [cur, back], (), [native], y_elems=y_elems
            )[0]
            earlier = kernel_call(
                step_kernel, [whole], args + [sums[0], back], (0,), [native], **static
            )[0]
    return (
        jnp.transpose(earlier, (0, 2, 1, 3)),
        jnp.transpose(later, (0, 2, 1, 3)),
        patch_sums[None],
    )


def solution(mesh):
    return jax.shard_map(
        on_device,
        mesh=mesh,
        in_specs=(
            P(None, "dom", "depth", None),
            P(None, "dom", "depth", None),
            P("dom", "depth", None),
            P("dom", "depth", None),
            P("dom", "depth", None),
            P(None, "depth", "dom", None),
            P("depth", "dom", None),
            P("depth", "dom", None),
            P("depth", "dom"),
        ),
        out_specs=(
            P(None, "dom", "depth", None),
            P(None, "dom", "depth", None),
            P("depth", "dom", None),
        ),
        check_vma=False,
    )
```

```python
import functools
import math

import jax
import jax.numpy as jnp
import ml_dtypes
import numpy as np
from jax import lax
from jax.experimental import pallas as pl
from jax.experimental.pallas import tpu as pltpu
from jax.sharding import PartitionSpec as P

PATCH_DEV = 2
REACH = 2

time_step = 0.01
lock_stiffness = 0.5

BLOCK = 16
PLANE = 5 * BLOCK


def basis_tables():
    points = [-1.0, -math.sqrt(3.0 / 7.0), 0.0, math.sqrt(3.0 / 7.0), 1.0]
    quad_weights = np.array([0.1, 49.0 / 90.0, 32.0 / 45.0, 49.0 / 90.0, 0.1])
    products = []
    for first in range(5):
        value = 1.0
        for other in range(5):
            if other != first:
                value = value * (points[first] - points[other])
        products.append(value)
    derivative = np.zeros((5, 5))
    for row in range(5):
        for column in range(5):
            if row == column:
                total = 0.0
                for other in range(5):
                    if other != row:
                        total = total + 1.0 / (points[row] - points[other])
                derivative[row, column] = total
            else:
                derivative[row, column] = (
                    products[row] / products[column] / (points[row] - points[column])
                )
    return (quad_weights, derivative)


def two_parts(table):
    high = table.astype(ml_dtypes.bfloat16)
    low = (table - high.astype(np.float64)).astype(ml_dtypes.bfloat16)
    return np.stack([high, low])


def element_stiffness():
    weights, derivative = basis_tables()
    eye = np.eye(5)
    slope = 2.0 * derivative
    grads = [
        np.kron(slope, np.kron(eye, eye)),
        np.kron(eye, np.kron(eye, slope)),
        np.kron(eye, np.kron(slope, eye)),
    ]
    quad = np.kron(weights, np.kron(weights, weights)) / 8.0
    first = np.zeros((125, 3, 125, 3))
    second = np.zeros((125, 3, 125, 3))
    lap = sum(g.T @ (quad[:, None] * g) for g in grads)
    for c in range(3):
        second[:, c, :, c] += lap
        for d in range(3):
            first[:, c, :, d] += grads[c].T @ (quad[:, None] * grads[d])
            second[:, c, :, d] += grads[d].T @ (quad[:, None] * grads[c])
    where = [
        node // 5 * BLOCK + node % 5 * 3 + c for node in range(125) for c in range(3)
    ]
    wide = []
    for small in (first, second):
        big = np.zeros((5 * PLANE, 5 * PLANE))
        big[np.ix_(where, where)] = small.reshape(375, 375)
        wide.append(big)
    return wide


OWN_COLS = 384
FAR_COLS = 128


@functools.cache
def stiffness_tables():
    wide = element_stiffness()
    own = 4 * PLANE
    parts = []
    for rows in (slice(0, own), slice(own, own + PLANE)):
        both = np.concatenate([w[rows] for w in wide])
        table = np.zeros((both.shape[0], OWN_COLS + FAR_COLS))
        table[:, :own] = both[:, :own]
        table[:, OWN_COLS : OWN_COLS + PLANE] = both[:, own:]
        parts.append(two_parts(table))
    return parts


@functools.cache
def back_table(y_elems, z_elems):
    lanes = y_elems * z_elems
    depth = 4 * z_elems
    back = np.zeros((4 * lanes, y_elems * depth), ml_dtypes.bfloat16)
    for yel in range(y_elems):
        for k in range(z_elems):
            for zl in range(4):
                back[zl * lanes + yel * z_elems + k, yel * depth + 4 * k + zl] = 1
    return back


@functools.cache
def mass_table(y_elems, z_elems):
    weights, _ = basis_tables()
    table = np.zeros((4, 5, BLOCK, y_elems, z_elems))
    for x in range(4):
        mx = 0.2 if x == 0 else weights[x]
        for zl in range(5):
            for yl in range(5):
                for yel in range(y_elems):
                    my = weights[yl]
                    if (yl == 0 and yel > 0) or (yl == 4 and yel < y_elems - 1):
                        my = 0.2
                    mz = np.full(z_elems, weights[zl])
                    if zl == 0:
                        mz[1:] = 0.2
                    if zl == 4:
                        mz[:] = 0.2
                    value = time_step * time_step * 8.0 / (mx * my * mz)
                    if zl == 4:
                        value[-1] = 0.0
                    table[x, zl, 3 * yl : 3 * yl + 3, yel] = value
    return table.reshape(4 * PLANE, y_elems * z_elems).astype(np.float32)


def pieces(value, count):
    out = []
    for _ in range(count):
        piece = value.astype(jnp.bfloat16)
        out.append(piece)
        value = value - piece.astype(jnp.float32)
    return out


def dot(a, b):
    return jnp.dot(a, b, preferred_element_type=jnp.float32)


def exact_dot(value, table, count=3):
    rows = value.shape[0]
    result = dot(jnp.concatenate(pieces(value, count), axis=0), table)
    total = result[:rows]
    for i in range(1, count):
        total = total + result[i * rows : (i + 1) * rows]
    return total


def split_dot(table_high, table_low, value):
    lanes = value.shape[1]
    high, low = pieces(value, 2)
    wide = dot(table_high, jnp.concatenate([high, low], axis=1))
    return wide[:, :lanes] + (wide[:, lanes:] + dot(table_low, high))


def ones_where(rule, shape):
    row = lax.broadcasted_iota(jnp.int32, shape, 0)
    column = lax.broadcasted_iota(jnp.int32, shape, 1)
    return jnp.where(rule(row, column), 1.0, 0.0).astype(jnp.bfloat16)


def gather_table(lanes, z_elems):
    return ones_where(lambda z, c: z == 4 * (c % z_elems) + c // lanes, (lanes, 5 * lanes))


def fault_table(lanes, z_elems):
    return ones_where(lambda z, c: z == 4 * (c % z_elems) + c // z_elems, (lanes, lanes))


def fault_table_back(lanes, z_elems):
    return ones_where(lambda c, z: z == 4 * (c % z_elems) + c // z_elems, (lanes, lanes))


def to_elements(native, scratch, table, y_elems):
    group = 4 * BLOCK
    scratch[...] = jnp.zeros_like(scratch)
    for c in range(3):
        for y in range(4 * y_elems + 1):
            rows = native(c, y)
            if y < 4 * y_elems:
                scratch[y // 4, pl.ds(y % 4 * 3 + c, 4, stride=BLOCK), :] = rows
            if y % 4 == 0 and y > 0:
                scratch[y // 4 - 1, pl.ds(12 + c, 4, stride=BLOCK), :] = rows
    high, middle, low = pieces(
        jnp.concatenate([scratch[i] for i in range(y_elems)], axis=0), 3
    )
    result = dot(
        jnp.concatenate([high, middle], axis=1), jnp.concatenate([table, table], axis=0)
    ) + dot(low, table)
    lanes = result.shape[1] // 5
    across = lax.broadcasted_iota(jnp.int32, (group, result.shape[1]), 1) % lanes // (
        lanes // y_elems
    )
    total = result[:group]
    for yel in range(1, y_elems):
        total = jnp.where(across == yel, result[yel * group : (yel + 1) * group], total)
    blocks = []
    for x in range(4):
        for zl in range(5):
            blocks.append(total[x * BLOCK : (x + 1) * BLOCK, zl * lanes : (zl + 1) * lanes])
    return jnp.concatenate(blocks, axis=0)


def from_elements(field, scratch, back_ref, out_ref, y_elems):
    rows = []
    for x in range(4):
        rows.append(
            jnp.concatenate(
                [field[x * PLANE + zl * BLOCK : x * PLANE + (zl + 1) * BLOCK] for zl in range(4)],
                axis=1,
            )
        )
    result = exact_dot(jnp.concatenate(rows, axis=0), back_ref[...])
    depth = result.shape[1] // y_elems
    for yel in range(y_elems):
        scratch[yel] = result[:, yel * depth : (yel + 1) * depth]
    for c in range(3):
        for y in range(4 * y_elems + 1):
            yel, yl = (y // 4, y % 4) if y < 4 * y_elems else (y_elems - 1, 4)
            out_ref[c, y] = scratch[yel, pl.ds(yl * 3 + c, 4, stride=BLOCK), :]


def block_iotas(lanes):
    return (
        lax.broadcasted_iota(jnp.int32, (8, lanes), 0),
        lax.broadcasted_iota(jnp.int32, (8, lanes), 1),
    )


def fault_message(field, z_elems):
    lanes = field.shape[1]
    row, lane = block_iotas(lanes)
    out = []
    for x in range(4):
        total = jnp.zeros((8, lanes), jnp.float32)
        for zl in range(4):
            at = x * PLANE + zl * BLOCK
            first = pltpu.roll(pltpu.roll(field[at : at + 8], 4, 0), zl * z_elems, 1)
            last = pltpu.roll(
                pltpu.roll(field[at + 8 : at + 16], 4, 0), (zl + 1) * z_elems % lanes, 1
            )
            here = lane // z_elems == zl
            total = jnp.where(here, jnp.where(row < 4, last, first), total)
        out.append(total)
    return jnp.concatenate(out, axis=0)


def swap_rows(message):
    parts = [pltpu.roll(message[i : i + 8], 4, 0) for i in range(0, message.shape[0], 8)]
    return jnp.concatenate(parts, axis=0)


def material_rows(lame_ref, shear_ref):
    y_elems, z_elems = lame_ref.shape
    both = jnp.concatenate([lame_ref[...], shear_ref[...]], axis=0)
    spread = ones_where(lambda k, c: c % z_elems == k, (z_elems, y_elems * z_elems))
    tiled = exact_dot(both, spread)
    row = lax.broadcasted_iota(jnp.int32, tiled.shape, 0)
    lane = lax.broadcasted_iota(jnp.int32, tiled.shape, 1)
    kept = jnp.where(row % y_elems == lane // z_elems, tiled, 0.0)
    return (
        jnp.sum(kept[:y_elems], axis=0, keepdims=True),
        jnp.sum(kept[y_elems:], axis=0, keepdims=True),
    )


def above_lanes(lanes, z_elems):
    return lax.broadcasted_iota(jnp.int32, (BLOCK, lanes), 1) % z_elems != 0


def edge_force(edge_ref, own, lame_row, shear_row, z_elems):
    lanes = own.shape[1]
    padded = jnp.concatenate(
        [own, jnp.zeros((OWN_COLS - own.shape[0], lanes), jnp.float32)], axis=0
    )
    result = split_dot(edge_ref[0, :, :OWN_COLS], edge_ref[1, :, :OWN_COLS], padded)
    force = lame_row * result[:PLANE] + shear_row * result[PLANE:]
    top = force[:BLOCK] + jnp.where(
        above_lanes(lanes, z_elems), pltpu.roll(force[4 * BLOCK :], 1, 1), 0.0
    )
    row = lax.broadcasted_iota(jnp.int32, top.shape, 0)
    top = jnp.where(row == BLOCK - 1, lame_row, top)
    second = jnp.where(row == BLOCK - 1, shear_row, force[BLOCK : 2 * BLOCK])
    return jnp.concatenate([top, second, force[2 * BLOCK : 4 * BLOCK]], axis=0)


def start_copies(pairs, sems):
    copies = [
        pltpu.make_async_copy(source, target, sems.at[i])
        for i, (source, target) in enumerate(pairs)
    ]
    for copy in copies:
        copy.start()
    return copies


def first_kernel(
    now_hbm,
    flags_hbm,
    weak_hbm,
    lame_hbm,
    shear_hbm,
    edge_hbm,
    cur_ref,
    right_ref,
    left_ref,
    fault_out_ref,
    material_ref,
    scratch,
    now_ref,
    flags_ref,
    weak_ref,
    lame_ref,
    shear_ref,
    edge_ref,
    sems,
):
    copies = start_copies(
        [
            (now_hbm, now_ref),
            (flags_hbm, flags_ref),
            (weak_hbm, weak_ref),
            (lame_hbm, lame_ref),
            (shear_hbm, shear_ref),
            (edge_hbm, edge_ref),
        ],
        sems,
    )
    y_elems, z_elems = lame_ref.shape
    lanes = y_elems * z_elems
    gather = gather_table(lanes, z_elems)
    fault = fault_table(lanes, z_elems)
    copies[0].wait()
    cur = to_elements(lambda c, y: now_ref[c, y], scratch, gather, y_elems)
    cur_ref[...] = cur
    steps = flags_ref.shape[0]
    copies[1].wait()
    copies[2].wait()
    weak = weak_ref[...]
    tangent = []
    for i in range(steps):
        flag = flags_ref[i]
        tangent.append(
            jnp.where(flag == 0, lock_stiffness, jnp.where(flag == 1, -weak, 0.0))
        )
    tangent = exact_dot(jnp.concatenate(tangent, axis=0), fault)
    fault_out_ref[...] = jnp.concatenate([fault_message(cur, z_elems), tangent], axis=0)
    copies[3].wait()
    copies[4].wait()
    lame_row, shear_row = material_rows(lame_ref, shear_ref)
    material_ref[...] = jnp.concatenate(
        [lame_row, shear_row, jnp.zeros((6, lanes), jnp.float32)], axis=0
    )
    copies[5].wait()
    right = edge_force(edge_ref, cur, lame_row, shear_row, z_elems)
    right_ref[...] = right
    left_ref[...] = cur[: 4 * BLOCK]


def setup_kernel(
    where_ref,
    next_hbm,
    density_hbm,
    flags_hbm,
    stress_hbm,
    mass_hbm,
    fol_ref,
    minv_ref,
    weight_ref,
    scratch,
    next_ref,
    density_ref,
    flags_ref,
    stress_ref,
    mass_ref,
    sems,
    *,
    y_elems,
    z_elems,
):
    copies = start_copies(
        [
            (next_hbm, next_ref),
            (density_hbm, density_ref),
            (flags_hbm, flags_ref),
            (stress_hbm, stress_ref),
            (mass_hbm, mass_ref),
        ],
        sems,
    )
    gather = gather_table(y_elems * z_elems, z_elems)
    fault = fault_table(y_elems * z_elems, z_elems)
    for copy in copies:
        copy.wait()
    fol_ref[...] = to_elements(lambda c, y: next_ref[c, y], scratch, gather, y_elems)
    density = to_elements(lambda c, y: density_ref[y], scratch, gather, y_elems)
    table = mass_ref[...]
    first = where_ref[0] == 0
    plane = lax.broadcasted_iota(jnp.int32, table.shape, 0) < PLANE
    table = jnp.where(jnp.logical_and(first, plane), 2.0 * table, table)
    minv_ref[...] = jnp.where(table > 0.0, table / jnp.where(table > 0.0, density, 1.0), 0.0)
    stress = stress_ref[...]
    weights = []
    for i in range(flags_ref.shape[0]):
        flag = flags_ref[i]
        weights.append(
            stress * jnp.where(flag == 1, 0.5, jnp.where(flag == 2, 1.0, 0.0))
        )
    weight_ref[...] = exact_dot(jnp.concatenate(weights, axis=0), fault)


def advance(
    step, place, last_place, cur, fol, minv, material, left_in, far_in, fault_in, tangents, main_ref, edge_ref,
    own_fault, y_elems, z_elems,
):
    lanes = cur.shape[1]
    far = jnp.where(place == last_place, 0.0, far_in)
    left = jnp.where(place == 0, 0.0, left_in)
    lane_wide = lax.broadcasted_iota(jnp.int32, (BLOCK, lanes), 1)
    below = jnp.where(
        lane_wide % z_elems != z_elems - 1, pltpu.roll(far[:BLOCK], lanes - 1, 1), 0.0
    )
    far = jnp.concatenate([far, below], axis=0)
    lame_row, shear_row = material[0:1], material[1:2]
    zeros = jnp.zeros((FAR_COLS - PLANE, lanes), jnp.float32)
    gap = jnp.zeros((OWN_COLS - 4 * PLANE, lanes), jnp.float32)
    result = split_dot(
        main_ref[0], main_ref[1], jnp.concatenate([cur, gap, far, zeros], axis=0)
    )
    force = lame_row * result[: 4 * PLANE] + shear_row * result[4 * PLANE :]
    touch = split_dot(
        edge_ref[0, :, OWN_COLS:],
        edge_ref[1, :, OWN_COLS:],
        jnp.concatenate([cur[:PLANE], zeros], axis=0),
    )
    left_lame = left[BLOCK - 1 : BLOCK]
    left_shear = left[2 * BLOCK - 1 : 2 * BLOCK]
    from_left = left_lame * touch[:PLANE] + left_shear * touch[PLANE:]
    from_left = jnp.concatenate([from_left[: 4 * BLOCK] + left, from_left[4 * BLOCK :]], axis=0)
    row, lane = block_iotas(lanes)
    across = lane // z_elems
    rows_first = row < 3
    rows_last = jnp.logical_and(row >= 4, row < 7)
    add_first = jnp.logical_and(rows_first, across > 0)
    take_last = jnp.logical_and(rows_last, across < y_elems - 1)
    pull_first = jnp.logical_and(rows_first, across == 0)
    pull_last = jnp.logical_and(rows_last, across == y_elems - 1)
    above = above_lanes(lanes, z_elems)
    below_t, own_t = tangents
    planes = []
    for x in range(4):
        blocks = []
        for zl in range(5):
            at = x * PLANE + zl * BLOCK
            block = force[at : at + BLOCK]
            if x == 0:
                block = block + from_left[zl * BLOCK : (zl + 1) * BLOCK]
            blocks.append(block)
        blocks[0] = blocks[0] + jnp.where(above, pltpu.roll(blocks[4], 1, 1), 0.0)
        stiff = jnp.where(
            jnp.logical_or(row == 1, row == 5),
            lock_stiffness,
            jnp.where(row < 4, below_t[4 * step + x : 4 * step + x + 1], own_t[4 * step + x : 4 * step + x + 1]),
        )
        pulled = stiff * (fault_in[8 * x : 8 * x + 8] - own_fault[8 * x : 8 * x + 8])
        for zl in range(4):
            low, high = blocks[zl][:8], blocks[zl][8:]
            low = low + jnp.where(
                add_first, pltpu.roll(pltpu.roll(high, 4, 0), z_elems, 1), 0.0
            )
            high = jnp.where(
                take_last, pltpu.roll(pltpu.roll(low, 4, 0), lanes - z_elems, 1), high
            )
            low = low - jnp.where(
                pull_first, pltpu.roll(pulled, (lanes - zl * z_elems) % lanes, 1), 0.0
            )
            high = high - jnp.where(
                pull_last,
                pltpu.roll(pulled, (lanes - (zl + 1) * z_elems) % lanes, 1),
                0.0,
            )
            blocks[zl] = jnp.concatenate([low, high], axis=0)
        blocks[4] = pltpu.roll(blocks[0], lanes - 1, 1)
        planes.extend(blocks)
    return (2.0 * cur - fol) - minv * jnp.concatenate(planes, axis=0)


def fault_input(up_ref, down_ref, count):
    if down_ref is None:
        return up_ref[:count]
    up, down = up_ref[:count], down_ref[:count]
    row = lax.broadcasted_iota(jnp.int32, up.shape, 0)
    return jnp.where(row % 8 < 4, up, down)


def step_kernel(*refs, step, last, last_place, pair, y_elems, z_elems):
    refs = list(refs)
    where_ref, cur_ref, fol_ref, minv_ref, material_ref, left_ref, far_ref = refs[:7]
    refs = refs[7:]
    up_ref = refs.pop(0)
    down_ref = None if pair else refs.pop(0)
    first_up_ref, own_ref, first_own_ref, main_ref, edge_ref = refs[:5]
    refs = refs[5:]
    place = where_ref[0]
    cur = cur_ref[...]
    tangents = (first_up_ref[32:], first_own_ref[32:])
    new = advance(
        step, place, last_place, cur, fol_ref[...], minv_ref[...], material_ref[...], left_ref[...], far_ref[...],
        fault_input(up_ref, down_ref, 32), tangents, main_ref, edge_ref, swap_rows(own_ref[:32]),
        y_elems, z_elems,
    )
    if last:
        _, back_ref, out_ref, scratch = refs
        from_elements(new, scratch, back_ref, out_ref, y_elems)
    else:
        new_ref, right_out, left_out, fault_out = refs
        new_ref[...] = new
        fault_out[...] = fault_message(new, z_elems)
        right = edge_force(edge_ref, new, material_ref[0:1], material_ref[1:2], z_elems)
        right_out[...] = right
        left_out[...] = new[: 4 * BLOCK]


def output_kernel(field_ref, back_ref, out_ref, scratch, *, y_elems):
    from_elements(field_ref[...], scratch, back_ref, out_ref, y_elems)


def patch_kernel(*refs, pair, steps, z_elems):
    where_ref, owner_ref, weight_ref = refs[:3]
    messages = refs[5:-5]
    home_out, out_a, out_b, out_c, out_d = refs[-5:]
    place = where_ref[0]
    lanes = weight_ref.shape[1]
    count = 2 if pair else 3
    grads = [jnp.zeros((8, lanes), jnp.float32) for _ in range(4)]
    for i in range(steps):
        group = messages[count * i : count * (i + 1)]
        slip = fault_input(group[1], None if pair else group[2], 32) - swap_rows(group[0][:32])
        for x in range(4):
            grads[x] = grads[x] + slip[8 * x : 8 * x + 8] * weight_ref[4 * i + x : 4 * i + x + 1]
    wide = 16
    number = lax.broadcasted_iota(jnp.int32, (wide, lanes), 0) + (place - REACH) * PATCH_DEV
    total = jnp.zeros((wide, lanes), jnp.float32)
    for x in range(4):
        total = total + jnp.where(number == owner_ref[0, x], grads[x][4:5], 0.0)
    total = exact_dot(total, fault_table_back(lanes, z_elems))
    rows = [total[2 * i : 2 * i + 2] for i in range(5)]
    home_out[...] = rows[2]
    out_a[...] = rows[3]
    out_b[...] = rows[1]
    out_c[...] = rows[4]
    out_d[...] = rows[0]


VMEM = pl.BlockSpec(memory_space=pltpu.VMEM)
HBM = pl.BlockSpec(memory_space=pltpu.HBM)
SMEM = pl.BlockSpec(memory_space=pltpu.SMEM)


def kernel_call(body, outs, args, in_smem, scratch=(), in_hbm=(), **static):
    shapes = [jax.ShapeDtypeStruct(s, jnp.float32) for s in outs]
    specs = [SMEM if i in in_smem else HBM if i in in_hbm else VMEM for i in range(len(args))]
    copied = [pltpu.VMEM(args[i].shape, args[i].dtype) for i in in_hbm]
    if in_hbm:
        copied.append(pltpu.SemaphoreType.DMA((len(in_hbm),)))
    return pl.pallas_call(
        functools.partial(body, **static) if static else body,
        out_shape=shapes,
        in_specs=specs,
        out_specs=[VMEM] * len(shapes),
        scratch_shapes=list(scratch) + copied,
        compiler_params=pltpu.CompilerParams(
            vmem_limit_bytes=(56 if in_hbm else 24) * 2**20
        ),
    )(*args)


def swapped(block, axis, distance, group):
    size = lax.axis_size(axis)
    route = {i: i for i in range(size)}
    for left in range(size - distance):
        if left // distance % 2 == group:
            route[left], route[left + distance] = left + distance, left
    return lax.ppermute(block, axis, list(route.items()))


def from_behind(block, axis, distance):
    size = lax.axis_size(axis)
    return lax.ppermute(block, axis, [((i - distance) % size, i) for i in range(size)])


def on_device(
    adjoint_now,
    adjoint_next,
    lame_first,
    shear_modulus,
    density,
    branch_flags,
    weak_slope,
    normal_stress,
    patch_owner,
):
    x_elems, y_elems, z_elems = lame_first.shape
    lanes = y_elems * z_elems
    assert x_elems == 1 and lanes == adjoint_now.shape[3]
    steps = branch_flags.shape[0]
    pair = lax.axis_size("depth") == 2
    place = lax.axis_index("dom").astype(jnp.int32).reshape(1)
    main_table, edge_table = (jnp.asarray(t) for t in stiffness_tables())
    back = jnp.asarray(back_table(y_elems, z_elems))
    mass = jnp.asarray(mass_table(y_elems, z_elems))
    now = jnp.transpose(adjoint_now, (0, 2, 1, 3))
    following = jnp.transpose(adjoint_next, (0, 2, 1, 3))
    rho = jnp.transpose(density, (1, 0, 2))
    flags = branch_flags[:, 0]
    native = pltpu.VMEM((y_elems, 4 * BLOCK, lanes), jnp.float32)
    field = (4 * PLANE, lanes)
    plane = (4 * BLOCK, lanes)

    def exchange(right, left, fault_rows):
        if pair:
            faults = [from_behind(fault_rows, "depth", 1)]
        else:
            faults = [from_behind(fault_rows, "depth", 1), from_behind(fault_rows, "depth", -1)]
        return from_behind(right, "dom", 1), from_behind(left, "dom", -1), faults

    cur, right, left, fault_rows, material = kernel_call(
        first_kernel,
        [field, plane, plane, (32 + 4 * steps, lanes), (8, lanes)],
        (
            now, flags, weak_slope[0], lame_first[0], shear_modulus[0], edge_table,
        ),
        (),
        [native],
        range(6),
    )
    first_fault = fault_rows
    left_in, far_in, fault_in = exchange(right, left, fault_rows)
    first_in = fault_in
    fol, minv, weight = kernel_call(
        setup_kernel,
        [field, field, (4 * steps, lanes)],
        (place, following, rho, flags, normal_stress[0], mass),
        (0,),
        [native],
        range(1, 6),
        y_elems=y_elems,
        z_elems=z_elems,
    )
    seen = []
    for step in range(steps):
        last = step == steps - 1
        seen += [fault_rows] + fault_in
        args = [place, cur, fol, minv, material, left_in, far_in] + fault_in
        args += [first_in[0], fault_rows, first_fault, main_table, edge_table]
        static = dict(
            step=step, last=last, last_place=lax.axis_size("dom") - 1, pair=pair, y_elems=y_elems,
            z_elems=z_elems,
        )
        if not last:
            new, right, left, new_fault = kernel_call(
                step_kernel, [field, plane, plane, (32, lanes)], args, (0,), **static
            )
            fol, cur, fault_rows = cur, new, new_fault
            left_in, far_in, fault_in = exchange(right, left, fault_rows)
        else:
            sums = kernel_call(
                patch_kernel,
                [(PATCH_DEV, lanes)] * 5,
                [place, patch_owner, weight, left_in, far_in] + seen,
                (0, 1),
                pair=pair,
                steps=steps,
                z_elems=z_elems,
            )
            patch_sums = sums[0]
            for out, distance in zip(sums[1:], (1, -1, 2, -2)):
                patch_sums = patch_sums + from_behind(out, "dom", distance)
            whole = (3, 4 * y_elems + 1, 4, lanes)
            later = kernel_call(
                output_kernel, [whole], [cur, back], (), [native], y_elems=y_elems
            )[0]
            earlier = kernel_call(
                step_kernel, [whole], args + [sums[0], back], (0,), [native], **static
            )[0]
    return (
        jnp.transpose(earlier, (0, 2, 1, 3)),
        jnp.transpose(later, (0, 2, 1, 3)),
        patch_sums[None],
    )


def solution(mesh):
    return jax.shard_map(
        on_device,
        mesh=mesh,
        in_specs=(
            P(None, "dom", "depth", None),
            P(None, "dom", "depth", None),
            P("dom", "depth", None),
            P("dom", "depth", None),
            P("dom", "depth", None),
            P(None, "depth", "dom", None),
            P("depth", "dom", None),
            P("depth", "dom", None),
            P("depth", "dom"),
        ),
        out_specs=(
            P(None, "dom", "depth", None),
            P(None, "dom", "depth", None),
            P("depth", "dom", None),
        ),
        check_vma=False,
    )
```

```python
import functools
import math

import jax
import jax.numpy as jnp
import ml_dtypes
import numpy as np
from jax import lax
from jax.experimental import pallas as pl
from jax.experimental.pallas import tpu as pltpu
from jax.sharding import PartitionSpec as P

PATCH_DEV = 2
REACH = 2

time_step = 0.01
lock_stiffness = 0.5

BLOCK = 16
PLANE = 5 * BLOCK


def basis_tables():
    points = [-1.0, -math.sqrt(3.0 / 7.0), 0.0, math.sqrt(3.0 / 7.0), 1.0]
    quad_weights = np.array([0.1, 49.0 / 90.0, 32.0 / 45.0, 49.0 / 90.0, 0.1])
    products = []
    for first in range(5):
        value = 1.0
        for other in range(5):
            if other != first:
                value = value * (points[first] - points[other])
        products.append(value)
    derivative = np.zeros((5, 5))
    for row in range(5):
        for column in range(5):
            if row == column:
                total = 0.0
                for other in range(5):
                    if other != row:
                        total = total + 1.0 / (points[row] - points[other])
                derivative[row, column] = total
            else:
                derivative[row, column] = (
                    products[row] / products[column] / (points[row] - points[column])
                )
    return (quad_weights, derivative)


def two_parts(table):
    high = table.astype(ml_dtypes.bfloat16)
    low = (table - high.astype(np.float64)).astype(ml_dtypes.bfloat16)
    return np.stack([high, low])


def element_stiffness():
    weights, derivative = basis_tables()
    eye = np.eye(5)
    slope = 2.0 * derivative
    grads = [
        np.kron(slope, np.kron(eye, eye)),
        np.kron(eye, np.kron(eye, slope)),
        np.kron(eye, np.kron(slope, eye)),
    ]
    quad = np.kron(weights, np.kron(weights, weights)) / 8.0
    first = np.zeros((125, 3, 125, 3))
    second = np.zeros((125, 3, 125, 3))
    lap = sum(g.T @ (quad[:, None] * g) for g in grads)
    for c in range(3):
        second[:, c, :, c] += lap
        for d in range(3):
            first[:, c, :, d] += grads[c].T @ (quad[:, None] * grads[d])
            second[:, c, :, d] += grads[d].T @ (quad[:, None] * grads[c])
    where = [
        node // 5 * BLOCK + node % 5 * 3 + c for node in range(125) for c in range(3)
    ]
    wide = []
    for small in (first, second):
        big = np.zeros((5 * PLANE, 5 * PLANE))
        big[np.ix_(where, where)] = small.reshape(375, 375)
        wide.append(big)
    return wide


OWN_COLS = 384
FAR_COLS = 128


@functools.cache
def stiffness_tables():
    wide = element_stiffness()
    own = 4 * PLANE
    parts = []
    for rows in (slice(0, own), slice(own, own + PLANE)):
        both = np.concatenate([w[rows] for w in wide])
        table = np.zeros((both.shape[0], OWN_COLS + FAR_COLS))
        table[:, :own] = both[:, :own]
        table[:, OWN_COLS : OWN_COLS + PLANE] = both[:, own:]
        parts.append(two_parts(table))
    return parts


@functools.cache
def back_table(y_elems, z_elems):
    lanes = y_elems * z_elems
    depth = 4 * z_elems
    back = np.zeros((4 * lanes, y_elems * depth), ml_dtypes.bfloat16)
    for yel in range(y_elems):
        for k in range(z_elems):
            for zl in range(4):
                back[zl * lanes + yel * z_elems + k, yel * depth + 4 * k + zl] = 1
    return back


@functools.cache
def mass_table(y_elems, z_elems):
    weights, _ = basis_tables()
    table = np.zeros((4, 5, BLOCK, y_elems, z_elems))
    for x in range(4):
        mx = 0.2 if x == 0 else weights[x]
        for zl in range(5):
            for yl in range(5):
                for yel in range(y_elems):
                    my = weights[yl]
                    if (yl == 0 and yel > 0) or (yl == 4 and yel < y_elems - 1):
                        my = 0.2
                    mz = np.full(z_elems, weights[zl])
                    if zl == 0:
                        mz[1:] = 0.2
                    if zl == 4:
                        mz[:] = 0.2
                    value = time_step * time_step * 8.0 / (mx * my * mz)
                    if zl == 4:
                        value[-1] = 0.0
                    table[x, zl, 3 * yl : 3 * yl + 3, yel] = value
    return table.reshape(4 * PLANE, y_elems * z_elems).astype(np.float32)


def pieces(value, count):
    out = []
    for _ in range(count):
        piece = value.astype(jnp.bfloat16)
        out.append(piece)
        value = value - piece.astype(jnp.float32)
    return out


def dot(a, b):
    return jnp.dot(a, b, preferred_element_type=jnp.float32)


def exact_dot(value, table, count=3):
    rows = value.shape[0]
    result = dot(jnp.concatenate(pieces(value, count), axis=0), table)
    total = result[:rows]
    for i in range(1, count):
        total = total + result[i * rows : (i + 1) * rows]
    return total


def split_dot(table_high, table_low, value):
    lanes = value.shape[1]
    high, low = pieces(value, 2)
    wide = dot(table_high, jnp.concatenate([high, low], axis=1))
    return wide[:, :lanes] + (wide[:, lanes:] + dot(table_low, high))


def ones_where(rule, shape):
    row = lax.broadcasted_iota(jnp.int32, shape, 0)
    column = lax.broadcasted_iota(jnp.int32, shape, 1)
    return jnp.where(rule(row, column), 1.0, 0.0).astype(jnp.bfloat16)


def gather_table(lanes, z_elems):
    return ones_where(lambda z, c: z == 4 * (c % z_elems) + c // lanes, (lanes, 5 * lanes))


def fault_table(lanes, z_elems):
    return ones_where(lambda z, c: z == 4 * (c % z_elems) + c // z_elems, (lanes, lanes))


def fault_table_back(lanes, z_elems):
    return ones_where(lambda c, z: z == 4 * (c % z_elems) + c // z_elems, (lanes, lanes))


def to_elements(native, scratch, table, y_elems):
    group = 4 * BLOCK
    scratch[...] = jnp.zeros_like(scratch)
    for c in range(3):
        for y in range(4 * y_elems + 1):
            rows = native(c, y)
            if y < 4 * y_elems:
                scratch[y // 4, pl.ds(y % 4 * 3 + c, 4, stride=BLOCK), :] = rows
            if y % 4 == 0 and y > 0:
                scratch[y // 4 - 1, pl.ds(12 + c, 4, stride=BLOCK), :] = rows
    high, middle, low = pieces(
        jnp.concatenate([scratch[i] for i in range(y_elems)], axis=0), 3
    )
    result = dot(
        jnp.concatenate([high, middle], axis=1), jnp.concatenate([table, table], axis=0)
    ) + dot(low, table)
    lanes = result.shape[1] // 5
    across = lax.broadcasted_iota(jnp.int32, (group, result.shape[1]), 1) % lanes // (
        lanes // y_elems
    )
    total = result[:group]
    for yel in range(1, y_elems):
        total = jnp.where(across == yel, result[yel * group : (yel + 1) * group], total)
    blocks = []
    for x in range(4):
        for zl in range(5):
            blocks.append(total[x * BLOCK : (x + 1) * BLOCK, zl * lanes : (zl + 1) * lanes])
    return jnp.concatenate(blocks, axis=0)


def from_elements(field, scratch, back_ref, out_ref, y_elems):
    rows = []
    for x in range(4):
        rows.append(
            jnp.concatenate(
                [field[x * PLANE + zl * BLOCK : x * PLANE + (zl + 1) * BLOCK] for zl in range(4)],
                axis=1,
            )
        )
    result = exact_dot(jnp.concatenate(rows, axis=0), back_ref[...])
    depth = result.shape[1] // y_elems
    for yel in range(y_elems):
        scratch[yel] = result[:, yel * depth : (yel + 1) * depth]
    for c in range(3):
        for y in range(4 * y_elems + 1):
            yel, yl = (y // 4, y % 4) if y < 4 * y_elems else (y_elems - 1, 4)
            out_ref[c, y] = scratch[yel, pl.ds(yl * 3 + c, 4, stride=BLOCK), :]


def block_iotas(lanes):
    return (
        lax.broadcasted_iota(jnp.int32, (8, lanes), 0),
        lax.broadcasted_iota(jnp.int32, (8, lanes), 1),
    )


def fault_message(field, z_elems):
    lanes = field.shape[1]
    row, lane = block_iotas(lanes)
    out = []
    for x in range(4):
        total = jnp.zeros((8, lanes), jnp.float32)
        for zl in range(4):
            at = x * PLANE + zl * BLOCK
            first = pltpu.roll(pltpu.roll(field[at : at + 8], 4, 0), zl * z_elems, 1)
            last = pltpu.roll(
                pltpu.roll(field[at + 8 : at + 16], 4, 0), (zl + 1) * z_elems % lanes, 1
            )
            here = lane // z_elems == zl
            total = jnp.where(here, jnp.where(row < 4, last, first), total)
        out.append(total)
    return jnp.concatenate(out, axis=0)


def swap_rows(message):
    parts = [pltpu.roll(message[i : i + 8], 4, 0) for i in range(0, message.shape[0], 8)]
    return jnp.concatenate(parts, axis=0)


def select_messages(parity, left, right):
    even = parity == 0
    return jnp.where(even, right, left), jnp.where(even, left, right)


def material_rows(lame_ref, shear_ref):
    y_elems, z_elems = lame_ref.shape
    both = jnp.concatenate([lame_ref[...], shear_ref[...]], axis=0)
    spread = ones_where(lambda k, c: c % z_elems == k, (z_elems, y_elems * z_elems))
    tiled = exact_dot(both, spread)
    row = lax.broadcasted_iota(jnp.int32, tiled.shape, 0)
    lane = lax.broadcasted_iota(jnp.int32, tiled.shape, 1)
    kept = jnp.where(row % y_elems == lane // z_elems, tiled, 0.0)
    return (
        jnp.sum(kept[:y_elems], axis=0, keepdims=True),
        jnp.sum(kept[y_elems:], axis=0, keepdims=True),
    )


def above_lanes(lanes, z_elems):
    return lax.broadcasted_iota(jnp.int32, (BLOCK, lanes), 1) % z_elems != 0


def edge_force(edge_ref, own, lame_row, shear_row, z_elems):
    lanes = own.shape[1]
    padded = jnp.concatenate(
        [own, jnp.zeros((OWN_COLS - own.shape[0], lanes), jnp.float32)], axis=0
    )
    result = split_dot(edge_ref[0, :, :OWN_COLS], edge_ref[1, :, :OWN_COLS], padded)
    force = lame_row * result[:PLANE] + shear_row * result[PLANE:]
    top = force[:BLOCK] + jnp.where(
        above_lanes(lanes, z_elems), pltpu.roll(force[4 * BLOCK :], 1, 1), 0.0
    )
    row = lax.broadcasted_iota(jnp.int32, top.shape, 0)
    top = jnp.where(row == BLOCK - 1, lame_row, top)
    second = jnp.where(row == BLOCK - 1, shear_row, force[BLOCK : 2 * BLOCK])
    return jnp.concatenate([top, second, force[2 * BLOCK : 4 * BLOCK]], axis=0)


def start_copies(pairs, sems):
    copies = [
        pltpu.make_async_copy(source, target, sems.at[i])
        for i, (source, target) in enumerate(pairs)
    ]
    for copy in copies:
        copy.start()
    return copies


def first_kernel(
    where_ref,
    now_hbm,
    flags_hbm,
    weak_hbm,
    lame_hbm,
    shear_hbm,
    edge_hbm,
    cur_ref,
    even_ref,
    odd_ref,
    fault_out_ref,
    material_ref,
    edge_ref,
    scratch,
    now_ref,
    flags_ref,
    weak_ref,
    lame_ref,
    shear_ref,
    sems,
):
    copies = start_copies(
        [
            (now_hbm, now_ref),
            (flags_hbm, flags_ref),
            (weak_hbm, weak_ref),
            (lame_hbm, lame_ref),
            (shear_hbm, shear_ref),
            (edge_hbm, edge_ref),
        ],
        sems,
    )
    y_elems, z_elems = lame_ref.shape
    lanes = y_elems * z_elems
    parity = where_ref[0] % 2
    gather = gather_table(lanes, z_elems)
    fault = fault_table(lanes, z_elems)
    copies[0].wait()
    cur = to_elements(lambda c, y: now_ref[c, y], scratch, gather, y_elems)
    cur_ref[...] = cur
    steps = flags_ref.shape[0]
    copies[1].wait()
    copies[2].wait()
    weak = weak_ref[...]
    tangent = []
    for i in range(steps):
        flag = flags_ref[i]
        tangent.append(
            jnp.where(flag == 0, lock_stiffness, jnp.where(flag == 1, -weak, 0.0))
        )
    tangent = exact_dot(jnp.concatenate(tangent, axis=0), fault)
    fault_out_ref[...] = jnp.concatenate([fault_message(cur, z_elems), tangent], axis=0)
    copies[3].wait()
    copies[4].wait()
    lame_row, shear_row = material_rows(lame_ref, shear_ref)
    material_ref[...] = jnp.concatenate(
        [lame_row, shear_row, jnp.zeros((6, lanes), jnp.float32)], axis=0
    )
    copies[5].wait()
    right = edge_force(edge_ref, cur, lame_row, shear_row, z_elems)
    even_ref[...], odd_ref[...] = select_messages(parity, cur[: 4 * BLOCK], right)


def setup_kernel(
    where_ref,
    next_hbm,
    density_hbm,
    flags_hbm,
    stress_hbm,
    mass_hbm,
    main_hbm,
    back_hbm,
    fol_ref,
    minv_ref,
    weight_ref,
    main_ref,
    back_ref,
    scratch,
    next_ref,
    density_ref,
    flags_ref,
    stress_ref,
    mass_ref,
    sems,
    *,
    y_elems,
    z_elems,
):
    copies = start_copies(
        [
            (next_hbm, next_ref),
            (density_hbm, density_ref),
            (flags_hbm, flags_ref),
            (stress_hbm, stress_ref),
            (mass_hbm, mass_ref),
            (main_hbm, main_ref),
            (back_hbm, back_ref),
        ],
        sems,
    )
    gather = gather_table(y_elems * z_elems, z_elems)
    fault = fault_table(y_elems * z_elems, z_elems)
    for copy in copies[:5]:
        copy.wait()
    fol_ref[...] = to_elements(lambda c, y: next_ref[c, y], scratch, gather, y_elems)
    density = to_elements(lambda c, y: density_ref[y], scratch, gather, y_elems)
    table = mass_ref[...]
    first = where_ref[0] == 0
    plane = lax.broadcasted_iota(jnp.int32, table.shape, 0) < PLANE
    table = jnp.where(jnp.logical_and(first, plane), 2.0 * table, table)
    minv_ref[...] = jnp.where(table > 0.0, table / jnp.where(table > 0.0, density, 1.0), 0.0)
    stress = stress_ref[...]
    weights = []
    for i in range(flags_ref.shape[0]):
        flag = flags_ref[i]
        weights.append(
            stress * jnp.where(flag == 1, 0.5, jnp.where(flag == 2, 1.0, 0.0))
        )
    weight_ref[...] = exact_dot(jnp.concatenate(weights, axis=0), fault)
    copies[5].wait()
    copies[6].wait()


def advance(
    step, place, last_place, cur, fol, minv, material, even_in, odd_in, fault_in, tangents, main_ref, edge_ref,
    own_fault, y_elems, z_elems,
):
    lanes = cur.shape[1]
    even = place % 2 == 0
    far = jnp.where(place == last_place, 0.0, jnp.where(even, even_in, odd_in))
    left = jnp.where(place == 0, 0.0, jnp.where(even, odd_in, even_in))
    lane_wide = lax.broadcasted_iota(jnp.int32, (BLOCK, lanes), 1)
    below = jnp.where(
        lane_wide % z_elems != z_elems - 1, pltpu.roll(far[:BLOCK], lanes - 1, 1), 0.0
    )
    far = jnp.concatenate([far, below], axis=0)
    lame_row, shear_row = material[0:1], material[1:2]
    zeros = jnp.zeros((FAR_COLS - PLANE, lanes), jnp.float32)
    gap = jnp.zeros((OWN_COLS - 4 * PLANE, lanes), jnp.float32)
    result = split_dot(
        main_ref[0], main_ref[1], jnp.concatenate([cur, gap, far, zeros], axis=0)
    )
    force = lame_row * result[: 4 * PLANE] + shear_row * result[4 * PLANE :]
    touch = split_dot(
        edge_ref[0, :, OWN_COLS:],
        edge_ref[1, :, OWN_COLS:],
        jnp.concatenate([cur[:PLANE], zeros], axis=0),
    )
    left_lame = left[BLOCK - 1 : BLOCK]
    left_shear = left[2 * BLOCK - 1 : 2 * BLOCK]
    from_left = left_lame * touch[:PLANE] + left_shear * touch[PLANE:]
    from_left = jnp.concatenate([from_left[: 4 * BLOCK] + left, from_left[4 * BLOCK :]], axis=0)
    row, lane = block_iotas(lanes)
    across = lane // z_elems
    rows_first = row < 3
    rows_last = jnp.logical_and(row >= 4, row < 7)
    add_first = jnp.logical_and(rows_first, across > 0)
    take_last = jnp.logical_and(rows_last, across < y_elems - 1)
    pull_first = jnp.logical_and(rows_first, across == 0)
    pull_last = jnp.logical_and(rows_last, across == y_elems - 1)
    above = above_lanes(lanes, z_elems)
    below_t, own_t = tangents
    planes = []
    for x in range(4):
        blocks = []
        for zl in range(5):
            at = x * PLANE + zl * BLOCK
            block = force[at : at + BLOCK]
            if x == 0:
                block = block + from_left[zl * BLOCK : (zl + 1) * BLOCK]
            blocks.append(block)
        blocks[0] = blocks[0] + jnp.where(above, pltpu.roll(blocks[4], 1, 1), 0.0)
        stiff = jnp.where(
            jnp.logical_or(row == 1, row == 5),
            lock_stiffness,
            jnp.where(row < 4, below_t[4 * step + x : 4 * step + x + 1], own_t[4 * step + x : 4 * step + x + 1]),
        )
        pulled = stiff * (fault_in[8 * x : 8 * x + 8] - own_fault[8 * x : 8 * x + 8])
        for zl in range(4):
            low, high = blocks[zl][:8], blocks[zl][8:]
            low = low + jnp.where(
                add_first, pltpu.roll(pltpu.roll(high, 4, 0), z_elems, 1), 0.0
            )
            high = jnp.where(
                take_last, pltpu.roll(pltpu.roll(low, 4, 0), lanes - z_elems, 1), high
            )
            low = low - jnp.where(
                pull_first, pltpu.roll(pulled, (lanes - zl * z_elems) % lanes, 1), 0.0
            )
            high = high - jnp.where(
                pull_last,
                pltpu.roll(pulled, (lanes - (zl + 1) * z_elems) % lanes, 1),
                0.0,
            )
            blocks[zl] = jnp.concatenate([low, high], axis=0)
        blocks[4] = pltpu.roll(blocks[0], lanes - 1, 1)
        planes.extend(blocks)
    return (2.0 * cur - fol) - minv * jnp.concatenate(planes, axis=0)


def fault_input(up_ref, down_ref, count):
    if down_ref is None:
        return up_ref[:count]
    up, down = up_ref[:count], down_ref[:count]
    row = lax.broadcasted_iota(jnp.int32, up.shape, 0)
    return jnp.where(row % 8 < 4, up, down)


def step_kernel(*refs, step, last, last_place, pair, y_elems, z_elems):
    refs = list(refs)
    where_ref, cur_ref, fol_ref, minv_ref, material_ref, even_ref, odd_ref = refs[:7]
    refs = refs[7:]
    up_ref = refs.pop(0)
    down_ref = None if pair else refs.pop(0)
    first_up_ref, own_ref, first_own_ref, main_ref, edge_ref = refs[:5]
    refs = refs[5:]
    place = where_ref[0]
    cur = cur_ref[...]
    tangents = (first_up_ref[32:], first_own_ref[32:])
    new = advance(
        step, place, last_place, cur, fol_ref[...], minv_ref[...], material_ref[...], even_ref[...], odd_ref[...],
        fault_input(up_ref, down_ref, 32), tangents, main_ref, edge_ref, swap_rows(own_ref[:32]),
        y_elems, z_elems,
    )
    if last:
        _, back_ref, out_ref, scratch = refs
        from_elements(new, scratch, back_ref, out_ref, y_elems)
    else:
        new_ref, even_out, odd_out, fault_out = refs
        new_ref[...] = new
        fault_out[...] = fault_message(new, z_elems)
        right = edge_force(edge_ref, new, material_ref[0:1], material_ref[1:2], z_elems)
        even_out[...], odd_out[...] = select_messages(place % 2, new[: 4 * BLOCK], right)


def output_kernel(field_ref, back_ref, out_ref, mark_ref, scratch, *, y_elems):
    mark_ref[...] = jnp.zeros_like(mark_ref)
    from_elements(field_ref[...], scratch, back_ref, out_ref, y_elems)


def patch_kernel(*refs, pair, steps, z_elems):
    where_ref, owner_ref, weight_ref = refs[:3]
    messages = refs[6:-5]
    home_out, out_a, out_b, out_c, out_d = refs[-5:]
    place = where_ref[0]
    lanes = weight_ref.shape[1]
    count = 2 if pair else 3
    grads = [jnp.zeros((8, lanes), jnp.float32) for _ in range(4)]
    for i in range(steps):
        group = messages[count * i : count * (i + 1)]
        slip = fault_input(group[1], None if pair else group[2], 32) - swap_rows(group[0][:32])
        for x in range(4):
            grads[x] = grads[x] + slip[8 * x : 8 * x + 8] * weight_ref[4 * i + x : 4 * i + x + 1]
    wide = 16
    number = lax.broadcasted_iota(jnp.int32, (wide, lanes), 0) + (place - REACH) * PATCH_DEV
    total = jnp.zeros((wide, lanes), jnp.float32)
    for x in range(4):
        total = total + jnp.where(number == owner_ref[0, x], grads[x][4:5], 0.0)
    total = exact_dot(total, fault_table_back(lanes, z_elems))
    rows = [total[2 * i : 2 * i + 2] for i in range(5)]
    home_out[...] = rows[2]
    even = place % 2 == 0
    out_a[...] = jnp.where(even, rows[3], rows[1])
    out_b[...] = jnp.where(even, rows[1], rows[3])
    low = place % 4 < 2
    out_c[...] = jnp.where(low, rows[4], rows[0])
    out_d[...] = jnp.where(low, rows[0], rows[4])


VMEM = pl.BlockSpec(memory_space=pltpu.VMEM)
HBM = pl.BlockSpec(memory_space=pltpu.HBM)
SMEM = pl.BlockSpec(memory_space=pltpu.SMEM)
ANY = pl.BlockSpec(memory_space=pl.ANY)


def kernel_call(body, outs, args, in_smem, scratch=(), in_hbm=(), kept=(), unread=(), **static):
    shapes = []
    for out in outs:
        shape, dtype = out if isinstance(out[0], tuple) else (out, jnp.float32)
        shapes.append((pltpu.VMEM if in_hbm else jax.ShapeDtypeStruct)(shape, dtype))
    specs = [VMEM] * len(args)
    for places, spec in ((in_smem, SMEM), (in_hbm, HBM), (unread, ANY)):
        for i in places:
            specs[i] = spec
    copied = [pltpu.VMEM(args[i].shape, args[i].dtype) for i in in_hbm if i not in kept]
    if in_hbm:
        copied.append(pltpu.SemaphoreType.DMA((len(in_hbm),)))
    return pl.pallas_call(
        functools.partial(body, **static) if static else body,
        out_shape=shapes,
        in_specs=specs,
        out_specs=[VMEM] * len(shapes),
        scratch_shapes=list(scratch) + copied,
        compiler_params=pltpu.CompilerParams(
            vmem_limit_bytes=(56 if in_hbm else 24) * 2**20
        ),
    )(*args)


def swapped(block, distance, group):
    size, across = lax.axis_size("dom"), lax.axis_size("depth")
    partner = {}
    for left in range(size - distance):
        if left // distance % 2 == group:
            partner[left], partner[left + distance] = left + distance, left
    route = []
    for i in range(size):
        for j in range(across):
            side = j if i in partner else min(j ^ 1, across - 1)
            route.append((i * across + j, partner.get(i, i) * across + side))
    return lax.ppermute(block, ("dom", "depth"), route)


def from_behind(block, axis, distance):
    size = lax.axis_size(axis)
    return lax.ppermute(block, axis, [((i - distance) % size, i) for i in range(size)])


def on_device(
    adjoint_now,
    adjoint_next,
    lame_first,
    shear_modulus,
    density,
    branch_flags,
    weak_slope,
    normal_stress,
    patch_owner,
):
    x_elems, y_elems, z_elems = lame_first.shape
    lanes = y_elems * z_elems
    assert x_elems == 1 and lanes == adjoint_now.shape[3]
    steps = branch_flags.shape[0]
    pair = lax.axis_size("depth") == 2
    place = lax.axis_index("dom").astype(jnp.int32).reshape(1)
    main_table, edge_table = (jnp.asarray(t) for t in stiffness_tables())
    back = jnp.asarray(back_table(y_elems, z_elems))
    mass = jnp.asarray(mass_table(y_elems, z_elems))
    now = jnp.transpose(adjoint_now, (0, 2, 1, 3))
    following = jnp.transpose(adjoint_next, (0, 2, 1, 3))
    rho = jnp.transpose(density, (1, 0, 2))
    flags = branch_flags[:, 0]
    native = pltpu.VMEM((y_elems, 4 * BLOCK, lanes), jnp.float32)
    field = (4 * PLANE, lanes)
    plane = (4 * BLOCK, lanes)

    def exchange(even, odd, fault_rows):
        if pair:
            faults = [from_behind(fault_rows, "depth", 1)]
        else:
            faults = [from_behind(fault_rows, "depth", 1), from_behind(fault_rows, "depth", -1)]
        return swapped(even, 1, 0), swapped(odd, 1, 1), faults

    cur, even, odd, fault_rows, material, edge_table = kernel_call(
        first_kernel,
        [
            field, plane, plane, (32 + 4 * steps, lanes), (8, lanes),
            (edge_table.shape, edge_table.dtype),
        ],
        (
            place, now, flags, weak_slope[0], lame_first[0], shear_modulus[0], edge_table,
        ),
        (0,),
        [native],
        range(1, 7),
        (6,),
    )
    first_fault = fault_rows
    even_in, odd_in, fault_in = exchange(even, odd, fault_rows)
    first_in = fault_in
    fol, minv, weight, main_table, back = kernel_call(
        setup_kernel,
        [
            field, field, (4 * steps, lanes), (main_table.shape, main_table.dtype),
            (back.shape, back.dtype),
        ],
        (place, following, rho, flags, normal_stress[0], mass, main_table, back),
        (0,),
        [native],
        range(1, 8),
        (6, 7),
        y_elems=y_elems,
        z_elems=z_elems,
    )
    seen = []
    for step in range(steps):
        last = step == steps - 1
        seen += [fault_rows] + fault_in
        args = [place, cur, fol, minv, material, even_in, odd_in] + fault_in
        args += [first_in[0], fault_rows, first_fault, main_table, edge_table]
        static = dict(
            step=step, last=last, last_place=lax.axis_size("dom") - 1, pair=pair, y_elems=y_elems,
            z_elems=z_elems,
        )
        if not last:
            new, even, odd, new_fault = kernel_call(
                step_kernel, [field, plane, plane, (32, lanes)], args, (0,), **static
            )
            fol, cur, fault_rows = cur, new, new_fault
            even_in, odd_in, fault_in = exchange(even, odd, fault_rows)
        else:
            whole = (3, 4 * y_elems + 1, 4, lanes)
            later, mark = kernel_call(
                output_kernel, [whole, (8, lanes)], [cur, back], (), [native], y_elems=y_elems
            )
            sums = kernel_call(
                patch_kernel,
                [(PATCH_DEV, lanes)] * 5,
                [place, patch_owner, weight, even_in, odd_in, mark] + seen,
                (0, 1),
                unread=(3, 4, 5),
                pair=pair,
                steps=steps,
                z_elems=z_elems,
            )
            patch_sums = sums[0]
            for out, distance, group in zip(sums[1:], (1, 1, 2, 2), (0, 1, 0, 1)):
                patch_sums = patch_sums + swapped(out, distance, group)
            earlier = kernel_call(
                step_kernel,
                [whole],
                args + [sums[0], back],
                (0,),
                [native],
                unread=(len(args),),
                **static,
            )[0]
    return (
        jnp.transpose(earlier, (0, 2, 1, 3)),
        jnp.transpose(later, (0, 2, 1, 3)),
        patch_sums[None],
    )


def solution(mesh):
    return jax.shard_map(
        on_device,
        mesh=mesh,
        in_specs=(
            P(None, "dom", "depth", None),
            P(None, "dom", "depth", None),
            P("dom", "depth", None),
            P("dom", "depth", None),
            P("dom", "depth", None),
            P(None, "depth", "dom", None),
            P("depth", "dom", None),
            P("depth", "dom", None),
            P("depth", "dom"),
        ),
        out_specs=(
            P(None, "dom", "depth", None),
            P(None, "dom", "depth", None),
            P("depth", "dom", None),
        ),
        check_vma=False,
    )
```

```python
import functools
import math

import jax
import jax.numpy as jnp
import ml_dtypes
import numpy as np
from jax import lax
from jax.experimental import pallas as pl
from jax.experimental.pallas import tpu as pltpu
from jax.sharding import PartitionSpec as P

PATCH_DEV = 2
REACH = 2

time_step = 0.01
lock_stiffness = 0.5

BLOCK = 16
PLANE = 5 * BLOCK


def basis_tables():
    points = [-1.0, -math.sqrt(3.0 / 7.0), 0.0, math.sqrt(3.0 / 7.0), 1.0]
    quad_weights = np.array([0.1, 49.0 / 90.0, 32.0 / 45.0, 49.0 / 90.0, 0.1])
    products = []
    for first in range(5):
        value = 1.0
        for other in range(5):
            if other != first:
                value = value * (points[first] - points[other])
        products.append(value)
    derivative = np.zeros((5, 5))
    for row in range(5):
        for column in range(5):
            if row == column:
                total = 0.0
                for other in range(5):
                    if other != row:
                        total = total + 1.0 / (points[row] - points[other])
                derivative[row, column] = total
            else:
                derivative[row, column] = (
                    products[row] / products[column] / (points[row] - points[column])
                )
    return (quad_weights, derivative)


def two_parts(table):
    high = table.astype(ml_dtypes.bfloat16)
    low = (table - high.astype(np.float64)).astype(ml_dtypes.bfloat16)
    return np.stack([high, low])


def element_stiffness():
    weights, derivative = basis_tables()
    eye = np.eye(5)
    slope = 2.0 * derivative
    grads = [
        np.kron(slope, np.kron(eye, eye)),
        np.kron(eye, np.kron(eye, slope)),
        np.kron(eye, np.kron(slope, eye)),
    ]
    quad = np.kron(weights, np.kron(weights, weights)) / 8.0
    first = np.zeros((125, 3, 125, 3))
    second = np.zeros((125, 3, 125, 3))
    lap = sum(g.T @ (quad[:, None] * g) for g in grads)
    for c in range(3):
        second[:, c, :, c] += lap
        for d in range(3):
            first[:, c, :, d] += grads[c].T @ (quad[:, None] * grads[d])
            second[:, c, :, d] += grads[d].T @ (quad[:, None] * grads[c])
    where = [
        node // 5 * BLOCK + node % 5 * 3 + c for node in range(125) for c in range(3)
    ]
    wide = []
    for small in (first, second):
        big = np.zeros((5 * PLANE, 5 * PLANE))
        big[np.ix_(where, where)] = small.reshape(375, 375)
        wide.append(big)
    return wide


OWN_COLS = 384


def padded_table(table, columns):
    return np.pad(table, ((0, 0), (0, columns - table.shape[1])))


@functools.cache
def stiffness_tables():
    wide = element_stiffness()
    own = 4 * PLANE
    inner = np.concatenate([w[:own] for w in wide])
    outer = np.concatenate([w[own:] for w in wide])

    def three(table):
        high, low = two_parts(table)
        return padded_table(np.concatenate([high, low, high], axis=1), 256)

    return (
        two_parts(padded_table(inner[:, :own], OWN_COLS)),
        three(inner[:, own:]),
        two_parts(padded_table(outer[:, :own], OWN_COLS)),
        three(outer[:, own:]),
    )


@functools.cache
def back_table(y_elems, z_elems):
    lanes = y_elems * z_elems
    depth = 4 * z_elems
    back = np.zeros((4 * lanes, y_elems * depth), ml_dtypes.bfloat16)
    for yel in range(y_elems):
        for k in range(z_elems):
            for zl in range(4):
                back[zl * lanes + yel * z_elems + k, yel * depth + 4 * k + zl] = 1
    return back


@functools.cache
def mass_table(y_elems, z_elems):
    weights, _ = basis_tables()
    table = np.zeros((4, 5, BLOCK, y_elems, z_elems))
    for x in range(4):
        mx = 0.2 if x == 0 else weights[x]
        for zl in range(5):
            for yl in range(5):
                for yel in range(y_elems):
                    my = weights[yl]
                    if (yl == 0 and yel > 0) or (yl == 4 and yel < y_elems - 1):
                        my = 0.2
                    mz = np.full(z_elems, weights[zl])
                    if zl == 0:
                        mz[1:] = 0.2
                    if zl == 4:
                        mz[:] = 0.2
                    value = time_step * time_step * 8.0 / (mx * my * mz)
                    if zl == 4:
                        value[-1] = 0.0
                    table[x, zl, 3 * yl : 3 * yl + 3, yel] = value
    return table.reshape(4 * PLANE, y_elems * z_elems).astype(np.float32)


def pieces(value, count):
    out = []
    for _ in range(count):
        piece = value.astype(jnp.bfloat16)
        out.append(piece)
        value = value - piece.astype(jnp.float32)
    return out


def dot(a, b):
    return jnp.dot(a, b, preferred_element_type=jnp.float32)


def exact_dot(value, table, count=3):
    rows = value.shape[0]
    result = dot(jnp.concatenate(pieces(value, count), axis=0), table)
    total = result[:rows]
    for i in range(1, count):
        total = total + result[i * rows : (i + 1) * rows]
    return total


def split_dot(table_high, table_low, value):
    lanes = value.shape[1]
    high, low = pieces(value, 2)
    wide = dot(table_high, jnp.concatenate([high, low], axis=1))
    return wide[:, :lanes] + (wide[:, lanes:] + dot(table_low, high))


def ones_where(rule, shape):
    row = lax.broadcasted_iota(jnp.int32, shape, 0)
    column = lax.broadcasted_iota(jnp.int32, shape, 1)
    return jnp.where(rule(row, column), 1.0, 0.0).astype(jnp.bfloat16)


def gather_table(lanes, z_elems):
    return ones_where(lambda z, c: z == 4 * (c % z_elems) + c // lanes, (lanes, 5 * lanes))


def fault_table(lanes, z_elems):
    return ones_where(lambda z, c: z == 4 * (c % z_elems) + c // z_elems, (lanes, lanes))


def fault_table_back(lanes, z_elems):
    return ones_where(lambda c, z: z == 4 * (c % z_elems) + c // z_elems, (lanes, lanes))


def stacked_dot(table, value):
    high, low = pieces(value, 2)
    gap = jnp.zeros((table.shape[1] - 3 * value.shape[0], value.shape[1]), jnp.bfloat16)
    return dot(table, jnp.concatenate([high, high, low, gap], axis=0))


def to_elements(native, scratch, table, y_elems):
    group = 4 * BLOCK
    scratch[...] = jnp.zeros_like(scratch)
    for c in range(3):
        for y in range(4 * y_elems + 1):
            rows = native(c, y)
            if y < 4 * y_elems:
                scratch[y // 4, pl.ds(y % 4 * 3 + c, 4, stride=BLOCK), :] = rows
            if y % 4 == 0 and y > 0:
                scratch[y // 4 - 1, pl.ds(12 + c, 4, stride=BLOCK), :] = rows
    high, middle, low = pieces(
        jnp.concatenate([scratch[i] for i in range(y_elems)], axis=0), 3
    )
    result = dot(
        jnp.concatenate([high, middle], axis=1), jnp.concatenate([table, table], axis=0)
    ) + dot(low, table)
    lanes = result.shape[1] // 5
    across = lax.broadcasted_iota(jnp.int32, (group, result.shape[1]), 1) % lanes // (
        lanes // y_elems
    )
    total = result[:group]
    for yel in range(1, y_elems):
        total = jnp.where(across == yel, result[yel * group : (yel + 1) * group], total)
    blocks = []
    for x in range(4):
        for zl in range(5):
            blocks.append(total[x * BLOCK : (x + 1) * BLOCK, zl * lanes : (zl + 1) * lanes])
    return jnp.concatenate(blocks, axis=0)


def from_elements(field, scratch, back_ref, out_ref, y_elems):
    rows = []
    for x in range(4):
        rows.append(
            jnp.concatenate(
                [field[x * PLANE + zl * BLOCK : x * PLANE + (zl + 1) * BLOCK] for zl in range(4)],
                axis=1,
            )
        )
    result = exact_dot(jnp.concatenate(rows, axis=0), back_ref[...])
    depth = result.shape[1] // y_elems
    for yel in range(y_elems):
        scratch[yel] = result[:, yel * depth : (yel + 1) * depth]
    for c in range(3):
        for y in range(4 * y_elems + 1):
            yel, yl = (y // 4, y % 4) if y < 4 * y_elems else (y_elems - 1, 4)
            out_ref[c, y] = scratch[yel, pl.ds(yl * 3 + c, 4, stride=BLOCK), :]


def block_iotas(lanes):
    return (
        lax.broadcasted_iota(jnp.int32, (8, lanes), 0),
        lax.broadcasted_iota(jnp.int32, (8, lanes), 1),
    )


def fault_message(field, z_elems):
    lanes = field.shape[1]
    row, lane = block_iotas(lanes)
    out = []
    for x in range(4):
        total = jnp.zeros((8, lanes), jnp.float32)
        for zl in range(4):
            at = x * PLANE + zl * BLOCK
            first = pltpu.roll(pltpu.roll(field[at : at + 8], 4, 0), zl * z_elems, 1)
            last = pltpu.roll(
                pltpu.roll(field[at + 8 : at + 16], 4, 0), (zl + 1) * z_elems % lanes, 1
            )
            here = lane // z_elems == zl
            total = jnp.where(here, jnp.where(row < 4, last, first), total)
        out.append(total)
    return jnp.concatenate(out, axis=0)


def swap_rows(message):
    parts = [pltpu.roll(message[i : i + 8], 4, 0) for i in range(0, message.shape[0], 8)]
    return jnp.concatenate(parts, axis=0)


def select_messages(parity, left, right):
    even = parity == 0
    return jnp.where(even, right, left), jnp.where(even, left, right)


def material_rows(lame_ref, shear_ref):
    y_elems, z_elems = lame_ref.shape
    both = jnp.concatenate([lame_ref[...], shear_ref[...]], axis=0)
    spread = ones_where(lambda k, c: c % z_elems == k, (z_elems, y_elems * z_elems))
    tiled = exact_dot(both, spread)
    row = lax.broadcasted_iota(jnp.int32, tiled.shape, 0)
    lane = lax.broadcasted_iota(jnp.int32, tiled.shape, 1)
    kept = jnp.where(row % y_elems == lane // z_elems, tiled, 0.0)
    return (
        jnp.sum(kept[:y_elems], axis=0, keepdims=True),
        jnp.sum(kept[y_elems:], axis=0, keepdims=True),
    )


def above_lanes(lanes, z_elems):
    return lax.broadcasted_iota(jnp.int32, (BLOCK, lanes), 1) % z_elems != 0


def edge_force(edge_ref, own, lame_row, shear_row, z_elems):
    lanes = own.shape[1]
    padded = jnp.concatenate(
        [own, jnp.zeros((OWN_COLS - own.shape[0], lanes), jnp.float32)], axis=0
    )
    result = split_dot(edge_ref[0], edge_ref[1], padded)
    force = lame_row * result[:PLANE] + shear_row * result[PLANE:]
    top = force[:BLOCK] + jnp.where(
        above_lanes(lanes, z_elems), pltpu.roll(force[4 * BLOCK :], 1, 1), 0.0
    )
    row = lax.broadcasted_iota(jnp.int32, top.shape, 0)
    top = jnp.where(row == BLOCK - 1, lame_row, top)
    second = jnp.where(row == BLOCK - 1, shear_row, force[BLOCK : 2 * BLOCK])
    return jnp.concatenate([top, second, force[2 * BLOCK : 4 * BLOCK]], axis=0)


def own_force(own_ref, cur, lame_row, shear_row):
    rows, lanes = cur.shape
    padded = jnp.concatenate([cur, jnp.zeros((OWN_COLS - rows, lanes), jnp.float32)], axis=0)
    result = split_dot(own_ref[0], own_ref[1], padded)
    return lame_row * result[:rows] + shear_row * result[rows:]


def start_copies(pairs, sems):
    copies = [
        pltpu.make_async_copy(source, target, sems.at[i])
        for i, (source, target) in enumerate(pairs)
    ]
    for copy in copies:
        copy.start()
    return copies


def first_kernel(
    where_ref,
    now_hbm,
    flags_hbm,
    weak_hbm,
    lame_hbm,
    shear_hbm,
    edge_hbm,
    cur_ref,
    even_ref,
    odd_ref,
    fault_out_ref,
    material_ref,
    edge_ref,
    scratch,
    now_ref,
    flags_ref,
    weak_ref,
    lame_ref,
    shear_ref,
    sems,
):
    copies = start_copies(
        [
            (now_hbm, now_ref),
            (flags_hbm, flags_ref),
            (weak_hbm, weak_ref),
            (lame_hbm, lame_ref),
            (shear_hbm, shear_ref),
            (edge_hbm, edge_ref),
        ],
        sems,
    )
    y_elems, z_elems = lame_ref.shape
    lanes = y_elems * z_elems
    parity = where_ref[0] % 2
    gather = gather_table(lanes, z_elems)
    fault = fault_table(lanes, z_elems)
    copies[1].wait()
    copies[2].wait()
    weak = weak_ref[...]
    tangent = []
    for i in range(flags_ref.shape[0]):
        flag = flags_ref[i]
        tangent.append(
            jnp.where(flag == 0, lock_stiffness, jnp.where(flag == 1, -weak, 0.0))
        )
    fault_out_ref[32:] = exact_dot(jnp.concatenate(tangent, axis=0), fault)
    copies[3].wait()
    copies[4].wait()
    lame_row, shear_row = material_rows(lame_ref, shear_ref)
    material_ref[...] = jnp.concatenate(
        [lame_row, shear_row, jnp.zeros((6, lanes), jnp.float32)], axis=0
    )
    copies[0].wait()
    cur = to_elements(lambda c, y: now_ref[c, y], scratch, gather, y_elems)
    copies[5].wait()
    right = edge_force(edge_ref, cur, lame_row, shear_row, z_elems)
    even_ref[...], odd_ref[...] = select_messages(parity, cur[: 4 * BLOCK], right)
    cur_ref[...] = cur
    fault_out_ref[:32] = fault_message(cur, z_elems)


def prepare_kernel(cur_ref, material_ref, own_ref, touch_ref, base_ref, edge_part_ref):
    cur = cur_ref[...]
    base_ref[...] = own_force(own_ref, cur, material_ref[0:1], material_ref[1:2])
    edge_part_ref[...] = stacked_dot(touch_ref[...], cur[:PLANE])


def setup_kernel(
    where_ref,
    next_hbm,
    density_hbm,
    flags_hbm,
    stress_hbm,
    mass_hbm,
    own_hbm,
    far_hbm,
    touch_hbm,
    back_hbm,
    fol_ref,
    minv_ref,
    weight_ref,
    own_ref,
    far_ref,
    touch_ref,
    back_ref,
    scratch,
    next_ref,
    density_ref,
    flags_ref,
    stress_ref,
    mass_ref,
    sems,
    *,
    y_elems,
    z_elems,
):
    copies = start_copies(
        [
            (next_hbm, next_ref),
            (density_hbm, density_ref),
            (flags_hbm, flags_ref),
            (stress_hbm, stress_ref),
            (mass_hbm, mass_ref),
            (own_hbm, own_ref),
            (far_hbm, far_ref),
            (touch_hbm, touch_ref),
            (back_hbm, back_ref),
        ],
        sems,
    )
    gather = gather_table(y_elems * z_elems, z_elems)
    fault = fault_table(y_elems * z_elems, z_elems)
    for copy in copies[:5]:
        copy.wait()
    fol_ref[...] = to_elements(lambda c, y: next_ref[c, y], scratch, gather, y_elems)
    density = to_elements(lambda c, y: density_ref[y], scratch, gather, y_elems)
    table = mass_ref[...]
    first = where_ref[0] == 0
    plane = lax.broadcasted_iota(jnp.int32, table.shape, 0) < PLANE
    table = jnp.where(jnp.logical_and(first, plane), 2.0 * table, table)
    minv_ref[...] = jnp.where(table > 0.0, table / jnp.where(table > 0.0, density, 1.0), 0.0)
    stress = stress_ref[...]
    weights = []
    for i in range(flags_ref.shape[0]):
        flag = flags_ref[i]
        weights.append(
            stress * jnp.where(flag == 1, 0.5, jnp.where(flag == 2, 1.0, 0.0))
        )
    weight_ref[...] = exact_dot(jnp.concatenate(weights, axis=0), fault)
    for copy in copies[5:]:
        copy.wait()


def advance(
    step, place, last_place, cur, fol, minv, base, touch, material, even_in, odd_in, fault_in, tangents, far_table, own_fault,
    y_elems, z_elems,
):
    lanes = cur.shape[1]
    even = place % 2 == 0
    far = jnp.where(place == last_place, 0.0, jnp.where(even, even_in, odd_in))
    left = jnp.where(place == 0, 0.0, jnp.where(even, odd_in, even_in))
    lane_wide = lax.broadcasted_iota(jnp.int32, (BLOCK, lanes), 1)
    below = jnp.where(
        lane_wide % z_elems != z_elems - 1, pltpu.roll(far[:BLOCK], lanes - 1, 1), 0.0
    )
    far = jnp.concatenate([far, below], axis=0)
    lame_row, shear_row = material[0:1], material[1:2]
    result = stacked_dot(far_table, far)
    force = base + (lame_row * result[: 4 * PLANE] + shear_row * result[4 * PLANE :])
    left_lame = left[BLOCK - 1 : BLOCK]
    left_shear = left[2 * BLOCK - 1 : 2 * BLOCK]
    from_left = left_lame * touch[:PLANE] + left_shear * touch[PLANE:]
    from_left = jnp.concatenate([from_left[: 4 * BLOCK] + left, from_left[4 * BLOCK :]], axis=0)
    row, lane = block_iotas(lanes)
    across = lane // z_elems
    rows_first = row < 3
    rows_last = jnp.logical_and(row >= 4, row < 7)
    add_first = jnp.logical_and(rows_first, across > 0)
    take_last = jnp.logical_and(rows_last, across < y_elems - 1)
    pull_first = jnp.logical_and(rows_first, across == 0)
    pull_last = jnp.logical_and(rows_last, across == y_elems - 1)
    above = above_lanes(lanes, z_elems)
    below_t, own_t = tangents
    planes = []
    for x in range(4):
        blocks = []
        for zl in range(5):
            at = x * PLANE + zl * BLOCK
            block = force[at : at + BLOCK]
            if x == 0:
                block = block + from_left[zl * BLOCK : (zl + 1) * BLOCK]
            blocks.append(block)
        blocks[0] = blocks[0] + jnp.where(above, pltpu.roll(blocks[4], 1, 1), 0.0)
        stiff = jnp.where(
            jnp.logical_or(row == 1, row == 5),
            lock_stiffness,
            jnp.where(row < 4, below_t[4 * step + x : 4 * step + x + 1], own_t[4 * step + x : 4 * step + x + 1]),
        )
        pulled = stiff * (fault_in[8 * x : 8 * x + 8] - own_fault[8 * x : 8 * x + 8])
        for zl in range(4):
            low, high = blocks[zl][:8], blocks[zl][8:]
            low = low + jnp.where(
                add_first, pltpu.roll(pltpu.roll(high, 4, 0), z_elems, 1), 0.0
            )
            high = jnp.where(
                take_last, pltpu.roll(pltpu.roll(low, 4, 0), lanes - z_elems, 1), high
            )
            low = low - jnp.where(
                pull_first, pltpu.roll(pulled, (lanes - zl * z_elems) % lanes, 1), 0.0
            )
            high = high - jnp.where(
                pull_last,
                pltpu.roll(pulled, (lanes - (zl + 1) * z_elems) % lanes, 1),
                0.0,
            )
            blocks[zl] = jnp.concatenate([low, high], axis=0)
        blocks[4] = pltpu.roll(blocks[0], lanes - 1, 1)
        planes.extend(blocks)
    return (2.0 * cur - fol) - minv * jnp.concatenate(planes, axis=0)


def fault_input(up_ref, down_ref, count):
    if down_ref is None:
        return up_ref[:count]
    up, down = up_ref[:count], down_ref[:count]
    row = lax.broadcasted_iota(jnp.int32, up.shape, 0)
    return jnp.where(row % 8 < 4, up, down)


def step_kernel(*refs, step, last, last_place, pair, y_elems, z_elems):
    refs = list(refs)
    where_ref, cur_ref, fol_ref, minv_ref, base_ref, touch_ref, material_ref = refs[:7]
    even_ref, odd_ref = refs[7:9]
    refs = refs[9:]
    up_ref = refs.pop(0)
    down_ref = None if pair else refs.pop(0)
    first_up_ref, own_ref, first_own_ref, far_ref, edge_ref = refs[:5]
    refs = refs[5:]
    place = where_ref[0]
    cur = cur_ref[...]
    tangents = (first_up_ref[32:], first_own_ref[32:])
    new = advance(
        step, place, last_place, cur, fol_ref[...], minv_ref[...], base_ref[...], touch_ref[...],
        material_ref[...], even_ref[...], odd_ref[...], fault_input(up_ref, down_ref, 32), tangents,
        far_ref[...], swap_rows(own_ref[:32]), y_elems, z_elems,
    )
    if last:
        _, back_ref, out_ref, scratch = refs
        from_elements(new, scratch, back_ref, out_ref, y_elems)
    else:
        new_ref, even_out, odd_out, fault_out = refs
        new_ref[...] = new
        fault_out[...] = fault_message(new, z_elems)
        right = edge_force(edge_ref, new, material_ref[0:1], material_ref[1:2], z_elems)
        even_out[...], odd_out[...] = select_messages(place % 2, new[: 4 * BLOCK], right)


def output_kernel(*refs, pair, steps, y_elems, z_elems):
    field_ref, back_ref, weight_ref = refs[:3]
    out_ref, grad_ref, table_ref, scratch = refs[-4:]
    messages = refs[3:-4]
    count = 2 if pair else 3
    grads = [jnp.zeros((8, weight_ref.shape[1]), jnp.float32) for _ in range(4)]
    for i in range(steps):
        group = messages[count * i : count * (i + 1)]
        slip = -swap_rows(group[0][:32])
        if i < steps - 1:
            slip = slip + fault_input(group[1], None if pair else group[2], 32)
        for x in range(4):
            grads[x] = grads[x] + slip[8 * x : 8 * x + 8] * weight_ref[4 * i + x : 4 * i + x + 1]
    grad_ref[...] = jnp.concatenate(grads, axis=0)
    table_ref[...] = fault_table_back(weight_ref.shape[1], z_elems)
    from_elements(field_ref[...], scratch, back_ref, out_ref, y_elems)


def patch_kernel(*refs, pair, steps):
    where_ref, owner_ref, weight_ref, grad_ref, table_ref, _, _, _, up_ref = refs[:9]
    down_ref = None if pair else refs[9]
    home_out, out_a, out_b, out_c, out_d = refs[-5:]
    place = where_ref[0]
    lanes = weight_ref.shape[1]
    slip = fault_input(up_ref, down_ref, 32)
    wide = 16
    number = lax.broadcasted_iota(jnp.int32, (wide, lanes), 0) + (place - REACH) * PATCH_DEV
    total = jnp.zeros((wide, lanes), jnp.float32)
    for x in range(4):
        at, k = 8 * x + 4, 4 * (steps - 1) + x
        grad = grad_ref[at : at + 1] + slip[at : at + 1] * weight_ref[k : k + 1]
        total = total + jnp.where(number == owner_ref[0, x], grad, 0.0)
    total = exact_dot(total, table_ref[...])
    rows = [total[2 * i : 2 * i + 2] for i in range(5)]
    home_out[...] = rows[2]
    even = place % 2 == 0
    out_a[...] = jnp.where(even, rows[3], rows[1])
    out_b[...] = jnp.where(even, rows[1], rows[3])
    low = place % 4 < 2
    out_c[...] = jnp.where(low, rows[4], rows[0])
    out_d[...] = jnp.where(low, rows[0], rows[4])


VMEM = pl.BlockSpec(memory_space=pltpu.VMEM)
HBM = pl.BlockSpec(memory_space=pltpu.HBM)
SMEM = pl.BlockSpec(memory_space=pltpu.SMEM)
ANY = pl.BlockSpec(memory_space=pl.ANY)


def kernel_call(body, outs, args, in_smem, scratch=(), in_hbm=(), kept=(), unread=(), **static):
    shapes = []
    for out in outs:
        shape, dtype = out if isinstance(out[0], tuple) else (out, jnp.float32)
        shapes.append((pltpu.VMEM if in_hbm else jax.ShapeDtypeStruct)(shape, dtype))
    specs = [VMEM] * len(args)
    for places, spec in ((in_smem, SMEM), (in_hbm, HBM), (unread, ANY)):
        for i in places:
            specs[i] = spec
    copied = [pltpu.VMEM(args[i].shape, args[i].dtype) for i in in_hbm if i not in kept]
    if in_hbm:
        copied.append(pltpu.SemaphoreType.DMA((len(in_hbm),)))
    return pl.pallas_call(
        functools.partial(body, **static) if static else body,
        out_shape=shapes,
        in_specs=specs,
        out_specs=[VMEM] * len(shapes),
        scratch_shapes=list(scratch) + copied,
        compiler_params=pltpu.CompilerParams(
            vmem_limit_bytes=(56 if in_hbm else 24) * 2**20
        ),
    )(*args)


def swapped(block, distance, group):
    size, across = lax.axis_size("dom"), lax.axis_size("depth")
    partner = {}
    for left in range(size - distance):
        if left // distance % 2 == group:
            partner[left], partner[left + distance] = left + distance, left
    route = []
    for i in range(size):
        for j in range(across):
            side = j if i in partner else min(j ^ 1, across - 1)
            route.append((i * across + j, partner.get(i, i) * across + side))
    return lax.ppermute(block, ("dom", "depth"), route)


def from_behind(block, axis, distance):
    size = lax.axis_size(axis)
    return lax.ppermute(block, axis, [((i - distance) % size, i) for i in range(size)])


def on_device(
    adjoint_now,
    adjoint_next,
    lame_first,
    shear_modulus,
    density,
    branch_flags,
    weak_slope,
    normal_stress,
    patch_owner,
):
    x_elems, y_elems, z_elems = lame_first.shape
    lanes = y_elems * z_elems
    assert x_elems == 1 and lanes == adjoint_now.shape[3]
    steps = branch_flags.shape[0]
    pair = lax.axis_size("depth") == 2
    place = lax.axis_index("dom").astype(jnp.int32).reshape(1)
    own_table, far_table, edge_table, touch_table = (jnp.asarray(t) for t in stiffness_tables())
    back = jnp.asarray(back_table(y_elems, z_elems))
    mass = jnp.asarray(mass_table(y_elems, z_elems))
    now = jnp.transpose(adjoint_now, (0, 2, 1, 3))
    following = jnp.transpose(adjoint_next, (0, 2, 1, 3))
    rho = jnp.transpose(density, (1, 0, 2))
    flags = branch_flags[:, 0]
    native = pltpu.VMEM((y_elems, 4 * BLOCK, lanes), jnp.float32)
    field = (4 * PLANE, lanes)
    plane = (4 * BLOCK, lanes)

    def exchange(even, odd, fault_rows):
        if pair:
            faults = [from_behind(fault_rows, "depth", 1)]
        else:
            faults = [from_behind(fault_rows, "depth", 1), from_behind(fault_rows, "depth", -1)]
        odd_in = swapped(odd, 1, 1)
        return swapped(even, 1, 0), odd_in, faults

    cur, even, odd, fault_rows, material, edge_table = kernel_call(
        first_kernel,
        [
            field, plane, plane, (32 + 4 * steps, lanes), (8, lanes),
            (edge_table.shape, edge_table.dtype),
        ],
        (
            place, now, flags, weak_slope[0], lame_first[0], shear_modulus[0], edge_table,
        ),
        (0,),
        [native],
        range(1, 7),
        (6,),
    )
    first_fault = fault_rows
    even_in, odd_in, fault_in = exchange(even, odd, fault_rows)
    first_in = fault_in
    tables = (own_table, far_table, touch_table, back)
    fol, minv, weight, own_table, far_table, touch_table, back = kernel_call(
        setup_kernel,
        [field, field, (4 * steps, lanes)] + [(t.shape, t.dtype) for t in tables],
        (place, following, rho, flags, normal_stress[0], mass) + tables,
        (0,),
        [native],
        range(1, 10),
        range(6, 10),
        y_elems=y_elems,
        z_elems=z_elems,
    )
    seen = []
    for step in range(steps):
        last = step == steps - 1
        seen += [fault_rows] + fault_in
        base, touch = kernel_call(
            prepare_kernel,
            [field, (2 * PLANE, lanes)],
            [cur, material, own_table, touch_table],
            (),
        )
        args = [place, cur, fol, minv, base, touch, material, even_in, odd_in] + fault_in
        args += [first_in[0], fault_rows, first_fault, far_table, edge_table]
        static = dict(
            step=step, last=last, last_place=lax.axis_size("dom") - 1, pair=pair, y_elems=y_elems,
            z_elems=z_elems,
        )
        if not last:
            new, even, odd, new_fault = kernel_call(
                step_kernel, [field, plane, plane, (32, lanes)], args, (0,), **static
            )
            fol, cur, fault_rows = cur, new, new_fault
            even_in, odd_in, fault_in = exchange(even, odd, fault_rows)
        else:
            whole = (3, 4 * y_elems + 1, 4, lanes)
            known = seen[: len(seen) - len(fault_in)]
            later, grad, table = kernel_call(
                output_kernel,
                [whole, (32, lanes), ((lanes, lanes), jnp.bfloat16)],
                [cur, back, weight] + known,
                (),
                [native],
                pair=pair,
                steps=steps,
                y_elems=y_elems,
                z_elems=z_elems,
            )
            sums = kernel_call(
                patch_kernel,
                [(PATCH_DEV, lanes)] * 5,
                [place, patch_owner, weight, grad, table, even_in, odd_in, touch] + fault_in,
                (0, 1),
                unread=(5, 6, 7),
                pair=pair,
                steps=steps,
            )
            patch_sums = sums[0]
            for i, distance, group in ((2, 1, 1), (4, 2, 1), (3, 2, 0), (1, 1, 0)):
                patch_sums = patch_sums + swapped(sums[i], distance, group)
            earlier = kernel_call(
                step_kernel,
                [whole],
                args + [sums[0], back],
                (0,),
                [native],
                unread=(len(args),),
                **static,
            )[0]
    return (
        jnp.transpose(earlier, (0, 2, 1, 3)),
        jnp.transpose(later, (0, 2, 1, 3)),
        patch_sums[None],
    )


def solution(mesh):
    return jax.shard_map(
        on_device,
        mesh=mesh,
        in_specs=(
            P(None, "dom", "depth", None),
            P(None, "dom", "depth", None),
            P("dom", "depth", None),
            P("dom", "depth", None),
            P("dom", "depth", None),
            P(None, "depth", "dom", None),
            P("depth", "dom", None),
            P("depth", "dom", None),
            P("depth", "dom"),
        ),
        out_specs=(
            P(None, "dom", "depth", None),
            P(None, "dom", "depth", None),
            P("depth", "dom", None),
        ),
        check_vma=False,
    )
```

```python
import functools
import math

import jax
import jax.numpy as jnp
import ml_dtypes
import numpy as np
from jax import lax
from jax.experimental import pallas as pl
from jax.experimental.pallas import tpu as pltpu
from jax.sharding import PartitionSpec as P

PATCH_DEV = 2
REACH = 2
PATCH_ROWS = 16

time_step = 0.01
lock_stiffness = 0.5

BLOCK = 16
PLANE = 5 * BLOCK


def basis_tables():
    points = [-1.0, -math.sqrt(3.0 / 7.0), 0.0, math.sqrt(3.0 / 7.0), 1.0]
    quad_weights = np.array([0.1, 49.0 / 90.0, 32.0 / 45.0, 49.0 / 90.0, 0.1])
    products = []
    for first in range(5):
        value = 1.0
        for other in range(5):
            if other != first:
                value = value * (points[first] - points[other])
        products.append(value)
    derivative = np.zeros((5, 5))
    for row in range(5):
        for column in range(5):
            if row == column:
                total = 0.0
                for other in range(5):
                    if other != row:
                        total = total + 1.0 / (points[row] - points[other])
                derivative[row, column] = total
            else:
                derivative[row, column] = (
                    products[row] / products[column] / (points[row] - points[column])
                )
    return (quad_weights, derivative)


def two_parts(table):
    high = table.astype(ml_dtypes.bfloat16)
    low = (table - high.astype(np.float64)).astype(ml_dtypes.bfloat16)
    return np.stack([high, low])


def element_stiffness():
    weights, derivative = basis_tables()
    eye = np.eye(5)
    slope = 2.0 * derivative
    grads = [
        np.kron(slope, np.kron(eye, eye)),
        np.kron(eye, np.kron(eye, slope)),
        np.kron(eye, np.kron(slope, eye)),
    ]
    quad = np.kron(weights, np.kron(weights, weights)) / 8.0
    first = np.zeros((125, 3, 125, 3))
    second = np.zeros((125, 3, 125, 3))
    lap = sum(g.T @ (quad[:, None] * g) for g in grads)
    for c in range(3):
        second[:, c, :, c] += lap
        for d in range(3):
            first[:, c, :, d] += grads[c].T @ (quad[:, None] * grads[d])
            second[:, c, :, d] += grads[d].T @ (quad[:, None] * grads[c])
    where = [
        node // 5 * BLOCK + node % 5 * 3 + c for node in range(125) for c in range(3)
    ]
    wide = []
    for small in (first, second):
        big = np.zeros((5 * PLANE, 5 * PLANE))
        big[np.ix_(where, where)] = small.reshape(375, 375)
        wide.append(big)
    return wide


OWN_COLS = 384


def padded_table(table, columns):
    return np.pad(table, ((0, 0), (0, columns - table.shape[1])))


@functools.cache
def stiffness_tables():
    wide = element_stiffness()
    own = 4 * PLANE
    inner = np.concatenate([w[:own] for w in wide])
    outer = np.concatenate([w[own:] for w in wide])

    def three(table):
        high, low = two_parts(table)
        return padded_table(np.concatenate([high, low, high], axis=1), 256)

    return (
        two_parts(padded_table(inner[:, :own], OWN_COLS)),
        three(inner[:, own:]),
        two_parts(padded_table(outer[:, :own], OWN_COLS)),
        three(outer[:, own:]),
    )


@functools.cache
def back_table(y_elems, z_elems):
    lanes = y_elems * z_elems
    depth = 4 * z_elems
    back = np.zeros((4 * lanes, y_elems * depth), ml_dtypes.bfloat16)
    for yel in range(y_elems):
        for k in range(z_elems):
            for zl in range(4):
                back[zl * lanes + yel * z_elems + k, yel * depth + 4 * k + zl] = 1
    return back


@functools.cache
def mass_table(y_elems, z_elems):
    weights, _ = basis_tables()
    table = np.zeros((4, 5, BLOCK, y_elems, z_elems))
    for x in range(4):
        mx = 0.2 if x == 0 else weights[x]
        for zl in range(5):
            for yl in range(5):
                for yel in range(y_elems):
                    my = weights[yl]
                    if (yl == 0 and yel > 0) or (yl == 4 and yel < y_elems - 1):
                        my = 0.2
                    mz = np.full(z_elems, weights[zl])
                    if zl == 0:
                        mz[1:] = 0.2
                    if zl == 4:
                        mz[:] = 0.2
                    value = time_step * time_step * 8.0 / (mx * my * mz)
                    if zl == 4:
                        value[-1] = 0.0
                    table[x, zl, 3 * yl : 3 * yl + 3, yel] = value
    return table.reshape(4 * PLANE, y_elems * z_elems).astype(np.float32)


def pieces(value, count):
    out = []
    for _ in range(count):
        piece = value.astype(jnp.bfloat16)
        out.append(piece)
        value = value - piece.astype(jnp.float32)
    return out


def dot(a, b):
    return jnp.dot(a, b, preferred_element_type=jnp.float32)


def exact_dot(value, table, count=3):
    rows = value.shape[0]
    result = dot(jnp.concatenate(pieces(value, count), axis=0), table)
    total = result[:rows]
    for i in range(1, count):
        total = total + result[i * rows : (i + 1) * rows]
    return total


def split_dot(table_high, table_low, value):
    lanes = value.shape[1]
    high, low = pieces(value, 2)
    wide = dot(table_high, jnp.concatenate([high, low], axis=1))
    return wide[:, :lanes] + (wide[:, lanes:] + dot(table_low, high))


def ones_where(rule, shape):
    row = lax.broadcasted_iota(jnp.int32, shape, 0)
    column = lax.broadcasted_iota(jnp.int32, shape, 1)
    return jnp.where(rule(row, column), 1.0, 0.0).astype(jnp.bfloat16)


def gather_table(lanes, z_elems):
    return ones_where(lambda z, c: z == 4 * (c % z_elems) + c // lanes, (lanes, 5 * lanes))


def fault_table(lanes, z_elems):
    return ones_where(lambda z, c: z == 4 * (c % z_elems) + c // z_elems, (lanes, lanes))


def fault_table_back(lanes, z_elems):
    return ones_where(lambda c, z: z == 4 * (c % z_elems) + c // z_elems, (lanes, lanes))


def stacked_dot(table, value):
    high, low = pieces(value, 2)
    gap = jnp.zeros((table.shape[1] - 3 * value.shape[0], value.shape[1]), jnp.bfloat16)
    return dot(table, jnp.concatenate([high, high, low, gap], axis=0))


def to_elements(native, scratch, table, y_elems):
    group = 4 * BLOCK
    scratch[...] = jnp.zeros_like(scratch)
    for c in range(3):
        for y in range(4 * y_elems + 1):
            rows = native(c, y)
            if y < 4 * y_elems:
                scratch[y // 4, pl.ds(y % 4 * 3 + c, 4, stride=BLOCK), :] = rows
            if y % 4 == 0 and y > 0:
                scratch[y // 4 - 1, pl.ds(12 + c, 4, stride=BLOCK), :] = rows
    high, middle, low = pieces(
        jnp.concatenate([scratch[i] for i in range(y_elems)], axis=0), 3
    )
    result = dot(
        jnp.concatenate([high, middle], axis=1), jnp.concatenate([table, table], axis=0)
    ) + dot(low, table)
    lanes = result.shape[1] // 5
    across = lax.broadcasted_iota(jnp.int32, (group, result.shape[1]), 1) % lanes // (
        lanes // y_elems
    )
    total = result[:group]
    for yel in range(1, y_elems):
        total = jnp.where(across == yel, result[yel * group : (yel + 1) * group], total)
    blocks = []
    for x in range(4):
        for zl in range(5):
            blocks.append(total[x * BLOCK : (x + 1) * BLOCK, zl * lanes : (zl + 1) * lanes])
    return jnp.concatenate(blocks, axis=0)


def from_elements(field, scratch, back_ref, out_ref, y_elems):
    rows = []
    for x in range(4):
        rows.append(
            jnp.concatenate(
                [field[x * PLANE + zl * BLOCK : x * PLANE + (zl + 1) * BLOCK] for zl in range(4)],
                axis=1,
            )
        )
    result = exact_dot(jnp.concatenate(rows, axis=0), back_ref[...])
    depth = result.shape[1] // y_elems
    for yel in range(y_elems):
        scratch[yel] = result[:, yel * depth : (yel + 1) * depth]
    for c in range(3):
        for y in range(4 * y_elems + 1):
            yel, yl = (y // 4, y % 4) if y < 4 * y_elems else (y_elems - 1, 4)
            out_ref[c, y] = scratch[yel, pl.ds(yl * 3 + c, 4, stride=BLOCK), :]


def block_iotas(lanes):
    return (
        lax.broadcasted_iota(jnp.int32, (8, lanes), 0),
        lax.broadcasted_iota(jnp.int32, (8, lanes), 1),
    )


def fault_message(field, z_elems):
    lanes = field.shape[1]
    row, lane = block_iotas(lanes)
    out = []
    for x in range(4):
        total = jnp.zeros((8, lanes), jnp.float32)
        for zl in range(4):
            at = x * PLANE + zl * BLOCK
            first = pltpu.roll(pltpu.roll(field[at : at + 8], 4, 0), zl * z_elems, 1)
            last = pltpu.roll(
                pltpu.roll(field[at + 8 : at + 16], 4, 0), (zl + 1) * z_elems % lanes, 1
            )
            here = lane // z_elems == zl
            total = jnp.where(here, jnp.where(row < 4, last, first), total)
        out.append(total)
    return jnp.concatenate(out, axis=0)


def swap_rows(message):
    parts = [pltpu.roll(message[i : i + 8], 4, 0) for i in range(0, message.shape[0], 8)]
    return jnp.concatenate(parts, axis=0)


def select_messages(parity, left, right):
    even = parity == 0
    return jnp.where(even, right, left), jnp.where(even, left, right)


def material_rows(lame_ref, shear_ref):
    y_elems, z_elems = lame_ref.shape
    both = jnp.concatenate([lame_ref[...], shear_ref[...]], axis=0)
    spread = ones_where(lambda k, c: c % z_elems == k, (z_elems, y_elems * z_elems))
    tiled = exact_dot(both, spread)
    row = lax.broadcasted_iota(jnp.int32, tiled.shape, 0)
    lane = lax.broadcasted_iota(jnp.int32, tiled.shape, 1)
    kept = jnp.where(row % y_elems == lane // z_elems, tiled, 0.0)
    return (
        jnp.sum(kept[:y_elems], axis=0, keepdims=True),
        jnp.sum(kept[y_elems:], axis=0, keepdims=True),
    )


def above_lanes(lanes, z_elems):
    return lax.broadcasted_iota(jnp.int32, (BLOCK, lanes), 1) % z_elems != 0


def edge_force(edge_ref, own, lame_row, shear_row, z_elems):
    lanes = own.shape[1]
    padded = jnp.concatenate(
        [own, jnp.zeros((OWN_COLS - own.shape[0], lanes), jnp.float32)], axis=0
    )
    result = split_dot(edge_ref[0], edge_ref[1], padded)
    force = lame_row * result[:PLANE] + shear_row * result[PLANE:]
    top = force[:BLOCK] + jnp.where(
        above_lanes(lanes, z_elems), pltpu.roll(force[4 * BLOCK :], 1, 1), 0.0
    )
    row = lax.broadcasted_iota(jnp.int32, top.shape, 0)
    top = jnp.where(row == BLOCK - 1, lame_row, top)
    second = jnp.where(row == BLOCK - 1, shear_row, force[BLOCK : 2 * BLOCK])
    return jnp.concatenate([top, second, force[2 * BLOCK : 4 * BLOCK]], axis=0)


def own_force(own_ref, cur, lame_row, shear_row):
    rows, lanes = cur.shape
    padded = jnp.concatenate([cur, jnp.zeros((OWN_COLS - rows, lanes), jnp.float32)], axis=0)
    result = split_dot(own_ref[0], own_ref[1], padded)
    return lame_row * result[:rows] + shear_row * result[rows:]


def start_copies(pairs, sems):
    copies = [
        pltpu.make_async_copy(source, target, sems.at[i])
        for i, (source, target) in enumerate(pairs)
    ]
    for copy in copies:
        copy.start()
    return copies


def first_kernel(
    now_hbm,
    flags_hbm,
    weak_hbm,
    lame_hbm,
    shear_hbm,
    edge_hbm,
    cur_ref,
    even_ref,
    odd_ref,
    fault_out_ref,
    material_ref,
    edge_ref,
    scratch,
    now_ref,
    flags_ref,
    weak_ref,
    lame_ref,
    shear_ref,
    sems,
):
    copies = start_copies(
        [
            (now_hbm, now_ref),
            (flags_hbm, flags_ref),
            (weak_hbm, weak_ref),
            (lame_hbm, lame_ref),
            (shear_hbm, shear_ref),
            (edge_hbm, edge_ref),
        ],
        sems,
    )
    y_elems, z_elems = lame_ref.shape
    lanes = y_elems * z_elems
    parity = lax.axis_index("dom") % 2
    gather = gather_table(lanes, z_elems)
    fault = fault_table(lanes, z_elems)
    copies[1].wait()
    copies[2].wait()
    weak = weak_ref[...]
    tangent = []
    for i in range(flags_ref.shape[0]):
        flag = flags_ref[i]
        tangent.append(
            jnp.where(flag == 0, lock_stiffness, jnp.where(flag == 1, -weak, 0.0))
        )
    fault_out_ref[32:] = exact_dot(jnp.concatenate(tangent, axis=0), fault)
    copies[3].wait()
    copies[4].wait()
    lame_row, shear_row = material_rows(lame_ref, shear_ref)
    material_ref[...] = jnp.concatenate(
        [lame_row, shear_row, jnp.zeros((6, lanes), jnp.float32)], axis=0
    )
    copies[0].wait()
    cur = to_elements(lambda c, y: now_ref[c, y], scratch, gather, y_elems)
    copies[5].wait()
    right = edge_force(edge_ref, cur, lame_row, shear_row, z_elems)
    even_ref[...], odd_ref[...] = select_messages(parity, cur[: 4 * BLOCK], right)
    cur_ref[...] = cur
    fault_out_ref[:32] = fault_message(cur, z_elems)


def prepare_kernel(cur_ref, material_ref, own_ref, touch_ref, base_ref, edge_part_ref):
    cur = cur_ref[...]
    base_ref[...] = own_force(own_ref, cur, material_ref[0:1], material_ref[1:2])
    edge_part_ref[...] = stacked_dot(touch_ref[...], cur[:PLANE])


def setup_kernel(
    next_hbm,
    density_hbm,
    flags_hbm,
    stress_hbm,
    mass_hbm,
    own_hbm,
    far_hbm,
    touch_hbm,
    back_hbm,
    fol_ref,
    minv_ref,
    weight_ref,
    own_ref,
    far_ref,
    touch_ref,
    back_ref,
    scratch,
    next_ref,
    density_ref,
    flags_ref,
    stress_ref,
    mass_ref,
    sems,
    *,
    y_elems,
    z_elems,
):
    copies = start_copies(
        [
            (next_hbm, next_ref),
            (density_hbm, density_ref),
            (flags_hbm, flags_ref),
            (stress_hbm, stress_ref),
            (mass_hbm, mass_ref),
            (own_hbm, own_ref),
            (far_hbm, far_ref),
            (touch_hbm, touch_ref),
            (back_hbm, back_ref),
        ],
        sems,
    )
    gather = gather_table(y_elems * z_elems, z_elems)
    fault = fault_table(y_elems * z_elems, z_elems)
    for copy in copies[:5]:
        copy.wait()
    fol_ref[...] = to_elements(lambda c, y: next_ref[c, y], scratch, gather, y_elems)
    density = to_elements(lambda c, y: density_ref[y], scratch, gather, y_elems)
    table = mass_ref[...]
    first = lax.axis_index("dom") == 0
    plane = lax.broadcasted_iota(jnp.int32, table.shape, 0) < PLANE
    table = jnp.where(jnp.logical_and(first, plane), 2.0 * table, table)
    minv_ref[...] = jnp.where(table > 0.0, table / jnp.where(table > 0.0, density, 1.0), 0.0)
    stress = stress_ref[...]
    weights = []
    for i in range(flags_ref.shape[0]):
        flag = flags_ref[i]
        weights.append(
            stress * jnp.where(flag == 1, 0.5, jnp.where(flag == 2, 1.0, 0.0))
        )
    weight_ref[...] = exact_dot(jnp.concatenate(weights, axis=0), fault)
    for copy in copies[5:]:
        copy.wait()


def advance(
    step, place, last_place, cur, fol, minv, base, touch, material, even_in, odd_in, fault_in, tangents, far_table, own_fault,
    y_elems, z_elems,
):
    lanes = cur.shape[1]
    even = place % 2 == 0
    far = jnp.where(place == last_place, 0.0, jnp.where(even, even_in, odd_in))
    left = jnp.where(place == 0, 0.0, jnp.where(even, odd_in, even_in))
    lane_wide = lax.broadcasted_iota(jnp.int32, (BLOCK, lanes), 1)
    below = jnp.where(
        lane_wide % z_elems != z_elems - 1, pltpu.roll(far[:BLOCK], lanes - 1, 1), 0.0
    )
    far = jnp.concatenate([far, below], axis=0)
    lame_row, shear_row = material[0:1], material[1:2]
    result = stacked_dot(far_table, far)
    force = base + (lame_row * result[: 4 * PLANE] + shear_row * result[4 * PLANE :])
    left_lame = left[BLOCK - 1 : BLOCK]
    left_shear = left[2 * BLOCK - 1 : 2 * BLOCK]
    from_left = left_lame * touch[:PLANE] + left_shear * touch[PLANE:]
    from_left = jnp.concatenate([from_left[: 4 * BLOCK] + left, from_left[4 * BLOCK :]], axis=0)
    row, lane = block_iotas(lanes)
    across = lane // z_elems
    rows_first = row < 3
    rows_last = jnp.logical_and(row >= 4, row < 7)
    add_first = jnp.logical_and(rows_first, across > 0)
    take_last = jnp.logical_and(rows_last, across < y_elems - 1)
    pull_first = jnp.logical_and(rows_first, across == 0)
    pull_last = jnp.logical_and(rows_last, across == y_elems - 1)
    above = above_lanes(lanes, z_elems)
    below_t, own_t = tangents
    planes = []
    for x in range(4):
        blocks = []
        for zl in range(5):
            at = x * PLANE + zl * BLOCK
            block = force[at : at + BLOCK]
            if x == 0:
                block = block + from_left[zl * BLOCK : (zl + 1) * BLOCK]
            blocks.append(block)
        blocks[0] = blocks[0] + jnp.where(above, pltpu.roll(blocks[4], 1, 1), 0.0)
        stiff = jnp.where(
            jnp.logical_or(row == 1, row == 5),
            lock_stiffness,
            jnp.where(row < 4, below_t[4 * step + x : 4 * step + x + 1], own_t[4 * step + x : 4 * step + x + 1]),
        )
        pulled = stiff * (fault_in[8 * x : 8 * x + 8] - own_fault[8 * x : 8 * x + 8])
        for zl in range(4):
            low, high = blocks[zl][:8], blocks[zl][8:]
            low = low + jnp.where(
                add_first, pltpu.roll(pltpu.roll(high, 4, 0), z_elems, 1), 0.0
            )
            high = jnp.where(
                take_last, pltpu.roll(pltpu.roll(low, 4, 0), lanes - z_elems, 1), high
            )
            low = low - jnp.where(
                pull_first, pltpu.roll(pulled, (lanes - zl * z_elems) % lanes, 1), 0.0
            )
            high = high - jnp.where(
                pull_last,
                pltpu.roll(pulled, (lanes - (zl + 1) * z_elems) % lanes, 1),
                0.0,
            )
            blocks[zl] = jnp.concatenate([low, high], axis=0)
        blocks[4] = pltpu.roll(blocks[0], lanes - 1, 1)
        planes.extend(blocks)
    return (2.0 * cur - fol) - minv * jnp.concatenate(planes, axis=0)


def fault_input(up_ref, down_ref, count):
    if down_ref is None:
        return up_ref[:count]
    up, down = up_ref[:count], down_ref[:count]
    row = lax.broadcasted_iota(jnp.int32, up.shape, 0)
    return jnp.where(row % 8 < 4, up, down)


def step_kernel(*refs, step, last, last_place, pair, y_elems, z_elems):
    refs = list(refs)
    cur_ref, fol_ref, minv_ref, base_ref, touch_ref, material_ref, even_ref, odd_ref = refs[:8]
    refs = refs[8:]
    up_ref = refs.pop(0)
    down_ref = None if pair else refs.pop(0)
    first_up_ref, own_ref, first_own_ref, far_ref, edge_ref = refs[:5]
    refs = refs[5:]
    place = lax.axis_index("dom")
    cur = cur_ref[...]
    tangents = (first_up_ref[32:], first_own_ref[32:])
    new = advance(
        step, place, last_place, cur, fol_ref[...], minv_ref[...], base_ref[...], touch_ref[...],
        material_ref[...], even_ref[...], odd_ref[...], fault_input(up_ref, down_ref, 32), tangents,
        far_ref[...], swap_rows(own_ref[:32]), y_elems, z_elems,
    )
    if last:
        _, back_ref, out_ref, scratch = refs
        from_elements(new, scratch, back_ref, out_ref, y_elems)
    else:
        new_ref, even_out, odd_out, fault_out = refs
        new_ref[...] = new
        fault_out[...] = fault_message(new, z_elems)
        right = edge_force(edge_ref, new, material_ref[0:1], material_ref[1:2], z_elems)
        even_out[...], odd_out[...] = select_messages(place % 2, new[: 4 * BLOCK], right)


def output_kernel(*refs, pair, steps, y_elems, z_elems):
    owner_ref, field_ref, back_ref, weight_ref = refs[:4]
    out_ref, grad_ref, mask_ref, table_ref, scratch = refs[-5:]
    messages = refs[4:-5]
    count = 2 if pair else 3
    grads = [jnp.zeros((8, weight_ref.shape[1]), jnp.float32) for _ in range(4)]
    for i in range(steps):
        group = messages[count * i : count * (i + 1)]
        slip = -swap_rows(group[0][:32])
        if i < steps - 1:
            slip = slip + fault_input(group[1], None if pair else group[2], 32)
        for x in range(4):
            grads[x] = grads[x] + slip[8 * x : 8 * x + 8] * weight_ref[4 * i + x : 4 * i + x + 1]
    grad_ref[...] = jnp.concatenate(grads, axis=0)
    shape = (PATCH_ROWS, weight_ref.shape[1])
    first = (lax.axis_index("dom") - REACH) * PATCH_DEV
    number = lax.broadcasted_iota(jnp.int32, shape, 0) + first
    for x in range(4):
        mask = jnp.where(number == owner_ref[0, x], 1.0, 0.0)
        mask_ref[PATCH_ROWS * x : PATCH_ROWS * (x + 1)] = mask
    table_ref[...] = fault_table_back(weight_ref.shape[1], z_elems)
    from_elements(field_ref[...], scratch, back_ref, out_ref, y_elems)


def patch_kernel(*refs, pair, steps):
    mask_ref, weight_ref, grad_ref, table_ref, _, _, _, up_ref = refs[:8]
    down_ref = None if pair else refs[8]
    home_out, out_a, out_b, out_c, out_d = refs[-5:]
    place = lax.axis_index("dom")
    slip = fault_input(up_ref, down_ref, 32)
    total = 0.0
    for x in range(4):
        at, k = 8 * x + 4, 4 * (steps - 1) + x
        grad = grad_ref[at : at + 1] + slip[at : at + 1] * weight_ref[k : k + 1]
        total = total + mask_ref[PATCH_ROWS * x : PATCH_ROWS * (x + 1)] * grad
    total = exact_dot(total, table_ref[...])
    rows = [total[2 * i : 2 * i + 2] for i in range(5)]
    home_out[...] = rows[2]
    even = place % 2 == 0
    out_a[...] = jnp.where(even, rows[3], rows[1])
    out_b[...] = jnp.where(even, rows[1], rows[3])
    low = place % 4 < 2
    out_c[...] = jnp.where(low, rows[4], rows[0])
    out_d[...] = jnp.where(low, rows[0], rows[4])


VMEM = pl.BlockSpec(memory_space=pltpu.VMEM)
HBM = pl.BlockSpec(memory_space=pltpu.HBM)
SMEM = pl.BlockSpec(memory_space=pltpu.SMEM)
ANY = pl.BlockSpec(memory_space=pl.ANY)


def kernel_call(body, outs, args, in_smem=(), scratch=(), in_hbm=(), kept=(), unread=(), **static):
    shapes = []
    for out in outs:
        shape, dtype = out if isinstance(out[0], tuple) else (out, jnp.float32)
        shapes.append((pltpu.VMEM if in_hbm else jax.ShapeDtypeStruct)(shape, dtype))
    specs = [VMEM] * len(args)
    for places, spec in ((in_smem, SMEM), (in_hbm, HBM), (unread, ANY)):
        for i in places:
            specs[i] = spec
    copied = [pltpu.VMEM(args[i].shape, args[i].dtype) for i in in_hbm if i not in kept]
    if in_hbm:
        copied.append(pltpu.SemaphoreType.DMA((len(in_hbm),)))
    return pl.pallas_call(
        functools.partial(body, **static) if static else body,
        out_shape=shapes,
        in_specs=specs,
        out_specs=[VMEM] * len(shapes),
        scratch_shapes=list(scratch) + copied,
        compiler_params=pltpu.CompilerParams(
            vmem_limit_bytes=(56 if in_hbm else 24) * 2**20
        ),
    )(*args)


def swapped(block, distance, group):
    size, across = lax.axis_size("dom"), lax.axis_size("depth")
    partner = {}
    for left in range(size - distance):
        if left // distance % 2 == group:
            partner[left], partner[left + distance] = left + distance, left
    route = []
    for i in range(size):
        for j in range(across):
            side = j if i in partner else min(j ^ 1, across - 1)
            route.append((i * across + j, partner.get(i, i) * across + side))
    return lax.ppermute(block, ("dom", "depth"), route)


def from_behind(block, axis, distance):
    size = lax.axis_size(axis)
    return lax.ppermute(block, axis, [((i - distance) % size, i) for i in range(size)])


def on_device(
    adjoint_now,
    adjoint_next,
    lame_first,
    shear_modulus,
    density,
    branch_flags,
    weak_slope,
    normal_stress,
    patch_owner,
):
    x_elems, y_elems, z_elems = lame_first.shape
    lanes = y_elems * z_elems
    assert x_elems == 1 and lanes == adjoint_now.shape[3]
    steps = branch_flags.shape[0]
    pair = lax.axis_size("depth") == 2
    own_table, far_table, edge_table, touch_table = (jnp.asarray(t) for t in stiffness_tables())
    back = jnp.asarray(back_table(y_elems, z_elems))
    mass = jnp.asarray(mass_table(y_elems, z_elems))
    now = jnp.transpose(adjoint_now, (0, 2, 1, 3))
    following = jnp.transpose(adjoint_next, (0, 2, 1, 3))
    rho = jnp.transpose(density, (1, 0, 2))
    flags = branch_flags[:, 0]
    native = pltpu.VMEM((y_elems, 4 * BLOCK, lanes), jnp.float32)
    field = (4 * PLANE, lanes)
    plane = (4 * BLOCK, lanes)

    def exchange(even, odd, fault_rows):
        if pair:
            faults = [from_behind(fault_rows, "depth", 1)]
        else:
            faults = [from_behind(fault_rows, "depth", 1), from_behind(fault_rows, "depth", -1)]
        odd_in = swapped(odd, 1, 1)
        return swapped(even, 1, 0), odd_in, faults

    cur, even, odd, fault_rows, material, edge_table = kernel_call(
        first_kernel,
        [
            field, plane, plane, (32 + 4 * steps, lanes), (8, lanes),
            (edge_table.shape, edge_table.dtype),
        ],
        (
            now, flags, weak_slope[0], lame_first[0], shear_modulus[0], edge_table,
        ),
        (),
        [native],
        range(6),
        (5,),
    )
    first_fault = fault_rows
    even_in, odd_in, fault_in = exchange(even, odd, fault_rows)
    first_in = fault_in
    tables = (own_table, far_table, touch_table, back)
    fol, minv, weight, own_table, far_table, touch_table, back = kernel_call(
        setup_kernel,
        [field, field, (4 * steps, lanes)] + [(t.shape, t.dtype) for t in tables],
        (following, rho, flags, normal_stress[0], mass) + tables,
        (),
        [native],
        range(9),
        range(5, 9),
        y_elems=y_elems,
        z_elems=z_elems,
    )
    seen = []
    for step in range(steps):
        last = step == steps - 1
        seen += [fault_rows] + fault_in
        base, touch = kernel_call(
            prepare_kernel,
            [field, (2 * PLANE, lanes)],
            [cur, material, own_table, touch_table],
            (),
        )
        args = [cur, fol, minv, base, touch, material, even_in, odd_in] + fault_in
        args += [first_in[0], fault_rows, first_fault, far_table, edge_table]
        static = dict(
            step=step, last=last, last_place=lax.axis_size("dom") - 1, pair=pair, y_elems=y_elems,
            z_elems=z_elems,
        )
        if not last:
            new, even, odd, new_fault = kernel_call(
                step_kernel, [field, plane, plane, (32, lanes)], args, **static
            )
            fol, cur, fault_rows = cur, new, new_fault
            even_in, odd_in, fault_in = exchange(even, odd, fault_rows)
        else:
            whole = (3, 4 * y_elems + 1, 4, lanes)
            known = seen[: len(seen) - len(fault_in)]
            later, grad, mask, table = kernel_call(
                output_kernel,
                [whole, (32, lanes), (4 * PATCH_ROWS, lanes), ((lanes, lanes), jnp.bfloat16)],
                [patch_owner, cur, back, weight] + known,
                (0,),
                [native],
                pair=pair,
                steps=steps,
                y_elems=y_elems,
                z_elems=z_elems,
            )
            sums = kernel_call(
                patch_kernel,
                [(PATCH_DEV, lanes)] * 5,
                [mask, weight, grad, table, even_in, odd_in, touch] + fault_in,
                unread=(4, 5, 6),
                pair=pair,
                steps=steps,
            )
            patch_sums = sums[0]
            for i, distance, group in ((2, 1, 1), (4, 2, 1), (3, 2, 0), (1, 1, 0)):
                patch_sums = patch_sums + swapped(sums[i], distance, group)
            earlier = kernel_call(
                step_kernel,
                [whole],
                args + [sums[0], back],
                scratch=[native],
                unread=(len(args),),
                **static,
            )[0]
    return (
        jnp.transpose(earlier, (0, 2, 1, 3)),
        jnp.transpose(later, (0, 2, 1, 3)),
        patch_sums[None],
    )


def solution(mesh):
    return jax.shard_map(
        on_device,
        mesh=mesh,
        in_specs=(
            P(None, "dom", "depth", None),
            P(None, "dom", "depth", None),
            P("dom", "depth", None),
            P("dom", "depth", None),
            P("dom", "depth", None),
            P(None, "depth", "dom", None),
            P("depth", "dom", None),
            P("depth", "dom", None),
            P("depth", "dom"),
        ),
        out_specs=(
            P(None, "dom", "depth", None),
            P(None, "dom", "depth", None),
            P("depth", "dom", None),
        ),
        check_vma=False,
    )
```

```python
import functools
import math

import jax
import jax.numpy as jnp
import ml_dtypes
import numpy as np
from jax import lax
from jax.experimental import pallas as pl
from jax.experimental.pallas import tpu as pltpu
from jax.sharding import PartitionSpec as P

PATCH_DEV = 2
REACH = 2
PATCH_ROWS = 16

time_step = 0.01
lock_stiffness = 0.5

BLOCK = 16
ROWS = ((0, 1, 2), (3, 4, 5), (11, 12, 13), (6, 7, 14), (8, 9, 10))
PLANE = 5 * BLOCK


def basis_tables():
    points = [-1.0, -math.sqrt(3.0 / 7.0), 0.0, math.sqrt(3.0 / 7.0), 1.0]
    quad_weights = np.array([0.1, 49.0 / 90.0, 32.0 / 45.0, 49.0 / 90.0, 0.1])
    products = []
    for first in range(5):
        value = 1.0
        for other in range(5):
            if other != first:
                value = value * (points[first] - points[other])
        products.append(value)
    derivative = np.zeros((5, 5))
    for row in range(5):
        for column in range(5):
            if row == column:
                total = 0.0
                for other in range(5):
                    if other != row:
                        total = total + 1.0 / (points[row] - points[other])
                derivative[row, column] = total
            else:
                derivative[row, column] = (
                    products[row] / products[column] / (points[row] - points[column])
                )
    return (quad_weights, derivative)


def two_parts(table):
    high = table.astype(ml_dtypes.bfloat16)
    low = (table - high.astype(np.float64)).astype(ml_dtypes.bfloat16)
    return np.stack([high, low])


def element_stiffness():
    weights, derivative = basis_tables()
    eye = np.eye(5)
    slope = 2.0 * derivative
    grads = [
        np.kron(slope, np.kron(eye, eye)),
        np.kron(eye, np.kron(eye, slope)),
        np.kron(eye, np.kron(slope, eye)),
    ]
    quad = np.kron(weights, np.kron(weights, weights)) / 8.0
    first = np.zeros((125, 3, 125, 3))
    second = np.zeros((125, 3, 125, 3))
    lap = sum(g.T @ (quad[:, None] * g) for g in grads)
    for c in range(3):
        second[:, c, :, c] += lap
        for d in range(3):
            first[:, c, :, d] += grads[c].T @ (quad[:, None] * grads[d])
            second[:, c, :, d] += grads[d].T @ (quad[:, None] * grads[c])
    where = [
        node // 5 * BLOCK + ROWS[node % 5][c] for node in range(125) for c in range(3)
    ]
    wide = []
    for small in (first, second):
        big = np.zeros((5 * PLANE, 5 * PLANE))
        big[np.ix_(where, where)] = small.reshape(375, 375)
        wide.append(big)
    return wide


OWN_COLS = 384


def padded_table(table, columns):
    return np.pad(table, ((0, 0), (0, columns - table.shape[1])))


@functools.cache
def stiffness_tables():
    wide = element_stiffness()
    own = 4 * PLANE
    planes = [slice(x * PLANE, (x + 1) * PLANE) for x in range(5)]
    inner = np.concatenate([w[:own, :own] for w in wide])

    def three(rows, columns):
        high, low = two_parts(np.concatenate([w[rows, columns] for w in wide]))
        return padded_table(np.concatenate([high, low, high], axis=1), 256)

    return (
        two_parts(padded_table(inner, OWN_COLS)),
        np.stack([three(planes[x], planes[4]) for x in range(4)]),
        np.stack([three(planes[4], planes[x]) for x in range(4)]),
        three(planes[4], planes[4]),
    )


@functools.cache
def back_table(y_elems, z_elems):
    lanes = y_elems * z_elems
    depth = 4 * z_elems
    back = np.zeros((4 * lanes, y_elems * depth), ml_dtypes.bfloat16)
    for yel in range(y_elems):
        for k in range(z_elems):
            for zl in range(4):
                back[zl * lanes + yel * z_elems + k, yel * depth + 4 * k + zl] = 1
    return back


@functools.cache
def mass_table(y_elems, z_elems):
    weights, _ = basis_tables()
    table = np.zeros((4, 5, BLOCK, y_elems, z_elems))
    for x in range(4):
        mx = 0.2 if x == 0 else weights[x]
        for zl in range(5):
            for yl in range(5):
                for yel in range(y_elems):
                    my = weights[yl]
                    if (yl == 0 and yel > 0) or (yl == 4 and yel < y_elems - 1):
                        my = 0.2
                    mz = np.full(z_elems, weights[zl])
                    if zl == 0:
                        mz[1:] = 0.2
                    if zl == 4:
                        mz[:] = 0.2
                    value = time_step * time_step * 8.0 / (mx * my * mz)
                    if zl == 4:
                        value[-1] = 0.0
                    table[x, zl, list(ROWS[yl]), yel] = value
    return table.reshape(4 * PLANE, y_elems * z_elems).astype(np.float32)


def pieces(value, count):
    out = []
    for _ in range(count):
        piece = value.astype(jnp.bfloat16)
        out.append(piece)
        value = value - piece.astype(jnp.float32)
    return out


def dot(a, b):
    return jnp.dot(a, b, preferred_element_type=jnp.float32)


def exact_dot(value, table, count=3):
    rows = value.shape[0]
    result = dot(jnp.concatenate(pieces(value, count), axis=0), table)
    total = result[:rows]
    for i in range(1, count):
        total = total + result[i * rows : (i + 1) * rows]
    return total


def split_dot(table_high, table_low, value):
    lanes = value.shape[1]
    high, low = pieces(value, 2)
    wide = dot(table_high, jnp.concatenate([high, low], axis=1))
    return wide[:, :lanes] + (wide[:, lanes:] + dot(table_low, high))


def ones_where(rule, shape):
    row = lax.broadcasted_iota(jnp.int32, shape, 0)
    column = lax.broadcasted_iota(jnp.int32, shape, 1)
    return jnp.where(rule(row, column), 1.0, 0.0).astype(jnp.bfloat16)


def gather_table(lanes, z_elems):
    return ones_where(lambda z, c: z == 4 * (c % z_elems) + c // lanes, (lanes, 5 * lanes))


def fault_table(lanes, z_elems):
    return ones_where(lambda z, c: z == 4 * (c % z_elems) + c // z_elems, (lanes, lanes))


def fault_table_back(lanes, z_elems):
    return ones_where(lambda c, z: z == 4 * (c % z_elems) + c // z_elems, (lanes, lanes))


def stacked(value):
    high, low = pieces(value, 2)
    gap = jnp.zeros((256 - 3 * value.shape[0], value.shape[1]), jnp.bfloat16)
    return jnp.concatenate([high, high, low, gap], axis=0)


def to_elements(native, scratch, table, y_elems):
    group = 4 * BLOCK
    scratch[...] = jnp.zeros_like(scratch)
    for c in range(3):
        for y in range(4 * y_elems + 1):
            rows = native(c, y)
            if y < 4 * y_elems:
                scratch[y // 4, pl.ds(ROWS[y % 4][c], 4, stride=BLOCK), :] = rows
            if y % 4 == 0 and y > 0:
                scratch[y // 4 - 1, pl.ds(ROWS[4][c], 4, stride=BLOCK), :] = rows
    high, middle, low = pieces(
        jnp.concatenate([scratch[i] for i in range(y_elems)], axis=0), 3
    )
    result = dot(
        jnp.concatenate([high, middle], axis=1), jnp.concatenate([table, table], axis=0)
    ) + dot(low, table)
    lanes = result.shape[1] // 5
    across = lax.broadcasted_iota(jnp.int32, (group, result.shape[1]), 1) % lanes // (
        lanes // y_elems
    )
    total = result[:group]
    for yel in range(1, y_elems):
        total = jnp.where(across == yel, result[yel * group : (yel + 1) * group], total)
    blocks = []
    for x in range(4):
        for zl in range(5):
            blocks.append(total[x * BLOCK : (x + 1) * BLOCK, zl * lanes : (zl + 1) * lanes])
    return jnp.concatenate(blocks, axis=0)


def from_elements(field, scratch, back_ref, out_ref, y_elems):
    rows = []
    for x in range(4):
        rows.append(
            jnp.concatenate(
                [field[x * PLANE + zl * BLOCK : x * PLANE + (zl + 1) * BLOCK] for zl in range(4)],
                axis=1,
            )
        )
    result = exact_dot(jnp.concatenate(rows, axis=0), back_ref[...])
    depth = result.shape[1] // y_elems
    for yel in range(y_elems):
        scratch[yel] = result[:, yel * depth : (yel + 1) * depth]
    for c in range(3):
        for y in range(4 * y_elems + 1):
            yel, yl = (y // 4, y % 4) if y < 4 * y_elems else (y_elems - 1, 4)
            out_ref[c, y] = scratch[yel, pl.ds(ROWS[yl][c], 4, stride=BLOCK), :]


def shifted(rows, lanes):
    lanes = lanes % rows.shape[1]
    return pltpu.roll(rows, lanes, 1) if lanes else rows


def block_iotas(lanes):
    return (
        lax.broadcasted_iota(jnp.int32, (8, lanes), 0),
        lax.broadcasted_iota(jnp.int32, (8, lanes), 1),
    )


def fault_message(plane, z_elems):
    lanes = plane.shape[1]
    row, lane = block_iotas(lanes)
    first = last = jnp.zeros((8, lanes), jnp.float32)
    for zl in range(4):
        at = zl * BLOCK
        here = lane // z_elems == zl
        first = jnp.where(here, shifted(plane[at : at + 8], zl * z_elems), first)
        last = jnp.where(here, shifted(plane[at + 8 : at + 16], (zl + 1) * z_elems), last)
    return jnp.where(row < 4, last, pltpu.roll(first, 4, 0))


def swap_rows(message):
    parts = [pltpu.roll(message[i : i + 8], 4, 0) for i in range(0, message.shape[0], 8)]
    return jnp.concatenate(parts, axis=0)


def select_messages(parity, left, right):
    even = parity == 0
    return jnp.where(even, right, left), jnp.where(even, left, right)


def material_rows(lame_ref, shear_ref):
    y_elems, z_elems = lame_ref.shape
    both = jnp.concatenate([lame_ref[...], shear_ref[...]], axis=0)
    spread = ones_where(lambda k, c: c % z_elems == k, (z_elems, y_elems * z_elems))
    tiled = exact_dot(both, spread)
    row = lax.broadcasted_iota(jnp.int32, tiled.shape, 0)
    lane = lax.broadcasted_iota(jnp.int32, tiled.shape, 1)
    kept = jnp.where(row % y_elems == lane // z_elems, tiled, 0.0)
    return (
        jnp.sum(kept[:y_elems], axis=0, keepdims=True),
        jnp.sum(kept[y_elems:], axis=0, keepdims=True),
    )


def above_lanes(lanes, z_elems):
    return lax.broadcasted_iota(jnp.int32, (BLOCK, lanes), 1) % z_elems != 0


def edge_message(result, lame_row, shear_row, z_elems):
    lanes = result.shape[1]
    force = lame_row * result[:PLANE] + shear_row * result[PLANE:]
    top = force[:BLOCK] + jnp.where(
        above_lanes(lanes, z_elems), pltpu.roll(force[4 * BLOCK :], 1, 1), 0.0
    )
    row = lax.broadcasted_iota(jnp.int32, top.shape, 0)
    top = jnp.where(row == BLOCK - 1, lame_row, top)
    second = jnp.where(row == BLOCK - 1, shear_row, force[BLOCK : 2 * BLOCK])
    return jnp.concatenate([top, second, force[2 * BLOCK : 4 * BLOCK]], axis=0)


def own_force(own_ref, cur, lame_row, shear_row):
    rows, lanes = cur.shape
    padded = jnp.concatenate([cur, jnp.zeros((OWN_COLS - rows, lanes), jnp.float32)], axis=0)
    result = split_dot(own_ref[0], own_ref[1], padded)
    return lame_row * result[:rows] + shear_row * result[rows:]


def start_copies(pairs, sems):
    copies = [
        pltpu.make_async_copy(source, target, sems.at[i])
        for i, (source, target) in enumerate(pairs)
    ]
    for copy in copies:
        copy.start()
    return copies


def first_kernel(
    now_hbm,
    flags_hbm,
    weak_hbm,
    lame_hbm,
    shear_hbm,
    edge_hbm,
    cur_ref,
    even_ref,
    odd_ref,
    fault_out_ref,
    material_ref,
    edge_ref,
    scratch,
    now_ref,
    flags_ref,
    weak_ref,
    lame_ref,
    shear_ref,
    sems,
):
    copies = start_copies(
        [
            (now_hbm, now_ref),
            (flags_hbm, flags_ref),
            (weak_hbm, weak_ref),
            (lame_hbm, lame_ref),
            (shear_hbm, shear_ref),
            (edge_hbm, edge_ref),
        ],
        sems,
    )
    y_elems, z_elems = lame_ref.shape
    lanes = y_elems * z_elems
    parity = lax.axis_index("dom") % 2
    gather = gather_table(lanes, z_elems)
    fault = fault_table(lanes, z_elems)
    copies[1].wait()
    copies[2].wait()
    weak = weak_ref[...]
    tangent = []
    for i in range(flags_ref.shape[0]):
        flag = flags_ref[i]
        tangent.append(
            jnp.where(flag == 0, lock_stiffness, jnp.where(flag == 1, -weak, 0.0))
        )
    fault_out_ref[32:] = exact_dot(jnp.concatenate(tangent, axis=0), fault)
    copies[3].wait()
    copies[4].wait()
    lame_row, shear_row = material_rows(lame_ref, shear_ref)
    material_ref[...] = jnp.concatenate(
        [lame_row, shear_row, jnp.zeros((6, lanes), jnp.float32)], axis=0
    )
    copies[0].wait()
    cur = to_elements(lambda c, y: now_ref[c, y], scratch, gather, y_elems)
    copies[5].wait()
    planes = [cur[x * PLANE : (x + 1) * PLANE] for x in range(4)]
    edge = sum(dot(edge_ref[x], stacked(planes[x])) for x in range(4))
    right = edge_message(edge, lame_row, shear_row, z_elems)
    even_ref[...], odd_ref[...] = select_messages(parity, cur[: 4 * BLOCK], right)
    cur_ref[...] = cur
    for x in range(4):
        fault_out_ref[8 * x : 8 * x + 8] = fault_message(planes[x], z_elems)


def prepare_kernel(cur_ref, material_ref, own_ref, touch_ref, base_ref, edge_part_ref):
    cur = cur_ref[...]
    base_ref[...] = own_force(own_ref, cur, material_ref[0:1], material_ref[1:2])
    edge_part_ref[...] = dot(touch_ref[...], stacked(cur[:PLANE]))


def setup_kernel(
    next_hbm,
    density_hbm,
    flags_hbm,
    stress_hbm,
    mass_hbm,
    own_hbm,
    far_hbm,
    touch_hbm,
    back_hbm,
    fol_ref,
    minv_ref,
    weight_ref,
    own_ref,
    far_ref,
    touch_ref,
    back_ref,
    scratch,
    next_ref,
    density_ref,
    flags_ref,
    stress_ref,
    mass_ref,
    sems,
    *,
    y_elems,
    z_elems,
):
    copies = start_copies(
        [
            (next_hbm, next_ref),
            (density_hbm, density_ref),
            (flags_hbm, flags_ref),
            (stress_hbm, stress_ref),
            (mass_hbm, mass_ref),
            (own_hbm, own_ref),
            (far_hbm, far_ref),
            (touch_hbm, touch_ref),
            (back_hbm, back_ref),
        ],
        sems,
    )
    gather = gather_table(y_elems * z_elems, z_elems)
    fault = fault_table(y_elems * z_elems, z_elems)
    for copy in copies[:5]:
        copy.wait()
    fol_ref[...] = to_elements(lambda c, y: next_ref[c, y], scratch, gather, y_elems)
    density = to_elements(lambda c, y: density_ref[y], scratch, gather, y_elems)
    table = mass_ref[...]
    first = lax.axis_index("dom") == 0
    plane = lax.broadcasted_iota(jnp.int32, table.shape, 0) < PLANE
    table = jnp.where(jnp.logical_and(first, plane), 2.0 * table, table)
    minv_ref[...] = jnp.where(table > 0.0, table / jnp.where(table > 0.0, density, 1.0), 0.0)
    stress = stress_ref[...]
    weights = []
    for i in range(flags_ref.shape[0]):
        flag = flags_ref[i]
        weights.append(
            stress * jnp.where(flag == 1, 0.5, jnp.where(flag == 2, 1.0, 0.0))
        )
    weight_ref[...] = exact_dot(jnp.concatenate(weights, axis=0), fault)
    for copy in copies[5:]:
        copy.wait()


def fault_input(up_ref, down_ref, count):
    if down_ref is None:
        return up_ref[:count]
    up, down = up_ref[:count], down_ref[:count]
    row = lax.broadcasted_iota(jnp.int32, up.shape, 0)
    return jnp.where(row % 8 < 4, up, down)


def step_kernel(*refs, step, last, extra, last_place, pair, y_elems, z_elems):
    cur_ref, fol_ref, minv_ref, base_ref, touch_ref, material_ref, even_ref, odd_ref = refs[:8]
    refs = list(refs[8:])
    up_ref = refs.pop(0)
    down_ref = None if pair else refs.pop(0)
    first_up_ref, own_ref, first_own_ref, far_ref, edge_ref = refs[:5]
    refs = refs[5 + extra :]
    if last:
        back_ref, out_ref, scratch = refs
    else:
        new_ref, even_out, odd_out, fault_out = refs
    place = lax.axis_index("dom")
    lanes = cur_ref.shape[1]
    even = place % 2 == 0
    far = jnp.where(place == last_place, 0.0, jnp.where(even, even_ref[...], odd_ref[...]))
    left = jnp.where(place == 0, 0.0, jnp.where(even, odd_ref[...], even_ref[...]))
    lane_wide = lax.broadcasted_iota(jnp.int32, (BLOCK, lanes), 1)
    below = jnp.where(
        lane_wide % z_elems != z_elems - 1, pltpu.roll(far[:BLOCK], lanes - 1, 1), 0.0
    )
    far = stacked(jnp.concatenate([far, below], axis=0))
    lame_row, shear_row = material_ref[0:1], material_ref[1:2]
    left_lame = left[BLOCK - 1 : BLOCK]
    left_shear = left[2 * BLOCK - 1 : 2 * BLOCK]
    from_left = left_lame * touch_ref[:PLANE] + left_shear * touch_ref[PLANE:]
    row, lane = block_iotas(lanes)
    across = lane // z_elems
    shared = row < 3
    add_first = jnp.logical_and(shared, across > 0)
    take_last = jnp.logical_and(shared, across < y_elems - 1)
    pull_first = jnp.logical_and(shared, across == 0)
    pull_last = jnp.logical_and(shared, across == y_elems - 1)
    above = above_lanes(lanes, z_elems)
    fault_in = fault_input(up_ref, down_ref, 32)
    planes = []
    edge = 0.0
    for x in range(4):
        rows = slice(x * PLANE, (x + 1) * PLANE)
        result = dot(far_ref[x], far)
        force = base_ref[rows] + (lame_row * result[:PLANE] + shear_row * result[PLANE:])
        blocks = [force[zl * BLOCK : (zl + 1) * BLOCK] for zl in range(5)]
        if x == 0:
            blocks = [b + from_left[i * BLOCK : (i + 1) * BLOCK] for i, b in enumerate(blocks)]
            blocks[:4] = [b + left[i * BLOCK : (i + 1) * BLOCK] for i, b in enumerate(blocks[:4])]
        blocks[0] = blocks[0] + jnp.where(above, pltpu.roll(blocks[4], 1, 1), 0.0)
        at, k = slice(8 * x, 8 * x + 8), slice(32 + 4 * step + x, 33 + 4 * step + x)
        stiff = jnp.where(
            jnp.logical_or(row == 1, row == 5),
            lock_stiffness,
            jnp.where(row < 4, first_up_ref[k], first_own_ref[k]),
        )
        pulled = stiff * (fault_in[at] - pltpu.roll(own_ref[at], 4, 0))
        pulled_last = pltpu.roll(pulled, 4, 0)
        for zl in range(4):
            low, high = blocks[zl][:8], blocks[zl][8:]
            low = low + jnp.where(add_first, shifted(high, z_elems), 0.0)
            high = jnp.where(take_last, shifted(low, -z_elems), high)
            low = low - jnp.where(pull_first, shifted(pulled, -zl * z_elems), 0.0)
            high = high - jnp.where(
                pull_last, shifted(pulled_last, -(zl + 1) * z_elems), 0.0
            )
            blocks[zl] = jnp.concatenate([low, high], axis=0)
        blocks[4] = pltpu.roll(blocks[0], lanes - 1, 1)
        plane = (2.0 * cur_ref[rows] - fol_ref[rows]) - minv_ref[rows] * jnp.concatenate(
            blocks, axis=0
        )
        if last:
            planes.append(plane)
        else:
            new_ref[rows] = plane
            fault_out[at] = fault_message(plane, z_elems)
            edge = edge + dot(edge_ref[x], stacked(plane))
            if x == 0:
                first = plane[: 4 * BLOCK]
    if last:
        from_elements(jnp.concatenate(planes, axis=0), scratch, back_ref, out_ref, y_elems)
    else:
        right = edge_message(edge, lame_row, shear_row, z_elems)
        even_out[...], odd_out[...] = select_messages(place % 2, first, right)


def mask_kernel(owner_ref, _, mask_ref):
    shape = (PATCH_ROWS, mask_ref.shape[1])
    first = (lax.axis_index("dom") - REACH) * PATCH_DEV
    number = lax.broadcasted_iota(jnp.int32, shape, 0) + first
    for x in range(4):
        mask = jnp.where(number == owner_ref[0, x], 1.0, 0.0)
        mask_ref[PATCH_ROWS * x : PATCH_ROWS * (x + 1)] = mask


def output_kernel(*refs, pair, steps, y_elems, z_elems):
    field_ref, back_ref, weight_ref = refs[:3]
    out_ref, grad_ref, table_ref, scratch = refs[-4:]
    messages = refs[3:-4]
    count = 2 if pair else 3
    grads = [jnp.zeros((8, weight_ref.shape[1]), jnp.float32) for _ in range(4)]
    for i in range(steps):
        group = messages[count * i : count * (i + 1)]
        slip = -swap_rows(group[0][:32])
        if i < steps - 1:
            slip = slip + fault_input(group[1], None if pair else group[2], 32)
        for x in range(4):
            grads[x] = grads[x] + slip[8 * x : 8 * x + 8] * weight_ref[4 * i + x : 4 * i + x + 1]
    grad_ref[...] = jnp.concatenate(grads, axis=0)
    table_ref[...] = fault_table_back(weight_ref.shape[1], z_elems)
    from_elements(field_ref[...], scratch, back_ref, out_ref, y_elems)


def patch_kernel(*refs, pair, steps):
    mask_ref, weight_ref, grad_ref, table_ref, _, _, _, up_ref = refs[:8]
    down_ref = None if pair else refs[8]
    home_out, out_a, out_b, out_c, out_d = refs[-5:]
    place = lax.axis_index("dom")
    slip = fault_input(up_ref, down_ref, 32)
    total = 0.0
    for x in range(4):
        at, k = 8 * x + 4, 4 * (steps - 1) + x
        grad = grad_ref[at : at + 1] + slip[at : at + 1] * weight_ref[k : k + 1]
        total = total + mask_ref[PATCH_ROWS * x : PATCH_ROWS * (x + 1)] * grad
    total = exact_dot(total, table_ref[...])
    rows = [total[2 * i : 2 * i + 2] for i in range(5)]
    home_out[...] = rows[2]
    even = place % 2 == 0
    out_a[...] = jnp.where(even, rows[3], rows[1])
    out_b[...] = jnp.where(even, rows[1], rows[3])
    low = place % 4 < 2
    out_c[...] = jnp.where(low, rows[4], rows[0])
    out_d[...] = jnp.where(low, rows[0], rows[4])


VMEM = pl.BlockSpec(memory_space=pltpu.VMEM)
HBM = pl.BlockSpec(memory_space=pltpu.HBM)
SMEM = pl.BlockSpec(memory_space=pltpu.SMEM)
ANY = pl.BlockSpec(memory_space=pl.ANY)


def kernel_call(body, outs, args, in_smem=(), scratch=(), in_hbm=(), kept=(), unread=(), **static):
    shapes = []
    for out in outs:
        shape, dtype = out if isinstance(out[0], tuple) else (out, jnp.float32)
        shapes.append((pltpu.VMEM if in_hbm else jax.ShapeDtypeStruct)(shape, dtype))
    specs = [VMEM] * len(args)
    for places, spec in ((in_smem, SMEM), (in_hbm, HBM), (unread, ANY)):
        for i in places:
            specs[i] = spec
    copied = [pltpu.VMEM(args[i].shape, args[i].dtype) for i in in_hbm if i not in kept]
    if in_hbm:
        copied.append(pltpu.SemaphoreType.DMA((len(in_hbm),)))
    return pl.pallas_call(
        functools.partial(body, **static) if static else body,
        out_shape=shapes,
        in_specs=specs,
        out_specs=[VMEM] * len(shapes),
        scratch_shapes=list(scratch) + copied,
        compiler_params=pltpu.CompilerParams(
            vmem_limit_bytes=(56 if in_hbm else 24) * 2**20
        ),
    )(*args)


def swapped(block, distance, group):
    size, across = lax.axis_size("dom"), lax.axis_size("depth")
    partner = {}
    for left in range(size - distance):
        if left // distance % 2 == group:
            partner[left], partner[left + distance] = left + distance, left
    route = []
    for i in range(size):
        for j in range(across):
            side = j if i in partner else min(j ^ 1, across - 1)
            route.append((i * across + j, partner.get(i, i) * across + side))
    return lax.ppermute(block, ("dom", "depth"), route)


def from_behind(block, axis, distance):
    size = lax.axis_size(axis)
    return lax.ppermute(block, axis, [((i - distance) % size, i) for i in range(size)])


def on_device(
    adjoint_now,
    adjoint_next,
    lame_first,
    shear_modulus,
    density,
    branch_flags,
    weak_slope,
    normal_stress,
    patch_owner,
):
    x_elems, y_elems, z_elems = lame_first.shape
    lanes = y_elems * z_elems
    assert x_elems == 1 and lanes == adjoint_now.shape[3]
    steps = branch_flags.shape[0]
    pair = lax.axis_size("depth") == 2
    own_table, far_table, edge_table, touch_table = (jnp.asarray(t) for t in stiffness_tables())
    back = jnp.asarray(back_table(y_elems, z_elems))
    mass = jnp.asarray(mass_table(y_elems, z_elems))
    now = jnp.transpose(adjoint_now, (0, 2, 1, 3))
    following = jnp.transpose(adjoint_next, (0, 2, 1, 3))
    rho = jnp.transpose(density, (1, 0, 2))
    flags = branch_flags[:, 0]
    native = pltpu.VMEM((y_elems, 4 * BLOCK, lanes), jnp.float32)
    field = (4 * PLANE, lanes)
    plane = (4 * BLOCK, lanes)

    def exchange(even, odd, fault_rows):
        if pair:
            faults = [from_behind(fault_rows, "depth", 1)]
        else:
            faults = [from_behind(fault_rows, "depth", 1), from_behind(fault_rows, "depth", -1)]
        odd_in = swapped(odd, 1, 1)
        return swapped(even, 1, 0), odd_in, faults

    cur, even, odd, fault_rows, material, edge_table = kernel_call(
        first_kernel,
        [
            field, plane, plane, (32 + 4 * steps, lanes), (8, lanes),
            (edge_table.shape, edge_table.dtype),
        ],
        (
            now, flags, weak_slope[0], lame_first[0], shear_modulus[0], edge_table,
        ),
        (),
        [native],
        range(6),
        (5,),
    )
    first_fault = fault_rows
    even_in, odd_in, fault_in = exchange(even, odd, fault_rows)
    first_in = fault_in
    tables = (own_table, far_table, touch_table, back)
    fol, minv, weight, own_table, far_table, touch_table, back = kernel_call(
        setup_kernel,
        [field, field, (4 * steps, lanes)] + [(t.shape, t.dtype) for t in tables],
        (following, rho, flags, normal_stress[0], mass) + tables,
        (),
        [native],
        range(9),
        range(5, 9),
        y_elems=y_elems,
        z_elems=z_elems,
    )
    seen = []
    for step in range(steps):
        last = step == steps - 1
        seen += [fault_rows] + fault_in
        base, touch = kernel_call(
            prepare_kernel,
            [field, (2 * PLANE, lanes)],
            [cur, material, own_table, touch_table],
            (),
        )
        args = [cur, fol, minv, base, touch, material, even_in, odd_in] + fault_in
        args += [first_in[0], fault_rows, first_fault, far_table, edge_table]
        static = dict(
            step=step, last=last, extra=1 if last or step == 1 else 0, last_place=lax.axis_size("dom") - 1, pair=pair, y_elems=y_elems,
            z_elems=z_elems,
        )
        if step == 1:
            mask = kernel_call(mask_kernel, [(4 * PATCH_ROWS, lanes)], [patch_owner, cur], (0,), unread=(1,))[0]
            args.append(mask)
        if not last:
            new, even, odd, new_fault = kernel_call(
                step_kernel,
                [field, plane, plane, (32, lanes)],
                args,
                unread=(len(args) - 1,) if step == 1 else (),
                **static,
            )
            fol, cur, fault_rows = cur, new, new_fault
            even_in, odd_in, fault_in = exchange(even, odd, fault_rows)
        else:
            whole = (3, 4 * y_elems + 1, 4, lanes)
            known = seen[: len(seen) - len(fault_in)]
            later, grad, table = kernel_call(
                output_kernel,
                [whole, (32, lanes), ((lanes, lanes), jnp.bfloat16)],
                [cur, back, weight] + known,
                (),
                [native],
                pair=pair,
                steps=steps,
                y_elems=y_elems,
                z_elems=z_elems,
            )
            sums = kernel_call(
                patch_kernel,
                [(PATCH_DEV, lanes)] * 5,
                [mask, weight, grad, table, even_in, odd_in, touch] + fault_in,
                unread=(4, 5, 6),
                pair=pair,
                steps=steps,
            )
            patch_sums = sums[0]
            for i, distance, group in ((2, 1, 1), (4, 2, 1), (3, 2, 0), (1, 1, 0)):
                patch_sums = patch_sums + swapped(sums[i], distance, group)
            earlier = kernel_call(
                step_kernel,
                [whole],
                args + [sums[0], back],
                scratch=[native],
                unread=(len(args),),
                **static,
            )[0]
    return (
        jnp.transpose(earlier, (0, 2, 1, 3)),
        jnp.transpose(later, (0, 2, 1, 3)),
        patch_sums[None],
    )


def solution(mesh):
    return jax.shard_map(
        on_device,
        mesh=mesh,
        in_specs=(
            P(None, "dom", "depth", None),
            P(None, "dom", "depth", None),
            P("dom", "depth", None),
            P("dom", "depth", None),
            P("dom", "depth", None),
            P(None, "depth", "dom", None),
            P("depth", "dom", None),
            P("depth", "dom", None),
            P("depth", "dom"),
        ),
        out_specs=(
            P(None, "dom", "depth", None),
            P(None, "dom", "depth", None),
            P("depth", "dom", None),
        ),
        check_vma=False,
    )
```

```python
import functools
import math

import jax
import jax.numpy as jnp
import ml_dtypes
import numpy as np
from jax import lax
from jax.experimental import pallas as pl
from jax.experimental.pallas import tpu as pltpu
from jax.sharding import PartitionSpec as P

PATCH_DEV = 2
REACH = 2
PATCH_ROWS = 16

time_step = 0.01
lock_stiffness = 0.5

BLOCK = 16
ROWS = ((0, 1, 2), (3, 4, 5), (11, 12, 13), (6, 7, 14), (8, 9, 10))
PLANE = 5 * BLOCK


def basis_tables():
    points = [-1.0, -math.sqrt(3.0 / 7.0), 0.0, math.sqrt(3.0 / 7.0), 1.0]
    quad_weights = np.array([0.1, 49.0 / 90.0, 32.0 / 45.0, 49.0 / 90.0, 0.1])
    products = []
    for first in range(5):
        value = 1.0
        for other in range(5):
            if other != first:
                value = value * (points[first] - points[other])
        products.append(value)
    derivative = np.zeros((5, 5))
    for row in range(5):
        for column in range(5):
            if row == column:
                total = 0.0
                for other in range(5):
                    if other != row:
                        total = total + 1.0 / (points[row] - points[other])
                derivative[row, column] = total
            else:
                derivative[row, column] = (
                    products[row] / products[column] / (points[row] - points[column])
                )
    return (quad_weights, derivative)


def two_parts(table):
    high = table.astype(ml_dtypes.bfloat16)
    low = (table - high.astype(np.float64)).astype(ml_dtypes.bfloat16)
    return np.stack([high, low])


def element_stiffness():
    weights, derivative = basis_tables()
    eye = np.eye(5)
    slope = 2.0 * derivative
    grads = [
        np.kron(slope, np.kron(eye, eye)),
        np.kron(eye, np.kron(eye, slope)),
        np.kron(eye, np.kron(slope, eye)),
    ]
    quad = np.kron(weights, np.kron(weights, weights)) / 8.0
    first = np.zeros((125, 3, 125, 3))
    second = np.zeros((125, 3, 125, 3))
    lap = sum(g.T @ (quad[:, None] * g) for g in grads)
    for c in range(3):
        second[:, c, :, c] += lap
        for d in range(3):
            first[:, c, :, d] += grads[c].T @ (quad[:, None] * grads[d])
            second[:, c, :, d] += grads[d].T @ (quad[:, None] * grads[c])
    where = [
        node // 5 * BLOCK + ROWS[node % 5][c] for node in range(125) for c in range(3)
    ]
    wide = []
    for small in (first, second):
        big = np.zeros((5 * PLANE, 5 * PLANE))
        big[np.ix_(where, where)] = small.reshape(375, 375)
        wide.append(big)
    return wide


OWN_COLS = 384


def padded_table(table, columns):
    return np.pad(table, ((0, 0), (0, columns - table.shape[1])))


@functools.cache
def stiffness_tables():
    wide = element_stiffness()
    own = 4 * PLANE
    planes = [slice(x * PLANE, (x + 1) * PLANE) for x in range(5)]
    inner = np.concatenate([w[:own, :own] for w in wide])

    def three(rows, columns):
        high, low = two_parts(np.concatenate([w[rows, columns] for w in wide]))
        return padded_table(np.concatenate([high, low, high], axis=1), 256)

    return (
        two_parts(padded_table(inner, OWN_COLS)),
        np.stack([three(planes[x], planes[4]) for x in range(4)]),
        np.stack([three(planes[4], planes[x]) for x in range(4)]),
        three(planes[4], planes[4]),
    )


@functools.cache
def back_table(y_elems, z_elems):
    lanes = y_elems * z_elems
    depth = 4 * z_elems
    back = np.zeros((4 * lanes, y_elems * depth), ml_dtypes.bfloat16)
    for yel in range(y_elems):
        for k in range(z_elems):
            for zl in range(4):
                back[zl * lanes + yel * z_elems + k, yel * depth + 4 * k + zl] = 1
    return back


@functools.cache
def mass_table(y_elems, z_elems):
    weights, _ = basis_tables()
    table = np.zeros((4, 5, BLOCK, y_elems, z_elems))
    for x in range(4):
        mx = 0.2 if x == 0 else weights[x]
        for zl in range(5):
            for yl in range(5):
                for yel in range(y_elems):
                    my = weights[yl]
                    if (yl == 0 and yel > 0) or (yl == 4 and yel < y_elems - 1):
                        my = 0.2
                    mz = np.full(z_elems, weights[zl])
                    if zl == 0:
                        mz[1:] = 0.2
                    if zl == 4:
                        mz[:] = 0.2
                    value = time_step * time_step * 8.0 / (mx * my * mz)
                    if zl == 4:
                        value[-1] = 0.0
                    table[x, zl, list(ROWS[yl]), yel] = value
    return table.reshape(4 * PLANE, y_elems * z_elems).astype(np.float32)


def pieces(value, count):
    out = []
    for _ in range(count):
        piece = value.astype(jnp.bfloat16)
        out.append(piece)
        value = value - piece.astype(jnp.float32)
    return out


def dot(a, b):
    return jnp.dot(a, b, preferred_element_type=jnp.float32)


def exact_dot(value, table, count=3):
    rows = value.shape[0]
    result = dot(jnp.concatenate(pieces(value, count), axis=0), table)
    total = result[:rows]
    for i in range(1, count):
        total = total + result[i * rows : (i + 1) * rows]
    return total


def split_dot(table_high, table_low, value):
    lanes = value.shape[1]
    high, low = pieces(value, 2)
    wide = dot(table_high, jnp.concatenate([high, low], axis=1))
    return wide[:, :lanes] + (wide[:, lanes:] + dot(table_low, high))


def ones_where(rule, shape):
    row = lax.broadcasted_iota(jnp.int32, shape, 0)
    column = lax.broadcasted_iota(jnp.int32, shape, 1)
    return jnp.where(rule(row, column), 1.0, 0.0).astype(jnp.bfloat16)


def gather_table(lanes, z_elems):
    return ones_where(lambda z, c: z == 4 * (c % z_elems) + c // lanes, (lanes, 5 * lanes))


def fault_table(lanes, z_elems):
    return ones_where(lambda z, c: z == 4 * (c % z_elems) + c // z_elems, (lanes, lanes))


def fault_table_back(lanes, z_elems):
    return ones_where(lambda c, z: z == 4 * (c % z_elems) + c // z_elems, (lanes, lanes))


def stacked(value):
    high, low = pieces(value, 2)
    gap = jnp.zeros((256 - 3 * value.shape[0], value.shape[1]), jnp.bfloat16)
    return jnp.concatenate([high, high, low, gap], axis=0)


def to_elements(native, scratch, table, y_elems, parts=3):
    group = 4 * BLOCK
    scratch[...] = jnp.zeros_like(scratch)
    for c in range(3):
        for y in range(4 * y_elems + 1):
            rows = native(c, y)
            if y < 4 * y_elems:
                scratch[y // 4, pl.ds(ROWS[y % 4][c], 4, stride=BLOCK), :] = rows
            if y % 4 == 0 and y > 0:
                scratch[y // 4 - 1, pl.ds(ROWS[4][c], 4, stride=BLOCK), :] = rows
    high, middle, *low = pieces(
        jnp.concatenate([scratch[i] for i in range(y_elems)], axis=0), parts
    )
    result = dot(
        jnp.concatenate([high, middle], axis=1), jnp.concatenate([table, table], axis=0)
    )
    for piece in low:
        result = result + dot(piece, table)
    lanes = result.shape[1] // 5
    across = lax.broadcasted_iota(jnp.int32, (group, result.shape[1]), 1) % lanes // (
        lanes // y_elems
    )
    total = result[:group]
    for yel in range(1, y_elems):
        total = jnp.where(across == yel, result[yel * group : (yel + 1) * group], total)
    blocks = []
    for x in range(4):
        for zl in range(5):
            blocks.append(total[x * BLOCK : (x + 1) * BLOCK, zl * lanes : (zl + 1) * lanes])
    return jnp.concatenate(blocks, axis=0)


def from_elements(field, scratch, back_ref, out_ref, y_elems):
    rows = []
    for x in range(4):
        rows.append(
            jnp.concatenate(
                [field[x * PLANE + zl * BLOCK : x * PLANE + (zl + 1) * BLOCK] for zl in range(4)],
                axis=1,
            )
        )
    result = exact_dot(jnp.concatenate(rows, axis=0), back_ref[...])
    depth = result.shape[1] // y_elems
    for yel in range(y_elems):
        scratch[yel] = result[:, yel * depth : (yel + 1) * depth]
    for c in range(3):
        for y in range(4 * y_elems + 1):
            yel, yl = (y // 4, y % 4) if y < 4 * y_elems else (y_elems - 1, 4)
            out_ref[c, y] = scratch[yel, pl.ds(ROWS[yl][c], 4, stride=BLOCK), :]


def shifted(rows, lanes):
    lanes = lanes % rows.shape[1]
    return pltpu.roll(rows, lanes, 1) if lanes else rows


def block_iotas(lanes):
    return (
        lax.broadcasted_iota(jnp.int32, (8, lanes), 0),
        lax.broadcasted_iota(jnp.int32, (8, lanes), 1),
    )


def fault_message(plane, z_elems):
    lanes = plane.shape[1]
    row, lane = block_iotas(lanes)
    first = last = jnp.zeros((8, lanes), jnp.float32)
    for zl in range(4):
        at = zl * BLOCK
        here = lane // z_elems == zl
        first = jnp.where(here, shifted(plane[at : at + 8], zl * z_elems), first)
        last = jnp.where(here, shifted(plane[at + 8 : at + 16], (zl + 1) * z_elems), last)
    return jnp.where(row < 4, last, pltpu.roll(first, 4, 0))


def swap_rows(message):
    parts = [pltpu.roll(message[i : i + 8], 4, 0) for i in range(0, message.shape[0], 8)]
    return jnp.concatenate(parts, axis=0)


def select_messages(parity, left, right):
    even = parity == 0
    return jnp.where(even, right, left), jnp.where(even, left, right)


def material_rows(lame_ref, shear_ref):
    y_elems, z_elems = lame_ref.shape
    both = jnp.concatenate([lame_ref[...], shear_ref[...]], axis=0)
    spread = ones_where(lambda k, c: c % z_elems == k, (z_elems, y_elems * z_elems))
    tiled = exact_dot(both, spread)
    row = lax.broadcasted_iota(jnp.int32, tiled.shape, 0)
    lane = lax.broadcasted_iota(jnp.int32, tiled.shape, 1)
    kept = jnp.where(row % y_elems == lane // z_elems, tiled, 0.0)
    return (
        jnp.sum(kept[:y_elems], axis=0, keepdims=True),
        jnp.sum(kept[y_elems:], axis=0, keepdims=True),
    )


def above_lanes(lanes, z_elems):
    return lax.broadcasted_iota(jnp.int32, (BLOCK, lanes), 1) % z_elems != 0


def edge_message(result, lame_row, shear_row, z_elems):
    lanes = result.shape[1]
    force = lame_row * result[:PLANE] + shear_row * result[PLANE:]
    top = force[:BLOCK] + jnp.where(
        above_lanes(lanes, z_elems), pltpu.roll(force[4 * BLOCK :], 1, 1), 0.0
    )
    row = lax.broadcasted_iota(jnp.int32, top.shape, 0)
    top = jnp.where(row == BLOCK - 1, lame_row, top)
    second = jnp.where(row == BLOCK - 1, shear_row, force[BLOCK : 2 * BLOCK])
    return jnp.concatenate([top, second, force[2 * BLOCK : 4 * BLOCK]], axis=0)


def own_force(own_ref, cur, lame_row, shear_row):
    rows, lanes = cur.shape
    padded = jnp.concatenate([cur, jnp.zeros((OWN_COLS - rows, lanes), jnp.float32)], axis=0)
    result = split_dot(own_ref[0], own_ref[1], padded)
    return lame_row * result[:rows] + shear_row * result[rows:]


def start_copies(pairs, sems):
    copies = [
        pltpu.make_async_copy(source, target, sems.at[i])
        for i, (source, target) in enumerate(pairs)
    ]
    for copy in copies:
        copy.start()
    return copies


def first_kernel(
    now_hbm,
    flags_hbm,
    weak_hbm,
    lame_hbm,
    shear_hbm,
    edge_hbm,
    own_hbm,
    far_hbm,
    touch_hbm,
    cur_ref,
    even_ref,
    odd_ref,
    fault_out_ref,
    material_ref,
    edge_ref,
    own_ref,
    far_ref,
    touch_ref,
    scratch,
    now_ref,
    flags_ref,
    weak_ref,
    lame_ref,
    shear_ref,
    sems,
):
    copies = start_copies(
        [
            (now_hbm, now_ref),
            (flags_hbm, flags_ref),
            (weak_hbm, weak_ref),
            (lame_hbm, lame_ref),
            (shear_hbm, shear_ref),
            (edge_hbm, edge_ref),
            (own_hbm, own_ref),
            (far_hbm, far_ref),
            (touch_hbm, touch_ref),
        ],
        sems,
    )
    y_elems, z_elems = lame_ref.shape
    lanes = y_elems * z_elems
    parity = lax.axis_index("dom") % 2
    gather = gather_table(lanes, z_elems)
    fault = fault_table(lanes, z_elems)
    copies[1].wait()
    copies[2].wait()
    weak = weak_ref[...]
    tangent = []
    for i in range(flags_ref.shape[0]):
        flag = flags_ref[i]
        tangent.append(
            jnp.where(flag == 0, lock_stiffness, jnp.where(flag == 1, -weak, 0.0))
        )
    fault_out_ref[32:] = exact_dot(jnp.concatenate(tangent, axis=0), fault)
    copies[3].wait()
    copies[4].wait()
    lame_row, shear_row = material_rows(lame_ref, shear_ref)
    material_ref[...] = jnp.concatenate(
        [lame_row, shear_row, jnp.zeros((6, lanes), jnp.float32)], axis=0
    )
    copies[0].wait()
    cur = to_elements(lambda c, y: now_ref[c, y], scratch, gather, y_elems)
    copies[5].wait()
    planes = [cur[x * PLANE : (x + 1) * PLANE] for x in range(4)]
    edge = sum(dot(edge_ref[x], stacked(planes[x])) for x in range(4))
    right = edge_message(edge, lame_row, shear_row, z_elems)
    even_ref[...], odd_ref[...] = select_messages(parity, cur[: 4 * BLOCK], right)
    cur_ref[...] = cur
    for x in range(4):
        fault_out_ref[8 * x : 8 * x + 8] = fault_message(planes[x], z_elems)
    for copy in copies[6:]:
        copy.wait()


def prepare_kernel(cur_ref, material_ref, own_ref, touch_ref, base_ref, edge_part_ref):
    cur = cur_ref[...]
    base_ref[...] = own_force(own_ref, cur, material_ref[0:1], material_ref[1:2])
    edge_part_ref[...] = dot(touch_ref[...], stacked(cur[:PLANE]))


def setup_kernel(
    next_hbm,
    density_hbm,
    flags_hbm,
    stress_hbm,
    mass_hbm,
    fol_ref,
    minv_ref,
    weight_ref,
    scratch,
    next_ref,
    density_ref,
    flags_ref,
    stress_ref,
    mass_ref,
    sems,
    *,
    y_elems,
    z_elems,
):
    copies = start_copies(
        [
            (next_hbm, next_ref),
            (density_hbm, density_ref),
            (flags_hbm, flags_ref),
            (stress_hbm, stress_ref),
            (mass_hbm, mass_ref),
        ],
        sems,
    )
    gather = gather_table(y_elems * z_elems, z_elems)
    fault = fault_table(y_elems * z_elems, z_elems)
    for copy in copies[:5]:
        copy.wait()
    fol_ref[...] = to_elements(lambda c, y: next_ref[c, y], scratch, gather, y_elems)
    density = to_elements(lambda c, y: density_ref[y], scratch, gather, y_elems, 2)
    table = mass_ref[...]
    first = lax.axis_index("dom") == 0
    plane = lax.broadcasted_iota(jnp.int32, table.shape, 0) < PLANE
    table = jnp.where(jnp.logical_and(first, plane), 2.0 * table, table)
    minv_ref[...] = jnp.where(table > 0.0, table / jnp.where(table > 0.0, density, 1.0), 0.0)
    stress = stress_ref[...]
    weights = []
    for i in range(flags_ref.shape[0]):
        flag = flags_ref[i]
        weights.append(
            stress * jnp.where(flag == 1, 0.5, jnp.where(flag == 2, 1.0, 0.0))
        )
    weight_ref[...] = exact_dot(jnp.concatenate(weights, axis=0), fault)


def fault_input(up_ref, down_ref, count):
    if down_ref is None:
        return up_ref[:count]
    up, down = up_ref[:count], down_ref[:count]
    row = lax.broadcasted_iota(jnp.int32, up.shape, 0)
    return jnp.where(row % 8 < 4, up, down)


def step_kernel(*refs, step, last, extra, last_place, pair, y_elems, z_elems):
    cur_ref, fol_ref, minv_ref, base_ref, touch_ref, material_ref, odd_ref, up_ref = refs[:8]
    refs = list(refs[8:])
    down_ref = None if pair else refs.pop(0)
    even_ref = refs.pop(0)
    first_up_ref, own_ref, first_own_ref, far_ref, edge_ref = refs[:5]
    refs = refs[5 + extra :]
    if last:
        back_ref, out_ref, scratch = refs
    else:
        new_ref, even_out, odd_out, fault_out = refs
    place = lax.axis_index("dom")
    lanes = cur_ref.shape[1]
    even = place % 2 == 0
    far = jnp.where(place == last_place, 0.0, jnp.where(even, even_ref[...], odd_ref[...]))
    left = jnp.where(place == 0, 0.0, jnp.where(even, odd_ref[...], even_ref[...]))
    lane_wide = lax.broadcasted_iota(jnp.int32, (BLOCK, lanes), 1)
    below = jnp.where(
        lane_wide % z_elems != z_elems - 1, pltpu.roll(far[:BLOCK], lanes - 1, 1), 0.0
    )
    far = stacked(jnp.concatenate([far, below], axis=0))
    lame_row, shear_row = material_ref[0:1], material_ref[1:2]
    left_lame = left[BLOCK - 1 : BLOCK]
    left_shear = left[2 * BLOCK - 1 : 2 * BLOCK]
    from_left = left_lame * touch_ref[:PLANE] + left_shear * touch_ref[PLANE:]
    row, lane = block_iotas(lanes)
    across = lane // z_elems
    shared = row < 3
    add_first = jnp.logical_and(shared, across > 0)
    take_last = jnp.logical_and(shared, across < y_elems - 1)
    pull_first = jnp.logical_and(shared, across == 0)
    pull_last = jnp.logical_and(shared, across == y_elems - 1)
    above = above_lanes(lanes, z_elems)
    fault_in = fault_input(up_ref, down_ref, 32)
    planes = []
    edge = 0.0
    for x in range(4):
        rows = slice(x * PLANE, (x + 1) * PLANE)
        result = dot(far_ref[x], far)
        force = base_ref[rows] + (lame_row * result[:PLANE] + shear_row * result[PLANE:])
        blocks = [force[zl * BLOCK : (zl + 1) * BLOCK] for zl in range(5)]
        if x == 0:
            blocks = [b + from_left[i * BLOCK : (i + 1) * BLOCK] for i, b in enumerate(blocks)]
            blocks[:4] = [b + left[i * BLOCK : (i + 1) * BLOCK] for i, b in enumerate(blocks[:4])]
        blocks[0], blocks[4] = (
            blocks[0] + jnp.where(above, pltpu.roll(blocks[4], 1, 1), 0.0),
            blocks[4] + pltpu.roll(blocks[0], lanes - 1, 1),
        )
        at, k = slice(8 * x, 8 * x + 8), slice(32 + 4 * step + x, 33 + 4 * step + x)
        stiff = jnp.where(
            jnp.logical_or(row == 1, row == 5),
            lock_stiffness,
            jnp.where(row < 4, first_up_ref[k], first_own_ref[k]),
        )
        pulled = stiff * (fault_in[at] - pltpu.roll(own_ref[at], 4, 0))
        pulled_last = pltpu.roll(pulled, 4, 0)
        for zl in range(5):
            low, high = blocks[zl][:8], blocks[zl][8:]
            move = zl * z_elems if zl < 4 else 1
            blocks[zl] = jnp.concatenate(
                [
                    low
                    + jnp.where(add_first, shifted(high, z_elems), 0.0)
                    - jnp.where(pull_first, shifted(pulled, -move), 0.0),
                    high
                    + jnp.where(take_last, shifted(low, -z_elems), 0.0)
                    - jnp.where(pull_last, shifted(pulled_last, -move - z_elems), 0.0),
                ],
                axis=0,
            )
        plane = (2.0 * cur_ref[rows] - fol_ref[rows]) - minv_ref[rows] * jnp.concatenate(
            blocks, axis=0
        )
        if last:
            planes.append(plane)
        else:
            new_ref[rows] = plane
            fault_out[at] = fault_message(plane, z_elems)
            edge = edge + dot(edge_ref[x], stacked(plane))
            if x == 0:
                first = plane[: 4 * BLOCK]
    if last:
        from_elements(jnp.concatenate(planes, axis=0), scratch, back_ref, out_ref, y_elems)
    else:
        right = edge_message(edge, lame_row, shear_row, z_elems)
        even_out[...], odd_out[...] = select_messages(place % 2, first, right)


def mask_kernel(owner_ref, _, mask_ref):
    shape = (PATCH_ROWS, mask_ref.shape[1])
    first = (lax.axis_index("dom") - REACH) * PATCH_DEV
    number = lax.broadcasted_iota(jnp.int32, shape, 0) + first
    for x in range(4):
        mask = jnp.where(number == owner_ref[0, x], 1.0, 0.0)
        mask_ref[PATCH_ROWS * x : PATCH_ROWS * (x + 1)] = mask


def output_kernel(*refs, pair, steps, y_elems, z_elems):
    field_ref, back_ref, weight_ref = refs[:3]
    out_ref, grad_ref, table_ref, scratch = refs[-4:]
    messages = refs[3:-4]
    count = 2 if pair else 3
    grads = [jnp.zeros((8, weight_ref.shape[1]), jnp.float32) for _ in range(4)]
    for i in range(steps):
        group = messages[count * i : count * (i + 1)]
        slip = -swap_rows(group[0][:32])
        if i < steps - 1:
            slip = slip + fault_input(group[1], None if pair else group[2], 32)
        for x in range(4):
            grads[x] = grads[x] + slip[8 * x : 8 * x + 8] * weight_ref[4 * i + x : 4 * i + x + 1]
    grad_ref[...] = jnp.concatenate(grads, axis=0)
    table_ref[...] = fault_table_back(weight_ref.shape[1], z_elems)
    from_elements(field_ref[...], scratch, back_ref, out_ref, y_elems)


def patch_kernel(*refs, pair, steps):
    mask_ref, weight_ref, grad_ref, table_ref, _, up_ref = refs[:6]
    down_ref = None if pair else refs[6]
    home_out, out_a, out_b, out_c, out_d = refs[-5:]
    place = lax.axis_index("dom")
    slip = fault_input(up_ref, down_ref, 32)
    total = 0.0
    for x in range(4):
        at, k = 8 * x + 4, 4 * (steps - 1) + x
        grad = grad_ref[at : at + 1] + slip[at : at + 1] * weight_ref[k : k + 1]
        total = total + mask_ref[PATCH_ROWS * x : PATCH_ROWS * (x + 1)] * grad
    total = exact_dot(total, table_ref[...])
    rows = [total[2 * i : 2 * i + 2] for i in range(5)]
    home_out[...] = rows[2]
    even = place % 2 == 0
    out_a[...] = jnp.where(even, rows[3], rows[1])
    out_b[...] = jnp.where(even, rows[1], rows[3])
    low = place % 4 < 2
    out_c[...] = jnp.where(low, rows[4], rows[0])
    out_d[...] = jnp.where(low, rows[0], rows[4])


VMEM = pl.BlockSpec(memory_space=pltpu.VMEM)
HBM = pl.BlockSpec(memory_space=pltpu.HBM)
SMEM = pl.BlockSpec(memory_space=pltpu.SMEM)
ANY = pl.BlockSpec(memory_space=pl.ANY)


def kernel_call(body, outs, args, in_smem=(), scratch=(), in_hbm=(), kept=(), unread=(), **static):
    shapes = []
    for out in outs:
        shape, dtype = out if isinstance(out[0], tuple) else (out, jnp.float32)
        shapes.append((pltpu.VMEM if in_hbm else jax.ShapeDtypeStruct)(shape, dtype))
    specs = [VMEM] * len(args)
    for places, spec in ((in_smem, SMEM), (in_hbm, HBM), (unread, ANY)):
        for i in places:
            specs[i] = spec
    copied = [pltpu.VMEM(args[i].shape, args[i].dtype) for i in in_hbm if i not in kept]
    if in_hbm:
        copied.append(pltpu.SemaphoreType.DMA((len(in_hbm),)))
    return pl.pallas_call(
        functools.partial(body, **static) if static else body,
        out_shape=shapes,
        in_specs=specs,
        out_specs=[VMEM] * len(shapes),
        scratch_shapes=list(scratch) + copied,
        compiler_params=pltpu.CompilerParams(
            vmem_limit_bytes=(56 if in_hbm else 24) * 2**20
        ),
    )(*args)


def swapped(block, distance, group):
    size, across = lax.axis_size("dom"), lax.axis_size("depth")
    partner = {}
    for left in range(size - distance):
        if left // distance % 2 == group:
            partner[left], partner[left + distance] = left + distance, left
    route = []
    for i in range(size):
        for j in range(across):
            side = j if i in partner else min(j ^ 1, across - 1)
            route.append((i * across + j, partner.get(i, i) * across + side))
    return lax.ppermute(block, ("dom", "depth"), route)


def from_behind(block, axis, distance):
    size = lax.axis_size(axis)
    return lax.ppermute(block, axis, [((i - distance) % size, i) for i in range(size)])


def on_device(
    adjoint_now,
    adjoint_next,
    lame_first,
    shear_modulus,
    density,
    branch_flags,
    weak_slope,
    normal_stress,
    patch_owner,
):
    x_elems, y_elems, z_elems = lame_first.shape
    lanes = y_elems * z_elems
    assert x_elems == 1 and lanes == adjoint_now.shape[3]
    steps = branch_flags.shape[0]
    pair = lax.axis_size("depth") == 2
    own_table, far_table, edge_table, touch_table = (jnp.asarray(t) for t in stiffness_tables())
    back = jnp.asarray(back_table(y_elems, z_elems))
    mass = jnp.asarray(mass_table(y_elems, z_elems))
    now = jnp.transpose(adjoint_now, (0, 2, 1, 3))
    following = jnp.transpose(adjoint_next, (0, 2, 1, 3))
    rho = jnp.transpose(density, (1, 0, 2))
    flags = branch_flags[:, 0]
    native = pltpu.VMEM((y_elems, 4 * BLOCK, lanes), jnp.float32)
    field = (4 * PLANE, lanes)
    plane = (4 * BLOCK, lanes)

    def exchange(even, odd, fault_rows):
        if pair:
            faults = [from_behind(fault_rows, "depth", 1)]
        else:
            faults = [from_behind(fault_rows, "depth", 1), from_behind(fault_rows, "depth", -1)]
        odd_in = swapped(odd, 1, 1)
        return swapped(even, 1, 0), odd_in, faults

    tables = (edge_table, own_table, far_table, touch_table)
    cur, even, odd, fault_rows, material, edge_table, own_table, far_table, touch_table = kernel_call(
        first_kernel,
        [field, plane, plane, (32 + 4 * steps, lanes), (8, lanes)]
        + [(t.shape, t.dtype) for t in tables],
        (now, flags, weak_slope[0], lame_first[0], shear_modulus[0]) + tables,
        scratch=[native],
        in_hbm=range(9),
        kept=range(5, 9),
    )
    first_fault = fault_rows
    even_in, odd_in, fault_in = exchange(even, odd, fault_rows)
    first_in = fault_in
    fol, minv, weight = kernel_call(
        setup_kernel,
        [field, field, (4 * steps, lanes)],
        (following, rho, flags, normal_stress[0], mass),
        scratch=[native],
        in_hbm=range(5),
        y_elems=y_elems,
        z_elems=z_elems,
    )
    seen = []
    for step in range(steps):
        last = step == steps - 1
        seen += [fault_rows] + fault_in
        base, touch = kernel_call(
            prepare_kernel,
            [field, (2 * PLANE, lanes)],
            [cur, material, own_table, touch_table],
            (),
        )
        args = [cur, fol, minv, base, touch, material, odd_in] + fault_in
        args += [even_in, first_in[0], fault_rows, first_fault, far_table, edge_table]
        static = dict(
            step=step, last=last, extra=1 if last or step == 1 else 0, last_place=lax.axis_size("dom") - 1, pair=pair, y_elems=y_elems,
            z_elems=z_elems,
        )
        if step == 1:
            mask = kernel_call(mask_kernel, [(4 * PATCH_ROWS, lanes)], [patch_owner, cur], (0,), unread=(1,))[0]
            args.append(mask)
        if not last:
            new, even, odd, new_fault = kernel_call(
                step_kernel,
                [field, plane, plane, (32, lanes)],
                args,
                unread=(len(args) - 1,) if step == 1 else (),
                **static,
            )
            fol, cur, fault_rows = cur, new, new_fault
            even_in, odd_in, fault_in = exchange(even, odd, fault_rows)
        else:
            whole = (3, 4 * y_elems + 1, 4, lanes)
            known = seen[: len(seen) - len(fault_in)]
            later, grad, table = kernel_call(
                output_kernel,
                [whole, (32, lanes), ((lanes, lanes), jnp.bfloat16)],
                [cur, back, weight] + known,
                (),
                [native],
                pair=pair,
                steps=steps,
                y_elems=y_elems,
                z_elems=z_elems,
            )
            sums = kernel_call(
                patch_kernel,
                [(PATCH_DEV, lanes)] * 5,
                [mask, weight, grad, table, odd_in] + fault_in + [even_in, touch],
                unread=(4, 5 + len(fault_in), 6 + len(fault_in)),
                pair=pair,
                steps=steps,
            )
            patch_sums = sums[0]
            for i, distance, group in ((2, 1, 1), (4, 2, 1), (3, 2, 0), (1, 1, 0)):
                patch_sums = patch_sums + swapped(sums[i], distance, group)
            earlier = kernel_call(
                step_kernel,
                [whole],
                args + [sums[0], back],
                scratch=[native],
                unread=(len(args),),
                **static,
            )[0]
    return (
        jnp.transpose(earlier, (0, 2, 1, 3)),
        jnp.transpose(later, (0, 2, 1, 3)),
        patch_sums[None],
    )


def solution(mesh):
    return jax.shard_map(
        on_device,
        mesh=mesh,
        in_specs=(
            P(None, "dom", "depth", None),
            P(None, "dom", "depth", None),
            P("dom", "depth", None),
            P("dom", "depth", None),
            P("dom", "depth", None),
            P(None, "depth", "dom", None),
            P("depth", "dom", None),
            P("depth", "dom", None),
            P("depth", "dom"),
        ),
        out_specs=(
            P(None, "dom", "depth", None),
            P(None, "dom", "depth", None),
            P("depth", "dom", None),
        ),
        check_vma=False,
    )
```

```python
import functools
import math

import jax
import jax.numpy as jnp
import ml_dtypes
import numpy as np
from jax import lax
from jax.experimental import pallas as pl
from jax.experimental.pallas import tpu as pltpu
from jax.sharding import PartitionSpec as P

PATCH_DEV = 2
REACH = 2
PATCH_ROWS = 16

time_step = 0.01
lock_stiffness = 0.5

BLOCK = 16
ROWS = ((0, 1, 2), (3, 4, 5), (11, 12, 13), (6, 7, 14), (8, 9, 10))
PLANE = 5 * BLOCK


def basis_tables():
    points = [-1.0, -math.sqrt(3.0 / 7.0), 0.0, math.sqrt(3.0 / 7.0), 1.0]
    quad_weights = np.array([0.1, 49.0 / 90.0, 32.0 / 45.0, 49.0 / 90.0, 0.1])
    products = []
    for first in range(5):
        value = 1.0
        for other in range(5):
            if other != first:
                value = value * (points[first] - points[other])
        products.append(value)
    derivative = np.zeros((5, 5))
    for row in range(5):
        for column in range(5):
            if row == column:
                total = 0.0
                for other in range(5):
                    if other != row:
                        total = total + 1.0 / (points[row] - points[other])
                derivative[row, column] = total
            else:
                derivative[row, column] = (
                    products[row] / products[column] / (points[row] - points[column])
                )
    return (quad_weights, derivative)


def two_parts(table):
    high = table.astype(ml_dtypes.bfloat16)
    low = (table - high.astype(np.float64)).astype(ml_dtypes.bfloat16)
    return np.stack([high, low])


def element_stiffness():
    weights, derivative = basis_tables()
    eye = np.eye(5)
    slope = 2.0 * derivative
    grads = [
        np.kron(slope, np.kron(eye, eye)),
        np.kron(eye, np.kron(eye, slope)),
        np.kron(eye, np.kron(slope, eye)),
    ]
    quad = np.kron(weights, np.kron(weights, weights)) / 8.0
    first = np.zeros((125, 3, 125, 3))
    second = np.zeros((125, 3, 125, 3))
    lap = sum(g.T @ (quad[:, None] * g) for g in grads)
    for c in range(3):
        second[:, c, :, c] += lap
        for d in range(3):
            first[:, c, :, d] += grads[c].T @ (quad[:, None] * grads[d])
            second[:, c, :, d] += grads[d].T @ (quad[:, None] * grads[c])
    where = [
        node // 5 * BLOCK + ROWS[node % 5][c] for node in range(125) for c in range(3)
    ]
    wide = []
    for small in (first, second):
        big = np.zeros((5 * PLANE, 5 * PLANE))
        big[np.ix_(where, where)] = small.reshape(375, 375)
        wide.append(big)
    return wide


OWN_COLS = 384


def padded_table(table, columns):
    return np.pad(table, ((0, 0), (0, columns - table.shape[1])))


@functools.cache
def stiffness_tables():
    wide = element_stiffness()
    own = 4 * PLANE
    planes = [slice(x * PLANE, (x + 1) * PLANE) for x in range(5)]
    inner = np.concatenate([w[:own, :own] for w in wide])

    def three(rows, columns):
        high, low = two_parts(np.concatenate([w[rows, columns] for w in wide]))
        return padded_table(np.concatenate([high, low, high], axis=1), 256)

    return (
        two_parts(padded_table(inner, OWN_COLS)),
        np.stack([three(planes[x], planes[4]) for x in range(4)]),
        np.stack([three(planes[4], planes[x]) for x in range(4)]),
        three(planes[4], planes[4]),
    )


@functools.cache
def back_table(y_elems, z_elems):
    lanes = y_elems * z_elems
    depth = 4 * z_elems
    back = np.zeros((4 * lanes, y_elems * depth), ml_dtypes.bfloat16)
    for yel in range(y_elems):
        for k in range(z_elems):
            for zl in range(4):
                back[zl * lanes + yel * z_elems + k, yel * depth + 4 * k + zl] = 1
    return back


@functools.cache
def mass_table(y_elems, z_elems):
    weights, _ = basis_tables()
    table = np.zeros((4, 5, BLOCK, y_elems, z_elems))
    for x in range(4):
        mx = 0.2 if x == 0 else weights[x]
        for zl in range(5):
            for yl in range(5):
                for yel in range(y_elems):
                    my = weights[yl]
                    if (yl == 0 and yel > 0) or (yl == 4 and yel < y_elems - 1):
                        my = 0.2
                    mz = np.full(z_elems, weights[zl])
                    if zl == 0:
                        mz[1:] = 0.2
                    if zl == 4:
                        mz[:] = 0.2
                    value = time_step * time_step * 8.0 / (mx * my * mz)
                    if zl == 4:
                        value[-1] = 0.0
                    table[x, zl, list(ROWS[yl]), yel] = value
    return table.reshape(4 * PLANE, y_elems * z_elems).astype(np.float32)


def pieces(value, count):
    out = []
    for _ in range(count):
        piece = value.astype(jnp.bfloat16)
        out.append(piece)
        value = value - piece.astype(jnp.float32)
    return out


def dot(a, b):
    return jnp.dot(a, b, preferred_element_type=jnp.float32)


def exact_dot(value, table, count=3):
    rows = value.shape[0]
    result = dot(jnp.concatenate(pieces(value, count), axis=0), table)
    total = result[:rows]
    for i in range(1, count):
        total = total + result[i * rows : (i + 1) * rows]
    return total


def split_dot(table_high, table_low, value):
    lanes = value.shape[1]
    high, low = pieces(value, 2)
    wide = dot(table_high, jnp.concatenate([high, low], axis=1))
    return wide[:, :lanes] + (wide[:, lanes:] + dot(table_low, high))


def ones_where(rule, shape):
    row = lax.broadcasted_iota(jnp.int32, shape, 0)
    column = lax.broadcasted_iota(jnp.int32, shape, 1)
    return jnp.where(rule(row, column), 1.0, 0.0).astype(jnp.bfloat16)


def gather_table(lanes, z_elems):
    return ones_where(lambda z, c: z == 4 * (c % z_elems) + c // lanes, (lanes, 5 * lanes))


def fault_table(lanes, z_elems):
    return ones_where(lambda z, c: z == 4 * (c % z_elems) + c // z_elems, (lanes, lanes))


def fault_table_back(lanes, z_elems):
    return ones_where(lambda c, z: z == 4 * (c % z_elems) + c // z_elems, (lanes, lanes))


def stacked(value):
    high, low = pieces(value, 2)
    gap = jnp.zeros((256 - 3 * value.shape[0], value.shape[1]), jnp.bfloat16)
    return jnp.concatenate([high, high, low, gap], axis=0)


def to_elements(native, scratch, table, y_elems, parts=3):
    group = 4 * BLOCK
    scratch[...] = jnp.zeros_like(scratch)
    for c in range(3):
        for y in range(4 * y_elems + 1):
            rows = native(c, y)
            if y < 4 * y_elems:
                scratch[y // 4, pl.ds(ROWS[y % 4][c], 4, stride=BLOCK), :] = rows
            if y % 4 == 0 and y > 0:
                scratch[y // 4 - 1, pl.ds(ROWS[4][c], 4, stride=BLOCK), :] = rows
    high, middle, *low = pieces(
        jnp.concatenate([scratch[i] for i in range(y_elems)], axis=0), parts
    )
    result = dot(
        jnp.concatenate([high, middle], axis=1), jnp.concatenate([table, table], axis=0)
    )
    for piece in low:
        result = result + dot(piece, table)
    lanes = result.shape[1] // 5
    across = lax.broadcasted_iota(jnp.int32, (group, result.shape[1]), 1) % lanes // (
        lanes // y_elems
    )
    total = result[:group]
    for yel in range(1, y_elems):
        total = jnp.where(across == yel, result[yel * group : (yel + 1) * group], total)
    blocks = []
    for x in range(4):
        for zl in range(5):
            blocks.append(total[x * BLOCK : (x + 1) * BLOCK, zl * lanes : (zl + 1) * lanes])
    return jnp.concatenate(blocks, axis=0)


def from_elements(field, scratch, back_ref, out_ref, y_elems):
    rows = []
    for x in range(4):
        rows.append(
            jnp.concatenate(
                [field[x * PLANE + zl * BLOCK : x * PLANE + (zl + 1) * BLOCK] for zl in range(4)],
                axis=1,
            )
        )
    result = exact_dot(jnp.concatenate(rows, axis=0), back_ref[...])
    depth = result.shape[1] // y_elems
    for yel in range(y_elems):
        scratch[yel] = result[:, yel * depth : (yel + 1) * depth]
    for c in range(3):
        for y in range(4 * y_elems + 1):
            yel, yl = (y // 4, y % 4) if y < 4 * y_elems else (y_elems - 1, 4)
            out_ref[c, y] = scratch[yel, pl.ds(ROWS[yl][c], 4, stride=BLOCK), :]


def shifted(rows, lanes):
    lanes = lanes % rows.shape[1]
    return pltpu.roll(rows, lanes, 1) if lanes else rows


def block_iotas(lanes):
    return (
        lax.broadcasted_iota(jnp.int32, (8, lanes), 0),
        lax.broadcasted_iota(jnp.int32, (8, lanes), 1),
    )


def fault_message(plane, z_elems):
    lanes = plane.shape[1]
    row, lane = block_iotas(lanes)
    first = last = jnp.zeros((8, lanes), jnp.float32)
    for zl in range(4):
        at = zl * BLOCK
        here = lane // z_elems == zl
        first = jnp.where(here, shifted(plane[at : at + 8], zl * z_elems), first)
        last = jnp.where(here, shifted(plane[at + 8 : at + 16], (zl + 1) * z_elems), last)
    return jnp.where(row < 4, last, pltpu.roll(first, 4, 0))


def swap_rows(message):
    parts = [pltpu.roll(message[i : i + 8], 4, 0) for i in range(0, message.shape[0], 8)]
    return jnp.concatenate(parts, axis=0)


def select_messages(parity, left, right):
    even = parity == 0
    return jnp.where(even, right, left), jnp.where(even, left, right)


def material_rows(lame_ref, shear_ref):
    y_elems, z_elems = lame_ref.shape
    both = jnp.concatenate([lame_ref[...], shear_ref[...]], axis=0)
    spread = ones_where(lambda k, c: c % z_elems == k, (z_elems, y_elems * z_elems))
    tiled = exact_dot(both, spread)
    row = lax.broadcasted_iota(jnp.int32, tiled.shape, 0)
    lane = lax.broadcasted_iota(jnp.int32, tiled.shape, 1)
    kept = jnp.where(row % y_elems == lane // z_elems, tiled, 0.0)
    return (
        jnp.sum(kept[:y_elems], axis=0, keepdims=True),
        jnp.sum(kept[y_elems:], axis=0, keepdims=True),
    )


def above_lanes(lanes, z_elems):
    return lax.broadcasted_iota(jnp.int32, (BLOCK, lanes), 1) % z_elems != 0


def edge_message(result, lame_row, shear_row, z_elems):
    lanes = result.shape[1]
    force = lame_row * result[:PLANE] + shear_row * result[PLANE:]
    top = force[:BLOCK] + jnp.where(
        above_lanes(lanes, z_elems), pltpu.roll(force[4 * BLOCK :], 1, 1), 0.0
    )
    row = lax.broadcasted_iota(jnp.int32, top.shape, 0)
    top = jnp.where(row == BLOCK - 1, lame_row, top)
    second = jnp.where(row == BLOCK - 1, shear_row, force[BLOCK : 2 * BLOCK])
    return jnp.concatenate([top, second, force[2 * BLOCK : 4 * BLOCK]], axis=0)


def own_force(own_ref, cur, lame_row, shear_row):
    rows, lanes = cur.shape
    padded = jnp.concatenate([cur, jnp.zeros((OWN_COLS - rows, lanes), jnp.float32)], axis=0)
    result = split_dot(own_ref[0], own_ref[1], padded)
    return lame_row * result[:rows] + shear_row * result[rows:]


def start_copies(pairs, sems):
    copies = [
        pltpu.make_async_copy(source, target, sems.at[i])
        for i, (source, target) in enumerate(pairs)
    ]
    for copy in copies:
        copy.start()
    return copies


def first_kernel(
    now_hbm,
    flags_hbm,
    weak_hbm,
    lame_hbm,
    shear_hbm,
    edge_hbm,
    own_hbm,
    far_hbm,
    touch_hbm,
    cur_ref,
    even_ref,
    odd_ref,
    fault_out_ref,
    material_ref,
    edge_ref,
    own_ref,
    far_ref,
    touch_ref,
    scratch,
    now_ref,
    flags_ref,
    weak_ref,
    lame_ref,
    shear_ref,
    sems,
):
    copies = start_copies(
        [
            (now_hbm, now_ref),
            (flags_hbm, flags_ref),
            (weak_hbm, weak_ref),
            (lame_hbm, lame_ref),
            (shear_hbm, shear_ref),
            (edge_hbm, edge_ref),
            (own_hbm, own_ref),
            (far_hbm, far_ref),
            (touch_hbm, touch_ref),
        ],
        sems,
    )
    y_elems, z_elems = lame_ref.shape
    lanes = y_elems * z_elems
    parity = lax.axis_index("dom") % 2
    gather = gather_table(lanes, z_elems)
    fault = fault_table(lanes, z_elems)
    copies[1].wait()
    copies[2].wait()
    weak = weak_ref[...]
    tangent = []
    for i in range(flags_ref.shape[0]):
        flag = flags_ref[i]
        tangent.append(
            jnp.where(flag == 0, lock_stiffness, jnp.where(flag == 1, -weak, 0.0))
        )
    fault_out_ref[32:] = exact_dot(jnp.concatenate(tangent, axis=0), fault)
    copies[3].wait()
    copies[4].wait()
    lame_row, shear_row = material_rows(lame_ref, shear_ref)
    material_ref[...] = jnp.concatenate(
        [lame_row, shear_row, jnp.zeros((6, lanes), jnp.float32)], axis=0
    )
    copies[0].wait()
    cur = to_elements(lambda c, y: now_ref[c, y], scratch, gather, y_elems)
    copies[5].wait()
    planes = [cur[x * PLANE : (x + 1) * PLANE] for x in range(4)]
    edge = sum(dot(edge_ref[x], stacked(planes[x])) for x in range(4))
    right = edge_message(edge, lame_row, shear_row, z_elems)
    even_ref[...], odd_ref[...] = select_messages(parity, cur[: 4 * BLOCK], right)
    cur_ref[...] = cur
    for x in range(4):
        fault_out_ref[8 * x : 8 * x + 8] = fault_message(planes[x], z_elems)
    for copy in copies[6:]:
        copy.wait()


def prepare_kernel(cur_ref, material_ref, own_ref, touch_ref, base_ref, edge_part_ref):
    cur = cur_ref[...]
    base_ref[...] = own_force(own_ref, cur, material_ref[0:1], material_ref[1:2])
    edge_part_ref[...] = dot(touch_ref[...], stacked(cur[:PLANE]))


def setup_kernel(
    next_hbm,
    density_hbm,
    flags_hbm,
    stress_hbm,
    mass_hbm,
    fol_ref,
    minv_ref,
    weight_ref,
    scratch,
    next_ref,
    density_ref,
    flags_ref,
    stress_ref,
    mass_ref,
    sems,
    *,
    y_elems,
    z_elems,
):
    copies = start_copies(
        [
            (next_hbm, next_ref),
            (density_hbm, density_ref),
            (flags_hbm, flags_ref),
            (stress_hbm, stress_ref),
            (mass_hbm, mass_ref),
        ],
        sems,
    )
    gather = gather_table(y_elems * z_elems, z_elems)
    fault = fault_table(y_elems * z_elems, z_elems)
    for copy in copies[:5]:
        copy.wait()
    fol_ref[...] = to_elements(lambda c, y: next_ref[c, y], scratch, gather, y_elems)
    density = to_elements(lambda c, y: density_ref[y], scratch, gather, y_elems, 2)
    table = mass_ref[...]
    first = lax.axis_index("dom") == 0
    plane = lax.broadcasted_iota(jnp.int32, table.shape, 0) < PLANE
    table = jnp.where(jnp.logical_and(first, plane), 2.0 * table, table)
    minv_ref[...] = jnp.where(table > 0.0, table / jnp.where(table > 0.0, density, 1.0), 0.0)
    stress = stress_ref[...]
    weights = []
    for i in range(flags_ref.shape[0]):
        flag = flags_ref[i]
        weights.append(
            stress * jnp.where(flag == 1, 0.5, jnp.where(flag == 2, 1.0, 0.0))
        )
    weight_ref[...] = exact_dot(jnp.concatenate(weights, axis=0), fault)


def fault_input(up_ref, down_ref, count):
    if down_ref is None:
        return up_ref[:count]
    up, down = up_ref[:count], down_ref[:count]
    row = lax.broadcasted_iota(jnp.int32, up.shape, 0)
    return jnp.where(row % 8 < 4, up, down)


def step_kernel(*refs, step, last, extra, last_place, pair, y_elems, z_elems):
    cur_ref, fol_ref, minv_ref, base_ref, touch_ref, material_ref, even_ref, odd_ref = refs[:8]
    refs = list(refs[8:])
    up_ref = refs.pop(0)
    down_ref = None if pair else refs.pop(0)
    first_up_ref, own_ref, first_own_ref, far_ref, edge_ref = refs[:5]
    refs = refs[5 + extra :]
    if last:
        back_ref, out_ref, scratch = refs
    else:
        new_ref, even_out, odd_out, fault_out = refs
    place = lax.axis_index("dom")
    lanes = cur_ref.shape[1]
    even = place % 2 == 0
    far = jnp.where(place == last_place, 0.0, jnp.where(even, even_ref[...], odd_ref[...]))
    left = jnp.where(place == 0, 0.0, jnp.where(even, odd_ref[...], even_ref[...]))
    lane_wide = lax.broadcasted_iota(jnp.int32, (BLOCK, lanes), 1)
    below = jnp.where(
        lane_wide % z_elems != z_elems - 1, pltpu.roll(far[:BLOCK], lanes - 1, 1), 0.0
    )
    far = stacked(jnp.concatenate([far, below], axis=0))
    lame_row, shear_row = material_ref[0:1], material_ref[1:2]
    left_lame = left[BLOCK - 1 : BLOCK]
    left_shear = left[2 * BLOCK - 1 : 2 * BLOCK]
    from_left = left_lame * touch_ref[:PLANE] + left_shear * touch_ref[PLANE:]
    row, lane = block_iotas(lanes)
    across = lane // z_elems
    shared = row < 3
    add_first = jnp.logical_and(shared, across > 0)
    take_last = jnp.logical_and(shared, across < y_elems - 1)
    pull_first = jnp.logical_and(shared, across == 0)
    pull_last = jnp.logical_and(shared, across == y_elems - 1)
    above = above_lanes(lanes, z_elems)
    fault_in = fault_input(up_ref, down_ref, 32)
    planes = []
    edge = 0.0
    for x in range(4):
        rows = slice(x * PLANE, (x + 1) * PLANE)
        result = dot(far_ref[x], far)
        force = base_ref[rows] + (lame_row * result[:PLANE] + shear_row * result[PLANE:])
        blocks = [force[zl * BLOCK : (zl + 1) * BLOCK] for zl in range(5)]
        if x == 0:
            blocks = [b + from_left[i * BLOCK : (i + 1) * BLOCK] for i, b in enumerate(blocks)]
            blocks[:4] = [b + left[i * BLOCK : (i + 1) * BLOCK] for i, b in enumerate(blocks[:4])]
        blocks[0], blocks[4] = (
            blocks[0] + jnp.where(above, pltpu.roll(blocks[4], 1, 1), 0.0),
            blocks[4] + pltpu.roll(blocks[0], lanes - 1, 1),
        )
        at, k = slice(8 * x, 8 * x + 8), slice(32 + 4 * step + x, 33 + 4 * step + x)
        stiff = jnp.where(
            jnp.logical_or(row == 1, row == 5),
            lock_stiffness,
            jnp.where(row < 4, first_up_ref[k], first_own_ref[k]),
        )
        pulled = stiff * (fault_in[at] - pltpu.roll(own_ref[at], 4, 0))
        pulled_last = pltpu.roll(pulled, 4, 0)
        for zl in range(5):
            low, high = blocks[zl][:8], blocks[zl][8:]
            move = zl * z_elems if zl < 4 else 1
            blocks[zl] = jnp.concatenate(
                [
                    low
                    + jnp.where(add_first, shifted(high, z_elems), 0.0)
                    - jnp.where(pull_first, shifted(pulled, -move), 0.0),
                    high
                    + jnp.where(take_last, shifted(low, -z_elems), 0.0)
                    - jnp.where(pull_last, shifted(pulled_last, -move - z_elems), 0.0),
                ],
                axis=0,
            )
        plane = (2.0 * cur_ref[rows] - fol_ref[rows]) - minv_ref[rows] * jnp.concatenate(
            blocks, axis=0
        )
        if last:
            planes.append(plane)
        else:
            new_ref[rows] = plane
            fault_out[at] = fault_message(plane, z_elems)
            edge = edge + dot(edge_ref[x], stacked(plane))
            if x == 0:
                first = plane[: 4 * BLOCK]
    if last:
        from_elements(jnp.concatenate(planes, axis=0), scratch, back_ref, out_ref, y_elems)
    else:
        right = edge_message(edge, lame_row, shear_row, z_elems)
        even_out[...], odd_out[...] = select_messages(place % 2, first, right)


def mask_kernel(owner_ref, _, mask_ref):
    shape = (PATCH_ROWS, mask_ref.shape[1])
    first = (lax.axis_index("dom") - REACH) * PATCH_DEV
    number = lax.broadcasted_iota(jnp.int32, shape, 0) + first
    for x in range(4):
        mask = jnp.where(number == owner_ref[0, x], 1.0, 0.0)
        mask_ref[PATCH_ROWS * x : PATCH_ROWS * (x + 1)] = mask


def output_kernel(*refs, pair, steps, y_elems, z_elems):
    field_ref, back_ref, weight_ref = refs[:3]
    out_ref, grad_ref, table_ref, scratch = refs[-4:]
    messages = refs[3:-4]
    count = 2 if pair else 3
    grads = [jnp.zeros((8, weight_ref.shape[1]), jnp.float32) for _ in range(4)]
    for i in range(steps):
        group = messages[count * i : count * (i + 1)]
        slip = -swap_rows(group[0][:32])
        if i < steps - 1:
            slip = slip + fault_input(group[1], None if pair else group[2], 32)
        for x in range(4):
            grads[x] = grads[x] + slip[8 * x : 8 * x + 8] * weight_ref[4 * i + x : 4 * i + x + 1]
    grad_ref[...] = jnp.concatenate(grads, axis=0)
    table_ref[...] = fault_table_back(weight_ref.shape[1], z_elems)
    from_elements(field_ref[...], scratch, back_ref, out_ref, y_elems)


def patch_kernel(*refs, pair, steps):
    mask_ref, weight_ref, grad_ref, table_ref, _, _, _, up_ref = refs[:8]
    down_ref = None if pair else refs[8]
    home_out, out_a, out_b, out_c, out_d = refs[-5:]
    place = lax.axis_index("dom")
    slip = fault_input(up_ref, down_ref, 32)
    total = 0.0
    for x in range(4):
        at, k = 8 * x + 4, 4 * (steps - 1) + x
        grad = grad_ref[at : at + 1] + slip[at : at + 1] * weight_ref[k : k + 1]
        total = total + mask_ref[PATCH_ROWS * x : PATCH_ROWS * (x + 1)] * grad
    total = exact_dot(total, table_ref[...])
    rows = [total[2 * i : 2 * i + 2] for i in range(5)]
    home_out[...] = rows[2]
    even = place % 2 == 0
    out_a[...] = jnp.where(even, rows[3], rows[1])
    out_b[...] = jnp.where(even, rows[1], rows[3])
    low = place % 4 < 2
    out_c[...] = jnp.where(low, rows[4], rows[0])
    out_d[...] = jnp.where(low, rows[0], rows[4])


VMEM = pl.BlockSpec(memory_space=pltpu.VMEM)
HBM = pl.BlockSpec(memory_space=pltpu.HBM)
SMEM = pl.BlockSpec(memory_space=pltpu.SMEM)
ANY = pl.BlockSpec(memory_space=pl.ANY)


def kernel_call(body, outs, args, in_smem=(), scratch=(), in_hbm=(), kept=(), unread=(), **static):
    shapes = []
    for out in outs:
        shape, dtype = out if isinstance(out[0], tuple) else (out, jnp.float32)
        shapes.append((pltpu.VMEM if in_hbm else jax.ShapeDtypeStruct)(shape, dtype))
    specs = [VMEM] * len(args)
    for places, spec in ((in_smem, SMEM), (in_hbm, HBM), (unread, ANY)):
        for i in places:
            specs[i] = spec
    copied = [pltpu.VMEM(args[i].shape, args[i].dtype) for i in in_hbm if i not in kept]
    if in_hbm:
        copied.append(pltpu.SemaphoreType.DMA((len(in_hbm),)))
    return pl.pallas_call(
        functools.partial(body, **static) if static else body,
        out_shape=shapes,
        in_specs=specs,
        out_specs=[VMEM] * len(shapes),
        scratch_shapes=list(scratch) + copied,
        compiler_params=pltpu.CompilerParams(
            vmem_limit_bytes=(56 if in_hbm else 24) * 2**20
        ),
    )(*args)


def swapped(block, distance, group):
    size, across = lax.axis_size("dom"), lax.axis_size("depth")
    partner = {}
    for left in range(size - distance):
        if left // distance % 2 == group:
            partner[left], partner[left + distance] = left + distance, left
    route = []
    for i in range(size):
        for j in range(across):
            side = j if i in partner else min(j ^ 1, across - 1)
            route.append((i * across + j, partner.get(i, i) * across + side))
    return lax.ppermute(block, ("dom", "depth"), route)


def from_behind(block, axis, distance):
    size = lax.axis_size(axis)
    return lax.ppermute(block, axis, [((i - distance) % size, i) for i in range(size)])


def on_device(
    adjoint_now,
    adjoint_next,
    lame_first,
    shear_modulus,
    density,
    branch_flags,
    weak_slope,
    normal_stress,
    patch_owner,
):
    x_elems, y_elems, z_elems = lame_first.shape
    lanes = y_elems * z_elems
    assert x_elems == 1 and lanes == adjoint_now.shape[3]
    steps = branch_flags.shape[0]
    pair = lax.axis_size("depth") == 2
    own_table, far_table, edge_table, touch_table = (jnp.asarray(t) for t in stiffness_tables())
    back = jnp.asarray(back_table(y_elems, z_elems))
    mass = jnp.asarray(mass_table(y_elems, z_elems))
    now = jnp.transpose(adjoint_now, (0, 2, 1, 3))
    following = jnp.transpose(adjoint_next, (0, 2, 1, 3))
    rho = jnp.transpose(density, (1, 0, 2))
    flags = branch_flags[:, 0]
    native = pltpu.VMEM((y_elems, 4 * BLOCK, lanes), jnp.float32)
    field = (4 * PLANE, lanes)
    plane = (4 * BLOCK, lanes)

    def exchange(even, odd, fault_rows):
        if pair:
            faults = [from_behind(fault_rows, "depth", 1)]
        else:
            faults = [from_behind(fault_rows, "depth", 1), from_behind(fault_rows, "depth", -1)]
        return swapped(even, 1, 0), swapped(odd, 1, 1), faults

    tables = (edge_table, own_table, far_table, touch_table)
    cur, even, odd, fault_rows, material, edge_table, own_table, far_table, touch_table = kernel_call(
        first_kernel,
        [field, plane, plane, (32 + 4 * steps, lanes), (8, lanes)]
        + [(t.shape, t.dtype) for t in tables],
        (now, flags, weak_slope[0], lame_first[0], shear_modulus[0]) + tables,
        scratch=[native],
        in_hbm=range(9),
        kept=range(5, 9),
    )
    first_fault = fault_rows
    even_in, odd_in, fault_in = exchange(even, odd, fault_rows)
    first_in = fault_in
    fol, minv, weight = kernel_call(
        setup_kernel,
        [field, field, (4 * steps, lanes)],
        (following, rho, flags, normal_stress[0], mass),
        scratch=[native],
        in_hbm=range(5),
        y_elems=y_elems,
        z_elems=z_elems,
    )
    seen = []
    for step in range(steps):
        last = step == steps - 1
        seen += [fault_rows] + fault_in
        base, touch = kernel_call(
            prepare_kernel,
            [field, (2 * PLANE, lanes)],
            [cur, material, own_table, touch_table],
            (),
        )
        args = [cur, fol, minv, base, touch, material, even_in, odd_in] + fault_in
        args += [first_in[0], fault_rows, first_fault, far_table, edge_table]
        static = dict(
            step=step, last=last, extra=1 if last or step == 1 else 0, last_place=lax.axis_size("dom") - 1, pair=pair, y_elems=y_elems,
            z_elems=z_elems,
        )
        if step == 1:
            mask = kernel_call(mask_kernel, [(4 * PATCH_ROWS, lanes)], [patch_owner, cur], (0,), unread=(1,))[0]
            args.append(mask)
        if not last:
            new, even, odd, new_fault = kernel_call(
                step_kernel,
                [field, plane, plane, (32, lanes)],
                args,
                unread=(len(args) - 1,) if step == 1 else (),
                **static,
            )
            fol, cur, fault_rows = cur, new, new_fault
            even_in, odd_in, fault_in = exchange(even, odd, fault_rows)
        else:
            whole = (3, 4 * y_elems + 1, 4, lanes)
            known = seen[: len(seen) - len(fault_in)]
            later, grad, table = kernel_call(
                output_kernel,
                [whole, (32, lanes), ((lanes, lanes), jnp.bfloat16)],
                [cur, back, weight] + known,
                (),
                [native],
                pair=pair,
                steps=steps,
                y_elems=y_elems,
                z_elems=z_elems,
            )
            sums = kernel_call(
                patch_kernel,
                [(PATCH_DEV, lanes)] * 5,
                [mask, weight, grad, table, even_in, odd_in, touch] + fault_in,
                unread=(4, 5, 6),
                pair=pair,
                steps=steps,
            )
            patch_sums = sums[0]
            for i, distance, group in ((2, 1, 1), (4, 2, 1), (3, 2, 0), (1, 1, 0)):
                patch_sums = patch_sums + swapped(sums[i], distance, group)
            earlier = kernel_call(
                step_kernel,
                [whole],
                args + [sums[0], back],
                scratch=[native],
                unread=(len(args),),
                **static,
            )[0]
    return (
        jnp.transpose(earlier, (0, 2, 1, 3)),
        jnp.transpose(later, (0, 2, 1, 3)),
        patch_sums[None],
    )


def solution(mesh):
    return jax.shard_map(
        on_device,
        mesh=mesh,
        in_specs=(
            P(None, "dom", "depth", None),
            P(None, "dom", "depth", None),
            P("dom", "depth", None),
            P("dom", "depth", None),
            P("dom", "depth", None),
            P(None, "depth", "dom", None),
            P("depth", "dom", None),
            P("depth", "dom", None),
            P("depth", "dom"),
        ),
        out_specs=(
            P(None, "dom", "depth", None),
            P(None, "dom", "depth", None),
            P("depth", "dom", None),
        ),
        check_vma=False,
    )
```

```python
import functools
import math

import jax
import jax.numpy as jnp
import ml_dtypes
import numpy as np
from jax import lax
from jax.experimental import pallas as pl
from jax.experimental.pallas import tpu as pltpu
from jax.sharding import PartitionSpec as P

PATCH_DEV = 2
REACH = 2
PATCH_ROWS = 16

time_step = 0.01
lock_stiffness = 0.5

BLOCK = 16
ROWS = ((0, 1, 2), (3, 4, 5), (11, 12, 13), (6, 7, 14), (8, 9, 10))
PLANE = 5 * BLOCK


def basis_tables():
    points = [-1.0, -math.sqrt(3.0 / 7.0), 0.0, math.sqrt(3.0 / 7.0), 1.0]
    quad_weights = np.array([0.1, 49.0 / 90.0, 32.0 / 45.0, 49.0 / 90.0, 0.1])
    products = []
    for first in range(5):
        value = 1.0
        for other in range(5):
            if other != first:
                value = value * (points[first] - points[other])
        products.append(value)
    derivative = np.zeros((5, 5))
    for row in range(5):
        for column in range(5):
            if row == column:
                total = 0.0
                for other in range(5):
                    if other != row:
                        total = total + 1.0 / (points[row] - points[other])
                derivative[row, column] = total
            else:
                derivative[row, column] = (
                    products[row] / products[column] / (points[row] - points[column])
                )
    return (quad_weights, derivative)


def two_parts(table):
    high = table.astype(ml_dtypes.bfloat16)
    low = (table - high.astype(np.float64)).astype(ml_dtypes.bfloat16)
    return np.stack([high, low])


def element_stiffness():
    weights, derivative = basis_tables()
    eye = np.eye(5)
    slope = 2.0 * derivative
    grads = [
        np.kron(slope, np.kron(eye, eye)),
        np.kron(eye, np.kron(eye, slope)),
        np.kron(eye, np.kron(slope, eye)),
    ]
    quad = np.kron(weights, np.kron(weights, weights)) / 8.0
    first = np.zeros((125, 3, 125, 3))
    second = np.zeros((125, 3, 125, 3))
    lap = sum(g.T @ (quad[:, None] * g) for g in grads)
    for c in range(3):
        second[:, c, :, c] += lap
        for d in range(3):
            first[:, c, :, d] += grads[c].T @ (quad[:, None] * grads[d])
            second[:, c, :, d] += grads[d].T @ (quad[:, None] * grads[c])
    where = [
        node // 5 * BLOCK + ROWS[node % 5][c] for node in range(125) for c in range(3)
    ]
    wide = []
    for small in (first, second):
        big = np.zeros((5 * PLANE, 5 * PLANE))
        big[np.ix_(where, where)] = small.reshape(375, 375)
        wide.append(big)
    return wide


OWN_COLS = 384


def padded_table(table, columns):
    return np.pad(table, ((0, 0), (0, columns - table.shape[1])))


@functools.cache
def stiffness_tables():
    wide = element_stiffness()
    own = 4 * PLANE
    planes = [slice(x * PLANE, (x + 1) * PLANE) for x in range(5)]
    inner = np.concatenate([w[:own, :own] for w in wide])

    def three(rows, columns):
        high, low = two_parts(np.concatenate([w[rows, columns] for w in wide]))
        return padded_table(np.concatenate([high, low, high], axis=1), 256)

    return (
        two_parts(padded_table(inner, OWN_COLS)),
        np.stack([three(planes[x], planes[4]) for x in range(4)]),
        np.stack([three(planes[4], planes[x]) for x in range(4)]),
        three(planes[4], planes[4]),
    )


@functools.cache
def back_table(y_elems, z_elems):
    lanes = y_elems * z_elems
    depth = 4 * z_elems
    back = np.zeros((4 * lanes, y_elems * depth), ml_dtypes.bfloat16)
    for yel in range(y_elems):
        for k in range(z_elems):
            for zl in range(4):
                back[zl * lanes + yel * z_elems + k, yel * depth + 4 * k + zl] = 1
    return back


@functools.cache
def mass_table(y_elems, z_elems):
    weights, _ = basis_tables()
    table = np.zeros((4, 5, BLOCK, y_elems, z_elems))
    for x in range(4):
        mx = 0.2 if x == 0 else weights[x]
        for zl in range(5):
            for yl in range(5):
                for yel in range(y_elems):
                    my = weights[yl]
                    if (yl == 0 and yel > 0) or (yl == 4 and yel < y_elems - 1):
                        my = 0.2
                    mz = np.full(z_elems, weights[zl])
                    if zl == 0:
                        mz[1:] = 0.2
                    if zl == 4:
                        mz[:] = 0.2
                    value = time_step * time_step * 8.0 / (mx * my * mz)
                    if zl == 4:
                        value[-1] = 0.0
                    table[x, zl, list(ROWS[yl]), yel] = value
    return table.reshape(4 * PLANE, y_elems * z_elems).astype(np.float32)


def pieces(value, count):
    out = []
    for _ in range(count):
        piece = value.astype(jnp.bfloat16)
        out.append(piece)
        value = value - piece.astype(jnp.float32)
    return out


def dot(a, b):
    return jnp.dot(a, b, preferred_element_type=jnp.float32)


def exact_dot(value, table, count=3):
    rows = value.shape[0]
    result = dot(jnp.concatenate(pieces(value, count), axis=0), table)
    total = result[:rows]
    for i in range(1, count):
        total = total + result[i * rows : (i + 1) * rows]
    return total


def split_dot(table_high, table_low, value):
    lanes = value.shape[1]
    high, low = pieces(value, 2)
    wide = dot(table_high, jnp.concatenate([high, low], axis=1))
    return wide[:, :lanes] + (wide[:, lanes:] + dot(table_low, high))


def ones_where(rule, shape):
    row = lax.broadcasted_iota(jnp.int32, shape, 0)
    column = lax.broadcasted_iota(jnp.int32, shape, 1)
    return jnp.where(rule(row, column), 1.0, 0.0).astype(jnp.bfloat16)


def gather_table(lanes, z_elems):
    return ones_where(lambda z, c: z == 4 * (c % z_elems) + c // lanes, (lanes, 5 * lanes))


def fault_table(lanes, z_elems):
    return ones_where(lambda z, c: z == 4 * (c % z_elems) + c // z_elems, (lanes, lanes))


def fault_table_back(lanes, z_elems):
    return ones_where(lambda c, z: z == 4 * (c % z_elems) + c // z_elems, (lanes, lanes))


def stacked(value):
    high, low = pieces(value, 2)
    gap = jnp.zeros((256 - 3 * value.shape[0], value.shape[1]), jnp.bfloat16)
    return jnp.concatenate([high, high, low, gap], axis=0)


def to_elements(native, scratch, table, y_elems, parts=3):
    group = 4 * BLOCK
    scratch[...] = jnp.zeros_like(scratch)
    for c in range(3):
        for y in range(4 * y_elems + 1):
            rows = native(c, y)
            if y < 4 * y_elems:
                scratch[y // 4, pl.ds(ROWS[y % 4][c], 4, stride=BLOCK), :] = rows
            if y % 4 == 0 and y > 0:
                scratch[y // 4 - 1, pl.ds(ROWS[4][c], 4, stride=BLOCK), :] = rows
    high, middle, *low = pieces(
        jnp.concatenate([scratch[i] for i in range(y_elems)], axis=0), parts
    )
    result = dot(
        jnp.concatenate([high, middle], axis=1), jnp.concatenate([table, table], axis=0)
    )
    for piece in low:
        result = result + dot(piece, table)
    lanes = result.shape[1] // 5
    across = lax.broadcasted_iota(jnp.int32, (group, result.shape[1]), 1) % lanes // (
        lanes // y_elems
    )
    total = result[:group]
    for yel in range(1, y_elems):
        total = jnp.where(across == yel, result[yel * group : (yel + 1) * group], total)
    blocks = []
    for x in range(4):
        for zl in range(5):
            blocks.append(total[x * BLOCK : (x + 1) * BLOCK, zl * lanes : (zl + 1) * lanes])
    return jnp.concatenate(blocks, axis=0)


def from_elements(field, scratch, back_ref, out_ref, y_elems):
    rows = []
    for x in range(4):
        rows.append(
            jnp.concatenate(
                [field[x * PLANE + zl * BLOCK : x * PLANE + (zl + 1) * BLOCK] for zl in range(4)],
                axis=1,
            )
        )
    result = exact_dot(jnp.concatenate(rows, axis=0), back_ref[...])
    depth = result.shape[1] // y_elems
    for yel in range(y_elems):
        scratch[yel] = result[:, yel * depth : (yel + 1) * depth]
    for c in range(3):
        for y in range(4 * y_elems + 1):
            yel, yl = (y // 4, y % 4) if y < 4 * y_elems else (y_elems - 1, 4)
            out_ref[c, y] = scratch[yel, pl.ds(ROWS[yl][c], 4, stride=BLOCK), :]


def shifted(rows, lanes):
    lanes = lanes % rows.shape[1]
    return pltpu.roll(rows, lanes, 1) if lanes else rows


def block_iotas(lanes):
    return (
        lax.broadcasted_iota(jnp.int32, (8, lanes), 0),
        lax.broadcasted_iota(jnp.int32, (8, lanes), 1),
    )


def fault_message(plane, z_elems):
    lanes = plane.shape[1]
    row, lane = block_iotas(lanes)
    first = last = jnp.zeros((8, lanes), jnp.float32)
    for zl in range(4):
        at = zl * BLOCK
        here = lane // z_elems == zl
        first = jnp.where(here, shifted(plane[at : at + 8], zl * z_elems), first)
        last = jnp.where(here, shifted(plane[at + 8 : at + 16], (zl + 1) * z_elems), last)
    return jnp.where(row < 4, last, pltpu.roll(first, 4, 0))


def swap_rows(message):
    parts = [pltpu.roll(message[i : i + 8], 4, 0) for i in range(0, message.shape[0], 8)]
    return jnp.concatenate(parts, axis=0)


def select_messages(parity, left, right):
    even = parity == 0
    return jnp.where(even, right, left), jnp.where(even, left, right)


def material_rows(lame_ref, shear_ref):
    y_elems, z_elems = lame_ref.shape
    both = jnp.concatenate([lame_ref[...], shear_ref[...]], axis=0)
    spread = ones_where(lambda k, c: c % z_elems == k, (z_elems, y_elems * z_elems))
    tiled = exact_dot(both, spread)
    row = lax.broadcasted_iota(jnp.int32, tiled.shape, 0)
    lane = lax.broadcasted_iota(jnp.int32, tiled.shape, 1)
    kept = jnp.where(row % y_elems == lane // z_elems, tiled, 0.0)
    return (
        jnp.sum(kept[:y_elems], axis=0, keepdims=True),
        jnp.sum(kept[y_elems:], axis=0, keepdims=True),
    )


def above_lanes(lanes, z_elems):
    return lax.broadcasted_iota(jnp.int32, (BLOCK, lanes), 1) % z_elems != 0


def edge_message(result, lame_row, shear_row, z_elems):
    lanes = result.shape[1]
    force = lame_row * result[:PLANE] + shear_row * result[PLANE:]
    top = force[:BLOCK] + jnp.where(
        above_lanes(lanes, z_elems), pltpu.roll(force[4 * BLOCK :], 1, 1), 0.0
    )
    row = lax.broadcasted_iota(jnp.int32, top.shape, 0)
    top = jnp.where(row == BLOCK - 1, lame_row, top)
    second = jnp.where(row == BLOCK - 1, shear_row, force[BLOCK : 2 * BLOCK])
    return jnp.concatenate([top, second, force[2 * BLOCK : 4 * BLOCK]], axis=0)


def own_force(own_ref, cur, lame_row, shear_row):
    rows, lanes = cur.shape
    padded = jnp.concatenate([cur, jnp.zeros((OWN_COLS - rows, lanes), jnp.float32)], axis=0)
    result = split_dot(own_ref[0], own_ref[1], padded)
    return lame_row * result[:rows] + shear_row * result[rows:]


def start_copies(pairs, sems):
    copies = [
        pltpu.make_async_copy(source, target, sems.at[i])
        for i, (source, target) in enumerate(pairs)
    ]
    for copy in copies:
        copy.start()
    return copies


def first_kernel(
    now_hbm,
    flags_hbm,
    weak_hbm,
    lame_hbm,
    shear_hbm,
    edge_hbm,
    own_hbm,
    far_hbm,
    touch_hbm,
    cur_ref,
    even_ref,
    even_rest,
    odd_ref,
    fault_out_ref,
    material_ref,
    edge_ref,
    own_ref,
    far_ref,
    touch_ref,
    scratch,
    now_ref,
    flags_ref,
    weak_ref,
    lame_ref,
    shear_ref,
    sems,
):
    copies = start_copies(
        [
            (now_hbm, now_ref),
            (flags_hbm, flags_ref),
            (weak_hbm, weak_ref),
            (lame_hbm, lame_ref),
            (shear_hbm, shear_ref),
            (edge_hbm, edge_ref),
            (own_hbm, own_ref),
            (far_hbm, far_ref),
            (touch_hbm, touch_ref),
        ],
        sems,
    )
    y_elems, z_elems = lame_ref.shape
    lanes = y_elems * z_elems
    parity = lax.axis_index("dom") % 2
    gather = gather_table(lanes, z_elems)
    fault = fault_table(lanes, z_elems)
    copies[1].wait()
    copies[2].wait()
    weak = weak_ref[...]
    tangent = []
    for i in range(flags_ref.shape[0]):
        flag = flags_ref[i]
        tangent.append(
            jnp.where(flag == 0, lock_stiffness, jnp.where(flag == 1, -weak, 0.0))
        )
    fault_out_ref[32:] = exact_dot(jnp.concatenate(tangent, axis=0), fault)
    copies[3].wait()
    copies[4].wait()
    lame_row, shear_row = material_rows(lame_ref, shear_ref)
    material_ref[...] = jnp.concatenate(
        [lame_row, shear_row, jnp.zeros((6, lanes), jnp.float32)], axis=0
    )
    copies[0].wait()
    cur = to_elements(lambda c, y: now_ref[c, y], scratch, gather, y_elems)
    copies[5].wait()
    planes = [cur[x * PLANE : (x + 1) * PLANE] for x in range(4)]
    edge = sum(dot(edge_ref[x], stacked(planes[x])) for x in range(4))
    right = edge_message(edge, lame_row, shear_row, z_elems)
    message, odd_ref[...] = select_messages(parity, cur[: 4 * BLOCK], right)
    even_ref[...], even_rest[...] = message[: 2 * BLOCK], message[2 * BLOCK :]
    cur_ref[...] = cur
    for x in range(4):
        fault_out_ref[8 * x : 8 * x + 8] = fault_message(planes[x], z_elems)
    for copy in copies[6:]:
        copy.wait()


def prepare_kernel(cur_ref, material_ref, own_ref, touch_ref, base_ref, edge_part_ref):
    cur = cur_ref[...]
    base_ref[...] = own_force(own_ref, cur, material_ref[0:1], material_ref[1:2])
    edge_part_ref[...] = dot(touch_ref[...], stacked(cur[:PLANE]))


def setup_kernel(
    next_hbm,
    density_hbm,
    flags_hbm,
    stress_hbm,
    mass_hbm,
    fol_ref,
    minv_ref,
    weight_ref,
    scratch,
    next_ref,
    density_ref,
    flags_ref,
    stress_ref,
    mass_ref,
    sems,
    *,
    y_elems,
    z_elems,
):
    copies = start_copies(
        [
            (next_hbm, next_ref),
            (density_hbm, density_ref),
            (flags_hbm, flags_ref),
            (stress_hbm, stress_ref),
            (mass_hbm, mass_ref),
        ],
        sems,
    )
    gather = gather_table(y_elems * z_elems, z_elems)
    fault = fault_table(y_elems * z_elems, z_elems)
    for copy in copies[:5]:
        copy.wait()
    fol_ref[...] = to_elements(lambda c, y: next_ref[c, y], scratch, gather, y_elems)
    density = to_elements(lambda c, y: density_ref[y], scratch, gather, y_elems, 2)
    table = mass_ref[...]
    first = lax.axis_index("dom") == 0
    plane = lax.broadcasted_iota(jnp.int32, table.shape, 0) < PLANE
    table = jnp.where(jnp.logical_and(first, plane), 2.0 * table, table)
    minv_ref[...] = jnp.where(table > 0.0, table / jnp.where(table > 0.0, density, 1.0), 0.0)
    stress = stress_ref[...]
    weights = []
    for i in range(flags_ref.shape[0]):
        flag = flags_ref[i]
        weights.append(
            stress * jnp.where(flag == 1, 0.5, jnp.where(flag == 2, 1.0, 0.0))
        )
    weight_ref[...] = exact_dot(jnp.concatenate(weights, axis=0), fault)


def fault_input(up_ref, down_ref, count):
    if down_ref is None:
        return up_ref[:count]
    up, down = up_ref[:count], down_ref[:count]
    row = lax.broadcasted_iota(jnp.int32, up.shape, 0)
    return jnp.where(row % 8 < 4, up, down)


def step_kernel(*refs, step, last, extra, last_place, pair, y_elems, z_elems):
    cur_ref, fol_ref, minv_ref, base_ref, touch_ref, material_ref, odd_ref, up_ref = refs[:8]
    refs = list(refs[8:])
    down_ref = None if pair else refs.pop(0)
    even_in = jnp.concatenate([refs.pop(0)[...], refs.pop(0)[...]], axis=0)
    first_up_ref, own_ref, first_own_ref, far_ref, edge_ref = refs[:5]
    refs = refs[5 + extra :]
    if last:
        back_ref, out_ref, scratch = refs
    else:
        new_ref, even_out, even_rest, odd_out, fault_out = refs
    place = lax.axis_index("dom")
    lanes = cur_ref.shape[1]
    even = place % 2 == 0
    far = jnp.where(place == last_place, 0.0, jnp.where(even, even_in, odd_ref[...]))
    left = jnp.where(place == 0, 0.0, jnp.where(even, odd_ref[...], even_in))
    lane_wide = lax.broadcasted_iota(jnp.int32, (BLOCK, lanes), 1)
    below = jnp.where(
        lane_wide % z_elems != z_elems - 1, pltpu.roll(far[:BLOCK], lanes - 1, 1), 0.0
    )
    far = stacked(jnp.concatenate([far, below], axis=0))
    lame_row, shear_row = material_ref[0:1], material_ref[1:2]
    left_lame = left[BLOCK - 1 : BLOCK]
    left_shear = left[2 * BLOCK - 1 : 2 * BLOCK]
    from_left = left_lame * touch_ref[:PLANE] + left_shear * touch_ref[PLANE:]
    row, lane = block_iotas(lanes)
    across = lane // z_elems
    shared = row < 3
    add_first = jnp.logical_and(shared, across > 0)
    take_last = jnp.logical_and(shared, across < y_elems - 1)
    pull_first = jnp.logical_and(shared, across == 0)
    pull_last = jnp.logical_and(shared, across == y_elems - 1)
    above = above_lanes(lanes, z_elems)
    fault_in = fault_input(up_ref, down_ref, 32)
    planes = []
    edge = 0.0
    for x in range(4):
        rows = slice(x * PLANE, (x + 1) * PLANE)
        result = dot(far_ref[x], far)
        force = base_ref[rows] + (lame_row * result[:PLANE] + shear_row * result[PLANE:])
        blocks = [force[zl * BLOCK : (zl + 1) * BLOCK] for zl in range(5)]
        if x == 0:
            blocks = [b + from_left[i * BLOCK : (i + 1) * BLOCK] for i, b in enumerate(blocks)]
            blocks[:4] = [b + left[i * BLOCK : (i + 1) * BLOCK] for i, b in enumerate(blocks[:4])]
        blocks[0], blocks[4] = (
            blocks[0] + jnp.where(above, pltpu.roll(blocks[4], 1, 1), 0.0),
            blocks[4] + pltpu.roll(blocks[0], lanes - 1, 1),
        )
        at, k = slice(8 * x, 8 * x + 8), slice(32 + 4 * step + x, 33 + 4 * step + x)
        stiff = jnp.where(
            jnp.logical_or(row == 1, row == 5),
            lock_stiffness,
            jnp.where(row < 4, first_up_ref[k], first_own_ref[k]),
        )
        pulled = stiff * (fault_in[at] - pltpu.roll(own_ref[at], 4, 0))
        pulled_last = pltpu.roll(pulled, 4, 0)
        for zl in range(5):
            low, high = blocks[zl][:8], blocks[zl][8:]
            move = zl * z_elems if zl < 4 else 1
            blocks[zl] = jnp.concatenate(
                [
                    low
                    + jnp.where(add_first, shifted(high, z_elems), 0.0)
                    - jnp.where(pull_first, shifted(pulled, -move), 0.0),
                    high
                    + jnp.where(take_last, shifted(low, -z_elems), 0.0)
                    - jnp.where(pull_last, shifted(pulled_last, -move - z_elems), 0.0),
                ],
                axis=0,
            )
        plane = (2.0 * cur_ref[rows] - fol_ref[rows]) - minv_ref[rows] * jnp.concatenate(
            blocks, axis=0
        )
        if last:
            planes.append(plane)
        else:
            new_ref[rows] = plane
            fault_out[at] = fault_message(plane, z_elems)
            edge = edge + dot(edge_ref[x], stacked(plane))
            if x == 0:
                first = plane[: 4 * BLOCK]
    if last:
        from_elements(jnp.concatenate(planes, axis=0), scratch, back_ref, out_ref, y_elems)
    else:
        right = edge_message(edge, lame_row, shear_row, z_elems)
        message, odd_out[...] = select_messages(place % 2, first, right)
        even_out[...], even_rest[...] = message[: 2 * BLOCK], message[2 * BLOCK :]


def mask_kernel(owner_ref, _, back_ref, mask_ref):
    shape = (PATCH_ROWS, mask_ref.shape[1])
    first = (lax.axis_index("dom") - REACH) * PATCH_DEV
    number = lax.broadcasted_iota(jnp.int32, shape, 0) + first
    for x in range(4):
        mask = jnp.where(number == owner_ref[0, x], 1.0, 0.0)
        mask_ref[PATCH_ROWS * x : PATCH_ROWS * (x + 1)] = mask


def output_kernel(*refs, pair, steps, y_elems, z_elems):
    field_ref, back_ref, weight_ref = refs[:3]
    out_ref, grad_ref, table_ref, scratch = refs[-4:]
    messages = refs[3:-4]
    count = 2 if pair else 3
    grads = [jnp.zeros((8, weight_ref.shape[1]), jnp.float32) for _ in range(4)]
    for i in range(steps):
        group = messages[count * i : count * (i + 1)]
        slip = -swap_rows(group[0][:32])
        if i < steps - 1:
            slip = slip + fault_input(group[1], None if pair else group[2], 32)
        for x in range(4):
            grads[x] = grads[x] + slip[8 * x : 8 * x + 8] * weight_ref[4 * i + x : 4 * i + x + 1]
    grad_ref[...] = jnp.concatenate(grads, axis=0)
    table_ref[...] = fault_table_back(weight_ref.shape[1], z_elems)
    from_elements(field_ref[...], scratch, back_ref, out_ref, y_elems)


def patch_kernel(*refs, pair, steps):
    mask_ref, weight_ref, grad_ref, table_ref, _, up_ref = refs[:6]
    down_ref = None if pair else refs[6]
    home_out, out_a, out_b, out_c, out_d = refs[-5:]
    place = lax.axis_index("dom")
    slip = fault_input(up_ref, down_ref, 32)
    total = 0.0
    for x in range(4):
        at, k = 8 * x + 4, 4 * (steps - 1) + x
        grad = grad_ref[at : at + 1] + slip[at : at + 1] * weight_ref[k : k + 1]
        total = total + mask_ref[PATCH_ROWS * x : PATCH_ROWS * (x + 1)] * grad
    total = exact_dot(total, table_ref[...])
    rows = [total[2 * i : 2 * i + 2] for i in range(5)]
    home_out[...] = rows[2]
    even = place % 2 == 0
    out_a[...] = jnp.where(even, rows[3], rows[1])
    out_b[...] = jnp.where(even, rows[1], rows[3])
    low = place % 4 < 2
    out_c[...] = jnp.where(low, rows[4], rows[0])
    out_d[...] = jnp.where(low, rows[0], rows[4])


VMEM = pl.BlockSpec(memory_space=pltpu.VMEM)
HBM = pl.BlockSpec(memory_space=pltpu.HBM)
SMEM = pl.BlockSpec(memory_space=pltpu.SMEM)
ANY = pl.BlockSpec(memory_space=pl.ANY)


def kernel_call(body, outs, args, in_smem=(), scratch=(), in_hbm=(), kept=(), unread=(), **static):
    shapes = []
    for out in outs:
        shape, dtype = out if isinstance(out[0], tuple) else (out, jnp.float32)
        shapes.append((pltpu.VMEM if in_hbm else jax.ShapeDtypeStruct)(shape, dtype))
    specs = [VMEM] * len(args)
    for places, spec in ((in_smem, SMEM), (in_hbm, HBM), (unread, ANY)):
        for i in places:
            specs[i] = spec
    copied = [pltpu.VMEM(args[i].shape, args[i].dtype) for i in in_hbm if i not in kept]
    if in_hbm:
        copied.append(pltpu.SemaphoreType.DMA((len(in_hbm),)))
    return pl.pallas_call(
        functools.partial(body, **static) if static else body,
        out_shape=shapes,
        in_specs=specs,
        out_specs=[VMEM] * len(shapes),
        scratch_shapes=list(scratch) + copied,
        compiler_params=pltpu.CompilerParams(
            vmem_limit_bytes=(56 if in_hbm else 24) * 2**20
        ),
    )(*args)


def swapped(block, distance, group):
    size, across = lax.axis_size("dom"), lax.axis_size("depth")
    partner = {}
    for left in range(size - distance):
        if left // distance % 2 == group:
            partner[left], partner[left + distance] = left + distance, left
    route = []
    for i in range(size):
        for j in range(across):
            side = j if i in partner else min(j ^ 1, across - 1)
            route.append((i * across + j, partner.get(i, i) * across + side))
    return lax.ppermute(block, ("dom", "depth"), route)


def from_behind(block, axis, distance):
    size = lax.axis_size(axis)
    return lax.ppermute(block, axis, [((i - distance) % size, i) for i in range(size)])


def on_device(
    adjoint_now,
    adjoint_next,
    lame_first,
    shear_modulus,
    density,
    branch_flags,
    weak_slope,
    normal_stress,
    patch_owner,
):
    x_elems, y_elems, z_elems = lame_first.shape
    lanes = y_elems * z_elems
    assert x_elems == 1 and lanes == adjoint_now.shape[3]
    steps = branch_flags.shape[0]
    pair = lax.axis_size("depth") == 2
    own_table, far_table, edge_table, touch_table = (jnp.asarray(t) for t in stiffness_tables())
    back = jnp.asarray(back_table(y_elems, z_elems))
    mass = jnp.asarray(mass_table(y_elems, z_elems))
    now = jnp.transpose(adjoint_now, (0, 2, 1, 3))
    following = jnp.transpose(adjoint_next, (0, 2, 1, 3))
    rho = jnp.transpose(density, (1, 0, 2))
    flags = branch_flags[:, 0]
    native = pltpu.VMEM((y_elems, 4 * BLOCK, lanes), jnp.float32)
    field = (4 * PLANE, lanes)
    plane = (4 * BLOCK, lanes)
    half = (2 * BLOCK, lanes)

    def exchange(even, odd, fault_rows):
        if pair:
            faults = [from_behind(fault_rows, "depth", 1)]
        else:
            faults = [from_behind(fault_rows, "depth", 1), from_behind(fault_rows, "depth", -1)]
        return [swapped(part, 1, 0) for part in even], swapped(odd, 1, 1), faults

    tables = (edge_table, own_table, far_table, touch_table)
    cur, *even, odd, fault_rows, material, edge_table, own_table, far_table, touch_table = kernel_call(
        first_kernel,
        [field, half, half, plane, (32 + 4 * steps, lanes), (8, lanes)]
        + [(t.shape, t.dtype) for t in tables],
        (now, flags, weak_slope[0], lame_first[0], shear_modulus[0]) + tables,
        scratch=[native],
        in_hbm=range(9),
        kept=range(5, 9),
    )
    first_fault = fault_rows
    even_in, odd_in, fault_in = exchange(even, odd, fault_rows)
    first_in = fault_in
    fol, minv, weight = kernel_call(
        setup_kernel,
        [field, field, (4 * steps, lanes)],
        (following, rho, flags, normal_stress[0], mass),
        scratch=[native],
        in_hbm=range(5),
        y_elems=y_elems,
        z_elems=z_elems,
    )
    seen = []
    for step in range(steps):
        last = step == steps - 1
        seen += [fault_rows] + fault_in
        base, touch = kernel_call(
            prepare_kernel,
            [field, (2 * PLANE, lanes)],
            [cur, material, own_table, touch_table],
            (),
        )
        args = [cur, fol, minv, base, touch, material, odd_in] + fault_in + even_in
        args += [first_in[0], fault_rows, first_fault, far_table, edge_table]
        static = dict(
            step=step, last=last, extra=1 if last or step == 1 else 0, last_place=lax.axis_size("dom") - 1, pair=pair, y_elems=y_elems,
            z_elems=z_elems,
        )
        if step == 1:
            mask = kernel_call(
                mask_kernel, [(4 * PATCH_ROWS, lanes)], [patch_owner, cur, back], (0,), unread=(1,)
            )[0]
            args.append(mask)
        if not last:
            new, *even, odd, new_fault = kernel_call(
                step_kernel,
                [field, half, half, plane, (32, lanes)],
                args,
                unread=(len(args) - 1,) if step == 1 else (),
                **static,
            )
            fol, cur, fault_rows = cur, new, new_fault
            even_in, odd_in, fault_in = exchange(even, odd, fault_rows)
        else:
            whole = (3, 4 * y_elems + 1, 4, lanes)
            known = seen[: len(seen) - len(fault_in)]
            later, grad, table = kernel_call(
                output_kernel,
                [whole, (32, lanes), ((lanes, lanes), jnp.bfloat16)],
                [cur, back, weight] + known,
                (),
                [native],
                pair=pair,
                steps=steps,
                y_elems=y_elems,
                z_elems=z_elems,
            )
            sums = kernel_call(
                patch_kernel,
                [(PATCH_DEV, lanes)] * 5,
                [mask, weight, grad, table, odd_in] + fault_in + even_in + [touch],
                unread=(4,) + tuple(range(5 + len(fault_in), 8 + len(fault_in))),
                pair=pair,
                steps=steps,
            )
            patch_sums = sums[0]
            for i, distance, group in ((2, 1, 1), (4, 2, 1), (3, 2, 0), (1, 1, 0)):
                patch_sums = patch_sums + swapped(sums[i], distance, group)
            earlier = kernel_call(
                step_kernel,
                [whole],
                args + [sums[0], back],
                scratch=[native],
                unread=(len(args),),
                **static,
            )[0]
    return (
        jnp.transpose(earlier, (0, 2, 1, 3)),
        jnp.transpose(later, (0, 2, 1, 3)),
        patch_sums[None],
    )


def solution(mesh):
    return jax.shard_map(
        on_device,
        mesh=mesh,
        in_specs=(
            P(None, "dom", "depth", None),
            P(None, "dom", "depth", None),
            P("dom", "depth", None),
            P("dom", "depth", None),
            P("dom", "depth", None),
            P(None, "depth", "dom", None),
            P("depth", "dom", None),
            P("depth", "dom", None),
            P("depth", "dom"),
        ),
        out_specs=(
            P(None, "dom", "depth", None),
            P(None, "dom", "depth", None),
            P("depth", "dom", None),
        ),
        check_vma=False,
    )
```

```python
import functools
import math

import jax
import jax.numpy as jnp
import ml_dtypes
import numpy as np
from jax import lax
from jax.experimental import pallas as pl
from jax.experimental.pallas import tpu as pltpu
from jax.sharding import PartitionSpec as P

PATCH_DEV = 2
REACH = 2
PATCH_ROWS = 16

time_step = 0.01
lock_stiffness = 0.5

BLOCK = 16
ROWS = ((0, 1, 2), (3, 4, 5), (11, 12, 13), (6, 7, 14), (8, 9, 10))
PLANE = 5 * BLOCK


def basis_tables():
    points = [-1.0, -math.sqrt(3.0 / 7.0), 0.0, math.sqrt(3.0 / 7.0), 1.0]
    quad_weights = np.array([0.1, 49.0 / 90.0, 32.0 / 45.0, 49.0 / 90.0, 0.1])
    products = []
    for first in range(5):
        value = 1.0
        for other in range(5):
            if other != first:
                value = value * (points[first] - points[other])
        products.append(value)
    derivative = np.zeros((5, 5))
    for row in range(5):
        for column in range(5):
            if row == column:
                total = 0.0
                for other in range(5):
                    if other != row:
                        total = total + 1.0 / (points[row] - points[other])
                derivative[row, column] = total
            else:
                derivative[row, column] = (
                    products[row] / products[column] / (points[row] - points[column])
                )
    return (quad_weights, derivative)


def two_parts(table):
    high = table.astype(ml_dtypes.bfloat16)
    low = (table - high.astype(np.float64)).astype(ml_dtypes.bfloat16)
    return np.stack([high, low])


def element_stiffness():
    weights, derivative = basis_tables()
    eye = np.eye(5)
    slope = 2.0 * derivative
    grads = [
        np.kron(slope, np.kron(eye, eye)),
        np.kron(eye, np.kron(eye, slope)),
        np.kron(eye, np.kron(slope, eye)),
    ]
    quad = np.kron(weights, np.kron(weights, weights)) / 8.0
    first = np.zeros((125, 3, 125, 3))
    second = np.zeros((125, 3, 125, 3))
    lap = sum(g.T @ (quad[:, None] * g) for g in grads)
    for c in range(3):
        second[:, c, :, c] += lap
        for d in range(3):
            first[:, c, :, d] += grads[c].T @ (quad[:, None] * grads[d])
            second[:, c, :, d] += grads[d].T @ (quad[:, None] * grads[c])
    where = [
        node // 5 * BLOCK + ROWS[node % 5][c] for node in range(125) for c in range(3)
    ]
    wide = []
    for small in (first, second):
        big = np.zeros((5 * PLANE, 5 * PLANE))
        big[np.ix_(where, where)] = small.reshape(375, 375)
        wide.append(big)
    return wide


OWN_COLS = 384


def padded_table(table, columns):
    return np.pad(table, ((0, 0), (0, columns - table.shape[1])))


@functools.cache
def stiffness_tables():
    wide = element_stiffness()
    own = 4 * PLANE
    planes = [slice(x * PLANE, (x + 1) * PLANE) for x in range(5)]
    inner = np.concatenate([w[:own, :own] for w in wide])

    def three(rows, columns):
        high, low = two_parts(np.concatenate([w[rows, columns] for w in wide]))
        return padded_table(np.concatenate([high, low, high], axis=1), 256)

    return (
        two_parts(padded_table(inner, OWN_COLS)),
        np.stack([three(planes[x], planes[4]) for x in range(4)]),
        np.stack([three(planes[4], planes[x]) for x in range(4)]),
        three(planes[4], planes[4]),
    )


@functools.cache
def back_table(y_elems, z_elems):
    lanes = y_elems * z_elems
    depth = 4 * z_elems
    back = np.zeros((4 * lanes, y_elems * depth), ml_dtypes.bfloat16)
    for yel in range(y_elems):
        for k in range(z_elems):
            for zl in range(4):
                back[zl * lanes + yel * z_elems + k, yel * depth + 4 * k + zl] = 1
    return back


@functools.cache
def mass_table(y_elems, z_elems):
    weights, _ = basis_tables()
    table = np.zeros((4, 5, BLOCK, y_elems, z_elems))
    for x in range(4):
        mx = 0.2 if x == 0 else weights[x]
        for zl in range(5):
            for yl in range(5):
                for yel in range(y_elems):
                    my = weights[yl]
                    if (yl == 0 and yel > 0) or (yl == 4 and yel < y_elems - 1):
                        my = 0.2
                    mz = np.full(z_elems, weights[zl])
                    if zl == 0:
                        mz[1:] = 0.2
                    if zl == 4:
                        mz[:] = 0.2
                    value = time_step * time_step * 8.0 / (mx * my * mz)
                    if zl == 4:
                        value[-1] = 0.0
                    table[x, zl, list(ROWS[yl]), yel] = value
    return table.reshape(4 * PLANE, y_elems * z_elems).astype(np.float32)


def pieces(value, count):
    out = []
    for _ in range(count):
        piece = value.astype(jnp.bfloat16)
        out.append(piece)
        value = value - piece.astype(jnp.float32)
    return out


def dot(a, b):
    return jnp.dot(a, b, preferred_element_type=jnp.float32)


def exact_dot(value, table, count=3):
    rows = value.shape[0]
    result = dot(jnp.concatenate(pieces(value, count), axis=0), table)
    total = result[:rows]
    for i in range(1, count):
        total = total + result[i * rows : (i + 1) * rows]
    return total


def split_dot(table_high, table_low, value):
    lanes = value.shape[1]
    high, low = pieces(value, 2)
    wide = dot(table_high, jnp.concatenate([high, low], axis=1))
    return wide[:, :lanes] + (wide[:, lanes:] + dot(table_low, high))


def ones_where(rule, shape):
    row = lax.broadcasted_iota(jnp.int32, shape, 0)
    column = lax.broadcasted_iota(jnp.int32, shape, 1)
    return jnp.where(rule(row, column), 1.0, 0.0).astype(jnp.bfloat16)


def gather_table(lanes, z_elems):
    return ones_where(lambda z, c: z == 4 * (c % z_elems) + c // lanes, (lanes, 5 * lanes))


def fault_table(lanes, z_elems):
    return ones_where(lambda z, c: z == 4 * (c % z_elems) + c // z_elems, (lanes, lanes))


def fault_table_back(lanes, z_elems):
    return ones_where(lambda c, z: z == 4 * (c % z_elems) + c // z_elems, (lanes, lanes))


def stacked(value):
    high, low = pieces(value, 2)
    gap = jnp.zeros((256 - 3 * value.shape[0], value.shape[1]), jnp.bfloat16)
    return jnp.concatenate([high, high, low, gap], axis=0)


def to_elements(native, scratch, table, y_elems, parts=3):
    group = 4 * BLOCK
    scratch[...] = jnp.zeros_like(scratch)
    for c in range(3):
        for y in range(4 * y_elems + 1):
            rows = native(c, y)
            if y < 4 * y_elems:
                scratch[y // 4, pl.ds(ROWS[y % 4][c], 4, stride=BLOCK), :] = rows
            if y % 4 == 0 and y > 0:
                scratch[y // 4 - 1, pl.ds(ROWS[4][c], 4, stride=BLOCK), :] = rows
    high, middle, *low = pieces(
        jnp.concatenate([scratch[i] for i in range(y_elems)], axis=0), parts
    )
    result = dot(
        jnp.concatenate([high, middle], axis=1), jnp.concatenate([table, table], axis=0)
    )
    for piece in low:
        result = result + dot(piece, table)
    lanes = result.shape[1] // 5
    across = lax.broadcasted_iota(jnp.int32, (group, result.shape[1]), 1) % lanes // (
        lanes // y_elems
    )
    total = result[:group]
    for yel in range(1, y_elems):
        total = jnp.where(across == yel, result[yel * group : (yel + 1) * group], total)
    blocks = []
    for x in range(4):
        for zl in range(5):
            blocks.append(total[x * BLOCK : (x + 1) * BLOCK, zl * lanes : (zl + 1) * lanes])
    return jnp.concatenate(blocks, axis=0)


def from_elements(field, scratch, back_ref, out_ref, y_elems):
    rows = []
    for x in range(4):
        rows.append(
            jnp.concatenate(
                [field[x * PLANE + zl * BLOCK : x * PLANE + (zl + 1) * BLOCK] for zl in range(4)],
                axis=1,
            )
        )
    result = exact_dot(jnp.concatenate(rows, axis=0), back_ref[...])
    depth = result.shape[1] // y_elems
    for yel in range(y_elems):
        scratch[yel] = result[:, yel * depth : (yel + 1) * depth]
    for c in range(3):
        for y in range(4 * y_elems + 1):
            yel, yl = (y // 4, y % 4) if y < 4 * y_elems else (y_elems - 1, 4)
            out_ref[c, y] = scratch[yel, pl.ds(ROWS[yl][c], 4, stride=BLOCK), :]


def shifted(rows, lanes):
    lanes = lanes % rows.shape[1]
    return pltpu.roll(rows, lanes, 1) if lanes else rows


def block_iotas(lanes):
    return (
        lax.broadcasted_iota(jnp.int32, (8, lanes), 0),
        lax.broadcasted_iota(jnp.int32, (8, lanes), 1),
    )


def fault_message(plane, z_elems):
    lanes = plane.shape[1]
    row, lane = block_iotas(lanes)
    first = last = jnp.zeros((8, lanes), jnp.float32)
    for zl in range(4):
        at = zl * BLOCK
        here = lane // z_elems == zl
        first = jnp.where(here, shifted(plane[at : at + 8], zl * z_elems), first)
        last = jnp.where(here, shifted(plane[at + 8 : at + 16], (zl + 1) * z_elems), last)
    return jnp.where(row < 4, last, pltpu.roll(first, 4, 0))


def swap_rows(message):
    parts = [pltpu.roll(message[i : i + 8], 4, 0) for i in range(0, message.shape[0], 8)]
    return jnp.concatenate(parts, axis=0)


def select_messages(parity, left, right):
    even = parity == 0
    return jnp.where(even, right, left), jnp.where(even, left, right)


def material_rows(lame_ref, shear_ref):
    y_elems, z_elems = lame_ref.shape
    both = jnp.concatenate([lame_ref[...], shear_ref[...]], axis=0)
    spread = ones_where(lambda k, c: c % z_elems == k, (z_elems, y_elems * z_elems))
    tiled = exact_dot(both, spread)
    row = lax.broadcasted_iota(jnp.int32, tiled.shape, 0)
    lane = lax.broadcasted_iota(jnp.int32, tiled.shape, 1)
    kept = jnp.where(row % y_elems == lane // z_elems, tiled, 0.0)
    return (
        jnp.sum(kept[:y_elems], axis=0, keepdims=True),
        jnp.sum(kept[y_elems:], axis=0, keepdims=True),
    )


def above_lanes(lanes, z_elems):
    return lax.broadcasted_iota(jnp.int32, (BLOCK, lanes), 1) % z_elems != 0


def edge_message(result, lame_row, shear_row, z_elems):
    lanes = result.shape[1]
    force = lame_row * result[:PLANE] + shear_row * result[PLANE:]
    top = force[:BLOCK] + jnp.where(
        above_lanes(lanes, z_elems), pltpu.roll(force[4 * BLOCK :], 1, 1), 0.0
    )
    row = lax.broadcasted_iota(jnp.int32, top.shape, 0)
    top = jnp.where(row == BLOCK - 1, lame_row, top)
    second = jnp.where(row == BLOCK - 1, shear_row, force[BLOCK : 2 * BLOCK])
    return jnp.concatenate([top, second, force[2 * BLOCK : 4 * BLOCK]], axis=0)


def own_force(own_ref, cur, lame_row, shear_row):
    rows, lanes = cur.shape
    padded = jnp.concatenate([cur, jnp.zeros((OWN_COLS - rows, lanes), jnp.float32)], axis=0)
    result = split_dot(own_ref[0], own_ref[1], padded)
    return lame_row * result[:rows] + shear_row * result[rows:]


def start_copies(pairs, sems):
    copies = [
        pltpu.make_async_copy(source, target, sems.at[i])
        for i, (source, target) in enumerate(pairs)
    ]
    for copy in copies:
        copy.start()
    return copies


def first_kernel(
    now_hbm,
    flags_hbm,
    weak_hbm,
    lame_hbm,
    shear_hbm,
    edge_hbm,
    own_hbm,
    far_hbm,
    touch_hbm,
    cur_ref,
    even_ref,
    even_rest,
    odd_ref,
    fault_out_ref,
    material_ref,
    edge_ref,
    own_ref,
    far_ref,
    touch_ref,
    scratch,
    now_ref,
    flags_ref,
    weak_ref,
    lame_ref,
    shear_ref,
    sems,
):
    copies = start_copies(
        [
            (now_hbm, now_ref),
            (flags_hbm, flags_ref),
            (weak_hbm, weak_ref),
            (lame_hbm, lame_ref),
            (shear_hbm, shear_ref),
            (edge_hbm, edge_ref),
            (own_hbm, own_ref),
            (far_hbm, far_ref),
            (touch_hbm, touch_ref),
        ],
        sems,
    )
    y_elems, z_elems = lame_ref.shape
    lanes = y_elems * z_elems
    parity = lax.axis_index("dom") % 2
    gather = gather_table(lanes, z_elems)
    fault = fault_table(lanes, z_elems)
    copies[1].wait()
    copies[2].wait()
    weak = weak_ref[...]
    tangent = []
    for i in range(flags_ref.shape[0]):
        flag = flags_ref[i]
        tangent.append(
            jnp.where(flag == 0, lock_stiffness, jnp.where(flag == 1, -weak, 0.0))
        )
    fault_out_ref[32:] = exact_dot(jnp.concatenate(tangent, axis=0), fault)
    copies[3].wait()
    copies[4].wait()
    lame_row, shear_row = material_rows(lame_ref, shear_ref)
    material_ref[...] = jnp.concatenate(
        [lame_row, shear_row, jnp.zeros((6, lanes), jnp.float32)], axis=0
    )
    copies[0].wait()
    cur = to_elements(lambda c, y: now_ref[c, y], scratch, gather, y_elems)
    copies[5].wait()
    planes = [cur[x * PLANE : (x + 1) * PLANE] for x in range(4)]
    edge = sum(dot(edge_ref[x], stacked(planes[x])) for x in range(4))
    right = edge_message(edge, lame_row, shear_row, z_elems)
    message, odd_ref[...] = select_messages(parity, cur[: 4 * BLOCK], right)
    even_ref[...], even_rest[...] = message[: 2 * BLOCK], message[2 * BLOCK :]
    cur_ref[...] = cur
    for x in range(4):
        fault_out_ref[8 * x : 8 * x + 8] = fault_message(planes[x], z_elems)
    for copy in copies[6:]:
        copy.wait()


def prepare_kernel(cur_ref, material_ref, own_ref, touch_ref, base_ref, edge_part_ref):
    cur = cur_ref[...]
    base_ref[...] = own_force(own_ref, cur, material_ref[0:1], material_ref[1:2])
    edge_part_ref[...] = dot(touch_ref[...], stacked(cur[:PLANE]))


def setup_kernel(
    next_hbm,
    density_hbm,
    flags_hbm,
    stress_hbm,
    mass_hbm,
    fol_ref,
    minv_ref,
    weight_ref,
    scratch,
    next_ref,
    density_ref,
    flags_ref,
    stress_ref,
    mass_ref,
    sems,
    *,
    y_elems,
    z_elems,
):
    copies = start_copies(
        [
            (next_hbm, next_ref),
            (density_hbm, density_ref),
            (flags_hbm, flags_ref),
            (stress_hbm, stress_ref),
            (mass_hbm, mass_ref),
        ],
        sems,
    )
    gather = gather_table(y_elems * z_elems, z_elems)
    fault = fault_table(y_elems * z_elems, z_elems)
    for copy in copies[:5]:
        copy.wait()
    fol_ref[...] = to_elements(lambda c, y: next_ref[c, y], scratch, gather, y_elems)
    density = to_elements(lambda c, y: density_ref[y], scratch, gather, y_elems, 2)
    table = mass_ref[...]
    first = lax.axis_index("dom") == 0
    plane = lax.broadcasted_iota(jnp.int32, table.shape, 0) < PLANE
    table = jnp.where(jnp.logical_and(first, plane), 2.0 * table, table)
    minv_ref[...] = jnp.where(table > 0.0, table / jnp.where(table > 0.0, density, 1.0), 0.0)
    stress = stress_ref[...]
    weights = []
    for i in range(flags_ref.shape[0]):
        flag = flags_ref[i]
        weights.append(
            stress * jnp.where(flag == 1, 0.5, jnp.where(flag == 2, 1.0, 0.0))
        )
    weight_ref[...] = exact_dot(jnp.concatenate(weights, axis=0), fault)


def fault_input(up_ref, down_ref, count):
    if down_ref is None:
        return up_ref[:count]
    up, down = up_ref[:count], down_ref[:count]
    row = lax.broadcasted_iota(jnp.int32, up.shape, 0)
    return jnp.where(row % 8 < 4, up, down)


def step_kernel(*refs, step, last, extra, last_place, pair, y_elems, z_elems):
    cur_ref, fol_ref, minv_ref, base_ref, touch_ref, material_ref, odd_ref, up_ref = refs[:8]
    refs = list(refs[8:])
    down_ref = None if pair else refs.pop(0)
    even_in = jnp.concatenate([refs.pop(0)[...], refs.pop(0)[...]], axis=0)
    first_up_ref, own_ref, first_own_ref, far_ref, edge_ref = refs[:5]
    refs = refs[5 + extra :]
    if last:
        back_ref, out_ref, scratch = refs
    else:
        new_ref, even_out, even_rest, odd_out, fault_out = refs
    place = lax.axis_index("dom")
    lanes = cur_ref.shape[1]
    even = place % 2 == 0
    far = jnp.where(place == last_place, 0.0, jnp.where(even, even_in, odd_ref[...]))
    left = jnp.where(place == 0, 0.0, jnp.where(even, odd_ref[...], even_in))
    lane_wide = lax.broadcasted_iota(jnp.int32, (BLOCK, lanes), 1)
    below = jnp.where(
        lane_wide % z_elems != z_elems - 1, pltpu.roll(far[:BLOCK], lanes - 1, 1), 0.0
    )
    far = stacked(jnp.concatenate([far, below], axis=0))
    lame_row, shear_row = material_ref[0:1], material_ref[1:2]
    left_lame = left[BLOCK - 1 : BLOCK]
    left_shear = left[2 * BLOCK - 1 : 2 * BLOCK]
    from_left = left_lame * touch_ref[:PLANE] + left_shear * touch_ref[PLANE:]
    row, lane = block_iotas(lanes)
    across = lane // z_elems
    shared = row < 3
    add_first = jnp.logical_and(shared, across > 0)
    take_last = jnp.logical_and(shared, across < y_elems - 1)
    pull_first = jnp.logical_and(shared, across == 0)
    pull_last = jnp.logical_and(shared, across == y_elems - 1)
    above = above_lanes(lanes, z_elems)
    fault_in = fault_input(up_ref, down_ref, 32)
    if not last:
        fault_out[32:] = jnp.zeros_like(fault_out[32:])
    planes = []
    edge = 0.0
    for x in range(4):
        rows = slice(x * PLANE, (x + 1) * PLANE)
        result = dot(far_ref[x], far)
        force = base_ref[rows] + (lame_row * result[:PLANE] + shear_row * result[PLANE:])
        blocks = [force[zl * BLOCK : (zl + 1) * BLOCK] for zl in range(5)]
        if x == 0:
            blocks = [b + from_left[i * BLOCK : (i + 1) * BLOCK] for i, b in enumerate(blocks)]
            blocks[:4] = [b + left[i * BLOCK : (i + 1) * BLOCK] for i, b in enumerate(blocks[:4])]
        blocks[0], blocks[4] = (
            blocks[0] + jnp.where(above, pltpu.roll(blocks[4], 1, 1), 0.0),
            blocks[4] + pltpu.roll(blocks[0], lanes - 1, 1),
        )
        at, k = slice(8 * x, 8 * x + 8), slice(32 + 4 * step + x, 33 + 4 * step + x)
        stiff = jnp.where(
            jnp.logical_or(row == 1, row == 5),
            lock_stiffness,
            jnp.where(row < 4, first_up_ref[k], first_own_ref[k]),
        )
        pulled = stiff * (fault_in[at] - pltpu.roll(own_ref[at], 4, 0))
        pulled_last = pltpu.roll(pulled, 4, 0)
        for zl in range(5):
            low, high = blocks[zl][:8], blocks[zl][8:]
            move = zl * z_elems if zl < 4 else 1
            blocks[zl] = jnp.concatenate(
                [
                    low
                    + jnp.where(add_first, shifted(high, z_elems), 0.0)
                    - jnp.where(pull_first, shifted(pulled, -move), 0.0),
                    high
                    + jnp.where(take_last, shifted(low, -z_elems), 0.0)
                    - jnp.where(pull_last, shifted(pulled_last, -move - z_elems), 0.0),
                ],
                axis=0,
            )
        plane = (2.0 * cur_ref[rows] - fol_ref[rows]) - minv_ref[rows] * jnp.concatenate(
            blocks, axis=0
        )
        if last:
            planes.append(plane)
        else:
            new_ref[rows] = plane
            fault_out[at] = fault_message(plane, z_elems)
            edge = edge + dot(edge_ref[x], stacked(plane))
            if x == 0:
                first = plane[: 4 * BLOCK]
    if last:
        from_elements(jnp.concatenate(planes, axis=0), scratch, back_ref, out_ref, y_elems)
    else:
        right = edge_message(edge, lame_row, shear_row, z_elems)
        message, odd_out[...] = select_messages(place % 2, first, right)
        even_out[...], even_rest[...] = message[: 2 * BLOCK], message[2 * BLOCK :]


def mask_kernel(owner_ref, _, back_ref, mask_ref):
    shape = (PATCH_ROWS, mask_ref.shape[1])
    first = (lax.axis_index("dom") - REACH) * PATCH_DEV
    number = lax.broadcasted_iota(jnp.int32, shape, 0) + first
    for x in range(4):
        mask = jnp.where(number == owner_ref[0, x], 1.0, 0.0)
        mask_ref[PATCH_ROWS * x : PATCH_ROWS * (x + 1)] = mask


def output_kernel(*refs, pair, steps, y_elems, z_elems):
    field_ref, back_ref, weight_ref = refs[:3]
    out_ref, grad_ref, table_ref, scratch = refs[-4:]
    messages = refs[3:-4]
    count = 2 if pair else 3
    grads = [jnp.zeros((8, weight_ref.shape[1]), jnp.float32) for _ in range(4)]
    for i in range(steps):
        group = messages[count * i : count * (i + 1)]
        slip = -swap_rows(group[0][:32])
        if i < steps - 1:
            slip = slip + fault_input(group[1], None if pair else group[2], 32)
        for x in range(4):
            grads[x] = grads[x] + slip[8 * x : 8 * x + 8] * weight_ref[4 * i + x : 4 * i + x + 1]
    grad_ref[...] = jnp.concatenate(grads, axis=0)
    table_ref[...] = fault_table_back(weight_ref.shape[1], z_elems)
    from_elements(field_ref[...], scratch, back_ref, out_ref, y_elems)


def patch_kernel(*refs, pair, steps):
    mask_ref, weight_ref, grad_ref, table_ref, _, up_ref = refs[:6]
    down_ref = None if pair else refs[6]
    home_out, out_a, out_b, out_c, out_d = refs[-5:]
    place = lax.axis_index("dom")
    slip = fault_input(up_ref, down_ref, 32)
    total = 0.0
    for x in range(4):
        at, k = 8 * x + 4, 4 * (steps - 1) + x
        grad = grad_ref[at : at + 1] + slip[at : at + 1] * weight_ref[k : k + 1]
        total = total + mask_ref[PATCH_ROWS * x : PATCH_ROWS * (x + 1)] * grad
    total = exact_dot(total, table_ref[...])
    rows = [total[2 * i : 2 * i + 2] for i in range(5)]
    home_out[...] = rows[2]
    even = place % 2 == 0
    out_a[...] = jnp.where(even, rows[3], rows[1])
    out_b[...] = jnp.where(even, rows[1], rows[3])
    low = place % 4 < 2
    out_c[...] = jnp.where(low, rows[4], rows[0])
    out_d[...] = jnp.where(low, rows[0], rows[4])


VMEM = pl.BlockSpec(memory_space=pltpu.VMEM)
HBM = pl.BlockSpec(memory_space=pltpu.HBM)
SMEM = pl.BlockSpec(memory_space=pltpu.SMEM)
ANY = pl.BlockSpec(memory_space=pl.ANY)


def kernel_call(body, outs, args, in_smem=(), scratch=(), in_hbm=(), kept=(), unread=(), **static):
    shapes = []
    for out in outs:
        shape, dtype = out if isinstance(out[0], tuple) else (out, jnp.float32)
        shapes.append((pltpu.VMEM if in_hbm else jax.ShapeDtypeStruct)(shape, dtype))
    specs = [VMEM] * len(args)
    for places, spec in ((in_smem, SMEM), (in_hbm, HBM), (unread, ANY)):
        for i in places:
            specs[i] = spec
    copied = [pltpu.VMEM(args[i].shape, args[i].dtype) for i in in_hbm if i not in kept]
    if in_hbm:
        copied.append(pltpu.SemaphoreType.DMA((len(in_hbm),)))
    return pl.pallas_call(
        functools.partial(body, **static) if static else body,
        out_shape=shapes,
        in_specs=specs,
        out_specs=[VMEM] * len(shapes),
        scratch_shapes=list(scratch) + copied,
        compiler_params=pltpu.CompilerParams(
            vmem_limit_bytes=(56 if in_hbm else 24) * 2**20
        ),
    )(*args)


def swapped(block, distance, group):
    size, across = lax.axis_size("dom"), lax.axis_size("depth")
    partner = {}
    for left in range(size - distance):
        if left // distance % 2 == group:
            partner[left], partner[left + distance] = left + distance, left
    route = []
    for i in range(size):
        for j in range(across):
            side = j if i in partner else min(j ^ 1, across - 1)
            route.append((i * across + j, partner.get(i, i) * across + side))
    return lax.ppermute(block, ("dom", "depth"), route)


def from_behind(block, axis, distance):
    size = lax.axis_size(axis)
    return lax.ppermute(block, axis, [((i - distance) % size, i) for i in range(size)])


def on_device(
    adjoint_now,
    adjoint_next,
    lame_first,
    shear_modulus,
    density,
    branch_flags,
    weak_slope,
    normal_stress,
    patch_owner,
):
    x_elems, y_elems, z_elems = lame_first.shape
    lanes = y_elems * z_elems
    assert x_elems == 1 and lanes == adjoint_now.shape[3]
    steps = branch_flags.shape[0]
    pair = lax.axis_size("depth") == 2
    own_table, far_table, edge_table, touch_table = (jnp.asarray(t) for t in stiffness_tables())
    back = jnp.asarray(back_table(y_elems, z_elems))
    mass = jnp.asarray(mass_table(y_elems, z_elems))
    now = jnp.transpose(adjoint_now, (0, 2, 1, 3))
    following = jnp.transpose(adjoint_next, (0, 2, 1, 3))
    rho = jnp.transpose(density, (1, 0, 2))
    flags = branch_flags[:, 0]
    native = pltpu.VMEM((y_elems, 4 * BLOCK, lanes), jnp.float32)
    field = (4 * PLANE, lanes)
    plane = (4 * BLOCK, lanes)
    half = (2 * BLOCK, lanes)

    def exchange(even, odd, fault_rows):
        if pair:
            faults = [from_behind(fault_rows, "depth", 1)]
        else:
            faults = [from_behind(fault_rows, "depth", 1), from_behind(fault_rows, "depth", -1)]
        return [swapped(part, 1, 0) for part in even], swapped(odd, 1, 1), faults

    tables = (edge_table, own_table, far_table, touch_table)
    cur, *even, odd, fault_rows, material, edge_table, own_table, far_table, touch_table = kernel_call(
        first_kernel,
        [field, half, half, plane, (32 + 4 * steps, lanes), (8, lanes)]
        + [(t.shape, t.dtype) for t in tables],
        (now, flags, weak_slope[0], lame_first[0], shear_modulus[0]) + tables,
        scratch=[native],
        in_hbm=range(9),
        kept=range(5, 9),
    )
    first_fault = fault_rows
    even_in, odd_in, fault_in = exchange(even, odd, fault_rows)
    first_in = fault_in
    fol, minv, weight = kernel_call(
        setup_kernel,
        [field, field, (4 * steps, lanes)],
        (following, rho, flags, normal_stress[0], mass),
        scratch=[native],
        in_hbm=range(5),
        y_elems=y_elems,
        z_elems=z_elems,
    )
    seen = []
    for step in range(steps):
        last = step == steps - 1
        seen += [fault_rows] + fault_in
        base, touch = kernel_call(
            prepare_kernel,
            [field, (2 * PLANE, lanes)],
            [cur, material, own_table, touch_table],
            (),
        )
        args = [cur, fol, minv, base, touch, material, odd_in] + fault_in + even_in
        args += [first_in[0], fault_rows, first_fault, far_table, edge_table]
        static = dict(
            step=step, last=last, extra=1 if last or step == 1 else 0, last_place=lax.axis_size("dom") - 1, pair=pair, y_elems=y_elems,
            z_elems=z_elems,
        )
        if step == 1:
            mask = kernel_call(
                mask_kernel, [(4 * PATCH_ROWS, lanes)], [patch_owner, cur, back], (0,), unread=(1,)
            )[0]
            args.append(mask)
        if not last:
            new, *even, odd, new_fault = kernel_call(
                step_kernel,
                [field, half, half, plane, (40, lanes)],
                args,
                unread=(len(args) - 1,) if step == 1 else (),
                **static,
            )
            fol, cur, fault_rows = cur, new, new_fault
            even_in, odd_in, fault_in = exchange(even, odd, fault_rows)
        else:
            whole = (3, 4 * y_elems + 1, 4, lanes)
            known = seen[: len(seen) - len(fault_in)]
            later, grad, table = kernel_call(
                output_kernel,
                [whole, (32, lanes), ((lanes, lanes), jnp.bfloat16)],
                [cur, back, weight] + known,
                (),
                [native],
                pair=pair,
                steps=steps,
                y_elems=y_elems,
                z_elems=z_elems,
            )
            sums = kernel_call(
                patch_kernel,
                [(PATCH_DEV, lanes)] * 5,
                [mask, weight, grad, table, odd_in] + fault_in + even_in + [touch],
                unread=(4,) + tuple(range(5 + len(fault_in), 8 + len(fault_in))),
                pair=pair,
                steps=steps,
            )
            patch_sums = sums[0]
            for i, distance, group in ((2, 1, 1), (4, 2, 1), (3, 2, 0), (1, 1, 0)):
                patch_sums = patch_sums + swapped(sums[i], distance, group)
            earlier = kernel_call(
                step_kernel,
                [whole],
                args + [sums[0], back],
                scratch=[native],
                unread=(len(args),),
                **static,
            )[0]
    return (
        jnp.transpose(earlier, (0, 2, 1, 3)),
        jnp.transpose(later, (0, 2, 1, 3)),
        patch_sums[None],
    )


def solution(mesh):
    return jax.shard_map(
        on_device,
        mesh=mesh,
        in_specs=(
            P(None, "dom", "depth", None),
            P(None, "dom", "depth", None),
            P("dom", "depth", None),
            P("dom", "depth", None),
            P("dom", "depth", None),
            P(None, "depth", "dom", None),
            P("depth", "dom", None),
            P("depth", "dom", None),
            P("depth", "dom"),
        ),
        out_specs=(
            P(None, "dom", "depth", None),
            P(None, "dom", "depth", None),
            P("depth", "dom", None),
        ),
        check_vma=False,
    )
```

```python
import functools
import math

import jax
import jax.numpy as jnp
import ml_dtypes
import numpy as np
from jax import lax
from jax.experimental import pallas as pl
from jax.experimental.pallas import tpu as pltpu
from jax.sharding import PartitionSpec as P

PATCH_DEV = 2
REACH = 2
PATCH_ROWS = 16
LATER = 7

time_step = 0.01
lock_stiffness = 0.5

BLOCK = 16
ROWS = ((0, 1, 2), (3, 4, 5), (11, 12, 13), (6, 7, 14), (8, 9, 10))
PLANE = 5 * BLOCK


def basis_tables():
    points = [-1.0, -math.sqrt(3.0 / 7.0), 0.0, math.sqrt(3.0 / 7.0), 1.0]
    quad_weights = np.array([0.1, 49.0 / 90.0, 32.0 / 45.0, 49.0 / 90.0, 0.1])
    products = []
    for first in range(5):
        value = 1.0
        for other in range(5):
            if other != first:
                value = value * (points[first] - points[other])
        products.append(value)
    derivative = np.zeros((5, 5))
    for row in range(5):
        for column in range(5):
            if row == column:
                total = 0.0
                for other in range(5):
                    if other != row:
                        total = total + 1.0 / (points[row] - points[other])
                derivative[row, column] = total
            else:
                derivative[row, column] = (
                    products[row] / products[column] / (points[row] - points[column])
                )
    return (quad_weights, derivative)


def two_parts(table):
    high = table.astype(ml_dtypes.bfloat16)
    low = (table - high.astype(np.float64)).astype(ml_dtypes.bfloat16)
    return np.stack([high, low])


def element_stiffness():
    weights, derivative = basis_tables()
    eye = np.eye(5)
    slope = 2.0 * derivative
    grads = [
        np.kron(slope, np.kron(eye, eye)),
        np.kron(eye, np.kron(eye, slope)),
        np.kron(eye, np.kron(slope, eye)),
    ]
    quad = np.kron(weights, np.kron(weights, weights)) / 8.0
    first = np.zeros((125, 3, 125, 3))
    second = np.zeros((125, 3, 125, 3))
    lap = sum(g.T @ (quad[:, None] * g) for g in grads)
    for c in range(3):
        second[:, c, :, c] += lap
        for d in range(3):
            first[:, c, :, d] += grads[c].T @ (quad[:, None] * grads[d])
            second[:, c, :, d] += grads[d].T @ (quad[:, None] * grads[c])
    where = [
        node // 5 * BLOCK + ROWS[node % 5][c] for node in range(125) for c in range(3)
    ]
    wide = []
    for small in (first, second):
        big = np.zeros((5 * PLANE, 5 * PLANE))
        big[np.ix_(where, where)] = small.reshape(375, 375)
        wide.append(big)
    return wide


OWN_COLS = 384


def padded_table(table, columns):
    return np.pad(table, ((0, 0), (0, columns - table.shape[1])))


@functools.cache
def stiffness_tables():
    wide = element_stiffness()
    own = 4 * PLANE
    planes = [slice(x * PLANE, (x + 1) * PLANE) for x in range(5)]
    inner = np.concatenate([w[:own, :own] for w in wide])

    def three(rows, columns):
        high, low = two_parts(np.concatenate([w[rows, columns] for w in wide]))
        return padded_table(np.concatenate([high, low, high], axis=1), 256)

    return (
        two_parts(padded_table(inner, OWN_COLS)),
        np.stack([three(planes[x], planes[4]) for x in range(4)]),
        np.stack([three(planes[4], planes[x]) for x in range(4)]),
        three(planes[4], planes[4]),
    )


@functools.cache
def back_table(y_elems, z_elems):
    lanes = y_elems * z_elems
    depth = 4 * z_elems
    back = np.zeros((4 * lanes, y_elems * depth), ml_dtypes.bfloat16)
    for yel in range(y_elems):
        for k in range(z_elems):
            for zl in range(4):
                back[zl * lanes + yel * z_elems + k, yel * depth + 4 * k + zl] = 1
    return back


@functools.cache
def mass_table(y_elems, z_elems):
    weights, _ = basis_tables()
    table = np.zeros((4, 5, BLOCK, y_elems, z_elems))
    for x in range(4):
        mx = 0.2 if x == 0 else weights[x]
        for zl in range(5):
            for yl in range(5):
                for yel in range(y_elems):
                    my = weights[yl]
                    if (yl == 0 and yel > 0) or (yl == 4 and yel < y_elems - 1):
                        my = 0.2
                    mz = np.full(z_elems, weights[zl])
                    if zl == 0:
                        mz[1:] = 0.2
                    if zl == 4:
                        mz[:] = 0.2
                    value = time_step * time_step * 8.0 / (mx * my * mz)
                    if zl == 4:
                        value[-1] = 0.0
                    table[x, zl, list(ROWS[yl]), yel] = value
    return table.reshape(4 * PLANE, y_elems * z_elems).astype(np.float32)


def pieces(value, count):
    out = []
    for _ in range(count):
        piece = value.astype(jnp.bfloat16)
        out.append(piece)
        value = value - piece.astype(jnp.float32)
    return out


def dot(a, b):
    return jnp.dot(a, b, preferred_element_type=jnp.float32)


def exact_dot(value, table, count=3):
    rows = value.shape[0]
    result = dot(jnp.concatenate(pieces(value, count), axis=0), table)
    total = result[:rows]
    for i in range(1, count):
        total = total + result[i * rows : (i + 1) * rows]
    return total


def split_dot(table_high, table_low, value):
    lanes = value.shape[1]
    high, low = pieces(value, 2)
    wide = dot(table_high, jnp.concatenate([high, low], axis=1))
    return wide[:, :lanes] + (wide[:, lanes:] + dot(table_low, high))


def ones_where(rule, shape):
    row = lax.broadcasted_iota(jnp.int32, shape, 0)
    column = lax.broadcasted_iota(jnp.int32, shape, 1)
    return jnp.where(rule(row, column), 1.0, 0.0).astype(jnp.bfloat16)


def gather_table(lanes, z_elems):
    return ones_where(lambda z, c: z == 4 * (c % z_elems) + c // lanes, (lanes, 5 * lanes))


def fault_table(lanes, z_elems):
    return ones_where(lambda z, c: z == 4 * (c % z_elems) + c // z_elems, (lanes, lanes))


def fault_table_back(lanes, z_elems):
    return ones_where(lambda c, z: z == 4 * (c % z_elems) + c // z_elems, (lanes, lanes))


def stacked(value):
    high, low = pieces(value, 2)
    gap = jnp.zeros((256 - 3 * value.shape[0], value.shape[1]), jnp.bfloat16)
    return jnp.concatenate([high, high, low, gap], axis=0)


def to_elements(native, scratch, table, y_elems, parts=3):
    group = 4 * BLOCK
    for c in range(3):
        for y in range(4 * y_elems + 1):
            rows = native(c, y)
            if y < 4 * y_elems:
                scratch[y // 4, pl.ds(ROWS[y % 4][c], 4, stride=BLOCK), :] = rows
            if y % 4 == 0 and y > 0:
                scratch[y // 4 - 1, pl.ds(ROWS[4][c], 4, stride=BLOCK), :] = rows
    high, middle, *low = pieces(
        jnp.concatenate([scratch[i] for i in range(y_elems)], axis=0), parts
    )
    result = dot(
        jnp.concatenate([high, middle], axis=1), jnp.concatenate([table, table], axis=0)
    )
    for piece in low:
        result = result + dot(piece, table)
    lanes = result.shape[1] // 5
    across = lax.broadcasted_iota(jnp.int32, (group, result.shape[1]), 1) % lanes // (
        lanes // y_elems
    )
    total = result[:group]
    for yel in range(1, y_elems):
        total = jnp.where(across == yel, result[yel * group : (yel + 1) * group], total)
    blocks = []
    for x in range(4):
        for zl in range(5):
            blocks.append(total[x * BLOCK : (x + 1) * BLOCK, zl * lanes : (zl + 1) * lanes])
    return jnp.concatenate(blocks, axis=0)


def from_elements(field, scratch, back_ref, out_ref, y_elems):
    rows = []
    for x in range(4):
        rows.append(
            jnp.concatenate(
                [field[x * PLANE + zl * BLOCK : x * PLANE + (zl + 1) * BLOCK] for zl in range(4)],
                axis=1,
            )
        )
    result = exact_dot(jnp.concatenate(rows, axis=0), back_ref[...])
    depth = result.shape[1] // y_elems
    for yel in range(y_elems):
        scratch[yel] = result[:, yel * depth : (yel + 1) * depth]
    for c in range(3):
        for y in range(4 * y_elems + 1):
            yel, yl = (y // 4, y % 4) if y < 4 * y_elems else (y_elems - 1, 4)
            out_ref[c, y] = scratch[yel, pl.ds(ROWS[yl][c], 4, stride=BLOCK), :]


def shifted(rows, lanes):
    lanes = lanes % rows.shape[1]
    return pltpu.roll(rows, lanes, 1) if lanes else rows


def block_iotas(lanes):
    return (
        lax.broadcasted_iota(jnp.int32, (8, lanes), 0),
        lax.broadcasted_iota(jnp.int32, (8, lanes), 1),
    )


def fault_message(plane, z_elems):
    lanes = plane.shape[1]
    row, lane = block_iotas(lanes)
    first = last = jnp.zeros((8, lanes), jnp.float32)
    for zl in range(4):
        at = zl * BLOCK
        here = lane // z_elems == zl
        first = jnp.where(here, shifted(plane[at : at + 8], zl * z_elems), first)
        last = jnp.where(here, shifted(plane[at + 8 : at + 16], (zl + 1) * z_elems), last)
    return jnp.where(row < 4, last, pltpu.roll(first, 4, 0))


def swap_rows(message):
    parts = [pltpu.roll(message[i : i + 8], 4, 0) for i in range(0, message.shape[0], 8)]
    return jnp.concatenate(parts, axis=0)


def select_messages(parity, left, right):
    even = parity == 0
    return jnp.where(even, right, left), jnp.where(even, left, right)


def material_rows(lame_ref, shear_ref):
    y_elems, z_elems = lame_ref.shape
    both = jnp.concatenate([lame_ref[...], shear_ref[...]], axis=0)
    spread = ones_where(lambda k, c: c % z_elems == k, (z_elems, y_elems * z_elems))
    tiled = exact_dot(both, spread)
    row = lax.broadcasted_iota(jnp.int32, tiled.shape, 0)
    lane = lax.broadcasted_iota(jnp.int32, tiled.shape, 1)
    kept = jnp.where(row % y_elems == lane // z_elems, tiled, 0.0)
    return (
        jnp.sum(kept[:y_elems], axis=0, keepdims=True),
        jnp.sum(kept[y_elems:], axis=0, keepdims=True),
    )


def above_lanes(lanes, z_elems):
    return lax.broadcasted_iota(jnp.int32, (BLOCK, lanes), 1) % z_elems != 0


def edge_message(result, lame_row, shear_row, z_elems):
    lanes = result.shape[1]
    force = lame_row * result[:PLANE] + shear_row * result[PLANE:]
    top = force[:BLOCK] + jnp.where(
        above_lanes(lanes, z_elems), pltpu.roll(force[4 * BLOCK :], 1, 1), 0.0
    )
    row = lax.broadcasted_iota(jnp.int32, top.shape, 0)
    top = jnp.where(row == BLOCK - 1, lame_row, top)
    second = jnp.where(row == BLOCK - 1, shear_row, force[BLOCK : 2 * BLOCK])
    return jnp.concatenate([top, second, force[2 * BLOCK : 4 * BLOCK]], axis=0)


def own_force(own_ref, cur, lame_row, shear_row):
    rows, lanes = cur.shape
    padded = jnp.concatenate([cur, jnp.zeros((OWN_COLS - rows, lanes), jnp.float32)], axis=0)
    result = split_dot(own_ref[0], own_ref[1], padded)
    return lame_row * result[:rows] + shear_row * result[rows:]


def start_copies(pairs, sems):
    copies = [
        pltpu.make_async_copy(source, target, sems.at[i])
        for i, (source, target) in enumerate(pairs)
    ]
    for copy in copies:
        copy.start()
    return copies


def first_kernel(
    now_hbm,
    flags_hbm,
    weak_hbm,
    lame_hbm,
    shear_hbm,
    *refs,
):
    later_hbm, refs = refs[:LATER], refs[LATER:]
    cur_ref, even_ref, even_rest, odd_ref, fault_out_ref, material_ref = refs[:6]
    later_refs, refs = refs[6 : 6 + LATER], refs[6 + LATER :]
    scratch, now_ref, flags_ref, weak_ref, lame_ref, shear_ref, sems = refs
    copies = start_copies(
        [
            (flags_hbm, flags_ref),
            (weak_hbm, weak_ref),
            (lame_hbm, lame_ref),
            (shear_hbm, shear_ref),
            (now_hbm, now_ref),
        ]
        + list(zip(later_hbm, later_refs)),
        sems,
    )
    edge_ref = later_refs[0]
    y_elems, z_elems = lame_ref.shape
    lanes = y_elems * z_elems
    parity = lax.axis_index("dom") % 2
    gather = gather_table(lanes, z_elems)
    fault = fault_table(lanes, z_elems)
    scratch[...] = jnp.zeros_like(scratch)
    for copy in copies[:6]:
        copy.wait()
    cur = to_elements(lambda c, y: now_ref[c, y], scratch, gather, y_elems)
    cur_ref[...] = cur
    lame_row, shear_row = material_rows(lame_ref, shear_ref)
    material_ref[...] = jnp.concatenate(
        [lame_row, shear_row, jnp.zeros((6, lanes), jnp.float32)], axis=0
    )
    planes = [cur[x * PLANE : (x + 1) * PLANE] for x in range(4)]
    edge = sum(dot(edge_ref[x], stacked(planes[x])) for x in range(4))
    right = edge_message(edge, lame_row, shear_row, z_elems)
    message, odd_ref[...] = select_messages(parity, cur[: 4 * BLOCK], right)
    even_ref[...], even_rest[...] = message[: 2 * BLOCK], message[2 * BLOCK :]
    weak = weak_ref[...]
    tangent = []
    for i in range(flags_ref.shape[0]):
        flag = flags_ref[i]
        tangent.append(
            jnp.where(flag == 0, lock_stiffness, jnp.where(flag == 1, -weak, 0.0))
        )
    for x in range(4):
        fault_out_ref[8 * x : 8 * x + 8] = fault_message(planes[x], z_elems)
    fault_out_ref[32:] = exact_dot(jnp.concatenate(tangent, axis=0), fault)
    for copy in copies[6:]:
        copy.wait()


def prepare_kernel(cur_ref, material_ref, own_ref, touch_ref, base_ref, edge_part_ref):
    cur = cur_ref[...]
    base_ref[...] = own_force(own_ref, cur, material_ref[0:1], material_ref[1:2])
    edge_part_ref[...] = dot(touch_ref[...], stacked(cur[:PLANE]))


def setup_kernel(next_ref, density_ref, mass_ref, fol_ref, minv_ref, scratch, *, y_elems, z_elems):
    gather = gather_table(y_elems * z_elems, z_elems)
    scratch[...] = jnp.zeros_like(scratch)
    fol_ref[...] = to_elements(lambda c, y: next_ref[c, y], scratch.at[0], gather, y_elems)
    density = to_elements(lambda c, y: density_ref[y], scratch.at[1], gather, y_elems, 2)
    table = mass_ref[...]
    first = lax.axis_index("dom") == 0
    plane = lax.broadcasted_iota(jnp.int32, table.shape, 0) < PLANE
    table = jnp.where(jnp.logical_and(first, plane), 2.0 * table, table)
    minv_ref[...] = jnp.where(table > 0.0, table / jnp.where(table > 0.0, density, 1.0), 0.0)


def fault_input(up_ref, down_ref, count):
    if down_ref is None:
        return up_ref[:count]
    up, down = up_ref[:count], down_ref[:count]
    row = lax.broadcasted_iota(jnp.int32, up.shape, 0)
    return jnp.where(row % 8 < 4, up, down)


def step_kernel(*refs, step, last, extra, last_place, pair, y_elems, z_elems):
    cur_ref, fol_ref, minv_ref, base_ref, touch_ref, material_ref, odd_ref, up_ref = refs[:8]
    refs = list(refs[8:])
    down_ref = None if pair else refs.pop(0)
    even_in = jnp.concatenate([refs.pop(0)[...], refs.pop(0)[...]], axis=0)
    first_up_ref, own_ref, first_own_ref, far_ref, edge_ref = refs[:5]
    refs = refs[5 + extra :]
    if last:
        back_ref, out_ref, scratch = refs
    else:
        new_ref, even_out, even_rest, odd_out, fault_out = refs
    place = lax.axis_index("dom")
    lanes = cur_ref.shape[1]
    even = place % 2 == 0
    far = jnp.where(place == last_place, 0.0, jnp.where(even, even_in, odd_ref[...]))
    left = jnp.where(place == 0, 0.0, jnp.where(even, odd_ref[...], even_in))
    lane_wide = lax.broadcasted_iota(jnp.int32, (BLOCK, lanes), 1)
    below = jnp.where(
        lane_wide % z_elems != z_elems - 1, pltpu.roll(far[:BLOCK], lanes - 1, 1), 0.0
    )
    far = stacked(jnp.concatenate([far, below], axis=0))
    lame_row, shear_row = material_ref[0:1], material_ref[1:2]
    left_lame = left[BLOCK - 1 : BLOCK]
    left_shear = left[2 * BLOCK - 1 : 2 * BLOCK]
    from_left = left_lame * touch_ref[:PLANE] + left_shear * touch_ref[PLANE:]
    row, lane = block_iotas(lanes)
    across = lane // z_elems
    shared = row < 3
    add_first = jnp.logical_and(shared, across > 0)
    take_last = jnp.logical_and(shared, across < y_elems - 1)
    pull_first = jnp.logical_and(shared, across == 0)
    pull_last = jnp.logical_and(shared, across == y_elems - 1)
    above = above_lanes(lanes, z_elems)
    fault_in = fault_input(up_ref, down_ref, 32)
    if not last:
        fault_out[32:] = jnp.zeros_like(fault_out[32:])
    planes = []
    edge = 0.0
    for x in range(4):
        rows = slice(x * PLANE, (x + 1) * PLANE)
        result = dot(far_ref[x], far)
        force = base_ref[rows] + (lame_row * result[:PLANE] + shear_row * result[PLANE:])
        blocks = [force[zl * BLOCK : (zl + 1) * BLOCK] for zl in range(5)]
        if x == 0:
            blocks = [b + from_left[i * BLOCK : (i + 1) * BLOCK] for i, b in enumerate(blocks)]
            blocks[:4] = [b + left[i * BLOCK : (i + 1) * BLOCK] for i, b in enumerate(blocks[:4])]
        blocks[0], blocks[4] = (
            blocks[0] + jnp.where(above, pltpu.roll(blocks[4], 1, 1), 0.0),
            blocks[4] + pltpu.roll(blocks[0], lanes - 1, 1),
        )
        at, k = slice(8 * x, 8 * x + 8), slice(32 + 4 * step + x, 33 + 4 * step + x)
        stiff = jnp.where(
            jnp.logical_or(row == 1, row == 5),
            lock_stiffness,
            jnp.where(row < 4, first_up_ref[k], first_own_ref[k]),
        )
        pulled = stiff * (fault_in[at] - pltpu.roll(own_ref[at], 4, 0))
        pulled_last = pltpu.roll(pulled, 4, 0)
        for zl in range(5):
            low, high = blocks[zl][:8], blocks[zl][8:]
            move = zl * z_elems if zl < 4 else 1
            blocks[zl] = jnp.concatenate(
                [
                    low
                    + jnp.where(add_first, shifted(high, z_elems), 0.0)
                    - jnp.where(pull_first, shifted(pulled, -move), 0.0),
                    high
                    + jnp.where(take_last, shifted(low, -z_elems), 0.0)
                    - jnp.where(pull_last, shifted(pulled_last, -move - z_elems), 0.0),
                ],
                axis=0,
            )
        plane = (2.0 * cur_ref[rows] - fol_ref[rows]) - minv_ref[rows] * jnp.concatenate(
            blocks, axis=0
        )
        if last:
            planes.append(plane)
        else:
            new_ref[rows] = plane
            fault_out[at] = fault_message(plane, z_elems)
            edge = edge + dot(edge_ref[x], stacked(plane))
            if x == 0:
                first = plane[: 4 * BLOCK]
    if last:
        from_elements(jnp.concatenate(planes, axis=0), scratch, back_ref, out_ref, y_elems)
    else:
        right = edge_message(edge, lame_row, shear_row, z_elems)
        message, odd_out[...] = select_messages(place % 2, first, right)
        even_out[...], even_rest[...] = message[: 2 * BLOCK], message[2 * BLOCK :]


def mask_kernel(owner_ref, _, back_ref, flags_ref, stress_ref, mask_ref, weight_ref, *, z_elems):
    shape = (PATCH_ROWS, mask_ref.shape[1])
    first = (lax.axis_index("dom") - REACH) * PATCH_DEV
    number = lax.broadcasted_iota(jnp.int32, shape, 0) + first
    for x in range(4):
        mask = jnp.where(number == owner_ref[0, x], 1.0, 0.0)
        mask_ref[PATCH_ROWS * x : PATCH_ROWS * (x + 1)] = mask
    stress = stress_ref[...]
    weights = []
    for i in range(flags_ref.shape[0]):
        flag = flags_ref[i]
        weights.append(
            stress * jnp.where(flag == 1, 0.5, jnp.where(flag == 2, 1.0, 0.0))
        )
    fault = fault_table(mask_ref.shape[1], z_elems)
    weight_ref[...] = exact_dot(jnp.concatenate(weights, axis=0), fault)


def output_kernel(*refs, pair, steps, y_elems, z_elems):
    field_ref, back_ref, weight_ref = refs[:3]
    out_ref, grad_ref, table_ref, scratch = refs[-4:]
    messages = refs[3:-4]
    count = 2 if pair else 3
    grads = [jnp.zeros((8, weight_ref.shape[1]), jnp.float32) for _ in range(4)]
    for i in range(steps):
        group = messages[count * i : count * (i + 1)]
        slip = -swap_rows(group[0][:32])
        if i < steps - 1:
            slip = slip + fault_input(group[1], None if pair else group[2], 32)
        for x in range(4):
            grads[x] = grads[x] + slip[8 * x : 8 * x + 8] * weight_ref[4 * i + x : 4 * i + x + 1]
    grad_ref[...] = jnp.concatenate(grads, axis=0)
    table_ref[...] = fault_table_back(weight_ref.shape[1], z_elems)
    from_elements(field_ref[...], scratch, back_ref, out_ref, y_elems)


def patch_kernel(*refs, pair, steps):
    mask_ref, weight_ref, grad_ref, table_ref, _, up_ref = refs[:6]
    down_ref = None if pair else refs[6]
    home_out, out_a, out_b, out_c, out_d = refs[-5:]
    place = lax.axis_index("dom")
    slip = fault_input(up_ref, down_ref, 32)
    total = 0.0
    for x in range(4):
        at, k = 8 * x + 4, 4 * (steps - 1) + x
        grad = grad_ref[at : at + 1] + slip[at : at + 1] * weight_ref[k : k + 1]
        total = total + mask_ref[PATCH_ROWS * x : PATCH_ROWS * (x + 1)] * grad
    total = exact_dot(total, table_ref[...])
    rows = [total[2 * i : 2 * i + 2] for i in range(5)]
    home_out[...] = rows[2]
    even = place % 2 == 0
    out_a[...] = jnp.where(even, rows[3], rows[1])
    out_b[...] = jnp.where(even, rows[1], rows[3])
    low = place % 4 < 2
    out_c[...] = jnp.where(low, rows[4], rows[0])
    out_d[...] = jnp.where(low, rows[0], rows[4])


VMEM = pl.BlockSpec(memory_space=pltpu.VMEM)
HBM = pl.BlockSpec(memory_space=pltpu.HBM)
SMEM = pl.BlockSpec(memory_space=pltpu.SMEM)
ANY = pl.BlockSpec(memory_space=pl.ANY)


def kernel_call(body, outs, args, in_smem=(), scratch=(), in_hbm=(), kept=(), unread=(), **static):
    shapes = []
    for out in outs:
        shape, dtype = out if isinstance(out[0], tuple) else (out, jnp.float32)
        shapes.append((pltpu.VMEM if in_hbm else jax.ShapeDtypeStruct)(shape, dtype))
    specs = [VMEM] * len(args)
    for places, spec in ((in_smem, SMEM), (in_hbm, HBM), (unread, ANY)):
        for i in places:
            specs[i] = spec
    copied = [pltpu.VMEM(args[i].shape, args[i].dtype) for i in in_hbm if i not in kept]
    if in_hbm:
        copied.append(pltpu.SemaphoreType.DMA((len(in_hbm),)))
    return pl.pallas_call(
        functools.partial(body, **static) if static else body,
        out_shape=shapes,
        in_specs=specs,
        out_specs=[VMEM] * len(shapes),
        scratch_shapes=list(scratch) + copied,
        compiler_params=pltpu.CompilerParams(
            vmem_limit_bytes=(56 if in_hbm else 24) * 2**20
        ),
    )(*args)


def swapped(block, distance, group):
    size, across = lax.axis_size("dom"), lax.axis_size("depth")
    partner = {}
    for left in range(size - distance):
        if left // distance % 2 == group:
            partner[left], partner[left + distance] = left + distance, left
    route = []
    for i in range(size):
        for j in range(across):
            side = j if i in partner else min(j ^ 1, across - 1)
            route.append((i * across + j, partner.get(i, i) * across + side))
    return lax.ppermute(block, ("dom", "depth"), route)


def from_behind(block, axis, distance):
    size = lax.axis_size(axis)
    return lax.ppermute(block, axis, [((i - distance) % size, i) for i in range(size)])


def on_device(
    adjoint_now,
    adjoint_next,
    lame_first,
    shear_modulus,
    density,
    branch_flags,
    weak_slope,
    normal_stress,
    patch_owner,
):
    x_elems, y_elems, z_elems = lame_first.shape
    lanes = y_elems * z_elems
    assert x_elems == 1 and lanes == adjoint_now.shape[3]
    steps = branch_flags.shape[0]
    pair = lax.axis_size("depth") == 2
    own_table, far_table, edge_table, touch_table = (jnp.asarray(t) for t in stiffness_tables())
    back = jnp.asarray(back_table(y_elems, z_elems))
    mass = jnp.asarray(mass_table(y_elems, z_elems))
    now = jnp.transpose(adjoint_now, (0, 2, 1, 3))
    following = jnp.transpose(adjoint_next, (0, 2, 1, 3))
    rho = jnp.transpose(density, (1, 0, 2))
    flags = branch_flags[:, 0]
    native = pltpu.VMEM((y_elems, 4 * BLOCK, lanes), jnp.float32)
    field = (4 * PLANE, lanes)
    plane = (4 * BLOCK, lanes)
    half = (2 * BLOCK, lanes)

    def exchange(even, odd, fault_rows):
        if pair:
            faults = [from_behind(fault_rows, "depth", 1)]
        else:
            faults = [from_behind(fault_rows, "depth", 1), from_behind(fault_rows, "depth", -1)]
        return [swapped(part, 1, 0) for part in even], swapped(odd, 1, 1), faults

    later_used = (edge_table, following, rho, mass, own_table, far_table, touch_table)
    assert len(later_used) == LATER
    cur, *even, odd, fault_rows, material, edge_table, following, rho, mass, own_table, far_table, touch_table = kernel_call(
        first_kernel,
        [field, half, half, plane, (32 + 4 * steps, lanes), (8, lanes)]
        + [(t.shape, t.dtype) for t in later_used],
        (now, flags, weak_slope[0], lame_first[0], shear_modulus[0]) + later_used,
        scratch=[native],
        in_hbm=range(5 + LATER),
        kept=range(5, 5 + LATER),
    )
    even_in, odd_in, fault_in = exchange(even, odd, fault_rows)
    first_fault, first_in = fault_rows, fault_in
    fol, minv = kernel_call(
        setup_kernel,
        [field, field],
        (following, rho, mass),
        scratch=[pltpu.VMEM((2, y_elems, 4 * BLOCK, lanes), jnp.float32)],
        y_elems=y_elems,
        z_elems=z_elems,
    )
    seen = []
    for step in range(steps):
        last = step == steps - 1
        seen += [fault_rows] + fault_in
        base, touch = kernel_call(
            prepare_kernel,
            [field, (2 * PLANE, lanes)],
            [cur, material, own_table, touch_table],
            (),
        )
        args = [cur, fol, minv, base, touch, material, odd_in] + fault_in + even_in
        args += [first_in[0], fault_rows, first_fault, far_table, edge_table]
        static = dict(
            step=step, last=last, extra=1 if last or step == 1 else 0, last_place=lax.axis_size("dom") - 1, pair=pair, y_elems=y_elems,
            z_elems=z_elems,
        )
        if step == 1:
            mask, weight = kernel_call(
                mask_kernel,
                [(4 * PATCH_ROWS, lanes), (4 * steps, lanes)],
                [patch_owner, cur, back, flags, normal_stress[0]],
                (0,),
                unread=(1,),
                z_elems=z_elems,
            )
            args.append(mask)
        if not last:
            new, *even, odd, new_fault = kernel_call(
                step_kernel,
                [field, half, half, plane, (40, lanes)],
                args,
                unread=(len(args) - 1,) if step == 1 else (),
                **static,
            )
            fol, cur, fault_rows = cur, new, new_fault
            even_in, odd_in, fault_in = exchange(even, odd, fault_rows)
        else:
            whole = (3, 4 * y_elems + 1, 4, lanes)
            known = seen[: len(seen) - len(fault_in)]
            later, grad, table = kernel_call(
                output_kernel,
                [whole, (32, lanes), ((lanes, lanes), jnp.bfloat16)],
                [cur, back, weight] + known,
                (),
                [native],
                pair=pair,
                steps=steps,
                y_elems=y_elems,
                z_elems=z_elems,
            )
            sums = kernel_call(
                patch_kernel,
                [(PATCH_DEV, lanes)] * 5,
                [mask, weight, grad, table, odd_in] + fault_in + even_in + [touch],
                unread=(4,) + tuple(range(5 + len(fault_in), 8 + len(fault_in))),
                pair=pair,
                steps=steps,
            )
            patch_sums = sums[0]
            for i, distance, group in ((2, 1, 1), (4, 2, 1), (3, 2, 0), (1, 1, 0)):
                patch_sums = patch_sums + swapped(sums[i], distance, group)
            earlier = kernel_call(
                step_kernel,
                [whole],
                args + [sums[0], back],
                scratch=[native],
                unread=(len(args),),
                **static,
            )[0]
    return (
        jnp.transpose(earlier, (0, 2, 1, 3)),
        jnp.transpose(later, (0, 2, 1, 3)),
        patch_sums[None],
    )


def solution(mesh):
    return jax.shard_map(
        on_device,
        mesh=mesh,
        in_specs=(
            P(None, "dom", "depth", None),
            P(None, "dom", "depth", None),
            P("dom", "depth", None),
            P("dom", "depth", None),
            P("dom", "depth", None),
            P(None, "depth", "dom", None),
            P("depth", "dom", None),
            P("depth", "dom", None),
            P("depth", "dom"),
        ),
        out_specs=(
            P(None, "dom", "depth", None),
            P(None, "dom", "depth", None),
            P("depth", "dom", None),
        ),
        check_vma=False,
    )
```

```python
import functools
import math

import jax
import jax.numpy as jnp
import ml_dtypes
import numpy as np
from jax import lax
from jax.experimental import pallas as pl
from jax.experimental.pallas import tpu as pltpu
from jax.sharding import PartitionSpec as P

PATCH_DEV = 2
REACH = 2
PATCH_ROWS = 16
LATER = 7

time_step = 0.01
lock_stiffness = 0.5

BLOCK = 16
ROWS = ((0, 1, 2), (3, 4, 5), (11, 12, 13), (6, 7, 14), (8, 9, 10))
PLANE = 5 * BLOCK


def basis_tables():
    points = [-1.0, -math.sqrt(3.0 / 7.0), 0.0, math.sqrt(3.0 / 7.0), 1.0]
    quad_weights = np.array([0.1, 49.0 / 90.0, 32.0 / 45.0, 49.0 / 90.0, 0.1])
    products = []
    for first in range(5):
        value = 1.0
        for other in range(5):
            if other != first:
                value = value * (points[first] - points[other])
        products.append(value)
    derivative = np.zeros((5, 5))
    for row in range(5):
        for column in range(5):
            if row == column:
                total = 0.0
                for other in range(5):
                    if other != row:
                        total = total + 1.0 / (points[row] - points[other])
                derivative[row, column] = total
            else:
                derivative[row, column] = (
                    products[row] / products[column] / (points[row] - points[column])
                )
    return (quad_weights, derivative)


def two_parts(table):
    high = table.astype(ml_dtypes.bfloat16)
    low = (table - high.astype(np.float64)).astype(ml_dtypes.bfloat16)
    return np.stack([high, low])


def element_stiffness():
    weights, derivative = basis_tables()
    eye = np.eye(5)
    slope = 2.0 * derivative
    grads = [
        np.kron(slope, np.kron(eye, eye)),
        np.kron(eye, np.kron(eye, slope)),
        np.kron(eye, np.kron(slope, eye)),
    ]
    quad = np.kron(weights, np.kron(weights, weights)) / 8.0
    first = np.zeros((125, 3, 125, 3))
    second = np.zeros((125, 3, 125, 3))
    lap = sum(g.T @ (quad[:, None] * g) for g in grads)
    for c in range(3):
        second[:, c, :, c] += lap
        for d in range(3):
            first[:, c, :, d] += grads[c].T @ (quad[:, None] * grads[d])
            second[:, c, :, d] += grads[d].T @ (quad[:, None] * grads[c])
    where = [
        node // 5 * BLOCK + ROWS[node % 5][c] for node in range(125) for c in range(3)
    ]
    wide = []
    for small in (first, second):
        big = np.zeros((5 * PLANE, 5 * PLANE))
        big[np.ix_(where, where)] = small.reshape(375, 375)
        wide.append(big)
    return wide


OWN_COLS = 384


def padded_table(table, columns):
    return np.pad(table, ((0, 0), (0, columns - table.shape[1])))


@functools.cache
def stiffness_tables():
    wide = element_stiffness()
    own = 4 * PLANE
    planes = [slice(x * PLANE, (x + 1) * PLANE) for x in range(5)]
    inner = np.concatenate([w[:own, :own] for w in wide])

    def three(table):
        high, low = two_parts(table)
        return padded_table(np.concatenate([high, low, high], axis=1), 256)

    def both(rows, columns):
        return three(np.concatenate([w[rows, columns] for w in wide]))

    return (
        two_parts(padded_table(inner, OWN_COLS)),
        np.concatenate([three(w[:own, planes[4]]) for w in wide], axis=1),
        np.concatenate([both(planes[4], planes[x]) for x in range(4)], axis=1),
        both(planes[4], planes[4]),
    )


@functools.cache
def back_table(y_elems, z_elems):
    lanes = y_elems * z_elems
    depth = 4 * z_elems
    back = np.zeros((4 * lanes, y_elems * depth), ml_dtypes.bfloat16)
    for yel in range(y_elems):
        for k in range(z_elems):
            for zl in range(4):
                back[zl * lanes + yel * z_elems + k, yel * depth + 4 * k + zl] = 1
    return back


@functools.cache
def mass_table(y_elems, z_elems):
    weights, _ = basis_tables()
    table = np.zeros((4, 5, BLOCK, y_elems, z_elems))
    for x in range(4):
        mx = 0.2 if x == 0 else weights[x]
        for zl in range(5):
            for yl in range(5):
                for yel in range(y_elems):
                    my = weights[yl]
                    if (yl == 0 and yel > 0) or (yl == 4 and yel < y_elems - 1):
                        my = 0.2
                    mz = np.full(z_elems, weights[zl])
                    if zl == 0:
                        mz[1:] = 0.2
                    if zl == 4:
                        mz[:] = 0.2
                    value = time_step * time_step * 8.0 / (mx * my * mz)
                    if zl == 4:
                        value[-1] = 0.0
                    table[x, zl, list(ROWS[yl]), yel] = value
    return table.reshape(4 * PLANE, y_elems * z_elems).astype(np.float32)


def pieces(value, count):
    out = []
    for _ in range(count):
        piece = value.astype(jnp.bfloat16)
        out.append(piece)
        value = value - piece.astype(jnp.float32)
    return out


def dot(a, b):
    return jnp.dot(a, b, preferred_element_type=jnp.float32)


def exact_dot(value, table, count=3):
    rows = value.shape[0]
    result = dot(jnp.concatenate(pieces(value, count), axis=0), table)
    total = result[:rows]
    for i in range(1, count):
        total = total + result[i * rows : (i + 1) * rows]
    return total


def split_dot(table_high, table_low, value):
    lanes = value.shape[1]
    high, low = pieces(value, 2)
    wide = dot(table_high, jnp.concatenate([high, low], axis=1))
    return wide[:, :lanes] + (wide[:, lanes:] + dot(table_low, high))


def ones_where(rule, shape):
    row = lax.broadcasted_iota(jnp.int32, shape, 0)
    column = lax.broadcasted_iota(jnp.int32, shape, 1)
    return jnp.where(rule(row, column), 1.0, 0.0).astype(jnp.bfloat16)


def gather_table(lanes, z_elems):
    return ones_where(lambda z, c: z == 4 * (c % z_elems) + c // lanes, (lanes, 5 * lanes))


def fault_table(lanes, z_elems):
    return ones_where(lambda z, c: z == 4 * (c % z_elems) + c // z_elems, (lanes, lanes))


def fault_table_back(lanes, z_elems):
    return ones_where(lambda c, z: z == 4 * (c % z_elems) + c // z_elems, (lanes, lanes))


def stacked(value):
    high, low = pieces(value, 2)
    gap = jnp.zeros((256 - 3 * value.shape[0], value.shape[1]), jnp.bfloat16)
    return jnp.concatenate([high, high, low, gap], axis=0)


def to_elements(native, scratch, table, y_elems, parts=3):
    group = 4 * BLOCK
    for c in range(3):
        for y in range(4 * y_elems + 1):
            rows = native(c, y)
            if y < 4 * y_elems:
                scratch[y // 4, pl.ds(ROWS[y % 4][c], 4, stride=BLOCK), :] = rows
            if y % 4 == 0 and y > 0:
                scratch[y // 4 - 1, pl.ds(ROWS[4][c], 4, stride=BLOCK), :] = rows
    high, middle, *low = pieces(
        jnp.concatenate([scratch[i] for i in range(y_elems)], axis=0), parts
    )
    result = dot(
        jnp.concatenate([high, middle], axis=1), jnp.concatenate([table, table], axis=0)
    )
    for piece in low:
        result = result + dot(piece, table)
    lanes = result.shape[1] // 5
    across = lax.broadcasted_iota(jnp.int32, (group, result.shape[1]), 1) % lanes // (
        lanes // y_elems
    )
    total = result[:group]
    for yel in range(1, y_elems):
        total = jnp.where(across == yel, result[yel * group : (yel + 1) * group], total)
    blocks = []
    for x in range(4):
        for zl in range(5):
            blocks.append(total[x * BLOCK : (x + 1) * BLOCK, zl * lanes : (zl + 1) * lanes])
    return jnp.concatenate(blocks, axis=0)


def from_elements(field, scratch, back_ref, out_ref, y_elems):
    rows = []
    for x in range(4):
        rows.append(
            jnp.concatenate(
                [field[x * PLANE + zl * BLOCK : x * PLANE + (zl + 1) * BLOCK] for zl in range(4)],
                axis=1,
            )
        )
    result = exact_dot(jnp.concatenate(rows, axis=0), back_ref[...])
    depth = result.shape[1] // y_elems
    for yel in range(y_elems):
        scratch[yel] = result[:, yel * depth : (yel + 1) * depth]
    for c in range(3):
        for y in range(4 * y_elems + 1):
            yel, yl = (y // 4, y % 4) if y < 4 * y_elems else (y_elems - 1, 4)
            out_ref[c, y] = scratch[yel, pl.ds(ROWS[yl][c], 4, stride=BLOCK), :]


def shifted(rows, lanes):
    lanes = lanes % rows.shape[1]
    return pltpu.roll(rows, lanes, 1) if lanes else rows


def block_iotas(lanes):
    return (
        lax.broadcasted_iota(jnp.int32, (8, lanes), 0),
        lax.broadcasted_iota(jnp.int32, (8, lanes), 1),
    )


def fault_message(plane, z_elems):
    lanes = plane.shape[1]
    row, lane = block_iotas(lanes)
    first = last = jnp.zeros((8, lanes), jnp.float32)
    for zl in range(4):
        at = zl * BLOCK
        here = lane // z_elems == zl
        first = jnp.where(here, shifted(plane[at : at + 8], zl * z_elems), first)
        last = jnp.where(here, shifted(plane[at + 8 : at + 16], (zl + 1) * z_elems), last)
    return jnp.where(row < 4, last, pltpu.roll(first, 4, 0))


def swap_rows(message):
    parts = [pltpu.roll(message[i : i + 8], 4, 0) for i in range(0, message.shape[0], 8)]
    return jnp.concatenate(parts, axis=0)


def select_messages(parity, left, right):
    even = parity == 0
    return jnp.where(even, right, left), jnp.where(even, left, right)


def material_rows(lame_ref, shear_ref):
    y_elems, z_elems = lame_ref.shape
    both = jnp.concatenate([lame_ref[...], shear_ref[...]], axis=0)
    spread = ones_where(lambda k, c: c % z_elems == k, (z_elems, y_elems * z_elems))
    tiled = exact_dot(both, spread)
    row = lax.broadcasted_iota(jnp.int32, tiled.shape, 0)
    lane = lax.broadcasted_iota(jnp.int32, tiled.shape, 1)
    kept = jnp.where(row % y_elems == lane // z_elems, tiled, 0.0)
    return (
        jnp.sum(kept[:y_elems], axis=0, keepdims=True),
        jnp.sum(kept[y_elems:], axis=0, keepdims=True),
    )


def above_lanes(lanes, z_elems):
    return lax.broadcasted_iota(jnp.int32, (BLOCK, lanes), 1) % z_elems != 0


def edge_message(result, lame_row, shear_row, z_elems):
    lanes = result.shape[1]
    force = lame_row * result[:PLANE] + shear_row * result[PLANE:]
    top = force[:BLOCK] + jnp.where(
        above_lanes(lanes, z_elems), pltpu.roll(force[4 * BLOCK :], 1, 1), 0.0
    )
    row = lax.broadcasted_iota(jnp.int32, top.shape, 0)
    top = jnp.where(row == BLOCK - 1, lame_row, top)
    second = jnp.where(row == BLOCK - 1, shear_row, force[BLOCK : 2 * BLOCK])
    return jnp.concatenate([top, second, force[2 * BLOCK : 4 * BLOCK]], axis=0)


def own_force(own_ref, cur, lame_row, shear_row):
    rows, lanes = cur.shape
    padded = jnp.concatenate([cur, jnp.zeros((OWN_COLS - rows, lanes), jnp.float32)], axis=0)
    result = split_dot(own_ref[0], own_ref[1], padded)
    return lame_row * result[:rows] + shear_row * result[rows:]


def start_copies(pairs, sems):
    copies = [
        pltpu.make_async_copy(source, target, sems.at[i])
        for i, (source, target) in enumerate(pairs)
    ]
    for copy in copies:
        copy.start()
    return copies


def first_kernel(
    now_hbm,
    flags_hbm,
    weak_hbm,
    lame_hbm,
    shear_hbm,
    *refs,
):
    later_hbm, refs = refs[:LATER], refs[LATER:]
    cur_ref, even_ref, even_rest, odd_ref, fault_out_ref, material_ref = refs[:6]
    later_refs, refs = refs[6 : 6 + LATER], refs[6 + LATER :]
    scratch, now_ref, flags_ref, weak_ref, lame_ref, shear_ref, sems = refs
    copies = start_copies(
        [
            (flags_hbm, flags_ref),
            (weak_hbm, weak_ref),
            (lame_hbm, lame_ref),
            (shear_hbm, shear_ref),
            (now_hbm, now_ref),
        ]
        + list(zip(later_hbm, later_refs)),
        sems,
    )
    edge_ref = later_refs[0]
    y_elems, z_elems = lame_ref.shape
    lanes = y_elems * z_elems
    parity = lax.axis_index("dom") % 2
    gather = gather_table(lanes, z_elems)
    fault = fault_table(lanes, z_elems)
    scratch[...] = jnp.zeros_like(scratch)
    for copy in copies[:6]:
        copy.wait()
    cur = to_elements(lambda c, y: now_ref[c, y], scratch, gather, y_elems)
    cur_ref[...] = cur
    lame_row, shear_row = material_rows(lame_ref, shear_ref)
    material_ref[...] = jnp.concatenate(
        [lame_row, shear_row, jnp.zeros((6, lanes), jnp.float32)], axis=0
    )
    planes = [cur[x * PLANE : (x + 1) * PLANE] for x in range(4)]
    edge = dot(edge_ref[...], jnp.concatenate([stacked(p) for p in planes], axis=0))
    right = edge_message(edge, lame_row, shear_row, z_elems)
    message, odd_ref[...] = select_messages(parity, cur[: 4 * BLOCK], right)
    even_ref[...], even_rest[...] = message[: 2 * BLOCK], message[2 * BLOCK :]
    weak = weak_ref[...]
    tangent = []
    for i in range(flags_ref.shape[0]):
        flag = flags_ref[i]
        tangent.append(
            jnp.where(flag == 0, lock_stiffness, jnp.where(flag == 1, -weak, 0.0))
        )
    for x in range(4):
        fault_out_ref[8 * x : 8 * x + 8] = fault_message(planes[x], z_elems)
    fault_out_ref[32:] = exact_dot(jnp.concatenate(tangent, axis=0), fault)
    for copy in copies[6:]:
        copy.wait()


def prepare_kernel(cur_ref, material_ref, own_ref, touch_ref, base_ref, edge_part_ref):
    cur = cur_ref[...]
    base_ref[...] = own_force(own_ref, cur, material_ref[0:1], material_ref[1:2])
    edge_part_ref[...] = dot(touch_ref[...], stacked(cur[:PLANE]))


def setup_kernel(next_ref, density_ref, mass_ref, fol_ref, minv_ref, scratch, *, y_elems, z_elems):
    gather = gather_table(y_elems * z_elems, z_elems)
    scratch[...] = jnp.zeros_like(scratch)
    fol_ref[...] = to_elements(lambda c, y: next_ref[c, y], scratch.at[0], gather, y_elems)
    density = to_elements(lambda c, y: density_ref[y], scratch.at[1], gather, y_elems, 2)
    table = mass_ref[...]
    first = lax.axis_index("dom") == 0
    plane = lax.broadcasted_iota(jnp.int32, table.shape, 0) < PLANE
    table = jnp.where(jnp.logical_and(first, plane), 2.0 * table, table)
    minv_ref[...] = jnp.where(table > 0.0, table / jnp.where(table > 0.0, density, 1.0), 0.0)


def fault_input(up_ref, down_ref, count):
    if down_ref is None:
        return up_ref[:count]
    up, down = up_ref[:count], down_ref[:count]
    row = lax.broadcasted_iota(jnp.int32, up.shape, 0)
    return jnp.where(row % 8 < 4, up, down)


def step_kernel(*refs, step, last, extra, last_place, pair, y_elems, z_elems):
    cur_ref, fol_ref, minv_ref, base_ref, touch_ref, material_ref, odd_ref, up_ref = refs[:8]
    refs = list(refs[8:])
    down_ref = None if pair else refs.pop(0)
    even_in = jnp.concatenate([refs.pop(0)[...], refs.pop(0)[...]], axis=0)
    first_up_ref, own_ref, first_own_ref, far_ref, edge_ref = refs[:5]
    refs = refs[5 + extra :]
    if last:
        back_ref, out_ref, scratch = refs
    else:
        new_ref, even_out, even_rest, odd_out, fault_out = refs
    place = lax.axis_index("dom")
    lanes = cur_ref.shape[1]
    even = place % 2 == 0
    far = jnp.where(place == last_place, 0.0, jnp.where(even, even_in, odd_ref[...]))
    left = jnp.where(place == 0, 0.0, jnp.where(even, odd_ref[...], even_in))
    lane_wide = lax.broadcasted_iota(jnp.int32, (BLOCK, lanes), 1)
    below = jnp.where(
        lane_wide % z_elems != z_elems - 1, pltpu.roll(far[:BLOCK], lanes - 1, 1), 0.0
    )
    far = jnp.concatenate([far, below], axis=0)
    lame_row, shear_row = material_ref[0:1], material_ref[1:2]
    far = jnp.concatenate([stacked(lame_row * far), stacked(shear_row * far)], axis=0)
    left_lame = left[BLOCK - 1 : BLOCK]
    left_shear = left[2 * BLOCK - 1 : 2 * BLOCK]
    from_left = left_lame * touch_ref[:PLANE] + left_shear * touch_ref[PLANE:]
    row, lane = block_iotas(lanes)
    across = lane // z_elems
    shared = row < 3
    add_first = jnp.logical_and(shared, across > 0)
    take_last = jnp.logical_and(shared, across < y_elems - 1)
    pull_first = jnp.logical_and(shared, across == 0)
    pull_last = jnp.logical_and(shared, across == y_elems - 1)
    above = above_lanes(lanes, z_elems)
    fault_in = fault_input(up_ref, down_ref, 32)
    if not last:
        fault_out[32:] = jnp.zeros_like(fault_out[32:])
    planes = []
    for x in range(4):
        rows = slice(x * PLANE, (x + 1) * PLANE)
        force = base_ref[rows] + dot(far_ref[rows], far)
        blocks = [force[zl * BLOCK : (zl + 1) * BLOCK] for zl in range(5)]
        if x == 0:
            blocks = [b + from_left[i * BLOCK : (i + 1) * BLOCK] for i, b in enumerate(blocks)]
            blocks[:4] = [b + left[i * BLOCK : (i + 1) * BLOCK] for i, b in enumerate(blocks[:4])]
        blocks[0], blocks[4] = (
            blocks[0] + jnp.where(above, pltpu.roll(blocks[4], 1, 1), 0.0),
            blocks[4] + pltpu.roll(blocks[0], lanes - 1, 1),
        )
        at, k = slice(8 * x, 8 * x + 8), slice(32 + 4 * step + x, 33 + 4 * step + x)
        stiff = jnp.where(
            jnp.logical_or(row == 1, row == 5),
            lock_stiffness,
            jnp.where(row < 4, first_up_ref[k], first_own_ref[k]),
        )
        pulled = stiff * (fault_in[at] - pltpu.roll(own_ref[at], 4, 0))
        pulled_last = pltpu.roll(pulled, 4, 0)
        for zl in range(5):
            low, high = blocks[zl][:8], blocks[zl][8:]
            move = zl * z_elems if zl < 4 else 1
            blocks[zl] = jnp.concatenate(
                [
                    low
                    + jnp.where(add_first, shifted(high, z_elems), 0.0)
                    - jnp.where(pull_first, shifted(pulled, -move), 0.0),
                    high
                    + jnp.where(take_last, shifted(low, -z_elems), 0.0)
                    - jnp.where(pull_last, shifted(pulled_last, -move - z_elems), 0.0),
                ],
                axis=0,
            )
        plane = (2.0 * cur_ref[rows] - fol_ref[rows]) - minv_ref[rows] * jnp.concatenate(
            blocks, axis=0
        )
        if last:
            planes.append(plane)
        else:
            new_ref[rows] = plane
            fault_out[at] = fault_message(plane, z_elems)
            planes.append(stacked(plane))
            if x == 0:
                first = plane[: 4 * BLOCK]
    if last:
        from_elements(jnp.concatenate(planes, axis=0), scratch, back_ref, out_ref, y_elems)
    else:
        edge = dot(edge_ref[...], jnp.concatenate(planes, axis=0))
        right = edge_message(edge, lame_row, shear_row, z_elems)
        message, odd_out[...] = select_messages(place % 2, first, right)
        even_out[...], even_rest[...] = message[: 2 * BLOCK], message[2 * BLOCK :]


def mask_kernel(owner_ref, _, back_ref, flags_ref, stress_ref, mask_ref, weight_ref, *, z_elems):
    shape = (PATCH_ROWS, mask_ref.shape[1])
    first = (lax.axis_index("dom") - REACH) * PATCH_DEV
    number = lax.broadcasted_iota(jnp.int32, shape, 0) + first
    for x in range(4):
        mask = jnp.where(number == owner_ref[0, x], 1.0, 0.0)
        mask_ref[PATCH_ROWS * x : PATCH_ROWS * (x + 1)] = mask
    stress = stress_ref[...]
    weights = []
    for i in range(flags_ref.shape[0]):
        flag = flags_ref[i]
        weights.append(
            stress * jnp.where(flag == 1, 0.5, jnp.where(flag == 2, 1.0, 0.0))
        )
    fault = fault_table(mask_ref.shape[1], z_elems)
    weight_ref[...] = exact_dot(jnp.concatenate(weights, axis=0), fault)


def output_kernel(*refs, pair, steps, y_elems, z_elems):
    field_ref, back_ref, weight_ref = refs[:3]
    out_ref, grad_ref, table_ref, scratch = refs[-4:]
    messages = refs[3:-4]
    count = 2 if pair else 3
    grads = [jnp.zeros((8, weight_ref.shape[1]), jnp.float32) for _ in range(4)]
    for i in range(steps):
        group = messages[count * i : count * (i + 1)]
        slip = -swap_rows(group[0][:32])
        if i < steps - 1:
            slip = slip + fault_input(group[1], None if pair else group[2], 32)
        for x in range(4):
            grads[x] = grads[x] + slip[8 * x : 8 * x + 8] * weight_ref[4 * i + x : 4 * i + x + 1]
    grad_ref[...] = jnp.concatenate(grads, axis=0)
    table_ref[...] = fault_table_back(weight_ref.shape[1], z_elems)
    from_elements(field_ref[...], scratch, back_ref, out_ref, y_elems)


def patch_kernel(*refs, pair, steps):
    mask_ref, weight_ref, grad_ref, table_ref, _, up_ref = refs[:6]
    down_ref = None if pair else refs[6]
    home_out, out_a, out_b, out_c, out_d = refs[-5:]
    place = lax.axis_index("dom")
    slip = fault_input(up_ref, down_ref, 32)
    total = 0.0
    for x in range(4):
        at, k = 8 * x + 4, 4 * (steps - 1) + x
        grad = grad_ref[at : at + 1] + slip[at : at + 1] * weight_ref[k : k + 1]
        total = total + mask_ref[PATCH_ROWS * x : PATCH_ROWS * (x + 1)] * grad
    total = exact_dot(total, table_ref[...])
    rows = [total[2 * i : 2 * i + 2] for i in range(5)]
    home_out[...] = rows[2]
    even = place % 2 == 0
    out_a[...] = jnp.where(even, rows[3], rows[1])
    out_b[...] = jnp.where(even, rows[1], rows[3])
    low = place % 4 < 2
    out_c[...] = jnp.where(low, rows[4], rows[0])
    out_d[...] = jnp.where(low, rows[0], rows[4])


VMEM = pl.BlockSpec(memory_space=pltpu.VMEM)
HBM = pl.BlockSpec(memory_space=pltpu.HBM)
SMEM = pl.BlockSpec(memory_space=pltpu.SMEM)
ANY = pl.BlockSpec(memory_space=pl.ANY)


def kernel_call(body, outs, args, in_smem=(), scratch=(), in_hbm=(), kept=(), unread=(), **static):
    shapes = []
    for out in outs:
        shape, dtype = out if isinstance(out[0], tuple) else (out, jnp.float32)
        shapes.append((pltpu.VMEM if in_hbm else jax.ShapeDtypeStruct)(shape, dtype))
    specs = [VMEM] * len(args)
    for places, spec in ((in_smem, SMEM), (in_hbm, HBM), (unread, ANY)):
        for i in places:
            specs[i] = spec
    copied = [pltpu.VMEM(args[i].shape, args[i].dtype) for i in in_hbm if i not in kept]
    if in_hbm:
        copied.append(pltpu.SemaphoreType.DMA((len(in_hbm),)))
    return pl.pallas_call(
        functools.partial(body, **static) if static else body,
        out_shape=shapes,
        in_specs=specs,
        out_specs=[VMEM] * len(shapes),
        scratch_shapes=list(scratch) + copied,
        compiler_params=pltpu.CompilerParams(
            vmem_limit_bytes=(56 if in_hbm else 24) * 2**20
        ),
    )(*args)


def swapped(block, distance, group):
    size, across = lax.axis_size("dom"), lax.axis_size("depth")
    partner = {}
    for left in range(size - distance):
        if left // distance % 2 == group:
            partner[left], partner[left + distance] = left + distance, left
    route = []
    for i in range(size):
        for j in range(across):
            side = j if i in partner else min(j ^ 1, across - 1)
            route.append((i * across + j, partner.get(i, i) * across + side))
    return lax.ppermute(block, ("dom", "depth"), route)


def from_behind(block, axis, distance):
    size = lax.axis_size(axis)
    return lax.ppermute(block, axis, [((i - distance) % size, i) for i in range(size)])


def on_device(
    adjoint_now,
    adjoint_next,
    lame_first,
    shear_modulus,
    density,
    branch_flags,
    weak_slope,
    normal_stress,
    patch_owner,
):
    x_elems, y_elems, z_elems = lame_first.shape
    lanes = y_elems * z_elems
    assert x_elems == 1 and lanes == adjoint_now.shape[3]
    steps = branch_flags.shape[0]
    pair = lax.axis_size("depth") == 2
    own_table, far_table, edge_table, touch_table = (jnp.asarray(t) for t in stiffness_tables())
    back = jnp.asarray(back_table(y_elems, z_elems))
    mass = jnp.asarray(mass_table(y_elems, z_elems))
    now = jnp.transpose(adjoint_now, (0, 2, 1, 3))
    following = jnp.transpose(adjoint_next, (0, 2, 1, 3))
    rho = jnp.transpose(density, (1, 0, 2))
    flags = branch_flags[:, 0]
    native = pltpu.VMEM((y_elems, 4 * BLOCK, lanes), jnp.float32)
    field = (4 * PLANE, lanes)
    plane = (4 * BLOCK, lanes)
    half = (2 * BLOCK, lanes)

    def exchange(even, odd, fault_rows):
        if pair:
            faults = [from_behind(fault_rows, "depth", 1)]
        else:
            faults = [from_behind(fault_rows, "depth", 1), from_behind(fault_rows, "depth", -1)]
        return [swapped(part, 1, 0) for part in even], swapped(odd, 1, 1), faults

    later_used = (edge_table, following, rho, mass, own_table, far_table, touch_table)
    assert len(later_used) == LATER
    cur, *even, odd, fault_rows, material, edge_table, following, rho, mass, own_table, far_table, touch_table = kernel_call(
        first_kernel,
        [field, half, half, plane, (32 + 4 * steps, lanes), (8, lanes)]
        + [(t.shape, t.dtype) for t in later_used],
        (now, flags, weak_slope[0], lame_first[0], shear_modulus[0]) + later_used,
        scratch=[native],
        in_hbm=range(5 + LATER),
        kept=range(5, 5 + LATER),
    )
    even_in, odd_in, fault_in = exchange(even, odd, fault_rows)
    first_fault, first_in = fault_rows, fault_in
    fol, minv = kernel_call(
        setup_kernel,
        [field, field],
        (following, rho, mass),
        scratch=[pltpu.VMEM((2, y_elems, 4 * BLOCK, lanes), jnp.float32)],
        y_elems=y_elems,
        z_elems=z_elems,
    )
    seen = []
    for step in range(steps):
        last = step == steps - 1
        seen += [fault_rows] + fault_in
        base, touch = kernel_call(
            prepare_kernel,
            [field, (2 * PLANE, lanes)],
            [cur, material, own_table, touch_table],
            (),
        )
        args = [cur, fol, minv, base, touch, material, odd_in] + fault_in + even_in
        args += [first_in[0], fault_rows, first_fault, far_table, edge_table]
        static = dict(
            step=step, last=last, extra=1 if last or step == 1 else 0, last_place=lax.axis_size("dom") - 1, pair=pair, y_elems=y_elems,
            z_elems=z_elems,
        )
        if step == 1:
            mask, weight = kernel_call(
                mask_kernel,
                [(4 * PATCH_ROWS, lanes), (4 * steps, lanes)],
                [patch_owner, cur, back, flags, normal_stress[0]],
                (0,),
                unread=(1,),
                z_elems=z_elems,
            )
            args.append(mask)
        if not last:
            new, *even, odd, new_fault = kernel_call(
                step_kernel,
                [field, half, half, plane, (40, lanes)],
                args,
                unread=(len(args) - 1,) if step == 1 else (),
                **static,
            )
            fol, cur, fault_rows = cur, new, new_fault
            even_in, odd_in, fault_in = exchange(even, odd, fault_rows)
        else:
            whole = (3, 4 * y_elems + 1, 4, lanes)
            known = seen[: len(seen) - len(fault_in)]
            later, grad, table = kernel_call(
                output_kernel,
                [whole, (32, lanes), ((lanes, lanes), jnp.bfloat16)],
                [cur, back, weight] + known,
                (),
                [native],
                pair=pair,
                steps=steps,
                y_elems=y_elems,
                z_elems=z_elems,
            )
            sums = kernel_call(
                patch_kernel,
                [(PATCH_DEV, lanes)] * 5,
                [mask, weight, grad, table, odd_in] + fault_in + even_in + [touch],
                unread=(4,) + tuple(range(5 + len(fault_in), 8 + len(fault_in))),
                pair=pair,
                steps=steps,
            )
            patch_sums = sums[0]
            for i, distance, group in ((2, 1, 1), (4, 2, 1), (3, 2, 0), (1, 1, 0)):
                patch_sums = patch_sums + swapped(sums[i], distance, group)
            earlier = kernel_call(
                step_kernel,
                [whole],
                args + [sums[0], back],
                scratch=[native],
                unread=(len(args),),
                **static,
            )[0]
    return (
        jnp.transpose(earlier, (0, 2, 1, 3)),
        jnp.transpose(later, (0, 2, 1, 3)),
        patch_sums[None],
    )


def solution(mesh):
    return jax.shard_map(
        on_device,
        mesh=mesh,
        in_specs=(
            P(None, "dom", "depth", None),
            P(None, "dom", "depth", None),
            P("dom", "depth", None),
            P("dom", "depth", None),
            P("dom", "depth", None),
            P(None, "depth", "dom", None),
            P("depth", "dom", None),
            P("depth", "dom", None),
            P("depth", "dom"),
        ),
        out_specs=(
            P(None, "dom", "depth", None),
            P(None, "dom", "depth", None),
            P("depth", "dom", None),
        ),
        check_vma=False,
    )
```

```python
import functools
import math

import jax
import jax.numpy as jnp
import ml_dtypes
import numpy as np
from jax import lax
from jax.experimental import pallas as pl
from jax.experimental.pallas import tpu as pltpu
from jax.sharding import PartitionSpec as P

PATCH_DEV = 2
REACH = 2
PATCH_ROWS = 16
LATER = 7
FAULT = 24
SENT_FAULT = 28
PARTS = (24, 24, 16)

time_step = 0.01
lock_stiffness = 0.5

BLOCK = 16
ROWS = ((0, 1, 2), (3, 4, 5), (11, 12, 13), (6, 7, 14), (8, 9, 10))
PLANE = 5 * BLOCK


def basis_tables():
    points = [-1.0, -math.sqrt(3.0 / 7.0), 0.0, math.sqrt(3.0 / 7.0), 1.0]
    quad_weights = np.array([0.1, 49.0 / 90.0, 32.0 / 45.0, 49.0 / 90.0, 0.1])
    products = []
    for first in range(5):
        value = 1.0
        for other in range(5):
            if other != first:
                value = value * (points[first] - points[other])
        products.append(value)
    derivative = np.zeros((5, 5))
    for row in range(5):
        for column in range(5):
            if row == column:
                total = 0.0
                for other in range(5):
                    if other != row:
                        total = total + 1.0 / (points[row] - points[other])
                derivative[row, column] = total
            else:
                derivative[row, column] = (
                    products[row] / products[column] / (points[row] - points[column])
                )
    return (quad_weights, derivative)


def two_parts(table):
    high = table.astype(ml_dtypes.bfloat16)
    low = (table - high.astype(np.float64)).astype(ml_dtypes.bfloat16)
    return np.stack([high, low])


def element_stiffness():
    weights, derivative = basis_tables()
    eye = np.eye(5)
    slope = 2.0 * derivative
    grads = [
        np.kron(slope, np.kron(eye, eye)),
        np.kron(eye, np.kron(eye, slope)),
        np.kron(eye, np.kron(slope, eye)),
    ]
    quad = np.kron(weights, np.kron(weights, weights)) / 8.0
    first = np.zeros((125, 3, 125, 3))
    second = np.zeros((125, 3, 125, 3))
    lap = sum(g.T @ (quad[:, None] * g) for g in grads)
    for c in range(3):
        second[:, c, :, c] += lap
        for d in range(3):
            first[:, c, :, d] += grads[c].T @ (quad[:, None] * grads[d])
            second[:, c, :, d] += grads[d].T @ (quad[:, None] * grads[c])
    where = [
        node // 5 * BLOCK + ROWS[node % 5][c] for node in range(125) for c in range(3)
    ]
    wide = []
    for small in (first, second):
        big = np.zeros((5 * PLANE, 5 * PLANE))
        big[np.ix_(where, where)] = small.reshape(375, 375)
        wide.append(big)
    return wide


OWN_COLS = 384


def padded_table(table, columns):
    return np.pad(table, ((0, 0), (0, columns - table.shape[1])))


@functools.cache
def stiffness_tables():
    wide = element_stiffness()
    own = 4 * PLANE
    planes = [slice(x * PLANE, (x + 1) * PLANE) for x in range(5)]
    inner = np.concatenate([w[:own, :own] for w in wide])

    def three(table):
        high, low = two_parts(table)
        return padded_table(np.concatenate([high, low, high], axis=1), 256)

    def both(rows, columns):
        return three(np.concatenate([w[rows, columns] for w in wide]))

    return (
        two_parts(padded_table(inner, OWN_COLS)),
        np.concatenate([three(w[:own, planes[4]]) for w in wide], axis=1),
        np.concatenate([both(planes[4], planes[x]) for x in range(4)], axis=1),
        both(planes[4], planes[4]),
    )


@functools.cache
def back_table(y_elems, z_elems):
    lanes = y_elems * z_elems
    depth = 4 * z_elems
    back = np.zeros((4 * lanes, y_elems * depth), ml_dtypes.bfloat16)
    for yel in range(y_elems):
        for k in range(z_elems):
            for zl in range(4):
                back[zl * lanes + yel * z_elems + k, yel * depth + 4 * k + zl] = 1
    return back


@functools.cache
def mass_table(y_elems, z_elems):
    weights, _ = basis_tables()
    table = np.zeros((4, 5, BLOCK, y_elems, z_elems))
    for x in range(4):
        mx = 0.2 if x == 0 else weights[x]
        for zl in range(5):
            for yl in range(5):
                for yel in range(y_elems):
                    my = weights[yl]
                    if (yl == 0 and yel > 0) or (yl == 4 and yel < y_elems - 1):
                        my = 0.2
                    mz = np.full(z_elems, weights[zl])
                    if zl == 0:
                        mz[1:] = 0.2
                    if zl == 4:
                        mz[:] = 0.2
                    value = time_step * time_step * 8.0 / (mx * my * mz)
                    if zl == 4:
                        value[-1] = 0.0
                    table[x, zl, list(ROWS[yl]), yel] = value
    return table.reshape(4 * PLANE, y_elems * z_elems).astype(np.float32)


def pieces(value, count):
    out = []
    for _ in range(count):
        piece = value.astype(jnp.bfloat16)
        out.append(piece)
        value = value - piece.astype(jnp.float32)
    return out


def dot(a, b):
    return jnp.dot(a, b, preferred_element_type=jnp.float32)


def exact_dot(value, table, count=3):
    rows = value.shape[0]
    result = dot(jnp.concatenate(pieces(value, count), axis=0), table)
    total = result[:rows]
    for i in range(1, count):
        total = total + result[i * rows : (i + 1) * rows]
    return total


def split_dot(table_high, table_low, value):
    lanes = value.shape[1]
    high, low = pieces(value, 2)
    wide = dot(table_high, jnp.concatenate([high, low], axis=1))
    return wide[:, :lanes] + (wide[:, lanes:] + dot(table_low, high))


def ones_where(rule, shape):
    row = lax.broadcasted_iota(jnp.int32, shape, 0)
    column = lax.broadcasted_iota(jnp.int32, shape, 1)
    return jnp.where(rule(row, column), 1.0, 0.0).astype(jnp.bfloat16)


def gather_table(lanes, z_elems):
    return ones_where(lambda z, c: z == 4 * (c % z_elems) + c // lanes, (lanes, 5 * lanes))


def fault_table(lanes, z_elems):
    return ones_where(lambda z, c: z == 4 * (c % z_elems) + c // z_elems, (lanes, lanes))


def fault_table_back(lanes, z_elems):
    return ones_where(lambda c, z: z == 4 * (c % z_elems) + c // z_elems, (lanes, lanes))


def stacked(value):
    high, low = pieces(value, 2)
    gap = jnp.zeros((256 - 3 * value.shape[0], value.shape[1]), jnp.bfloat16)
    return jnp.concatenate([high, high, low, gap], axis=0)


def to_elements(native, scratch, table, y_elems, parts=3):
    group = 4 * BLOCK
    for c in range(3):
        for y in range(4 * y_elems + 1):
            rows = native(c, y)
            if y < 4 * y_elems:
                scratch[y // 4, pl.ds(ROWS[y % 4][c], 4, stride=BLOCK), :] = rows
            if y % 4 == 0 and y > 0:
                scratch[y // 4 - 1, pl.ds(ROWS[4][c], 4, stride=BLOCK), :] = rows
    high, middle, *low = pieces(
        jnp.concatenate([scratch[i] for i in range(y_elems)], axis=0), parts
    )
    result = dot(
        jnp.concatenate([high, middle], axis=1), jnp.concatenate([table, table], axis=0)
    )
    for piece in low:
        result = result + dot(piece, table)
    lanes = result.shape[1] // 5
    across = lax.broadcasted_iota(jnp.int32, (group, result.shape[1]), 1) % lanes // (
        lanes // y_elems
    )
    total = result[:group]
    for yel in range(1, y_elems):
        total = jnp.where(across == yel, result[yel * group : (yel + 1) * group], total)
    blocks = []
    for x in range(4):
        for zl in range(5):
            blocks.append(total[x * BLOCK : (x + 1) * BLOCK, zl * lanes : (zl + 1) * lanes])
    return jnp.concatenate(blocks, axis=0)


def from_elements(field, scratch, back_ref, out_ref, y_elems, stored=None):
    rows = []
    for x in range(4):
        rows.append(
            jnp.concatenate(
                [field[x * PLANE + zl * BLOCK : x * PLANE + (zl + 1) * BLOCK] for zl in range(4)],
                axis=1,
            )
        )
    result = exact_dot(jnp.concatenate(rows, axis=0), back_ref[...])
    depth = result.shape[1] // y_elems
    for yel in range(y_elems):
        scratch[yel] = result[:, yel * depth : (yel + 1) * depth]
    for c in range(3):
        for y in range(4 * y_elems + 1):
            yel, yl = (y // 4, y % 4) if y < 4 * y_elems else (y_elems - 1, 4)
            out_ref[c, y] = scratch[yel, pl.ds(ROWS[yl][c], 4, stride=BLOCK), :]
        if stored is not None:
            stored(c)


def shifted(rows, lanes):
    lanes = lanes % rows.shape[1]
    return pltpu.roll(rows, lanes, 1) if lanes else rows


def block_iotas(lanes):
    return (
        lax.broadcasted_iota(jnp.int32, (8, lanes), 0),
        lax.broadcasted_iota(jnp.int32, (8, lanes), 1),
    )


def store_fault(out_ref, x, plane, z_elems):
    lanes = plane.shape[1]
    _, lane = block_iotas(lanes)
    first = last = jnp.zeros((8, lanes), jnp.float32)
    for zl in range(4):
        at = zl * BLOCK
        here = lane // z_elems == zl
        first = jnp.where(here, shifted(plane[at : at + 8], zl * z_elems), first)
        last = jnp.where(here, shifted(plane[at + 8 : at + 16], (zl + 1) * z_elems), last)
    out_ref[pl.ds(x, 3, stride=8), :] = last[:3]
    out_ref[pl.ds(4 + x, 3, stride=8), :] = first[:3]


def select_messages(parity, left, right):
    even = parity == 0
    return jnp.where(even, right, left), jnp.where(even, left, right)


def material_rows(lame_ref, shear_ref):
    y_elems, z_elems = lame_ref.shape
    both = jnp.concatenate([lame_ref[...], shear_ref[...]], axis=0)
    spread = ones_where(lambda k, c: c % z_elems == k, (z_elems, y_elems * z_elems))
    tiled = exact_dot(both, spread)
    row = lax.broadcasted_iota(jnp.int32, tiled.shape, 0)
    lane = lax.broadcasted_iota(jnp.int32, tiled.shape, 1)
    kept = jnp.where(row % y_elems == lane // z_elems, tiled, 0.0)
    return (
        jnp.sum(kept[:y_elems], axis=0, keepdims=True),
        jnp.sum(kept[y_elems:], axis=0, keepdims=True),
    )


def above_lanes(lanes, z_elems):
    return lax.broadcasted_iota(jnp.int32, (BLOCK, lanes), 1) % z_elems != 0


def edge_message(result, lame_row, shear_row, z_elems):
    lanes = result.shape[1]
    force = lame_row * result[:PLANE] + shear_row * result[PLANE:]
    top = force[:BLOCK] + jnp.where(
        above_lanes(lanes, z_elems), pltpu.roll(force[4 * BLOCK :], 1, 1), 0.0
    )
    row = lax.broadcasted_iota(jnp.int32, top.shape, 0)
    top = jnp.where(row == BLOCK - 1, lame_row, top)
    second = jnp.where(row == BLOCK - 1, shear_row, force[BLOCK : 2 * BLOCK])
    return jnp.concatenate([top, second, force[2 * BLOCK : 4 * BLOCK]], axis=0)


def own_force(own_ref, cur, lame_row, shear_row):
    rows, lanes = cur.shape
    padded = jnp.concatenate([cur, jnp.zeros((OWN_COLS - rows, lanes), jnp.float32)], axis=0)
    result = split_dot(own_ref[0], own_ref[1], padded)
    return lame_row * result[:rows] + shear_row * result[rows:]


def start_copies(pairs, sems):
    copies = [
        pltpu.make_async_copy(source, target, sems.at[i])
        for i, (source, target) in enumerate(pairs)
    ]
    for copy in copies:
        copy.start()
    return copies


def first_kernel(
    now_hbm,
    flags_hbm,
    weak_hbm,
    lame_hbm,
    shear_hbm,
    *refs,
):
    later_hbm, refs = refs[:LATER], refs[LATER:]
    cur_ref, *even_refs, odd_ref, fault_out_ref, material_ref = refs[:7]
    later_refs, refs = refs[7 : 7 + LATER], refs[7 + LATER :]
    scratch, now_ref, flags_ref, weak_ref, lame_ref, shear_ref, sems = refs
    copies = start_copies(
        [
            (flags_hbm, flags_ref),
            (weak_hbm, weak_ref),
            (lame_hbm, lame_ref),
            (shear_hbm, shear_ref),
            (now_hbm, now_ref),
        ]
        + list(zip(later_hbm, later_refs)),
        sems,
    )
    edge_ref = later_refs[0]
    y_elems, z_elems = lame_ref.shape
    lanes = y_elems * z_elems
    parity = lax.axis_index("dom") % 2
    gather = gather_table(lanes, z_elems)
    fault = fault_table(lanes, z_elems)
    scratch[...] = jnp.zeros_like(scratch)
    for copy in copies[:6]:
        copy.wait()
    cur = to_elements(lambda c, y: now_ref[c, y], scratch, gather, y_elems)
    cur_ref[...] = cur
    lame_row, shear_row = material_rows(lame_ref, shear_ref)
    material_ref[...] = jnp.concatenate(
        [lame_row, shear_row, jnp.zeros((6, lanes), jnp.float32)], axis=0
    )
    planes = [cur[x * PLANE : (x + 1) * PLANE] for x in range(4)]
    edge = dot(edge_ref[...], jnp.concatenate([stacked(p) for p in planes], axis=0))
    right = edge_message(edge, lame_row, shear_row, z_elems)
    message, odd_ref[...] = select_messages(parity, cur[: 4 * BLOCK], right)
    for even_ref, at in zip(even_refs, (0, PARTS[0], PARTS[0] + PARTS[1])):
        even_ref[...] = message[at : at + even_ref.shape[0]]
    weak = weak_ref[...]
    tangent = []
    for i in range(flags_ref.shape[0]):
        flag = flags_ref[i]
        tangent.append(
            jnp.where(flag == 0, lock_stiffness, jnp.where(flag == 1, -weak, 0.0))
        )
    for x in range(4):
        store_fault(fault_out_ref, x, planes[x], z_elems)
    fault_out_ref[FAULT:] = exact_dot(jnp.concatenate(tangent, axis=0), fault)
    for copy in copies[6:]:
        copy.wait()


def prepare_kernel(cur_ref, material_ref, own_ref, touch_ref, base_ref, edge_part_ref):
    cur = cur_ref[...]
    base_ref[...] = own_force(own_ref, cur, material_ref[0:1], material_ref[1:2])
    edge_part_ref[...] = dot(touch_ref[...], stacked(cur[:PLANE]))


def setup_kernel(next_ref, density_ref, mass_ref, fol_ref, minv_ref, scratch, *, y_elems, z_elems):
    gather = gather_table(y_elems * z_elems, z_elems)
    scratch[...] = jnp.zeros_like(scratch)
    fol_ref[...] = to_elements(lambda c, y: next_ref[c, y], scratch.at[0], gather, y_elems)
    density = to_elements(lambda c, y: density_ref[y], scratch.at[1], gather, y_elems, 2)
    table = mass_ref[...]
    first = lax.axis_index("dom") == 0
    plane = lax.broadcasted_iota(jnp.int32, table.shape, 0) < PLANE
    table = jnp.where(jnp.logical_and(first, plane), 2.0 * table, table)
    minv_ref[...] = jnp.where(table > 0.0, table / jnp.where(table > 0.0, density, 1.0), 0.0)


def step_kernel(*refs, step, last, extra, last_place, pair, y_elems, z_elems):
    cur_ref, fol_ref, minv_ref, base_ref, touch_ref, material_ref, odd_ref, up_ref = refs[:8]
    refs = list(refs[8:])
    down_ref = None if pair else refs.pop(0)
    even_in = jnp.concatenate([refs.pop(0)[...] for _ in PARTS], axis=0)
    down_ref = up_ref if pair else down_ref
    first_up_ref, own_ref, first_own_ref, far_ref, edge_ref = refs[:5]
    refs = refs[5 + extra :]
    if last:
        later_ref, back_ref, out_hbm, later_hbm, scratch, out_ref, sems = refs
        copies = start_copies([(later_ref, later_hbm)], sems)
    else:
        new_ref, *even_outs, odd_out, fault_out = refs
    place = lax.axis_index("dom")
    lanes = cur_ref.shape[1]
    even = place % 2 == 0
    far = jnp.where(place == last_place, 0.0, jnp.where(even, even_in, odd_ref[...]))
    left = jnp.where(place == 0, 0.0, jnp.where(even, odd_ref[...], even_in))
    lane_wide = lax.broadcasted_iota(jnp.int32, (BLOCK, lanes), 1)
    below = jnp.where(
        lane_wide % z_elems != z_elems - 1, pltpu.roll(far[:BLOCK], lanes - 1, 1), 0.0
    )
    far = jnp.concatenate([far, below], axis=0)
    lame_row, shear_row = material_ref[0:1], material_ref[1:2]
    far = jnp.concatenate([stacked(lame_row * far), stacked(shear_row * far)], axis=0)
    left_lame = left[BLOCK - 1 : BLOCK]
    left_shear = left[2 * BLOCK - 1 : 2 * BLOCK]
    from_left = left_lame * touch_ref[:PLANE] + left_shear * touch_ref[PLANE:]
    row, lane = block_iotas(lanes)
    across = lane // z_elems
    shared = row < 3
    add_first = jnp.logical_and(shared, across > 0)
    take_last = jnp.logical_and(shared, across < y_elems - 1)
    pull_first = jnp.logical_and(shared, across == 0)
    pull_last = jnp.logical_and(shared, across == y_elems - 1)
    above = above_lanes(lanes, z_elems)
    middle = lax.broadcasted_iota(jnp.int32, (3, lanes), 0) == 1
    gap = jnp.zeros((5, lanes), jnp.float32)
    if not last:
        fault_out[FAULT:] = jnp.zeros_like(fault_out[FAULT:])
    planes = []
    for x in range(4):
        rows = slice(x * PLANE, (x + 1) * PLANE)
        force = base_ref[rows] + dot(far_ref[rows], far)
        blocks = [force[zl * BLOCK : (zl + 1) * BLOCK] for zl in range(5)]
        if x == 0:
            blocks = [b + from_left[i * BLOCK : (i + 1) * BLOCK] for i, b in enumerate(blocks)]
            blocks[:4] = [b + left[i * BLOCK : (i + 1) * BLOCK] for i, b in enumerate(blocks[:4])]
        blocks[0], blocks[4] = (
            blocks[0] + jnp.where(above, pltpu.roll(blocks[4], 1, 1), 0.0),
            blocks[4] + pltpu.roll(blocks[0], lanes - 1, 1),
        )
        lasts, firsts = pl.ds(x, 3, stride=8), pl.ds(4 + x, 3, stride=8)
        k = slice(FAULT + 4 * step + x, FAULT + 4 * step + x + 1)
        below_stiff = jnp.where(middle, lock_stiffness, first_up_ref[k])
        own_stiff = jnp.where(middle, lock_stiffness, first_own_ref[k])
        pulled = jnp.concatenate(
            [below_stiff * (up_ref[lasts, :] - own_ref[firsts, :]), gap], axis=0
        )
        pulled_last = jnp.concatenate(
            [own_stiff * (down_ref[firsts, :] - own_ref[lasts, :]), gap], axis=0
        )
        for zl in range(5):
            low, high = blocks[zl][:8], blocks[zl][8:]
            move = zl * z_elems if zl < 4 else 1
            blocks[zl] = jnp.concatenate(
                [
                    low
                    + jnp.where(add_first, shifted(high, z_elems), 0.0)
                    - jnp.where(pull_first, shifted(pulled, -move), 0.0),
                    high
                    + jnp.where(take_last, shifted(low, -z_elems), 0.0)
                    - jnp.where(pull_last, shifted(pulled_last, -move - z_elems), 0.0),
                ],
                axis=0,
            )
        plane = (2.0 * cur_ref[rows] - fol_ref[rows]) - minv_ref[rows] * jnp.concatenate(
            blocks, axis=0
        )
        if last:
            planes.append(plane)
        else:
            new_ref[rows] = plane
            store_fault(fault_out, x, plane, z_elems)
            planes.append(stacked(plane))
            if x == 0:
                first = plane[: 4 * BLOCK]
    if last:

        def send(c):
            copy = pltpu.make_async_copy(out_ref.at[c], out_hbm.at[c], sems.at[1 + c])
            copy.start()
            copies.append(copy)

        from_elements(
            jnp.concatenate(planes, axis=0), scratch, back_ref, out_ref, y_elems, send
        )
        for copy in copies:
            copy.wait()
    else:
        edge = dot(edge_ref[...], jnp.concatenate(planes, axis=0))
        right = edge_message(edge, lame_row, shear_row, z_elems)
        message, odd_out[...] = select_messages(place % 2, first, right)
        for even_out, at in zip(even_outs, (0, PARTS[0], PARTS[0] + PARTS[1])):
            even_out[...] = message[at : at + even_out.shape[0]]


def mask_kernel(owner_ref, _, back_ref, flags_ref, stress_ref, mask_ref, weight_ref, *, z_elems):
    shape = (PATCH_ROWS, mask_ref.shape[1])
    first = (lax.axis_index("dom") - REACH) * PATCH_DEV
    number = lax.broadcasted_iota(jnp.int32, shape, 0) + first
    for x in range(4):
        mask = jnp.where(number == owner_ref[0, x], 1.0, 0.0)
        mask_ref[PATCH_ROWS * x : PATCH_ROWS * (x + 1)] = mask
    stress = stress_ref[...]
    weights = []
    for i in range(flags_ref.shape[0]):
        flag = flags_ref[i]
        weights.append(
            stress * jnp.where(flag == 1, 0.5, jnp.where(flag == 2, 1.0, 0.0))
        )
    fault = fault_table(mask_ref.shape[1], z_elems)
    weight_ref[...] = exact_dot(jnp.concatenate(weights, axis=0), fault)


def output_kernel(*refs, pair, steps, y_elems, z_elems):
    field_ref, back_ref, weight_ref = refs[:3]
    out_ref, grad_ref, table_ref, scratch = refs[-4:]
    messages = refs[3:-4]
    count = 2 if pair else 3
    grad = 0.0
    for i in range(steps):
        group = messages[count * i : count * (i + 1)]
        slip = -group[0][:4]
        if i < steps - 1:
            slip = slip + group[-1][4:8]
        grad = grad + slip * weight_ref[4 * i : 4 * i + 4]
    grad_ref[...] = grad
    table_ref[...] = fault_table_back(weight_ref.shape[1], z_elems)
    from_elements(field_ref[...], scratch, back_ref, out_ref, y_elems)


def patch_kernel(*refs, pair, steps):
    mask_ref, weight_ref, grad_ref, table_ref, _ = refs[:5]
    first_ref = refs[5] if pair else refs[6]
    home_out, out_a, out_b, out_c, out_d = refs[-5:]
    place = lax.axis_index("dom")
    grad = grad_ref[...] + first_ref[4:8] * weight_ref[4 * (steps - 1) : 4 * steps]
    total = 0.0
    for x in range(4):
        total = total + mask_ref[PATCH_ROWS * x : PATCH_ROWS * (x + 1)] * grad[x : x + 1]
    total = exact_dot(total, table_ref[...])
    rows = [total[2 * i : 2 * i + 2] for i in range(5)]
    home_out[...] = rows[2]
    even = place % 2 == 0
    out_a[...] = jnp.where(even, rows[3], rows[1])
    out_b[...] = jnp.where(even, rows[1], rows[3])
    low = place % 4 < 2
    out_c[...] = jnp.where(low, rows[4], rows[0])
    out_d[...] = jnp.where(low, rows[0], rows[4])


VMEM = pl.BlockSpec(memory_space=pltpu.VMEM)
HBM = pl.BlockSpec(memory_space=pltpu.HBM)
SMEM = pl.BlockSpec(memory_space=pltpu.SMEM)
ANY = pl.BlockSpec(memory_space=pl.ANY)


def kernel_call(body, outs, args, in_smem=(), scratch=(), in_hbm=(), kept=(), unread=(), stay=False, out_spec=VMEM, **static):
    shapes = []
    for out in outs:
        shape, dtype = out if isinstance(out[0], tuple) else (out, jnp.float32)
        shapes.append((pltpu.VMEM if in_hbm or stay else jax.ShapeDtypeStruct)(shape, dtype))
    specs = [VMEM] * len(args)
    for places, spec in ((in_smem, SMEM), (in_hbm, HBM), (unread, ANY)):
        for i in places:
            specs[i] = spec
    copied = [pltpu.VMEM(args[i].shape, args[i].dtype) for i in in_hbm if i not in kept]
    if in_hbm:
        copied.append(pltpu.SemaphoreType.DMA((len(in_hbm),)))
    return pl.pallas_call(
        functools.partial(body, **static) if static else body,
        out_shape=shapes,
        in_specs=specs,
        out_specs=[out_spec] * len(shapes),
        scratch_shapes=list(scratch) + copied,
        compiler_params=pltpu.CompilerParams(
            vmem_limit_bytes=(56 if in_hbm else 24) * 2**20
        ),
    )(*args)


def swapped(block, distance, group):
    size, across = lax.axis_size("dom"), lax.axis_size("depth")
    partner = {}
    for left in range(size - distance):
        if left // distance % 2 == group:
            partner[left], partner[left + distance] = left + distance, left
    route = []
    for i in range(size):
        for j in range(across):
            side = j if i in partner else min(j ^ 1, across - 1)
            route.append((i * across + j, partner.get(i, i) * across + side))
    return lax.ppermute(block, ("dom", "depth"), route)


def from_behind(block, axis, distance):
    size = lax.axis_size(axis)
    return lax.ppermute(block, axis, [((i - distance) % size, i) for i in range(size)])


def on_device(
    adjoint_now,
    adjoint_next,
    lame_first,
    shear_modulus,
    density,
    branch_flags,
    weak_slope,
    normal_stress,
    patch_owner,
):
    x_elems, y_elems, z_elems = lame_first.shape
    lanes = y_elems * z_elems
    assert x_elems == 1 and lanes == adjoint_now.shape[3]
    steps = branch_flags.shape[0]
    pair = lax.axis_size("depth") == 2
    own_table, far_table, edge_table, touch_table = (jnp.asarray(t) for t in stiffness_tables())
    back = jnp.asarray(back_table(y_elems, z_elems))
    mass = jnp.asarray(mass_table(y_elems, z_elems))
    now = jnp.transpose(adjoint_now, (0, 2, 1, 3))
    following = jnp.transpose(adjoint_next, (0, 2, 1, 3))
    rho = jnp.transpose(density, (1, 0, 2))
    flags = branch_flags[:, 0]
    native = pltpu.VMEM((y_elems, 4 * BLOCK, lanes), jnp.float32)
    field = (4 * PLANE, lanes)
    plane = (4 * BLOCK, lanes)
    parts = [(rows, lanes) for rows in PARTS]

    def exchange(even, odd, fault_rows):
        if pair:
            faults = [from_behind(fault_rows, "depth", 1)]
        else:
            faults = [from_behind(fault_rows, "depth", 1), from_behind(fault_rows, "depth", -1)]
        return [swapped(part, 1, 0) for part in even], swapped(odd, 1, 1), faults

    later_used = (edge_table, following, rho, mass, own_table, far_table, touch_table)
    assert len(later_used) == LATER
    cur, *even, odd, fault_rows, material, edge_table, following, rho, mass, own_table, far_table, touch_table = kernel_call(
        first_kernel,
        [field] + parts + [plane, (FAULT + 4 * steps, lanes), (8, lanes)]
        + [(t.shape, t.dtype) for t in later_used],
        (now, flags, weak_slope[0], lame_first[0], shear_modulus[0]) + later_used,
        scratch=[native],
        in_hbm=range(5 + LATER),
        kept=range(5, 5 + LATER),
    )
    even_in, odd_in, fault_in = exchange(even, odd, fault_rows)
    first_fault, first_in = fault_rows, fault_in
    fol, minv = kernel_call(
        setup_kernel,
        [field, field],
        (following, rho, mass),
        scratch=[pltpu.VMEM((2, y_elems, 4 * BLOCK, lanes), jnp.float32)],
        y_elems=y_elems,
        z_elems=z_elems,
    )
    seen = []
    for step in range(steps):
        last = step == steps - 1
        seen += [fault_rows] + fault_in
        base, touch = kernel_call(
            prepare_kernel,
            [field, (2 * PLANE, lanes)],
            [cur, material, own_table, touch_table],
            (),
        )
        args = [cur, fol, minv, base, touch, material, odd_in] + fault_in + even_in
        args += [first_in[0], fault_rows, first_fault, far_table, edge_table]
        static = dict(
            step=step, last=last, extra=1 if last or step == 1 else 0, last_place=lax.axis_size("dom") - 1, pair=pair, y_elems=y_elems,
            z_elems=z_elems,
        )
        if step == 1:
            mask, weight = kernel_call(
                mask_kernel,
                [(4 * PATCH_ROWS, lanes), (4 * steps, lanes)],
                [patch_owner, cur, back, flags, normal_stress[0]],
                (0,),
                unread=(1,),
                z_elems=z_elems,
            )
            args.append(mask)
        if not last:
            new, *even, odd, new_fault = kernel_call(
                step_kernel,
                [field] + parts + [plane, (SENT_FAULT, lanes)],
                args,
                unread=(len(args) - 1,) if step == 1 else (),
                **static,
            )
            fol, cur, fault_rows = cur, new, new_fault
            even_in, odd_in, fault_in = exchange(even, odd, fault_rows)
        else:
            whole = (3, 4 * y_elems + 1, 4, lanes)
            known = seen[: len(seen) - len(fault_in)]
            later, grad, table = kernel_call(
                output_kernel,
                [whole, (4, lanes), ((lanes, lanes), jnp.bfloat16)],
                [cur, back, weight] + known,
                scratch=[native],
                stay=True,
                pair=pair,
                steps=steps,
                y_elems=y_elems,
                z_elems=z_elems,
            )
            sums = kernel_call(
                patch_kernel,
                [(PATCH_DEV, lanes)] * 5,
                [mask, weight, grad, table, odd_in] + fault_in + even_in + [touch],
                unread=(4,) + tuple(range(5 + len(fault_in), 9 + len(fault_in))),
                pair=pair,
                steps=steps,
            )
            patch_sums = sums[0]
            for i, distance, group in ((2, 1, 1), (4, 2, 1), (3, 2, 0), (1, 1, 0)):
                patch_sums = patch_sums + swapped(sums[i], distance, group)
            earlier, later = kernel_call(
                step_kernel,
                [whole, whole],
                args + [sums[0], later, back],
                scratch=[
                    native, pltpu.VMEM(whole, jnp.float32), pltpu.SemaphoreType.DMA((4,)),
                ],
                unread=(len(args),),
                out_spec=HBM,
                **static,
            )
    return (
        jnp.transpose(earlier, (0, 2, 1, 3)),
        jnp.transpose(later, (0, 2, 1, 3)),
        patch_sums[None],
    )


def solution(mesh):
    return jax.shard_map(
        on_device,
        mesh=mesh,
        in_specs=(
            P(None, "dom", "depth", None),
            P(None, "dom", "depth", None),
            P("dom", "depth", None),
            P("dom", "depth", None),
            P("dom", "depth", None),
            P(None, "depth", "dom", None),
            P("depth", "dom", None),
            P("depth", "dom", None),
            P("depth", "dom"),
        ),
        out_specs=(
            P(None, "dom", "depth", None),
            P(None, "dom", "depth", None),
            P("depth", "dom", None),
        ),
        check_vma=False,
    )
```

```python
import functools
import math

import jax
import jax.numpy as jnp
import ml_dtypes
import numpy as np
from jax import lax
from jax.experimental import pallas as pl
from jax.experimental.pallas import tpu as pltpu
from jax.sharding import PartitionSpec as P

PATCH_DEV = 2
REACH = 2
PATCH_ROWS = 16
LATER = 11
FAULT = 24
SENT_FAULT = 28
PARTS = (24, 24, 16)

time_step = 0.01
lock_stiffness = 0.5

BLOCK = 16
ROWS = ((0, 1, 2), (3, 4, 5), (11, 12, 13), (6, 7, 14), (8, 9, 10))
PLANE = 5 * BLOCK


def basis_tables():
    points = [-1.0, -math.sqrt(3.0 / 7.0), 0.0, math.sqrt(3.0 / 7.0), 1.0]
    quad_weights = np.array([0.1, 49.0 / 90.0, 32.0 / 45.0, 49.0 / 90.0, 0.1])
    products = []
    for first in range(5):
        value = 1.0
        for other in range(5):
            if other != first:
                value = value * (points[first] - points[other])
        products.append(value)
    derivative = np.zeros((5, 5))
    for row in range(5):
        for column in range(5):
            if row == column:
                total = 0.0
                for other in range(5):
                    if other != row:
                        total = total + 1.0 / (points[row] - points[other])
                derivative[row, column] = total
            else:
                derivative[row, column] = (
                    products[row] / products[column] / (points[row] - points[column])
                )
    return (quad_weights, derivative)


def two_parts(table):
    high = table.astype(ml_dtypes.bfloat16)
    low = (table - high.astype(np.float64)).astype(ml_dtypes.bfloat16)
    return np.stack([high, low])


def element_stiffness():
    weights, derivative = basis_tables()
    eye = np.eye(5)
    slope = 2.0 * derivative
    grads = [
        np.kron(slope, np.kron(eye, eye)),
        np.kron(eye, np.kron(eye, slope)),
        np.kron(eye, np.kron(slope, eye)),
    ]
    quad = np.kron(weights, np.kron(weights, weights)) / 8.0
    first = np.zeros((125, 3, 125, 3))
    second = np.zeros((125, 3, 125, 3))
    lap = sum(g.T @ (quad[:, None] * g) for g in grads)
    for c in range(3):
        second[:, c, :, c] += lap
        for d in range(3):
            first[:, c, :, d] += grads[c].T @ (quad[:, None] * grads[d])
            second[:, c, :, d] += grads[d].T @ (quad[:, None] * grads[c])
    where = [
        node // 5 * BLOCK + ROWS[node % 5][c] for node in range(125) for c in range(3)
    ]
    wide = []
    for small in (first, second):
        big = np.zeros((5 * PLANE, 5 * PLANE))
        big[np.ix_(where, where)] = small.reshape(375, 375)
        wide.append(big)
    return wide


OWN_COLS = 384


def padded_table(table, columns):
    return np.pad(table, ((0, 0), (0, columns - table.shape[1])))


@functools.cache
def stiffness_tables():
    wide = element_stiffness()
    own = 4 * PLANE
    planes = [slice(x * PLANE, (x + 1) * PLANE) for x in range(5)]
    inner = np.concatenate([w[:own, :own] for w in wide])

    def three(table):
        high, low = two_parts(table)
        return padded_table(np.concatenate([high, low, high], axis=1), 256)

    def both(rows, columns):
        return three(np.concatenate([w[rows, columns] for w in wide]))

    return (
        two_parts(padded_table(inner, OWN_COLS)),
        np.concatenate([three(w[:own, planes[4]]) for w in wide], axis=1),
        np.concatenate([both(planes[4], planes[x]) for x in range(4)], axis=1),
        both(planes[4], planes[4]),
    )


@functools.cache
def back_table(y_elems, z_elems):
    lanes = y_elems * z_elems
    depth = 4 * z_elems
    back = np.zeros((4 * lanes, y_elems * depth), ml_dtypes.bfloat16)
    for yel in range(y_elems):
        for k in range(z_elems):
            for zl in range(4):
                back[zl * lanes + yel * z_elems + k, yel * depth + 4 * k + zl] = 1
    return back


@functools.cache
def mass_table(y_elems, z_elems):
    weights, _ = basis_tables()
    table = np.zeros((4, 5, BLOCK, y_elems, z_elems))
    for x in range(4):
        mx = 0.2 if x == 0 else weights[x]
        for zl in range(5):
            for yl in range(5):
                for yel in range(y_elems):
                    my = weights[yl]
                    if (yl == 0 and yel > 0) or (yl == 4 and yel < y_elems - 1):
                        my = 0.2
                    mz = np.full(z_elems, weights[zl])
                    if zl == 0:
                        mz[1:] = 0.2
                    if zl == 4:
                        mz[:] = 0.2
                    value = time_step * time_step * 8.0 / (mx * my * mz)
                    if zl == 4:
                        value[-1] = 0.0
                    table[x, zl, list(ROWS[yl]), yel] = value
    return table.reshape(4 * PLANE, y_elems * z_elems).astype(np.float32)


def pieces(value, count):
    out = []
    for _ in range(count):
        piece = value.astype(jnp.bfloat16)
        out.append(piece)
        value = value - piece.astype(jnp.float32)
    return out


def dot(a, b):
    return jnp.dot(a, b, preferred_element_type=jnp.float32)


def exact_dot(value, table, count=3):
    rows = value.shape[0]
    result = dot(jnp.concatenate(pieces(value, count), axis=0), table)
    total = result[:rows]
    for i in range(1, count):
        total = total + result[i * rows : (i + 1) * rows]
    return total


def split_dot(table_high, table_low, value):
    lanes = value.shape[1]
    high, low = pieces(value, 2)
    wide = dot(table_high, jnp.concatenate([high, low], axis=1))
    return wide[:, :lanes] + (wide[:, lanes:] + dot(table_low, high))


def ones_where(rule, shape):
    row = lax.broadcasted_iota(jnp.int32, shape, 0)
    column = lax.broadcasted_iota(jnp.int32, shape, 1)
    return jnp.where(rule(row, column), 1.0, 0.0).astype(jnp.bfloat16)


def gather_table(lanes, z_elems):
    return ones_where(lambda z, c: z == 4 * (c % z_elems) + c // lanes, (lanes, 5 * lanes))


def fault_table(lanes, z_elems):
    return ones_where(lambda z, c: z == 4 * (c % z_elems) + c // z_elems, (lanes, lanes))


def fault_table_back(lanes, z_elems):
    return ones_where(lambda c, z: z == 4 * (c % z_elems) + c // z_elems, (lanes, lanes))


def stacked(value):
    high, low = pieces(value, 2)
    gap = jnp.zeros((256 - 3 * value.shape[0], value.shape[1]), jnp.bfloat16)
    return jnp.concatenate([high, high, low, gap], axis=0)


def to_elements(native, scratch, table, y_elems, parts=3):
    group = 4 * BLOCK
    for c in range(3):
        for y in range(4 * y_elems + 1):
            rows = native(c, y)
            if y < 4 * y_elems:
                scratch[y // 4, pl.ds(ROWS[y % 4][c], 4, stride=BLOCK), :] = rows
            if y % 4 == 0 and y > 0:
                scratch[y // 4 - 1, pl.ds(ROWS[4][c], 4, stride=BLOCK), :] = rows
    high, middle, *low = pieces(
        jnp.concatenate([scratch[i] for i in range(y_elems)], axis=0), parts
    )
    result = dot(
        jnp.concatenate([high, middle], axis=1), jnp.concatenate([table, table], axis=0)
    )
    for piece in low:
        result = result + dot(piece, table)
    lanes = result.shape[1] // 5
    across = lax.broadcasted_iota(jnp.int32, (group, result.shape[1]), 1) % lanes // (
        lanes // y_elems
    )
    total = result[:group]
    for yel in range(1, y_elems):
        total = jnp.where(across == yel, result[yel * group : (yel + 1) * group], total)
    blocks = []
    for x in range(4):
        for zl in range(5):
            blocks.append(total[x * BLOCK : (x + 1) * BLOCK, zl * lanes : (zl + 1) * lanes])
    return jnp.concatenate(blocks, axis=0)


def from_elements(field, scratch, back_ref, out_ref, y_elems, stored=None):
    rows = []
    for x in range(4):
        rows.append(
            jnp.concatenate(
                [field[x * PLANE + zl * BLOCK : x * PLANE + (zl + 1) * BLOCK] for zl in range(4)],
                axis=1,
            )
        )
    result = exact_dot(jnp.concatenate(rows, axis=0), back_ref[...])
    depth = result.shape[1] // y_elems
    for yel in range(y_elems):
        scratch[yel] = result[:, yel * depth : (yel + 1) * depth]
    for c in range(3):
        for y in range(4 * y_elems + 1):
            yel, yl = (y // 4, y % 4) if y < 4 * y_elems else (y_elems - 1, 4)
            out_ref[c, y] = scratch[yel, pl.ds(ROWS[yl][c], 4, stride=BLOCK), :]
        if stored is not None:
            stored(c)


def shifted(rows, lanes):
    lanes = lanes % rows.shape[1]
    return pltpu.roll(rows, lanes, 1) if lanes else rows


def block_iotas(lanes):
    return (
        lax.broadcasted_iota(jnp.int32, (8, lanes), 0),
        lax.broadcasted_iota(jnp.int32, (8, lanes), 1),
    )


def store_fault(out_ref, x, plane, z_elems):
    lanes = plane.shape[1]
    _, lane = block_iotas(lanes)
    first = last = jnp.zeros((8, lanes), jnp.float32)
    for zl in range(4):
        at = zl * BLOCK
        here = lane // z_elems == zl
        first = jnp.where(here, shifted(plane[at : at + 8], zl * z_elems), first)
        last = jnp.where(here, shifted(plane[at + 8 : at + 16], (zl + 1) * z_elems), last)
    out_ref[pl.ds(x, 3, stride=8), :] = last[:3]
    out_ref[pl.ds(4 + x, 3, stride=8), :] = first[:3]


def select_messages(parity, left, right):
    even = parity == 0
    return jnp.where(even, right, left), jnp.where(even, left, right)


def material_rows(lame_ref, shear_ref):
    y_elems, z_elems = lame_ref.shape
    both = jnp.concatenate([lame_ref[...], shear_ref[...]], axis=0)
    spread = ones_where(lambda k, c: c % z_elems == k, (z_elems, y_elems * z_elems))
    tiled = exact_dot(both, spread)
    row = lax.broadcasted_iota(jnp.int32, tiled.shape, 0)
    lane = lax.broadcasted_iota(jnp.int32, tiled.shape, 1)
    kept = jnp.where(row % y_elems == lane // z_elems, tiled, 0.0)
    return (
        jnp.sum(kept[:y_elems], axis=0, keepdims=True),
        jnp.sum(kept[y_elems:], axis=0, keepdims=True),
    )


def above_lanes(lanes, z_elems):
    return lax.broadcasted_iota(jnp.int32, (BLOCK, lanes), 1) % z_elems != 0


def edge_message(result, lame_row, shear_row, z_elems):
    lanes = result.shape[1]
    force = lame_row * result[:PLANE] + shear_row * result[PLANE:]
    top = force[:BLOCK] + jnp.where(
        above_lanes(lanes, z_elems), pltpu.roll(force[4 * BLOCK :], 1, 1), 0.0
    )
    row = lax.broadcasted_iota(jnp.int32, top.shape, 0)
    top = jnp.where(row == BLOCK - 1, lame_row, top)
    second = jnp.where(row == BLOCK - 1, shear_row, force[BLOCK : 2 * BLOCK])
    return jnp.concatenate([top, second, force[2 * BLOCK : 4 * BLOCK]], axis=0)


def own_force(own_ref, cur, lame_row, shear_row):
    rows, lanes = cur.shape
    padded = jnp.concatenate([cur, jnp.zeros((OWN_COLS - rows, lanes), jnp.float32)], axis=0)
    result = split_dot(own_ref[0], own_ref[1], padded)
    return lame_row * result[:rows] + shear_row * result[rows:]


def start_copies(pairs, sems):
    copies = [
        pltpu.make_async_copy(source, target, sems.at[i])
        for i, (source, target) in enumerate(pairs)
    ]
    for copy in copies:
        copy.start()
    return copies


def first_kernel(
    now_hbm,
    flags_hbm,
    weak_hbm,
    lame_hbm,
    shear_hbm,
    *refs,
):
    later_hbm, refs = refs[:LATER], refs[LATER:]
    cur_ref, *even_refs, odd_ref, fault_out_ref, material_ref = refs[:7]
    later_refs, refs = refs[7 : 7 + LATER], refs[7 + LATER :]
    scratch, now_ref, flags_ref, weak_ref, lame_ref, shear_ref, sems = refs
    copies = start_copies(
        [
            (flags_hbm, flags_ref),
            (weak_hbm, weak_ref),
            (lame_hbm, lame_ref),
            (shear_hbm, shear_ref),
            (now_hbm, now_ref),
        ]
        + list(zip(later_hbm, later_refs)),
        sems,
    )
    edge_ref = later_refs[0]
    y_elems, z_elems = lame_ref.shape
    lanes = y_elems * z_elems
    parity = lax.axis_index("dom") % 2
    gather = gather_table(lanes, z_elems)
    fault = fault_table(lanes, z_elems)
    scratch[...] = jnp.zeros_like(scratch)
    for copy in copies[:6]:
        copy.wait()
    cur = to_elements(lambda c, y: now_ref[c, y], scratch, gather, y_elems)
    cur_ref[...] = cur
    lame_row, shear_row = material_rows(lame_ref, shear_ref)
    material_ref[...] = jnp.concatenate(
        [lame_row, shear_row, jnp.zeros((6, lanes), jnp.float32)], axis=0
    )
    planes = [cur[x * PLANE : (x + 1) * PLANE] for x in range(4)]
    edge = dot(edge_ref[...], jnp.concatenate([stacked(p) for p in planes], axis=0))
    right = edge_message(edge, lame_row, shear_row, z_elems)
    message, odd_ref[...] = select_messages(parity, cur[: 4 * BLOCK], right)
    for even_ref, at in zip(even_refs, (0, PARTS[0], PARTS[0] + PARTS[1])):
        even_ref[...] = message[at : at + even_ref.shape[0]]
    weak = weak_ref[...]
    tangent = []
    for i in range(flags_ref.shape[0]):
        flag = flags_ref[i]
        tangent.append(
            jnp.where(flag == 0, lock_stiffness, jnp.where(flag == 1, -weak, 0.0))
        )
    for x in range(4):
        store_fault(fault_out_ref, x, planes[x], z_elems)
    fault_out_ref[FAULT:] = exact_dot(jnp.concatenate(tangent, axis=0), fault)
    for copy in copies[6:]:
        copy.wait()


def prepare_kernel(cur_ref, material_ref, own_ref, touch_ref, base_ref, edge_part_ref):
    cur = cur_ref[...]
    base_ref[...] = own_force(own_ref, cur, material_ref[0:1], material_ref[1:2])
    edge_part_ref[...] = dot(touch_ref[...], stacked(cur[:PLANE]))


def setup_kernel(next_ref, density_ref, mass_ref, fol_ref, minv_ref, scratch, *, y_elems, z_elems):
    gather = gather_table(y_elems * z_elems, z_elems)
    scratch[...] = jnp.zeros_like(scratch)
    fol_ref[...] = to_elements(lambda c, y: next_ref[c, y], scratch.at[0], gather, y_elems)
    density = to_elements(lambda c, y: density_ref[y], scratch.at[1], gather, y_elems, 2)
    table = mass_ref[...]
    first = lax.axis_index("dom") == 0
    plane = lax.broadcasted_iota(jnp.int32, table.shape, 0) < PLANE
    table = jnp.where(jnp.logical_and(first, plane), 2.0 * table, table)
    minv_ref[...] = jnp.where(table > 0.0, table / jnp.where(table > 0.0, density, 1.0), 0.0)


def step_kernel(*refs, step, last, extra, last_place, pair, y_elems, z_elems):
    cur_ref, fol_ref, minv_ref, base_ref, touch_ref, material_ref, odd_ref, up_ref = refs[:8]
    refs = list(refs[8:])
    down_ref = None if pair else refs.pop(0)
    even_in = jnp.concatenate([refs.pop(0)[...] for _ in PARTS], axis=0)
    down_ref = up_ref if pair else down_ref
    first_up_ref, own_ref, first_own_ref, far_ref, edge_ref = refs[:5]
    refs = refs[5 + extra :]
    if last:
        later_ref, back_ref, out_hbm, later_hbm, scratch, out_ref, sems = refs
        copies = start_copies([(later_ref, later_hbm)], sems)
    else:
        new_ref, *even_outs, odd_out, fault_out = refs
    place = lax.axis_index("dom")
    lanes = cur_ref.shape[1]
    even = place % 2 == 0
    far = jnp.where(place == last_place, 0.0, jnp.where(even, even_in, odd_ref[...]))
    left = jnp.where(place == 0, 0.0, jnp.where(even, odd_ref[...], even_in))
    lane_wide = lax.broadcasted_iota(jnp.int32, (BLOCK, lanes), 1)
    below = jnp.where(
        lane_wide % z_elems != z_elems - 1, pltpu.roll(far[:BLOCK], lanes - 1, 1), 0.0
    )
    far = jnp.concatenate([far, below], axis=0)
    lame_row, shear_row = material_ref[0:1], material_ref[1:2]
    far = jnp.concatenate([stacked(lame_row * far), stacked(shear_row * far)], axis=0)
    left_lame = left[BLOCK - 1 : BLOCK]
    left_shear = left[2 * BLOCK - 1 : 2 * BLOCK]
    from_left = left_lame * touch_ref[:PLANE] + left_shear * touch_ref[PLANE:]
    row, lane = block_iotas(lanes)
    across = lane // z_elems
    shared = row < 3
    add_first = jnp.logical_and(shared, across > 0)
    take_last = jnp.logical_and(shared, across < y_elems - 1)
    pull_first = jnp.logical_and(shared, across == 0)
    pull_last = jnp.logical_and(shared, across == y_elems - 1)
    above = above_lanes(lanes, z_elems)
    middle = lax.broadcasted_iota(jnp.int32, (3, lanes), 0) == 1
    gap = jnp.zeros((5, lanes), jnp.float32)
    if not last:
        fault_out[FAULT:] = jnp.zeros_like(fault_out[FAULT:])
    planes = []
    for x in range(4):
        rows = slice(x * PLANE, (x + 1) * PLANE)
        force = base_ref[rows] + dot(far_ref[rows], far)
        blocks = [force[zl * BLOCK : (zl + 1) * BLOCK] for zl in range(5)]
        if x == 0:
            blocks = [b + from_left[i * BLOCK : (i + 1) * BLOCK] for i, b in enumerate(blocks)]
            blocks[:4] = [b + left[i * BLOCK : (i + 1) * BLOCK] for i, b in enumerate(blocks[:4])]
        blocks[0], blocks[4] = (
            blocks[0] + jnp.where(above, pltpu.roll(blocks[4], 1, 1), 0.0),
            blocks[4] + pltpu.roll(blocks[0], lanes - 1, 1),
        )
        lasts, firsts = pl.ds(x, 3, stride=8), pl.ds(4 + x, 3, stride=8)
        k = slice(FAULT + 4 * step + x, FAULT + 4 * step + x + 1)
        below_stiff = jnp.where(middle, lock_stiffness, first_up_ref[k])
        own_stiff = jnp.where(middle, lock_stiffness, first_own_ref[k])
        pulled = jnp.concatenate(
            [below_stiff * (up_ref[lasts, :] - own_ref[firsts, :]), gap], axis=0
        )
        pulled_last = jnp.concatenate(
            [own_stiff * (down_ref[firsts, :] - own_ref[lasts, :]), gap], axis=0
        )
        for zl in range(5):
            low, high = blocks[zl][:8], blocks[zl][8:]
            move = zl * z_elems if zl < 4 else 1
            blocks[zl] = jnp.concatenate(
                [
                    low
                    + jnp.where(add_first, shifted(high, z_elems), 0.0)
                    - jnp.where(pull_first, shifted(pulled, -move), 0.0),
                    high
                    + jnp.where(take_last, shifted(low, -z_elems), 0.0)
                    - jnp.where(pull_last, shifted(pulled_last, -move - z_elems), 0.0),
                ],
                axis=0,
            )
        plane = (2.0 * cur_ref[rows] - fol_ref[rows]) - minv_ref[rows] * jnp.concatenate(
            blocks, axis=0
        )
        if last:
            planes.append(plane)
        else:
            new_ref[rows] = plane
            store_fault(fault_out, x, plane, z_elems)
            planes.append(stacked(plane))
            if x == 0:
                first = plane[: 4 * BLOCK]
    if last:

        def send(c):
            copy = pltpu.make_async_copy(out_ref.at[c], out_hbm.at[c], sems.at[1 + c])
            copy.start()
            copies.append(copy)

        from_elements(
            jnp.concatenate(planes, axis=0), scratch, back_ref, out_ref, y_elems, send
        )
        for copy in copies:
            copy.wait()
    else:
        edge = dot(edge_ref[...], jnp.concatenate(planes, axis=0))
        right = edge_message(edge, lame_row, shear_row, z_elems)
        message, odd_out[...] = select_messages(place % 2, first, right)
        for even_out, at in zip(even_outs, (0, PARTS[0], PARTS[0] + PARTS[1])):
            even_out[...] = message[at : at + even_out.shape[0]]


def mask_kernel(owner_ref, flags_ref, stress_ref, _, mask_ref, weight_ref, *, z_elems):
    shape = (PATCH_ROWS, mask_ref.shape[1])
    first = (lax.axis_index("dom") - REACH) * PATCH_DEV
    number = lax.broadcasted_iota(jnp.int32, shape, 0) + first
    for x in range(4):
        mask = jnp.where(number == owner_ref[:, x : x + 1], 1.0, 0.0)
        mask_ref[PATCH_ROWS * x : PATCH_ROWS * (x + 1)] = mask
    stress = stress_ref[...]
    weights = []
    for i in range(flags_ref.shape[0]):
        flag = flags_ref[i]
        weights.append(
            stress * jnp.where(flag == 1, 0.5, jnp.where(flag == 2, 1.0, 0.0))
        )
    fault = fault_table(mask_ref.shape[1], z_elems)
    weight_ref[...] = exact_dot(jnp.concatenate(weights, axis=0), fault)


def output_kernel(*refs, pair, steps, y_elems, z_elems):
    field_ref, back_ref, weight_ref = refs[:3]
    out_ref, grad_ref, table_ref, scratch = refs[-4:]
    messages = refs[3:-4]
    count = 2 if pair else 3
    grad = 0.0
    for i in range(steps):
        group = messages[count * i : count * (i + 1)]
        slip = -group[0][:4]
        if i < steps - 1:
            slip = slip + group[-1][4:8]
        grad = grad + slip * weight_ref[4 * i : 4 * i + 4]
    grad_ref[...] = grad
    table_ref[...] = fault_table_back(weight_ref.shape[1], z_elems)
    from_elements(field_ref[...], scratch, back_ref, out_ref, y_elems)


def patch_kernel(*refs, pair, steps):
    mask_ref, weight_ref, grad_ref, table_ref, _ = refs[:5]
    first_ref = refs[5] if pair else refs[6]
    home_out, out_a, out_b, out_c, out_d = refs[-5:]
    place = lax.axis_index("dom")
    grad = grad_ref[...] + first_ref[4:8] * weight_ref[4 * (steps - 1) : 4 * steps]
    total = 0.0
    for x in range(4):
        total = total + mask_ref[PATCH_ROWS * x : PATCH_ROWS * (x + 1)] * grad[x : x + 1]
    total = exact_dot(total, table_ref[...])
    rows = [total[2 * i : 2 * i + 2] for i in range(5)]
    home_out[...] = rows[2]
    even = place % 2 == 0
    out_a[...] = jnp.where(even, rows[3], rows[1])
    out_b[...] = jnp.where(even, rows[1], rows[3])
    low = place % 4 < 2
    out_c[...] = jnp.where(low, rows[4], rows[0])
    out_d[...] = jnp.where(low, rows[0], rows[4])


VMEM = pl.BlockSpec(memory_space=pltpu.VMEM)
HBM = pl.BlockSpec(memory_space=pltpu.HBM)
SMEM = pl.BlockSpec(memory_space=pltpu.SMEM)
ANY = pl.BlockSpec(memory_space=pl.ANY)


def kernel_call(body, outs, args, in_smem=(), scratch=(), in_hbm=(), kept=(), unread=(), stay=False, out_spec=VMEM, **static):
    shapes = []
    for out in outs:
        shape, dtype = out if isinstance(out[0], tuple) else (out, jnp.float32)
        shapes.append((pltpu.VMEM if in_hbm or stay else jax.ShapeDtypeStruct)(shape, dtype))
    specs = [VMEM] * len(args)
    for places, spec in ((in_smem, SMEM), (in_hbm, HBM), (unread, ANY)):
        for i in places:
            specs[i] = spec
    copied = [pltpu.VMEM(args[i].shape, args[i].dtype) for i in in_hbm if i not in kept]
    if in_hbm:
        copied.append(pltpu.SemaphoreType.DMA((len(in_hbm),)))
    return pl.pallas_call(
        functools.partial(body, **static) if static else body,
        out_shape=shapes,
        in_specs=specs,
        out_specs=[out_spec] * len(shapes),
        scratch_shapes=list(scratch) + copied,
        compiler_params=pltpu.CompilerParams(
            vmem_limit_bytes=(56 if in_hbm else 24) * 2**20
        ),
    )(*args)


def swapped(block, distance, group):
    size, across = lax.axis_size("dom"), lax.axis_size("depth")
    partner = {}
    for left in range(size - distance):
        if left // distance % 2 == group:
            partner[left], partner[left + distance] = left + distance, left
    route = []
    for i in range(size):
        for j in range(across):
            side = j if i in partner else min(j ^ 1, across - 1)
            route.append((i * across + j, partner.get(i, i) * across + side))
    return lax.ppermute(block, ("dom", "depth"), route)


def from_behind(block, axis, distance):
    size = lax.axis_size(axis)
    return lax.ppermute(block, axis, [((i - distance) % size, i) for i in range(size)])


def on_device(
    adjoint_now,
    adjoint_next,
    lame_first,
    shear_modulus,
    density,
    branch_flags,
    weak_slope,
    normal_stress,
    patch_owner,
):
    x_elems, y_elems, z_elems = lame_first.shape
    lanes = y_elems * z_elems
    assert x_elems == 1 and lanes == adjoint_now.shape[3]
    steps = branch_flags.shape[0]
    pair = lax.axis_size("depth") == 2
    own_table, far_table, edge_table, touch_table = (jnp.asarray(t) for t in stiffness_tables())
    back = jnp.asarray(back_table(y_elems, z_elems))
    mass = jnp.asarray(mass_table(y_elems, z_elems))
    now = jnp.transpose(adjoint_now, (0, 2, 1, 3))
    following = jnp.transpose(adjoint_next, (0, 2, 1, 3))
    rho = jnp.transpose(density, (1, 0, 2))
    flags = branch_flags[:, 0]
    native = pltpu.VMEM((y_elems, 4 * BLOCK, lanes), jnp.float32)
    field = (4 * PLANE, lanes)
    plane = (4 * BLOCK, lanes)
    parts = [(rows, lanes) for rows in PARTS]

    def exchange(even, odd, fault_rows):
        if pair:
            faults = [from_behind(fault_rows, "depth", 1)]
        else:
            faults = [from_behind(fault_rows, "depth", 1), from_behind(fault_rows, "depth", -1)]
        return [swapped(part, 1, 0) for part in even], swapped(odd, 1, 1), faults

    later_used = (
        edge_table, following, rho, mass, own_table, far_table, touch_table, back, flags,
        normal_stress[0], patch_owner,
    )
    assert len(later_used) == LATER
    first_out = kernel_call(
        first_kernel,
        [field] + parts + [plane, (FAULT + 4 * steps, lanes), (8, lanes)]
        + [(t.shape, t.dtype) for t in later_used],
        (now, flags, weak_slope[0], lame_first[0], shear_modulus[0]) + later_used,
        scratch=[native],
        in_hbm=range(5 + LATER),
        kept=range(5, 5 + LATER),
    )
    cur, *even, odd, fault_rows, material = first_out[:-LATER]
    edge_table, following, rho, mass, own_table, far_table, touch_table, back = first_out[-LATER:-3]
    flags, stress, owner = first_out[-3:]
    even_in, odd_in, fault_in = exchange(even, odd, fault_rows)
    first_fault, first_in = fault_rows, fault_in
    fol, minv = kernel_call(
        setup_kernel,
        [field, field],
        (following, rho, mass),
        scratch=[pltpu.VMEM((2, y_elems, 4 * BLOCK, lanes), jnp.float32)],
        y_elems=y_elems,
        z_elems=z_elems,
    )
    seen = []
    for step in range(steps):
        last = step == steps - 1
        seen += [fault_rows] + fault_in
        base, touch = kernel_call(
            prepare_kernel,
            [field, (2 * PLANE, lanes)],
            [cur, material, own_table, touch_table],
            (),
        )
        args = [cur, fol, minv, base, touch, material, odd_in] + fault_in + even_in
        args += [first_in[0], fault_rows, first_fault, far_table, edge_table]
        static = dict(
            step=step, last=last, extra=1 if last or step == 1 else 0, last_place=lax.axis_size("dom") - 1, pair=pair, y_elems=y_elems,
            z_elems=z_elems,
        )
        if step == 1:
            mask, weight = kernel_call(
                mask_kernel,
                [(4 * PATCH_ROWS, lanes), (4 * steps, lanes)],
                [owner, flags, stress, cur],
                unread=(3,),
                z_elems=z_elems,
            )
            args.append(mask)
        if not last:
            new, *even, odd, new_fault = kernel_call(
                step_kernel,
                [field] + parts + [plane, (SENT_FAULT, lanes)],
                args,
                unread=(len(args) - 1,) if step == 1 else (),
                **static,
            )
            fol, cur, fault_rows = cur, new, new_fault
            even_in, odd_in, fault_in = exchange(even, odd, fault_rows)
        else:
            whole = (3, 4 * y_elems + 1, 4, lanes)
            known = seen[: len(seen) - len(fault_in)]
            later, grad, table = kernel_call(
                output_kernel,
                [whole, (4, lanes), ((lanes, lanes), jnp.bfloat16)],
                [cur, back, weight] + known,
                scratch=[native],
                stay=True,
                pair=pair,
                steps=steps,
                y_elems=y_elems,
                z_elems=z_elems,
            )
            sums = kernel_call(
                patch_kernel,
                [(PATCH_DEV, lanes)] * 5,
                [mask, weight, grad, table, odd_in] + fault_in + even_in + [touch],
                unread=(4,) + tuple(range(5 + len(fault_in), 9 + len(fault_in))),
                pair=pair,
                steps=steps,
            )
            patch_sums = sums[0]
            for i, distance, group in ((2, 1, 1), (4, 2, 1), (3, 2, 0), (1, 1, 0)):
                patch_sums = patch_sums + swapped(sums[i], distance, group)
            earlier, later = kernel_call(
                step_kernel,
                [whole, whole],
                args + [sums[0], later, back],
                scratch=[
                    native, pltpu.VMEM(whole, jnp.float32), pltpu.SemaphoreType.DMA((4,)),
                ],
                unread=(len(args),),
                out_spec=HBM,
                **static,
            )
    return (
        jnp.transpose(earlier, (0, 2, 1, 3)),
        jnp.transpose(later, (0, 2, 1, 3)),
        patch_sums[None],
    )


def solution(mesh):
    return jax.shard_map(
        on_device,
        mesh=mesh,
        in_specs=(
            P(None, "dom", "depth", None),
            P(None, "dom", "depth", None),
            P("dom", "depth", None),
            P("dom", "depth", None),
            P("dom", "depth", None),
            P(None, "depth", "dom", None),
            P("depth", "dom", None),
            P("depth", "dom", None),
            P("depth", "dom"),
        ),
        out_specs=(
            P(None, "dom", "depth", None),
            P(None, "dom", "depth", None),
            P("depth", "dom", None),
        ),
        check_vma=False,
    )
```

```python
import functools
import math

import jax
import jax.numpy as jnp
import ml_dtypes
import numpy as np
from jax import lax
from jax.experimental import pallas as pl
from jax.experimental.pallas import tpu as pltpu
from jax.sharding import PartitionSpec as P

PATCH_DEV = 2
REACH = 2
PATCH_ROWS = 16
LATER = 11
FAULT = 24
SENT_FAULT = 28
PARTS = (24, 24, 16)

time_step = 0.01
lock_stiffness = 0.5

BLOCK = 16
ROWS = ((0, 1, 2), (3, 4, 5), (11, 12, 13), (6, 7, 14), (8, 9, 10))
PLANE = 5 * BLOCK


def basis_tables():
    points = [-1.0, -math.sqrt(3.0 / 7.0), 0.0, math.sqrt(3.0 / 7.0), 1.0]
    quad_weights = np.array([0.1, 49.0 / 90.0, 32.0 / 45.0, 49.0 / 90.0, 0.1])
    products = []
    for first in range(5):
        value = 1.0
        for other in range(5):
            if other != first:
                value = value * (points[first] - points[other])
        products.append(value)
    derivative = np.zeros((5, 5))
    for row in range(5):
        for column in range(5):
            if row == column:
                total = 0.0
                for other in range(5):
                    if other != row:
                        total = total + 1.0 / (points[row] - points[other])
                derivative[row, column] = total
            else:
                derivative[row, column] = (
                    products[row] / products[column] / (points[row] - points[column])
                )
    return (quad_weights, derivative)


def two_parts(table):
    high = table.astype(ml_dtypes.bfloat16)
    low = (table - high.astype(np.float64)).astype(ml_dtypes.bfloat16)
    return np.stack([high, low])


def element_stiffness():
    weights, derivative = basis_tables()
    eye = np.eye(5)
    slope = 2.0 * derivative
    grads = [
        np.kron(slope, np.kron(eye, eye)),
        np.kron(eye, np.kron(eye, slope)),
        np.kron(eye, np.kron(slope, eye)),
    ]
    quad = np.kron(weights, np.kron(weights, weights)) / 8.0
    first = np.zeros((125, 3, 125, 3))
    second = np.zeros((125, 3, 125, 3))
    lap = sum(g.T @ (quad[:, None] * g) for g in grads)
    for c in range(3):
        second[:, c, :, c] += lap
        for d in range(3):
            first[:, c, :, d] += grads[c].T @ (quad[:, None] * grads[d])
            second[:, c, :, d] += grads[d].T @ (quad[:, None] * grads[c])
    where = [
        node // 5 * BLOCK + ROWS[node % 5][c] for node in range(125) for c in range(3)
    ]
    wide = []
    for small in (first, second):
        big = np.zeros((5 * PLANE, 5 * PLANE))
        big[np.ix_(where, where)] = small.reshape(375, 375)
        wide.append(big)
    return wide


OWN_COLS = 384


def padded_table(table, columns):
    return np.pad(table, ((0, 0), (0, columns - table.shape[1])))


@functools.cache
def stiffness_tables():
    wide = element_stiffness()
    own = 4 * PLANE
    planes = [slice(x * PLANE, (x + 1) * PLANE) for x in range(5)]
    inner = np.concatenate([w[:own, :own] for w in wide])

    def three(table):
        high, low = two_parts(table)
        return padded_table(np.concatenate([high, low, high], axis=1), 256)

    def both(rows, columns):
        return three(np.concatenate([w[rows, columns] for w in wide]))

    return (
        two_parts(padded_table(inner, OWN_COLS)),
        np.concatenate([three(w[:own, planes[4]]) for w in wide], axis=1),
        np.concatenate([both(planes[4], planes[x]) for x in range(4)], axis=1),
        both(planes[4], planes[4]),
    )


@functools.cache
def back_table(y_elems, z_elems):
    lanes = y_elems * z_elems
    depth = 4 * z_elems
    back = np.zeros((4 * lanes, y_elems * depth), ml_dtypes.bfloat16)
    for yel in range(y_elems):
        for k in range(z_elems):
            for zl in range(4):
                back[zl * lanes + yel * z_elems + k, yel * depth + 4 * k + zl] = 1
    return back


@functools.cache
def mass_table(y_elems, z_elems):
    weights, _ = basis_tables()
    table = np.zeros((4, 5, BLOCK, y_elems, z_elems))
    for x in range(4):
        mx = 0.2 if x == 0 else weights[x]
        for zl in range(5):
            for yl in range(5):
                for yel in range(y_elems):
                    my = weights[yl]
                    if (yl == 0 and yel > 0) or (yl == 4 and yel < y_elems - 1):
                        my = 0.2
                    mz = np.full(z_elems, weights[zl])
                    if zl == 0:
                        mz[1:] = 0.2
                    if zl == 4:
                        mz[:] = 0.2
                    value = time_step * time_step * 8.0 / (mx * my * mz)
                    if zl == 4:
                        value[-1] = 0.0
                    table[x, zl, list(ROWS[yl]), yel] = value
    return table.reshape(4 * PLANE, y_elems * z_elems).astype(np.float32)


def pieces(value, count):
    out = []
    for _ in range(count):
        piece = value.astype(jnp.bfloat16)
        out.append(piece)
        value = value - piece.astype(jnp.float32)
    return out


def dot(a, b):
    return jnp.dot(a, b, preferred_element_type=jnp.float32)


def exact_dot(value, table, count=3):
    rows = value.shape[0]
    result = dot(jnp.concatenate(pieces(value, count), axis=0), table)
    total = result[:rows]
    for i in range(1, count):
        total = total + result[i * rows : (i + 1) * rows]
    return total


def split_dot(table_high, table_low, value):
    lanes = value.shape[1]
    high, low = pieces(value, 2)
    wide = dot(table_high, jnp.concatenate([high, low], axis=1))
    return wide[:, :lanes] + (wide[:, lanes:] + dot(table_low, high))


def ones_where(rule, shape):
    row = lax.broadcasted_iota(jnp.int32, shape, 0)
    column = lax.broadcasted_iota(jnp.int32, shape, 1)
    return jnp.where(rule(row, column), 1.0, 0.0).astype(jnp.bfloat16)


def gather_table(lanes, z_elems):
    return ones_where(lambda z, c: z == 4 * (c % z_elems) + c // lanes, (lanes, 5 * lanes))


def fault_table(lanes, z_elems):
    return ones_where(lambda z, c: z == 4 * (c % z_elems) + c // z_elems, (lanes, lanes))


def fault_table_back(lanes, z_elems):
    return ones_where(lambda c, z: z == 4 * (c % z_elems) + c // z_elems, (lanes, lanes))


def stacked(value):
    high, low = pieces(value, 2)
    gap = jnp.zeros((256 - 3 * value.shape[0], value.shape[1]), jnp.bfloat16)
    return jnp.concatenate([high, high, low, gap], axis=0)


def to_elements(native, scratch, table, y_elems, parts=3):
    group = 4 * BLOCK
    for c in range(3):
        for y in range(4 * y_elems + 1):
            rows = native(c, y)
            if y < 4 * y_elems:
                scratch[y // 4, pl.ds(ROWS[y % 4][c], 4, stride=BLOCK), :] = rows
            if y % 4 == 0 and y > 0:
                scratch[y // 4 - 1, pl.ds(ROWS[4][c], 4, stride=BLOCK), :] = rows
    high, middle, *low = pieces(
        jnp.concatenate([scratch[i] for i in range(y_elems)], axis=0), parts
    )
    result = dot(
        jnp.concatenate([high, middle], axis=1), jnp.concatenate([table, table], axis=0)
    )
    for piece in low:
        result = result + dot(piece, table)
    lanes = result.shape[1] // 5
    across = lax.broadcasted_iota(jnp.int32, (group, result.shape[1]), 1) % lanes // (
        lanes // y_elems
    )
    total = result[:group]
    for yel in range(1, y_elems):
        total = jnp.where(across == yel, result[yel * group : (yel + 1) * group], total)
    blocks = []
    for x in range(4):
        for zl in range(5):
            blocks.append(total[x * BLOCK : (x + 1) * BLOCK, zl * lanes : (zl + 1) * lanes])
    return jnp.concatenate(blocks, axis=0)


def from_elements(field, scratch, back_ref, out_ref, y_elems, stored=None):
    rows = []
    for x in range(4):
        rows.append(
            jnp.concatenate(
                [field[x * PLANE + zl * BLOCK : x * PLANE + (zl + 1) * BLOCK] for zl in range(4)],
                axis=1,
            )
        )
    result = exact_dot(jnp.concatenate(rows, axis=0), back_ref[...])
    depth = result.shape[1] // y_elems
    for yel in range(y_elems):
        scratch[yel] = result[:, yel * depth : (yel + 1) * depth]
    for c in range(3):
        for y in range(4 * y_elems + 1):
            yel, yl = (y // 4, y % 4) if y < 4 * y_elems else (y_elems - 1, 4)
            out_ref[c, y] = scratch[yel, pl.ds(ROWS[yl][c], 4, stride=BLOCK), :]
        if stored is not None:
            stored(c)


def shifted(rows, lanes):
    lanes = lanes % rows.shape[1]
    return pltpu.roll(rows, lanes, 1) if lanes else rows


def block_iotas(lanes):
    return (
        lax.broadcasted_iota(jnp.int32, (8, lanes), 0),
        lax.broadcasted_iota(jnp.int32, (8, lanes), 1),
    )


def store_fault(out_ref, x, plane, z_elems):
    lanes = plane.shape[1]
    _, lane = block_iotas(lanes)
    first = last = jnp.zeros((8, lanes), jnp.float32)
    for zl in range(4):
        at = zl * BLOCK
        here = lane // z_elems == zl
        first = jnp.where(here, shifted(plane[at : at + 8], zl * z_elems), first)
        last = jnp.where(here, shifted(plane[at + 8 : at + 16], (zl + 1) * z_elems), last)
    out_ref[pl.ds(x, 3, stride=8), :] = last[:3]
    out_ref[pl.ds(4 + x, 3, stride=8), :] = first[:3]


def select_messages(parity, left, right):
    even = parity == 0
    return jnp.where(even, right, left), jnp.where(even, left, right)


def material_rows(lame_ref, shear_ref):
    y_elems, z_elems = lame_ref.shape
    both = jnp.concatenate([lame_ref[...], shear_ref[...]], axis=0)
    spread = ones_where(lambda k, c: c % z_elems == k, (z_elems, y_elems * z_elems))
    tiled = exact_dot(both, spread)
    row = lax.broadcasted_iota(jnp.int32, tiled.shape, 0)
    lane = lax.broadcasted_iota(jnp.int32, tiled.shape, 1)
    kept = jnp.where(row % y_elems == lane // z_elems, tiled, 0.0)
    return (
        jnp.sum(kept[:y_elems], axis=0, keepdims=True),
        jnp.sum(kept[y_elems:], axis=0, keepdims=True),
    )


def above_lanes(lanes, z_elems):
    return lax.broadcasted_iota(jnp.int32, (BLOCK, lanes), 1) % z_elems != 0


def edge_message(result, lame_row, shear_row, z_elems):
    lanes = result.shape[1]
    force = lame_row * result[:PLANE] + shear_row * result[PLANE:]
    top = force[:BLOCK] + jnp.where(
        above_lanes(lanes, z_elems), pltpu.roll(force[4 * BLOCK :], 1, 1), 0.0
    )
    row = lax.broadcasted_iota(jnp.int32, top.shape, 0)
    top = jnp.where(row == BLOCK - 1, lame_row, top)
    second = jnp.where(row == BLOCK - 1, shear_row, force[BLOCK : 2 * BLOCK])
    return jnp.concatenate([top, second, force[2 * BLOCK : 4 * BLOCK]], axis=0)


def own_force(own_ref, cur, lame_row, shear_row):
    rows, lanes = cur.shape
    padded = jnp.concatenate([cur, jnp.zeros((OWN_COLS - rows, lanes), jnp.float32)], axis=0)
    result = split_dot(own_ref[0], own_ref[1], padded)
    return lame_row * result[:rows] + shear_row * result[rows:]


def start_copies(pairs, sems):
    copies = [
        pltpu.make_async_copy(source, target, sems.at[i])
        for i, (source, target) in enumerate(pairs)
    ]
    for copy in copies:
        copy.start()
    return copies


def first_kernel(
    now_hbm,
    flags_hbm,
    weak_hbm,
    lame_hbm,
    shear_hbm,
    *refs,
):
    later_hbm, refs = refs[:LATER], refs[LATER:]
    cur_ref, *even_refs, odd_ref, fault_out_ref, material_ref = refs[:7]
    later_refs, refs = refs[7 : 7 + LATER], refs[7 + LATER :]
    scratch, now_ref, flags_ref, weak_ref, lame_ref, shear_ref, sems = refs
    copies = start_copies(
        [
            (now_hbm, now_ref),
            (later_hbm[0], later_refs[0]),
            (lame_hbm, lame_ref),
            (shear_hbm, shear_ref),
            (flags_hbm, flags_ref),
            (weak_hbm, weak_ref),
        ]
        + list(zip(later_hbm[1:], later_refs[1:])),
        sems,
    )
    edge_ref = later_refs[0]
    y_elems, z_elems = lame_ref.shape
    lanes = y_elems * z_elems
    parity = lax.axis_index("dom") % 2
    gather = gather_table(lanes, z_elems)
    fault = fault_table(lanes, z_elems)
    scratch[...] = jnp.zeros_like(scratch)
    for copy in copies[:6]:
        copy.wait()
    cur = to_elements(lambda c, y: now_ref[c, y], scratch, gather, y_elems)
    cur_ref[...] = cur
    lame_row, shear_row = material_rows(lame_ref, shear_ref)
    material_ref[...] = jnp.concatenate(
        [lame_row, shear_row, jnp.zeros((6, lanes), jnp.float32)], axis=0
    )
    planes = [cur[x * PLANE : (x + 1) * PLANE] for x in range(4)]
    edge = dot(edge_ref[...], jnp.concatenate([stacked(p) for p in planes], axis=0))
    right = edge_message(edge, lame_row, shear_row, z_elems)
    message, odd_ref[...] = select_messages(parity, cur[: 4 * BLOCK], right)
    for even_ref, at in zip(even_refs, (0, PARTS[0], PARTS[0] + PARTS[1])):
        even_ref[...] = message[at : at + even_ref.shape[0]]
    weak = weak_ref[...]
    tangent = []
    for i in range(flags_ref.shape[0]):
        flag = flags_ref[i]
        tangent.append(
            jnp.where(flag == 0, lock_stiffness, jnp.where(flag == 1, -weak, 0.0))
        )
    for x in range(4):
        store_fault(fault_out_ref, x, planes[x], z_elems)
    fault_out_ref[FAULT:] = exact_dot(jnp.concatenate(tangent, axis=0), fault)
    for copy in copies[6:]:
        copy.wait()


def prepare_kernel(cur_ref, material_ref, own_ref, touch_ref, base_ref, edge_part_ref):
    cur = cur_ref[...]
    base_ref[...] = own_force(own_ref, cur, material_ref[0:1], material_ref[1:2])
    edge_part_ref[...] = dot(touch_ref[...], stacked(cur[:PLANE]))


def setup_kernel(next_ref, density_ref, mass_ref, fol_ref, minv_ref, scratch, *, y_elems, z_elems):
    gather = gather_table(y_elems * z_elems, z_elems)
    scratch[...] = jnp.zeros_like(scratch)
    fol_ref[...] = to_elements(lambda c, y: next_ref[c, y], scratch.at[0], gather, y_elems)
    density = to_elements(lambda c, y: density_ref[y], scratch.at[1], gather, y_elems, 2)
    table = mass_ref[...]
    first = lax.axis_index("dom") == 0
    plane = lax.broadcasted_iota(jnp.int32, table.shape, 0) < PLANE
    table = jnp.where(jnp.logical_and(first, plane), 2.0 * table, table)
    minv_ref[...] = jnp.where(table > 0.0, table / jnp.where(table > 0.0, density, 1.0), 0.0)


def step_kernel(*refs, step, last, extra, last_place, pair, y_elems, z_elems):
    cur_ref, fol_ref, minv_ref, base_ref, touch_ref, material_ref, odd_ref, up_ref = refs[:8]
    refs = list(refs[8:])
    down_ref = None if pair else refs.pop(0)
    even_in = jnp.concatenate([refs.pop(0)[...] for _ in PARTS], axis=0)
    down_ref = up_ref if pair else down_ref
    first_up_ref, own_ref, first_own_ref, far_ref, edge_ref = refs[:5]
    refs = refs[5 + extra :]
    if last:
        later_ref, back_ref, out_hbm, later_hbm, scratch, out_ref, sems = refs
        copies = start_copies([(later_ref, later_hbm)], sems)
    else:
        new_ref, *even_outs, odd_out, fault_out = refs
    place = lax.axis_index("dom")
    lanes = cur_ref.shape[1]
    even = place % 2 == 0
    far = jnp.where(place == last_place, 0.0, jnp.where(even, even_in, odd_ref[...]))
    left = jnp.where(place == 0, 0.0, jnp.where(even, odd_ref[...], even_in))
    lane_wide = lax.broadcasted_iota(jnp.int32, (BLOCK, lanes), 1)
    below = jnp.where(
        lane_wide % z_elems != z_elems - 1, pltpu.roll(far[:BLOCK], lanes - 1, 1), 0.0
    )
    far = jnp.concatenate([far, below], axis=0)
    lame_row, shear_row = material_ref[0:1], material_ref[1:2]
    far = jnp.concatenate([stacked(lame_row * far), stacked(shear_row * far)], axis=0)
    left_lame = left[BLOCK - 1 : BLOCK]
    left_shear = left[2 * BLOCK - 1 : 2 * BLOCK]
    from_left = left_lame * touch_ref[:PLANE] + left_shear * touch_ref[PLANE:]
    row, lane = block_iotas(lanes)
    across = lane // z_elems
    shared = row < 3
    add_first = jnp.logical_and(shared, across > 0)
    take_last = jnp.logical_and(shared, across < y_elems - 1)
    pull_first = jnp.logical_and(shared, across == 0)
    pull_last = jnp.logical_and(shared, across == y_elems - 1)
    above = above_lanes(lanes, z_elems)
    middle = lax.broadcasted_iota(jnp.int32, (3, lanes), 0) == 1
    gap = jnp.zeros((5, lanes), jnp.float32)
    if not last:
        fault_out[FAULT:] = jnp.zeros_like(fault_out[FAULT:])
    planes = []
    for x in range(4):
        rows = slice(x * PLANE, (x + 1) * PLANE)
        force = base_ref[rows] + dot(far_ref[rows], far)
        blocks = [force[zl * BLOCK : (zl + 1) * BLOCK] for zl in range(5)]
        if x == 0:
            blocks = [b + from_left[i * BLOCK : (i + 1) * BLOCK] for i, b in enumerate(blocks)]
            blocks[:4] = [b + left[i * BLOCK : (i + 1) * BLOCK] for i, b in enumerate(blocks[:4])]
        blocks[0], blocks[4] = (
            blocks[0] + jnp.where(above, pltpu.roll(blocks[4], 1, 1), 0.0),
            blocks[4] + pltpu.roll(blocks[0], lanes - 1, 1),
        )
        lasts, firsts = pl.ds(x, 3, stride=8), pl.ds(4 + x, 3, stride=8)
        k = slice(FAULT + 4 * step + x, FAULT + 4 * step + x + 1)
        below_stiff = jnp.where(middle, lock_stiffness, first_up_ref[k])
        own_stiff = jnp.where(middle, lock_stiffness, first_own_ref[k])
        pulled = jnp.concatenate(
            [below_stiff * (up_ref[lasts, :] - own_ref[firsts, :]), gap], axis=0
        )
        pulled_last = jnp.concatenate(
            [own_stiff * (down_ref[firsts, :] - own_ref[lasts, :]), gap], axis=0
        )
        for zl in range(5):
            low, high = blocks[zl][:8], blocks[zl][8:]
            move = zl * z_elems if zl < 4 else 1
            blocks[zl] = jnp.concatenate(
                [
                    low
                    + jnp.where(add_first, shifted(high, z_elems), 0.0)
                    - jnp.where(pull_first, shifted(pulled, -move), 0.0),
                    high
                    + jnp.where(take_last, shifted(low, -z_elems), 0.0)
                    - jnp.where(pull_last, shifted(pulled_last, -move - z_elems), 0.0),
                ],
                axis=0,
            )
        plane = (2.0 * cur_ref[rows] - fol_ref[rows]) - minv_ref[rows] * jnp.concatenate(
            blocks, axis=0
        )
        if last:
            planes.append(plane)
        else:
            new_ref[rows] = plane
            store_fault(fault_out, x, plane, z_elems)
            planes.append(stacked(plane))
            if x == 0:
                first = plane[: 4 * BLOCK]
    if last:

        def send(c):
            copy = pltpu.make_async_copy(out_ref.at[c], out_hbm.at[c], sems.at[1 + c])
            copy.start()
            copies.append(copy)

        from_elements(
            jnp.concatenate(planes, axis=0), scratch, back_ref, out_ref, y_elems, send
        )
        for copy in copies:
            copy.wait()
    else:
        edge = dot(edge_ref[...], jnp.concatenate(planes, axis=0))
        right = edge_message(edge, lame_row, shear_row, z_elems)
        message, odd_out[...] = select_messages(place % 2, first, right)
        for even_out, at in zip(even_outs, (0, PARTS[0], PARTS[0] + PARTS[1])):
            even_out[...] = message[at : at + even_out.shape[0]]


def mask_kernel(owner_ref, flags_ref, stress_ref, _, mask_ref, weight_ref, *, z_elems):
    shape = (PATCH_ROWS, mask_ref.shape[1])
    first = (lax.axis_index("dom") - REACH) * PATCH_DEV
    number = lax.broadcasted_iota(jnp.int32, shape, 0) + first
    for x in range(4):
        mask = jnp.where(number == owner_ref[:, x : x + 1], 1.0, 0.0)
        mask_ref[PATCH_ROWS * x : PATCH_ROWS * (x + 1)] = mask
    stress = stress_ref[...]
    weights = []
    for i in range(flags_ref.shape[0]):
        flag = flags_ref[i]
        weights.append(
            stress * jnp.where(flag == 1, 0.5, jnp.where(flag == 2, 1.0, 0.0))
        )
    fault = fault_table(mask_ref.shape[1], z_elems)
    weight_ref[...] = exact_dot(jnp.concatenate(weights, axis=0), fault)


def output_kernel(*refs, pair, steps, y_elems, z_elems):
    field_ref, back_ref, weight_ref = refs[:3]
    out_ref, grad_ref, table_ref, scratch = refs[-4:]
    messages = refs[3:-4]
    count = 2 if pair else 3
    grad = 0.0
    for i in range(steps):
        group = messages[count * i : count * (i + 1)]
        slip = -group[0][:4]
        if i < steps - 1:
            slip = slip + group[-1][4:8]
        grad = grad + slip * weight_ref[4 * i : 4 * i + 4]
    grad_ref[...] = grad
    table_ref[...] = fault_table_back(weight_ref.shape[1], z_elems)
    from_elements(field_ref[...], scratch, back_ref, out_ref, y_elems)


def patch_kernel(*refs, pair, steps):
    mask_ref, weight_ref, grad_ref, table_ref, _ = refs[:5]
    first_ref = refs[5] if pair else refs[6]
    home_out, out_a, out_b, out_c, out_d = refs[-5:]
    place = lax.axis_index("dom")
    grad = grad_ref[...] + first_ref[4:8] * weight_ref[4 * (steps - 1) : 4 * steps]
    total = 0.0
    for x in range(4):
        total = total + mask_ref[PATCH_ROWS * x : PATCH_ROWS * (x + 1)] * grad[x : x + 1]
    total = exact_dot(total, table_ref[...])
    rows = [total[2 * i : 2 * i + 2] for i in range(5)]
    home_out[...] = rows[2]
    even = place % 2 == 0
    out_a[...] = jnp.where(even, rows[3], rows[1])
    out_b[...] = jnp.where(even, rows[1], rows[3])
    low = place % 4 < 2
    out_c[...] = jnp.where(low, rows[4], rows[0])
    out_d[...] = jnp.where(low, rows[0], rows[4])


VMEM = pl.BlockSpec(memory_space=pltpu.VMEM)
HBM = pl.BlockSpec(memory_space=pltpu.HBM)
SMEM = pl.BlockSpec(memory_space=pltpu.SMEM)
ANY = pl.BlockSpec(memory_space=pl.ANY)


def kernel_call(body, outs, args, in_smem=(), scratch=(), in_hbm=(), kept=(), unread=(), stay=False, out_spec=VMEM, **static):
    shapes = []
    for out in outs:
        shape, dtype = out if isinstance(out[0], tuple) else (out, jnp.float32)
        shapes.append((pltpu.VMEM if in_hbm or stay else jax.ShapeDtypeStruct)(shape, dtype))
    specs = [VMEM] * len(args)
    for places, spec in ((in_smem, SMEM), (in_hbm, HBM), (unread, ANY)):
        for i in places:
            specs[i] = spec
    copied = [pltpu.VMEM(args[i].shape, args[i].dtype) for i in in_hbm if i not in kept]
    if in_hbm:
        copied.append(pltpu.SemaphoreType.DMA((len(in_hbm),)))
    return pl.pallas_call(
        functools.partial(body, **static) if static else body,
        out_shape=shapes,
        in_specs=specs,
        out_specs=[out_spec] * len(shapes),
        scratch_shapes=list(scratch) + copied,
        compiler_params=pltpu.CompilerParams(
            vmem_limit_bytes=(56 if in_hbm else 24) * 2**20
        ),
    )(*args)


def swapped(block, distance, group):
    size, across = lax.axis_size("dom"), lax.axis_size("depth")
    partner = {}
    for left in range(size - distance):
        if left // distance % 2 == group:
            partner[left], partner[left + distance] = left + distance, left
    route = []
    for i in range(size):
        for j in range(across):
            side = j if i in partner else min(j ^ 1, across - 1)
            route.append((i * across + j, partner.get(i, i) * across + side))
    return lax.ppermute(block, ("dom", "depth"), route)


def from_behind(block, axis, distance):
    size = lax.axis_size(axis)
    return lax.ppermute(block, axis, [((i - distance) % size, i) for i in range(size)])


def on_device(
    adjoint_now,
    adjoint_next,
    lame_first,
    shear_modulus,
    density,
    branch_flags,
    weak_slope,
    normal_stress,
    patch_owner,
):
    x_elems, y_elems, z_elems = lame_first.shape
    lanes = y_elems * z_elems
    assert x_elems == 1 and lanes == adjoint_now.shape[3]
    steps = branch_flags.shape[0]
    pair = lax.axis_size("depth") == 2
    own_table, far_table, edge_table, touch_table = (jnp.asarray(t) for t in stiffness_tables())
    back = jnp.asarray(back_table(y_elems, z_elems))
    mass = jnp.asarray(mass_table(y_elems, z_elems))
    now = jnp.transpose(adjoint_now, (0, 2, 1, 3))
    following = jnp.transpose(adjoint_next, (0, 2, 1, 3))
    rho = jnp.transpose(density, (1, 0, 2))
    flags = branch_flags[:, 0]
    native = pltpu.VMEM((y_elems, 4 * BLOCK, lanes), jnp.float32)
    field = (4 * PLANE, lanes)
    plane = (4 * BLOCK, lanes)
    parts = [(rows, lanes) for rows in PARTS]

    def exchange(even, odd, fault_rows):
        if pair:
            faults = [from_behind(fault_rows, "depth", 1)]
        else:
            faults = [from_behind(fault_rows, "depth", 1), from_behind(fault_rows, "depth", -1)]
        return [swapped(part, 1, 0) for part in even], swapped(odd, 1, 1), faults

    later_used = (
        edge_table, following, rho, mass, own_table, far_table, touch_table, back, flags,
        normal_stress[0], patch_owner,
    )
    assert len(later_used) == LATER
    first_out = kernel_call(
        first_kernel,
        [field] + parts + [plane, (FAULT + 4 * steps, lanes), (8, lanes)]
        + [(t.shape, t.dtype) for t in later_used],
        (now, flags, weak_slope[0], lame_first[0], shear_modulus[0]) + later_used,
        scratch=[native],
        in_hbm=range(5 + LATER),
        kept=range(5, 5 + LATER),
    )
    cur, *even, odd, fault_rows, material = first_out[:-LATER]
    edge_table, following, rho, mass, own_table, far_table, touch_table, back = first_out[-LATER:-3]
    flags, stress, owner = first_out[-3:]
    even_in, odd_in, fault_in = exchange(even, odd, fault_rows)
    first_fault, first_in = fault_rows, fault_in
    fol, minv = kernel_call(
        setup_kernel,
        [field, field],
        (following, rho, mass),
        scratch=[pltpu.VMEM((2, y_elems, 4 * BLOCK, lanes), jnp.float32)],
        y_elems=y_elems,
        z_elems=z_elems,
    )
    seen = []
    for step in range(steps):
        last = step == steps - 1
        seen += [fault_rows] + fault_in
        base, touch = kernel_call(
            prepare_kernel,
            [field, (2 * PLANE, lanes)],
            [cur, material, own_table, touch_table],
            (),
        )
        args = [cur, fol, minv, base, touch, material, odd_in] + fault_in + even_in
        args += [first_in[0], fault_rows, first_fault, far_table, edge_table]
        static = dict(
            step=step, last=last, extra=1 if last or step == 1 else 0, last_place=lax.axis_size("dom") - 1, pair=pair, y_elems=y_elems,
            z_elems=z_elems,
        )
        if step == 1:
            mask, weight = kernel_call(
                mask_kernel,
                [(4 * PATCH_ROWS, lanes), (4 * steps, lanes)],
                [owner, flags, stress, cur],
                unread=(3,),
                z_elems=z_elems,
            )
            args.append(mask)
        if not last:
            new, *even, odd, new_fault = kernel_call(
                step_kernel,
                [field] + parts + [plane, (SENT_FAULT, lanes)],
                args,
                unread=(len(args) - 1,) if step == 1 else (),
                **static,
            )
            fol, cur, fault_rows = cur, new, new_fault
            even_in, odd_in, fault_in = exchange(even, odd, fault_rows)
        else:
            whole = (3, 4 * y_elems + 1, 4, lanes)
            known = seen[: len(seen) - len(fault_in)]
            later, grad, table = kernel_call(
                output_kernel,
                [whole, (4, lanes), ((lanes, lanes), jnp.bfloat16)],
                [cur, back, weight] + known,
                scratch=[native],
                stay=True,
                pair=pair,
                steps=steps,
                y_elems=y_elems,
                z_elems=z_elems,
            )
            sums = kernel_call(
                patch_kernel,
                [(PATCH_DEV, lanes)] * 5,
                [mask, weight, grad, table, odd_in] + fault_in + even_in + [touch],
                unread=(4,) + tuple(range(5 + len(fault_in), 9 + len(fault_in))),
                pair=pair,
                steps=steps,
            )
            patch_sums = sums[0]
            for i, distance, group in ((4, 2, 1), (2, 1, 1), (3, 2, 0), (1, 1, 0)):
                patch_sums = patch_sums + swapped(sums[i], distance, group)
            earlier, later = kernel_call(
                step_kernel,
                [whole, whole],
                args + [sums[0], later, back],
                scratch=[
                    native, pltpu.VMEM(whole, jnp.float32), pltpu.SemaphoreType.DMA((4,)),
                ],
                unread=(len(args),),
                out_spec=HBM,
                **static,
            )
    return (
        jnp.transpose(earlier, (0, 2, 1, 3)),
        jnp.transpose(later, (0, 2, 1, 3)),
        patch_sums[None],
    )


def solution(mesh):
    return jax.shard_map(
        on_device,
        mesh=mesh,
        in_specs=(
            P(None, "dom", "depth", None),
            P(None, "dom", "depth", None),
            P("dom", "depth", None),
            P("dom", "depth", None),
            P("dom", "depth", None),
            P(None, "depth", "dom", None),
            P("depth", "dom", None),
            P("depth", "dom", None),
            P("depth", "dom"),
        ),
        out_specs=(
            P(None, "dom", "depth", None),
            P(None, "dom", "depth", None),
            P("depth", "dom", None),
        ),
        check_vma=False,
    )
```

```python
import functools
import math

import jax
import jax.numpy as jnp
import ml_dtypes
import numpy as np
from jax import lax
from jax.experimental import pallas as pl
from jax.experimental.pallas import tpu as pltpu
from jax.sharding import PartitionSpec as P

PATCH_DEV = 2
REACH = 2
PATCH_ROWS = 16
LATER = 11
FAULT = 24
SENT_FAULT = 28
PARTS = (24, 24, 16)

time_step = 0.01
lock_stiffness = 0.5

BLOCK = 16
ROWS = ((0, 1, 2), (3, 4, 5), (11, 12, 13), (6, 7, 14), (8, 9, 10))
PLANE = 5 * BLOCK


def basis_tables():
    points = [-1.0, -math.sqrt(3.0 / 7.0), 0.0, math.sqrt(3.0 / 7.0), 1.0]
    quad_weights = np.array([0.1, 49.0 / 90.0, 32.0 / 45.0, 49.0 / 90.0, 0.1])
    products = []
    for first in range(5):
        value = 1.0
        for other in range(5):
            if other != first:
                value = value * (points[first] - points[other])
        products.append(value)
    derivative = np.zeros((5, 5))
    for row in range(5):
        for column in range(5):
            if row == column:
                total = 0.0
                for other in range(5):
                    if other != row:
                        total = total + 1.0 / (points[row] - points[other])
                derivative[row, column] = total
            else:
                derivative[row, column] = (
                    products[row] / products[column] / (points[row] - points[column])
                )
    return (quad_weights, derivative)


def two_parts(table):
    high = table.astype(ml_dtypes.bfloat16)
    low = (table - high.astype(np.float64)).astype(ml_dtypes.bfloat16)
    return np.stack([high, low])


def element_stiffness():
    weights, derivative = basis_tables()
    eye = np.eye(5)
    slope = 2.0 * derivative
    grads = [
        np.kron(slope, np.kron(eye, eye)),
        np.kron(eye, np.kron(eye, slope)),
        np.kron(eye, np.kron(slope, eye)),
    ]
    quad = np.kron(weights, np.kron(weights, weights)) / 8.0
    first = np.zeros((125, 3, 125, 3))
    second = np.zeros((125, 3, 125, 3))
    lap = sum(g.T @ (quad[:, None] * g) for g in grads)
    for c in range(3):
        second[:, c, :, c] += lap
        for d in range(3):
            first[:, c, :, d] += grads[c].T @ (quad[:, None] * grads[d])
            second[:, c, :, d] += grads[d].T @ (quad[:, None] * grads[c])
    where = [
        node // 5 * BLOCK + ROWS[node % 5][c] for node in range(125) for c in range(3)
    ]
    wide = []
    for small in (first, second):
        big = np.zeros((5 * PLANE, 5 * PLANE))
        big[np.ix_(where, where)] = small.reshape(375, 375)
        wide.append(big)
    return wide


OWN_COLS = 384


def padded_table(table, columns):
    return np.pad(table, ((0, 0), (0, columns - table.shape[1])))


@functools.cache
def stiffness_tables():
    wide = element_stiffness()
    own = 4 * PLANE
    planes = [slice(x * PLANE, (x + 1) * PLANE) for x in range(5)]
    inner = np.concatenate([w[:own, :own] for w in wide])

    def three(table):
        high, low = two_parts(table)
        return padded_table(np.concatenate([high, low, high], axis=1), 256)

    def both(rows, columns):
        return three(np.concatenate([w[rows, columns] for w in wide]))

    return (
        two_parts(padded_table(inner, OWN_COLS)),
        np.concatenate([three(w[:own, planes[4]]) for w in wide], axis=1),
        np.concatenate([both(planes[4], planes[x]) for x in range(4)], axis=1),
        both(planes[4], planes[4]),
    )


@functools.cache
def back_table(y_elems, z_elems):
    lanes = y_elems * z_elems
    depth = 4 * z_elems
    back = np.zeros((4 * lanes, y_elems * depth), ml_dtypes.bfloat16)
    for yel in range(y_elems):
        for k in range(z_elems):
            for zl in range(4):
                back[zl * lanes + yel * z_elems + k, yel * depth + 4 * k + zl] = 1
    return back


@functools.cache
def mass_table(y_elems, z_elems):
    weights, _ = basis_tables()
    table = np.zeros((4, 5, BLOCK, y_elems, z_elems))
    for x in range(4):
        mx = 0.2 if x == 0 else weights[x]
        for zl in range(5):
            for yl in range(5):
                for yel in range(y_elems):
                    my = weights[yl]
                    if (yl == 0 and yel > 0) or (yl == 4 and yel < y_elems - 1):
                        my = 0.2
                    mz = np.full(z_elems, weights[zl])
                    if zl == 0:
                        mz[1:] = 0.2
                    if zl == 4:
                        mz[:] = 0.2
                    value = time_step * time_step * 8.0 / (mx * my * mz)
                    if zl == 4:
                        value[-1] = 0.0
                    table[x, zl, list(ROWS[yl]), yel] = value
    return table.reshape(4 * PLANE, y_elems * z_elems).astype(np.float32)


def pieces(value, count):
    out = []
    for _ in range(count):
        piece = value.astype(jnp.bfloat16)
        out.append(piece)
        value = value - piece.astype(jnp.float32)
    return out


def dot(a, b):
    return jnp.dot(a, b, preferred_element_type=jnp.float32)


def exact_dot(value, table, count=3):
    rows = value.shape[0]
    result = dot(jnp.concatenate(pieces(value, count), axis=0), table)
    total = result[:rows]
    for i in range(1, count):
        total = total + result[i * rows : (i + 1) * rows]
    return total


def split_dot(table_high, table_low, value):
    lanes = value.shape[1]
    high, low = pieces(value, 2)
    wide = dot(table_high, jnp.concatenate([high, low], axis=1))
    return wide[:, :lanes] + (wide[:, lanes:] + dot(table_low, high))


def over(value, size):
    if size & (size - 1) == 0:
        return lax.shift_right_logical(value, np.int32(size.bit_length() - 1))
    return lax.div(value, np.int32(size))


def within(value, size):
    return value & (size - 1) if size & (size - 1) == 0 else lax.rem(value, np.int32(size))


def ones_where(shape, axis, wanted):
    line = (shape[0], 1) if axis == 0 else (1, shape[1])
    target = wanted(lax.broadcasted_iota(jnp.int32, line, axis))
    number = lax.broadcasted_iota(jnp.int32, shape, 1 - axis)
    return jnp.where(number == target, 1.0, 0.0).astype(jnp.bfloat16)


def gather_table(lanes, z_elems):
    return ones_where(
        (lanes, 5 * lanes), 1, lambda c: 4 * within(c, z_elems) + over(c, lanes)
    )


def fault_table(lanes, z_elems):
    return ones_where((lanes, lanes), 1, lambda c: 4 * within(c, z_elems) + over(c, z_elems))


def fault_table_back(lanes, z_elems):
    return ones_where((lanes, lanes), 0, lambda c: 4 * within(c, z_elems) + over(c, z_elems))


def stacked(value):
    high, low = pieces(value, 2)
    gap = jnp.zeros((256 - 3 * value.shape[0], value.shape[1]), jnp.bfloat16)
    return jnp.concatenate([high, high, low, gap], axis=0)


def to_elements(native, scratch, table, y_elems, parts=3):
    group = 4 * BLOCK
    for c in range(3):
        for y in range(4 * y_elems + 1):
            rows = native(c, y)
            if y < 4 * y_elems:
                scratch[y // 4, pl.ds(ROWS[y % 4][c], 4, stride=BLOCK), :] = rows
            if y % 4 == 0 and y > 0:
                scratch[y // 4 - 1, pl.ds(ROWS[4][c], 4, stride=BLOCK), :] = rows
    high, middle, *low = pieces(
        jnp.concatenate([scratch[i] for i in range(y_elems)], axis=0), parts
    )
    result = dot(
        jnp.concatenate([high, middle], axis=1), jnp.concatenate([table, table], axis=0)
    )
    for piece in low:
        result = result + dot(piece, table)
    lanes = result.shape[1] // 5
    across = lax.broadcasted_iota(jnp.int32, (1, result.shape[1]), 1)
    across = over(within(across, lanes), lanes // y_elems)
    total = result[:group]
    for yel in range(1, y_elems):
        total = jnp.where(across == yel, result[yel * group : (yel + 1) * group], total)
    blocks = []
    for x in range(4):
        for zl in range(5):
            blocks.append(total[x * BLOCK : (x + 1) * BLOCK, zl * lanes : (zl + 1) * lanes])
    return jnp.concatenate(blocks, axis=0)


def from_elements(field, scratch, back_ref, out_ref, y_elems, stored=None):
    rows = []
    for x in range(4):
        rows.append(
            jnp.concatenate(
                [field[x * PLANE + zl * BLOCK : x * PLANE + (zl + 1) * BLOCK] for zl in range(4)],
                axis=1,
            )
        )
    result = exact_dot(jnp.concatenate(rows, axis=0), back_ref[...])
    depth = result.shape[1] // y_elems
    for yel in range(y_elems):
        scratch[yel] = result[:, yel * depth : (yel + 1) * depth]
    for c in range(3):
        for y in range(4 * y_elems + 1):
            yel, yl = (y // 4, y % 4) if y < 4 * y_elems else (y_elems - 1, 4)
            out_ref[c, y] = scratch[yel, pl.ds(ROWS[yl][c], 4, stride=BLOCK), :]
        if stored is not None:
            stored(c)


def shifted(rows, lanes):
    lanes = lanes % rows.shape[1]
    return pltpu.roll(rows, lanes, 1) if lanes else rows


def block_iotas(lanes):
    return (
        lax.broadcasted_iota(jnp.int32, (8, lanes), 0),
        lax.broadcasted_iota(jnp.int32, (8, lanes), 1),
    )


def store_fault(out_ref, x, plane, z_elems):
    lanes = plane.shape[1]
    _, lane = block_iotas(lanes)
    first = last = jnp.zeros((8, lanes), jnp.float32)
    for zl in range(4):
        at = zl * BLOCK
        here = over(lane, z_elems) == zl
        first = jnp.where(here, shifted(plane[at : at + 8], zl * z_elems), first)
        last = jnp.where(here, shifted(plane[at + 8 : at + 16], (zl + 1) * z_elems), last)
    out_ref[pl.ds(x, 3, stride=8), :] = last[:3]
    out_ref[pl.ds(4 + x, 3, stride=8), :] = first[:3]


def select_messages(parity, left, right):
    even = parity == 0
    return jnp.where(even, right, left), jnp.where(even, left, right)


def material_rows(lame_ref, shear_ref):
    y_elems, z_elems = lame_ref.shape
    both = jnp.concatenate([lame_ref[...], shear_ref[...]], axis=0)
    spread = ones_where((z_elems, y_elems * z_elems), 1, lambda c: within(c, z_elems))
    tiled = exact_dot(both, spread)
    row = lax.broadcasted_iota(jnp.int32, tiled.shape, 0)
    lane = lax.broadcasted_iota(jnp.int32, tiled.shape, 1)
    kept = jnp.where(within(row, y_elems) == over(lane, z_elems), tiled, 0.0)
    return (
        jnp.sum(kept[:y_elems], axis=0, keepdims=True),
        jnp.sum(kept[y_elems:], axis=0, keepdims=True),
    )


def above_lanes(lanes, z_elems):
    return within(lax.broadcasted_iota(jnp.int32, (BLOCK, lanes), 1), z_elems) != 0


def edge_message(result, lame_row, shear_row, z_elems):
    lanes = result.shape[1]
    force = lame_row * result[:PLANE] + shear_row * result[PLANE:]
    top = force[:BLOCK] + jnp.where(
        above_lanes(lanes, z_elems), pltpu.roll(force[4 * BLOCK :], 1, 1), 0.0
    )
    row = lax.broadcasted_iota(jnp.int32, top.shape, 0)
    top = jnp.where(row == BLOCK - 1, lame_row, top)
    second = jnp.where(row == BLOCK - 1, shear_row, force[BLOCK : 2 * BLOCK])
    return jnp.concatenate([top, second, force[2 * BLOCK : 4 * BLOCK]], axis=0)


def own_force(own_ref, cur, lame_row, shear_row):
    rows, lanes = cur.shape
    padded = jnp.concatenate([cur, jnp.zeros((OWN_COLS - rows, lanes), jnp.float32)], axis=0)
    result = split_dot(own_ref[0], own_ref[1], padded)
    return lame_row * result[:rows] + shear_row * result[rows:]


def start_copies(pairs, sems):
    copies = [
        pltpu.make_async_copy(source, target, sems.at[i])
        for i, (source, target) in enumerate(pairs)
    ]
    for copy in copies:
        copy.start()
    return copies


def first_kernel(
    now_hbm,
    flags_hbm,
    weak_hbm,
    lame_hbm,
    shear_hbm,
    *refs,
):
    later_hbm, refs = refs[:LATER], refs[LATER:]
    cur_ref, *even_refs, odd_ref, fault_out_ref, material_ref = refs[:7]
    later_refs, refs = refs[7 : 7 + LATER], refs[7 + LATER :]
    scratch, now_ref, flags_ref, weak_ref, lame_ref, shear_ref, sems = refs
    copies = start_copies(
        [
            (now_hbm, now_ref),
            (later_hbm[0], later_refs[0]),
            (lame_hbm, lame_ref),
            (shear_hbm, shear_ref),
            (flags_hbm, flags_ref),
            (weak_hbm, weak_ref),
        ]
        + list(zip(later_hbm[1:], later_refs[1:])),
        sems,
    )
    edge_ref = later_refs[0]
    y_elems, z_elems = lame_ref.shape
    lanes = y_elems * z_elems
    parity = lax.axis_index("dom") % 2
    gather = gather_table(lanes, z_elems)
    fault = fault_table(lanes, z_elems)
    scratch[...] = jnp.zeros_like(scratch)
    for copy in copies[:6]:
        copy.wait()
    cur = to_elements(lambda c, y: now_ref[c, y], scratch, gather, y_elems)
    cur_ref[...] = cur
    lame_row, shear_row = material_rows(lame_ref, shear_ref)
    material_ref[...] = jnp.concatenate(
        [lame_row, shear_row, jnp.zeros((6, lanes), jnp.float32)], axis=0
    )
    planes = [cur[x * PLANE : (x + 1) * PLANE] for x in range(4)]
    edge = dot(edge_ref[...], jnp.concatenate([stacked(p) for p in planes], axis=0))
    right = edge_message(edge, lame_row, shear_row, z_elems)
    message, odd_ref[...] = select_messages(parity, cur[: 4 * BLOCK], right)
    for even_ref, at in zip(even_refs, (0, PARTS[0], PARTS[0] + PARTS[1])):
        even_ref[...] = message[at : at + even_ref.shape[0]]
    weak = weak_ref[...]
    tangent = []
    for i in range(flags_ref.shape[0]):
        flag = flags_ref[i]
        tangent.append(
            jnp.where(flag == 0, lock_stiffness, jnp.where(flag == 1, -weak, 0.0))
        )
    for x in range(4):
        store_fault(fault_out_ref, x, planes[x], z_elems)
    fault_out_ref[FAULT:] = exact_dot(jnp.concatenate(tangent, axis=0), fault)
    for copy in copies[6:]:
        copy.wait()


def prepare_kernel(cur_ref, material_ref, own_ref, touch_ref, base_ref, edge_part_ref):
    cur = cur_ref[...]
    base_ref[...] = own_force(own_ref, cur, material_ref[0:1], material_ref[1:2])
    edge_part_ref[...] = dot(touch_ref[...], stacked(cur[:PLANE]))


def setup_kernel(next_ref, density_ref, mass_ref, fol_ref, minv_ref, scratch, *, y_elems, z_elems):
    gather = gather_table(y_elems * z_elems, z_elems)
    scratch[...] = jnp.zeros_like(scratch)
    fol_ref[...] = to_elements(lambda c, y: next_ref[c, y], scratch.at[0], gather, y_elems)
    density = to_elements(lambda c, y: density_ref[y], scratch.at[1], gather, y_elems, 2)
    table = mass_ref[...]
    first = lax.axis_index("dom") == 0
    plane = lax.broadcasted_iota(jnp.int32, table.shape, 0) < PLANE
    table = jnp.where(jnp.logical_and(first, plane), 2.0 * table, table)
    minv_ref[...] = jnp.where(table > 0.0, table / jnp.where(table > 0.0, density, 1.0), 0.0)


def step_kernel(*refs, step, last, extra, last_place, pair, y_elems, z_elems):
    cur_ref, fol_ref, minv_ref, base_ref, touch_ref, material_ref, odd_ref, up_ref = refs[:8]
    refs = list(refs[8:])
    down_ref = None if pair else refs.pop(0)
    even_in = jnp.concatenate([refs.pop(0)[...] for _ in PARTS], axis=0)
    down_ref = up_ref if pair else down_ref
    first_up_ref, own_ref, first_own_ref, far_ref, edge_ref = refs[:5]
    refs = refs[5 + extra :]
    if last:
        later_ref, back_ref, out_hbm, later_hbm, scratch, out_ref, sems = refs
        copies = start_copies([(later_ref, later_hbm)], sems)
    else:
        new_ref, *even_outs, odd_out, fault_out = refs
    place = lax.axis_index("dom")
    lanes = cur_ref.shape[1]
    even = place % 2 == 0
    far = jnp.where(place == last_place, 0.0, jnp.where(even, even_in, odd_ref[...]))
    left = jnp.where(place == 0, 0.0, jnp.where(even, odd_ref[...], even_in))
    lane_wide = lax.broadcasted_iota(jnp.int32, (BLOCK, lanes), 1)
    below = jnp.where(
        within(lane_wide, z_elems) != z_elems - 1, pltpu.roll(far[:BLOCK], lanes - 1, 1), 0.0
    )
    far = jnp.concatenate([far, below], axis=0)
    lame_row, shear_row = material_ref[0:1], material_ref[1:2]
    far = jnp.concatenate([stacked(lame_row * far), stacked(shear_row * far)], axis=0)
    left_lame = left[BLOCK - 1 : BLOCK]
    left_shear = left[2 * BLOCK - 1 : 2 * BLOCK]
    from_left = left_lame * touch_ref[:PLANE] + left_shear * touch_ref[PLANE:]
    row, lane = block_iotas(lanes)
    across = over(lane, z_elems)
    shared = row < 3
    add_first = jnp.logical_and(shared, across > 0)
    take_last = jnp.logical_and(shared, across < y_elems - 1)
    pull_first = jnp.logical_and(shared, across == 0)
    pull_last = jnp.logical_and(shared, across == y_elems - 1)
    above = above_lanes(lanes, z_elems)
    middle = lax.broadcasted_iota(jnp.int32, (3, lanes), 0) == 1
    gap = jnp.zeros((5, lanes), jnp.float32)
    if not last:
        fault_out[FAULT:] = jnp.zeros_like(fault_out[FAULT:])
    planes = []
    for x in range(4):
        rows = slice(x * PLANE, (x + 1) * PLANE)
        force = base_ref[rows] + dot(far_ref[rows], far)
        blocks = [force[zl * BLOCK : (zl + 1) * BLOCK] for zl in range(5)]
        if x == 0:
            blocks = [b + from_left[i * BLOCK : (i + 1) * BLOCK] for i, b in enumerate(blocks)]
            blocks[:4] = [b + left[i * BLOCK : (i + 1) * BLOCK] for i, b in enumerate(blocks[:4])]
        blocks[0], blocks[4] = (
            blocks[0] + jnp.where(above, pltpu.roll(blocks[4], 1, 1), 0.0),
            blocks[4] + pltpu.roll(blocks[0], lanes - 1, 1),
        )
        lasts, firsts = pl.ds(x, 3, stride=8), pl.ds(4 + x, 3, stride=8)
        k = slice(FAULT + 4 * step + x, FAULT + 4 * step + x + 1)
        below_stiff = jnp.where(middle, lock_stiffness, first_up_ref[k])
        own_stiff = jnp.where(middle, lock_stiffness, first_own_ref[k])
        pulled = jnp.concatenate(
            [below_stiff * (up_ref[lasts, :] - own_ref[firsts, :]), gap], axis=0
        )
        pulled_last = jnp.concatenate(
            [own_stiff * (down_ref[firsts, :] - own_ref[lasts, :]), gap], axis=0
        )
        for zl in range(5):
            low, high = blocks[zl][:8], blocks[zl][8:]
            move = zl * z_elems if zl < 4 else 1
            blocks[zl] = jnp.concatenate(
                [
                    low
                    + jnp.where(add_first, shifted(high, z_elems), 0.0)
                    - jnp.where(pull_first, shifted(pulled, -move), 0.0),
                    high
                    + jnp.where(take_last, shifted(low, -z_elems), 0.0)
                    - jnp.where(pull_last, shifted(pulled_last, -move - z_elems), 0.0),
                ],
                axis=0,
            )
        plane = (2.0 * cur_ref[rows] - fol_ref[rows]) - minv_ref[rows] * jnp.concatenate(
            blocks, axis=0
        )
        if last:
            planes.append(plane)
        else:
            new_ref[rows] = plane
            store_fault(fault_out, x, plane, z_elems)
            planes.append(stacked(plane))
            if x == 0:
                first = plane[: 4 * BLOCK]
    if last:

        def send(c):
            copy = pltpu.make_async_copy(out_ref.at[c], out_hbm.at[c], sems.at[1 + c])
            copy.start()
            copies.append(copy)

        from_elements(
            jnp.concatenate(planes, axis=0), scratch, back_ref, out_ref, y_elems, send
        )
        for copy in copies:
            copy.wait()
    else:
        edge = dot(edge_ref[...], jnp.concatenate(planes, axis=0))
        right = edge_message(edge, lame_row, shear_row, z_elems)
        message, odd_out[...] = select_messages(place % 2, first, right)
        for even_out, at in zip(even_outs, (0, PARTS[0], PARTS[0] + PARTS[1])):
            even_out[...] = message[at : at + even_out.shape[0]]


def mask_kernel(owner_ref, flags_ref, stress_ref, _, mask_ref, weight_ref, *, z_elems):
    shape = (PATCH_ROWS, mask_ref.shape[1])
    first = (lax.axis_index("dom") - REACH) * PATCH_DEV
    number = lax.broadcasted_iota(jnp.int32, shape, 0) + first
    for x in range(4):
        mask = jnp.where(number == owner_ref[:, x : x + 1], 1.0, 0.0)
        mask_ref[PATCH_ROWS * x : PATCH_ROWS * (x + 1)] = mask
    stress = stress_ref[...]
    weights = []
    for i in range(flags_ref.shape[0]):
        flag = flags_ref[i]
        weights.append(
            stress * jnp.where(flag == 1, 0.5, jnp.where(flag == 2, 1.0, 0.0))
        )
    fault = fault_table(mask_ref.shape[1], z_elems)
    weight_ref[...] = exact_dot(jnp.concatenate(weights, axis=0), fault)


def output_kernel(*refs, pair, steps, y_elems, z_elems):
    field_ref, back_ref, weight_ref = refs[:3]
    out_ref, grad_ref, table_ref, scratch = refs[-4:]
    messages = refs[3:-4]
    count = 2 if pair else 3
    grad = 0.0
    for i in range(steps):
        group = messages[count * i : count * (i + 1)]
        slip = -group[0][:4]
        if i < steps - 1:
            slip = slip + group[-1][4:8]
        grad = grad + slip * weight_ref[4 * i : 4 * i + 4]
    grad_ref[...] = grad
    table_ref[...] = fault_table_back(weight_ref.shape[1], z_elems)
    from_elements(field_ref[...], scratch, back_ref, out_ref, y_elems)


def patch_kernel(*refs, pair, steps):
    mask_ref, weight_ref, grad_ref, table_ref, _ = refs[:5]
    first_ref = refs[5] if pair else refs[6]
    home_out, out_a, out_b, out_c, out_d = refs[-5:]
    place = lax.axis_index("dom")
    grad = grad_ref[...] + first_ref[4:8] * weight_ref[4 * (steps - 1) : 4 * steps]
    total = 0.0
    for x in range(4):
        total = total + mask_ref[PATCH_ROWS * x : PATCH_ROWS * (x + 1)] * grad[x : x + 1]
    total = exact_dot(total, table_ref[...])
    rows = [total[2 * i : 2 * i + 2] for i in range(5)]
    home_out[...] = rows[2]
    even = place % 2 == 0
    out_a[...] = jnp.where(even, rows[3], rows[1])
    out_b[...] = jnp.where(even, rows[1], rows[3])
    low = place % 4 < 2
    out_c[...] = jnp.where(low, rows[4], rows[0])
    out_d[...] = jnp.where(low, rows[0], rows[4])


VMEM = pl.BlockSpec(memory_space=pltpu.VMEM)
HBM = pl.BlockSpec(memory_space=pltpu.HBM)
SMEM = pl.BlockSpec(memory_space=pltpu.SMEM)
ANY = pl.BlockSpec(memory_space=pl.ANY)


def kernel_call(body, outs, args, in_smem=(), scratch=(), in_hbm=(), kept=(), unread=(), stay=False, out_spec=VMEM, **static):
    shapes = []
    for out in outs:
        shape, dtype = out if isinstance(out[0], tuple) else (out, jnp.float32)
        shapes.append((pltpu.VMEM if in_hbm or stay else jax.ShapeDtypeStruct)(shape, dtype))
    specs = [VMEM] * len(args)
    for places, spec in ((in_smem, SMEM), (in_hbm, HBM), (unread, ANY)):
        for i in places:
            specs[i] = spec
    copied = [pltpu.VMEM(args[i].shape, args[i].dtype) for i in in_hbm if i not in kept]
    if in_hbm:
        copied.append(pltpu.SemaphoreType.DMA((len(in_hbm),)))
    return pl.pallas_call(
        functools.partial(body, **static) if static else body,
        out_shape=shapes,
        in_specs=specs,
        out_specs=[out_spec] * len(shapes),
        scratch_shapes=list(scratch) + copied,
        compiler_params=pltpu.CompilerParams(
            vmem_limit_bytes=(56 if in_hbm else 24) * 2**20
        ),
    )(*args)


def swapped(block, distance, group):
    size, across = lax.axis_size("dom"), lax.axis_size("depth")
    partner = {}
    for left in range(size - distance):
        if left // distance % 2 == group:
            partner[left], partner[left + distance] = left + distance, left
    route = []
    for i in range(size):
        for j in range(across):
            side = j if i in partner else min(j ^ 1, across - 1)
            route.append((i * across + j, partner.get(i, i) * across + side))
    return lax.ppermute(block, ("dom", "depth"), route)


def from_behind(block, axis, distance):
    size = lax.axis_size(axis)
    return lax.ppermute(block, axis, [((i - distance) % size, i) for i in range(size)])


def on_device(
    adjoint_now,
    adjoint_next,
    lame_first,
    shear_modulus,
    density,
    branch_flags,
    weak_slope,
    normal_stress,
    patch_owner,
):
    x_elems, y_elems, z_elems = lame_first.shape
    lanes = y_elems * z_elems
    assert x_elems == 1 and lanes == adjoint_now.shape[3]
    steps = branch_flags.shape[0]
    pair = lax.axis_size("depth") == 2
    own_table, far_table, edge_table, touch_table = (jnp.asarray(t) for t in stiffness_tables())
    back = jnp.asarray(back_table(y_elems, z_elems))
    mass = jnp.asarray(mass_table(y_elems, z_elems))
    now = jnp.transpose(adjoint_now, (0, 2, 1, 3))
    following = jnp.transpose(adjoint_next, (0, 2, 1, 3))
    rho = jnp.transpose(density, (1, 0, 2))
    flags = branch_flags[:, 0]
    native = pltpu.VMEM((y_elems, 4 * BLOCK, lanes), jnp.float32)
    field = (4 * PLANE, lanes)
    plane = (4 * BLOCK, lanes)
    parts = [(rows, lanes) for rows in PARTS]

    def exchange(even, odd, fault_rows):
        if pair:
            faults = [from_behind(fault_rows, "depth", 1)]
        else:
            faults = [from_behind(fault_rows, "depth", 1), from_behind(fault_rows, "depth", -1)]
        return [swapped(part, 1, 0) for part in even], swapped(odd, 1, 1), faults

    later_used = (
        edge_table, following, rho, mass, own_table, far_table, touch_table, back, flags,
        normal_stress[0], patch_owner,
    )
    assert len(later_used) == LATER
    first_out = kernel_call(
        first_kernel,
        [field] + parts + [plane, (FAULT + 4 * steps, lanes), (8, lanes)]
        + [(t.shape, t.dtype) for t in later_used],
        (now, flags, weak_slope[0], lame_first[0], shear_modulus[0]) + later_used,
        scratch=[native],
        in_hbm=range(5 + LATER),
        kept=range(5, 5 + LATER),
    )
    cur, *even, odd, fault_rows, material = first_out[:-LATER]
    edge_table, following, rho, mass, own_table, far_table, touch_table, back = first_out[-LATER:-3]
    flags, stress, owner = first_out[-3:]
    even_in, odd_in, fault_in = exchange(even, odd, fault_rows)
    first_fault, first_in = fault_rows, fault_in
    fol, minv = kernel_call(
        setup_kernel,
        [field, field],
        (following, rho, mass),
        scratch=[pltpu.VMEM((2, y_elems, 4 * BLOCK, lanes), jnp.float32)],
        y_elems=y_elems,
        z_elems=z_elems,
    )
    seen = []
    for step in range(steps):
        last = step == steps - 1
        seen += [fault_rows] + fault_in
        base, touch = kernel_call(
            prepare_kernel,
            [field, (2 * PLANE, lanes)],
            [cur, material, own_table, touch_table],
            (),
        )
        args = [cur, fol, minv, base, touch, material, odd_in] + fault_in + even_in
        args += [first_in[0], fault_rows, first_fault, far_table, edge_table]
        static = dict(
            step=step, last=last, extra=1 if last or step == 1 else 0, last_place=lax.axis_size("dom") - 1, pair=pair, y_elems=y_elems,
            z_elems=z_elems,
        )
        if step == 1:
            mask, weight = kernel_call(
                mask_kernel,
                [(4 * PATCH_ROWS, lanes), (4 * steps, lanes)],
                [owner, flags, stress, cur],
                unread=(3,),
                z_elems=z_elems,
            )
            args.append(mask)
        if not last:
            new, *even, odd, new_fault = kernel_call(
                step_kernel,
                [field] + parts + [plane, (SENT_FAULT, lanes)],
                args,
                unread=(len(args) - 1,) if step == 1 else (),
                **static,
            )
            fol, cur, fault_rows = cur, new, new_fault
            even_in, odd_in, fault_in = exchange(even, odd, fault_rows)
        else:
            whole = (3, 4 * y_elems + 1, 4, lanes)
            known = seen[: len(seen) - len(fault_in)]
            later, grad, table = kernel_call(
                output_kernel,
                [whole, (4, lanes), ((lanes, lanes), jnp.bfloat16)],
                [cur, back, weight] + known,
                scratch=[native],
                stay=True,
                pair=pair,
                steps=steps,
                y_elems=y_elems,
                z_elems=z_elems,
            )
            sums = kernel_call(
                patch_kernel,
                [(PATCH_DEV, lanes)] * 5,
                [mask, weight, grad, table, odd_in] + fault_in + even_in + [touch],
                unread=(4,) + tuple(range(5 + len(fault_in), 9 + len(fault_in))),
                pair=pair,
                steps=steps,
            )
            patch_sums = sums[0]
            for i, distance, group in ((4, 2, 1), (2, 1, 1), (3, 2, 0), (1, 1, 0)):
                patch_sums = patch_sums + swapped(sums[i], distance, group)
            earlier, later = kernel_call(
                step_kernel,
                [whole, whole],
                args + [sums[0], later, back],
                scratch=[
                    native, pltpu.VMEM(whole, jnp.float32), pltpu.SemaphoreType.DMA((4,)),
                ],
                unread=(len(args),),
                out_spec=HBM,
                **static,
            )
    return (
        jnp.transpose(earlier, (0, 2, 1, 3)),
        jnp.transpose(later, (0, 2, 1, 3)),
        patch_sums[None],
    )


def solution(mesh):
    return jax.shard_map(
        on_device,
        mesh=mesh,
        in_specs=(
            P(None, "dom", "depth", None),
            P(None, "dom", "depth", None),
            P("dom", "depth", None),
            P("dom", "depth", None),
            P("dom", "depth", None),
            P(None, "depth", "dom", None),
            P("depth", "dom", None),
            P("depth", "dom", None),
            P("depth", "dom"),
        ),
        out_specs=(
            P(None, "dom", "depth", None),
            P(None, "dom", "depth", None),
            P("depth", "dom", None),
        ),
        check_vma=False,
    )
```

```python
import functools
import math

import jax
import jax.numpy as jnp
import ml_dtypes
import numpy as np
from jax import lax
from jax.experimental import pallas as pl
from jax.experimental.pallas import tpu as pltpu
from jax.sharding import PartitionSpec as P

PATCH_DEV = 2
REACH = 2
PATCH_ROWS = 16
LATER = 11
FAULT = 24
SENT_FAULT = 28
SENT = 56
PARTS = (24, 16, 16)

time_step = 0.01
lock_stiffness = 0.5

BLOCK = 16
ROWS = ((4, 5, 6), (0, 1, 2), (8, 9, 10), (3, 7, 11), (12, 13, 14))
PLANE = 5 * BLOCK


def basis_tables():
    points = [-1.0, -math.sqrt(3.0 / 7.0), 0.0, math.sqrt(3.0 / 7.0), 1.0]
    quad_weights = np.array([0.1, 49.0 / 90.0, 32.0 / 45.0, 49.0 / 90.0, 0.1])
    products = []
    for first in range(5):
        value = 1.0
        for other in range(5):
            if other != first:
                value = value * (points[first] - points[other])
        products.append(value)
    derivative = np.zeros((5, 5))
    for row in range(5):
        for column in range(5):
            if row == column:
                total = 0.0
                for other in range(5):
                    if other != row:
                        total = total + 1.0 / (points[row] - points[other])
                derivative[row, column] = total
            else:
                derivative[row, column] = (
                    products[row] / products[column] / (points[row] - points[column])
                )
    return (quad_weights, derivative)


def two_parts(table):
    high = table.astype(ml_dtypes.bfloat16)
    low = (table - high.astype(np.float64)).astype(ml_dtypes.bfloat16)
    return np.stack([high, low])


def element_stiffness():
    weights, derivative = basis_tables()
    eye = np.eye(5)
    slope = 2.0 * derivative
    grads = [
        np.kron(slope, np.kron(eye, eye)),
        np.kron(eye, np.kron(eye, slope)),
        np.kron(eye, np.kron(slope, eye)),
    ]
    quad = np.kron(weights, np.kron(weights, weights)) / 8.0
    first = np.zeros((125, 3, 125, 3))
    second = np.zeros((125, 3, 125, 3))
    lap = sum(g.T @ (quad[:, None] * g) for g in grads)
    for c in range(3):
        second[:, c, :, c] += lap
        for d in range(3):
            first[:, c, :, d] += grads[c].T @ (quad[:, None] * grads[d])
            second[:, c, :, d] += grads[d].T @ (quad[:, None] * grads[c])
    where = [
        node // 5 * BLOCK + ROWS[node % 5][c] for node in range(125) for c in range(3)
    ]
    wide = []
    for small in (first, second):
        big = np.zeros((5 * PLANE, 5 * PLANE))
        big[np.ix_(where, where)] = small.reshape(375, 375)
        wide.append(big)
    return wide


OWN_COLS = 384


def padded_table(table, columns):
    return np.pad(table, ((0, 0), (0, columns - table.shape[1])))


@functools.cache
def stiffness_tables():
    wide = element_stiffness()
    own = 4 * PLANE
    planes = [slice(x * PLANE, (x + 1) * PLANE) for x in range(5)]
    inner = np.concatenate([w[:own, :own] for w in wide])

    def three(table):
        high, low = two_parts(table)
        return padded_table(np.concatenate([high, low, high], axis=1), 256)

    def both(rows, columns):
        return three(np.concatenate([w[rows, columns] for w in wide]))

    return (
        two_parts(padded_table(inner, OWN_COLS)),
        np.concatenate([three(w[:own, planes[4]]) for w in wide], axis=1),
        np.concatenate([both(planes[4], planes[x]) for x in range(4)], axis=1),
        both(planes[4], planes[4]),
    )


@functools.cache
def back_table(y_elems, z_elems):
    lanes = y_elems * z_elems
    depth = 4 * z_elems
    back = np.zeros((4 * lanes, y_elems * depth), ml_dtypes.bfloat16)
    for yel in range(y_elems):
        for k in range(z_elems):
            for zl in range(4):
                back[zl * lanes + yel * z_elems + k, yel * depth + 4 * k + zl] = 1
    return back


@functools.cache
def mass_table(y_elems, z_elems):
    weights, _ = basis_tables()
    table = np.zeros((4, 5, BLOCK, y_elems, z_elems))
    for x in range(4):
        mx = 0.2 if x == 0 else weights[x]
        for zl in range(5):
            for yl in range(5):
                for yel in range(y_elems):
                    my = weights[yl]
                    if (yl == 0 and yel > 0) or (yl == 4 and yel < y_elems - 1):
                        my = 0.2
                    mz = np.full(z_elems, weights[zl])
                    if zl == 0:
                        mz[1:] = 0.2
                    if zl == 4:
                        mz[:] = 0.2
                    value = time_step * time_step * 8.0 / (mx * my * mz)
                    if zl == 4:
                        value[-1] = 0.0
                    table[x, zl, list(ROWS[yl]), yel] = value
    return table.reshape(4 * PLANE, y_elems * z_elems).astype(np.float32)


def pieces(value, count):
    out = []
    for _ in range(count):
        piece = value.astype(jnp.bfloat16)
        out.append(piece)
        value = value - piece.astype(jnp.float32)
    return out


def dot(a, b):
    return jnp.dot(a, b, preferred_element_type=jnp.float32)


def exact_dot(value, table, count=3):
    rows = value.shape[0]
    result = dot(jnp.concatenate(pieces(value, count), axis=0), table)
    total = result[:rows]
    for i in range(1, count):
        total = total + result[i * rows : (i + 1) * rows]
    return total


def split_dot(table_high, table_low, value):
    lanes = value.shape[1]
    high, low = pieces(value, 2)
    wide = dot(table_high, jnp.concatenate([high, low], axis=1))
    return wide[:, :lanes] + (wide[:, lanes:] + dot(table_low, high))


def over(value, size):
    if size & (size - 1) == 0:
        return lax.shift_right_logical(value, np.int32(size.bit_length() - 1))
    return lax.div(value, np.int32(size))


def within(value, size):
    return value & (size - 1) if size & (size - 1) == 0 else lax.rem(value, np.int32(size))


def ones_where(shape, axis, wanted):
    line = (shape[0], 1) if axis == 0 else (1, shape[1])
    target = wanted(lax.broadcasted_iota(jnp.int32, line, axis))
    number = lax.broadcasted_iota(jnp.int32, shape, 1 - axis)
    return jnp.where(number == target, 1.0, 0.0).astype(jnp.bfloat16)


def gather_table(lanes, z_elems):
    return ones_where(
        (lanes, 5 * lanes), 1, lambda c: 4 * within(c, z_elems) + over(c, lanes)
    )


def fault_table(lanes, z_elems):
    return ones_where((lanes, lanes), 1, lambda c: 4 * within(c, z_elems) + over(c, z_elems))


def fault_table_back(lanes, z_elems):
    return ones_where((lanes, lanes), 0, lambda c: 4 * within(c, z_elems) + over(c, z_elems))


def stacked(value):
    high, low = pieces(value, 2)
    gap = jnp.zeros((256 - 3 * value.shape[0], value.shape[1]), jnp.bfloat16)
    return jnp.concatenate([high, high, low, gap], axis=0)


def to_elements(native, scratch, table, y_elems, parts=3):
    group = 4 * BLOCK
    for c in range(3):
        for y in range(4 * y_elems + 1):
            rows = native(c, y)
            if y < 4 * y_elems:
                scratch[y // 4, pl.ds(ROWS[y % 4][c], 4, stride=BLOCK), :] = rows
            if y % 4 == 0 and y > 0:
                scratch[y // 4 - 1, pl.ds(ROWS[4][c], 4, stride=BLOCK), :] = rows
    high, middle, *low = pieces(
        jnp.concatenate([scratch[i] for i in range(y_elems)], axis=0), parts
    )
    result = dot(
        jnp.concatenate([high, middle], axis=1), jnp.concatenate([table, table], axis=0)
    )
    for piece in low:
        result = result + dot(piece, table)
    lanes = result.shape[1] // 5
    across = lax.broadcasted_iota(jnp.int32, (1, result.shape[1]), 1)
    across = over(within(across, lanes), lanes // y_elems)
    total = result[:group]
    for yel in range(1, y_elems):
        total = jnp.where(across == yel, result[yel * group : (yel + 1) * group], total)
    blocks = []
    for x in range(4):
        for zl in range(5):
            blocks.append(total[x * BLOCK : (x + 1) * BLOCK, zl * lanes : (zl + 1) * lanes])
    return jnp.concatenate(blocks, axis=0)


def from_elements(field, scratch, back_ref, out_ref, y_elems, stored=None):
    rows = []
    for x in range(4):
        rows.append(
            jnp.concatenate(
                [field[x * PLANE + zl * BLOCK : x * PLANE + (zl + 1) * BLOCK] for zl in range(4)],
                axis=1,
            )
        )
    result = exact_dot(jnp.concatenate(rows, axis=0), back_ref[...])
    depth = result.shape[1] // y_elems
    for yel in range(y_elems):
        scratch[yel] = result[:, yel * depth : (yel + 1) * depth]
    for c in range(3):
        for y in range(4 * y_elems + 1):
            yel, yl = (y // 4, y % 4) if y < 4 * y_elems else (y_elems - 1, 4)
            out_ref[c, y] = scratch[yel, pl.ds(ROWS[yl][c], 4, stride=BLOCK), :]
        if stored is not None:
            stored(c)


def shifted(rows, lanes):
    lanes = lanes % rows.shape[1]
    return pltpu.roll(rows, lanes, 1) if lanes else rows


def block_iotas(lanes):
    return (
        lax.broadcasted_iota(jnp.int32, (8, lanes), 0),
        lax.broadcasted_iota(jnp.int32, (8, lanes), 1),
    )


def store_fault(out_ref, x, plane, z_elems):
    lanes = plane.shape[1]
    _, lane = block_iotas(lanes)
    first = last = jnp.zeros((8, lanes), jnp.float32)
    for zl in range(4):
        at = zl * BLOCK
        here = over(lane, z_elems) == zl
        first = jnp.where(here, shifted(plane[at : at + 8], zl * z_elems), first)
        last = jnp.where(here, shifted(plane[at + 8 : at + 16], (zl + 1) * z_elems), last)
    out_ref[pl.ds(x, 3, stride=8), :] = last[4:7]
    out_ref[pl.ds(4 + x, 3, stride=8), :] = first[4:7]
    return last


def sent_plane(plane, last):
    return packed(
        [plane[i * BLOCK : i * BLOCK + 8] for i in range(4)],
        [plane[i * BLOCK + 8 : (i + 1) * BLOCK] for i in range(4)],
        last,
    )


def select_messages(parity, left, right):
    even = parity == 0
    return jnp.where(even, right, left), jnp.where(even, left, right)


def material_rows(lame_ref, shear_ref):
    y_elems, z_elems = lame_ref.shape
    both = jnp.concatenate([lame_ref[...], shear_ref[...]], axis=0)
    spread = ones_where((z_elems, y_elems * z_elems), 1, lambda c: within(c, z_elems))
    tiled = exact_dot(both, spread)
    row = lax.broadcasted_iota(jnp.int32, tiled.shape, 0)
    lane = lax.broadcasted_iota(jnp.int32, tiled.shape, 1)
    kept = jnp.where(within(row, y_elems) == over(lane, z_elems), tiled, 0.0)
    return (
        jnp.sum(kept[:y_elems], axis=0, keepdims=True),
        jnp.sum(kept[y_elems:], axis=0, keepdims=True),
    )


def above_lanes(lanes, z_elems):
    return within(lax.broadcasted_iota(jnp.int32, (BLOCK, lanes), 1), z_elems) != 0


def shared_rows(row):
    return jnp.logical_and(row >= 4, row < 7)


def packed(lows, highs, last):
    row, _ = block_iotas(last.shape[1])
    pairs = [
        jnp.where(row < 4, highs[i], pltpu.roll(highs[i + 1], 4, 0)) for i in (0, 2)
    ]
    return jnp.concatenate(list(lows) + pairs + [last], axis=0)


def unpacked(sent):
    parts = [sent[i : i + 8] for i in range(0, SENT, 8)]
    highs = [parts[4], pltpu.roll(parts[4], 4, 0), parts[5], pltpu.roll(parts[5], 4, 0)]
    return parts[:4], highs, parts[6]


def far_plane(sent, z_elems):
    lanes = sent.shape[1]
    lows, highs, last = unpacked(sent)
    row, lane = block_iotas(lanes)
    inner = lane < lanes - z_elems
    below = within(lane, z_elems) != z_elems - 1
    rows = []
    for zl in range(4):
        node = jnp.where(
            inner, shifted(lows[zl], -z_elems), shifted(last, -(zl + 1) * z_elems)
        )
        rows += [lows[zl], jnp.where(row < 4, highs[zl], node)]
    node = jnp.where(inner, shifted(lows[0], -z_elems - 1), shifted(last, -z_elems - 1))
    rows.append(jnp.where(below, shifted(lows[0], -1), 0.0))
    rows.append(jnp.where(below, jnp.where(row < 4, shifted(highs[0], -1), node), 0.0))
    return jnp.concatenate(rows, axis=0)


def left_blocks(sent, z_elems):
    lanes = sent.shape[1]
    lows, highs, last = unpacked(sent)
    row, lane = block_iotas(lanes)
    outer = jnp.logical_and(lane >= lanes - z_elems, shared_rows(row))
    blocks = []
    for zl in range(4):
        node = jnp.where(outer, shifted(last, -(zl + 1) * z_elems), 0.0)
        blocks.append(jnp.concatenate([lows[zl], jnp.where(row < 4, highs[zl], node)], axis=0))
    return blocks, last[0:1], last[1:2]


def edge_message(result, lame_row, shear_row, z_elems):
    lanes = result.shape[1]
    force = lame_row * result[:PLANE] + shear_row * result[PLANE:]
    lows = [force[i * BLOCK : i * BLOCK + 8] for i in range(5)]
    highs = [force[i * BLOCK + 8 : (i + 1) * BLOCK] for i in range(5)]
    row, lane = block_iotas(lanes)
    take = jnp.logical_and(shared_rows(row), over(lane, z_elems) > 0)
    above = within(lane, z_elems) != 0
    corner = jnp.where(above, shifted(highs[4], z_elems + 1), 0.0)
    ends = [shifted(highs[zl], (zl + 1) * z_elems) for zl in range(4)]
    ends[0] = ends[0] + corner
    new_lows = [lows[zl] + jnp.where(take, shifted(highs[zl], z_elems), 0.0) for zl in range(4)]
    new_lows[0] = (
        new_lows[0]
        + jnp.where(above, shifted(lows[4], 1), 0.0)
        + jnp.where(take, corner, 0.0)
    )
    highs[0] = highs[0] + jnp.where(above, shifted(highs[4], 1), 0.0)
    last = ends[3]
    for zl in range(3):
        last = jnp.where(over(lane, z_elems) == zl, ends[zl], last)
    last = jnp.where(row == 0, lame_row, jnp.where(row == 1, shear_row, last))
    return packed(new_lows, highs, last)


def own_force(own_ref, cur, lame_row, shear_row):
    rows, lanes = cur.shape
    padded = jnp.concatenate([cur, jnp.zeros((OWN_COLS - rows, lanes), jnp.float32)], axis=0)
    result = split_dot(own_ref[0], own_ref[1], padded)
    return lame_row * result[:rows] + shear_row * result[rows:]


def start_copies(pairs, sems):
    copies = [
        pltpu.make_async_copy(source, target, sems.at[i])
        for i, (source, target) in enumerate(pairs)
    ]
    for copy in copies:
        copy.start()
    return copies


def first_kernel(
    now_hbm,
    flags_hbm,
    weak_hbm,
    lame_hbm,
    shear_hbm,
    *refs,
):
    later_hbm, refs = refs[:LATER], refs[LATER:]
    cur_ref, *even_refs, odd_ref, fault_out_ref, material_ref = refs[:7]
    later_refs, refs = refs[7 : 7 + LATER], refs[7 + LATER :]
    scratch, now_ref, flags_ref, weak_ref, lame_ref, shear_ref, sems = refs
    copies = start_copies(
        [
            (now_hbm, now_ref),
            (later_hbm[0], later_refs[0]),
            (lame_hbm, lame_ref),
            (shear_hbm, shear_ref),
            (flags_hbm, flags_ref),
            (weak_hbm, weak_ref),
        ]
        + list(zip(later_hbm[1:], later_refs[1:])),
        sems,
    )
    edge_ref = later_refs[0]
    y_elems, z_elems = lame_ref.shape
    lanes = y_elems * z_elems
    parity = lax.axis_index("dom") % 2
    gather = gather_table(lanes, z_elems)
    fault = fault_table(lanes, z_elems)
    scratch[...] = jnp.zeros_like(scratch)
    for copy in copies[:6]:
        copy.wait()
    cur = to_elements(lambda c, y: now_ref[c, y], scratch, gather, y_elems)
    cur_ref[...] = cur
    lame_row, shear_row = material_rows(lame_ref, shear_ref)
    material_ref[...] = jnp.concatenate(
        [lame_row, shear_row, jnp.zeros((6, lanes), jnp.float32)], axis=0
    )
    planes = [cur[x * PLANE : (x + 1) * PLANE] for x in range(4)]
    edge = dot(edge_ref[...], jnp.concatenate([stacked(p) for p in planes], axis=0))
    right = edge_message(edge, lame_row, shear_row, z_elems)
    lasts = [store_fault(fault_out_ref, x, planes[x], z_elems) for x in range(4)]
    message, odd_ref[...] = select_messages(parity, sent_plane(planes[0], lasts[0]), right)
    for even_ref, at in zip(even_refs, (0, PARTS[0], PARTS[0] + PARTS[1])):
        even_ref[...] = message[at : at + even_ref.shape[0]]
    weak = weak_ref[...]
    tangent = []
    for i in range(flags_ref.shape[0]):
        flag = flags_ref[i]
        tangent.append(
            jnp.where(flag == 0, lock_stiffness, jnp.where(flag == 1, -weak, 0.0))
        )
    fault_out_ref[FAULT:] = exact_dot(jnp.concatenate(tangent, axis=0), fault)
    for copy in copies[6:]:
        copy.wait()


def prepare_kernel(cur_ref, material_ref, own_ref, touch_ref, base_ref, edge_part_ref):
    cur = cur_ref[...]
    base_ref[...] = own_force(own_ref, cur, material_ref[0:1], material_ref[1:2])
    edge_part_ref[...] = dot(touch_ref[...], stacked(cur[:PLANE]))


def setup_kernel(next_ref, density_ref, mass_ref, fol_ref, minv_ref, scratch, *, y_elems, z_elems):
    gather = gather_table(y_elems * z_elems, z_elems)
    scratch[...] = jnp.zeros_like(scratch)
    fol_ref[...] = to_elements(lambda c, y: next_ref[c, y], scratch.at[0], gather, y_elems)
    density = to_elements(lambda c, y: density_ref[y], scratch.at[1], gather, y_elems, 2)
    table = mass_ref[...]
    first = lax.axis_index("dom") == 0
    plane = lax.broadcasted_iota(jnp.int32, table.shape, 0) < PLANE
    table = jnp.where(jnp.logical_and(first, plane), 2.0 * table, table)
    minv_ref[...] = jnp.where(table > 0.0, table / jnp.where(table > 0.0, density, 1.0), 0.0)


def step_kernel(*refs, step, last, extra, last_place, pair, y_elems, z_elems):
    cur_ref, fol_ref, minv_ref, base_ref, touch_ref, material_ref, odd_ref, up_ref = refs[:8]
    refs = list(refs[8:])
    down_ref = None if pair else refs.pop(0)
    even_in = jnp.concatenate([refs.pop(0)[...] for _ in PARTS], axis=0)
    down_ref = up_ref if pair else down_ref
    first_up_ref, own_ref, first_own_ref, far_ref, edge_ref = refs[:5]
    refs = refs[5 + extra :]
    if last:
        later_ref, back_ref, out_hbm, later_hbm, scratch, out_ref, sems = refs
        copies = start_copies([(later_ref, later_hbm)], sems)
    else:
        new_ref, *even_outs, odd_out, fault_out = refs
    place = lax.axis_index("dom")
    lanes = cur_ref.shape[1]
    even = place % 2 == 0
    far = jnp.where(place == last_place, 0.0, jnp.where(even, even_in, odd_ref[...]))
    left = jnp.where(place == 0, 0.0, jnp.where(even, odd_ref[...], even_in))
    far = far_plane(far, z_elems)
    left, left_lame, left_shear = left_blocks(left, z_elems)
    lame_row, shear_row = material_ref[0:1], material_ref[1:2]
    far = jnp.concatenate([stacked(lame_row * far), stacked(shear_row * far)], axis=0)
    from_left = left_lame * touch_ref[:PLANE] + left_shear * touch_ref[PLANE:]
    row, lane = block_iotas(lanes)
    across = over(lane, z_elems)
    shared = shared_rows(row)
    add_first = jnp.logical_and(shared, across > 0)
    take_last = jnp.logical_and(shared, across < y_elems - 1)
    pull_first = jnp.logical_and(shared, across == 0)
    pull_last = jnp.logical_and(shared, across == y_elems - 1)
    above = above_lanes(lanes, z_elems)
    middle = lax.broadcasted_iota(jnp.int32, (3, lanes), 0) == 1
    gap = jnp.zeros((4, lanes), jnp.float32)
    if not last:
        fault_out[FAULT:] = jnp.zeros_like(fault_out[FAULT:])
    planes = []
    for x in range(4):
        rows = slice(x * PLANE, (x + 1) * PLANE)
        force = base_ref[rows] + dot(far_ref[rows], far)
        blocks = [force[zl * BLOCK : (zl + 1) * BLOCK] for zl in range(5)]
        if x == 0:
            blocks = [b + from_left[i * BLOCK : (i + 1) * BLOCK] for i, b in enumerate(blocks)]
            blocks[:4] = [b + left[i] for i, b in enumerate(blocks[:4])]
        blocks[0], blocks[4] = (
            blocks[0] + jnp.where(above, pltpu.roll(blocks[4], 1, 1), 0.0),
            blocks[4] + pltpu.roll(blocks[0], lanes - 1, 1),
        )
        lasts, firsts = pl.ds(x, 3, stride=8), pl.ds(4 + x, 3, stride=8)
        k = slice(FAULT + 4 * step + x, FAULT + 4 * step + x + 1)
        below_stiff = jnp.where(middle, lock_stiffness, first_up_ref[k])
        own_stiff = jnp.where(middle, lock_stiffness, first_own_ref[k])
        pulled = jnp.concatenate(
            [gap, below_stiff * (up_ref[lasts, :] - own_ref[firsts, :]), gap[:1]], axis=0
        )
        pulled_last = jnp.concatenate(
            [gap, own_stiff * (down_ref[firsts, :] - own_ref[lasts, :]), gap[:1]], axis=0
        )
        for zl in range(5):
            low, high = blocks[zl][:8], blocks[zl][8:]
            move = zl * z_elems if zl < 4 else 1
            blocks[zl] = jnp.concatenate(
                [
                    low
                    + jnp.where(add_first, shifted(high, z_elems), 0.0)
                    - jnp.where(pull_first, shifted(pulled, -move), 0.0),
                    high
                    + jnp.where(take_last, shifted(low, -z_elems), 0.0)
                    - jnp.where(pull_last, shifted(pulled_last, -move - z_elems), 0.0),
                ],
                axis=0,
            )
        plane = (2.0 * cur_ref[rows] - fol_ref[rows]) - minv_ref[rows] * jnp.concatenate(
            blocks, axis=0
        )
        if last:
            planes.append(plane)
        else:
            new_ref[rows] = plane
            end = store_fault(fault_out, x, plane, z_elems)
            planes.append(stacked(plane))
            if x == 0:
                first = sent_plane(plane, end)
    if last:

        def send(c):
            copy = pltpu.make_async_copy(out_ref.at[c], out_hbm.at[c], sems.at[1 + c])
            copy.start()
            copies.append(copy)

        from_elements(
            jnp.concatenate(planes, axis=0), scratch, back_ref, out_ref, y_elems, send
        )
        for copy in copies:
            copy.wait()
    else:
        edge = dot(edge_ref[...], jnp.concatenate(planes, axis=0))
        right = edge_message(edge, lame_row, shear_row, z_elems)
        message, odd_out[...] = select_messages(place % 2, first, right)
        for even_out, at in zip(even_outs, (0, PARTS[0], PARTS[0] + PARTS[1])):
            even_out[...] = message[at : at + even_out.shape[0]]


def mask_kernel(owner_ref, flags_ref, stress_ref, _, mask_ref, weight_ref, *, z_elems):
    shape = (PATCH_ROWS, mask_ref.shape[1])
    first = (lax.axis_index("dom") - REACH) * PATCH_DEV
    number = lax.broadcasted_iota(jnp.int32, shape, 0) + first
    for x in range(4):
        mask = jnp.where(number == owner_ref[:, x : x + 1], 1.0, 0.0)
        mask_ref[PATCH_ROWS * x : PATCH_ROWS * (x + 1)] = mask
    stress = stress_ref[...]
    weights = []
    for i in range(flags_ref.shape[0]):
        flag = flags_ref[i]
        weights.append(
            stress * jnp.where(flag == 1, 0.5, jnp.where(flag == 2, 1.0, 0.0))
        )
    fault = fault_table(mask_ref.shape[1], z_elems)
    weight_ref[...] = exact_dot(jnp.concatenate(weights, axis=0), fault)


def output_kernel(*refs, pair, steps, y_elems, z_elems):
    field_ref, back_ref, weight_ref = refs[:3]
    out_ref, grad_ref, table_ref, scratch = refs[-4:]
    messages = refs[3:-4]
    count = 2 if pair else 3
    grad = 0.0
    for i in range(steps):
        group = messages[count * i : count * (i + 1)]
        slip = -group[0][:4]
        if i < steps - 1:
            slip = slip + group[-1][4:8]
        grad = grad + slip * weight_ref[4 * i : 4 * i + 4]
    grad_ref[...] = grad
    table_ref[...] = fault_table_back(weight_ref.shape[1], z_elems)
    from_elements(field_ref[...], scratch, back_ref, out_ref, y_elems)


def patch_kernel(*refs, pair, steps):
    mask_ref, weight_ref, grad_ref, table_ref, _ = refs[:5]
    first_ref = refs[5] if pair else refs[6]
    home_out, out_a, out_b, out_c, out_d = refs[-5:]
    place = lax.axis_index("dom")
    grad = grad_ref[...] + first_ref[4:8] * weight_ref[4 * (steps - 1) : 4 * steps]
    total = 0.0
    for x in range(4):
        total = total + mask_ref[PATCH_ROWS * x : PATCH_ROWS * (x + 1)] * grad[x : x + 1]
    total = exact_dot(total, table_ref[...])
    rows = [total[2 * i : 2 * i + 2] for i in range(5)]
    home_out[...] = rows[2]
    even = place % 2 == 0
    out_a[...] = jnp.where(even, rows[3], rows[1])
    out_b[...] = jnp.where(even, rows[1], rows[3])
    low = place % 4 < 2
    out_c[...] = jnp.where(low, rows[4], rows[0])
    out_d[...] = jnp.where(low, rows[0], rows[4])


VMEM = pl.BlockSpec(memory_space=pltpu.VMEM)
HBM = pl.BlockSpec(memory_space=pltpu.HBM)
SMEM = pl.BlockSpec(memory_space=pltpu.SMEM)
ANY = pl.BlockSpec(memory_space=pl.ANY)


def kernel_call(body, outs, args, in_smem=(), scratch=(), in_hbm=(), kept=(), unread=(), stay=False, out_spec=VMEM, **static):
    shapes = []
    for out in outs:
        shape, dtype = out if isinstance(out[0], tuple) else (out, jnp.float32)
        shapes.append((pltpu.VMEM if in_hbm or stay else jax.ShapeDtypeStruct)(shape, dtype))
    specs = [VMEM] * len(args)
    for places, spec in ((in_smem, SMEM), (in_hbm, HBM), (unread, ANY)):
        for i in places:
            specs[i] = spec
    copied = [pltpu.VMEM(args[i].shape, args[i].dtype) for i in in_hbm if i not in kept]
    if in_hbm:
        copied.append(pltpu.SemaphoreType.DMA((len(in_hbm),)))
    return pl.pallas_call(
        functools.partial(body, **static) if static else body,
        out_shape=shapes,
        in_specs=specs,
        out_specs=[out_spec] * len(shapes),
        scratch_shapes=list(scratch) + copied,
        compiler_params=pltpu.CompilerParams(
            vmem_limit_bytes=(56 if in_hbm else 24) * 2**20
        ),
    )(*args)


def swapped(block, distance, group):
    size, across = lax.axis_size("dom"), lax.axis_size("depth")
    partner = {}
    for left in range(size - distance):
        if left // distance % 2 == group:
            partner[left], partner[left + distance] = left + distance, left
    route = []
    for i in range(size):
        for j in range(across):
            side = j if i in partner else min(j ^ 1, across - 1)
            route.append((i * across + j, partner.get(i, i) * across + side))
    return lax.ppermute(block, ("dom", "depth"), route)


def from_behind(block, axis, distance):
    size = lax.axis_size(axis)
    return lax.ppermute(block, axis, [((i - distance) % size, i) for i in range(size)])


def on_device(
    adjoint_now,
    adjoint_next,
    lame_first,
    shear_modulus,
    density,
    branch_flags,
    weak_slope,
    normal_stress,
    patch_owner,
):
    x_elems, y_elems, z_elems = lame_first.shape
    lanes = y_elems * z_elems
    assert x_elems == 1 and lanes == adjoint_now.shape[3]
    steps = branch_flags.shape[0]
    pair = lax.axis_size("depth") == 2
    own_table, far_table, edge_table, touch_table = (jnp.asarray(t) for t in stiffness_tables())
    back = jnp.asarray(back_table(y_elems, z_elems))
    mass = jnp.asarray(mass_table(y_elems, z_elems))
    now = jnp.transpose(adjoint_now, (0, 2, 1, 3))
    following = jnp.transpose(adjoint_next, (0, 2, 1, 3))
    rho = jnp.transpose(density, (1, 0, 2))
    flags = branch_flags[:, 0]
    native = pltpu.VMEM((y_elems, 4 * BLOCK, lanes), jnp.float32)
    field = (4 * PLANE, lanes)
    plane = (SENT, lanes)
    parts = [(rows, lanes) for rows in PARTS]

    def exchange(even, odd, fault_rows):
        if pair:
            faults = [from_behind(fault_rows, "depth", 1)]
        else:
            faults = [from_behind(fault_rows, "depth", 1), from_behind(fault_rows, "depth", -1)]
        return [swapped(part, 1, 0) for part in even], swapped(odd, 1, 1), faults

    later_used = (
        edge_table, following, rho, mass, own_table, far_table, touch_table, back, flags,
        normal_stress[0], patch_owner,
    )
    assert len(later_used) == LATER
    first_out = kernel_call(
        first_kernel,
        [field] + parts + [plane, (FAULT + 4 * steps, lanes), (8, lanes)]
        + [(t.shape, t.dtype) for t in later_used],
        (now, flags, weak_slope[0], lame_first[0], shear_modulus[0]) + later_used,
        scratch=[native],
        in_hbm=range(5 + LATER),
        kept=range(5, 5 + LATER),
    )
    cur, *even, odd, fault_rows, material = first_out[:-LATER]
    edge_table, following, rho, mass, own_table, far_table, touch_table, back = first_out[-LATER:-3]
    flags, stress, owner = first_out[-3:]
    even_in, odd_in, fault_in = exchange(even, odd, fault_rows)
    first_fault, first_in = fault_rows, fault_in
    fol, minv = kernel_call(
        setup_kernel,
        [field, field],
        (following, rho, mass),
        scratch=[pltpu.VMEM((2, y_elems, 4 * BLOCK, lanes), jnp.float32)],
        y_elems=y_elems,
        z_elems=z_elems,
    )
    seen = []
    for step in range(steps):
        last = step == steps - 1
        seen += [fault_rows] + fault_in
        base, touch = kernel_call(
            prepare_kernel,
            [field, (2 * PLANE, lanes)],
            [cur, material, own_table, touch_table],
            (),
        )
        args = [cur, fol, minv, base, touch, material, odd_in] + fault_in + even_in
        args += [first_in[0], fault_rows, first_fault, far_table, edge_table]
        static = dict(
            step=step, last=last, extra=1 if last or step == 1 else 0, last_place=lax.axis_size("dom") - 1, pair=pair, y_elems=y_elems,
            z_elems=z_elems,
        )
        if step == 1:
            mask, weight = kernel_call(
                mask_kernel,
                [(4 * PATCH_ROWS, lanes), (4 * steps, lanes)],
                [owner, flags, stress, cur],
                unread=(3,),
                z_elems=z_elems,
            )
            args.append(mask)
        if not last:
            new, *even, odd, new_fault = kernel_call(
                step_kernel,
                [field] + parts + [plane, (SENT_FAULT, lanes)],
                args,
                unread=(len(args) - 1,) if step == 1 else (),
                **static,
            )
            fol, cur, fault_rows = cur, new, new_fault
            even_in, odd_in, fault_in = exchange(even, odd, fault_rows)
        else:
            whole = (3, 4 * y_elems + 1, 4, lanes)
            known = seen[: len(seen) - len(fault_in)]
            later, grad, table = kernel_call(
                output_kernel,
                [whole, (4, lanes), ((lanes, lanes), jnp.bfloat16)],
                [cur, back, weight] + known,
                scratch=[native],
                stay=True,
                pair=pair,
                steps=steps,
                y_elems=y_elems,
                z_elems=z_elems,
            )
            sums = kernel_call(
                patch_kernel,
                [(PATCH_DEV, lanes)] * 5,
                [mask, weight, grad, table, odd_in] + fault_in + even_in + [touch],
                unread=(4,) + tuple(range(5 + len(fault_in), 9 + len(fault_in))),
                pair=pair,
                steps=steps,
            )
            patch_sums = sums[0]
            for i, distance, group in ((4, 2, 1), (2, 1, 1), (3, 2, 0), (1, 1, 0)):
                patch_sums = patch_sums + swapped(sums[i], distance, group)
            earlier, later = kernel_call(
                step_kernel,
                [whole, whole],
                args + [sums[0], later, back],
                scratch=[
                    native, pltpu.VMEM(whole, jnp.float32), pltpu.SemaphoreType.DMA((4,)),
                ],
                unread=(len(args),),
                out_spec=HBM,
                **static,
            )
    return (
        jnp.transpose(earlier, (0, 2, 1, 3)),
        jnp.transpose(later, (0, 2, 1, 3)),
        patch_sums[None],
    )


def solution(mesh):
    return jax.shard_map(
        on_device,
        mesh=mesh,
        in_specs=(
            P(None, "dom", "depth", None),
            P(None, "dom", "depth", None),
            P("dom", "depth", None),
            P("dom", "depth", None),
            P("dom", "depth", None),
            P(None, "depth", "dom", None),
            P("depth", "dom", None),
            P("depth", "dom", None),
            P("depth", "dom"),
        ),
        out_specs=(
            P(None, "dom", "depth", None),
            P(None, "dom", "depth", None),
            P("depth", "dom", None),
        ),
        check_vma=False,
    )
```

```python
import functools
import math

import jax
import jax.numpy as jnp
import ml_dtypes
import numpy as np
from jax import lax
from jax.experimental import pallas as pl
from jax.experimental.pallas import tpu as pltpu
from jax.sharding import PartitionSpec as P

PATCH_DEV = 2
REACH = 2
PATCH_ROWS = 16
LATER = 11
FAULT = 24
SENT_FAULT = 24
SENT = 56
PARTS = (56,)

time_step = 0.01
lock_stiffness = 0.5

BLOCK = 16
ROWS = ((4, 5, 6), (0, 1, 2), (8, 9, 10), (3, 7, 11), (12, 13, 14))
PLANE = 5 * BLOCK


def basis_tables():
    points = [-1.0, -math.sqrt(3.0 / 7.0), 0.0, math.sqrt(3.0 / 7.0), 1.0]
    quad_weights = np.array([0.1, 49.0 / 90.0, 32.0 / 45.0, 49.0 / 90.0, 0.1])
    products = []
    for first in range(5):
        value = 1.0
        for other in range(5):
            if other != first:
                value = value * (points[first] - points[other])
        products.append(value)
    derivative = np.zeros((5, 5))
    for row in range(5):
        for column in range(5):
            if row == column:
                total = 0.0
                for other in range(5):
                    if other != row:
                        total = total + 1.0 / (points[row] - points[other])
                derivative[row, column] = total
            else:
                derivative[row, column] = (
                    products[row] / products[column] / (points[row] - points[column])
                )
    return (quad_weights, derivative)


def two_parts(table):
    high = table.astype(ml_dtypes.bfloat16)
    low = (table - high.astype(np.float64)).astype(ml_dtypes.bfloat16)
    return np.stack([high, low])


def element_stiffness():
    weights, derivative = basis_tables()
    eye = np.eye(5)
    slope = 2.0 * derivative
    grads = [
        np.kron(slope, np.kron(eye, eye)),
        np.kron(eye, np.kron(eye, slope)),
        np.kron(eye, np.kron(slope, eye)),
    ]
    quad = np.kron(weights, np.kron(weights, weights)) / 8.0
    first = np.zeros((125, 3, 125, 3))
    second = np.zeros((125, 3, 125, 3))
    lap = sum(g.T @ (quad[:, None] * g) for g in grads)
    for c in range(3):
        second[:, c, :, c] += lap
        for d in range(3):
            first[:, c, :, d] += grads[c].T @ (quad[:, None] * grads[d])
            second[:, c, :, d] += grads[d].T @ (quad[:, None] * grads[c])
    where = [
        node // 5 * BLOCK + ROWS[node % 5][c] for node in range(125) for c in range(3)
    ]
    wide = []
    for small in (first, second):
        big = np.zeros((5 * PLANE, 5 * PLANE))
        big[np.ix_(where, where)] = small.reshape(375, 375)
        wide.append(big)
    return wide


OWN_COLS = 384


def padded_table(table, columns):
    return np.pad(table, ((0, 0), (0, columns - table.shape[1])))


@functools.cache
def stiffness_tables():
    wide = element_stiffness()
    own = 4 * PLANE
    planes = [slice(x * PLANE, (x + 1) * PLANE) for x in range(5)]
    inner = np.concatenate([w[:own, :own] for w in wide])

    def three(table):
        high, low = two_parts(table)
        return padded_table(np.concatenate([high, low, high], axis=1), 256)

    def both(rows, columns):
        return three(np.concatenate([w[rows, columns] for w in wide]))

    return (
        two_parts(padded_table(inner, OWN_COLS)),
        np.concatenate([three(w[:own, planes[4]]) for w in wide], axis=1),
        np.concatenate([both(planes[4], planes[x]) for x in range(4)], axis=1),
        both(planes[4], planes[4]),
    )


@functools.cache
def back_table(y_elems, z_elems):
    lanes = y_elems * z_elems
    depth = 4 * z_elems
    back = np.zeros((4 * lanes, y_elems * depth), ml_dtypes.bfloat16)
    for yel in range(y_elems):
        for k in range(z_elems):
            for zl in range(4):
                back[zl * lanes + yel * z_elems + k, yel * depth + 4 * k + zl] = 1
    return back


@functools.cache
def mass_table(y_elems, z_elems):
    weights, _ = basis_tables()
    table = np.zeros((4, 5, BLOCK, y_elems, z_elems))
    for x in range(4):
        mx = 0.2 if x == 0 else weights[x]
        for zl in range(5):
            for yl in range(5):
                for yel in range(y_elems):
                    my = weights[yl]
                    if (yl == 0 and yel > 0) or (yl == 4 and yel < y_elems - 1):
                        my = 0.2
                    mz = np.full(z_elems, weights[zl])
                    if zl == 0:
                        mz[1:] = 0.2
                    if zl == 4:
                        mz[:] = 0.2
                    value = time_step * time_step * 8.0 / (mx * my * mz)
                    if zl == 4:
                        value[-1] = 0.0
                    table[x, zl, list(ROWS[yl]), yel] = value
    return table.reshape(4 * PLANE, y_elems * z_elems).astype(np.float32)


def pieces(value, count):
    out = []
    for _ in range(count):
        piece = value.astype(jnp.bfloat16)
        out.append(piece)
        value = value - piece.astype(jnp.float32)
    return out


def dot(a, b):
    return jnp.dot(a, b, preferred_element_type=jnp.float32)


def exact_dot(value, table, count=3):
    rows = value.shape[0]
    result = dot(jnp.concatenate(pieces(value, count), axis=0), table)
    total = result[:rows]
    for i in range(1, count):
        total = total + result[i * rows : (i + 1) * rows]
    return total


def split_dot(table_high, table_low, value):
    lanes = value.shape[1]
    high, low = pieces(value, 2)
    wide = dot(table_high, jnp.concatenate([high, low], axis=1))
    return wide[:, :lanes] + (wide[:, lanes:] + dot(table_low, high))


def over(value, size):
    if size & (size - 1) == 0:
        return lax.shift_right_logical(value, np.int32(size.bit_length() - 1))
    return lax.div(value, np.int32(size))


def within(value, size):
    return value & (size - 1) if size & (size - 1) == 0 else lax.rem(value, np.int32(size))


def ones_where(shape, axis, wanted):
    line = (shape[0], 1) if axis == 0 else (1, shape[1])
    target = wanted(lax.broadcasted_iota(jnp.int32, line, axis))
    number = lax.broadcasted_iota(jnp.int32, shape, 1 - axis)
    return jnp.where(number == target, 1.0, 0.0).astype(jnp.bfloat16)


def gather_table(lanes, z_elems):
    return ones_where(
        (lanes, 5 * lanes), 1, lambda c: 4 * within(c, z_elems) + over(c, lanes)
    )


def fault_table(lanes, z_elems):
    return ones_where((lanes, lanes), 1, lambda c: 4 * within(c, z_elems) + over(c, z_elems))


def fault_table_back(lanes, z_elems):
    return ones_where((lanes, lanes), 0, lambda c: 4 * within(c, z_elems) + over(c, z_elems))


def stacked(value):
    high, low = pieces(value, 2)
    gap = jnp.zeros((256 - 3 * value.shape[0], value.shape[1]), jnp.bfloat16)
    return jnp.concatenate([high, high, low, gap], axis=0)


def to_elements(native, scratch, table, y_elems, parts=3):
    group = 4 * BLOCK
    for c in range(3):
        for y in range(4 * y_elems + 1):
            rows = native(c, y)
            if y < 4 * y_elems:
                scratch[y // 4, pl.ds(ROWS[y % 4][c], 4, stride=BLOCK), :] = rows
            if y % 4 == 0 and y > 0:
                scratch[y // 4 - 1, pl.ds(ROWS[4][c], 4, stride=BLOCK), :] = rows
    high, middle, *low = pieces(
        jnp.concatenate([scratch[i] for i in range(y_elems)], axis=0), parts
    )
    result = dot(
        jnp.concatenate([high, middle], axis=1), jnp.concatenate([table, table], axis=0)
    )
    for piece in low:
        result = result + dot(piece, table)
    lanes = result.shape[1] // 5
    across = lax.broadcasted_iota(jnp.int32, (1, result.shape[1]), 1)
    across = over(within(across, lanes), lanes // y_elems)
    total = result[:group]
    for yel in range(1, y_elems):
        total = jnp.where(across == yel, result[yel * group : (yel + 1) * group], total)
    blocks = []
    for x in range(4):
        for zl in range(5):
            blocks.append(total[x * BLOCK : (x + 1) * BLOCK, zl * lanes : (zl + 1) * lanes])
    return jnp.concatenate(blocks, axis=0)


def from_elements(field, scratch, back_ref, out_ref, y_elems, stored=None):
    rows = []
    for x in range(4):
        rows.append(
            jnp.concatenate(
                [field[x * PLANE + zl * BLOCK : x * PLANE + (zl + 1) * BLOCK] for zl in range(4)],
                axis=1,
            )
        )
    result = exact_dot(jnp.concatenate(rows, axis=0), back_ref[...])
    depth = result.shape[1] // y_elems
    for yel in range(y_elems):
        scratch[yel] = result[:, yel * depth : (yel + 1) * depth]
    for c in range(3):
        for y in range(4 * y_elems + 1):
            yel, yl = (y // 4, y % 4) if y < 4 * y_elems else (y_elems - 1, 4)
            out_ref[c, y] = scratch[yel, pl.ds(ROWS[yl][c], 4, stride=BLOCK), :]
        if stored is not None:
            stored(c)


def shifted(rows, lanes):
    lanes = lanes % rows.shape[1]
    return pltpu.roll(rows, lanes, 1) if lanes else rows


def block_iotas(lanes):
    return (
        lax.broadcasted_iota(jnp.int32, (8, lanes), 0),
        lax.broadcasted_iota(jnp.int32, (8, lanes), 1),
    )


def store_fault(out_ref, x, plane, z_elems):
    lanes = plane.shape[1]
    _, lane = block_iotas(lanes)
    first = last = jnp.zeros((8, lanes), jnp.float32)
    for zl in range(4):
        at = zl * BLOCK
        here = over(lane, z_elems) == zl
        first = jnp.where(here, shifted(plane[at : at + 8], zl * z_elems), first)
        last = jnp.where(here, shifted(plane[at + 8 : at + 16], (zl + 1) * z_elems), last)
    out_ref[pl.ds(x, 3, stride=8), :] = last[4:7]
    out_ref[pl.ds(4 + x, 3, stride=8), :] = first[4:7]
    return last


def sent_plane(plane, last):
    return packed(
        [plane[i * BLOCK : i * BLOCK + 8] for i in range(4)],
        [plane[i * BLOCK + 8 : (i + 1) * BLOCK] for i in range(4)],
        last,
    )


def select_messages(parity, left, right):
    even = parity == 0
    return jnp.where(even, right, left), jnp.where(even, left, right)


def material_rows(lame_ref, shear_ref):
    y_elems, z_elems = lame_ref.shape
    both = jnp.concatenate([lame_ref[...], shear_ref[...]], axis=0)
    spread = ones_where((z_elems, y_elems * z_elems), 1, lambda c: within(c, z_elems))
    tiled = exact_dot(both, spread)
    row = lax.broadcasted_iota(jnp.int32, tiled.shape, 0)
    lane = lax.broadcasted_iota(jnp.int32, tiled.shape, 1)
    kept = jnp.where(within(row, y_elems) == over(lane, z_elems), tiled, 0.0)
    return (
        jnp.sum(kept[:y_elems], axis=0, keepdims=True),
        jnp.sum(kept[y_elems:], axis=0, keepdims=True),
    )


def above_lanes(lanes, z_elems):
    return within(lax.broadcasted_iota(jnp.int32, (BLOCK, lanes), 1), z_elems) != 0


def shared_rows(row):
    return jnp.logical_and(row >= 4, row < 7)


def packed(lows, highs, last):
    row, _ = block_iotas(last.shape[1])
    pairs = [
        jnp.where(row < 4, highs[i], pltpu.roll(highs[i + 1], 4, 0)) for i in (0, 2)
    ]
    return jnp.concatenate(list(lows) + pairs + [last], axis=0)


def unpacked(sent):
    parts = [sent[i : i + 8] for i in range(0, SENT, 8)]
    highs = [parts[4], pltpu.roll(parts[4], 4, 0), parts[5], pltpu.roll(parts[5], 4, 0)]
    return parts[:4], highs, parts[6]


def far_plane(sent, z_elems):
    lanes = sent.shape[1]
    lows, highs, last = unpacked(sent)
    row, lane = block_iotas(lanes)
    inner = lane < lanes - z_elems
    below = within(lane, z_elems) != z_elems - 1
    rows = []
    for zl in range(4):
        node = jnp.where(
            inner, shifted(lows[zl], -z_elems), shifted(last, -(zl + 1) * z_elems)
        )
        rows += [lows[zl], jnp.where(row < 4, highs[zl], node)]
    node = jnp.where(inner, shifted(lows[0], -z_elems - 1), shifted(last, -z_elems - 1))
    rows.append(jnp.where(below, shifted(lows[0], -1), 0.0))
    rows.append(jnp.where(below, jnp.where(row < 4, shifted(highs[0], -1), node), 0.0))
    return jnp.concatenate(rows, axis=0)


def left_blocks(sent, z_elems):
    lanes = sent.shape[1]
    lows, highs, last = unpacked(sent)
    row, lane = block_iotas(lanes)
    outer = jnp.logical_and(lane >= lanes - z_elems, shared_rows(row))
    blocks = []
    for zl in range(4):
        node = jnp.where(outer, shifted(last, -(zl + 1) * z_elems), 0.0)
        blocks.append(jnp.concatenate([lows[zl], jnp.where(row < 4, highs[zl], node)], axis=0))
    return blocks, last[0:1], last[1:2]


def edge_message(result, lame_row, shear_row, z_elems):
    lanes = result.shape[1]
    force = lame_row * result[:PLANE] + shear_row * result[PLANE:]
    lows = [force[i * BLOCK : i * BLOCK + 8] for i in range(5)]
    highs = [force[i * BLOCK + 8 : (i + 1) * BLOCK] for i in range(5)]
    row, lane = block_iotas(lanes)
    take = jnp.logical_and(shared_rows(row), over(lane, z_elems) > 0)
    above = within(lane, z_elems) != 0
    corner = jnp.where(above, shifted(highs[4], z_elems + 1), 0.0)
    ends = [shifted(highs[zl], (zl + 1) * z_elems) for zl in range(4)]
    ends[0] = ends[0] + corner
    new_lows = [lows[zl] + jnp.where(take, shifted(highs[zl], z_elems), 0.0) for zl in range(4)]
    new_lows[0] = (
        new_lows[0]
        + jnp.where(above, shifted(lows[4], 1), 0.0)
        + jnp.where(take, corner, 0.0)
    )
    highs[0] = highs[0] + jnp.where(above, shifted(highs[4], 1), 0.0)
    last = ends[3]
    for zl in range(3):
        last = jnp.where(over(lane, z_elems) == zl, ends[zl], last)
    last = jnp.where(row == 0, lame_row, jnp.where(row == 1, shear_row, last))
    return packed(new_lows, highs, last)


def own_force(own_ref, cur, lame_row, shear_row):
    rows, lanes = cur.shape
    padded = jnp.concatenate([cur, jnp.zeros((OWN_COLS - rows, lanes), jnp.float32)], axis=0)
    result = split_dot(own_ref[0], own_ref[1], padded)
    return lame_row * result[:rows] + shear_row * result[rows:]


def start_copies(pairs, sems):
    copies = [
        pltpu.make_async_copy(source, target, sems.at[i])
        for i, (source, target) in enumerate(pairs)
    ]
    for copy in copies:
        copy.start()
    return copies


def first_kernel(
    now_hbm,
    flags_hbm,
    weak_hbm,
    lame_hbm,
    shear_hbm,
    *refs,
):
    later_hbm, refs = refs[:LATER], refs[LATER:]
    cur_ref, *even_refs, odd_ref, fault_out_ref, material_ref = refs[:5]
    later_refs, refs = refs[5 : 5 + LATER], refs[5 + LATER :]
    scratch, now_ref, flags_ref, weak_ref, lame_ref, shear_ref, sems = refs
    copies = start_copies(
        [
            (now_hbm, now_ref),
            (later_hbm[0], later_refs[0]),
            (lame_hbm, lame_ref),
            (shear_hbm, shear_ref),
            (flags_hbm, flags_ref),
            (weak_hbm, weak_ref),
        ]
        + list(zip(later_hbm[1:], later_refs[1:])),
        sems,
    )
    edge_ref = later_refs[0]
    y_elems, z_elems = lame_ref.shape
    lanes = y_elems * z_elems
    parity = lax.axis_index("dom") % 2
    gather = gather_table(lanes, z_elems)
    fault = fault_table(lanes, z_elems)
    scratch[...] = jnp.zeros_like(scratch)
    for copy in copies[:6]:
        copy.wait()
    cur = to_elements(lambda c, y: now_ref[c, y], scratch, gather, y_elems)
    cur_ref[...] = cur
    lame_row, shear_row = material_rows(lame_ref, shear_ref)
    material_ref[...] = jnp.concatenate(
        [lame_row, shear_row, jnp.zeros((6, lanes), jnp.float32)], axis=0
    )
    planes = [cur[x * PLANE : (x + 1) * PLANE] for x in range(4)]
    edge = dot(edge_ref[...], jnp.concatenate([stacked(p) for p in planes], axis=0))
    right = edge_message(edge, lame_row, shear_row, z_elems)
    lasts = [store_fault(fault_out_ref, x, planes[x], z_elems) for x in range(4)]
    message, odd_ref[...] = select_messages(parity, sent_plane(planes[0], lasts[0]), right)
    even_refs[0][...] = message
    weak = weak_ref[...]
    tangent = []
    for i in range(flags_ref.shape[0]):
        flag = flags_ref[i]
        tangent.append(
            jnp.where(flag == 0, lock_stiffness, jnp.where(flag == 1, -weak, 0.0))
        )
    fault_out_ref[FAULT:] = exact_dot(jnp.concatenate(tangent, axis=0), fault)
    for copy in copies[6:]:
        copy.wait()


def prepare_kernel(cur_ref, material_ref, own_ref, touch_ref, base_ref, edge_part_ref):
    cur = cur_ref[...]
    base_ref[...] = own_force(own_ref, cur, material_ref[0:1], material_ref[1:2])
    edge_part_ref[...] = dot(touch_ref[...], stacked(cur[:PLANE]))


def setup_kernel(next_ref, density_ref, mass_ref, fol_ref, minv_ref, scratch, *, y_elems, z_elems):
    gather = gather_table(y_elems * z_elems, z_elems)
    scratch[...] = jnp.zeros_like(scratch)
    fol_ref[...] = to_elements(lambda c, y: next_ref[c, y], scratch.at[0], gather, y_elems)
    density = to_elements(lambda c, y: density_ref[y], scratch.at[1], gather, y_elems, 2)
    table = mass_ref[...]
    first = lax.axis_index("dom") == 0
    plane = lax.broadcasted_iota(jnp.int32, table.shape, 0) < PLANE
    table = jnp.where(jnp.logical_and(first, plane), 2.0 * table, table)
    minv_ref[...] = jnp.where(table > 0.0, table / jnp.where(table > 0.0, density, 1.0), 0.0)


def step_kernel(*refs, step, last, extra, last_place, pair, y_elems, z_elems):
    cur_ref, fol_ref, minv_ref, base_ref, touch_ref, material_ref, even_ref, odd_ref, up_ref = refs[:9]
    refs = list(refs[9:])
    down_ref = None if pair else refs.pop(0)
    even_in = even_ref[...]
    down_ref = up_ref if pair else down_ref
    first_up_ref, own_ref, first_own_ref, far_ref, edge_ref = refs[:5]
    refs = refs[5 + extra :]
    if last:
        later_ref, back_ref, out_hbm, later_hbm, scratch, out_ref, sems = refs
        copies = start_copies([(later_ref, later_hbm)], sems)
    else:
        new_ref, *even_outs, odd_out, fault_out = refs
    place = lax.axis_index("dom")
    lanes = cur_ref.shape[1]
    even = place % 2 == 0
    far = jnp.where(place == last_place, 0.0, jnp.where(even, even_in, odd_ref[...]))
    left = jnp.where(place == 0, 0.0, jnp.where(even, odd_ref[...], even_in))
    far = far_plane(far, z_elems)
    left, left_lame, left_shear = left_blocks(left, z_elems)
    lame_row, shear_row = material_ref[0:1], material_ref[1:2]
    far = jnp.concatenate([stacked(lame_row * far), stacked(shear_row * far)], axis=0)
    from_left = left_lame * touch_ref[:PLANE] + left_shear * touch_ref[PLANE:]
    row, lane = block_iotas(lanes)
    across = over(lane, z_elems)
    shared = shared_rows(row)
    add_first = jnp.logical_and(shared, across > 0)
    take_last = jnp.logical_and(shared, across < y_elems - 1)
    pull_first = jnp.logical_and(shared, across == 0)
    pull_last = jnp.logical_and(shared, across == y_elems - 1)
    above = above_lanes(lanes, z_elems)
    middle = lax.broadcasted_iota(jnp.int32, (3, lanes), 0) == 1
    gap = jnp.zeros((4, lanes), jnp.float32)
    planes = []
    for x in range(4):
        rows = slice(x * PLANE, (x + 1) * PLANE)
        force = base_ref[rows] + dot(far_ref[rows], far)
        blocks = [force[zl * BLOCK : (zl + 1) * BLOCK] for zl in range(5)]
        if x == 0:
            blocks = [b + from_left[i * BLOCK : (i + 1) * BLOCK] for i, b in enumerate(blocks)]
            blocks[:4] = [b + left[i] for i, b in enumerate(blocks[:4])]
        blocks[0], blocks[4] = (
            blocks[0] + jnp.where(above, pltpu.roll(blocks[4], 1, 1), 0.0),
            blocks[4] + pltpu.roll(blocks[0], lanes - 1, 1),
        )
        lasts, firsts = pl.ds(x, 3, stride=8), pl.ds(4 + x, 3, stride=8)
        k = slice(FAULT + 4 * step + x, FAULT + 4 * step + x + 1)
        below_stiff = jnp.where(middle, lock_stiffness, first_up_ref[k])
        own_stiff = jnp.where(middle, lock_stiffness, first_own_ref[k])
        pulled = jnp.concatenate(
            [gap, below_stiff * (up_ref[lasts, :] - own_ref[firsts, :]), gap[:1]], axis=0
        )
        pulled_last = jnp.concatenate(
            [gap, own_stiff * (down_ref[firsts, :] - own_ref[lasts, :]), gap[:1]], axis=0
        )
        for zl in range(5):
            low, high = blocks[zl][:8], blocks[zl][8:]
            move = zl * z_elems if zl < 4 else 1
            blocks[zl] = jnp.concatenate(
                [
                    low
                    + jnp.where(add_first, shifted(high, z_elems), 0.0)
                    - jnp.where(pull_first, shifted(pulled, -move), 0.0),
                    high
                    + jnp.where(take_last, shifted(low, -z_elems), 0.0)
                    - jnp.where(pull_last, shifted(pulled_last, -move - z_elems), 0.0),
                ],
                axis=0,
            )
        plane = (2.0 * cur_ref[rows] - fol_ref[rows]) - minv_ref[rows] * jnp.concatenate(
            blocks, axis=0
        )
        if last:
            planes.append(plane)
        else:
            new_ref[rows] = plane
            end = store_fault(fault_out, x, plane, z_elems)
            planes.append(stacked(plane))
            if x == 0:
                first = sent_plane(plane, end)
    if last:

        def send(c):
            copy = pltpu.make_async_copy(out_ref.at[c], out_hbm.at[c], sems.at[1 + c])
            copy.start()
            copies.append(copy)

        from_elements(
            jnp.concatenate(planes, axis=0), scratch, back_ref, out_ref, y_elems, send
        )
        for copy in copies:
            copy.wait()
    else:
        edge = dot(edge_ref[...], jnp.concatenate(planes, axis=0))
        right = edge_message(edge, lame_row, shear_row, z_elems)
        message, odd_out[...] = select_messages(place % 2, first, right)
        even_outs[0][...] = message


def mask_kernel(owner_ref, flags_ref, stress_ref, _, mask_ref, weight_ref, *, z_elems):
    shape = (PATCH_ROWS, mask_ref.shape[1])
    first = (lax.axis_index("dom") - REACH) * PATCH_DEV
    number = lax.broadcasted_iota(jnp.int32, shape, 0) + first
    for x in range(4):
        mask = jnp.where(number == owner_ref[:, x : x + 1], 1.0, 0.0)
        mask_ref[PATCH_ROWS * x : PATCH_ROWS * (x + 1)] = mask
    stress = stress_ref[...]
    weights = []
    for i in range(flags_ref.shape[0]):
        flag = flags_ref[i]
        weights.append(
            stress * jnp.where(flag == 1, 0.5, jnp.where(flag == 2, 1.0, 0.0))
        )
    fault = fault_table(mask_ref.shape[1], z_elems)
    weight_ref[...] = exact_dot(jnp.concatenate(weights, axis=0), fault)


def output_kernel(*refs, pair, steps, y_elems, z_elems):
    field_ref, back_ref, weight_ref = refs[:3]
    out_ref, grad_ref, table_ref, scratch = refs[-4:]
    messages = refs[3:-4]
    count = 2 if pair else 3
    grad = 0.0
    for i in range(steps):
        group = messages[count * i : count * (i + 1)]
        slip = -group[0][:4]
        if i < steps - 1:
            slip = slip + group[-1][4:8]
        grad = grad + slip * weight_ref[4 * i : 4 * i + 4]
    grad_ref[...] = grad
    table_ref[...] = fault_table_back(weight_ref.shape[1], z_elems)
    from_elements(field_ref[...], scratch, back_ref, out_ref, y_elems)


def patch_kernel(*refs, pair, steps):
    mask_ref, weight_ref, grad_ref, table_ref = refs[:4]
    first_ref = refs[6] if pair else refs[7]
    home_out, out_a, out_b, out_c, out_d = refs[-5:]
    place = lax.axis_index("dom")
    grad = grad_ref[...] + first_ref[4:8] * weight_ref[4 * (steps - 1) : 4 * steps]
    total = 0.0
    for x in range(4):
        total = total + mask_ref[PATCH_ROWS * x : PATCH_ROWS * (x + 1)] * grad[x : x + 1]
    total = exact_dot(total, table_ref[...])
    rows = [total[2 * i : 2 * i + 2] for i in range(5)]
    home_out[...] = rows[2]
    even = place % 2 == 0
    out_a[...] = jnp.where(even, rows[3], rows[1])
    out_b[...] = jnp.where(even, rows[1], rows[3])
    low = place % 4 < 2
    out_c[...] = jnp.where(low, rows[4], rows[0])
    out_d[...] = jnp.where(low, rows[0], rows[4])


VMEM = pl.BlockSpec(memory_space=pltpu.VMEM)
HBM = pl.BlockSpec(memory_space=pltpu.HBM)
SMEM = pl.BlockSpec(memory_space=pltpu.SMEM)
ANY = pl.BlockSpec(memory_space=pl.ANY)


def kernel_call(body, outs, args, in_smem=(), scratch=(), in_hbm=(), kept=(), unread=(), stay=False, out_spec=VMEM, **static):
    shapes = []
    for out in outs:
        shape, dtype = out if isinstance(out[0], tuple) else (out, jnp.float32)
        shapes.append((pltpu.VMEM if in_hbm or stay else jax.ShapeDtypeStruct)(shape, dtype))
    specs = [VMEM] * len(args)
    for places, spec in ((in_smem, SMEM), (in_hbm, HBM), (unread, ANY)):
        for i in places:
            specs[i] = spec
    copied = [pltpu.VMEM(args[i].shape, args[i].dtype) for i in in_hbm if i not in kept]
    if in_hbm:
        copied.append(pltpu.SemaphoreType.DMA((len(in_hbm),)))
    return pl.pallas_call(
        functools.partial(body, **static) if static else body,
        out_shape=shapes,
        in_specs=specs,
        out_specs=[out_spec] * len(shapes),
        scratch_shapes=list(scratch) + copied,
        compiler_params=pltpu.CompilerParams(
            vmem_limit_bytes=(56 if in_hbm else 24) * 2**20
        ),
    )(*args)


def swapped(block, distance, group):
    size, across = lax.axis_size("dom"), lax.axis_size("depth")
    partner = {}
    for left in range(size - distance):
        if left // distance % 2 == group:
            partner[left], partner[left + distance] = left + distance, left
    route = []
    for i in range(size):
        for j in range(across):
            side = j if i in partner else min(j ^ 1, across - 1)
            route.append((i * across + j, partner.get(i, i) * across + side))
    return lax.ppermute(block, ("dom", "depth"), route)


def from_behind(block, axis, distance):
    size = lax.axis_size(axis)
    return lax.ppermute(block, axis, [((i - distance) % size, i) for i in range(size)])


def on_device(
    adjoint_now,
    adjoint_next,
    lame_first,
    shear_modulus,
    density,
    branch_flags,
    weak_slope,
    normal_stress,
    patch_owner,
):
    x_elems, y_elems, z_elems = lame_first.shape
    lanes = y_elems * z_elems
    assert x_elems == 1 and lanes == adjoint_now.shape[3]
    steps = branch_flags.shape[0]
    pair = lax.axis_size("depth") == 2
    own_table, far_table, edge_table, touch_table = (jnp.asarray(t) for t in stiffness_tables())
    back = jnp.asarray(back_table(y_elems, z_elems))
    mass = jnp.asarray(mass_table(y_elems, z_elems))
    now = jnp.transpose(adjoint_now, (0, 2, 1, 3))
    following = jnp.transpose(adjoint_next, (0, 2, 1, 3))
    rho = jnp.transpose(density, (1, 0, 2))
    flags = branch_flags[:, 0]
    native = pltpu.VMEM((y_elems, 4 * BLOCK, lanes), jnp.float32)
    field = (4 * PLANE, lanes)
    plane = (SENT, lanes)
    parts = [(rows, lanes) for rows in PARTS]

    def exchange(even, odd, fault_rows):
        if pair:
            faults = [from_behind(fault_rows, "depth", 1)]
        else:
            faults = [from_behind(fault_rows, "depth", 1), from_behind(fault_rows, "depth", -1)]
        return [swapped(part, 1, 0) for part in even], swapped(odd, 1, 1), faults

    later_used = (
        edge_table, following, rho, mass, own_table, far_table, touch_table, back, flags,
        normal_stress[0], patch_owner,
    )
    assert len(later_used) == LATER
    first_out = kernel_call(
        first_kernel,
        [field] + parts + [plane, (FAULT + 4 * steps, lanes), (8, lanes)]
        + [(t.shape, t.dtype) for t in later_used],
        (now, flags, weak_slope[0], lame_first[0], shear_modulus[0]) + later_used,
        scratch=[native],
        in_hbm=range(5 + LATER),
        kept=range(5, 5 + LATER),
    )
    cur, *even, odd, fault_rows, material = first_out[:-LATER]
    edge_table, following, rho, mass, own_table, far_table, touch_table, back = first_out[-LATER:-3]
    flags, stress, owner = first_out[-3:]
    even_in, odd_in, fault_in = exchange(even, odd, fault_rows)
    first_fault, first_in = fault_rows, fault_in
    fol, minv = kernel_call(
        setup_kernel,
        [field, field],
        (following, rho, mass),
        scratch=[pltpu.VMEM((2, y_elems, 4 * BLOCK, lanes), jnp.float32)],
        y_elems=y_elems,
        z_elems=z_elems,
    )
    seen = []
    for step in range(steps):
        last = step == steps - 1
        seen += [fault_rows] + fault_in
        base, touch = kernel_call(
            prepare_kernel,
            [field, (2 * PLANE, lanes)],
            [cur, material, own_table, touch_table],
            (),
        )
        args = [cur, fol, minv, base, touch, material] + even_in + [odd_in] + fault_in
        args += [first_in[0], fault_rows, first_fault, far_table, edge_table]
        static = dict(
            step=step, last=last, extra=1 if last or step == 1 else 0, last_place=lax.axis_size("dom") - 1, pair=pair, y_elems=y_elems,
            z_elems=z_elems,
        )
        if step == 1:
            mask, weight = kernel_call(
                mask_kernel,
                [(4 * PATCH_ROWS, lanes), (4 * steps, lanes)],
                [owner, flags, stress, cur],
                unread=(3,),
                z_elems=z_elems,
            )
            args.append(mask)
        if not last:
            new, *even, odd, new_fault = kernel_call(
                step_kernel,
                [field] + parts + [plane, (SENT_FAULT, lanes)],
                args,
                unread=(len(args) - 1,) if step == 1 else (),
                **static,
            )
            fol, cur, fault_rows = cur, new, new_fault
            even_in, odd_in, fault_in = exchange(even, odd, fault_rows)
        else:
            whole = (3, 4 * y_elems + 1, 4, lanes)
            known = seen[: len(seen) - len(fault_in)]
            later, grad, table = kernel_call(
                output_kernel,
                [whole, (4, lanes), ((lanes, lanes), jnp.bfloat16)],
                [cur, back, weight] + known,
                scratch=[native],
                stay=True,
                pair=pair,
                steps=steps,
                y_elems=y_elems,
                z_elems=z_elems,
            )
            sums = kernel_call(
                patch_kernel,
                [(PATCH_DEV, lanes)] * 5,
                [mask, weight, grad, table] + even_in + [odd_in] + fault_in + [touch],
                unread=(4, 5, 6 + len(fault_in)),
                pair=pair,
                steps=steps,
            )
            patch_sums = sums[0]
            for i, distance, group in ((4, 2, 1), (2, 1, 1), (3, 2, 0), (1, 1, 0)):
                patch_sums = patch_sums + swapped(sums[i], distance, group)
            earlier, later = kernel_call(
                step_kernel,
                [whole, whole],
                args + [sums[0], later, back],
                scratch=[
                    native, pltpu.VMEM(whole, jnp.float32), pltpu.SemaphoreType.DMA((4,)),
                ],
                unread=(len(args),),
                out_spec=HBM,
                **static,
            )
    return (
        jnp.transpose(earlier, (0, 2, 1, 3)),
        jnp.transpose(later, (0, 2, 1, 3)),
        patch_sums[None],
    )


def solution(mesh):
    return jax.shard_map(
        on_device,
        mesh=mesh,
        in_specs=(
            P(None, "dom", "depth", None),
            P(None, "dom", "depth", None),
            P("dom", "depth", None),
            P("dom", "depth", None),
            P("dom", "depth", None),
            P(None, "depth", "dom", None),
            P("depth", "dom", None),
            P("depth", "dom", None),
            P("depth", "dom"),
        ),
        out_specs=(
            P(None, "dom", "depth", None),
            P(None, "dom", "depth", None),
            P("depth", "dom", None),
        ),
        check_vma=False,
    )
```

```python
import functools
import math

import jax
import jax.numpy as jnp
import ml_dtypes
import numpy as np
from jax import lax
from jax.experimental import pallas as pl
from jax.experimental.pallas import tpu as pltpu
from jax.sharding import PartitionSpec as P

PATCH_DEV = 2
REACH = 2
PATCH_ROWS = 16
LATER = 11
FAULT = 24
SENT_FAULT = 28
PARTS = (24, 24, 16)

time_step = 0.01
lock_stiffness = 0.5

BLOCK = 16
ROWS = ((0, 1, 2), (3, 4, 5), (11, 12, 13), (6, 7, 14), (8, 9, 10))
PLANE = 5 * BLOCK


def basis_tables():
    points = [-1.0, -math.sqrt(3.0 / 7.0), 0.0, math.sqrt(3.0 / 7.0), 1.0]
    quad_weights = np.array([0.1, 49.0 / 90.0, 32.0 / 45.0, 49.0 / 90.0, 0.1])
    products = []
    for first in range(5):
        value = 1.0
        for other in range(5):
            if other != first:
                value = value * (points[first] - points[other])
        products.append(value)
    derivative = np.zeros((5, 5))
    for row in range(5):
        for column in range(5):
            if row == column:
                total = 0.0
                for other in range(5):
                    if other != row:
                        total = total + 1.0 / (points[row] - points[other])
                derivative[row, column] = total
            else:
                derivative[row, column] = (
                    products[row] / products[column] / (points[row] - points[column])
                )
    return (quad_weights, derivative)


def two_parts(table):
    high = table.astype(ml_dtypes.bfloat16)
    low = (table - high.astype(np.float64)).astype(ml_dtypes.bfloat16)
    return np.stack([high, low])


def element_stiffness():
    weights, derivative = basis_tables()
    eye = np.eye(5)
    slope = 2.0 * derivative
    grads = [
        np.kron(slope, np.kron(eye, eye)),
        np.kron(eye, np.kron(eye, slope)),
        np.kron(eye, np.kron(slope, eye)),
    ]
    quad = np.kron(weights, np.kron(weights, weights)) / 8.0
    first = np.zeros((125, 3, 125, 3))
    second = np.zeros((125, 3, 125, 3))
    lap = sum(g.T @ (quad[:, None] * g) for g in grads)
    for c in range(3):
        second[:, c, :, c] += lap
        for d in range(3):
            first[:, c, :, d] += grads[c].T @ (quad[:, None] * grads[d])
            second[:, c, :, d] += grads[d].T @ (quad[:, None] * grads[c])
    where = [
        node // 5 * BLOCK + ROWS[node % 5][c] for node in range(125) for c in range(3)
    ]
    wide = []
    for small in (first, second):
        big = np.zeros((5 * PLANE, 5 * PLANE))
        big[np.ix_(where, where)] = small.reshape(375, 375)
        wide.append(big)
    return wide


OWN_COLS = 384


def padded_table(table, columns):
    return np.pad(table, ((0, 0), (0, columns - table.shape[1])))


@functools.cache
def stiffness_tables():
    wide = element_stiffness()
    own = 4 * PLANE
    planes = [slice(x * PLANE, (x + 1) * PLANE) for x in range(5)]
    inner = np.concatenate([w[:own, :own] for w in wide])

    def three(table):
        high, low = two_parts(table)
        return padded_table(np.concatenate([high, low, high], axis=1), 256)

    def both(rows, columns):
        return three(np.concatenate([w[rows, columns] for w in wide]))

    return (
        two_parts(padded_table(inner, OWN_COLS)),
        np.concatenate([three(w[:own, planes[4]]) for w in wide], axis=1),
        np.concatenate([both(planes[4], planes[x]) for x in range(4)], axis=1),
        both(planes[4], planes[4]),
    )


@functools.cache
def back_table(y_elems, z_elems):
    lanes = y_elems * z_elems
    depth = 4 * z_elems
    back = np.zeros((4 * lanes, y_elems * depth), ml_dtypes.bfloat16)
    for yel in range(y_elems):
        for k in range(z_elems):
            for zl in range(4):
                back[zl * lanes + yel * z_elems + k, yel * depth + 4 * k + zl] = 1
    return back


@functools.cache
def mass_table(y_elems, z_elems):
    weights, _ = basis_tables()
    table = np.zeros((4, 5, BLOCK, y_elems, z_elems))
    for x in range(4):
        mx = 0.2 if x == 0 else weights[x]
        for zl in range(5):
            for yl in range(5):
                for yel in range(y_elems):
                    my = weights[yl]
                    if (yl == 0 and yel > 0) or (yl == 4 and yel < y_elems - 1):
                        my = 0.2
                    mz = np.full(z_elems, weights[zl])
                    if zl == 0:
                        mz[1:] = 0.2
                    if zl == 4:
                        mz[:] = 0.2
                    value = time_step * time_step * 8.0 / (mx * my * mz)
                    if zl == 4:
                        value[-1] = 0.0
                    table[x, zl, list(ROWS[yl]), yel] = value
    return table.reshape(4 * PLANE, y_elems * z_elems).astype(np.float32)


def pieces(value, count):
    out = []
    for _ in range(count):
        piece = value.astype(jnp.bfloat16)
        out.append(piece)
        value = value - piece.astype(jnp.float32)
    return out


def dot(a, b):
    return jnp.dot(a, b, preferred_element_type=jnp.float32)


def exact_dot(value, table, count=3):
    rows = value.shape[0]
    result = dot(jnp.concatenate(pieces(value, count), axis=0), table)
    total = result[:rows]
    for i in range(1, count):
        total = total + result[i * rows : (i + 1) * rows]
    return total


def split_dot(table_high, table_low, value):
    lanes = value.shape[1]
    high, low = pieces(value, 2)
    wide = dot(table_high, jnp.concatenate([high, low], axis=1))
    return wide[:, :lanes] + (wide[:, lanes:] + dot(table_low, high))


def over(value, size):
    if size & (size - 1) == 0:
        return lax.shift_right_logical(value, np.int32(size.bit_length() - 1))
    return lax.div(value, np.int32(size))


def within(value, size):
    return value & (size - 1) if size & (size - 1) == 0 else lax.rem(value, np.int32(size))


def ones_where(shape, axis, wanted):
    line = (shape[0], 1) if axis == 0 else (1, shape[1])
    target = wanted(lax.broadcasted_iota(jnp.int32, line, axis))
    number = lax.broadcasted_iota(jnp.int32, shape, 1 - axis)
    return jnp.where(number == target, 1.0, 0.0).astype(jnp.bfloat16)


def gather_table(lanes, z_elems):
    return ones_where(
        (lanes, 5 * lanes), 1, lambda c: 4 * within(c, z_elems) + over(c, lanes)
    )


def fault_table(lanes, z_elems):
    return ones_where((lanes, lanes), 1, lambda c: 4 * within(c, z_elems) + over(c, z_elems))


def fault_table_back(lanes, z_elems):
    return ones_where((lanes, lanes), 0, lambda c: 4 * within(c, z_elems) + over(c, z_elems))


def stacked(value):
    high, low = pieces(value, 2)
    gap = jnp.zeros((256 - 3 * value.shape[0], value.shape[1]), jnp.bfloat16)
    return jnp.concatenate([high, high, low, gap], axis=0)


def to_elements(native, scratch, table, y_elems, parts=3):
    group = 4 * BLOCK
    for c in range(3):
        for y in range(4 * y_elems + 1):
            rows = native(c, y)
            if y < 4 * y_elems:
                scratch[y // 4, pl.ds(ROWS[y % 4][c], 4, stride=BLOCK), :] = rows
            if y % 4 == 0 and y > 0:
                scratch[y // 4 - 1, pl.ds(ROWS[4][c], 4, stride=BLOCK), :] = rows
    high, middle, *low = pieces(
        jnp.concatenate([scratch[i] for i in range(y_elems)], axis=0), parts
    )
    result = dot(
        jnp.concatenate([high, middle], axis=1), jnp.concatenate([table, table], axis=0)
    )
    for piece in low:
        result = result + dot(piece, table)
    lanes = result.shape[1] // 5
    across = lax.broadcasted_iota(jnp.int32, (1, result.shape[1]), 1)
    across = over(within(across, lanes), lanes // y_elems)
    total = result[:group]
    for yel in range(1, y_elems):
        total = jnp.where(across == yel, result[yel * group : (yel + 1) * group], total)
    blocks = []
    for x in range(4):
        for zl in range(5):
            blocks.append(total[x * BLOCK : (x + 1) * BLOCK, zl * lanes : (zl + 1) * lanes])
    return jnp.concatenate(blocks, axis=0)


def from_elements(field, scratch, back_ref, out_ref, y_elems, stored=None):
    rows = []
    for x in range(4):
        rows.append(
            jnp.concatenate(
                [field[x * PLANE + zl * BLOCK : x * PLANE + (zl + 1) * BLOCK] for zl in range(4)],
                axis=1,
            )
        )
    result = exact_dot(jnp.concatenate(rows, axis=0), back_ref[...])
    depth = result.shape[1] // y_elems
    for yel in range(y_elems):
        scratch[yel] = result[:, yel * depth : (yel + 1) * depth]
    for c in range(3):
        for y in range(4 * y_elems + 1):
            yel, yl = (y // 4, y % 4) if y < 4 * y_elems else (y_elems - 1, 4)
            out_ref[c, y] = scratch[yel, pl.ds(ROWS[yl][c], 4, stride=BLOCK), :]
        if stored is not None:
            stored(c)


def shifted(rows, lanes):
    lanes = lanes % rows.shape[1]
    return pltpu.roll(rows, lanes, 1) if lanes else rows


def block_iotas(lanes):
    return (
        lax.broadcasted_iota(jnp.int32, (8, lanes), 0),
        lax.broadcasted_iota(jnp.int32, (8, lanes), 1),
    )


def store_fault(out_ref, x, plane, z_elems):
    lanes = plane.shape[1]
    _, lane = block_iotas(lanes)
    first = last = jnp.zeros((8, lanes), jnp.float32)
    for zl in range(4):
        at = zl * BLOCK
        here = over(lane, z_elems) == zl
        first = jnp.where(here, shifted(plane[at : at + 8], zl * z_elems), first)
        last = jnp.where(here, shifted(plane[at + 8 : at + 16], (zl + 1) * z_elems), last)
    out_ref[pl.ds(x, 3, stride=8), :] = last[:3]
    out_ref[pl.ds(4 + x, 3, stride=8), :] = first[:3]


def select_messages(parity, left, right):
    even = parity == 0
    return jnp.where(even, right, left), jnp.where(even, left, right)


def material_rows(lame_ref, shear_ref):
    y_elems, z_elems = lame_ref.shape
    both = jnp.concatenate([lame_ref[...], shear_ref[...]], axis=0)
    spread = ones_where((z_elems, y_elems * z_elems), 1, lambda c: within(c, z_elems))
    tiled = exact_dot(both, spread)
    row = lax.broadcasted_iota(jnp.int32, tiled.shape, 0)
    lane = lax.broadcasted_iota(jnp.int32, tiled.shape, 1)
    kept = jnp.where(within(row, y_elems) == over(lane, z_elems), tiled, 0.0)
    return (
        jnp.sum(kept[:y_elems], axis=0, keepdims=True),
        jnp.sum(kept[y_elems:], axis=0, keepdims=True),
    )


def above_lanes(lanes, z_elems):
    return within(lax.broadcasted_iota(jnp.int32, (BLOCK, lanes), 1), z_elems) != 0


def edge_message(result, lame_row, shear_row, z_elems):
    lanes = result.shape[1]
    force = lame_row * result[:PLANE] + shear_row * result[PLANE:]
    top = force[:BLOCK] + jnp.where(
        above_lanes(lanes, z_elems), pltpu.roll(force[4 * BLOCK :], 1, 1), 0.0
    )
    row = lax.broadcasted_iota(jnp.int32, top.shape, 0)
    top = jnp.where(row == BLOCK - 1, lame_row, top)
    second = jnp.where(row == BLOCK - 1, shear_row, force[BLOCK : 2 * BLOCK])
    return jnp.concatenate([top, second, force[2 * BLOCK : 4 * BLOCK]], axis=0)


def own_force(own_ref, cur, lame_row, shear_row):
    rows, lanes = cur.shape
    padded = jnp.concatenate([cur, jnp.zeros((OWN_COLS - rows, lanes), jnp.float32)], axis=0)
    result = split_dot(own_ref[0], own_ref[1], padded)
    return lame_row * result[:rows] + shear_row * result[rows:]


def start_copies(pairs, sems):
    copies = [
        pltpu.make_async_copy(source, target, sems.at[i])
        for i, (source, target) in enumerate(pairs)
    ]
    for copy in copies:
        copy.start()
    return copies


def first_kernel(
    now_hbm,
    flags_hbm,
    weak_hbm,
    lame_hbm,
    shear_hbm,
    *refs,
):
    later_hbm, refs = refs[:LATER], refs[LATER:]
    cur_ref, *even_refs, odd_ref, fault_out_ref, material_ref = refs[:7]
    later_refs, refs = refs[7 : 7 + LATER], refs[7 + LATER :]
    scratch, now_ref, flags_ref, weak_ref, lame_ref, shear_ref, sems = refs
    copies = start_copies(
        [
            (now_hbm, now_ref),
            (lame_hbm, lame_ref),
            (shear_hbm, shear_ref),
            (flags_hbm, flags_ref),
            (weak_hbm, weak_ref),
            (later_hbm[0], later_refs[0]),
        ]
        + list(zip(later_hbm[1:], later_refs[1:])),
        sems,
    )
    edge_ref = later_refs[0]
    y_elems, z_elems = lame_ref.shape
    lanes = y_elems * z_elems
    parity = lax.axis_index("dom") % 2
    gather = gather_table(lanes, z_elems)
    fault = fault_table(lanes, z_elems)
    scratch[...] = jnp.zeros_like(scratch)
    for copy in copies[1:5]:
        copy.wait()
    lame_row, shear_row = material_rows(lame_ref, shear_ref)
    material_ref[...] = jnp.concatenate(
        [lame_row, shear_row, jnp.zeros((6, lanes), jnp.float32)], axis=0
    )
    weak = weak_ref[...]
    tangent = []
    for i in range(flags_ref.shape[0]):
        flag = flags_ref[i]
        tangent.append(
            jnp.where(flag == 0, lock_stiffness, jnp.where(flag == 1, -weak, 0.0))
        )
    fault_out_ref[FAULT:] = exact_dot(jnp.concatenate(tangent, axis=0), fault)
    copies[0].wait()
    cur = to_elements(lambda c, y: now_ref[c, y], scratch, gather, y_elems)
    cur_ref[...] = cur
    planes = [cur[x * PLANE : (x + 1) * PLANE] for x in range(4)]
    for x in range(4):
        store_fault(fault_out_ref, x, planes[x], z_elems)
    copies[5].wait()
    edge = dot(edge_ref[...], jnp.concatenate([stacked(p) for p in planes], axis=0))
    right = edge_message(edge, lame_row, shear_row, z_elems)
    message, odd_ref[...] = select_messages(parity, cur[: 4 * BLOCK], right)
    for even_ref, at in zip(even_refs, (0, PARTS[0], PARTS[0] + PARTS[1])):
        even_ref[...] = message[at : at + even_ref.shape[0]]
    for copy in copies[6:]:
        copy.wait()


def prepare_kernel(cur_ref, material_ref, own_ref, touch_ref, base_ref, edge_part_ref):
    cur = cur_ref[...]
    base_ref[...] = own_force(own_ref, cur, material_ref[0:1], material_ref[1:2])
    edge_part_ref[...] = dot(touch_ref[...], stacked(cur[:PLANE]))


def setup_kernel(next_ref, density_ref, mass_ref, fol_ref, minv_ref, scratch, *, y_elems, z_elems):
    gather = gather_table(y_elems * z_elems, z_elems)
    scratch[...] = jnp.zeros_like(scratch)
    fol_ref[...] = to_elements(lambda c, y: next_ref[c, y], scratch.at[0], gather, y_elems)
    density = to_elements(lambda c, y: density_ref[y], scratch.at[1], gather, y_elems, 2)
    table = mass_ref[...]
    first = lax.axis_index("dom") == 0
    plane = lax.broadcasted_iota(jnp.int32, table.shape, 0) < PLANE
    table = jnp.where(jnp.logical_and(first, plane), 2.0 * table, table)
    minv_ref[...] = jnp.where(table > 0.0, table / jnp.where(table > 0.0, density, 1.0), 0.0)


def step_kernel(*refs, step, last, extra, last_place, pair, y_elems, z_elems):
    cur_ref, fol_ref, minv_ref, base_ref, touch_ref, material_ref, odd_ref, up_ref = refs[:8]
    refs = list(refs[8:])
    down_ref = None if pair else refs.pop(0)
    even_in = jnp.concatenate([refs.pop(0)[...] for _ in PARTS], axis=0)
    down_ref = up_ref if pair else down_ref
    first_up_ref, own_ref, first_own_ref, far_ref, edge_ref = refs[:5]
    refs = refs[5 + extra :]
    if last:
        later_ref, back_ref, out_hbm, later_hbm, scratch, out_ref, sems = refs
        copies = start_copies([(later_ref, later_hbm)], sems)
    else:
        new_ref, *even_outs, odd_out, fault_out = refs
    place = lax.axis_index("dom")
    lanes = cur_ref.shape[1]
    even = place % 2 == 0
    far = jnp.where(place == last_place, 0.0, jnp.where(even, even_in, odd_ref[...]))
    left = jnp.where(place == 0, 0.0, jnp.where(even, odd_ref[...], even_in))
    lane_wide = lax.broadcasted_iota(jnp.int32, (BLOCK, lanes), 1)
    below = jnp.where(
        within(lane_wide, z_elems) != z_elems - 1, pltpu.roll(far[:BLOCK], lanes - 1, 1), 0.0
    )
    far = jnp.concatenate([far, below], axis=0)
    lame_row, shear_row = material_ref[0:1], material_ref[1:2]
    far = jnp.concatenate([stacked(lame_row * far), stacked(shear_row * far)], axis=0)
    left_lame = left[BLOCK - 1 : BLOCK]
    left_shear = left[2 * BLOCK - 1 : 2 * BLOCK]
    from_left = left_lame * touch_ref[:PLANE] + left_shear * touch_ref[PLANE:]
    row, lane = block_iotas(lanes)
    across = over(lane, z_elems)
    shared = row < 3
    add_first = jnp.logical_and(shared, across > 0)
    take_last = jnp.logical_and(shared, across < y_elems - 1)
    pull_first = jnp.logical_and(shared, across == 0)
    pull_last = jnp.logical_and(shared, across == y_elems - 1)
    above = above_lanes(lanes, z_elems)
    middle = lax.broadcasted_iota(jnp.int32, (3, lanes), 0) == 1
    gap = jnp.zeros((5, lanes), jnp.float32)
    if not last:
        fault_out[FAULT:] = jnp.zeros_like(fault_out[FAULT:])
    planes = []
    for x in range(4):
        rows = slice(x * PLANE, (x + 1) * PLANE)
        force = base_ref[rows] + dot(far_ref[rows], far)
        blocks = [force[zl * BLOCK : (zl + 1) * BLOCK] for zl in range(5)]
        if x == 0:
            blocks = [b + from_left[i * BLOCK : (i + 1) * BLOCK] for i, b in enumerate(blocks)]
            blocks[:4] = [b + left[i * BLOCK : (i + 1) * BLOCK] for i, b in enumerate(blocks[:4])]
        blocks[0], blocks[4] = (
            blocks[0] + jnp.where(above, pltpu.roll(blocks[4], 1, 1), 0.0),
            blocks[4] + pltpu.roll(blocks[0], lanes - 1, 1),
        )
        lasts, firsts = pl.ds(x, 3, stride=8), pl.ds(4 + x, 3, stride=8)
        k = slice(FAULT + 4 * step + x, FAULT + 4 * step + x + 1)
        below_stiff = jnp.where(middle, lock_stiffness, first_up_ref[k])
        own_stiff = jnp.where(middle, lock_stiffness, first_own_ref[k])
        pulled = jnp.concatenate(
            [below_stiff * (up_ref[lasts, :] - own_ref[firsts, :]), gap], axis=0
        )
        pulled_last = jnp.concatenate(
            [own_stiff * (down_ref[firsts, :] - own_ref[lasts, :]), gap], axis=0
        )
        for zl in range(5):
            low, high = blocks[zl][:8], blocks[zl][8:]
            move = zl * z_elems if zl < 4 else 1
            blocks[zl] = jnp.concatenate(
                [
                    low
                    + jnp.where(add_first, shifted(high, z_elems), 0.0)
                    - jnp.where(pull_first, shifted(pulled, -move), 0.0),
                    high
                    + jnp.where(take_last, shifted(low, -z_elems), 0.0)
                    - jnp.where(pull_last, shifted(pulled_last, -move - z_elems), 0.0),
                ],
                axis=0,
            )
        plane = (2.0 * cur_ref[rows] - fol_ref[rows]) - minv_ref[rows] * jnp.concatenate(
            blocks, axis=0
        )
        if last:
            planes.append(plane)
        else:
            new_ref[rows] = plane
            store_fault(fault_out, x, plane, z_elems)
            planes.append(stacked(plane))
            if x == 0:
                first = plane[: 4 * BLOCK]
    if last:

        def send(c):
            copy = pltpu.make_async_copy(out_ref.at[c], out_hbm.at[c], sems.at[1 + c])
            copy.start()
            copies.append(copy)

        from_elements(
            jnp.concatenate(planes, axis=0), scratch, back_ref, out_ref, y_elems, send
        )
        for copy in copies:
            copy.wait()
    else:
        edge = dot(edge_ref[...], jnp.concatenate(planes, axis=0))
        right = edge_message(edge, lame_row, shear_row, z_elems)
        message, odd_out[...] = select_messages(place % 2, first, right)
        for even_out, at in zip(even_outs, (0, PARTS[0], PARTS[0] + PARTS[1])):
            even_out[...] = message[at : at + even_out.shape[0]]


def mask_kernel(owner_ref, flags_ref, stress_ref, _, mask_ref, weight_ref, *, z_elems):
    shape = (PATCH_ROWS, mask_ref.shape[1])
    first = (lax.axis_index("dom") - REACH) * PATCH_DEV
    number = lax.broadcasted_iota(jnp.int32, shape, 0) + first
    for x in range(4):
        mask = jnp.where(number == owner_ref[:, x : x + 1], 1.0, 0.0)
        mask_ref[PATCH_ROWS * x : PATCH_ROWS * (x + 1)] = mask
    stress = stress_ref[...]
    weights = []
    for i in range(flags_ref.shape[0]):
        flag = flags_ref[i]
        weights.append(
            stress * jnp.where(flag == 1, 0.5, jnp.where(flag == 2, 1.0, 0.0))
        )
    fault = fault_table(mask_ref.shape[1], z_elems)
    weight_ref[...] = exact_dot(jnp.concatenate(weights, axis=0), fault)


def output_kernel(*refs, pair, steps, y_elems, z_elems):
    field_ref, back_ref, weight_ref = refs[:3]
    out_ref, grad_ref, table_ref, scratch = refs[-4:]
    messages = refs[3:-4]
    count = 2 if pair else 3
    grad = 0.0
    for i in range(steps):
        group = messages[count * i : count * (i + 1)]
        slip = -group[0][:4]
        if i < steps - 1:
            slip = slip + group[-1][4:8]
        grad = grad + slip * weight_ref[4 * i : 4 * i + 4]
    grad_ref[...] = grad
    table_ref[...] = fault_table_back(weight_ref.shape[1], z_elems)
    from_elements(field_ref[...], scratch, back_ref, out_ref, y_elems)


def patch_kernel(*refs, pair, steps):
    mask_ref, weight_ref, grad_ref, table_ref, _ = refs[:5]
    first_ref = refs[5] if pair else refs[6]
    home_out, out_a, out_b, out_c, out_d = refs[-5:]
    place = lax.axis_index("dom")
    grad = grad_ref[...] + first_ref[4:8] * weight_ref[4 * (steps - 1) : 4 * steps]
    total = 0.0
    for x in range(4):
        total = total + mask_ref[PATCH_ROWS * x : PATCH_ROWS * (x + 1)] * grad[x : x + 1]
    total = exact_dot(total, table_ref[...])
    rows = [total[2 * i : 2 * i + 2] for i in range(5)]
    home_out[...] = rows[2]
    even = place % 2 == 0
    out_a[...] = jnp.where(even, rows[3], rows[1])
    out_b[...] = jnp.where(even, rows[1], rows[3])
    low = place % 4 < 2
    out_c[...] = jnp.where(low, rows[4], rows[0])
    out_d[...] = jnp.where(low, rows[0], rows[4])


def sum_kernel(*refs):
    refs[-1][...] = sum(ref[...] for ref in refs[:-1])


VMEM = pl.BlockSpec(memory_space=pltpu.VMEM)
HBM = pl.BlockSpec(memory_space=pltpu.HBM)
SMEM = pl.BlockSpec(memory_space=pltpu.SMEM)
ANY = pl.BlockSpec(memory_space=pl.ANY)


def kernel_call(body, outs, args, in_smem=(), scratch=(), in_hbm=(), kept=(), unread=(), stay=False, out_spec=VMEM, **static):
    shapes = []
    for out in outs:
        shape, dtype = out if isinstance(out[0], tuple) else (out, jnp.float32)
        shapes.append((pltpu.VMEM if in_hbm or stay else jax.ShapeDtypeStruct)(shape, dtype))
    specs = [VMEM] * len(args)
    for places, spec in ((in_smem, SMEM), (in_hbm, HBM), (unread, ANY)):
        for i in places:
            specs[i] = spec
    copied = [pltpu.VMEM(args[i].shape, args[i].dtype) for i in in_hbm if i not in kept]
    if in_hbm:
        copied.append(pltpu.SemaphoreType.DMA((len(in_hbm),)))
    return pl.pallas_call(
        functools.partial(body, **static) if static else body,
        out_shape=shapes,
        in_specs=specs,
        out_specs=[out_spec] * len(shapes),
        scratch_shapes=list(scratch) + copied,
        compiler_params=pltpu.CompilerParams(
            vmem_limit_bytes=(56 if in_hbm else 24) * 2**20
        ),
    )(*args)


def swapped(block, distance, group):
    size, across = lax.axis_size("dom"), lax.axis_size("depth")
    partner = {}
    for left in range(size - distance):
        if left // distance % 2 == group:
            partner[left], partner[left + distance] = left + distance, left
    route = []
    for i in range(size):
        for j in range(across):
            side = j if i in partner else min(j ^ 1, across - 1)
            route.append((i * across + j, partner.get(i, i) * across + side))
    return lax.ppermute(block, ("dom", "depth"), route)


def from_behind(block, axis, distance):
    size = lax.axis_size(axis)
    return lax.ppermute(block, axis, [((i - distance) % size, i) for i in range(size)])


def on_device(
    adjoint_now,
    adjoint_next,
    lame_first,
    shear_modulus,
    density,
    branch_flags,
    weak_slope,
    normal_stress,
    patch_owner,
):
    x_elems, y_elems, z_elems = lame_first.shape
    lanes = y_elems * z_elems
    assert x_elems == 1 and lanes == adjoint_now.shape[3]
    steps = branch_flags.shape[0]
    pair = lax.axis_size("depth") == 2
    own_table, far_table, edge_table, touch_table = (jnp.asarray(t) for t in stiffness_tables())
    back = jnp.asarray(back_table(y_elems, z_elems))
    mass = jnp.asarray(mass_table(y_elems, z_elems))
    now = jnp.transpose(adjoint_now, (0, 2, 1, 3))
    following = jnp.transpose(adjoint_next, (0, 2, 1, 3))
    rho = jnp.transpose(density, (1, 0, 2))
    flags = branch_flags[:, 0]
    native = pltpu.VMEM((y_elems, 4 * BLOCK, lanes), jnp.float32)
    field = (4 * PLANE, lanes)
    plane = (4 * BLOCK, lanes)
    parts = [(rows, lanes) for rows in PARTS]

    def exchange(even, odd, fault_rows):
        if pair:
            faults = [from_behind(fault_rows, "depth", 1)]
        else:
            faults = [from_behind(fault_rows, "depth", 1), from_behind(fault_rows, "depth", -1)]
        return [swapped(part, 1, 0) for part in even], swapped(odd, 1, 1), faults

    later_used = (
        edge_table, following, rho, mass, own_table, far_table, touch_table, back, flags,
        normal_stress[0], patch_owner,
    )
    assert len(later_used) == LATER
    first_out = kernel_call(
        first_kernel,
        [field] + parts + [plane, (FAULT + 4 * steps, lanes), (8, lanes)]
        + [(t.shape, t.dtype) for t in later_used],
        (now, flags, weak_slope[0], lame_first[0], shear_modulus[0]) + later_used,
        scratch=[native],
        in_hbm=range(5 + LATER),
        kept=range(5, 5 + LATER),
    )
    cur, *even, odd, fault_rows, material = first_out[:-LATER]
    edge_table, following, rho, mass, own_table, far_table, touch_table, back = first_out[-LATER:-3]
    flags, stress, owner = first_out[-3:]
    even_in, odd_in, fault_in = exchange(even, odd, fault_rows)
    first_fault, first_in = fault_rows, fault_in
    fol, minv = kernel_call(
        setup_kernel,
        [field, field],
        (following, rho, mass),
        scratch=[pltpu.VMEM((2, y_elems, 4 * BLOCK, lanes), jnp.float32)],
        y_elems=y_elems,
        z_elems=z_elems,
    )
    seen = []
    for step in range(steps):
        last = step == steps - 1
        seen += [fault_rows] + fault_in
        base, touch = kernel_call(
            prepare_kernel,
            [field, (2 * PLANE, lanes)],
            [cur, material, own_table, touch_table],
            (),
        )
        args = [cur, fol, minv, base, touch, material, odd_in] + fault_in + even_in
        args += [first_in[0], fault_rows, first_fault, far_table, edge_table]
        static = dict(
            step=step, last=last, extra=1 if last or step == 1 else 0, last_place=lax.axis_size("dom") - 1, pair=pair, y_elems=y_elems,
            z_elems=z_elems,
        )
        if step == 1:
            mask, weight = kernel_call(
                mask_kernel,
                [(4 * PATCH_ROWS, lanes), (4 * steps, lanes)],
                [owner, flags, stress, cur],
                unread=(3,),
                z_elems=z_elems,
            )
            args.append(mask)
        if not last:
            new, *even, odd, new_fault = kernel_call(
                step_kernel,
                [field] + parts + [plane, (SENT_FAULT, lanes)],
                args,
                unread=(len(args) - 1,) if step == 1 else (),
                **static,
            )
            fol, cur, fault_rows = cur, new, new_fault
            even_in, odd_in, fault_in = exchange(even, odd, fault_rows)
        else:
            whole = (3, 4 * y_elems + 1, 4, lanes)
            known = seen[: len(seen) - len(fault_in)]
            later, grad, table = kernel_call(
                output_kernel,
                [whole, (4, lanes), ((lanes, lanes), jnp.bfloat16)],
                [cur, back, weight] + known,
                scratch=[native],
                stay=True,
                pair=pair,
                steps=steps,
                y_elems=y_elems,
                z_elems=z_elems,
            )
            sums = kernel_call(
                patch_kernel,
                [(PATCH_DEV, lanes)] * 5,
                [mask, weight, grad, table, odd_in] + fault_in + even_in + [touch],
                unread=(4,) + tuple(range(5 + len(fault_in), 9 + len(fault_in))),
                pair=pair,
                steps=steps,
            )
            shares = [sums[0]]
            for i, distance, group in ((4, 2, 1), (2, 1, 1), (3, 2, 0), (1, 1, 0)):
                shares.append(swapped(sums[i], distance, group))
            patch_sums = kernel_call(sum_kernel, [(PATCH_DEV, lanes)], shares)[0]
            earlier, later = kernel_call(
                step_kernel,
                [whole, whole],
                args + [sums[0], later, back],
                scratch=[
                    native, pltpu.VMEM(whole, jnp.float32), pltpu.SemaphoreType.DMA((4,)),
                ],
                unread=(len(args),),
                out_spec=HBM,
                **static,
            )
    return (
        jnp.transpose(earlier, (0, 2, 1, 3)),
        jnp.transpose(later, (0, 2, 1, 3)),
        patch_sums[None],
    )


def solution(mesh):
    return jax.shard_map(
        on_device,
        mesh=mesh,
        in_specs=(
            P(None, "dom", "depth", None),
            P(None, "dom", "depth", None),
            P("dom", "depth", None),
            P("dom", "depth", None),
            P("dom", "depth", None),
            P(None, "depth", "dom", None),
            P("depth", "dom", None),
            P("depth", "dom", None),
            P("depth", "dom"),
        ),
        out_specs=(
            P(None, "dom", "depth", None),
            P(None, "dom", "depth", None),
            P("depth", "dom", None),
        ),
        check_vma=False,
    )
```

```python
import functools
import math

import jax
import jax.numpy as jnp
import ml_dtypes
import numpy as np
from jax import lax
from jax.experimental import pallas as pl
from jax.experimental.pallas import tpu as pltpu
from jax.sharding import PartitionSpec as P

PATCH_DEV = 2
REACH = 2
PATCH_ROWS = 16
LATER = 11
FAULT = 24
SENT_FAULT = 28
PARTS = (24, 24, 16)

time_step = 0.01
lock_stiffness = 0.5

BLOCK = 16
ROWS = ((0, 1, 2), (3, 4, 5), (11, 12, 13), (6, 7, 14), (8, 9, 10))
PLANE = 5 * BLOCK


def basis_tables():
    points = [-1.0, -math.sqrt(3.0 / 7.0), 0.0, math.sqrt(3.0 / 7.0), 1.0]
    quad_weights = np.array([0.1, 49.0 / 90.0, 32.0 / 45.0, 49.0 / 90.0, 0.1])
    products = []
    for first in range(5):
        value = 1.0
        for other in range(5):
            if other != first:
                value = value * (points[first] - points[other])
        products.append(value)
    derivative = np.zeros((5, 5))
    for row in range(5):
        for column in range(5):
            if row == column:
                total = 0.0
                for other in range(5):
                    if other != row:
                        total = total + 1.0 / (points[row] - points[other])
                derivative[row, column] = total
            else:
                derivative[row, column] = (
                    products[row] / products[column] / (points[row] - points[column])
                )
    return (quad_weights, derivative)


def two_parts(table):
    high = table.astype(ml_dtypes.bfloat16)
    low = (table - high.astype(np.float64)).astype(ml_dtypes.bfloat16)
    return np.stack([high, low])


def element_stiffness():
    weights, derivative = basis_tables()
    eye = np.eye(5)
    slope = 2.0 * derivative
    grads = [
        np.kron(slope, np.kron(eye, eye)),
        np.kron(eye, np.kron(eye, slope)),
        np.kron(eye, np.kron(slope, eye)),
    ]
    quad = np.kron(weights, np.kron(weights, weights)) / 8.0
    first = np.zeros((125, 3, 125, 3))
    second = np.zeros((125, 3, 125, 3))
    lap = sum(g.T @ (quad[:, None] * g) for g in grads)
    for c in range(3):
        second[:, c, :, c] += lap
        for d in range(3):
            first[:, c, :, d] += grads[c].T @ (quad[:, None] * grads[d])
            second[:, c, :, d] += grads[d].T @ (quad[:, None] * grads[c])
    where = [
        node // 5 * BLOCK + ROWS[node % 5][c] for node in range(125) for c in range(3)
    ]
    wide = []
    for small in (first, second):
        big = np.zeros((5 * PLANE, 5 * PLANE))
        big[np.ix_(where, where)] = small.reshape(375, 375)
        wide.append(big)
    return wide


OWN_COLS = 384


def padded_table(table, columns):
    return np.pad(table, ((0, 0), (0, columns - table.shape[1])))


@functools.cache
def stiffness_tables():
    wide = element_stiffness()
    own = 4 * PLANE
    planes = [slice(x * PLANE, (x + 1) * PLANE) for x in range(5)]
    inner = np.concatenate([w[:own, :own] for w in wide])

    def three(table):
        high, low = two_parts(table)
        return padded_table(np.concatenate([high, low, high], axis=1), 256)

    def both(rows, columns):
        return three(np.concatenate([w[rows, columns] for w in wide]))

    return (
        two_parts(padded_table(inner, OWN_COLS)),
        np.concatenate([three(w[:own, planes[4]]) for w in wide], axis=1),
        np.concatenate([both(planes[4], planes[x]) for x in range(4)], axis=1),
        both(planes[4], planes[4]),
    )


@functools.cache
def back_table(y_elems, z_elems):
    lanes = y_elems * z_elems
    depth = 4 * z_elems
    back = np.zeros((4 * lanes, y_elems * depth), ml_dtypes.bfloat16)
    for yel in range(y_elems):
        for k in range(z_elems):
            for zl in range(4):
                back[zl * lanes + yel * z_elems + k, yel * depth + 4 * k + zl] = 1
    return back


@functools.cache
def mass_table(y_elems, z_elems):
    weights, _ = basis_tables()
    table = np.zeros((4, 5, BLOCK, y_elems, z_elems))
    for x in range(4):
        mx = 0.2 if x == 0 else weights[x]
        for zl in range(5):
            for yl in range(5):
                for yel in range(y_elems):
                    my = weights[yl]
                    if (yl == 0 and yel > 0) or (yl == 4 and yel < y_elems - 1):
                        my = 0.2
                    mz = np.full(z_elems, weights[zl])
                    if zl == 0:
                        mz[1:] = 0.2
                    if zl == 4:
                        mz[:] = 0.2
                    value = time_step * time_step * 8.0 / (mx * my * mz)
                    if zl == 4:
                        value[-1] = 0.0
                    table[x, zl, list(ROWS[yl]), yel] = value
    return table.reshape(4 * PLANE, y_elems * z_elems).astype(np.float32)


def pieces(value, count):
    out = []
    for _ in range(count):
        piece = value.astype(jnp.bfloat16)
        out.append(piece)
        value = value - piece.astype(jnp.float32)
    return out


def dot(a, b):
    return jnp.dot(a, b, preferred_element_type=jnp.float32)


def exact_dot(value, table, count=3):
    rows = value.shape[0]
    result = dot(jnp.concatenate(pieces(value, count), axis=0), table)
    total = result[:rows]
    for i in range(1, count):
        total = total + result[i * rows : (i + 1) * rows]
    return total


def split_dot(table_high, table_low, value):
    lanes = value.shape[1]
    high, low = pieces(value, 2)
    wide = dot(table_high, jnp.concatenate([high, low], axis=1))
    return wide[:, :lanes] + (wide[:, lanes:] + dot(table_low, high))


def over(value, size):
    if size & (size - 1) == 0:
        return lax.shift_right_logical(value, np.int32(size.bit_length() - 1))
    return lax.div(value, np.int32(size))


def within(value, size):
    return value & (size - 1) if size & (size - 1) == 0 else lax.rem(value, np.int32(size))


def ones_where(shape, axis, wanted):
    line = (shape[0], 1) if axis == 0 else (1, shape[1])
    target = wanted(lax.broadcasted_iota(jnp.int32, line, axis))
    number = lax.broadcasted_iota(jnp.int32, shape, 1 - axis)
    return jnp.where(number == target, 1.0, 0.0).astype(jnp.bfloat16)


def gather_table(lanes, z_elems):
    return ones_where(
        (lanes, 5 * lanes), 1, lambda c: 4 * within(c, z_elems) + over(c, lanes)
    )


def fault_table(lanes, z_elems):
    return ones_where((lanes, lanes), 1, lambda c: 4 * within(c, z_elems) + over(c, z_elems))


def fault_table_back(lanes, z_elems):
    return ones_where((lanes, lanes), 0, lambda c: 4 * within(c, z_elems) + over(c, z_elems))


def stacked(value):
    high, low = pieces(value, 2)
    gap = jnp.zeros((256 - 3 * value.shape[0], value.shape[1]), jnp.bfloat16)
    return jnp.concatenate([high, high, low, gap], axis=0)


def to_elements(native, scratch, table, y_elems, parts=3):
    group = 4 * BLOCK
    for c in range(3):
        for y in range(4 * y_elems + 1):
            rows = native(c, y)
            if y < 4 * y_elems:
                scratch[y // 4, pl.ds(ROWS[y % 4][c], 4, stride=BLOCK), :] = rows
            if y % 4 == 0 and y > 0:
                scratch[y // 4 - 1, pl.ds(ROWS[4][c], 4, stride=BLOCK), :] = rows
    high, middle, *low = pieces(
        jnp.concatenate([scratch[i] for i in range(y_elems)], axis=0), parts
    )
    result = dot(
        jnp.concatenate([high, middle], axis=1), jnp.concatenate([table, table], axis=0)
    )
    for piece in low:
        result = result + dot(piece, table)
    lanes = result.shape[1] // 5
    across = lax.broadcasted_iota(jnp.int32, (1, result.shape[1]), 1)
    across = over(within(across, lanes), lanes // y_elems)
    total = result[:group]
    for yel in range(1, y_elems):
        total = jnp.where(across == yel, result[yel * group : (yel + 1) * group], total)
    blocks = []
    for x in range(4):
        for zl in range(5):
            blocks.append(total[x * BLOCK : (x + 1) * BLOCK, zl * lanes : (zl + 1) * lanes])
    return jnp.concatenate(blocks, axis=0)


def from_elements(field, scratch, back_ref, out_ref, y_elems, stored=None):
    rows = []
    for x in range(4):
        rows.append(
            jnp.concatenate(
                [field[x * PLANE + zl * BLOCK : x * PLANE + (zl + 1) * BLOCK] for zl in range(4)],
                axis=1,
            )
        )
    result = exact_dot(jnp.concatenate(rows, axis=0), back_ref[...])
    depth = result.shape[1] // y_elems
    for yel in range(y_elems):
        scratch[yel] = result[:, yel * depth : (yel + 1) * depth]
    for c in range(3):
        for y in range(4 * y_elems + 1):
            yel, yl = (y // 4, y % 4) if y < 4 * y_elems else (y_elems - 1, 4)
            out_ref[c, y] = scratch[yel, pl.ds(ROWS[yl][c], 4, stride=BLOCK), :]
        if stored is not None:
            stored(c)


def shifted(rows, lanes):
    lanes = lanes % rows.shape[1]
    return pltpu.roll(rows, lanes, 1) if lanes else rows


def block_iotas(lanes):
    return (
        lax.broadcasted_iota(jnp.int32, (8, lanes), 0),
        lax.broadcasted_iota(jnp.int32, (8, lanes), 1),
    )


def store_fault(out_ref, x, plane, z_elems):
    lanes = plane.shape[1]
    _, lane = block_iotas(lanes)
    first = last = jnp.zeros((8, lanes), jnp.float32)
    for zl in range(4):
        at = zl * BLOCK
        here = over(lane, z_elems) == zl
        first = jnp.where(here, shifted(plane[at : at + 8], zl * z_elems), first)
        last = jnp.where(here, shifted(plane[at + 8 : at + 16], (zl + 1) * z_elems), last)
    out_ref[pl.ds(x, 3, stride=8), :] = last[:3]
    out_ref[pl.ds(4 + x, 3, stride=8), :] = first[:3]


def select_messages(parity, left, right):
    even = parity == 0
    return jnp.where(even, right, left), jnp.where(even, left, right)


def material_rows(lame_ref, shear_ref):
    y_elems, z_elems = lame_ref.shape
    both = jnp.concatenate([lame_ref[...], shear_ref[...]], axis=0)
    spread = ones_where((z_elems, y_elems * z_elems), 1, lambda c: within(c, z_elems))
    tiled = exact_dot(both, spread)
    row = lax.broadcasted_iota(jnp.int32, tiled.shape, 0)
    lane = lax.broadcasted_iota(jnp.int32, tiled.shape, 1)
    kept = jnp.where(within(row, y_elems) == over(lane, z_elems), tiled, 0.0)
    return (
        jnp.sum(kept[:y_elems], axis=0, keepdims=True),
        jnp.sum(kept[y_elems:], axis=0, keepdims=True),
    )


def above_lanes(lanes, z_elems):
    return within(lax.broadcasted_iota(jnp.int32, (BLOCK, lanes), 1), z_elems) != 0


def edge_message(result, lame_row, shear_row, z_elems):
    lanes = result.shape[1]
    force = lame_row * result[:PLANE] + shear_row * result[PLANE:]
    top = force[:BLOCK] + jnp.where(
        above_lanes(lanes, z_elems), pltpu.roll(force[4 * BLOCK :], 1, 1), 0.0
    )
    row = lax.broadcasted_iota(jnp.int32, top.shape, 0)
    top = jnp.where(row == BLOCK - 1, lame_row, top)
    second = jnp.where(row == BLOCK - 1, shear_row, force[BLOCK : 2 * BLOCK])
    return jnp.concatenate([top, second, force[2 * BLOCK : 4 * BLOCK]], axis=0)


def own_force(own_ref, cur, lame_row, shear_row):
    rows, lanes = cur.shape
    padded = jnp.concatenate([cur, jnp.zeros((OWN_COLS - rows, lanes), jnp.float32)], axis=0)
    result = split_dot(own_ref[0], own_ref[1], padded)
    return lame_row * result[:rows] + shear_row * result[rows:]


def start_copies(pairs, sems):
    copies = [
        pltpu.make_async_copy(source, target, sems.at[i])
        for i, (source, target) in enumerate(pairs)
    ]
    for copy in copies:
        copy.start()
    return copies


def first_kernel(
    now_hbm,
    flags_hbm,
    weak_hbm,
    lame_hbm,
    shear_hbm,
    *refs,
):
    later_hbm, refs = refs[:LATER], refs[LATER:]
    cur_ref, *even_refs, odd_ref, fault_out_ref, material_ref = refs[:7]
    later_refs, refs = refs[7 : 7 + LATER], refs[7 + LATER :]
    scratch, now_ref, flags_ref, weak_ref, lame_ref, shear_ref, sems = refs
    copies = start_copies(
        [
            (now_hbm, now_ref),
            (lame_hbm, lame_ref),
            (shear_hbm, shear_ref),
            (flags_hbm, flags_ref),
            (weak_hbm, weak_ref),
            (later_hbm[0], later_refs[0]),
        ]
        + list(zip(later_hbm[1:], later_refs[1:])),
        sems,
    )
    edge_ref = later_refs[0]
    y_elems, z_elems = lame_ref.shape
    lanes = y_elems * z_elems
    parity = lax.axis_index("dom") % 2
    gather = gather_table(lanes, z_elems)
    fault = fault_table(lanes, z_elems)
    scratch[...] = jnp.zeros_like(scratch)
    for copy in copies[1:5]:
        copy.wait()
    lame_row, shear_row = material_rows(lame_ref, shear_ref)
    material_ref[...] = jnp.concatenate(
        [lame_row, shear_row, jnp.zeros((6, lanes), jnp.float32)], axis=0
    )
    weak = weak_ref[...]
    tangent = []
    for i in range(flags_ref.shape[0]):
        flag = flags_ref[i]
        tangent.append(
            jnp.where(flag == 0, lock_stiffness, jnp.where(flag == 1, -weak, 0.0))
        )
    fault_out_ref[FAULT:] = exact_dot(jnp.concatenate(tangent, axis=0), fault)
    copies[0].wait()
    cur = to_elements(lambda c, y: now_ref[c, y], scratch, gather, y_elems)
    cur_ref[...] = cur
    planes = [cur[x * PLANE : (x + 1) * PLANE] for x in range(4)]
    for x in range(4):
        store_fault(fault_out_ref, x, planes[x], z_elems)
    copies[5].wait()
    edge = dot(edge_ref[...], jnp.concatenate([stacked(p) for p in planes], axis=0))
    right = edge_message(edge, lame_row, shear_row, z_elems)
    message, odd_ref[...] = select_messages(parity, cur[: 4 * BLOCK], right)
    for even_ref, at in zip(even_refs, (0, PARTS[0], PARTS[0] + PARTS[1])):
        even_ref[...] = message[at : at + even_ref.shape[0]]
    for copy in copies[6:]:
        copy.wait()


def prepare_kernel(cur_ref, material_ref, own_ref, touch_ref, base_ref, edge_part_ref):
    cur = cur_ref[...]
    base_ref[...] = own_force(own_ref, cur, material_ref[0:1], material_ref[1:2])
    edge_part_ref[...] = dot(touch_ref[...], stacked(cur[:PLANE]))


def setup_kernel(next_ref, density_ref, mass_ref, fol_ref, minv_ref, scratch, *, y_elems, z_elems):
    gather = gather_table(y_elems * z_elems, z_elems)
    scratch[...] = jnp.zeros_like(scratch)
    fol_ref[...] = to_elements(lambda c, y: next_ref[c, y], scratch.at[0], gather, y_elems)
    density = to_elements(lambda c, y: density_ref[y], scratch.at[1], gather, y_elems, 2)
    table = mass_ref[...]
    first = lax.axis_index("dom") == 0
    plane = lax.broadcasted_iota(jnp.int32, table.shape, 0) < PLANE
    table = jnp.where(jnp.logical_and(first, plane), 2.0 * table, table)
    minv_ref[...] = jnp.where(table > 0.0, table / jnp.where(table > 0.0, density, 1.0), 0.0)


def step_kernel(*refs, step, last, extra, last_place, pair, y_elems, z_elems):
    cur_ref, fol_ref, minv_ref, base_ref, touch_ref, material_ref, odd_ref, up_ref = refs[:8]
    refs = list(refs[8:])
    down_ref = None if pair else refs.pop(0)
    even_in = jnp.concatenate([refs.pop(0)[...] for _ in PARTS], axis=0)
    down_ref = up_ref if pair else down_ref
    first_up_ref, own_ref, first_own_ref, far_ref, edge_ref = refs[:5]
    refs = refs[5 + extra :]
    if last:
        later_ref, back_ref, out_hbm, later_hbm, scratch, out_ref, sems = refs
        copies = start_copies([(later_ref, later_hbm)], sems)
    else:
        new_ref, *even_outs, odd_out, fault_out = refs
    place = lax.axis_index("dom")
    lanes = cur_ref.shape[1]
    even = place % 2 == 0
    far = jnp.where(place == last_place, 0.0, jnp.where(even, even_in, odd_ref[...]))
    left = jnp.where(place == 0, 0.0, jnp.where(even, odd_ref[...], even_in))
    lane_wide = lax.broadcasted_iota(jnp.int32, (BLOCK, lanes), 1)
    below = jnp.where(
        within(lane_wide, z_elems) != z_elems - 1, pltpu.roll(far[:BLOCK], lanes - 1, 1), 0.0
    )
    far = jnp.concatenate([far, below], axis=0)
    lame_row, shear_row = material_ref[0:1], material_ref[1:2]
    far = jnp.concatenate([stacked(lame_row * far), stacked(shear_row * far)], axis=0)
    left_lame = left[BLOCK - 1 : BLOCK]
    left_shear = left[2 * BLOCK - 1 : 2 * BLOCK]
    from_left = left_lame * touch_ref[:PLANE] + left_shear * touch_ref[PLANE:]
    row, lane = block_iotas(lanes)
    across = over(lane, z_elems)
    shared = row < 3
    add_first = jnp.logical_and(shared, across > 0)
    take_last = jnp.logical_and(shared, across < y_elems - 1)
    pull_first = jnp.logical_and(shared, across == 0)
    pull_last = jnp.logical_and(shared, across == y_elems - 1)
    above = above_lanes(lanes, z_elems)
    middle = lax.broadcasted_iota(jnp.int32, (3, lanes), 0) == 1
    gap = jnp.zeros((5, lanes), jnp.float32)
    if not last:
        fault_out[FAULT:] = jnp.zeros_like(fault_out[FAULT:])
    planes = []
    for x in range(4):
        rows = slice(x * PLANE, (x + 1) * PLANE)
        force = base_ref[rows] + dot(far_ref[rows], far)
        blocks = [force[zl * BLOCK : (zl + 1) * BLOCK] for zl in range(5)]
        if x == 0:
            blocks = [b + from_left[i * BLOCK : (i + 1) * BLOCK] for i, b in enumerate(blocks)]
            blocks[:4] = [b + left[i * BLOCK : (i + 1) * BLOCK] for i, b in enumerate(blocks[:4])]
        blocks[0], blocks[4] = (
            blocks[0] + jnp.where(above, pltpu.roll(blocks[4], 1, 1), 0.0),
            blocks[4] + pltpu.roll(blocks[0], lanes - 1, 1),
        )
        lasts, firsts = pl.ds(x, 3, stride=8), pl.ds(4 + x, 3, stride=8)
        k = slice(FAULT + 4 * step + x, FAULT + 4 * step + x + 1)
        below_stiff = jnp.where(middle, lock_stiffness, first_up_ref[k])
        own_stiff = jnp.where(middle, lock_stiffness, first_own_ref[k])
        pulled = jnp.concatenate(
            [below_stiff * (up_ref[lasts, :] - own_ref[firsts, :]), gap], axis=0
        )
        pulled_last = jnp.concatenate(
            [own_stiff * (down_ref[firsts, :] - own_ref[lasts, :]), gap], axis=0
        )
        for zl in range(5):
            low, high = blocks[zl][:8], blocks[zl][8:]
            move = zl * z_elems if zl < 4 else 1
            blocks[zl] = jnp.concatenate(
                [
                    low
                    + jnp.where(add_first, shifted(high, z_elems), 0.0)
                    - jnp.where(pull_first, shifted(pulled, -move), 0.0),
                    high
                    + jnp.where(take_last, shifted(low, -z_elems), 0.0)
                    - jnp.where(pull_last, shifted(pulled_last, -move - z_elems), 0.0),
                ],
                axis=0,
            )
        plane = (2.0 * cur_ref[rows] - fol_ref[rows]) - minv_ref[rows] * jnp.concatenate(
            blocks, axis=0
        )
        if last:
            planes.append(plane)
        else:
            new_ref[rows] = plane
            store_fault(fault_out, x, plane, z_elems)
            planes.append(stacked(plane))
            if x == 0:
                first = plane[: 4 * BLOCK]
    if last:

        def send(c):
            copy = pltpu.make_async_copy(out_ref.at[c], out_hbm.at[c], sems.at[1 + c])
            copy.start()
            copies.append(copy)

        from_elements(
            jnp.concatenate(planes, axis=0), scratch, back_ref, out_ref, y_elems, send
        )
        for copy in copies:
            copy.wait()
    else:
        edge = dot(edge_ref[...], jnp.concatenate(planes, axis=0))
        right = edge_message(edge, lame_row, shear_row, z_elems)
        message, odd_out[...] = select_messages(place % 2, first, right)
        for even_out, at in zip(even_outs, (0, PARTS[0], PARTS[0] + PARTS[1])):
            even_out[...] = message[at : at + even_out.shape[0]]


def mask_kernel(owner_ref, flags_ref, stress_ref, _, mask_ref, weight_ref, *, z_elems):
    shape = (PATCH_ROWS, mask_ref.shape[1])
    first = (lax.axis_index("dom") - REACH) * PATCH_DEV
    number = lax.broadcasted_iota(jnp.int32, shape, 0) + first
    for x in range(4):
        mask = jnp.where(number == owner_ref[:, x : x + 1], 1.0, 0.0)
        mask_ref[PATCH_ROWS * x : PATCH_ROWS * (x + 1)] = mask
    stress = stress_ref[...]
    weights = []
    for i in range(flags_ref.shape[0]):
        flag = flags_ref[i]
        weights.append(
            stress * jnp.where(flag == 1, 0.5, jnp.where(flag == 2, 1.0, 0.0))
        )
    fault = fault_table(mask_ref.shape[1], z_elems)
    weight_ref[...] = exact_dot(jnp.concatenate(weights, axis=0), fault)


def output_kernel(*refs, pair, steps, y_elems, z_elems):
    field_ref, back_ref, weight_ref = refs[:3]
    out_ref, grad_ref, table_ref, scratch = refs[-4:]
    messages = refs[3:-4]
    count = 2 if pair else 3
    grad = 0.0
    for i in range(steps):
        group = messages[count * i : count * (i + 1)]
        slip = -group[0][:4]
        if i < steps - 1:
            slip = slip + group[-1][4:8]
        grad = grad + slip * weight_ref[4 * i : 4 * i + 4]
    grad_ref[...] = grad
    table_ref[...] = fault_table_back(weight_ref.shape[1], z_elems)
    from_elements(field_ref[...], scratch, back_ref, out_ref, y_elems)


def patch_kernel(*refs, pair, steps):
    mask_ref, weight_ref, grad_ref, table_ref, _ = refs[:5]
    first_ref = refs[5] if pair else refs[6]
    home_out, out_a, out_b, out_c, out_d = refs[-5:]
    place = lax.axis_index("dom")
    grad = grad_ref[...] + first_ref[4:8] * weight_ref[4 * (steps - 1) : 4 * steps]
    total = 0.0
    for x in range(4):
        total = total + mask_ref[PATCH_ROWS * x : PATCH_ROWS * (x + 1)] * grad[x : x + 1]
    total = exact_dot(total, table_ref[...])
    rows = [total[2 * i : 2 * i + 2] for i in range(5)]
    home_out[...] = rows[2]
    even = place % 2 == 0
    out_a[...] = jnp.where(even, rows[3], rows[1])
    out_b[...] = jnp.where(even, rows[1], rows[3])
    low = place % 4 < 2
    out_c[...] = jnp.where(low, rows[4], rows[0])
    out_d[...] = jnp.where(low, rows[0], rows[4])


def sum_kernel(*refs):
    refs[-1][...] = sum(ref[...] for ref in refs[:-1])


VMEM = pl.BlockSpec(memory_space=pltpu.VMEM)
HBM = pl.BlockSpec(memory_space=pltpu.HBM)
SMEM = pl.BlockSpec(memory_space=pltpu.SMEM)
ANY = pl.BlockSpec(memory_space=pl.ANY)


def kernel_call(body, outs, args, in_smem=(), scratch=(), in_hbm=(), kept=(), unread=(), stay=False, out_spec=VMEM, **static):
    shapes = []
    for out in outs:
        shape, dtype = out if isinstance(out[0], tuple) else (out, jnp.float32)
        shapes.append((pltpu.VMEM if in_hbm or stay else jax.ShapeDtypeStruct)(shape, dtype))
    specs = [VMEM] * len(args)
    for places, spec in ((in_smem, SMEM), (in_hbm, HBM), (unread, ANY)):
        for i in places:
            specs[i] = spec
    copied = [pltpu.VMEM(args[i].shape, args[i].dtype) for i in in_hbm if i not in kept]
    if in_hbm:
        copied.append(pltpu.SemaphoreType.DMA((len(in_hbm),)))
    return pl.pallas_call(
        functools.partial(body, **static) if static else body,
        out_shape=shapes,
        in_specs=specs,
        out_specs=[out_spec] * len(shapes),
        scratch_shapes=list(scratch) + copied,
        compiler_params=pltpu.CompilerParams(
            vmem_limit_bytes=(56 if in_hbm else 24) * 2**20
        ),
    )(*args)


def swapped(block, distance, group):
    size, across = lax.axis_size("dom"), lax.axis_size("depth")
    partner = {}
    for left in range(size - distance):
        if left // distance % 2 == group:
            partner[left], partner[left + distance] = left + distance, left
    route = []
    for i in range(size):
        for j in range(across):
            other, side = partner.get(i, i), j
            if i not in partner and i ^ 1 < size and i ^ 1 not in partner:
                other = i ^ 1
            elif i not in partner:
                side = min(j ^ 1, across - 1)
            route.append((i * across + j, other * across + side))
    return lax.ppermute(block, ("dom", "depth"), route)


def from_behind(block, axis, distance):
    size = lax.axis_size(axis)
    return lax.ppermute(block, axis, [((i - distance) % size, i) for i in range(size)])


def on_device(
    adjoint_now,
    adjoint_next,
    lame_first,
    shear_modulus,
    density,
    branch_flags,
    weak_slope,
    normal_stress,
    patch_owner,
):
    x_elems, y_elems, z_elems = lame_first.shape
    lanes = y_elems * z_elems
    assert x_elems == 1 and lanes == adjoint_now.shape[3]
    steps = branch_flags.shape[0]
    pair = lax.axis_size("depth") == 2
    own_table, far_table, edge_table, touch_table = (jnp.asarray(t) for t in stiffness_tables())
    back = jnp.asarray(back_table(y_elems, z_elems))
    mass = jnp.asarray(mass_table(y_elems, z_elems))
    now = jnp.transpose(adjoint_now, (0, 2, 1, 3))
    following = jnp.transpose(adjoint_next, (0, 2, 1, 3))
    rho = jnp.transpose(density, (1, 0, 2))
    flags = branch_flags[:, 0]
    native = pltpu.VMEM((y_elems, 4 * BLOCK, lanes), jnp.float32)
    field = (4 * PLANE, lanes)
    plane = (4 * BLOCK, lanes)
    parts = [(rows, lanes) for rows in PARTS]

    def exchange(even, odd, fault_rows):
        if pair:
            faults = [from_behind(fault_rows, "depth", 1)]
        else:
            faults = [from_behind(fault_rows, "depth", 1), from_behind(fault_rows, "depth", -1)]
        return [swapped(part, 1, 0) for part in even], swapped(odd, 1, 1), faults

    later_used = (
        edge_table, following, rho, mass, own_table, far_table, touch_table, back, flags,
        normal_stress[0], patch_owner,
    )
    assert len(later_used) == LATER
    first_out = kernel_call(
        first_kernel,
        [field] + parts + [plane, (FAULT + 4 * steps, lanes), (8, lanes)]
        + [(t.shape, t.dtype) for t in later_used],
        (now, flags, weak_slope[0], lame_first[0], shear_modulus[0]) + later_used,
        scratch=[native],
        in_hbm=range(5 + LATER),
        kept=range(5, 5 + LATER),
    )
    cur, *even, odd, fault_rows, material = first_out[:-LATER]
    edge_table, following, rho, mass, own_table, far_table, touch_table, back = first_out[-LATER:-3]
    flags, stress, owner = first_out[-3:]
    even_in, odd_in, fault_in = exchange(even, odd, fault_rows)
    first_fault, first_in = fault_rows, fault_in
    fol, minv = kernel_call(
        setup_kernel,
        [field, field],
        (following, rho, mass),
        scratch=[pltpu.VMEM((2, y_elems, 4 * BLOCK, lanes), jnp.float32)],
        y_elems=y_elems,
        z_elems=z_elems,
    )
    seen = []
    for step in range(steps):
        last = step == steps - 1
        seen += [fault_rows] + fault_in
        base, touch = kernel_call(
            prepare_kernel,
            [field, (2 * PLANE, lanes)],
            [cur, material, own_table, touch_table],
            (),
        )
        args = [cur, fol, minv, base, touch, material, odd_in] + fault_in + even_in
        args += [first_in[0], fault_rows, first_fault, far_table, edge_table]
        static = dict(
            step=step, last=last, extra=1 if last or step == 1 else 0, last_place=lax.axis_size("dom") - 1, pair=pair, y_elems=y_elems,
            z_elems=z_elems,
        )
        if step == 1:
            mask, weight = kernel_call(
                mask_kernel,
                [(4 * PATCH_ROWS, lanes), (4 * steps, lanes)],
                [owner, flags, stress, cur],
                unread=(3,),
                z_elems=z_elems,
            )
            args.append(mask)
        if not last:
            new, *even, odd, new_fault = kernel_call(
                step_kernel,
                [field] + parts + [plane, (SENT_FAULT, lanes)],
                args,
                unread=(len(args) - 1,) if step == 1 else (),
                **static,
            )
            fol, cur, fault_rows = cur, new, new_fault
            even_in, odd_in, fault_in = exchange(even, odd, fault_rows)
        else:
            whole = (3, 4 * y_elems + 1, 4, lanes)
            known = seen[: len(seen) - len(fault_in)]
            later, grad, table = kernel_call(
                output_kernel,
                [whole, (4, lanes), ((lanes, lanes), jnp.bfloat16)],
                [cur, back, weight] + known,
                scratch=[native],
                stay=True,
                pair=pair,
                steps=steps,
                y_elems=y_elems,
                z_elems=z_elems,
            )
            sums = kernel_call(
                patch_kernel,
                [(PATCH_DEV, lanes)] * 5,
                [mask, weight, grad, table, odd_in] + fault_in + even_in + [touch],
                unread=(4,) + tuple(range(5 + len(fault_in), 9 + len(fault_in))),
                pair=pair,
                steps=steps,
            )
            shares = [sums[0]]
            for i, distance, group in ((3, 2, 0), (2, 1, 1), (4, 2, 1), (1, 1, 0)):
                shares.append(swapped(sums[i], distance, group))
            patch_sums = kernel_call(sum_kernel, [(PATCH_DEV, lanes)], shares)[0]
            earlier, later = kernel_call(
                step_kernel,
                [whole, whole],
                args + [sums[0], later, back],
                scratch=[
                    native, pltpu.VMEM(whole, jnp.float32), pltpu.SemaphoreType.DMA((4,)),
                ],
                unread=(len(args),),
                out_spec=HBM,
                **static,
            )
    return (
        jnp.transpose(earlier, (0, 2, 1, 3)),
        jnp.transpose(later, (0, 2, 1, 3)),
        patch_sums[None],
    )


def solution(mesh):
    return jax.shard_map(
        on_device,
        mesh=mesh,
        in_specs=(
            P(None, "dom", "depth", None),
            P(None, "dom", "depth", None),
            P("dom", "depth", None),
            P("dom", "depth", None),
            P("dom", "depth", None),
            P(None, "depth", "dom", None),
            P("depth", "dom", None),
            P("depth", "dom", None),
            P("depth", "dom"),
        ),
        out_specs=(
            P(None, "dom", "depth", None),
            P(None, "dom", "depth", None),
            P("depth", "dom", None),
        ),
        check_vma=False,
    )
```

```python
import functools
import math

import jax
import jax.numpy as jnp
import ml_dtypes
import numpy as np
from jax import lax
from jax.experimental import pallas as pl
from jax.experimental.pallas import tpu as pltpu
from jax.sharding import PartitionSpec as P

PATCH_DEV = 2
REACH = 2
PATCH_ROWS = 16
LATER = 11
FAULT = 24
SENT_FAULT = 28
SENT = 56
PARTS = (24, 16, 16)

time_step = 0.01
lock_stiffness = 0.5

BLOCK = 16
ROWS = ((4, 5, 6), (0, 1, 2), (8, 9, 10), (3, 7, 11), (12, 13, 14))
PLANE = 5 * BLOCK


def basis_tables():
    points = [-1.0, -math.sqrt(3.0 / 7.0), 0.0, math.sqrt(3.0 / 7.0), 1.0]
    quad_weights = np.array([0.1, 49.0 / 90.0, 32.0 / 45.0, 49.0 / 90.0, 0.1])
    products = []
    for first in range(5):
        value = 1.0
        for other in range(5):
            if other != first:
                value = value * (points[first] - points[other])
        products.append(value)
    derivative = np.zeros((5, 5))
    for row in range(5):
        for column in range(5):
            if row == column:
                total = 0.0
                for other in range(5):
                    if other != row:
                        total = total + 1.0 / (points[row] - points[other])
                derivative[row, column] = total
            else:
                derivative[row, column] = (
                    products[row] / products[column] / (points[row] - points[column])
                )
    return (quad_weights, derivative)


def two_parts(table):
    high = table.astype(ml_dtypes.bfloat16)
    low = (table - high.astype(np.float64)).astype(ml_dtypes.bfloat16)
    return np.stack([high, low])


def element_stiffness():
    weights, derivative = basis_tables()
    eye = np.eye(5)
    slope = 2.0 * derivative
    grads = [
        np.kron(slope, np.kron(eye, eye)),
        np.kron(eye, np.kron(eye, slope)),
        np.kron(eye, np.kron(slope, eye)),
    ]
    quad = np.kron(weights, np.kron(weights, weights)) / 8.0
    first = np.zeros((125, 3, 125, 3))
    second = np.zeros((125, 3, 125, 3))
    lap = sum(g.T @ (quad[:, None] * g) for g in grads)
    for c in range(3):
        second[:, c, :, c] += lap
        for d in range(3):
            first[:, c, :, d] += grads[c].T @ (quad[:, None] * grads[d])
            second[:, c, :, d] += grads[d].T @ (quad[:, None] * grads[c])
    where = [
        node // 5 * BLOCK + ROWS[node % 5][c] for node in range(125) for c in range(3)
    ]
    wide = []
    for small in (first, second):
        big = np.zeros((5 * PLANE, 5 * PLANE))
        big[np.ix_(where, where)] = small.reshape(375, 375)
        wide.append(big)
    return wide


OWN_COLS = 384


def padded_table(table, columns):
    return np.pad(table, ((0, 0), (0, columns - table.shape[1])))


@functools.cache
def stiffness_tables():
    wide = element_stiffness()
    own = 4 * PLANE
    planes = [slice(x * PLANE, (x + 1) * PLANE) for x in range(5)]
    inner = np.concatenate([w[:own, :own] for w in wide])

    def three(table):
        high, low = two_parts(table)
        return padded_table(np.concatenate([high, low, high], axis=1), 256)

    def both(rows, columns):
        return three(np.concatenate([w[rows, columns] for w in wide]))

    return (
        two_parts(padded_table(inner, OWN_COLS)),
        np.concatenate([three(w[:own, planes[4]]) for w in wide], axis=1),
        np.concatenate([both(planes[4], planes[x]) for x in range(4)], axis=1),
        both(planes[4], planes[4]),
    )


@functools.cache
def back_table(y_elems, z_elems):
    lanes = y_elems * z_elems
    depth = 4 * z_elems
    back = np.zeros((4 * lanes, y_elems * depth), ml_dtypes.bfloat16)
    for yel in range(y_elems):
        for k in range(z_elems):
            for zl in range(4):
                back[zl * lanes + yel * z_elems + k, yel * depth + 4 * k + zl] = 1
    return back


@functools.cache
def mass_table(y_elems, z_elems):
    weights, _ = basis_tables()
    table = np.zeros((4, 5, BLOCK, y_elems, z_elems))
    for x in range(4):
        mx = 0.2 if x == 0 else weights[x]
        for zl in range(5):
            for yl in range(5):
                for yel in range(y_elems):
                    my = weights[yl]
                    if (yl == 0 and yel > 0) or (yl == 4 and yel < y_elems - 1):
                        my = 0.2
                    mz = np.full(z_elems, weights[zl])
                    if zl == 0:
                        mz[1:] = 0.2
                    if zl == 4:
                        mz[:] = 0.2
                    value = time_step * time_step * 8.0 / (mx * my * mz)
                    if zl == 4:
                        value[-1] = 0.0
                    table[x, zl, list(ROWS[yl]), yel] = value
    return table.reshape(4 * PLANE, y_elems * z_elems).astype(np.float32)


def pieces(value, count):
    out = []
    for _ in range(count):
        piece = value.astype(jnp.bfloat16)
        out.append(piece)
        value = value - piece.astype(jnp.float32)
    return out


def dot(a, b):
    return jnp.dot(a, b, preferred_element_type=jnp.float32)


def exact_dot(value, table, count=3):
    rows = value.shape[0]
    result = dot(jnp.concatenate(pieces(value, count), axis=0), table)
    total = result[:rows]
    for i in range(1, count):
        total = total + result[i * rows : (i + 1) * rows]
    return total


def split_dot(table_high, table_low, value):
    lanes = value.shape[1]
    high, low = pieces(value, 2)
    wide = dot(table_high, jnp.concatenate([high, low], axis=1))
    return wide[:, :lanes] + (wide[:, lanes:] + dot(table_low, high))


def over(value, size):
    if size & (size - 1) == 0:
        return lax.shift_right_logical(value, np.int32(size.bit_length() - 1))
    return lax.div(value, np.int32(size))


def within(value, size):
    return value & (size - 1) if size & (size - 1) == 0 else lax.rem(value, np.int32(size))


def ones_where(shape, axis, wanted):
    line = (shape[0], 1) if axis == 0 else (1, shape[1])
    target = wanted(lax.broadcasted_iota(jnp.int32, line, axis))
    number = lax.broadcasted_iota(jnp.int32, shape, 1 - axis)
    return jnp.where(number == target, 1.0, 0.0).astype(jnp.bfloat16)


def gather_table(lanes, z_elems):
    return ones_where(
        (lanes, 5 * lanes), 1, lambda c: 4 * within(c, z_elems) + over(c, lanes)
    )


def fault_table(lanes, z_elems):
    return ones_where((lanes, lanes), 1, lambda c: 4 * within(c, z_elems) + over(c, z_elems))


def fault_table_back(lanes, z_elems):
    return ones_where((lanes, lanes), 0, lambda c: 4 * within(c, z_elems) + over(c, z_elems))


def stacked(value):
    high, low = pieces(value, 2)
    gap = jnp.zeros((256 - 3 * value.shape[0], value.shape[1]), jnp.bfloat16)
    return jnp.concatenate([high, high, low, gap], axis=0)


def to_elements(native, scratch, table, y_elems, parts=3):
    group = 4 * BLOCK
    for c in range(3):
        for y in range(4 * y_elems + 1):
            rows = native(c, y)
            if y < 4 * y_elems:
                scratch[y // 4, pl.ds(ROWS[y % 4][c], 4, stride=BLOCK), :] = rows
            if y % 4 == 0 and y > 0:
                scratch[y // 4 - 1, pl.ds(ROWS[4][c], 4, stride=BLOCK), :] = rows
    high, middle, *low = pieces(
        jnp.concatenate([scratch[i] for i in range(y_elems)], axis=0), parts
    )
    result = dot(
        jnp.concatenate([high, middle], axis=1), jnp.concatenate([table, table], axis=0)
    )
    for piece in low:
        result = result + dot(piece, table)
    lanes = result.shape[1] // 5
    across = lax.broadcasted_iota(jnp.int32, (1, result.shape[1]), 1)
    across = over(within(across, lanes), lanes // y_elems)
    total = result[:group]
    for yel in range(1, y_elems):
        total = jnp.where(across == yel, result[yel * group : (yel + 1) * group], total)
    blocks = []
    for x in range(4):
        for zl in range(5):
            blocks.append(total[x * BLOCK : (x + 1) * BLOCK, zl * lanes : (zl + 1) * lanes])
    return jnp.concatenate(blocks, axis=0)


def from_elements(field, scratch, back_ref, out_ref, y_elems, stored=None):
    rows = []
    for x in range(4):
        rows.append(
            jnp.concatenate(
                [field[x * PLANE + zl * BLOCK : x * PLANE + (zl + 1) * BLOCK] for zl in range(4)],
                axis=1,
            )
        )
    result = exact_dot(jnp.concatenate(rows, axis=0), back_ref[...])
    depth = result.shape[1] // y_elems
    for yel in range(y_elems):
        scratch[yel] = result[:, yel * depth : (yel + 1) * depth]
    for c in range(3):
        for y in range(4 * y_elems + 1):
            yel, yl = (y // 4, y % 4) if y < 4 * y_elems else (y_elems - 1, 4)
            out_ref[c, y] = scratch[yel, pl.ds(ROWS[yl][c], 4, stride=BLOCK), :]
        if stored is not None:
            stored(c)


def shifted(rows, lanes):
    lanes = lanes % rows.shape[1]
    return pltpu.roll(rows, lanes, 1) if lanes else rows


def block_iotas(lanes):
    return (
        lax.broadcasted_iota(jnp.int32, (8, lanes), 0),
        lax.broadcasted_iota(jnp.int32, (8, lanes), 1),
    )


def store_fault(out_ref, x, plane, z_elems):
    lanes = plane.shape[1]
    _, lane = block_iotas(lanes)
    first = last = jnp.zeros((8, lanes), jnp.float32)
    for zl in range(4):
        at = zl * BLOCK
        here = over(lane, z_elems) == zl
        first = jnp.where(here, shifted(plane[at : at + 8], zl * z_elems), first)
        last = jnp.where(here, shifted(plane[at + 8 : at + 16], (zl + 1) * z_elems), last)
    out_ref[pl.ds(x, 3, stride=8), :] = last[4:7]
    out_ref[pl.ds(4 + x, 3, stride=8), :] = first[4:7]
    return last


def sent_plane(plane, last):
    return packed(
        [plane[i * BLOCK : i * BLOCK + 8] for i in range(4)],
        [plane[i * BLOCK + 8 : (i + 1) * BLOCK] for i in range(4)],
        last,
    )


def select_messages(parity, left, right):
    even = parity == 0
    return jnp.where(even, right, left), jnp.where(even, left, right)


def material_rows(lame_ref, shear_ref):
    y_elems, z_elems = lame_ref.shape
    both = jnp.concatenate([lame_ref[...], shear_ref[...]], axis=0)
    spread = ones_where((z_elems, y_elems * z_elems), 1, lambda c: within(c, z_elems))
    tiled = exact_dot(both, spread)
    row = lax.broadcasted_iota(jnp.int32, tiled.shape, 0)
    lane = lax.broadcasted_iota(jnp.int32, tiled.shape, 1)
    kept = jnp.where(within(row, y_elems) == over(lane, z_elems), tiled, 0.0)
    return (
        jnp.sum(kept[:y_elems], axis=0, keepdims=True),
        jnp.sum(kept[y_elems:], axis=0, keepdims=True),
    )


def above_lanes(lanes, z_elems):
    return within(lax.broadcasted_iota(jnp.int32, (BLOCK, lanes), 1), z_elems) != 0


def shared_rows(row):
    return jnp.logical_and(row >= 4, row < 7)


def packed(lows, highs, last):
    row, _ = block_iotas(last.shape[1])
    pairs = [
        jnp.where(row < 4, highs[i], pltpu.roll(highs[i + 1], 4, 0)) for i in (0, 2)
    ]
    return jnp.concatenate(list(lows) + pairs + [last], axis=0)


def unpacked(sent):
    parts = [sent[i : i + 8] for i in range(0, SENT, 8)]
    highs = [parts[4], pltpu.roll(parts[4], 4, 0), parts[5], pltpu.roll(parts[5], 4, 0)]
    return parts[:4], highs, parts[6]


def far_plane(sent, z_elems):
    lanes = sent.shape[1]
    lows, highs, last = unpacked(sent)
    row, lane = block_iotas(lanes)
    inner = lane < lanes - z_elems
    below = within(lane, z_elems) != z_elems - 1
    rows = []
    for zl in range(4):
        node = jnp.where(
            inner, shifted(lows[zl], -z_elems), shifted(last, -(zl + 1) * z_elems)
        )
        rows += [lows[zl], jnp.where(row < 4, highs[zl], node)]
    node = jnp.where(inner, shifted(lows[0], -z_elems - 1), shifted(last, -z_elems - 1))
    rows.append(jnp.where(below, shifted(lows[0], -1), 0.0))
    rows.append(jnp.where(below, jnp.where(row < 4, shifted(highs[0], -1), node), 0.0))
    return jnp.concatenate(rows, axis=0)


def left_blocks(sent, z_elems):
    lanes = sent.shape[1]
    lows, highs, last = unpacked(sent)
    row, lane = block_iotas(lanes)
    outer = jnp.logical_and(lane >= lanes - z_elems, shared_rows(row))
    blocks = []
    for zl in range(4):
        node = jnp.where(outer, shifted(last, -(zl + 1) * z_elems), 0.0)
        blocks.append(jnp.concatenate([lows[zl], jnp.where(row < 4, highs[zl], node)], axis=0))
    return blocks, last[0:1], last[1:2]


def edge_message(result, lame_row, shear_row, z_elems):
    lanes = result.shape[1]
    force = lame_row * result[:PLANE] + shear_row * result[PLANE:]
    lows = [force[i * BLOCK : i * BLOCK + 8] for i in range(5)]
    highs = [force[i * BLOCK + 8 : (i + 1) * BLOCK] for i in range(5)]
    row, lane = block_iotas(lanes)
    take = jnp.logical_and(shared_rows(row), over(lane, z_elems) > 0)
    above = within(lane, z_elems) != 0
    corner = jnp.where(above, shifted(highs[4], z_elems + 1), 0.0)
    ends = [shifted(highs[zl], (zl + 1) * z_elems) for zl in range(4)]
    ends[0] = ends[0] + corner
    new_lows = [lows[zl] + jnp.where(take, shifted(highs[zl], z_elems), 0.0) for zl in range(4)]
    new_lows[0] = (
        new_lows[0]
        + jnp.where(above, shifted(lows[4], 1), 0.0)
        + jnp.where(take, corner, 0.0)
    )
    highs[0] = highs[0] + jnp.where(above, shifted(highs[4], 1), 0.0)
    last = ends[3]
    for zl in range(3):
        last = jnp.where(over(lane, z_elems) == zl, ends[zl], last)
    last = jnp.where(row == 0, lame_row, jnp.where(row == 1, shear_row, last))
    return packed(new_lows, highs, last)


def own_force(own_ref, cur, lame_row, shear_row):
    rows, lanes = cur.shape
    padded = jnp.concatenate([cur, jnp.zeros((OWN_COLS - rows, lanes), jnp.float32)], axis=0)
    result = split_dot(own_ref[0], own_ref[1], padded)
    return lame_row * result[:rows] + shear_row * result[rows:]


def start_copies(pairs, sems):
    copies = [
        pltpu.make_async_copy(source, target, sems.at[i])
        for i, (source, target) in enumerate(pairs)
    ]
    for copy in copies:
        copy.start()
    return copies


def first_kernel(
    now_hbm,
    flags_hbm,
    weak_hbm,
    lame_hbm,
    shear_hbm,
    *refs,
):
    later_hbm, refs = refs[:LATER], refs[LATER:]
    cur_ref, *even_refs, odd_ref, fault_out_ref, material_ref = refs[:7]
    later_refs, refs = refs[7 : 7 + LATER], refs[7 + LATER :]
    scratch, now_ref, flags_ref, weak_ref, lame_ref, shear_ref, sems = refs
    copies = start_copies(
        [
            (now_hbm, now_ref),
            (lame_hbm, lame_ref),
            (shear_hbm, shear_ref),
            (flags_hbm, flags_ref),
            (weak_hbm, weak_ref),
            (later_hbm[0], later_refs[0]),
        ]
        + list(zip(later_hbm[1:], later_refs[1:])),
        sems,
    )
    edge_ref = later_refs[0]
    y_elems, z_elems = lame_ref.shape
    lanes = y_elems * z_elems
    parity = lax.axis_index("dom") % 2
    gather = gather_table(lanes, z_elems)
    fault = fault_table(lanes, z_elems)
    scratch[...] = jnp.zeros_like(scratch)
    for copy in copies[1:5]:
        copy.wait()
    lame_row, shear_row = material_rows(lame_ref, shear_ref)
    material_ref[...] = jnp.concatenate(
        [lame_row, shear_row, jnp.zeros((6, lanes), jnp.float32)], axis=0
    )
    weak = weak_ref[...]
    tangent = []
    for i in range(flags_ref.shape[0]):
        flag = flags_ref[i]
        tangent.append(
            jnp.where(flag == 0, lock_stiffness, jnp.where(flag == 1, -weak, 0.0))
        )
    fault_out_ref[FAULT:] = exact_dot(jnp.concatenate(tangent, axis=0), fault)
    copies[0].wait()
    cur = to_elements(lambda c, y: now_ref[c, y], scratch, gather, y_elems)
    cur_ref[...] = cur
    planes = [cur[x * PLANE : (x + 1) * PLANE] for x in range(4)]
    lasts = [store_fault(fault_out_ref, x, planes[x], z_elems) for x in range(4)]
    copies[5].wait()
    edge = dot(edge_ref[...], jnp.concatenate([stacked(p) for p in planes], axis=0))
    right = edge_message(edge, lame_row, shear_row, z_elems)
    message, odd_ref[...] = select_messages(parity, sent_plane(planes[0], lasts[0]), right)
    for even_ref, at in zip(even_refs, (0, PARTS[0], PARTS[0] + PARTS[1])):
        even_ref[...] = message[at : at + even_ref.shape[0]]
    for copy in copies[6:]:
        copy.wait()


def prepare_kernel(cur_ref, material_ref, own_ref, touch_ref, base_ref, edge_part_ref):
    cur = cur_ref[...]
    base_ref[...] = own_force(own_ref, cur, material_ref[0:1], material_ref[1:2])
    edge_part_ref[...] = dot(touch_ref[...], stacked(cur[:PLANE]))


def setup_kernel(next_ref, density_ref, mass_ref, fol_ref, minv_ref, scratch, *, y_elems, z_elems):
    gather = gather_table(y_elems * z_elems, z_elems)
    scratch[...] = jnp.zeros_like(scratch)
    fol_ref[...] = to_elements(lambda c, y: next_ref[c, y], scratch.at[0], gather, y_elems)
    density = to_elements(lambda c, y: density_ref[y], scratch.at[1], gather, y_elems, 2)
    table = mass_ref[...]
    first = lax.axis_index("dom") == 0
    plane = lax.broadcasted_iota(jnp.int32, table.shape, 0) < PLANE
    table = jnp.where(jnp.logical_and(first, plane), 2.0 * table, table)
    minv_ref[...] = jnp.where(table > 0.0, table / jnp.where(table > 0.0, density, 1.0), 0.0)


def step_kernel(*refs, step, last, extra, last_place, pair, y_elems, z_elems):
    cur_ref, fol_ref, minv_ref, base_ref, touch_ref, material_ref, odd_ref, up_ref = refs[:8]
    refs = list(refs[8:])
    down_ref = None if pair else refs.pop(0)
    even_in = jnp.concatenate([refs.pop(0)[...] for _ in PARTS], axis=0)
    down_ref = up_ref if pair else down_ref
    first_up_ref, own_ref, first_own_ref, far_ref, edge_ref = refs[:5]
    refs = refs[5 + extra :]
    if last:
        later_ref, back_ref, out_hbm, later_hbm, scratch, out_ref, sems = refs
        copies = start_copies([(later_ref, later_hbm)], sems)
    else:
        new_ref, *even_outs, odd_out, fault_out = refs
    place = lax.axis_index("dom")
    lanes = cur_ref.shape[1]
    even = place % 2 == 0
    far = jnp.where(place == last_place, 0.0, jnp.where(even, even_in, odd_ref[...]))
    left = jnp.where(place == 0, 0.0, jnp.where(even, odd_ref[...], even_in))
    far = far_plane(far, z_elems)
    left, left_lame, left_shear = left_blocks(left, z_elems)
    lame_row, shear_row = material_ref[0:1], material_ref[1:2]
    far = jnp.concatenate([stacked(lame_row * far), stacked(shear_row * far)], axis=0)
    from_left = left_lame * touch_ref[:PLANE] + left_shear * touch_ref[PLANE:]
    row, lane = block_iotas(lanes)
    across = over(lane, z_elems)
    shared = shared_rows(row)
    add_first = jnp.logical_and(shared, across > 0)
    take_last = jnp.logical_and(shared, across < y_elems - 1)
    pull_first = jnp.logical_and(shared, across == 0)
    pull_last = jnp.logical_and(shared, across == y_elems - 1)
    above = above_lanes(lanes, z_elems)
    middle = lax.broadcasted_iota(jnp.int32, (3, lanes), 0) == 1
    gap = jnp.zeros((4, lanes), jnp.float32)
    if not last:
        fault_out[FAULT:] = jnp.zeros_like(fault_out[FAULT:])
    planes = []
    for x in range(4):
        rows = slice(x * PLANE, (x + 1) * PLANE)
        force = base_ref[rows] + dot(far_ref[rows], far)
        blocks = [force[zl * BLOCK : (zl + 1) * BLOCK] for zl in range(5)]
        if x == 0:
            blocks = [b + from_left[i * BLOCK : (i + 1) * BLOCK] for i, b in enumerate(blocks)]
            blocks[:4] = [b + left[i] for i, b in enumerate(blocks[:4])]
        blocks[0], blocks[4] = (
            blocks[0] + jnp.where(above, pltpu.roll(blocks[4], 1, 1), 0.0),
            blocks[4] + pltpu.roll(blocks[0], lanes - 1, 1),
        )
        lasts, firsts = pl.ds(x, 3, stride=8), pl.ds(4 + x, 3, stride=8)
        k = slice(FAULT + 4 * step + x, FAULT + 4 * step + x + 1)
        below_stiff = jnp.where(middle, lock_stiffness, first_up_ref[k])
        own_stiff = jnp.where(middle, lock_stiffness, first_own_ref[k])
        pulled = jnp.concatenate(
            [gap, below_stiff * (up_ref[lasts, :] - own_ref[firsts, :]), gap[:1]], axis=0
        )
        pulled_last = jnp.concatenate(
            [gap, own_stiff * (down_ref[firsts, :] - own_ref[lasts, :]), gap[:1]], axis=0
        )
        for zl in range(5):
            low, high = blocks[zl][:8], blocks[zl][8:]
            move = zl * z_elems if zl < 4 else 1
            blocks[zl] = jnp.concatenate(
                [
                    low
                    + jnp.where(add_first, shifted(high, z_elems), 0.0)
                    - jnp.where(pull_first, shifted(pulled, -move), 0.0),
                    high
                    + jnp.where(take_last, shifted(low, -z_elems), 0.0)
                    - jnp.where(pull_last, shifted(pulled_last, -move - z_elems), 0.0),
                ],
                axis=0,
            )
        plane = (2.0 * cur_ref[rows] - fol_ref[rows]) - minv_ref[rows] * jnp.concatenate(
            blocks, axis=0
        )
        if last:
            planes.append(plane)
        else:
            new_ref[rows] = plane
            end = store_fault(fault_out, x, plane, z_elems)
            planes.append(stacked(plane))
            if x == 0:
                first = sent_plane(plane, end)
    if last:

        def send(c):
            copy = pltpu.make_async_copy(out_ref.at[c], out_hbm.at[c], sems.at[1 + c])
            copy.start()
            copies.append(copy)

        from_elements(
            jnp.concatenate(planes, axis=0), scratch, back_ref, out_ref, y_elems, send
        )
        for copy in copies:
            copy.wait()
    else:
        edge = dot(edge_ref[...], jnp.concatenate(planes, axis=0))
        right = edge_message(edge, lame_row, shear_row, z_elems)
        message, odd_out[...] = select_messages(place % 2, first, right)
        for even_out, at in zip(even_outs, (0, PARTS[0], PARTS[0] + PARTS[1])):
            even_out[...] = message[at : at + even_out.shape[0]]


def mask_kernel(owner_ref, flags_ref, stress_ref, _, mask_ref, weight_ref, *, z_elems):
    shape = (PATCH_ROWS, mask_ref.shape[1])
    first = (lax.axis_index("dom") - REACH) * PATCH_DEV
    number = lax.broadcasted_iota(jnp.int32, shape, 0) + first
    for x in range(4):
        mask = jnp.where(number == owner_ref[:, x : x + 1], 1.0, 0.0)
        mask_ref[PATCH_ROWS * x : PATCH_ROWS * (x + 1)] = mask
    stress = stress_ref[...]
    weights = []
    for i in range(flags_ref.shape[0]):
        flag = flags_ref[i]
        weights.append(
            stress * jnp.where(flag == 1, 0.5, jnp.where(flag == 2, 1.0, 0.0))
        )
    fault = fault_table(mask_ref.shape[1], z_elems)
    weight_ref[...] = exact_dot(jnp.concatenate(weights, axis=0), fault)


def output_kernel(*refs, pair, steps, y_elems, z_elems):
    field_ref, back_ref, weight_ref = refs[:3]
    out_ref, grad_ref, table_ref, scratch = refs[-4:]
    messages = refs[3:-4]
    count = 2 if pair else 3
    grad = 0.0
    for i in range(steps):
        group = messages[count * i : count * (i + 1)]
        slip = -group[0][:4]
        if i < steps - 1:
            slip = slip + group[-1][4:8]
        grad = grad + slip * weight_ref[4 * i : 4 * i + 4]
    grad_ref[...] = grad
    table_ref[...] = fault_table_back(weight_ref.shape[1], z_elems)
    from_elements(field_ref[...], scratch, back_ref, out_ref, y_elems)


def patch_kernel(*refs, pair, steps):
    mask_ref, weight_ref, grad_ref, table_ref, _ = refs[:5]
    first_ref = refs[5] if pair else refs[6]
    home_out, out_a, out_b, out_c, out_d = refs[-5:]
    place = lax.axis_index("dom")
    grad = grad_ref[...] + first_ref[4:8] * weight_ref[4 * (steps - 1) : 4 * steps]
    total = 0.0
    for x in range(4):
        total = total + mask_ref[PATCH_ROWS * x : PATCH_ROWS * (x + 1)] * grad[x : x + 1]
    total = exact_dot(total, table_ref[...])
    rows = [total[2 * i : 2 * i + 2] for i in range(5)]
    home_out[...] = rows[2]
    even = place % 2 == 0
    out_a[...] = jnp.where(even, rows[3], rows[1])
    out_b[...] = jnp.where(even, rows[1], rows[3])
    low = place % 4 < 2
    out_c[...] = jnp.where(low, rows[4], rows[0])
    out_d[...] = jnp.where(low, rows[0], rows[4])


def sum_kernel(*refs):
    refs[-1][...] = sum(ref[...] for ref in refs[:-1])


VMEM = pl.BlockSpec(memory_space=pltpu.VMEM)
HBM = pl.BlockSpec(memory_space=pltpu.HBM)
SMEM = pl.BlockSpec(memory_space=pltpu.SMEM)
ANY = pl.BlockSpec(memory_space=pl.ANY)


def kernel_call(body, outs, args, in_smem=(), scratch=(), in_hbm=(), kept=(), unread=(), stay=False, out_spec=VMEM, **static):
    shapes = []
    for out in outs:
        shape, dtype = out if isinstance(out[0], tuple) else (out, jnp.float32)
        shapes.append((pltpu.VMEM if in_hbm or stay else jax.ShapeDtypeStruct)(shape, dtype))
    specs = [VMEM] * len(args)
    for places, spec in ((in_smem, SMEM), (in_hbm, HBM), (unread, ANY)):
        for i in places:
            specs[i] = spec
    copied = [pltpu.VMEM(args[i].shape, args[i].dtype) for i in in_hbm if i not in kept]
    if in_hbm:
        copied.append(pltpu.SemaphoreType.DMA((len(in_hbm),)))
    return pl.pallas_call(
        functools.partial(body, **static) if static else body,
        out_shape=shapes,
        in_specs=specs,
        out_specs=[out_spec] * len(shapes),
        scratch_shapes=list(scratch) + copied,
        compiler_params=pltpu.CompilerParams(
            vmem_limit_bytes=(56 if in_hbm else 24) * 2**20
        ),
    )(*args)


def swapped(block, distance, group):
    size, across = lax.axis_size("dom"), lax.axis_size("depth")
    partner = {}
    for left in range(size - distance):
        if left // distance % 2 == group:
            partner[left], partner[left + distance] = left + distance, left
    route = []
    for i in range(size):
        for j in range(across):
            other, side = partner.get(i, i), j
            if i not in partner and i ^ 1 < size and i ^ 1 not in partner:
                other = i ^ 1
            elif i not in partner:
                side = min(j ^ 1, across - 1)
            route.append((i * across + j, other * across + side))
    return lax.ppermute(block, ("dom", "depth"), route)


def from_behind(block, axis, distance):
    size = lax.axis_size(axis)
    return lax.ppermute(block, axis, [((i - distance) % size, i) for i in range(size)])


def on_device(
    adjoint_now,
    adjoint_next,
    lame_first,
    shear_modulus,
    density,
    branch_flags,
    weak_slope,
    normal_stress,
    patch_owner,
):
    x_elems, y_elems, z_elems = lame_first.shape
    lanes = y_elems * z_elems
    assert x_elems == 1 and lanes == adjoint_now.shape[3]
    steps = branch_flags.shape[0]
    pair = lax.axis_size("depth") == 2
    own_table, far_table, edge_table, touch_table = (jnp.asarray(t) for t in stiffness_tables())
    back = jnp.asarray(back_table(y_elems, z_elems))
    mass = jnp.asarray(mass_table(y_elems, z_elems))
    now = jnp.transpose(adjoint_now, (0, 2, 1, 3))
    following = jnp.transpose(adjoint_next, (0, 2, 1, 3))
    rho = jnp.transpose(density, (1, 0, 2))
    flags = branch_flags[:, 0]
    native = pltpu.VMEM((y_elems, 4 * BLOCK, lanes), jnp.float32)
    field = (4 * PLANE, lanes)
    plane = (SENT, lanes)
    parts = [(rows, lanes) for rows in PARTS]

    def exchange(even, odd, fault_rows):
        if pair:
            faults = [from_behind(fault_rows, "depth", 1)]
        else:
            faults = [from_behind(fault_rows, "depth", 1), from_behind(fault_rows, "depth", -1)]
        return [swapped(part, 1, 0) for part in even], swapped(odd, 1, 1), faults

    later_used = (
        edge_table, following, rho, mass, own_table, far_table, touch_table, back, flags,
        normal_stress[0], patch_owner,
    )
    assert len(later_used) == LATER
    first_out = kernel_call(
        first_kernel,
        [field] + parts + [plane, (FAULT + 4 * steps, lanes), (8, lanes)]
        + [(t.shape, t.dtype) for t in later_used],
        (now, flags, weak_slope[0], lame_first[0], shear_modulus[0]) + later_used,
        scratch=[native],
        in_hbm=range(5 + LATER),
        kept=range(5, 5 + LATER),
    )
    cur, *even, odd, fault_rows, material = first_out[:-LATER]
    edge_table, following, rho, mass, own_table, far_table, touch_table, back = first_out[-LATER:-3]
    flags, stress, owner = first_out[-3:]
    even_in, odd_in, fault_in = exchange(even, odd, fault_rows)
    first_fault, first_in = fault_rows, fault_in
    fol, minv = kernel_call(
        setup_kernel,
        [field, field],
        (following, rho, mass),
        scratch=[pltpu.VMEM((2, y_elems, 4 * BLOCK, lanes), jnp.float32)],
        y_elems=y_elems,
        z_elems=z_elems,
    )
    seen = []
    for step in range(steps):
        last = step == steps - 1
        seen += [fault_rows] + fault_in
        base, touch = kernel_call(
            prepare_kernel,
            [field, (2 * PLANE, lanes)],
            [cur, material, own_table, touch_table],
            (),
        )
        args = [cur, fol, minv, base, touch, material, odd_in] + fault_in + even_in
        args += [first_in[0], fault_rows, first_fault, far_table, edge_table]
        static = dict(
            step=step, last=last, extra=1 if last or step == 1 else 0, last_place=lax.axis_size("dom") - 1, pair=pair, y_elems=y_elems,
            z_elems=z_elems,
        )
        if step == 1:
            mask, weight = kernel_call(
                mask_kernel,
                [(4 * PATCH_ROWS, lanes), (4 * steps, lanes)],
                [owner, flags, stress, cur],
                unread=(3,),
                z_elems=z_elems,
            )
            args.append(mask)
        if not last:
            new, *even, odd, new_fault = kernel_call(
                step_kernel,
                [field] + parts + [plane, (SENT_FAULT, lanes)],
                args,
                unread=(len(args) - 1,) if step == 1 else (),
                **static,
            )
            fol, cur, fault_rows = cur, new, new_fault
            even_in, odd_in, fault_in = exchange(even, odd, fault_rows)
        else:
            whole = (3, 4 * y_elems + 1, 4, lanes)
            known = seen[: len(seen) - len(fault_in)]
            later, grad, table = kernel_call(
                output_kernel,
                [whole, (4, lanes), ((lanes, lanes), jnp.bfloat16)],
                [cur, back, weight] + known,
                scratch=[native],
                stay=True,
                pair=pair,
                steps=steps,
                y_elems=y_elems,
                z_elems=z_elems,
            )
            sums = kernel_call(
                patch_kernel,
                [(PATCH_DEV, lanes)] * 5,
                [mask, weight, grad, table, odd_in] + fault_in + even_in + [touch],
                unread=(4,) + tuple(range(5 + len(fault_in), 9 + len(fault_in))),
                pair=pair,
                steps=steps,
            )
            shares = [sums[0]]
            for i, distance, group in ((3, 2, 0), (2, 1, 1), (4, 2, 1), (1, 1, 0)):
                shares.append(swapped(sums[i], distance, group))
            patch_sums = kernel_call(sum_kernel, [(PATCH_DEV, lanes)], shares)[0]
            earlier, later = kernel_call(
                step_kernel,
                [whole, whole],
                args + [sums[0], later, back],
                scratch=[
                    native, pltpu.VMEM(whole, jnp.float32), pltpu.SemaphoreType.DMA((4,)),
                ],
                unread=(len(args),),
                out_spec=HBM,
                **static,
            )
    return (
        jnp.transpose(earlier, (0, 2, 1, 3)),
        jnp.transpose(later, (0, 2, 1, 3)),
        patch_sums[None],
    )


def solution(mesh):
    return jax.shard_map(
        on_device,
        mesh=mesh,
        in_specs=(
            P(None, "dom", "depth", None),
            P(None, "dom", "depth", None),
            P("dom", "depth", None),
            P("dom", "depth", None),
            P("dom", "depth", None),
            P(None, "depth", "dom", None),
            P("depth", "dom", None),
            P("depth", "dom", None),
            P("depth", "dom"),
        ),
        out_specs=(
            P(None, "dom", "depth", None),
            P(None, "dom", "depth", None),
            P("depth", "dom", None),
        ),
        check_vma=False,
    )
```

```python
import functools
import math

import jax
import jax.numpy as jnp
import ml_dtypes
import numpy as np
from jax import lax
from jax.experimental import pallas as pl
from jax.experimental.pallas import tpu as pltpu
from jax.sharding import PartitionSpec as P

PATCH_DEV = 2
REACH = 2
PATCH_ROWS = 16
LATER = 11
FAULT = 24
SENT_FAULT = 28
PARTS = (24, 24, 16)

time_step = 0.01
lock_stiffness = 0.5

BLOCK = 16
ROWS = ((0, 1, 2), (3, 4, 5), (11, 12, 13), (6, 7, 14), (8, 9, 10))
PLANE = 5 * BLOCK


def basis_tables():
    points = [-1.0, -math.sqrt(3.0 / 7.0), 0.0, math.sqrt(3.0 / 7.0), 1.0]
    quad_weights = np.array([0.1, 49.0 / 90.0, 32.0 / 45.0, 49.0 / 90.0, 0.1])
    products = []
    for first in range(5):
        value = 1.0
        for other in range(5):
            if other != first:
                value = value * (points[first] - points[other])
        products.append(value)
    derivative = np.zeros((5, 5))
    for row in range(5):
        for column in range(5):
            if row == column:
                total = 0.0
                for other in range(5):
                    if other != row:
                        total = total + 1.0 / (points[row] - points[other])
                derivative[row, column] = total
            else:
                derivative[row, column] = (
                    products[row] / products[column] / (points[row] - points[column])
                )
    return (quad_weights, derivative)


def two_parts(table):
    high = table.astype(ml_dtypes.bfloat16)
    low = (table - high.astype(np.float64)).astype(ml_dtypes.bfloat16)
    return np.stack([high, low])


def element_stiffness():
    weights, derivative = basis_tables()
    eye = np.eye(5)
    slope = 2.0 * derivative
    grads = [
        np.kron(slope, np.kron(eye, eye)),
        np.kron(eye, np.kron(eye, slope)),
        np.kron(eye, np.kron(slope, eye)),
    ]
    quad = np.kron(weights, np.kron(weights, weights)) / 8.0
    first = np.zeros((125, 3, 125, 3))
    second = np.zeros((125, 3, 125, 3))
    lap = sum(g.T @ (quad[:, None] * g) for g in grads)
    for c in range(3):
        second[:, c, :, c] += lap
        for d in range(3):
            first[:, c, :, d] += grads[c].T @ (quad[:, None] * grads[d])
            second[:, c, :, d] += grads[d].T @ (quad[:, None] * grads[c])
    where = [
        node // 5 * BLOCK + ROWS[node % 5][c] for node in range(125) for c in range(3)
    ]
    wide = []
    for small in (first, second):
        big = np.zeros((5 * PLANE, 5 * PLANE))
        big[np.ix_(where, where)] = small.reshape(375, 375)
        wide.append(big)
    return wide


OWN_COLS = 384


def padded_table(table, columns):
    return np.pad(table, ((0, 0), (0, columns - table.shape[1])))


@functools.cache
def stiffness_tables():
    wide = element_stiffness()
    own = 4 * PLANE
    planes = [slice(x * PLANE, (x + 1) * PLANE) for x in range(5)]
    inner = np.concatenate([w[:own, :own] for w in wide])

    def three(table):
        high, low = two_parts(table)
        return padded_table(np.concatenate([high, low, high], axis=1), 256)

    def both(rows, columns):
        return three(np.concatenate([w[rows, columns] for w in wide]))

    return (
        two_parts(padded_table(inner, OWN_COLS)),
        np.concatenate([three(w[:own, planes[4]]) for w in wide], axis=1),
        np.concatenate([both(planes[4], planes[x]) for x in range(4)], axis=1),
        both(planes[4], planes[4]),
    )


@functools.cache
def back_table(y_elems, z_elems):
    lanes = y_elems * z_elems
    depth = 4 * z_elems
    back = np.zeros((4 * lanes, y_elems * depth), ml_dtypes.bfloat16)
    for yel in range(y_elems):
        for k in range(z_elems):
            for zl in range(4):
                back[zl * lanes + yel * z_elems + k, yel * depth + 4 * k + zl] = 1
    return back


@functools.cache
def mass_table(y_elems, z_elems):
    weights, _ = basis_tables()
    table = np.zeros((4, 5, BLOCK, y_elems, z_elems))
    for x in range(4):
        mx = 0.2 if x == 0 else weights[x]
        for zl in range(5):
            for yl in range(5):
                for yel in range(y_elems):
                    my = weights[yl]
                    if (yl == 0 and yel > 0) or (yl == 4 and yel < y_elems - 1):
                        my = 0.2
                    mz = np.full(z_elems, weights[zl])
                    if zl == 0:
                        mz[1:] = 0.2
                    if zl == 4:
                        mz[:] = 0.2
                    value = time_step * time_step * 8.0 / (mx * my * mz)
                    if zl == 4:
                        value[-1] = 0.0
                    table[x, zl, list(ROWS[yl]), yel] = value
    return table.reshape(4 * PLANE, y_elems * z_elems).astype(np.float32)


def pieces(value, count):
    out = []
    for _ in range(count):
        piece = value.astype(jnp.bfloat16)
        out.append(piece)
        value = value - piece.astype(jnp.float32)
    return out


def dot(a, b):
    return jnp.dot(a, b, preferred_element_type=jnp.float32)


def exact_dot(value, table, count=3):
    rows = value.shape[0]
    result = dot(jnp.concatenate(pieces(value, count), axis=0), table)
    total = result[:rows]
    for i in range(1, count):
        total = total + result[i * rows : (i + 1) * rows]
    return total


def split_dot(table_high, table_low, value):
    lanes = value.shape[1]
    high, low = pieces(value, 2)
    wide = dot(table_high, jnp.concatenate([high, low], axis=1))
    return wide[:, :lanes] + (wide[:, lanes:] + dot(table_low, high))


def over(value, size):
    if size & (size - 1) == 0:
        return lax.shift_right_logical(value, np.int32(size.bit_length() - 1))
    return lax.div(value, np.int32(size))


def within(value, size):
    return value & (size - 1) if size & (size - 1) == 0 else lax.rem(value, np.int32(size))


def ones_where(shape, axis, wanted):
    line = (shape[0], 1) if axis == 0 else (1, shape[1])
    target = wanted(lax.broadcasted_iota(jnp.int32, line, axis))
    number = lax.broadcasted_iota(jnp.int32, shape, 1 - axis)
    return jnp.where(number == target, 1.0, 0.0).astype(jnp.bfloat16)


def gather_table(lanes, z_elems):
    return ones_where(
        (lanes, 5 * lanes), 1, lambda c: 4 * within(c, z_elems) + over(c, lanes)
    )


def fault_table(lanes, z_elems):
    return ones_where((lanes, lanes), 1, lambda c: 4 * within(c, z_elems) + over(c, z_elems))


def fault_table_back(lanes, z_elems):
    return ones_where((lanes, lanes), 0, lambda c: 4 * within(c, z_elems) + over(c, z_elems))


def stacked(value):
    high, low = pieces(value, 2)
    gap = jnp.zeros((256 - 3 * value.shape[0], value.shape[1]), jnp.bfloat16)
    return jnp.concatenate([high, high, low, gap], axis=0)


def to_elements(native, scratch, table, y_elems, parts=3):
    group = 4 * BLOCK
    for c in range(3):
        for y in range(4 * y_elems + 1):
            rows = native(c, y)
            if y < 4 * y_elems:
                scratch[y // 4, pl.ds(ROWS[y % 4][c], 4, stride=BLOCK), :] = rows
            if y % 4 == 0 and y > 0:
                scratch[y // 4 - 1, pl.ds(ROWS[4][c], 4, stride=BLOCK), :] = rows
    high, middle, *low = pieces(
        jnp.concatenate([scratch[i] for i in range(y_elems)], axis=0), parts
    )
    result = dot(
        jnp.concatenate([high, middle], axis=1), jnp.concatenate([table, table], axis=0)
    )
    for piece in low:
        result = result + dot(piece, table)
    lanes = result.shape[1] // 5
    across = lax.broadcasted_iota(jnp.int32, (1, result.shape[1]), 1)
    across = over(within(across, lanes), lanes // y_elems)
    total = result[:group]
    for yel in range(1, y_elems):
        total = jnp.where(across == yel, result[yel * group : (yel + 1) * group], total)
    blocks = []
    for x in range(4):
        for zl in range(5):
            blocks.append(total[x * BLOCK : (x + 1) * BLOCK, zl * lanes : (zl + 1) * lanes])
    return jnp.concatenate(blocks, axis=0)


def from_elements(field, scratch, back_ref, out_ref, y_elems, stored=None):
    rows = []
    for x in range(4):
        rows.append(
            jnp.concatenate(
                [field[x * PLANE + zl * BLOCK : x * PLANE + (zl + 1) * BLOCK] for zl in range(4)],
                axis=1,
            )
        )
    result = exact_dot(jnp.concatenate(rows, axis=0), back_ref[...])
    depth = result.shape[1] // y_elems
    for yel in range(y_elems):
        scratch[yel] = result[:, yel * depth : (yel + 1) * depth]
    for c in range(3):
        for y in range(4 * y_elems + 1):
            yel, yl = (y // 4, y % 4) if y < 4 * y_elems else (y_elems - 1, 4)
            out_ref[c, y] = scratch[yel, pl.ds(ROWS[yl][c], 4, stride=BLOCK), :]
        if stored is not None:
            stored(c)


def shifted(rows, lanes):
    lanes = lanes % rows.shape[1]
    return pltpu.roll(rows, lanes, 1) if lanes else rows


def block_iotas(lanes):
    return (
        lax.broadcasted_iota(jnp.int32, (8, lanes), 0),
        lax.broadcasted_iota(jnp.int32, (8, lanes), 1),
    )


def store_fault(out_ref, x, plane, z_elems):
    lanes = plane.shape[1]
    _, lane = block_iotas(lanes)
    first = last = jnp.zeros((8, lanes), jnp.float32)
    for zl in range(4):
        at = zl * BLOCK
        here = over(lane, z_elems) == zl
        first = jnp.where(here, shifted(plane[at : at + 8], zl * z_elems), first)
        last = jnp.where(here, shifted(plane[at + 8 : at + 16], (zl + 1) * z_elems), last)
    out_ref[pl.ds(x, 3, stride=8), :] = last[:3]
    out_ref[pl.ds(4 + x, 3, stride=8), :] = first[:3]


def select_messages(parity, left, right):
    even = parity == 0
    return jnp.where(even, right, left), jnp.where(even, left, right)


def material_rows(lame_ref, shear_ref):
    y_elems, z_elems = lame_ref.shape
    both = jnp.concatenate([lame_ref[...], shear_ref[...]], axis=0)
    spread = ones_where((z_elems, y_elems * z_elems), 1, lambda c: within(c, z_elems))
    tiled = exact_dot(both, spread)
    row = lax.broadcasted_iota(jnp.int32, tiled.shape, 0)
    lane = lax.broadcasted_iota(jnp.int32, tiled.shape, 1)
    kept = jnp.where(within(row, y_elems) == over(lane, z_elems), tiled, 0.0)
    return (
        jnp.sum(kept[:y_elems], axis=0, keepdims=True),
        jnp.sum(kept[y_elems:], axis=0, keepdims=True),
    )


def above_lanes(lanes, z_elems):
    return within(lax.broadcasted_iota(jnp.int32, (BLOCK, lanes), 1), z_elems) != 0


def edge_message(result, lame_row, shear_row, z_elems):
    lanes = result.shape[1]
    force = lame_row * result[:PLANE] + shear_row * result[PLANE:]
    top = force[:BLOCK] + jnp.where(
        above_lanes(lanes, z_elems), pltpu.roll(force[4 * BLOCK :], 1, 1), 0.0
    )
    row = lax.broadcasted_iota(jnp.int32, top.shape, 0)
    top = jnp.where(row == BLOCK - 1, lame_row, top)
    second = jnp.where(row == BLOCK - 1, shear_row, force[BLOCK : 2 * BLOCK])
    return jnp.concatenate([top, second, force[2 * BLOCK : 4 * BLOCK]], axis=0)


def edge_of(field_ref, edge_ref, material_ref, z_elems):
    planes = [stacked(field_ref[x * PLANE : (x + 1) * PLANE]) for x in range(4)]
    edge = dot(edge_ref[...], jnp.concatenate(planes, axis=0))
    return edge_message(edge, material_ref[0:1], material_ref[1:2], z_elems)


def own_force(own_ref, cur, lame_row, shear_row):
    rows, lanes = cur.shape
    padded = jnp.concatenate([cur, jnp.zeros((OWN_COLS - rows, lanes), jnp.float32)], axis=0)
    result = split_dot(own_ref[0], own_ref[1], padded)
    return lame_row * result[:rows] + shear_row * result[rows:]


def start_copies(pairs, sems):
    copies = [
        pltpu.make_async_copy(source, target, sems.at[i])
        for i, (source, target) in enumerate(pairs)
    ]
    for copy in copies:
        copy.start()
    return copies


def first_kernel(
    now_hbm,
    flags_hbm,
    weak_hbm,
    lame_hbm,
    shear_hbm,
    *refs,
):
    later_hbm, refs = refs[:LATER], refs[LATER:]
    cur_ref, *even_refs, odd_ref, fault_out_ref, material_ref = refs[:7]
    later_refs, refs = refs[7 : 7 + LATER], refs[7 + LATER :]
    scratch, now_ref, flags_ref, weak_ref, lame_ref, shear_ref, sems = refs
    copies = start_copies(
        [
            (now_hbm, now_ref),
            (lame_hbm, lame_ref),
            (shear_hbm, shear_ref),
            (flags_hbm, flags_ref),
            (weak_hbm, weak_ref),
            (later_hbm[0], later_refs[0]),
        ]
        + list(zip(later_hbm[1:], later_refs[1:])),
        sems,
    )
    edge_ref = later_refs[0]
    y_elems, z_elems = lame_ref.shape
    lanes = y_elems * z_elems
    parity = lax.axis_index("dom") % 2
    gather = gather_table(lanes, z_elems)
    fault = fault_table(lanes, z_elems)
    scratch[...] = jnp.zeros_like(scratch)
    for copy in copies[1:5]:
        copy.wait()
    lame_row, shear_row = material_rows(lame_ref, shear_ref)
    material_ref[...] = jnp.concatenate(
        [lame_row, shear_row, jnp.zeros((6, lanes), jnp.float32)], axis=0
    )
    weak = weak_ref[...]
    tangent = []
    for i in range(flags_ref.shape[0]):
        flag = flags_ref[i]
        tangent.append(
            jnp.where(flag == 0, lock_stiffness, jnp.where(flag == 1, -weak, 0.0))
        )
    fault_out_ref[FAULT:] = exact_dot(jnp.concatenate(tangent, axis=0), fault)
    copies[0].wait()
    cur = to_elements(lambda c, y: now_ref[c, y], scratch, gather, y_elems)
    cur_ref[...] = cur
    planes = [cur[x * PLANE : (x + 1) * PLANE] for x in range(4)]
    for x in range(4):
        store_fault(fault_out_ref, x, planes[x], z_elems)
    copies[5].wait()
    edge = dot(edge_ref[...], jnp.concatenate([stacked(p) for p in planes], axis=0))
    right = edge_message(edge, lame_row, shear_row, z_elems)
    message, odd_ref[...] = select_messages(parity, cur[: 4 * BLOCK], right)
    for even_ref, at in zip(even_refs, (0, PARTS[0], PARTS[0] + PARTS[1])):
        even_ref[...] = message[at : at + even_ref.shape[0]]
    for copy in copies[6:]:
        copy.wait()


def prepare_kernel(cur_ref, material_ref, own_ref, touch_ref, base_ref, edge_part_ref):
    cur = cur_ref[...]
    base_ref[...] = own_force(own_ref, cur, material_ref[0:1], material_ref[1:2])
    edge_part_ref[...] = dot(touch_ref[...], stacked(cur[:PLANE]))


def setup_kernel(next_ref, density_ref, mass_ref, fol_ref, minv_ref, scratch, *, y_elems, z_elems):
    gather = gather_table(y_elems * z_elems, z_elems)
    scratch[...] = jnp.zeros_like(scratch)
    fol_ref[...] = to_elements(lambda c, y: next_ref[c, y], scratch.at[0], gather, y_elems)
    density = to_elements(lambda c, y: density_ref[y], scratch.at[1], gather, y_elems, 2)
    table = mass_ref[...]
    first = lax.axis_index("dom") == 0
    plane = lax.broadcasted_iota(jnp.int32, table.shape, 0) < PLANE
    table = jnp.where(jnp.logical_and(first, plane), 2.0 * table, table)
    minv_ref[...] = jnp.where(table > 0.0, table / jnp.where(table > 0.0, density, 1.0), 0.0)


def step_kernel(*refs, step, last, extra, last_place, pair, y_elems, z_elems):
    cur_ref, fol_ref, minv_ref, base_ref, touch_ref, material_ref, odd_ref, up_ref = refs[:8]
    refs = list(refs[8:])
    down_ref = None if pair else refs.pop(0)
    even_in = jnp.concatenate([refs.pop(0)[...] for _ in PARTS], axis=0)
    down_ref = up_ref if pair else down_ref
    first_up_ref, own_ref, first_own_ref, far_ref, edge_ref = refs[:5]
    refs = refs[5 + extra :]
    if last:
        later_ref, back_ref, out_hbm, later_hbm, scratch, out_ref, sems = refs
        copies = start_copies([(later_ref, later_hbm)], sems)
    else:
        new_ref, odd_out, fault_out = refs
    place = lax.axis_index("dom")
    lanes = cur_ref.shape[1]
    even = place % 2 == 0
    far = jnp.where(place == last_place, 0.0, jnp.where(even, even_in, odd_ref[...]))
    left = jnp.where(place == 0, 0.0, jnp.where(even, odd_ref[...], even_in))
    lane_wide = lax.broadcasted_iota(jnp.int32, (BLOCK, lanes), 1)
    below = jnp.where(
        within(lane_wide, z_elems) != z_elems - 1, pltpu.roll(far[:BLOCK], lanes - 1, 1), 0.0
    )
    far = jnp.concatenate([far, below], axis=0)
    lame_row, shear_row = material_ref[0:1], material_ref[1:2]
    far = jnp.concatenate([stacked(lame_row * far), stacked(shear_row * far)], axis=0)
    left_lame = left[BLOCK - 1 : BLOCK]
    left_shear = left[2 * BLOCK - 1 : 2 * BLOCK]
    from_left = left_lame * touch_ref[:PLANE] + left_shear * touch_ref[PLANE:]
    row, lane = block_iotas(lanes)
    across = over(lane, z_elems)
    shared = row < 3
    add_first = jnp.logical_and(shared, across > 0)
    take_last = jnp.logical_and(shared, across < y_elems - 1)
    pull_first = jnp.logical_and(shared, across == 0)
    pull_last = jnp.logical_and(shared, across == y_elems - 1)
    above = above_lanes(lanes, z_elems)
    middle = lax.broadcasted_iota(jnp.int32, (3, lanes), 0) == 1
    gap = jnp.zeros((5, lanes), jnp.float32)
    if not last:
        fault_out[FAULT:] = jnp.zeros_like(fault_out[FAULT:])
    planes = []
    for x in range(4):
        rows = slice(x * PLANE, (x + 1) * PLANE)
        force = base_ref[rows] + dot(far_ref[rows], far)
        blocks = [force[zl * BLOCK : (zl + 1) * BLOCK] for zl in range(5)]
        if x == 0:
            blocks = [b + from_left[i * BLOCK : (i + 1) * BLOCK] for i, b in enumerate(blocks)]
            blocks[:4] = [b + left[i * BLOCK : (i + 1) * BLOCK] for i, b in enumerate(blocks[:4])]
        blocks[0], blocks[4] = (
            blocks[0] + jnp.where(above, pltpu.roll(blocks[4], 1, 1), 0.0),
            blocks[4] + pltpu.roll(blocks[0], lanes - 1, 1),
        )
        lasts, firsts = pl.ds(x, 3, stride=8), pl.ds(4 + x, 3, stride=8)
        k = slice(FAULT + 4 * step + x, FAULT + 4 * step + x + 1)
        below_stiff = jnp.where(middle, lock_stiffness, first_up_ref[k])
        own_stiff = jnp.where(middle, lock_stiffness, first_own_ref[k])
        pulled = jnp.concatenate(
            [below_stiff * (up_ref[lasts, :] - own_ref[firsts, :]), gap], axis=0
        )
        pulled_last = jnp.concatenate(
            [own_stiff * (down_ref[firsts, :] - own_ref[lasts, :]), gap], axis=0
        )
        for zl in range(5):
            low, high = blocks[zl][:8], blocks[zl][8:]
            move = zl * z_elems if zl < 4 else 1
            blocks[zl] = jnp.concatenate(
                [
                    low
                    + jnp.where(add_first, shifted(high, z_elems), 0.0)
                    - jnp.where(pull_first, shifted(pulled, -move), 0.0),
                    high
                    + jnp.where(take_last, shifted(low, -z_elems), 0.0)
                    - jnp.where(pull_last, shifted(pulled_last, -move - z_elems), 0.0),
                ],
                axis=0,
            )
        plane = (2.0 * cur_ref[rows] - fol_ref[rows]) - minv_ref[rows] * jnp.concatenate(
            blocks, axis=0
        )
        if last:
            planes.append(plane)
        else:
            new_ref[rows] = plane
            store_fault(fault_out, x, plane, z_elems)
            if x == 0:
                first = plane[: 4 * BLOCK]
    if last:

        def send(c):
            copy = pltpu.make_async_copy(out_ref.at[c], out_hbm.at[c], sems.at[1 + c])
            copy.start()
            copies.append(copy)

        from_elements(
            jnp.concatenate(planes, axis=0), scratch, back_ref, out_ref, y_elems, send
        )
        for copy in copies:
            copy.wait()
    else:
        odd_out[...] = first

        @pl.when(jnp.logical_not(even))
        def _():
            odd_out[...] = edge_of(new_ref, edge_ref, material_ref, z_elems)


def on_chip_kernel(cur_ref, material_ref, edge_ref, *even_outs, z_elems):
    message = even_outs[-1]
    even_outs = even_outs[:-1]
    message[...] = cur_ref[: 4 * BLOCK]

    @pl.when(lax.axis_index("dom") % 2 == 0)
    def _():
        message[...] = edge_of(cur_ref, edge_ref, material_ref, z_elems)

    for even_out, at in zip(even_outs, (0, PARTS[0], PARTS[0] + PARTS[1])):
        even_out[...] = message[at : at + even_out.shape[0]]


def mask_kernel(owner_ref, flags_ref, stress_ref, _, mask_ref, weight_ref, *, z_elems):
    shape = (PATCH_ROWS, mask_ref.shape[1])
    first = (lax.axis_index("dom") - REACH) * PATCH_DEV
    number = lax.broadcasted_iota(jnp.int32, shape, 0) + first
    for x in range(4):
        mask = jnp.where(number == owner_ref[:, x : x + 1], 1.0, 0.0)
        mask_ref[PATCH_ROWS * x : PATCH_ROWS * (x + 1)] = mask
    stress = stress_ref[...]
    weights = []
    for i in range(flags_ref.shape[0]):
        flag = flags_ref[i]
        weights.append(
            stress * jnp.where(flag == 1, 0.5, jnp.where(flag == 2, 1.0, 0.0))
        )
    fault = fault_table(mask_ref.shape[1], z_elems)
    weight_ref[...] = exact_dot(jnp.concatenate(weights, axis=0), fault)


def output_kernel(*refs, pair, steps, y_elems, z_elems):
    field_ref, back_ref, weight_ref = refs[:3]
    out_ref, grad_ref, table_ref, scratch = refs[-4:]
    messages = refs[3:-4]
    count = 2 if pair else 3
    grad = 0.0
    for i in range(steps):
        group = messages[count * i : count * (i + 1)]
        slip = -group[0][:4]
        if i < steps - 1:
            slip = slip + group[-1][4:8]
        grad = grad + slip * weight_ref[4 * i : 4 * i + 4]
    grad_ref[...] = grad
    table_ref[...] = fault_table_back(weight_ref.shape[1], z_elems)
    from_elements(field_ref[...], scratch, back_ref, out_ref, y_elems)


def patch_kernel(*refs, pair, steps):
    mask_ref, weight_ref, grad_ref, table_ref, _ = refs[:5]
    first_ref = refs[5] if pair else refs[6]
    home_out, out_a, out_b, out_c, out_d = refs[-5:]
    place = lax.axis_index("dom")
    grad = grad_ref[...] + first_ref[4:8] * weight_ref[4 * (steps - 1) : 4 * steps]
    total = 0.0
    for x in range(4):
        total = total + mask_ref[PATCH_ROWS * x : PATCH_ROWS * (x + 1)] * grad[x : x + 1]
    total = exact_dot(total, table_ref[...])
    rows = [total[2 * i : 2 * i + 2] for i in range(5)]
    home_out[...] = rows[2]
    even = place % 2 == 0
    out_a[...] = jnp.where(even, rows[3], rows[1])
    out_b[...] = jnp.where(even, rows[1], rows[3])
    low = place % 4 < 2
    out_c[...] = jnp.where(low, rows[4], rows[0])
    out_d[...] = jnp.where(low, rows[0], rows[4])


def sum_kernel(*refs):
    refs[-1][...] = sum(ref[...] for ref in refs[:-1])


VMEM = pl.BlockSpec(memory_space=pltpu.VMEM)
HBM = pl.BlockSpec(memory_space=pltpu.HBM)
SMEM = pl.BlockSpec(memory_space=pltpu.SMEM)
ANY = pl.BlockSpec(memory_space=pl.ANY)


def kernel_call(body, outs, args, in_smem=(), scratch=(), in_hbm=(), kept=(), unread=(), stay=False, out_spec=VMEM, **static):
    shapes = []
    for out in outs:
        shape, dtype = out if isinstance(out[0], tuple) else (out, jnp.float32)
        shapes.append((pltpu.VMEM if in_hbm or stay else jax.ShapeDtypeStruct)(shape, dtype))
    specs = [VMEM] * len(args)
    for places, spec in ((in_smem, SMEM), (in_hbm, HBM), (unread, ANY)):
        for i in places:
            specs[i] = spec
    copied = [pltpu.VMEM(args[i].shape, args[i].dtype) for i in in_hbm if i not in kept]
    if in_hbm:
        copied.append(pltpu.SemaphoreType.DMA((len(in_hbm),)))
    return pl.pallas_call(
        functools.partial(body, **static) if static else body,
        out_shape=shapes,
        in_specs=specs,
        out_specs=[out_spec] * len(shapes),
        scratch_shapes=list(scratch) + copied,
        compiler_params=pltpu.CompilerParams(
            vmem_limit_bytes=(56 if in_hbm else 24) * 2**20
        ),
    )(*args)


def swapped(block, distance, group):
    size, across = lax.axis_size("dom"), lax.axis_size("depth")
    partner = {}
    for left in range(size - distance):
        if left // distance % 2 == group:
            partner[left], partner[left + distance] = left + distance, left
    route = []
    for i in range(size):
        for j in range(across):
            other, side = partner.get(i, i), j
            if i not in partner and i ^ 1 < size and i ^ 1 not in partner:
                other = i ^ 1
            elif i not in partner:
                side = min(j ^ 1, across - 1)
            route.append((i * across + j, other * across + side))
    return lax.ppermute(block, ("dom", "depth"), route)


def from_behind(block, axis, distance):
    size = lax.axis_size(axis)
    return lax.ppermute(block, axis, [((i - distance) % size, i) for i in range(size)])


def on_device(
    adjoint_now,
    adjoint_next,
    lame_first,
    shear_modulus,
    density,
    branch_flags,
    weak_slope,
    normal_stress,
    patch_owner,
):
    x_elems, y_elems, z_elems = lame_first.shape
    lanes = y_elems * z_elems
    assert x_elems == 1 and lanes == adjoint_now.shape[3]
    steps = branch_flags.shape[0]
    pair = lax.axis_size("depth") == 2
    own_table, far_table, edge_table, touch_table = (jnp.asarray(t) for t in stiffness_tables())
    back = jnp.asarray(back_table(y_elems, z_elems))
    mass = jnp.asarray(mass_table(y_elems, z_elems))
    now = jnp.transpose(adjoint_now, (0, 2, 1, 3))
    following = jnp.transpose(adjoint_next, (0, 2, 1, 3))
    rho = jnp.transpose(density, (1, 0, 2))
    flags = branch_flags[:, 0]
    native = pltpu.VMEM((y_elems, 4 * BLOCK, lanes), jnp.float32)
    field = (4 * PLANE, lanes)
    plane = (4 * BLOCK, lanes)
    parts = [(rows, lanes) for rows in PARTS]

    def exchange(even, odd, fault_rows):
        if pair:
            faults = [from_behind(fault_rows, "depth", 1)]
        else:
            faults = [from_behind(fault_rows, "depth", 1), from_behind(fault_rows, "depth", -1)]
        return [swapped(part, 1, 0) for part in even], swapped(odd, 1, 1), faults

    later_used = (
        edge_table, following, rho, mass, own_table, far_table, touch_table, back, flags,
        normal_stress[0], patch_owner,
    )
    assert len(later_used) == LATER
    first_out = kernel_call(
        first_kernel,
        [field] + parts + [plane, (FAULT + 4 * steps, lanes), (8, lanes)]
        + [(t.shape, t.dtype) for t in later_used],
        (now, flags, weak_slope[0], lame_first[0], shear_modulus[0]) + later_used,
        scratch=[native],
        in_hbm=range(5 + LATER),
        kept=range(5, 5 + LATER),
    )
    cur, *even, odd, fault_rows, material = first_out[:-LATER]
    edge_table, following, rho, mass, own_table, far_table, touch_table, back = first_out[-LATER:-3]
    flags, stress, owner = first_out[-3:]
    even_in, odd_in, fault_in = exchange(even, odd, fault_rows)
    first_fault, first_in = fault_rows, fault_in
    fol, minv = kernel_call(
        setup_kernel,
        [field, field],
        (following, rho, mass),
        scratch=[pltpu.VMEM((2, y_elems, 4 * BLOCK, lanes), jnp.float32)],
        y_elems=y_elems,
        z_elems=z_elems,
    )
    seen = []
    for step in range(steps):
        last = step == steps - 1
        seen += [fault_rows] + fault_in
        base, touch = kernel_call(
            prepare_kernel,
            [field, (2 * PLANE, lanes)],
            [cur, material, own_table, touch_table],
            (),
        )
        args = [cur, fol, minv, base, touch, material, odd_in] + fault_in + even_in
        args += [first_in[0], fault_rows, first_fault, far_table, edge_table]
        static = dict(
            step=step, last=last, extra=1 if last or step == 1 else 0, last_place=lax.axis_size("dom") - 1, pair=pair, y_elems=y_elems,
            z_elems=z_elems,
        )
        if step == 1:
            mask, weight = kernel_call(
                mask_kernel,
                [(4 * PATCH_ROWS, lanes), (4 * steps, lanes)],
                [owner, flags, stress, cur],
                unread=(3,),
                z_elems=z_elems,
            )
            args.append(mask)
        if not last:
            new, odd, new_fault = kernel_call(
                step_kernel,
                [field, plane, (SENT_FAULT, lanes)],
                args,
                unread=(len(args) - 1,) if step == 1 else (),
                **static,
            )
            fol, cur, fault_rows = cur, new, new_fault
            even = kernel_call(
                on_chip_kernel,
                parts,
                [cur, material, edge_table],
                scratch=[pltpu.VMEM(plane, jnp.float32)],
                z_elems=z_elems,
            )
            even_in, odd_in, fault_in = exchange(even, odd, fault_rows)
        else:
            whole = (3, 4 * y_elems + 1, 4, lanes)
            known = seen[: len(seen) - len(fault_in)]
            later, grad, table = kernel_call(
                output_kernel,
                [whole, (4, lanes), ((lanes, lanes), jnp.bfloat16)],
                [cur, back, weight] + known,
                scratch=[native],
                stay=True,
                pair=pair,
                steps=steps,
                y_elems=y_elems,
                z_elems=z_elems,
            )
            sums = kernel_call(
                patch_kernel,
                [(PATCH_DEV, lanes)] * 5,
                [mask, weight, grad, table, odd_in] + fault_in + even_in + [touch],
                unread=(4,) + tuple(range(5 + len(fault_in), 9 + len(fault_in))),
                pair=pair,
                steps=steps,
            )
            shares = [sums[0]]
            for i, distance, group in ((3, 2, 0), (2, 1, 1), (4, 2, 1), (1, 1, 0)):
                shares.append(swapped(sums[i], distance, group))
            patch_sums = kernel_call(sum_kernel, [(PATCH_DEV, lanes)], shares)[0]
            earlier, later = kernel_call(
                step_kernel,
                [whole, whole],
                args + [sums[0], later, back],
                scratch=[
                    native, pltpu.VMEM(whole, jnp.float32), pltpu.SemaphoreType.DMA((4,)),
                ],
                unread=(len(args),),
                out_spec=HBM,
                **static,
            )
    return (
        jnp.transpose(earlier, (0, 2, 1, 3)),
        jnp.transpose(later, (0, 2, 1, 3)),
        patch_sums[None],
    )


def solution(mesh):
    return jax.shard_map(
        on_device,
        mesh=mesh,
        in_specs=(
            P(None, "dom", "depth", None),
            P(None, "dom", "depth", None),
            P("dom", "depth", None),
            P("dom", "depth", None),
            P("dom", "depth", None),
            P(None, "depth", "dom", None),
            P("depth", "dom", None),
            P("depth", "dom", None),
            P("depth", "dom"),
        ),
        out_specs=(
            P(None, "dom", "depth", None),
            P(None, "dom", "depth", None),
            P("depth", "dom", None),
        ),
        check_vma=False,
    )
```

```python
import functools
import math

import jax
import jax.numpy as jnp
import ml_dtypes
import numpy as np
from jax import lax
from jax.experimental import pallas as pl
from jax.experimental.pallas import tpu as pltpu
from jax.sharding import PartitionSpec as P

PATCH_DEV = 2
REACH = 2
PATCH_ROWS = 16
LATER = 11
FAULT = 24
SENT_FAULT = 28
PARTS = (24, 24, 16)

time_step = 0.01
lock_stiffness = 0.5

BLOCK = 16
ROWS = ((0, 1, 2), (3, 4, 5), (11, 12, 13), (6, 7, 14), (8, 9, 10))
PLANE = 5 * BLOCK


def basis_tables():
    points = [-1.0, -math.sqrt(3.0 / 7.0), 0.0, math.sqrt(3.0 / 7.0), 1.0]
    quad_weights = np.array([0.1, 49.0 / 90.0, 32.0 / 45.0, 49.0 / 90.0, 0.1])
    products = []
    for first in range(5):
        value = 1.0
        for other in range(5):
            if other != first:
                value = value * (points[first] - points[other])
        products.append(value)
    derivative = np.zeros((5, 5))
    for row in range(5):
        for column in range(5):
            if row == column:
                total = 0.0
                for other in range(5):
                    if other != row:
                        total = total + 1.0 / (points[row] - points[other])
                derivative[row, column] = total
            else:
                derivative[row, column] = (
                    products[row] / products[column] / (points[row] - points[column])
                )
    return (quad_weights, derivative)


def two_parts(table):
    high = table.astype(ml_dtypes.bfloat16)
    low = (table - high.astype(np.float64)).astype(ml_dtypes.bfloat16)
    return np.stack([high, low])


def element_stiffness():
    weights, derivative = basis_tables()
    eye = np.eye(5)
    slope = 2.0 * derivative
    grads = [
        np.kron(slope, np.kron(eye, eye)),
        np.kron(eye, np.kron(eye, slope)),
        np.kron(eye, np.kron(slope, eye)),
    ]
    quad = np.kron(weights, np.kron(weights, weights)) / 8.0
    first = np.zeros((125, 3, 125, 3))
    second = np.zeros((125, 3, 125, 3))
    lap = sum(g.T @ (quad[:, None] * g) for g in grads)
    for c in range(3):
        second[:, c, :, c] += lap
        for d in range(3):
            first[:, c, :, d] += grads[c].T @ (quad[:, None] * grads[d])
            second[:, c, :, d] += grads[d].T @ (quad[:, None] * grads[c])
    where = [
        node // 5 * BLOCK + ROWS[node % 5][c] for node in range(125) for c in range(3)
    ]
    wide = []
    for small in (first, second):
        big = np.zeros((5 * PLANE, 5 * PLANE))
        big[np.ix_(where, where)] = small.reshape(375, 375)
        wide.append(big)
    return wide


OWN_COLS = 384


def padded_table(table, columns):
    return np.pad(table, ((0, 0), (0, columns - table.shape[1])))


@functools.cache
def stiffness_tables():
    wide = element_stiffness()
    own = 4 * PLANE
    planes = [slice(x * PLANE, (x + 1) * PLANE) for x in range(5)]
    inner = np.concatenate([w[:own, :own] for w in wide])

    def three(table):
        high, low = two_parts(table)
        return padded_table(np.concatenate([high, low, high], axis=1), 256)

    def both(rows, columns):
        return three(np.concatenate([w[rows, columns] for w in wide]))

    return (
        two_parts(padded_table(inner, OWN_COLS)),
        np.concatenate([three(w[:own, planes[4]]) for w in wide], axis=1),
        np.concatenate([both(planes[4], planes[x]) for x in range(4)], axis=1),
        both(planes[4], planes[4]),
    )


@functools.cache
def back_table(y_elems, z_elems):
    lanes = y_elems * z_elems
    depth = 4 * z_elems
    back = np.zeros((4 * lanes, y_elems * depth), ml_dtypes.bfloat16)
    for yel in range(y_elems):
        for k in range(z_elems):
            for zl in range(4):
                back[zl * lanes + yel * z_elems + k, yel * depth + 4 * k + zl] = 1
    return back


@functools.cache
def mass_table(y_elems, z_elems):
    weights, _ = basis_tables()
    table = np.zeros((4, 5, BLOCK, y_elems, z_elems))
    for x in range(4):
        mx = 0.2 if x == 0 else weights[x]
        for zl in range(5):
            for yl in range(5):
                for yel in range(y_elems):
                    my = weights[yl]
                    if (yl == 0 and yel > 0) or (yl == 4 and yel < y_elems - 1):
                        my = 0.2
                    mz = np.full(z_elems, weights[zl])
                    if zl == 0:
                        mz[1:] = 0.2
                    if zl == 4:
                        mz[:] = 0.2
                    value = time_step * time_step * 8.0 / (mx * my * mz)
                    if zl == 4:
                        value[-1] = 0.0
                    table[x, zl, list(ROWS[yl]), yel] = value
    return table.reshape(4 * PLANE, y_elems * z_elems).astype(np.float32)


def pieces(value, count):
    out = []
    for _ in range(count):
        piece = value.astype(jnp.bfloat16)
        out.append(piece)
        value = value - piece.astype(jnp.float32)
    return out


def dot(a, b):
    return jnp.dot(a, b, preferred_element_type=jnp.float32)


def exact_dot(value, table, count=3):
    rows = value.shape[0]
    result = dot(jnp.concatenate(pieces(value, count), axis=0), table)
    total = result[:rows]
    for i in range(1, count):
        total = total + result[i * rows : (i + 1) * rows]
    return total


def split_dot(table_high, table_low, value):
    lanes = value.shape[1]
    high, low = pieces(value, 2)
    wide = dot(table_high, jnp.concatenate([high, low], axis=1))
    return wide[:, :lanes] + (wide[:, lanes:] + dot(table_low, high))


def over(value, size):
    if size & (size - 1) == 0:
        return lax.shift_right_logical(value, np.int32(size.bit_length() - 1))
    return lax.div(value, np.int32(size))


def within(value, size):
    return value & (size - 1) if size & (size - 1) == 0 else lax.rem(value, np.int32(size))


def ones_where(shape, axis, wanted):
    line = (shape[0], 1) if axis == 0 else (1, shape[1])
    target = wanted(lax.broadcasted_iota(jnp.int32, line, axis))
    number = lax.broadcasted_iota(jnp.int32, shape, 1 - axis)
    return jnp.where(number == target, 1.0, 0.0).astype(jnp.bfloat16)


def gather_table(lanes, z_elems):
    return ones_where(
        (lanes, 5 * lanes), 1, lambda c: 4 * within(c, z_elems) + over(c, lanes)
    )


def fault_table(lanes, z_elems):
    return ones_where((lanes, lanes), 1, lambda c: 4 * within(c, z_elems) + over(c, z_elems))


def fault_table_back(lanes, z_elems):
    return ones_where((lanes, lanes), 0, lambda c: 4 * within(c, z_elems) + over(c, z_elems))


def stacked(value):
    high, low = pieces(value, 2)
    gap = jnp.zeros((256 - 3 * value.shape[0], value.shape[1]), jnp.bfloat16)
    return jnp.concatenate([high, high, low, gap], axis=0)


def to_elements(native, scratch, table, y_elems, parts=3):
    group = 4 * BLOCK
    for c in range(3):
        for y in range(4 * y_elems + 1):
            rows = native(c, y)
            if y < 4 * y_elems:
                scratch[y // 4, pl.ds(ROWS[y % 4][c], 4, stride=BLOCK), :] = rows
            if y % 4 == 0 and y > 0:
                scratch[y // 4 - 1, pl.ds(ROWS[4][c], 4, stride=BLOCK), :] = rows
    high, middle, *low = pieces(
        jnp.concatenate([scratch[i] for i in range(y_elems)], axis=0), parts
    )
    result = dot(
        jnp.concatenate([high, middle], axis=1), jnp.concatenate([table, table], axis=0)
    )
    for piece in low:
        result = result + dot(piece, table)
    lanes = result.shape[1] // 5
    across = lax.broadcasted_iota(jnp.int32, (1, result.shape[1]), 1)
    across = over(within(across, lanes), lanes // y_elems)
    total = result[:group]
    for yel in range(1, y_elems):
        total = jnp.where(across == yel, result[yel * group : (yel + 1) * group], total)
    blocks = []
    for x in range(4):
        for zl in range(5):
            blocks.append(total[x * BLOCK : (x + 1) * BLOCK, zl * lanes : (zl + 1) * lanes])
    return jnp.concatenate(blocks, axis=0)


def from_elements(field, scratch, back_ref, out_ref, y_elems, stored=None):
    rows = []
    for x in range(4):
        rows.append(
            jnp.concatenate(
                [field[x * PLANE + zl * BLOCK : x * PLANE + (zl + 1) * BLOCK] for zl in range(4)],
                axis=1,
            )
        )
    result = exact_dot(jnp.concatenate(rows, axis=0), back_ref[...])
    depth = result.shape[1] // y_elems
    for yel in range(y_elems):
        scratch[yel] = result[:, yel * depth : (yel + 1) * depth]
    for c in range(3):
        for y in range(4 * y_elems + 1):
            yel, yl = (y // 4, y % 4) if y < 4 * y_elems else (y_elems - 1, 4)
            out_ref[c, y] = scratch[yel, pl.ds(ROWS[yl][c], 4, stride=BLOCK), :]
        if stored is not None:
            stored(c)


def shifted(rows, lanes):
    lanes = lanes % rows.shape[1]
    return pltpu.roll(rows, lanes, 1) if lanes else rows


def block_iotas(lanes):
    return (
        lax.broadcasted_iota(jnp.int32, (8, lanes), 0),
        lax.broadcasted_iota(jnp.int32, (8, lanes), 1),
    )


def store_fault(out_ref, x, plane, z_elems):
    lanes = plane.shape[1]
    _, lane = block_iotas(lanes)
    first = last = jnp.zeros((8, lanes), jnp.float32)
    for zl in range(4):
        at = zl * BLOCK
        here = over(lane, z_elems) == zl
        first = jnp.where(here, shifted(plane[at : at + 8], zl * z_elems), first)
        last = jnp.where(here, shifted(plane[at + 8 : at + 16], (zl + 1) * z_elems), last)
    out_ref[pl.ds(x, 3, stride=8), :] = last[:3]
    out_ref[pl.ds(4 + x, 3, stride=8), :] = first[:3]


def material_rows(lame_ref, shear_ref):
    y_elems, z_elems = lame_ref.shape
    both = jnp.concatenate([lame_ref[...], shear_ref[...]], axis=0)
    spread = ones_where((z_elems, y_elems * z_elems), 1, lambda c: within(c, z_elems))
    tiled = exact_dot(both, spread)
    row = lax.broadcasted_iota(jnp.int32, tiled.shape, 0)
    lane = lax.broadcasted_iota(jnp.int32, tiled.shape, 1)
    kept = jnp.where(within(row, y_elems) == over(lane, z_elems), tiled, 0.0)
    return (
        jnp.sum(kept[:y_elems], axis=0, keepdims=True),
        jnp.sum(kept[y_elems:], axis=0, keepdims=True),
    )


def above_lanes(lanes, z_elems):
    return within(lax.broadcasted_iota(jnp.int32, (BLOCK, lanes), 1), z_elems) != 0


def edge_message(result, lame_row, shear_row, z_elems):
    lanes = result.shape[1]
    force = lame_row * result[:PLANE] + shear_row * result[PLANE:]
    top = force[:BLOCK] + jnp.where(
        above_lanes(lanes, z_elems), pltpu.roll(force[4 * BLOCK :], 1, 1), 0.0
    )
    row = lax.broadcasted_iota(jnp.int32, top.shape, 0)
    top = jnp.where(row == BLOCK - 1, lame_row, top)
    second = jnp.where(row == BLOCK - 1, shear_row, force[BLOCK : 2 * BLOCK])
    return jnp.concatenate([top, second, force[2 * BLOCK : 4 * BLOCK]], axis=0)


def edge_of(field_ref, edge_ref, material_ref, z_elems):
    planes = [stacked(field_ref[x * PLANE : (x + 1) * PLANE]) for x in range(4)]
    edge = dot(edge_ref[...], jnp.concatenate(planes, axis=0))
    return edge_message(edge, material_ref[0:1], material_ref[1:2], z_elems)


def own_force(own_ref, cur, lame_row, shear_row):
    rows, lanes = cur.shape
    padded = jnp.concatenate([cur, jnp.zeros((OWN_COLS - rows, lanes), jnp.float32)], axis=0)
    result = split_dot(own_ref[0], own_ref[1], padded)
    return lame_row * result[:rows] + shear_row * result[rows:]


def start_copies(pairs, sems):
    copies = [
        pltpu.make_async_copy(source, target, sems.at[i])
        for i, (source, target) in enumerate(pairs)
    ]
    for copy in copies:
        copy.start()
    return copies


def first_kernel(
    now_hbm,
    flags_hbm,
    weak_hbm,
    lame_hbm,
    shear_hbm,
    *refs,
):
    later_hbm, refs = refs[:LATER], refs[LATER:]
    cur_ref, odd_ref, fault_out_ref, material_ref = refs[:4]
    later_refs, refs = refs[4 : 4 + LATER], refs[4 + LATER :]
    scratch, now_ref, flags_ref, weak_ref, lame_ref, shear_ref, sems = refs
    copies = start_copies(
        [
            (now_hbm, now_ref),
            (lame_hbm, lame_ref),
            (shear_hbm, shear_ref),
            (flags_hbm, flags_ref),
            (weak_hbm, weak_ref),
            (later_hbm[0], later_refs[0]),
        ]
        + list(zip(later_hbm[1:], later_refs[1:])),
        sems,
    )
    edge_ref = later_refs[0]
    y_elems, z_elems = lame_ref.shape
    lanes = y_elems * z_elems
    gather = gather_table(lanes, z_elems)
    fault = fault_table(lanes, z_elems)
    scratch[...] = jnp.zeros_like(scratch)
    for copy in copies[1:5]:
        copy.wait()
    lame_row, shear_row = material_rows(lame_ref, shear_ref)
    material_ref[...] = jnp.concatenate(
        [lame_row, shear_row, jnp.zeros((6, lanes), jnp.float32)], axis=0
    )
    weak = weak_ref[...]
    tangent = []
    for i in range(flags_ref.shape[0]):
        flag = flags_ref[i]
        tangent.append(
            jnp.where(flag == 0, lock_stiffness, jnp.where(flag == 1, -weak, 0.0))
        )
    fault_out_ref[FAULT:] = exact_dot(jnp.concatenate(tangent, axis=0), fault)
    copies[0].wait()
    cur = to_elements(lambda c, y: now_ref[c, y], scratch, gather, y_elems)
    cur_ref[...] = cur
    planes = [cur[x * PLANE : (x + 1) * PLANE] for x in range(4)]
    for x in range(4):
        store_fault(fault_out_ref, x, planes[x], z_elems)
    odd_ref[...] = cur[: 4 * BLOCK]
    copies[5].wait()

    @pl.when(lax.axis_index("dom") % 2 == 1)
    def _():
        odd_ref[...] = edge_of(cur_ref, edge_ref, material_ref, z_elems)

    for copy in copies[6:]:
        copy.wait()


def prepare_kernel(cur_ref, material_ref, own_ref, touch_ref, base_ref, edge_part_ref):
    cur = cur_ref[...]
    base_ref[...] = own_force(own_ref, cur, material_ref[0:1], material_ref[1:2])
    edge_part_ref[...] = dot(touch_ref[...], stacked(cur[:PLANE]))


def setup_kernel(next_ref, density_ref, mass_ref, fol_ref, minv_ref, scratch, *, y_elems, z_elems):
    gather = gather_table(y_elems * z_elems, z_elems)
    scratch[...] = jnp.zeros_like(scratch)
    fol_ref[...] = to_elements(lambda c, y: next_ref[c, y], scratch.at[0], gather, y_elems)
    density = to_elements(lambda c, y: density_ref[y], scratch.at[1], gather, y_elems, 2)
    table = mass_ref[...]
    first = lax.axis_index("dom") == 0
    plane = lax.broadcasted_iota(jnp.int32, table.shape, 0) < PLANE
    table = jnp.where(jnp.logical_and(first, plane), 2.0 * table, table)
    minv_ref[...] = jnp.where(table > 0.0, table / jnp.where(table > 0.0, density, 1.0), 0.0)


def step_kernel(*refs, step, last, extra, last_place, pair, y_elems, z_elems):
    cur_ref, fol_ref, minv_ref, base_ref, touch_ref, material_ref, odd_ref, up_ref = refs[:8]
    refs = list(refs[8:])
    down_ref = None if pair else refs.pop(0)
    even_in = jnp.concatenate([refs.pop(0)[...] for _ in PARTS], axis=0)
    down_ref = up_ref if pair else down_ref
    first_up_ref, own_ref, first_own_ref, far_ref, edge_ref = refs[:5]
    refs = refs[5 + extra :]
    if last:
        later_ref, back_ref, out_hbm, later_hbm, scratch, out_ref, sems = refs
        copies = start_copies([(later_ref, later_hbm)], sems)
    else:
        new_ref, odd_out, fault_out = refs
    place = lax.axis_index("dom")
    lanes = cur_ref.shape[1]
    even = place % 2 == 0
    far = jnp.where(place == last_place, 0.0, jnp.where(even, even_in, odd_ref[...]))
    left = jnp.where(place == 0, 0.0, jnp.where(even, odd_ref[...], even_in))
    lane_wide = lax.broadcasted_iota(jnp.int32, (BLOCK, lanes), 1)
    below = jnp.where(
        within(lane_wide, z_elems) != z_elems - 1, pltpu.roll(far[:BLOCK], lanes - 1, 1), 0.0
    )
    far = jnp.concatenate([far, below], axis=0)
    lame_row, shear_row = material_ref[0:1], material_ref[1:2]
    far = jnp.concatenate([stacked(lame_row * far), stacked(shear_row * far)], axis=0)
    left_lame = left[BLOCK - 1 : BLOCK]
    left_shear = left[2 * BLOCK - 1 : 2 * BLOCK]
    from_left = left_lame * touch_ref[:PLANE] + left_shear * touch_ref[PLANE:]
    row, lane = block_iotas(lanes)
    across = over(lane, z_elems)
    shared = row < 3
    add_first = jnp.logical_and(shared, across > 0)
    take_last = jnp.logical_and(shared, across < y_elems - 1)
    pull_first = jnp.logical_and(shared, across == 0)
    pull_last = jnp.logical_and(shared, across == y_elems - 1)
    above = above_lanes(lanes, z_elems)
    middle = lax.broadcasted_iota(jnp.int32, (3, lanes), 0) == 1
    gap = jnp.zeros((5, lanes), jnp.float32)
    if not last:
        fault_out[FAULT:] = jnp.zeros_like(fault_out[FAULT:])
    planes = []
    for x in range(4):
        rows = slice(x * PLANE, (x + 1) * PLANE)
        force = base_ref[rows] + dot(far_ref[rows], far)
        blocks = [force[zl * BLOCK : (zl + 1) * BLOCK] for zl in range(5)]
        if x == 0:
            blocks = [b + from_left[i * BLOCK : (i + 1) * BLOCK] for i, b in enumerate(blocks)]
            blocks[:4] = [b + left[i * BLOCK : (i + 1) * BLOCK] for i, b in enumerate(blocks[:4])]
        blocks[0], blocks[4] = (
            blocks[0] + jnp.where(above, pltpu.roll(blocks[4], 1, 1), 0.0),
            blocks[4] + pltpu.roll(blocks[0], lanes - 1, 1),
        )
        lasts, firsts = pl.ds(x, 3, stride=8), pl.ds(4 + x, 3, stride=8)
        k = slice(FAULT + 4 * step + x, FAULT + 4 * step + x + 1)
        below_stiff = jnp.where(middle, lock_stiffness, first_up_ref[k])
        own_stiff = jnp.where(middle, lock_stiffness, first_own_ref[k])
        pulled = jnp.concatenate(
            [below_stiff * (up_ref[lasts, :] - own_ref[firsts, :]), gap], axis=0
        )
        pulled_last = jnp.concatenate(
            [own_stiff * (down_ref[firsts, :] - own_ref[lasts, :]), gap], axis=0
        )
        for zl in range(5):
            low, high = blocks[zl][:8], blocks[zl][8:]
            move = zl * z_elems if zl < 4 else 1
            blocks[zl] = jnp.concatenate(
                [
                    low
                    + jnp.where(add_first, shifted(high, z_elems), 0.0)
                    - jnp.where(pull_first, shifted(pulled, -move), 0.0),
                    high
                    + jnp.where(take_last, shifted(low, -z_elems), 0.0)
                    - jnp.where(pull_last, shifted(pulled_last, -move - z_elems), 0.0),
                ],
                axis=0,
            )
        plane = (2.0 * cur_ref[rows] - fol_ref[rows]) - minv_ref[rows] * jnp.concatenate(
            blocks, axis=0
        )
        if last:
            planes.append(plane)
        else:
            new_ref[rows] = plane
            store_fault(fault_out, x, plane, z_elems)
            if x == 0:
                first = plane[: 4 * BLOCK]
    if last:

        def send(c):
            copy = pltpu.make_async_copy(out_ref.at[c], out_hbm.at[c], sems.at[1 + c])
            copy.start()
            copies.append(copy)

        from_elements(
            jnp.concatenate(planes, axis=0), scratch, back_ref, out_ref, y_elems, send
        )
        for copy in copies:
            copy.wait()
    else:
        odd_out[...] = first

        @pl.when(jnp.logical_not(even))
        def _():
            odd_out[...] = edge_of(new_ref, edge_ref, material_ref, z_elems)


def on_chip_kernel(cur_ref, material_ref, edge_ref, *even_outs, z_elems):
    message = even_outs[-1]
    even_outs = even_outs[:-1]
    message[...] = cur_ref[: 4 * BLOCK]

    @pl.when(lax.axis_index("dom") % 2 == 0)
    def _():
        message[...] = edge_of(cur_ref, edge_ref, material_ref, z_elems)

    for even_out, at in zip(even_outs, (0, PARTS[0], PARTS[0] + PARTS[1])):
        even_out[...] = message[at : at + even_out.shape[0]]


def mask_kernel(owner_ref, flags_ref, stress_ref, _, mask_ref, weight_ref, *, z_elems):
    shape = (PATCH_ROWS, mask_ref.shape[1])
    first = (lax.axis_index("dom") - REACH) * PATCH_DEV
    number = lax.broadcasted_iota(jnp.int32, shape, 0) + first
    for x in range(4):
        mask = jnp.where(number == owner_ref[:, x : x + 1], 1.0, 0.0)
        mask_ref[PATCH_ROWS * x : PATCH_ROWS * (x + 1)] = mask
    stress = stress_ref[...]
    weights = []
    for i in range(flags_ref.shape[0]):
        flag = flags_ref[i]
        weights.append(
            stress * jnp.where(flag == 1, 0.5, jnp.where(flag == 2, 1.0, 0.0))
        )
    fault = fault_table(mask_ref.shape[1], z_elems)
    weight_ref[...] = exact_dot(jnp.concatenate(weights, axis=0), fault)


def output_kernel(*refs, pair, steps, y_elems, z_elems):
    field_ref, back_ref, weight_ref = refs[:3]
    out_ref, grad_ref, table_ref, scratch = refs[-4:]
    messages = refs[3:-4]
    count = 2 if pair else 3
    grad = 0.0
    for i in range(steps):
        group = messages[count * i : count * (i + 1)]
        slip = -group[0][:4]
        if i < steps - 1:
            slip = slip + group[-1][4:8]
        grad = grad + slip * weight_ref[4 * i : 4 * i + 4]
    grad_ref[...] = grad
    table_ref[...] = fault_table_back(weight_ref.shape[1], z_elems)
    from_elements(field_ref[...], scratch, back_ref, out_ref, y_elems)


def patch_kernel(*refs, pair, steps):
    mask_ref, weight_ref, grad_ref, table_ref, _ = refs[:5]
    first_ref = refs[5] if pair else refs[6]
    home_out, out_a, out_b, out_c, out_d = refs[-5:]
    place = lax.axis_index("dom")
    grad = grad_ref[...] + first_ref[4:8] * weight_ref[4 * (steps - 1) : 4 * steps]
    total = 0.0
    for x in range(4):
        total = total + mask_ref[PATCH_ROWS * x : PATCH_ROWS * (x + 1)] * grad[x : x + 1]
    total = exact_dot(total, table_ref[...])
    rows = [total[2 * i : 2 * i + 2] for i in range(5)]
    home_out[...] = rows[2]
    even = place % 2 == 0
    out_a[...] = jnp.where(even, rows[3], rows[1])
    out_b[...] = jnp.where(even, rows[1], rows[3])
    low = place % 4 < 2
    out_c[...] = jnp.where(low, rows[4], rows[0])
    out_d[...] = jnp.where(low, rows[0], rows[4])


def sum_kernel(*refs):
    refs[-1][...] = sum(ref[...] for ref in refs[:-1])


VMEM = pl.BlockSpec(memory_space=pltpu.VMEM)
HBM = pl.BlockSpec(memory_space=pltpu.HBM)
SMEM = pl.BlockSpec(memory_space=pltpu.SMEM)
ANY = pl.BlockSpec(memory_space=pl.ANY)


def kernel_call(body, outs, args, in_smem=(), scratch=(), in_hbm=(), kept=(), unread=(), stay=False, out_spec=VMEM, **static):
    shapes = []
    for out in outs:
        shape, dtype = out if isinstance(out[0], tuple) else (out, jnp.float32)
        shapes.append((pltpu.VMEM if in_hbm or stay else jax.ShapeDtypeStruct)(shape, dtype))
    specs = [VMEM] * len(args)
    for places, spec in ((in_smem, SMEM), (in_hbm, HBM), (unread, ANY)):
        for i in places:
            specs[i] = spec
    copied = [pltpu.VMEM(args[i].shape, args[i].dtype) for i in in_hbm if i not in kept]
    if in_hbm:
        copied.append(pltpu.SemaphoreType.DMA((len(in_hbm),)))
    return pl.pallas_call(
        functools.partial(body, **static) if static else body,
        out_shape=shapes,
        in_specs=specs,
        out_specs=[out_spec] * len(shapes),
        scratch_shapes=list(scratch) + copied,
        compiler_params=pltpu.CompilerParams(
            vmem_limit_bytes=(56 if in_hbm else 24) * 2**20
        ),
    )(*args)


def swapped(block, distance, group):
    size, across = lax.axis_size("dom"), lax.axis_size("depth")
    partner = {}
    for left in range(size - distance):
        if left // distance % 2 == group:
            partner[left], partner[left + distance] = left + distance, left
    route = []
    for i in range(size):
        for j in range(across):
            other, side = partner.get(i, i), j
            if i not in partner and i ^ 1 < size and i ^ 1 not in partner:
                other = i ^ 1
            elif i not in partner:
                side = min(j ^ 1, across - 1)
            route.append((i * across + j, other * across + side))
    return lax.ppermute(block, ("dom", "depth"), route)


def from_behind(block, axis, distance):
    size = lax.axis_size(axis)
    return lax.ppermute(block, axis, [((i - distance) % size, i) for i in range(size)])


def on_device(
    adjoint_now,
    adjoint_next,
    lame_first,
    shear_modulus,
    density,
    branch_flags,
    weak_slope,
    normal_stress,
    patch_owner,
):
    x_elems, y_elems, z_elems = lame_first.shape
    lanes = y_elems * z_elems
    assert x_elems == 1 and lanes == adjoint_now.shape[3]
    steps = branch_flags.shape[0]
    pair = lax.axis_size("depth") == 2
    own_table, far_table, edge_table, touch_table = (jnp.asarray(t) for t in stiffness_tables())
    back = jnp.asarray(back_table(y_elems, z_elems))
    mass = jnp.asarray(mass_table(y_elems, z_elems))
    now = jnp.transpose(adjoint_now, (0, 2, 1, 3))
    following = jnp.transpose(adjoint_next, (0, 2, 1, 3))
    rho = jnp.transpose(density, (1, 0, 2))
    flags = branch_flags[:, 0]
    native = pltpu.VMEM((y_elems, 4 * BLOCK, lanes), jnp.float32)
    field = (4 * PLANE, lanes)
    plane = (4 * BLOCK, lanes)
    parts = [(rows, lanes) for rows in PARTS]

    def exchange(even, odd, fault_rows):
        if pair:
            faults = [from_behind(fault_rows, "depth", 1)]
        else:
            faults = [from_behind(fault_rows, "depth", 1), from_behind(fault_rows, "depth", -1)]
        return [swapped(part, 1, 0) for part in even], swapped(odd, 1, 1), faults

    later_used = (
        edge_table, following, rho, mass, own_table, far_table, touch_table, back, flags,
        normal_stress[0], patch_owner,
    )
    assert len(later_used) == LATER
    first_out = kernel_call(
        first_kernel,
        [field, plane, (FAULT + 4 * steps, lanes), (8, lanes)]
        + [(t.shape, t.dtype) for t in later_used],
        (now, flags, weak_slope[0], lame_first[0], shear_modulus[0]) + later_used,
        scratch=[native],
        in_hbm=range(5 + LATER),
        kept=range(5, 5 + LATER),
    )
    cur, odd, fault_rows, material = first_out[:-LATER]
    edge_table, following, rho, mass, own_table, far_table, touch_table, back = first_out[-LATER:-3]
    flags, stress, owner = first_out[-3:]

    def on_chip(field):
        return kernel_call(
            on_chip_kernel,
            parts,
            [field, material, edge_table],
            scratch=[pltpu.VMEM(plane, jnp.float32)],
            z_elems=z_elems,
        )

    even_in, odd_in, fault_in = exchange(on_chip(cur), odd, fault_rows)
    first_fault, first_in = fault_rows, fault_in
    fol, minv = kernel_call(
        setup_kernel,
        [field, field],
        (following, rho, mass),
        scratch=[pltpu.VMEM((2, y_elems, 4 * BLOCK, lanes), jnp.float32)],
        y_elems=y_elems,
        z_elems=z_elems,
    )
    seen = []
    for step in range(steps):
        last = step == steps - 1
        seen += [fault_rows] + fault_in
        base, touch = kernel_call(
            prepare_kernel,
            [field, (2 * PLANE, lanes)],
            [cur, material, own_table, touch_table],
            (),
        )
        args = [cur, fol, minv, base, touch, material, odd_in] + fault_in + even_in
        args += [first_in[0], fault_rows, first_fault, far_table, edge_table]
        static = dict(
            step=step, last=last, extra=1 if last or step == 1 else 0, last_place=lax.axis_size("dom") - 1, pair=pair, y_elems=y_elems,
            z_elems=z_elems,
        )
        if step == 1:
            mask, weight = kernel_call(
                mask_kernel,
                [(4 * PATCH_ROWS, lanes), (4 * steps, lanes)],
                [owner, flags, stress, cur],
                unread=(3,),
                z_elems=z_elems,
            )
            args.append(mask)
        if not last:
            new, odd, new_fault = kernel_call(
                step_kernel,
                [field, plane, (SENT_FAULT, lanes)],
                args,
                unread=(len(args) - 1,) if step == 1 else (),
                **static,
            )
            fol, cur, fault_rows = cur, new, new_fault
            even_in, odd_in, fault_in = exchange(on_chip(cur), odd, fault_rows)
        else:
            whole = (3, 4 * y_elems + 1, 4, lanes)
            known = seen[: len(seen) - len(fault_in)]
            later, grad, table = kernel_call(
                output_kernel,
                [whole, (4, lanes), ((lanes, lanes), jnp.bfloat16)],
                [cur, back, weight] + known,
                scratch=[native],
                stay=True,
                pair=pair,
                steps=steps,
                y_elems=y_elems,
                z_elems=z_elems,
            )
            sums = kernel_call(
                patch_kernel,
                [(PATCH_DEV, lanes)] * 5,
                [mask, weight, grad, table, odd_in] + fault_in + even_in + [touch],
                unread=(4,) + tuple(range(5 + len(fault_in), 9 + len(fault_in))),
                pair=pair,
                steps=steps,
            )
            shares = [sums[0]]
            for i, distance, group in ((3, 2, 0), (2, 1, 1), (4, 2, 1), (1, 1, 0)):
                shares.append(swapped(sums[i], distance, group))
            patch_sums = kernel_call(sum_kernel, [(PATCH_DEV, lanes)], shares)[0]
            earlier, later = kernel_call(
                step_kernel,
                [whole, whole],
                args + [sums[0], later, back],
                scratch=[
                    native, pltpu.VMEM(whole, jnp.float32), pltpu.SemaphoreType.DMA((4,)),
                ],
                unread=(len(args),),
                out_spec=HBM,
                **static,
            )
    return (
        jnp.transpose(earlier, (0, 2, 1, 3)),
        jnp.transpose(later, (0, 2, 1, 3)),
        patch_sums[None],
    )


def solution(mesh):
    return jax.shard_map(
        on_device,
        mesh=mesh,
        in_specs=(
            P(None, "dom", "depth", None),
            P(None, "dom", "depth", None),
            P("dom", "depth", None),
            P("dom", "depth", None),
            P("dom", "depth", None),
            P(None, "depth", "dom", None),
            P("depth", "dom", None),
            P("depth", "dom", None),
            P("depth", "dom"),
        ),
        out_specs=(
            P(None, "dom", "depth", None),
            P(None, "dom", "depth", None),
            P("depth", "dom", None),
        ),
        check_vma=False,
    )
```

```python
import functools
import math

import jax
import jax.numpy as jnp
import ml_dtypes
import numpy as np
from jax import lax
from jax.experimental import pallas as pl
from jax.experimental.pallas import tpu as pltpu
from jax.sharding import PartitionSpec as P

PATCH_DEV = 2
REACH = 2
PATCH_ROWS = 16
LATER = 10
FAULT = 24
SENT_FAULT = 28
PARTS = (24, 24, 16)

time_step = 0.01
lock_stiffness = 0.5

BLOCK = 16
ROWS = ((0, 1, 2), (3, 4, 5), (11, 12, 13), (6, 7, 14), (8, 9, 10))
PLANE = 5 * BLOCK


def basis_tables():
    points = [-1.0, -math.sqrt(3.0 / 7.0), 0.0, math.sqrt(3.0 / 7.0), 1.0]
    quad_weights = np.array([0.1, 49.0 / 90.0, 32.0 / 45.0, 49.0 / 90.0, 0.1])
    products = []
    for first in range(5):
        value = 1.0
        for other in range(5):
            if other != first:
                value = value * (points[first] - points[other])
        products.append(value)
    derivative = np.zeros((5, 5))
    for row in range(5):
        for column in range(5):
            if row == column:
                total = 0.0
                for other in range(5):
                    if other != row:
                        total = total + 1.0 / (points[row] - points[other])
                derivative[row, column] = total
            else:
                derivative[row, column] = (
                    products[row] / products[column] / (points[row] - points[column])
                )
    return (quad_weights, derivative)


def two_parts(table):
    high = table.astype(ml_dtypes.bfloat16)
    low = (table - high.astype(np.float64)).astype(ml_dtypes.bfloat16)
    return np.stack([high, low])


def element_stiffness():
    weights, derivative = basis_tables()
    eye = np.eye(5)
    slope = 2.0 * derivative
    grads = [
        np.kron(slope, np.kron(eye, eye)),
        np.kron(eye, np.kron(eye, slope)),
        np.kron(eye, np.kron(slope, eye)),
    ]
    quad = np.kron(weights, np.kron(weights, weights)) / 8.0
    first = np.zeros((125, 3, 125, 3))
    second = np.zeros((125, 3, 125, 3))
    lap = sum(g.T @ (quad[:, None] * g) for g in grads)
    for c in range(3):
        second[:, c, :, c] += lap
        for d in range(3):
            first[:, c, :, d] += grads[c].T @ (quad[:, None] * grads[d])
            second[:, c, :, d] += grads[d].T @ (quad[:, None] * grads[c])
    where = [
        node // 5 * BLOCK + ROWS[node % 5][c] for node in range(125) for c in range(3)
    ]
    wide = []
    for small in (first, second):
        big = np.zeros((5 * PLANE, 5 * PLANE))
        big[np.ix_(where, where)] = small.reshape(375, 375)
        wide.append(big)
    return wide


OWN_COLS = 384


def padded_table(table, columns):
    return np.pad(table, ((0, 0), (0, columns - table.shape[1])))


@functools.cache
def stiffness_tables():
    wide = element_stiffness()
    own = 4 * PLANE
    planes = [slice(x * PLANE, (x + 1) * PLANE) for x in range(5)]
    inner = np.concatenate([w[:own, :own] for w in wide])

    def three(table):
        high, low = two_parts(table)
        return padded_table(np.concatenate([high, low, high], axis=1), 256)

    def both(rows, columns):
        return three(np.concatenate([w[rows, columns] for w in wide]))

    return (
        two_parts(padded_table(inner, OWN_COLS)),
        np.concatenate([three(w[:own, planes[4]]) for w in wide], axis=1),
        np.concatenate([both(planes[4], planes[x]) for x in range(4)], axis=1),
        both(planes[4], planes[4]),
    )


@functools.cache
def back_table(y_elems, z_elems):
    lanes = y_elems * z_elems
    depth = 4 * z_elems
    back = np.zeros((4 * lanes, y_elems * depth), ml_dtypes.bfloat16)
    for yel in range(y_elems):
        for k in range(z_elems):
            for zl in range(4):
                back[zl * lanes + yel * z_elems + k, yel * depth + 4 * k + zl] = 1
    return back


@functools.cache
def mass_table(y_elems, z_elems):
    weights, _ = basis_tables()
    table = np.zeros((4, 5, BLOCK, y_elems, z_elems))
    for x in range(4):
        mx = 0.2 if x == 0 else weights[x]
        for zl in range(5):
            for yl in range(5):
                for yel in range(y_elems):
                    my = weights[yl]
                    if (yl == 0 and yel > 0) or (yl == 4 and yel < y_elems - 1):
                        my = 0.2
                    mz = np.full(z_elems, weights[zl])
                    if zl == 0:
                        mz[1:] = 0.2
                    if zl == 4:
                        mz[:] = 0.2
                    value = time_step * time_step * 8.0 / (mx * my * mz)
                    if zl == 4:
                        value[-1] = 0.0
                    table[x, zl, list(ROWS[yl]), yel] = value
    return table.reshape(4 * PLANE, y_elems * z_elems).astype(np.float32)


def pieces(value, count):
    out = []
    for _ in range(count):
        piece = value.astype(jnp.bfloat16)
        out.append(piece)
        value = value - piece.astype(jnp.float32)
    return out


def dot(a, b):
    return jnp.dot(a, b, preferred_element_type=jnp.float32)


def exact_dot(value, table, count=3):
    rows = value.shape[0]
    result = dot(jnp.concatenate(pieces(value, count), axis=0), table)
    total = result[:rows]
    for i in range(1, count):
        total = total + result[i * rows : (i + 1) * rows]
    return total


def split_dot(table_high, table_low, value):
    lanes = value.shape[1]
    high, low = pieces(value, 2)
    wide = dot(table_high, jnp.concatenate([high, low], axis=1))
    return wide[:, :lanes] + (wide[:, lanes:] + dot(table_low, high))


def over(value, size):
    if size & (size - 1) == 0:
        return lax.shift_right_logical(value, np.int32(size.bit_length() - 1))
    return lax.div(value, np.int32(size))


def within(value, size):
    return value & (size - 1) if size & (size - 1) == 0 else lax.rem(value, np.int32(size))


def ones_where(shape, axis, wanted):
    line = (shape[0], 1) if axis == 0 else (1, shape[1])
    target = wanted(lax.broadcasted_iota(jnp.int32, line, axis))
    number = lax.broadcasted_iota(jnp.int32, shape, 1 - axis)
    return jnp.where(number == target, 1.0, 0.0).astype(jnp.bfloat16)


def gather_table(lanes, z_elems):
    return ones_where(
        (lanes, 5 * lanes), 1, lambda c: 4 * within(c, z_elems) + over(c, lanes)
    )


def fault_table(lanes, z_elems):
    return ones_where((lanes, lanes), 1, lambda c: 4 * within(c, z_elems) + over(c, z_elems))


def fault_table_back(lanes, z_elems):
    return ones_where((lanes, lanes), 0, lambda c: 4 * within(c, z_elems) + over(c, z_elems))


def stacked(value):
    high, low = pieces(value, 2)
    gap = jnp.zeros((256 - 3 * value.shape[0], value.shape[1]), jnp.bfloat16)
    return jnp.concatenate([high, high, low, gap], axis=0)


def to_elements(native, scratch, table, y_elems, parts=3):
    group = 4 * BLOCK
    for c in range(3):
        for y in range(4 * y_elems + 1):
            rows = native(c, y)
            if y < 4 * y_elems:
                scratch[y // 4, pl.ds(ROWS[y % 4][c], 4, stride=BLOCK), :] = rows
            if y % 4 == 0 and y > 0:
                scratch[y // 4 - 1, pl.ds(ROWS[4][c], 4, stride=BLOCK), :] = rows
    high, middle, *low = pieces(
        jnp.concatenate([scratch[i] for i in range(y_elems)], axis=0), parts
    )
    result = dot(
        jnp.concatenate([high, middle], axis=1), jnp.concatenate([table, table], axis=0)
    )
    for piece in low:
        result = result + dot(piece, table)
    lanes = result.shape[1] // 5
    across = lax.broadcasted_iota(jnp.int32, (1, result.shape[1]), 1)
    across = over(within(across, lanes), lanes // y_elems)
    total = result[:group]
    for yel in range(1, y_elems):
        total = jnp.where(across == yel, result[yel * group : (yel + 1) * group], total)
    blocks = []
    for x in range(4):
        for zl in range(5):
            blocks.append(total[x * BLOCK : (x + 1) * BLOCK, zl * lanes : (zl + 1) * lanes])
    return jnp.concatenate(blocks, axis=0)


def from_elements(field, scratch, back_ref, out_ref, y_elems, stored=None):
    rows = []
    for x in range(4):
        rows.append(
            jnp.concatenate(
                [field[x * PLANE + zl * BLOCK : x * PLANE + (zl + 1) * BLOCK] for zl in range(4)],
                axis=1,
            )
        )
    result = exact_dot(jnp.concatenate(rows, axis=0), back_ref[...])
    depth = result.shape[1] // y_elems
    for yel in range(y_elems):
        scratch[yel] = result[:, yel * depth : (yel + 1) * depth]
    for c in range(3):
        for y in range(4 * y_elems + 1):
            yel, yl = (y // 4, y % 4) if y < 4 * y_elems else (y_elems - 1, 4)
            out_ref[c, y] = scratch[yel, pl.ds(ROWS[yl][c], 4, stride=BLOCK), :]
        if stored is not None:
            stored(c)


def shifted(rows, lanes):
    lanes = lanes % rows.shape[1]
    return pltpu.roll(rows, lanes, 1) if lanes else rows


def block_iotas(lanes):
    return (
        lax.broadcasted_iota(jnp.int32, (8, lanes), 0),
        lax.broadcasted_iota(jnp.int32, (8, lanes), 1),
    )


def store_fault(out_ref, x, plane, z_elems):
    lanes = plane.shape[1]
    _, lane = block_iotas(lanes)
    first = last = jnp.zeros((8, lanes), jnp.float32)
    for zl in range(4):
        at = zl * BLOCK
        here = over(lane, z_elems) == zl
        first = jnp.where(here, shifted(plane[at : at + 8], zl * z_elems), first)
        last = jnp.where(here, shifted(plane[at + 8 : at + 16], (zl + 1) * z_elems), last)
    out_ref[pl.ds(x, 3, stride=8), :] = last[:3]
    out_ref[pl.ds(4 + x, 3, stride=8), :] = first[:3]


def material_rows(lame_ref, shear_ref):
    y_elems, z_elems = lame_ref.shape
    both = jnp.concatenate([lame_ref[...], shear_ref[...]], axis=0)
    spread = ones_where((z_elems, y_elems * z_elems), 1, lambda c: within(c, z_elems))
    tiled = exact_dot(both, spread)
    row = lax.broadcasted_iota(jnp.int32, tiled.shape, 0)
    lane = lax.broadcasted_iota(jnp.int32, tiled.shape, 1)
    kept = jnp.where(within(row, y_elems) == over(lane, z_elems), tiled, 0.0)
    return (
        jnp.sum(kept[:y_elems], axis=0, keepdims=True),
        jnp.sum(kept[y_elems:], axis=0, keepdims=True),
    )


def above_lanes(lanes, z_elems):
    return within(lax.broadcasted_iota(jnp.int32, (BLOCK, lanes), 1), z_elems) != 0


def edge_message(result, lame_row, shear_row, z_elems):
    lanes = result.shape[1]
    force = lame_row * result[:PLANE] + shear_row * result[PLANE:]
    top = force[:BLOCK] + jnp.where(
        above_lanes(lanes, z_elems), pltpu.roll(force[4 * BLOCK :], 1, 1), 0.0
    )
    row = lax.broadcasted_iota(jnp.int32, top.shape, 0)
    top = jnp.where(row == BLOCK - 1, lame_row, top)
    second = jnp.where(row == BLOCK - 1, shear_row, force[BLOCK : 2 * BLOCK])
    return jnp.concatenate([top, second, force[2 * BLOCK : 4 * BLOCK]], axis=0)


def edge_of(field_ref, edge_ref, material_ref, z_elems):
    planes = [stacked(field_ref[x * PLANE : (x + 1) * PLANE]) for x in range(4)]
    edge = dot(edge_ref[...], jnp.concatenate(planes, axis=0))
    return edge_message(edge, material_ref[0:1], material_ref[1:2], z_elems)


def own_force(own_ref, cur, lame_row, shear_row):
    rows, lanes = cur.shape
    padded = jnp.concatenate([cur, jnp.zeros((OWN_COLS - rows, lanes), jnp.float32)], axis=0)
    result = split_dot(own_ref[0], own_ref[1], padded)
    return lame_row * result[:rows] + shear_row * result[rows:]


def start_copies(pairs, sems):
    copies = [
        pltpu.make_async_copy(source, target, sems.at[i])
        for i, (source, target) in enumerate(pairs)
    ]
    for copy in copies:
        copy.start()
    return copies


def first_kernel(
    now_hbm,
    flags_hbm,
    weak_hbm,
    lame_hbm,
    shear_hbm,
    *refs,
):
    later_hbm, refs = refs[:LATER], refs[LATER:]
    cur_ref, odd_ref, fault_out_ref, material_ref = refs[:4]
    later_refs, refs = refs[4 : 4 + LATER], refs[4 + LATER :]
    scratch, now_ref, flags_ref, weak_ref, lame_ref, shear_ref, sems = refs
    copies = start_copies(
        [
            (now_hbm, now_ref),
            (lame_hbm, lame_ref),
            (shear_hbm, shear_ref),
            (flags_hbm, flags_ref),
            (weak_hbm, weak_ref),
            (later_hbm[0], later_refs[0]),
        ]
        + list(zip(later_hbm[1:], later_refs[1:])),
        sems,
    )
    edge_ref = later_refs[0]
    y_elems, z_elems = lame_ref.shape
    lanes = y_elems * z_elems
    gather = gather_table(lanes, z_elems)
    fault = fault_table(lanes, z_elems)
    scratch[...] = jnp.zeros_like(scratch)
    for copy in copies[1:5]:
        copy.wait()
    lame_row, shear_row = material_rows(lame_ref, shear_ref)
    material_ref[...] = jnp.concatenate(
        [lame_row, shear_row, jnp.zeros((6, lanes), jnp.float32)], axis=0
    )
    weak = weak_ref[...]
    tangent = []
    for i in range(flags_ref.shape[0]):
        flag = flags_ref[i]
        tangent.append(
            jnp.where(flag == 0, lock_stiffness, jnp.where(flag == 1, -weak, 0.0))
        )
    fault_out_ref[FAULT:] = exact_dot(jnp.concatenate(tangent, axis=0), fault)
    copies[0].wait()
    cur = to_elements(lambda c, y: now_ref[c, y], scratch, gather, y_elems)
    cur_ref[...] = cur
    planes = [cur[x * PLANE : (x + 1) * PLANE] for x in range(4)]
    for x in range(4):
        store_fault(fault_out_ref, x, planes[x], z_elems)
    odd_ref[...] = cur[: 4 * BLOCK]
    copies[5].wait()

    @pl.when(lax.axis_index("dom") % 2 == 1)
    def _():
        odd_ref[...] = edge_of(cur_ref, edge_ref, material_ref, z_elems)

    for copy in copies[6:]:
        copy.wait()


def prepare_kernel(cur_ref, material_ref, own_ref, touch_ref, base_ref, edge_part_ref):
    cur = cur_ref[...]
    base_ref[...] = own_force(own_ref, cur, material_ref[0:1], material_ref[1:2])
    edge_part_ref[...] = dot(touch_ref[...], stacked(cur[:PLANE]))


def setup_kernel(next_ref, density_ref, mass_ref, fol_ref, minv_ref, scratch, *, y_elems, z_elems):
    gather = gather_table(y_elems * z_elems, z_elems)
    scratch[...] = jnp.zeros_like(scratch)
    fol_ref[...] = to_elements(lambda c, y: next_ref[c, y], scratch.at[0], gather, y_elems)
    density = to_elements(lambda c, y: density_ref[y], scratch.at[1], gather, y_elems, 2)
    table = mass_ref[...]
    first = lax.axis_index("dom") == 0
    plane = lax.broadcasted_iota(jnp.int32, table.shape, 0) < PLANE
    table = jnp.where(jnp.logical_and(first, plane), 2.0 * table, table)
    minv_ref[...] = jnp.where(table > 0.0, table / jnp.where(table > 0.0, density, 1.0), 0.0)


def step_kernel(*refs, step, last, extra, last_place, pair, y_elems, z_elems):
    cur_ref, fol_ref, minv_ref, base_ref, touch_ref, material_ref, odd_ref, up_ref = refs[:8]
    refs = list(refs[8:])
    down_ref = None if pair else refs.pop(0)
    even_in = jnp.concatenate([refs.pop(0)[...] for _ in PARTS], axis=0)
    down_ref = up_ref if pair else down_ref
    first_up_ref, own_ref, first_own_ref, far_ref, edge_ref = refs[:5]
    refs = refs[5 + extra :]
    if last:
        later_ref, back_ref, out_hbm, later_hbm, scratch, out_ref, sems = refs
        copies = start_copies([(later_ref, later_hbm)], sems)
    else:
        new_ref, odd_out, fault_out = refs
    place = lax.axis_index("dom")
    lanes = cur_ref.shape[1]
    even = place % 2 == 0
    far = jnp.where(place == last_place, 0.0, jnp.where(even, even_in, odd_ref[...]))
    left = jnp.where(place == 0, 0.0, jnp.where(even, odd_ref[...], even_in))
    lane_wide = lax.broadcasted_iota(jnp.int32, (BLOCK, lanes), 1)
    below = jnp.where(
        within(lane_wide, z_elems) != z_elems - 1, pltpu.roll(far[:BLOCK], lanes - 1, 1), 0.0
    )
    far = jnp.concatenate([far, below], axis=0)
    lame_row, shear_row = material_ref[0:1], material_ref[1:2]
    far = jnp.concatenate([stacked(lame_row * far), stacked(shear_row * far)], axis=0)
    left_lame = left[BLOCK - 1 : BLOCK]
    left_shear = left[2 * BLOCK - 1 : 2 * BLOCK]
    from_left = left_lame * touch_ref[:PLANE] + left_shear * touch_ref[PLANE:]
    row, lane = block_iotas(lanes)
    across = over(lane, z_elems)
    shared = row < 3
    add_first = jnp.logical_and(shared, across > 0)
    take_last = jnp.logical_and(shared, across < y_elems - 1)
    pull_first = jnp.logical_and(shared, across == 0)
    pull_last = jnp.logical_and(shared, across == y_elems - 1)
    above = above_lanes(lanes, z_elems)
    middle = lax.broadcasted_iota(jnp.int32, (3, lanes), 0) == 1
    gap = jnp.zeros((5, lanes), jnp.float32)
    if not last:
        fault_out[FAULT:] = jnp.zeros_like(fault_out[FAULT:])
    planes = []
    for x in range(4):
        rows = slice(x * PLANE, (x + 1) * PLANE)
        force = base_ref[rows] + dot(far_ref[rows], far)
        blocks = [force[zl * BLOCK : (zl + 1) * BLOCK] for zl in range(5)]
        if x == 0:
            blocks = [b + from_left[i * BLOCK : (i + 1) * BLOCK] for i, b in enumerate(blocks)]
            blocks[:4] = [b + left[i * BLOCK : (i + 1) * BLOCK] for i, b in enumerate(blocks[:4])]
        blocks[0], blocks[4] = (
            blocks[0] + jnp.where(above, pltpu.roll(blocks[4], 1, 1), 0.0),
            blocks[4] + pltpu.roll(blocks[0], lanes - 1, 1),
        )
        lasts, firsts = pl.ds(x, 3, stride=8), pl.ds(4 + x, 3, stride=8)
        k = slice(FAULT + 4 * step + x, FAULT + 4 * step + x + 1)
        below_stiff = jnp.where(middle, lock_stiffness, first_up_ref[k])
        own_stiff = jnp.where(middle, lock_stiffness, first_own_ref[k])
        pulled = jnp.concatenate(
            [below_stiff * (up_ref[lasts, :] - own_ref[firsts, :]), gap], axis=0
        )
        pulled_last = jnp.concatenate(
            [own_stiff * (down_ref[firsts, :] - own_ref[lasts, :]), gap], axis=0
        )
        for zl in range(5):
            low, high = blocks[zl][:8], blocks[zl][8:]
            move = zl * z_elems if zl < 4 else 1
            blocks[zl] = jnp.concatenate(
                [
                    low
                    + jnp.where(add_first, shifted(high, z_elems), 0.0)
                    - jnp.where(pull_first, shifted(pulled, -move), 0.0),
                    high
                    + jnp.where(take_last, shifted(low, -z_elems), 0.0)
                    - jnp.where(pull_last, shifted(pulled_last, -move - z_elems), 0.0),
                ],
                axis=0,
            )
        plane = (2.0 * cur_ref[rows] - fol_ref[rows]) - minv_ref[rows] * jnp.concatenate(
            blocks, axis=0
        )
        if last:
            planes.append(plane)
        else:
            new_ref[rows] = plane
            store_fault(fault_out, x, plane, z_elems)
            if x == 0:
                first = plane[: 4 * BLOCK]
    if last:

        def send(c):
            copy = pltpu.make_async_copy(out_ref.at[c], out_hbm.at[c], sems.at[1 + c])
            copy.start()
            copies.append(copy)

        from_elements(
            jnp.concatenate(planes, axis=0), scratch, back_ref, out_ref, y_elems, send
        )
        for copy in copies:
            copy.wait()
    else:
        odd_out[...] = first

        @pl.when(jnp.logical_not(even))
        def _():
            odd_out[...] = edge_of(new_ref, edge_ref, material_ref, z_elems)


def on_chip_kernel(cur_ref, material_ref, edge_ref, *even_outs, z_elems):
    message = even_outs[-1]
    even_outs = even_outs[:-1]
    message[...] = cur_ref[: 4 * BLOCK]

    @pl.when(lax.axis_index("dom") % 2 == 0)
    def _():
        message[...] = edge_of(cur_ref, edge_ref, material_ref, z_elems)

    for even_out, at in zip(even_outs, (0, PARTS[0], PARTS[0] + PARTS[1])):
        even_out[...] = message[at : at + even_out.shape[0]]


def mask_kernel(owner_ref, flags_ref, stress_ref, _, mask_ref, weight_ref, *, z_elems):
    shape = (PATCH_ROWS, mask_ref.shape[1])
    first = (lax.axis_index("dom") - REACH) * PATCH_DEV
    number = lax.broadcasted_iota(jnp.int32, shape, 0) + first
    for x in range(4):
        mask = jnp.where(number == owner_ref[:, x : x + 1], 1.0, 0.0)
        mask_ref[PATCH_ROWS * x : PATCH_ROWS * (x + 1)] = mask
    stress = stress_ref[...]
    weights = []
    for i in range(flags_ref.shape[0]):
        flag = flags_ref[i]
        weights.append(
            stress * jnp.where(flag == 1, 0.5, jnp.where(flag == 2, 1.0, 0.0))
        )
    fault = fault_table(mask_ref.shape[1], z_elems)
    weight_ref[...] = exact_dot(jnp.concatenate(weights, axis=0), fault)


def output_kernel(*refs, pair, steps, y_elems, z_elems):
    field_ref, back_ref, weight_ref = refs[:3]
    out_ref, grad_ref, table_ref, scratch = refs[-4:]
    messages = refs[3:-4]
    count = 2 if pair else 3
    grad = 0.0
    for i in range(steps):
        group = messages[count * i : count * (i + 1)]
        slip = -group[0][:4]
        if i < steps - 1:
            slip = slip + group[-1][4:8]
        grad = grad + slip * weight_ref[4 * i : 4 * i + 4]
    grad_ref[...] = grad
    table_ref[...] = fault_table_back(weight_ref.shape[1], z_elems)
    from_elements(field_ref[...], scratch, back_ref, out_ref, y_elems)


def patch_kernel(*refs, pair, steps):
    mask_ref, weight_ref, grad_ref, table_ref, _ = refs[:5]
    first_ref = refs[5] if pair else refs[6]
    home_out, out_a, out_b, out_c, out_d = refs[-5:]
    place = lax.axis_index("dom")
    grad = grad_ref[...] + first_ref[4:8] * weight_ref[4 * (steps - 1) : 4 * steps]
    total = 0.0
    for x in range(4):
        total = total + mask_ref[PATCH_ROWS * x : PATCH_ROWS * (x + 1)] * grad[x : x + 1]
    total = exact_dot(total, table_ref[...])
    rows = [total[2 * i : 2 * i + 2] for i in range(5)]
    home_out[...] = rows[2]
    even = place % 2 == 0
    out_a[...] = jnp.where(even, rows[3], rows[1])
    out_b[...] = jnp.where(even, rows[1], rows[3])
    low = place % 4 < 2
    out_c[...] = jnp.where(low, rows[4], rows[0])
    out_d[...] = jnp.where(low, rows[0], rows[4])


def sum_kernel(*refs):
    refs[-1][...] = sum(ref[...] for ref in refs[:-1])


VMEM = pl.BlockSpec(memory_space=pltpu.VMEM)
HBM = pl.BlockSpec(memory_space=pltpu.HBM)
SMEM = pl.BlockSpec(memory_space=pltpu.SMEM)
ANY = pl.BlockSpec(memory_space=pl.ANY)


def kernel_call(body, outs, args, in_smem=(), scratch=(), in_hbm=(), kept=(), unread=(), stay=False, out_spec=VMEM, **static):
    shapes = []
    for out in outs:
        shape, dtype = out if isinstance(out[0], tuple) else (out, jnp.float32)
        shapes.append((pltpu.VMEM if in_hbm or stay else jax.ShapeDtypeStruct)(shape, dtype))
    specs = [VMEM] * len(args)
    for places, spec in ((in_smem, SMEM), (in_hbm, HBM), (unread, ANY)):
        for i in places:
            specs[i] = spec
    copied = [pltpu.VMEM(args[i].shape, args[i].dtype) for i in in_hbm if i not in kept]
    if in_hbm:
        copied.append(pltpu.SemaphoreType.DMA((len(in_hbm),)))
    return pl.pallas_call(
        functools.partial(body, **static) if static else body,
        out_shape=shapes,
        in_specs=specs,
        out_specs=[out_spec] * len(shapes),
        scratch_shapes=list(scratch) + copied,
        compiler_params=pltpu.CompilerParams(
            vmem_limit_bytes=(56 if in_hbm else 24) * 2**20
        ),
    )(*args)


def swapped(block, distance, group):
    size, across = lax.axis_size("dom"), lax.axis_size("depth")
    partner = {}
    for left in range(size - distance):
        if left // distance % 2 == group:
            partner[left], partner[left + distance] = left + distance, left
    route = []
    for i in range(size):
        for j in range(across):
            other, side = partner.get(i, i), j
            if i not in partner and i ^ 1 < size and i ^ 1 not in partner:
                other = i ^ 1
            elif i not in partner:
                side = min(j ^ 1, across - 1)
            route.append((i * across + j, other * across + side))
    return lax.ppermute(block, ("dom", "depth"), route)


def from_behind(block, axis, distance):
    size = lax.axis_size(axis)
    return lax.ppermute(block, axis, [((i - distance) % size, i) for i in range(size)])


def on_device(
    adjoint_now,
    adjoint_next,
    lame_first,
    shear_modulus,
    density,
    branch_flags,
    weak_slope,
    normal_stress,
    patch_owner,
):
    x_elems, y_elems, z_elems = lame_first.shape
    lanes = y_elems * z_elems
    assert x_elems == 1 and lanes == adjoint_now.shape[3]
    steps = branch_flags.shape[0]
    pair = lax.axis_size("depth") == 2
    own_table, far_table, edge_table, touch_table = (jnp.asarray(t) for t in stiffness_tables())
    back = jnp.asarray(back_table(y_elems, z_elems))
    mass = jnp.asarray(mass_table(y_elems, z_elems))
    now = jnp.transpose(adjoint_now, (0, 2, 1, 3))
    following = jnp.transpose(adjoint_next, (0, 2, 1, 3))
    rho = jnp.transpose(density, (1, 0, 2))
    flags = branch_flags[:, 0]
    native = pltpu.VMEM((y_elems, 4 * BLOCK, lanes), jnp.float32)
    field = (4 * PLANE, lanes)
    plane = (4 * BLOCK, lanes)
    parts = [(rows, lanes) for rows in PARTS]

    def exchange(even, odd, fault_rows):
        if pair:
            faults = [from_behind(fault_rows, "depth", 1)]
        else:
            faults = [from_behind(fault_rows, "depth", 1), from_behind(fault_rows, "depth", -1)]
        return [swapped(part, 1, 0) for part in even], swapped(odd, 1, 1), faults

    later_used = (
        edge_table, following, rho, mass, own_table, far_table, touch_table, flags,
        normal_stress[0], patch_owner,
    )
    assert len(later_used) == LATER
    first_out = kernel_call(
        first_kernel,
        [field, plane, (FAULT + 4 * steps, lanes), (8, lanes)]
        + [(t.shape, t.dtype) for t in later_used],
        (now, flags, weak_slope[0], lame_first[0], shear_modulus[0]) + later_used,
        scratch=[native],
        in_hbm=range(5 + LATER),
        kept=range(5, 5 + LATER),
    )
    cur, odd, fault_rows, material = first_out[:-LATER]
    edge_table, following, rho, mass, own_table, far_table, touch_table = first_out[-LATER:-3]
    flags, stress, owner = first_out[-3:]

    def on_chip(field):
        return kernel_call(
            on_chip_kernel,
            parts,
            [field, material, edge_table],
            scratch=[pltpu.VMEM(plane, jnp.float32)],
            z_elems=z_elems,
        )

    even_in, odd_in, fault_in = exchange(on_chip(cur), odd, fault_rows)
    first_fault, first_in = fault_rows, fault_in
    fol, minv = kernel_call(
        setup_kernel,
        [field, field],
        (following, rho, mass),
        scratch=[pltpu.VMEM((2, y_elems, 4 * BLOCK, lanes), jnp.float32)],
        y_elems=y_elems,
        z_elems=z_elems,
    )
    seen = []
    for step in range(steps):
        last = step == steps - 1
        seen += [fault_rows] + fault_in
        base, touch = kernel_call(
            prepare_kernel,
            [field, (2 * PLANE, lanes)],
            [cur, material, own_table, touch_table],
            (),
        )
        args = [cur, fol, minv, base, touch, material, odd_in] + fault_in + even_in
        args += [first_in[0], fault_rows, first_fault, far_table, edge_table]
        static = dict(
            step=step, last=last, extra=1 if last or step == 1 else 0, last_place=lax.axis_size("dom") - 1, pair=pair, y_elems=y_elems,
            z_elems=z_elems,
        )
        if step == 1:
            mask, weight = kernel_call(
                mask_kernel,
                [(4 * PATCH_ROWS, lanes), (4 * steps, lanes)],
                [owner, flags, stress, cur],
                unread=(3,),
                z_elems=z_elems,
            )
            args.append(mask)
        if not last:
            new, odd, new_fault = kernel_call(
                step_kernel,
                [field, plane, (SENT_FAULT, lanes)],
                args,
                unread=(len(args) - 1,) if step == 1 else (),
                **static,
            )
            fol, cur, fault_rows = cur, new, new_fault
            even_in, odd_in, fault_in = exchange(on_chip(cur), odd, fault_rows)
        else:
            whole = (3, 4 * y_elems + 1, 4, lanes)
            known = seen[: len(seen) - len(fault_in)]
            later, grad, table = kernel_call(
                output_kernel,
                [whole, (4, lanes), ((lanes, lanes), jnp.bfloat16)],
                [cur, back, weight] + known,
                scratch=[native],
                stay=True,
                pair=pair,
                steps=steps,
                y_elems=y_elems,
                z_elems=z_elems,
            )
            sums = kernel_call(
                patch_kernel,
                [(PATCH_DEV, lanes)] * 5,
                [mask, weight, grad, table, odd_in] + fault_in + even_in + [touch],
                unread=(4,) + tuple(range(5 + len(fault_in), 9 + len(fault_in))),
                pair=pair,
                steps=steps,
            )
            shares = [sums[0]]
            for i, distance, group in ((3, 2, 0), (2, 1, 1), (4, 2, 1), (1, 1, 0)):
                shares.append(swapped(sums[i], distance, group))
            patch_sums = kernel_call(sum_kernel, [(PATCH_DEV, lanes)], shares)[0]
            earlier, later = kernel_call(
                step_kernel,
                [whole, whole],
                args + [sums[0], later, back],
                scratch=[
                    native, pltpu.VMEM(whole, jnp.float32), pltpu.SemaphoreType.DMA((4,)),
                ],
                unread=(len(args),),
                out_spec=HBM,
                **static,
            )
    return (
        jnp.transpose(earlier, (0, 2, 1, 3)),
        jnp.transpose(later, (0, 2, 1, 3)),
        patch_sums[None],
    )


def solution(mesh):
    return jax.shard_map(
        on_device,
        mesh=mesh,
        in_specs=(
            P(None, "dom", "depth", None),
            P(None, "dom", "depth", None),
            P("dom", "depth", None),
            P("dom", "depth", None),
            P("dom", "depth", None),
            P(None, "depth", "dom", None),
            P("depth", "dom", None),
            P("depth", "dom", None),
            P("depth", "dom"),
        ),
        out_specs=(
            P(None, "dom", "depth", None),
            P(None, "dom", "depth", None),
            P("depth", "dom", None),
        ),
        check_vma=False,
    )
```

```python
import functools
import math

import jax
import jax.numpy as jnp
import ml_dtypes
import numpy as np
from jax import lax
from jax.experimental import pallas as pl
from jax.experimental.pallas import tpu as pltpu
from jax.sharding import PartitionSpec as P

PATCH_DEV = 2
REACH = 2
PATCH_ROWS = 16
LATER = 10
FAULT = 24
SENT_FAULT = 28
PARTS = (24, 24, 16)

time_step = 0.01
lock_stiffness = 0.5

BLOCK = 16
ROWS = ((0, 1, 2), (3, 4, 5), (11, 12, 13), (6, 7, 14), (8, 9, 10))
PLANE = 5 * BLOCK


def basis_tables():
    points = [-1.0, -math.sqrt(3.0 / 7.0), 0.0, math.sqrt(3.0 / 7.0), 1.0]
    quad_weights = np.array([0.1, 49.0 / 90.0, 32.0 / 45.0, 49.0 / 90.0, 0.1])
    products = []
    for first in range(5):
        value = 1.0
        for other in range(5):
            if other != first:
                value = value * (points[first] - points[other])
        products.append(value)
    derivative = np.zeros((5, 5))
    for row in range(5):
        for column in range(5):
            if row == column:
                total = 0.0
                for other in range(5):
                    if other != row:
                        total = total + 1.0 / (points[row] - points[other])
                derivative[row, column] = total
            else:
                derivative[row, column] = (
                    products[row] / products[column] / (points[row] - points[column])
                )
    return (quad_weights, derivative)


def two_parts(table):
    high = table.astype(ml_dtypes.bfloat16)
    low = (table - high.astype(np.float64)).astype(ml_dtypes.bfloat16)
    return np.stack([high, low])


def element_stiffness():
    weights, derivative = basis_tables()
    eye = np.eye(5)
    slope = 2.0 * derivative
    grads = [
        np.kron(slope, np.kron(eye, eye)),
        np.kron(eye, np.kron(eye, slope)),
        np.kron(eye, np.kron(slope, eye)),
    ]
    quad = np.kron(weights, np.kron(weights, weights)) / 8.0
    first = np.zeros((125, 3, 125, 3))
    second = np.zeros((125, 3, 125, 3))
    lap = sum(g.T @ (quad[:, None] * g) for g in grads)
    for c in range(3):
        second[:, c, :, c] += lap
        for d in range(3):
            first[:, c, :, d] += grads[c].T @ (quad[:, None] * grads[d])
            second[:, c, :, d] += grads[d].T @ (quad[:, None] * grads[c])
    where = [
        node // 5 * BLOCK + ROWS[node % 5][c] for node in range(125) for c in range(3)
    ]
    wide = []
    for small in (first, second):
        big = np.zeros((5 * PLANE, 5 * PLANE))
        big[np.ix_(where, where)] = small.reshape(375, 375)
        wide.append(big)
    return wide


OWN_COLS = 384


def padded_table(table, columns):
    return np.pad(table, ((0, 0), (0, columns - table.shape[1])))


@functools.cache
def stiffness_tables():
    wide = element_stiffness()
    own = 4 * PLANE
    planes = [slice(x * PLANE, (x + 1) * PLANE) for x in range(5)]
    inner = np.concatenate([w[:own, :own] for w in wide])

    def three(table):
        high, low = two_parts(table)
        return padded_table(np.concatenate([high, low, high], axis=1), 256)

    def both(rows, columns):
        return three(np.concatenate([w[rows, columns] for w in wide]))

    return (
        two_parts(padded_table(inner, OWN_COLS)),
        np.concatenate([three(w[:own, planes[4]]) for w in wide], axis=1),
        np.concatenate([both(planes[4], planes[x]) for x in range(4)], axis=1),
        both(planes[4], planes[4]),
    )


@functools.cache
def back_table(y_elems, z_elems):
    lanes = y_elems * z_elems
    depth = 4 * z_elems
    back = np.zeros((4 * lanes, y_elems * depth), ml_dtypes.bfloat16)
    for yel in range(y_elems):
        for k in range(z_elems):
            for zl in range(4):
                back[zl * lanes + yel * z_elems + k, yel * depth + 4 * k + zl] = 1
    return back


@functools.cache
def mass_table(y_elems, z_elems):
    weights, _ = basis_tables()
    table = np.zeros((4, 5, BLOCK, y_elems, z_elems))
    for x in range(4):
        mx = 0.2 if x == 0 else weights[x]
        for zl in range(5):
            for yl in range(5):
                for yel in range(y_elems):
                    my = weights[yl]
                    if (yl == 0 and yel > 0) or (yl == 4 and yel < y_elems - 1):
                        my = 0.2
                    mz = np.full(z_elems, weights[zl])
                    if zl == 0:
                        mz[1:] = 0.2
                    if zl == 4:
                        mz[:] = 0.2
                    value = time_step * time_step * 8.0 / (mx * my * mz)
                    if zl == 4:
                        value[-1] = 0.0
                    table[x, zl, list(ROWS[yl]), yel] = value
    return table.reshape(4 * PLANE, y_elems * z_elems).astype(np.float32)


def pieces(value, count):
    out = []
    for _ in range(count):
        piece = value.astype(jnp.bfloat16)
        out.append(piece)
        value = value - piece.astype(jnp.float32)
    return out


def dot(a, b):
    return jnp.dot(a, b, preferred_element_type=jnp.float32)


def exact_dot(value, table, count=3):
    rows = value.shape[0]
    result = dot(jnp.concatenate(pieces(value, count), axis=0), table)
    total = result[:rows]
    for i in range(1, count):
        total = total + result[i * rows : (i + 1) * rows]
    return total


def split_dot(table_high, table_low, value):
    lanes = value.shape[1]
    high, low = pieces(value, 2)
    wide = dot(table_high, jnp.concatenate([high, low], axis=1))
    return wide[:, :lanes] + (wide[:, lanes:] + dot(table_low, high))


def over(value, size):
    if size & (size - 1) == 0:
        return lax.shift_right_logical(value, np.int32(size.bit_length() - 1))
    return lax.div(value, np.int32(size))


def within(value, size):
    return value & (size - 1) if size & (size - 1) == 0 else lax.rem(value, np.int32(size))


def ones_where(shape, axis, wanted):
    line = (shape[0], 1) if axis == 0 else (1, shape[1])
    target = wanted(lax.broadcasted_iota(jnp.int32, line, axis))
    number = lax.broadcasted_iota(jnp.int32, shape, 1 - axis)
    return jnp.where(number == target, 1.0, 0.0).astype(jnp.bfloat16)


def gather_table(lanes, z_elems):
    return ones_where(
        (lanes, 5 * lanes), 1, lambda c: 4 * within(c, z_elems) + over(c, lanes)
    )


def fault_table(lanes, z_elems):
    return ones_where((lanes, lanes), 1, lambda c: 4 * within(c, z_elems) + over(c, z_elems))


def fault_table_back(lanes, z_elems):
    return ones_where((lanes, lanes), 0, lambda c: 4 * within(c, z_elems) + over(c, z_elems))


def stacked(value):
    high, low = pieces(value, 2)
    gap = jnp.zeros((256 - 3 * value.shape[0], value.shape[1]), jnp.bfloat16)
    return jnp.concatenate([high, high, low, gap], axis=0)


def to_elements(native, scratch, table, y_elems, parts=3):
    group = 4 * BLOCK
    for c in range(3):
        for y in range(4 * y_elems + 1):
            rows = native(c, y)
            if y < 4 * y_elems:
                scratch[y // 4, pl.ds(ROWS[y % 4][c], 4, stride=BLOCK), :] = rows
            if y % 4 == 0 and y > 0:
                scratch[y // 4 - 1, pl.ds(ROWS[4][c], 4, stride=BLOCK), :] = rows
    high, middle, *low = pieces(
        jnp.concatenate([scratch[i] for i in range(y_elems)], axis=0), parts
    )
    result = dot(
        jnp.concatenate([high, middle], axis=1), jnp.concatenate([table, table], axis=0)
    )
    for piece in low:
        result = result + dot(piece, table)
    lanes = result.shape[1] // 5
    across = lax.broadcasted_iota(jnp.int32, (1, result.shape[1]), 1)
    across = over(within(across, lanes), lanes // y_elems)
    total = result[:group]
    for yel in range(1, y_elems):
        total = jnp.where(across == yel, result[yel * group : (yel + 1) * group], total)
    blocks = []
    for x in range(4):
        for zl in range(5):
            blocks.append(total[x * BLOCK : (x + 1) * BLOCK, zl * lanes : (zl + 1) * lanes])
    return jnp.concatenate(blocks, axis=0)


def from_elements(field, scratch, back_ref, out_ref, y_elems, stored=None):
    rows = []
    for x in range(4):
        rows.append(
            jnp.concatenate(
                [field[x * PLANE + zl * BLOCK : x * PLANE + (zl + 1) * BLOCK] for zl in range(4)],
                axis=1,
            )
        )
    result = exact_dot(jnp.concatenate(rows, axis=0), back_ref[...])
    depth = result.shape[1] // y_elems
    for yel in range(y_elems):
        scratch[yel] = result[:, yel * depth : (yel + 1) * depth]
    for c in range(3):
        for y in range(4 * y_elems + 1):
            yel, yl = (y // 4, y % 4) if y < 4 * y_elems else (y_elems - 1, 4)
            out_ref[c, y] = scratch[yel, pl.ds(ROWS[yl][c], 4, stride=BLOCK), :]
        if stored is not None:
            stored(c)


def shifted(rows, lanes):
    lanes = lanes % rows.shape[1]
    return pltpu.roll(rows, lanes, 1) if lanes else rows


def block_iotas(lanes):
    return (
        lax.broadcasted_iota(jnp.int32, (8, lanes), 0),
        lax.broadcasted_iota(jnp.int32, (8, lanes), 1),
    )


def store_fault(out_ref, x, plane, z_elems):
    lanes = plane.shape[1]
    _, lane = block_iotas(lanes)
    first = last = jnp.zeros((8, lanes), jnp.float32)
    for zl in range(4):
        at = zl * BLOCK
        here = over(lane, z_elems) == zl
        first = jnp.where(here, shifted(plane[at : at + 8], zl * z_elems), first)
        last = jnp.where(here, shifted(plane[at + 8 : at + 16], (zl + 1) * z_elems), last)
    out_ref[pl.ds(x, 3, stride=8), :] = last[:3]
    out_ref[pl.ds(4 + x, 3, stride=8), :] = first[:3]


def material_rows(lame_ref, shear_ref):
    y_elems, z_elems = lame_ref.shape
    both = jnp.concatenate([lame_ref[...], shear_ref[...]], axis=0)
    spread = ones_where((z_elems, y_elems * z_elems), 1, lambda c: within(c, z_elems))
    tiled = exact_dot(both, spread)
    row = lax.broadcasted_iota(jnp.int32, tiled.shape, 0)
    lane = lax.broadcasted_iota(jnp.int32, tiled.shape, 1)
    kept = jnp.where(within(row, y_elems) == over(lane, z_elems), tiled, 0.0)
    return (
        jnp.sum(kept[:y_elems], axis=0, keepdims=True),
        jnp.sum(kept[y_elems:], axis=0, keepdims=True),
    )


def above_lanes(lanes, z_elems):
    return within(lax.broadcasted_iota(jnp.int32, (BLOCK, lanes), 1), z_elems) != 0


def edge_message(result, lame_row, shear_row, z_elems):
    lanes = result.shape[1]
    force = lame_row * result[:PLANE] + shear_row * result[PLANE:]
    top = force[:BLOCK] + jnp.where(
        above_lanes(lanes, z_elems), pltpu.roll(force[4 * BLOCK :], 1, 1), 0.0
    )
    row = lax.broadcasted_iota(jnp.int32, top.shape, 0)
    top = jnp.where(row == BLOCK - 1, lame_row, top)
    second = jnp.where(row == BLOCK - 1, shear_row, force[BLOCK : 2 * BLOCK])
    return jnp.concatenate([top, second, force[2 * BLOCK : 4 * BLOCK]], axis=0)


def edge_of(field_ref, edge_ref, material_ref, z_elems):
    planes = [stacked(field_ref[x * PLANE : (x + 1) * PLANE]) for x in range(4)]
    edge = dot(edge_ref[...], jnp.concatenate(planes, axis=0))
    return edge_message(edge, material_ref[0:1], material_ref[1:2], z_elems)


def own_force(own_ref, cur, lame_row, shear_row):
    rows, lanes = cur.shape
    padded = jnp.concatenate([cur, jnp.zeros((OWN_COLS - rows, lanes), jnp.float32)], axis=0)
    result = split_dot(own_ref[0], own_ref[1], padded)
    return lame_row * result[:rows] + shear_row * result[rows:]


def start_copies(pairs, sems):
    copies = [
        pltpu.make_async_copy(source, target, sems.at[i])
        for i, (source, target) in enumerate(pairs)
    ]
    for copy in copies:
        copy.start()
    return copies


def first_kernel(
    now_hbm,
    flags_hbm,
    weak_hbm,
    lame_hbm,
    shear_hbm,
    *refs,
):
    later_hbm, refs = refs[:LATER], refs[LATER:]
    cur_ref, odd_ref, fault_out_ref, material_ref = refs[:4]
    later_refs, refs = refs[4 : 4 + LATER], refs[4 + LATER :]
    scratch, now_ref, flags_ref, weak_ref, lame_ref, shear_ref, sems = refs
    copies = start_copies(
        [
            (now_hbm, now_ref),
            (lame_hbm, lame_ref),
            (shear_hbm, shear_ref),
            (flags_hbm, flags_ref),
            (weak_hbm, weak_ref),
            (later_hbm[0], later_refs[0]),
        ]
        + list(zip(later_hbm[1:], later_refs[1:])),
        sems,
    )
    edge_ref = later_refs[0]
    y_elems, z_elems = lame_ref.shape
    lanes = y_elems * z_elems
    gather = gather_table(lanes, z_elems)
    fault = fault_table(lanes, z_elems)
    scratch[...] = jnp.zeros_like(scratch)
    for copy in copies[1:5]:
        copy.wait()
    lame_row, shear_row = material_rows(lame_ref, shear_ref)
    material_ref[...] = jnp.concatenate(
        [lame_row, shear_row, jnp.zeros((6, lanes), jnp.float32)], axis=0
    )
    weak = weak_ref[...]
    tangent = []
    for i in range(flags_ref.shape[0]):
        flag = flags_ref[i]
        tangent.append(
            jnp.where(flag == 0, lock_stiffness, jnp.where(flag == 1, -weak, 0.0))
        )
    fault_out_ref[FAULT:] = exact_dot(jnp.concatenate(tangent, axis=0), fault)
    copies[0].wait()
    cur = to_elements(lambda c, y: now_ref[c, y], scratch, gather, y_elems)
    cur_ref[...] = cur
    planes = [cur[x * PLANE : (x + 1) * PLANE] for x in range(4)]
    for x in range(4):
        store_fault(fault_out_ref, x, planes[x], z_elems)
    odd_ref[...] = cur[: 4 * BLOCK]
    copies[5].wait()

    @pl.when(lax.axis_index("dom") % 2 == 1)
    def _():
        odd_ref[...] = edge_of(cur_ref, edge_ref, material_ref, z_elems)

    for copy in copies[6:]:
        copy.wait()


def prepare_kernel(cur_ref, material_ref, own_ref, touch_ref, base_ref, edge_part_ref):
    cur = cur_ref[...]
    base_ref[...] = own_force(own_ref, cur, material_ref[0:1], material_ref[1:2])
    edge_part_ref[...] = dot(touch_ref[...], stacked(cur[:PLANE]))


def setup_kernel(next_ref, density_ref, mass_ref, fol_ref, minv_ref, scratch, *, y_elems, z_elems):
    gather = gather_table(y_elems * z_elems, z_elems)
    scratch[...] = jnp.zeros_like(scratch)
    fol_ref[...] = to_elements(lambda c, y: next_ref[c, y], scratch.at[0], gather, y_elems)
    density = to_elements(lambda c, y: density_ref[y], scratch.at[1], gather, y_elems, 2)
    table = mass_ref[...]
    first = lax.axis_index("dom") == 0
    plane = lax.broadcasted_iota(jnp.int32, table.shape, 0) < PLANE
    table = jnp.where(jnp.logical_and(first, plane), 2.0 * table, table)
    minv_ref[...] = jnp.where(table > 0.0, table / jnp.where(table > 0.0, density, 1.0), 0.0)


def step_kernel(*refs, step, last, extra, last_place, pair, y_elems, z_elems):
    cur_ref, fol_ref, minv_ref, base_ref, touch_ref, material_ref, odd_ref, up_ref = refs[:8]
    refs = list(refs[8:])
    down_ref = None if pair else refs.pop(0)
    even_in = jnp.concatenate([refs.pop(0)[...] for _ in PARTS], axis=0)
    down_ref = up_ref if pair else down_ref
    first_up_ref, own_ref, first_own_ref, far_ref, edge_ref = refs[:5]
    refs = refs[5 + extra :]
    if last:
        later_ref, back_ref, out_hbm, later_hbm, scratch, out_ref, sems = refs
        copies = start_copies([(later_ref, later_hbm)], sems)
    else:
        new_ref, odd_out, fault_out = refs
    place = lax.axis_index("dom")
    lanes = cur_ref.shape[1]
    even = place % 2 == 0
    far = jnp.where(place == last_place, 0.0, jnp.where(even, even_in, odd_ref[...]))
    left = jnp.where(place == 0, 0.0, jnp.where(even, odd_ref[...], even_in))
    lane_wide = lax.broadcasted_iota(jnp.int32, (BLOCK, lanes), 1)
    below = jnp.where(
        within(lane_wide, z_elems) != z_elems - 1, pltpu.roll(far[:BLOCK], lanes - 1, 1), 0.0
    )
    far = jnp.concatenate([far, below], axis=0)
    lame_row, shear_row = material_ref[0:1], material_ref[1:2]
    far = jnp.concatenate([stacked(lame_row * far), stacked(shear_row * far)], axis=0)
    left_lame = left[BLOCK - 1 : BLOCK]
    left_shear = left[2 * BLOCK - 1 : 2 * BLOCK]
    from_left = left_lame * touch_ref[:PLANE] + left_shear * touch_ref[PLANE:]
    row, lane = block_iotas(lanes)
    across = over(lane, z_elems)
    shared = row < 3
    add_first = jnp.logical_and(shared, across > 0)
    take_last = jnp.logical_and(shared, across < y_elems - 1)
    pull_first = jnp.logical_and(shared, across == 0)
    pull_last = jnp.logical_and(shared, across == y_elems - 1)
    above = above_lanes(lanes, z_elems)
    middle = lax.broadcasted_iota(jnp.int32, (3, lanes), 0) == 1
    gap = jnp.zeros((5, lanes), jnp.float32)
    if not last:
        fault_out[FAULT:] = jnp.zeros_like(fault_out[FAULT:])
    planes = []
    for x in range(4):
        rows = slice(x * PLANE, (x + 1) * PLANE)
        force = base_ref[rows] + dot(far_ref[rows], far)
        blocks = [force[zl * BLOCK : (zl + 1) * BLOCK] for zl in range(5)]
        if x == 0:
            blocks = [b + from_left[i * BLOCK : (i + 1) * BLOCK] for i, b in enumerate(blocks)]
            blocks[:4] = [b + left[i * BLOCK : (i + 1) * BLOCK] for i, b in enumerate(blocks[:4])]
        blocks[0], blocks[4] = (
            blocks[0] + jnp.where(above, pltpu.roll(blocks[4], 1, 1), 0.0),
            blocks[4] + pltpu.roll(blocks[0], lanes - 1, 1),
        )
        lasts, firsts = pl.ds(x, 3, stride=8), pl.ds(4 + x, 3, stride=8)
        k = slice(FAULT + 4 * step + x, FAULT + 4 * step + x + 1)
        below_stiff = jnp.where(middle, lock_stiffness, first_up_ref[k])
        own_stiff = jnp.where(middle, lock_stiffness, first_own_ref[k])
        pulled = jnp.concatenate(
            [below_stiff * (up_ref[lasts, :] - own_ref[firsts, :]), gap], axis=0
        )
        pulled_last = jnp.concatenate(
            [own_stiff * (down_ref[firsts, :] - own_ref[lasts, :]), gap], axis=0
        )
        for zl in range(5):
            low, high = blocks[zl][:8], blocks[zl][8:]
            move = zl * z_elems if zl < 4 else 1
            blocks[zl] = jnp.concatenate(
                [
                    low
                    + jnp.where(add_first, shifted(high, z_elems), 0.0)
                    - jnp.where(pull_first, shifted(pulled, -move), 0.0),
                    high
                    + jnp.where(take_last, shifted(low, -z_elems), 0.0)
                    - jnp.where(pull_last, shifted(pulled_last, -move - z_elems), 0.0),
                ],
                axis=0,
            )
        plane = (2.0 * cur_ref[rows] - fol_ref[rows]) - minv_ref[rows] * jnp.concatenate(
            blocks, axis=0
        )
        if last:
            planes.append(plane)
        else:
            new_ref[rows] = plane
            store_fault(fault_out, x, plane, z_elems)
            if x == 0:
                first = plane[: 4 * BLOCK]
    if last:

        def send(c):
            copy = pltpu.make_async_copy(out_ref.at[c], out_hbm.at[c], sems.at[1 + c])
            copy.start()
            copies.append(copy)

        from_elements(
            jnp.concatenate(planes, axis=0), scratch, back_ref, out_ref, y_elems, send
        )
        for copy in copies:
            copy.wait()
    else:
        odd_out[...] = first

        @pl.when(jnp.logical_not(even))
        def _():
            odd_out[...] = edge_of(new_ref, edge_ref, material_ref, z_elems)


def on_chip_kernel(cur_ref, material_ref, edge_ref, *even_outs, z_elems):
    message = even_outs[-1]
    even_outs = even_outs[:-1]
    message[...] = cur_ref[: 4 * BLOCK]

    @pl.when(lax.axis_index("dom") % 2 == 0)
    def _():
        message[...] = edge_of(cur_ref, edge_ref, material_ref, z_elems)

    for even_out, at in zip(even_outs, (0, PARTS[0], PARTS[0] + PARTS[1])):
        even_out[...] = message[at : at + even_out.shape[0]]


def mask_kernel(owner_ref, flags_ref, stress_ref, _, back_ref, mask_ref, weight_ref, *, z_elems):
    shape = (PATCH_ROWS, mask_ref.shape[1])
    first = (lax.axis_index("dom") - REACH) * PATCH_DEV
    number = lax.broadcasted_iota(jnp.int32, shape, 0) + first
    for x in range(4):
        mask = jnp.where(number == owner_ref[:, x : x + 1], 1.0, 0.0)
        mask_ref[PATCH_ROWS * x : PATCH_ROWS * (x + 1)] = mask
    stress = stress_ref[...]
    weights = []
    for i in range(flags_ref.shape[0]):
        flag = flags_ref[i]
        weights.append(
            stress * jnp.where(flag == 1, 0.5, jnp.where(flag == 2, 1.0, 0.0))
        )
    fault = fault_table(mask_ref.shape[1], z_elems)
    weight_ref[...] = exact_dot(jnp.concatenate(weights, axis=0), fault)


def output_kernel(*refs, pair, steps, y_elems, z_elems):
    field_ref, back_ref, weight_ref = refs[:3]
    out_ref, grad_ref, table_ref, scratch = refs[-4:]
    messages = refs[3:-4]
    count = 2 if pair else 3
    grad = 0.0
    for i in range(steps):
        group = messages[count * i : count * (i + 1)]
        slip = -group[0][:4]
        if i < steps - 1:
            slip = slip + group[-1][4:8]
        grad = grad + slip * weight_ref[4 * i : 4 * i + 4]
    grad_ref[...] = grad
    table_ref[...] = fault_table_back(weight_ref.shape[1], z_elems)
    from_elements(field_ref[...], scratch, back_ref, out_ref, y_elems)


def patch_kernel(*refs, pair, steps):
    mask_ref, weight_ref, grad_ref, table_ref, _ = refs[:5]
    first_ref = refs[5] if pair else refs[6]
    home_out, out_a, out_b, out_c, out_d = refs[-5:]
    place = lax.axis_index("dom")
    grad = grad_ref[...] + first_ref[4:8] * weight_ref[4 * (steps - 1) : 4 * steps]
    total = 0.0
    for x in range(4):
        total = total + mask_ref[PATCH_ROWS * x : PATCH_ROWS * (x + 1)] * grad[x : x + 1]
    total = exact_dot(total, table_ref[...])
    rows = [total[2 * i : 2 * i + 2] for i in range(5)]
    home_out[...] = rows[2]
    even = place % 2 == 0
    out_a[...] = jnp.where(even, rows[3], rows[1])
    out_b[...] = jnp.where(even, rows[1], rows[3])
    low = place % 4 < 2
    out_c[...] = jnp.where(low, rows[4], rows[0])
    out_d[...] = jnp.where(low, rows[0], rows[4])


def sum_kernel(*refs):
    refs[-1][...] = sum(ref[...] for ref in refs[:-1])


VMEM = pl.BlockSpec(memory_space=pltpu.VMEM)
HBM = pl.BlockSpec(memory_space=pltpu.HBM)
SMEM = pl.BlockSpec(memory_space=pltpu.SMEM)
ANY = pl.BlockSpec(memory_space=pl.ANY)


def kernel_call(body, outs, args, in_smem=(), scratch=(), in_hbm=(), kept=(), unread=(), stay=False, out_spec=VMEM, **static):
    shapes = []
    for out in outs:
        shape, dtype = out if isinstance(out[0], tuple) else (out, jnp.float32)
        shapes.append((pltpu.VMEM if in_hbm or stay else jax.ShapeDtypeStruct)(shape, dtype))
    specs = [VMEM] * len(args)
    for places, spec in ((in_smem, SMEM), (in_hbm, HBM), (unread, ANY)):
        for i in places:
            specs[i] = spec
    copied = [pltpu.VMEM(args[i].shape, args[i].dtype) for i in in_hbm if i not in kept]
    if in_hbm:
        copied.append(pltpu.SemaphoreType.DMA((len(in_hbm),)))
    return pl.pallas_call(
        functools.partial(body, **static) if static else body,
        out_shape=shapes,
        in_specs=specs,
        out_specs=[out_spec] * len(shapes),
        scratch_shapes=list(scratch) + copied,
        compiler_params=pltpu.CompilerParams(
            vmem_limit_bytes=(56 if in_hbm else 24) * 2**20
        ),
    )(*args)


def swapped(block, distance, group):
    size, across = lax.axis_size("dom"), lax.axis_size("depth")
    partner = {}
    for left in range(size - distance):
        if left // distance % 2 == group:
            partner[left], partner[left + distance] = left + distance, left
    route = []
    for i in range(size):
        for j in range(across):
            other, side = partner.get(i, i), j
            if i not in partner and i ^ 1 < size and i ^ 1 not in partner:
                other = i ^ 1
            elif i not in partner:
                side = min(j ^ 1, across - 1)
            route.append((i * across + j, other * across + side))
    return lax.ppermute(block, ("dom", "depth"), route)


def from_behind(block, axis, distance):
    size = lax.axis_size(axis)
    return lax.ppermute(block, axis, [((i - distance) % size, i) for i in range(size)])


def on_device(
    adjoint_now,
    adjoint_next,
    lame_first,
    shear_modulus,
    density,
    branch_flags,
    weak_slope,
    normal_stress,
    patch_owner,
):
    x_elems, y_elems, z_elems = lame_first.shape
    lanes = y_elems * z_elems
    assert x_elems == 1 and lanes == adjoint_now.shape[3]
    steps = branch_flags.shape[0]
    pair = lax.axis_size("depth") == 2
    own_table, far_table, edge_table, touch_table = (jnp.asarray(t) for t in stiffness_tables())
    back = jnp.asarray(back_table(y_elems, z_elems))
    mass = jnp.asarray(mass_table(y_elems, z_elems))
    now = jnp.transpose(adjoint_now, (0, 2, 1, 3))
    following = jnp.transpose(adjoint_next, (0, 2, 1, 3))
    rho = jnp.transpose(density, (1, 0, 2))
    flags = branch_flags[:, 0]
    native = pltpu.VMEM((y_elems, 4 * BLOCK, lanes), jnp.float32)
    field = (4 * PLANE, lanes)
    plane = (4 * BLOCK, lanes)
    parts = [(rows, lanes) for rows in PARTS]

    def exchange(even, odd, fault_rows):
        if pair:
            faults = [from_behind(fault_rows, "depth", 1)]
        else:
            faults = [from_behind(fault_rows, "depth", 1), from_behind(fault_rows, "depth", -1)]
        return [swapped(part, 1, 0) for part in even], swapped(odd, 1, 1), faults

    later_used = (
        edge_table, following, rho, mass, own_table, far_table, touch_table, flags,
        normal_stress[0], patch_owner,
    )
    assert len(later_used) == LATER
    first_out = kernel_call(
        first_kernel,
        [field, plane, (FAULT + 4 * steps, lanes), (8, lanes)]
        + [(t.shape, t.dtype) for t in later_used],
        (now, flags, weak_slope[0], lame_first[0], shear_modulus[0]) + later_used,
        scratch=[native],
        in_hbm=range(5 + LATER),
        kept=range(5, 5 + LATER),
    )
    cur, odd, fault_rows, material = first_out[:-LATER]
    edge_table, following, rho, mass, own_table, far_table, touch_table = first_out[-LATER:-3]
    flags, stress, owner = first_out[-3:]

    def on_chip(field):
        return kernel_call(
            on_chip_kernel,
            parts,
            [field, material, edge_table],
            scratch=[pltpu.VMEM(plane, jnp.float32)],
            z_elems=z_elems,
        )

    even_in, odd_in, fault_in = exchange(on_chip(cur), odd, fault_rows)
    first_fault, first_in = fault_rows, fault_in
    fol, minv = kernel_call(
        setup_kernel,
        [field, field],
        (following, rho, mass),
        scratch=[pltpu.VMEM((2, y_elems, 4 * BLOCK, lanes), jnp.float32)],
        y_elems=y_elems,
        z_elems=z_elems,
    )
    seen = []
    for step in range(steps):
        last = step == steps - 1
        seen += [fault_rows] + fault_in
        base, touch = kernel_call(
            prepare_kernel,
            [field, (2 * PLANE, lanes)],
            [cur, material, own_table, touch_table],
            (),
        )
        args = [cur, fol, minv, base, touch, material, odd_in] + fault_in + even_in
        args += [first_in[0], fault_rows, first_fault, far_table, edge_table]
        static = dict(
            step=step, last=last, extra=1 if last or step == 1 else 0, last_place=lax.axis_size("dom") - 1, pair=pair, y_elems=y_elems,
            z_elems=z_elems,
        )
        if step == 1:
            mask, weight = kernel_call(
                mask_kernel,
                [(4 * PATCH_ROWS, lanes), (4 * steps, lanes)],
                [owner, flags, stress, cur, back],
                unread=(3,),
                z_elems=z_elems,
            )
            args.append(mask)
        if not last:
            new, odd, new_fault = kernel_call(
                step_kernel,
                [field, plane, (SENT_FAULT, lanes)],
                args,
                unread=(len(args) - 1,) if step == 1 else (),
                **static,
            )
            fol, cur, fault_rows = cur, new, new_fault
            even_in, odd_in, fault_in = exchange(on_chip(cur), odd, fault_rows)
        else:
            whole = (3, 4 * y_elems + 1, 4, lanes)
            known = seen[: len(seen) - len(fault_in)]
            later, grad, table = kernel_call(
                output_kernel,
                [whole, (4, lanes), ((lanes, lanes), jnp.bfloat16)],
                [cur, back, weight] + known,
                scratch=[native],
                stay=True,
                pair=pair,
                steps=steps,
                y_elems=y_elems,
                z_elems=z_elems,
            )
            sums = kernel_call(
                patch_kernel,
                [(PATCH_DEV, lanes)] * 5,
                [mask, weight, grad, table, odd_in] + fault_in + even_in + [touch],
                unread=(4,) + tuple(range(5 + len(fault_in), 9 + len(fault_in))),
                pair=pair,
                steps=steps,
            )
            shares = [sums[0]]
            for i, distance, group in ((3, 2, 0), (2, 1, 1), (4, 2, 1), (1, 1, 0)):
                shares.append(swapped(sums[i], distance, group))
            patch_sums = kernel_call(sum_kernel, [(PATCH_DEV, lanes)], shares)[0]
            earlier, later = kernel_call(
                step_kernel,
                [whole, whole],
                args + [sums[0], later, back],
                scratch=[
                    native, pltpu.VMEM(whole, jnp.float32), pltpu.SemaphoreType.DMA((4,)),
                ],
                unread=(len(args),),
                out_spec=HBM,
                **static,
            )
    return (
        jnp.transpose(earlier, (0, 2, 1, 3)),
        jnp.transpose(later, (0, 2, 1, 3)),
        patch_sums[None],
    )


def solution(mesh):
    return jax.shard_map(
        on_device,
        mesh=mesh,
        in_specs=(
            P(None, "dom", "depth", None),
            P(None, "dom", "depth", None),
            P("dom", "depth", None),
            P("dom", "depth", None),
            P("dom", "depth", None),
            P(None, "depth", "dom", None),
            P("depth", "dom", None),
            P("depth", "dom", None),
            P("depth", "dom"),
        ),
        out_specs=(
            P(None, "dom", "depth", None),
            P(None, "dom", "depth", None),
            P("depth", "dom", None),
        ),
        check_vma=False,
    )
```

```python
import functools
import math

import jax
import jax.numpy as jnp
import ml_dtypes
import numpy as np
from jax import lax
from jax.experimental import pallas as pl
from jax.experimental.pallas import tpu as pltpu
from jax.sharding import PartitionSpec as P

PATCH_DEV = 2
REACH = 2
PATCH_ROWS = 16
LATER = 9
FAULT = 24
SENT_FAULT = 28
PARTS = (24, 24, 16)

time_step = 0.01
lock_stiffness = 0.5

BLOCK = 16
ROWS = ((0, 1, 2), (3, 4, 5), (11, 12, 13), (6, 7, 14), (8, 9, 10))
PLANE = 5 * BLOCK


def basis_tables():
    points = [-1.0, -math.sqrt(3.0 / 7.0), 0.0, math.sqrt(3.0 / 7.0), 1.0]
    quad_weights = np.array([0.1, 49.0 / 90.0, 32.0 / 45.0, 49.0 / 90.0, 0.1])
    products = []
    for first in range(5):
        value = 1.0
        for other in range(5):
            if other != first:
                value = value * (points[first] - points[other])
        products.append(value)
    derivative = np.zeros((5, 5))
    for row in range(5):
        for column in range(5):
            if row == column:
                total = 0.0
                for other in range(5):
                    if other != row:
                        total = total + 1.0 / (points[row] - points[other])
                derivative[row, column] = total
            else:
                derivative[row, column] = (
                    products[row] / products[column] / (points[row] - points[column])
                )
    return (quad_weights, derivative)


def two_parts(table):
    high = table.astype(ml_dtypes.bfloat16)
    low = (table - high.astype(np.float64)).astype(ml_dtypes.bfloat16)
    return np.stack([high, low])


def element_stiffness():
    weights, derivative = basis_tables()
    eye = np.eye(5)
    slope = 2.0 * derivative
    grads = [
        np.kron(slope, np.kron(eye, eye)),
        np.kron(eye, np.kron(eye, slope)),
        np.kron(eye, np.kron(slope, eye)),
    ]
    quad = np.kron(weights, np.kron(weights, weights)) / 8.0
    first = np.zeros((125, 3, 125, 3))
    second = np.zeros((125, 3, 125, 3))
    lap = sum(g.T @ (quad[:, None] * g) for g in grads)
    for c in range(3):
        second[:, c, :, c] += lap
        for d in range(3):
            first[:, c, :, d] += grads[c].T @ (quad[:, None] * grads[d])
            second[:, c, :, d] += grads[d].T @ (quad[:, None] * grads[c])
    where = [
        node // 5 * BLOCK + ROWS[node % 5][c] for node in range(125) for c in range(3)
    ]
    wide = []
    for small in (first, second):
        big = np.zeros((5 * PLANE, 5 * PLANE))
        big[np.ix_(where, where)] = small.reshape(375, 375)
        wide.append(big)
    return wide


OWN_COLS = 384


def padded_table(table, columns):
    return np.pad(table, ((0, 0), (0, columns - table.shape[1])))


@functools.cache
def stiffness_tables():
    wide = element_stiffness()
    own = 4 * PLANE
    planes = [slice(x * PLANE, (x + 1) * PLANE) for x in range(5)]
    inner = np.concatenate([w[:own, :own] for w in wide])

    def three(table):
        high, low = two_parts(table)
        return padded_table(np.concatenate([high, low, high], axis=1), 256)

    def both(rows, columns):
        return three(np.concatenate([w[rows, columns] for w in wide]))

    return (
        two_parts(padded_table(inner, OWN_COLS)),
        np.concatenate([three(w[:own, planes[4]]) for w in wide], axis=1),
        np.concatenate([both(planes[4], planes[x]) for x in range(4)], axis=1),
        both(planes[4], planes[4]),
    )


@functools.cache
def back_table(y_elems, z_elems):
    lanes = y_elems * z_elems
    depth = 4 * z_elems
    back = np.zeros((4 * lanes, y_elems * depth), ml_dtypes.bfloat16)
    for yel in range(y_elems):
        for k in range(z_elems):
            for zl in range(4):
                back[zl * lanes + yel * z_elems + k, yel * depth + 4 * k + zl] = 1
    return back


@functools.cache
def mass_table(y_elems, z_elems):
    weights, _ = basis_tables()
    table = np.zeros((4, 5, BLOCK, y_elems, z_elems))
    for x in range(4):
        mx = 0.2 if x == 0 else weights[x]
        for zl in range(5):
            for yl in range(5):
                for yel in range(y_elems):
                    my = weights[yl]
                    if (yl == 0 and yel > 0) or (yl == 4 and yel < y_elems - 1):
                        my = 0.2
                    mz = np.full(z_elems, weights[zl])
                    if zl == 0:
                        mz[1:] = 0.2
                    if zl == 4:
                        mz[:] = 0.2
                    value = time_step * time_step * 8.0 / (mx * my * mz)
                    if zl == 4:
                        value[-1] = 0.0
                    table[x, zl, list(ROWS[yl]), yel] = value
    return table.reshape(4 * PLANE, y_elems * z_elems).astype(np.float32)


def pieces(value, count):
    out = []
    for _ in range(count):
        piece = value.astype(jnp.bfloat16)
        out.append(piece)
        value = value - piece.astype(jnp.float32)
    return out


def dot(a, b):
    return jnp.dot(a, b, preferred_element_type=jnp.float32)


def exact_dot(value, table, count=3):
    rows = value.shape[0]
    result = dot(jnp.concatenate(pieces(value, count), axis=0), table)
    total = result[:rows]
    for i in range(1, count):
        total = total + result[i * rows : (i + 1) * rows]
    return total


def split_dot(table_high, table_low, value):
    lanes = value.shape[1]
    high, low = pieces(value, 2)
    wide = dot(table_high, jnp.concatenate([high, low], axis=1))
    return wide[:, :lanes] + (wide[:, lanes:] + dot(table_low, high))


def over(value, size):
    if size & (size - 1) == 0:
        return lax.shift_right_logical(value, np.int32(size.bit_length() - 1))
    return lax.div(value, np.int32(size))


def within(value, size):
    return value & (size - 1) if size & (size - 1) == 0 else lax.rem(value, np.int32(size))


def ones_where(shape, axis, wanted):
    line = (shape[0], 1) if axis == 0 else (1, shape[1])
    target = wanted(lax.broadcasted_iota(jnp.int32, line, axis))
    number = lax.broadcasted_iota(jnp.int32, shape, 1 - axis)
    return jnp.where(number == target, 1.0, 0.0).astype(jnp.bfloat16)


def gather_table(lanes, z_elems):
    return ones_where(
        (lanes, 5 * lanes), 1, lambda c: 4 * within(c, z_elems) + over(c, lanes)
    )


def fault_table(lanes, z_elems):
    return ones_where((lanes, lanes), 1, lambda c: 4 * within(c, z_elems) + over(c, z_elems))


def fault_table_back(lanes, z_elems):
    return ones_where((lanes, lanes), 0, lambda c: 4 * within(c, z_elems) + over(c, z_elems))


def stacked(value):
    high, low = pieces(value, 2)
    gap = jnp.zeros((256 - 3 * value.shape[0], value.shape[1]), jnp.bfloat16)
    return jnp.concatenate([high, high, low, gap], axis=0)


def to_elements(native, scratch, table, y_elems, parts=3):
    group = 4 * BLOCK
    for c in range(3):
        for y in range(4 * y_elems + 1):
            rows = native(c, y)
            if y < 4 * y_elems:
                scratch[y // 4, pl.ds(ROWS[y % 4][c], 4, stride=BLOCK), :] = rows
            if y % 4 == 0 and y > 0:
                scratch[y // 4 - 1, pl.ds(ROWS[4][c], 4, stride=BLOCK), :] = rows
    high, middle, *low = pieces(
        jnp.concatenate([scratch[i] for i in range(y_elems)], axis=0), parts
    )
    result = dot(
        jnp.concatenate([high, middle], axis=1), jnp.concatenate([table, table], axis=0)
    )
    for piece in low:
        result = result + dot(piece, table)
    lanes = result.shape[1] // 5
    across = lax.broadcasted_iota(jnp.int32, (1, result.shape[1]), 1)
    across = over(within(across, lanes), lanes // y_elems)
    total = result[:group]
    for yel in range(1, y_elems):
        total = jnp.where(across == yel, result[yel * group : (yel + 1) * group], total)
    blocks = []
    for x in range(4):
        for zl in range(5):
            blocks.append(total[x * BLOCK : (x + 1) * BLOCK, zl * lanes : (zl + 1) * lanes])
    return jnp.concatenate(blocks, axis=0)


def from_elements(field, scratch, back_ref, out_ref, y_elems, stored=None):
    rows = []
    for x in range(4):
        rows.append(
            jnp.concatenate(
                [field[x * PLANE + zl * BLOCK : x * PLANE + (zl + 1) * BLOCK] for zl in range(4)],
                axis=1,
            )
        )
    result = exact_dot(jnp.concatenate(rows, axis=0), back_ref[...])
    depth = result.shape[1] // y_elems
    for yel in range(y_elems):
        scratch[yel] = result[:, yel * depth : (yel + 1) * depth]
    for c in range(3):
        for y in range(4 * y_elems + 1):
            yel, yl = (y // 4, y % 4) if y < 4 * y_elems else (y_elems - 1, 4)
            out_ref[c, y] = scratch[yel, pl.ds(ROWS[yl][c], 4, stride=BLOCK), :]
        if stored is not None:
            stored(c)


def shifted(rows, lanes):
    lanes = lanes % rows.shape[1]
    return pltpu.roll(rows, lanes, 1) if lanes else rows


def block_iotas(lanes):
    return (
        lax.broadcasted_iota(jnp.int32, (8, lanes), 0),
        lax.broadcasted_iota(jnp.int32, (8, lanes), 1),
    )


def store_fault(out_ref, x, plane, z_elems):
    lanes = plane.shape[1]
    _, lane = block_iotas(lanes)
    first = last = jnp.zeros((8, lanes), jnp.float32)
    for zl in range(4):
        at = zl * BLOCK
        here = over(lane, z_elems) == zl
        first = jnp.where(here, shifted(plane[at : at + 8], zl * z_elems), first)
        last = jnp.where(here, shifted(plane[at + 8 : at + 16], (zl + 1) * z_elems), last)
    out_ref[pl.ds(x, 3, stride=8), :] = last[:3]
    out_ref[pl.ds(4 + x, 3, stride=8), :] = first[:3]


def material_rows(lame_ref, shear_ref):
    y_elems, z_elems = lame_ref.shape
    both = jnp.concatenate([lame_ref[...], shear_ref[...]], axis=0)
    spread = ones_where((z_elems, y_elems * z_elems), 1, lambda c: within(c, z_elems))
    tiled = exact_dot(both, spread)
    row = lax.broadcasted_iota(jnp.int32, tiled.shape, 0)
    lane = lax.broadcasted_iota(jnp.int32, tiled.shape, 1)
    kept = jnp.where(within(row, y_elems) == over(lane, z_elems), tiled, 0.0)
    return (
        jnp.sum(kept[:y_elems], axis=0, keepdims=True),
        jnp.sum(kept[y_elems:], axis=0, keepdims=True),
    )


def above_lanes(lanes, z_elems):
    return within(lax.broadcasted_iota(jnp.int32, (BLOCK, lanes), 1), z_elems) != 0


def edge_message(result, lame_row, shear_row, z_elems):
    lanes = result.shape[1]
    force = lame_row * result[:PLANE] + shear_row * result[PLANE:]
    top = force[:BLOCK] + jnp.where(
        above_lanes(lanes, z_elems), pltpu.roll(force[4 * BLOCK :], 1, 1), 0.0
    )
    row = lax.broadcasted_iota(jnp.int32, top.shape, 0)
    top = jnp.where(row == BLOCK - 1, lame_row, top)
    second = jnp.where(row == BLOCK - 1, shear_row, force[BLOCK : 2 * BLOCK])
    return jnp.concatenate([top, second, force[2 * BLOCK : 4 * BLOCK]], axis=0)


def edge_of(field_ref, edge_ref, material_ref, z_elems):
    planes = [stacked(field_ref[x * PLANE : (x + 1) * PLANE]) for x in range(4)]
    edge = dot(edge_ref[...], jnp.concatenate(planes, axis=0))
    return edge_message(edge, material_ref[0:1], material_ref[1:2], z_elems)


def own_force(own_ref, cur, lame_row, shear_row):
    rows, lanes = cur.shape
    padded = jnp.concatenate([cur, jnp.zeros((OWN_COLS - rows, lanes), jnp.float32)], axis=0)
    result = split_dot(own_ref[0], own_ref[1], padded)
    return lame_row * result[:rows] + shear_row * result[rows:]


def start_copies(pairs, sems):
    copies = [
        pltpu.make_async_copy(source, target, sems.at[i])
        for i, (source, target) in enumerate(pairs)
    ]
    for copy in copies:
        copy.start()
    return copies


def first_kernel(
    now_hbm,
    flags_hbm,
    weak_hbm,
    lame_hbm,
    shear_hbm,
    *refs,
):
    later_hbm, refs = refs[:LATER], refs[LATER:]
    cur_ref, odd_ref, fault_out_ref, material_ref = refs[:4]
    later_refs, refs = refs[4 : 4 + LATER], refs[4 + LATER :]
    scratch, now_ref, flags_ref, weak_ref, lame_ref, shear_ref, sems = refs
    copies = start_copies(
        [
            (now_hbm, now_ref),
            (lame_hbm, lame_ref),
            (shear_hbm, shear_ref),
            (flags_hbm, flags_ref),
            (weak_hbm, weak_ref),
            (later_hbm[0], later_refs[0]),
        ]
        + list(zip(later_hbm[1:], later_refs[1:])),
        sems,
    )
    edge_ref = later_refs[0]
    y_elems, z_elems = lame_ref.shape
    lanes = y_elems * z_elems
    gather = gather_table(lanes, z_elems)
    fault = fault_table(lanes, z_elems)
    scratch[...] = jnp.zeros_like(scratch)
    for copy in copies[1:5]:
        copy.wait()
    lame_row, shear_row = material_rows(lame_ref, shear_ref)
    material_ref[...] = jnp.concatenate(
        [lame_row, shear_row, jnp.zeros((6, lanes), jnp.float32)], axis=0
    )
    weak = weak_ref[...]
    tangent = []
    for i in range(flags_ref.shape[0]):
        flag = flags_ref[i]
        tangent.append(
            jnp.where(flag == 0, lock_stiffness, jnp.where(flag == 1, -weak, 0.0))
        )
    fault_out_ref[FAULT:] = exact_dot(jnp.concatenate(tangent, axis=0), fault)
    copies[0].wait()
    cur = to_elements(lambda c, y: now_ref[c, y], scratch, gather, y_elems)
    cur_ref[...] = cur
    planes = [cur[x * PLANE : (x + 1) * PLANE] for x in range(4)]
    for x in range(4):
        store_fault(fault_out_ref, x, planes[x], z_elems)
    odd_ref[...] = cur[: 4 * BLOCK]
    copies[5].wait()

    @pl.when(lax.axis_index("dom") % 2 == 1)
    def _():
        odd_ref[...] = edge_of(cur_ref, edge_ref, material_ref, z_elems)

    for copy in copies[6:]:
        copy.wait()


def prepare_kernel(cur_ref, material_ref, own_ref, touch_ref, base_ref, edge_part_ref):
    cur = cur_ref[...]
    base_ref[...] = own_force(own_ref, cur, material_ref[0:1], material_ref[1:2])
    edge_part_ref[...] = dot(touch_ref[...], stacked(cur[:PLANE]))


def setup_kernel(next_ref, density_ref, mass_ref, fol_ref, minv_ref, scratch, *, y_elems, z_elems):
    gather = gather_table(y_elems * z_elems, z_elems)
    scratch[...] = jnp.zeros_like(scratch)
    fol_ref[...] = to_elements(lambda c, y: next_ref[c, y], scratch.at[0], gather, y_elems)
    density = to_elements(lambda c, y: density_ref[y], scratch.at[1], gather, y_elems, 2)
    table = mass_ref[...]
    first = lax.axis_index("dom") == 0
    plane = lax.broadcasted_iota(jnp.int32, table.shape, 0) < PLANE
    table = jnp.where(jnp.logical_and(first, plane), 2.0 * table, table)
    minv_ref[...] = jnp.where(table > 0.0, table / jnp.where(table > 0.0, density, 1.0), 0.0)


def step_kernel(*refs, step, last, extra, last_place, pair, y_elems, z_elems):
    cur_ref, fol_ref, minv_ref, base_ref, touch_ref, material_ref, odd_ref, up_ref = refs[:8]
    refs = list(refs[8:])
    down_ref = None if pair else refs.pop(0)
    even_in = jnp.concatenate([refs.pop(0)[...] for _ in PARTS], axis=0)
    down_ref = up_ref if pair else down_ref
    first_up_ref, own_ref, first_own_ref, far_ref, edge_ref = refs[:5]
    refs = refs[5 + extra :]
    if last:
        later_ref, back_ref, out_hbm, later_hbm, scratch, out_ref, sems = refs
        copies = start_copies([(later_ref, later_hbm)], sems)
    else:
        new_ref, odd_out, fault_out = refs
    place = lax.axis_index("dom")
    lanes = cur_ref.shape[1]
    even = place % 2 == 0
    far = jnp.where(place == last_place, 0.0, jnp.where(even, even_in, odd_ref[...]))
    left = jnp.where(place == 0, 0.0, jnp.where(even, odd_ref[...], even_in))
    lane_wide = lax.broadcasted_iota(jnp.int32, (BLOCK, lanes), 1)
    below = jnp.where(
        within(lane_wide, z_elems) != z_elems - 1, pltpu.roll(far[:BLOCK], lanes - 1, 1), 0.0
    )
    far = jnp.concatenate([far, below], axis=0)
    lame_row, shear_row = material_ref[0:1], material_ref[1:2]
    far = jnp.concatenate([stacked(lame_row * far), stacked(shear_row * far)], axis=0)
    left_lame = left[BLOCK - 1 : BLOCK]
    left_shear = left[2 * BLOCK - 1 : 2 * BLOCK]
    from_left = left_lame * touch_ref[:PLANE] + left_shear * touch_ref[PLANE:]
    row, lane = block_iotas(lanes)
    across = over(lane, z_elems)
    shared = row < 3
    add_first = jnp.logical_and(shared, across > 0)
    take_last = jnp.logical_and(shared, across < y_elems - 1)
    pull_first = jnp.logical_and(shared, across == 0)
    pull_last = jnp.logical_and(shared, across == y_elems - 1)
    above = above_lanes(lanes, z_elems)
    middle = lax.broadcasted_iota(jnp.int32, (3, lanes), 0) == 1
    gap = jnp.zeros((5, lanes), jnp.float32)
    if not last:
        fault_out[FAULT:] = jnp.zeros_like(fault_out[FAULT:])
    planes = []
    for x in range(4):
        rows = slice(x * PLANE, (x + 1) * PLANE)
        force = base_ref[rows] + dot(far_ref[rows], far)
        blocks = [force[zl * BLOCK : (zl + 1) * BLOCK] for zl in range(5)]
        if x == 0:
            blocks = [b + from_left[i * BLOCK : (i + 1) * BLOCK] for i, b in enumerate(blocks)]
            blocks[:4] = [b + left[i * BLOCK : (i + 1) * BLOCK] for i, b in enumerate(blocks[:4])]
        blocks[0], blocks[4] = (
            blocks[0] + jnp.where(above, pltpu.roll(blocks[4], 1, 1), 0.0),
            blocks[4] + pltpu.roll(blocks[0], lanes - 1, 1),
        )
        lasts, firsts = pl.ds(x, 3, stride=8), pl.ds(4 + x, 3, stride=8)
        k = slice(FAULT + 4 * step + x, FAULT + 4 * step + x + 1)
        below_stiff = jnp.where(middle, lock_stiffness, first_up_ref[k])
        own_stiff = jnp.where(middle, lock_stiffness, first_own_ref[k])
        pulled = jnp.concatenate(
            [below_stiff * (up_ref[lasts, :] - own_ref[firsts, :]), gap], axis=0
        )
        pulled_last = jnp.concatenate(
            [own_stiff * (down_ref[firsts, :] - own_ref[lasts, :]), gap], axis=0
        )
        for zl in range(5):
            low, high = blocks[zl][:8], blocks[zl][8:]
            move = zl * z_elems if zl < 4 else 1
            blocks[zl] = jnp.concatenate(
                [
                    low
                    + jnp.where(add_first, shifted(high, z_elems), 0.0)
                    - jnp.where(pull_first, shifted(pulled, -move), 0.0),
                    high
                    + jnp.where(take_last, shifted(low, -z_elems), 0.0)
                    - jnp.where(pull_last, shifted(pulled_last, -move - z_elems), 0.0),
                ],
                axis=0,
            )
        plane = (2.0 * cur_ref[rows] - fol_ref[rows]) - minv_ref[rows] * jnp.concatenate(
            blocks, axis=0
        )
        if last:
            planes.append(plane)
        else:
            new_ref[rows] = plane
            store_fault(fault_out, x, plane, z_elems)
            if x == 0:
                first = plane[: 4 * BLOCK]
    if last:

        def send(c):
            copy = pltpu.make_async_copy(out_ref.at[c], out_hbm.at[c], sems.at[1 + c])
            copy.start()
            copies.append(copy)

        from_elements(
            jnp.concatenate(planes, axis=0), scratch, back_ref, out_ref, y_elems, send
        )
        for copy in copies:
            copy.wait()
    else:
        odd_out[...] = first

        @pl.when(jnp.logical_not(even))
        def _():
            odd_out[...] = edge_of(new_ref, edge_ref, material_ref, z_elems)


def on_chip_kernel(cur_ref, material_ref, edge_ref, *even_outs, z_elems):
    message = even_outs[-1]
    even_outs = even_outs[:-1]
    message[...] = cur_ref[: 4 * BLOCK]

    @pl.when(lax.axis_index("dom") % 2 == 0)
    def _():
        message[...] = edge_of(cur_ref, edge_ref, material_ref, z_elems)

    for even_out, at in zip(even_outs, (0, PARTS[0], PARTS[0] + PARTS[1])):
        even_out[...] = message[at : at + even_out.shape[0]]


def mask_kernel(owner_ref, flags_ref, stress_ref, _, back_ref, mask_ref, weight_ref, *, z_elems):
    shape = (PATCH_ROWS, mask_ref.shape[1])
    first = (lax.axis_index("dom") - REACH) * PATCH_DEV
    number = lax.broadcasted_iota(jnp.int32, shape, 0) + first
    for x in range(4):
        mask = jnp.where(number == owner_ref[:, x : x + 1], 1.0, 0.0)
        mask_ref[PATCH_ROWS * x : PATCH_ROWS * (x + 1)] = mask
    stress = stress_ref[...]
    weights = []
    for i in range(flags_ref.shape[0]):
        flag = flags_ref[i]
        weights.append(
            stress * jnp.where(flag == 1, 0.5, jnp.where(flag == 2, 1.0, 0.0))
        )
    fault = fault_table(mask_ref.shape[1], z_elems)
    weight_ref[...] = exact_dot(jnp.concatenate(weights, axis=0), fault)


def output_kernel(*refs, pair, steps, y_elems, z_elems):
    field_ref, back_ref, weight_ref = refs[:3]
    out_ref, grad_ref, table_ref, scratch = refs[-4:]
    messages = refs[3:-4]
    count = 2 if pair else 3
    grad = 0.0
    for i in range(steps):
        group = messages[count * i : count * (i + 1)]
        slip = -group[0][:4]
        if i < steps - 1:
            slip = slip + group[-1][4:8]
        grad = grad + slip * weight_ref[4 * i : 4 * i + 4]
    grad_ref[...] = grad
    table_ref[...] = fault_table_back(weight_ref.shape[1], z_elems)
    from_elements(field_ref[...], scratch, back_ref, out_ref, y_elems)


def patch_kernel(*refs, pair, steps):
    mask_ref, weight_ref, grad_ref, table_ref, _ = refs[:5]
    first_ref = refs[5] if pair else refs[6]
    home_out, out_a, out_b, out_c, out_d = refs[-5:]
    place = lax.axis_index("dom")
    grad = grad_ref[...] + first_ref[4:8] * weight_ref[4 * (steps - 1) : 4 * steps]
    total = 0.0
    for x in range(4):
        total = total + mask_ref[PATCH_ROWS * x : PATCH_ROWS * (x + 1)] * grad[x : x + 1]
    total = exact_dot(total, table_ref[...])
    rows = [total[2 * i : 2 * i + 2] for i in range(5)]
    home_out[...] = rows[2]
    even = place % 2 == 0
    out_a[...] = jnp.where(even, rows[3], rows[1])
    out_b[...] = jnp.where(even, rows[1], rows[3])
    low = place % 4 < 2
    out_c[...] = jnp.where(low, rows[4], rows[0])
    out_d[...] = jnp.where(low, rows[0], rows[4])


def sum_kernel(*refs):
    refs[-1][...] = sum(ref[...] for ref in refs[:-1])


VMEM = pl.BlockSpec(memory_space=pltpu.VMEM)
HBM = pl.BlockSpec(memory_space=pltpu.HBM)
SMEM = pl.BlockSpec(memory_space=pltpu.SMEM)
ANY = pl.BlockSpec(memory_space=pl.ANY)


def kernel_call(body, outs, args, in_smem=(), scratch=(), in_hbm=(), kept=(), unread=(), stay=False, out_spec=VMEM, **static):
    shapes = []
    for out in outs:
        shape, dtype = out if isinstance(out[0], tuple) else (out, jnp.float32)
        shapes.append((pltpu.VMEM if in_hbm or stay else jax.ShapeDtypeStruct)(shape, dtype))
    specs = [VMEM] * len(args)
    for places, spec in ((in_smem, SMEM), (in_hbm, HBM), (unread, ANY)):
        for i in places:
            specs[i] = spec
    copied = [pltpu.VMEM(args[i].shape, args[i].dtype) for i in in_hbm if i not in kept]
    if in_hbm:
        copied.append(pltpu.SemaphoreType.DMA((len(in_hbm),)))
    return pl.pallas_call(
        functools.partial(body, **static) if static else body,
        out_shape=shapes,
        in_specs=specs,
        out_specs=[out_spec] * len(shapes),
        scratch_shapes=list(scratch) + copied,
        compiler_params=pltpu.CompilerParams(
            vmem_limit_bytes=(56 if in_hbm else 24) * 2**20
        ),
    )(*args)


def swapped(block, distance, group):
    size, across = lax.axis_size("dom"), lax.axis_size("depth")
    partner = {}
    for left in range(size - distance):
        if left // distance % 2 == group:
            partner[left], partner[left + distance] = left + distance, left
    route = []
    for i in range(size):
        for j in range(across):
            other, side = partner.get(i, i), j
            if i not in partner and i ^ 1 < size and i ^ 1 not in partner:
                other = i ^ 1
            elif i not in partner:
                side = min(j ^ 1, across - 1)
            route.append((i * across + j, other * across + side))
    return lax.ppermute(block, ("dom", "depth"), route)


def from_behind(block, axis, distance):
    size = lax.axis_size(axis)
    return lax.ppermute(block, axis, [((i - distance) % size, i) for i in range(size)])


def on_device(
    adjoint_now,
    adjoint_next,
    lame_first,
    shear_modulus,
    density,
    branch_flags,
    weak_slope,
    normal_stress,
    patch_owner,
):
    x_elems, y_elems, z_elems = lame_first.shape
    lanes = y_elems * z_elems
    assert x_elems == 1 and lanes == adjoint_now.shape[3]
    steps = branch_flags.shape[0]
    pair = lax.axis_size("depth") == 2
    own_table, far_table, edge_table, touch_table = (jnp.asarray(t) for t in stiffness_tables())
    back = jnp.asarray(back_table(y_elems, z_elems))
    mass = jnp.asarray(mass_table(y_elems, z_elems))
    now = jnp.transpose(adjoint_now, (0, 2, 1, 3))
    following = jnp.transpose(adjoint_next, (0, 2, 1, 3))
    rho = jnp.transpose(density, (1, 0, 2))
    flags = branch_flags[:, 0]
    native = pltpu.VMEM((y_elems, 4 * BLOCK, lanes), jnp.float32)
    field = (4 * PLANE, lanes)
    plane = (4 * BLOCK, lanes)
    parts = [(rows, lanes) for rows in PARTS]

    def exchange(even, odd, fault_rows):
        if pair:
            faults = [from_behind(fault_rows, "depth", 1)]
        else:
            faults = [from_behind(fault_rows, "depth", 1), from_behind(fault_rows, "depth", -1)]
        return [swapped(part, 1, 0) for part in even], swapped(odd, 1, 1), faults

    later_used = (
        edge_table, following, rho, mass, own_table, touch_table, flags,
        normal_stress[0], patch_owner,
    )
    assert len(later_used) == LATER
    first_out = kernel_call(
        first_kernel,
        [field, plane, (FAULT + 4 * steps, lanes), (8, lanes)]
        + [(t.shape, t.dtype) for t in later_used],
        (now, flags, weak_slope[0], lame_first[0], shear_modulus[0]) + later_used,
        scratch=[native],
        in_hbm=range(5 + LATER),
        kept=range(5, 5 + LATER),
    )
    cur, odd, fault_rows, material = first_out[:-LATER]
    edge_table, following, rho, mass, own_table, touch_table = first_out[-LATER:-3]
    flags, stress, owner = first_out[-3:]

    def on_chip(field):
        return kernel_call(
            on_chip_kernel,
            parts,
            [field, material, edge_table],
            scratch=[pltpu.VMEM(plane, jnp.float32)],
            z_elems=z_elems,
        )

    even_in, odd_in, fault_in = exchange(on_chip(cur), odd, fault_rows)
    first_fault, first_in = fault_rows, fault_in
    fol, minv = kernel_call(
        setup_kernel,
        [field, field],
        (following, rho, mass),
        scratch=[pltpu.VMEM((2, y_elems, 4 * BLOCK, lanes), jnp.float32)],
        y_elems=y_elems,
        z_elems=z_elems,
    )
    seen = []
    for step in range(steps):
        last = step == steps - 1
        seen += [fault_rows] + fault_in
        base, touch = kernel_call(
            prepare_kernel,
            [field, (2 * PLANE, lanes)],
            [cur, material, own_table, touch_table],
            (),
        )
        args = [cur, fol, minv, base, touch, material, odd_in] + fault_in + even_in
        args += [first_in[0], fault_rows, first_fault, far_table, edge_table]
        static = dict(
            step=step, last=last, extra=1 if last or step == 1 else 0, last_place=lax.axis_size("dom") - 1, pair=pair, y_elems=y_elems,
            z_elems=z_elems,
        )
        if step == 1:
            mask, weight = kernel_call(
                mask_kernel,
                [(4 * PATCH_ROWS, lanes), (4 * steps, lanes)],
                [owner, flags, stress, cur, back],
                unread=(3,),
                z_elems=z_elems,
            )
            args.append(mask)
        if not last:
            new, odd, new_fault = kernel_call(
                step_kernel,
                [field, plane, (SENT_FAULT, lanes)],
                args,
                unread=(len(args) - 1,) if step == 1 else (),
                **static,
            )
            fol, cur, fault_rows = cur, new, new_fault
            even_in, odd_in, fault_in = exchange(on_chip(cur), odd, fault_rows)
        else:
            whole = (3, 4 * y_elems + 1, 4, lanes)
            known = seen[: len(seen) - len(fault_in)]
            later, grad, table = kernel_call(
                output_kernel,
                [whole, (4, lanes), ((lanes, lanes), jnp.bfloat16)],
                [cur, back, weight] + known,
                scratch=[native],
                stay=True,
                pair=pair,
                steps=steps,
                y_elems=y_elems,
                z_elems=z_elems,
            )
            sums = kernel_call(
                patch_kernel,
                [(PATCH_DEV, lanes)] * 5,
                [mask, weight, grad, table, odd_in] + fault_in + even_in + [touch],
                unread=(4,) + tuple(range(5 + len(fault_in), 9 + len(fault_in))),
                pair=pair,
                steps=steps,
            )
            shares = [sums[0]]
            for i, distance, group in ((3, 2, 0), (2, 1, 1), (4, 2, 1), (1, 1, 0)):
                shares.append(swapped(sums[i], distance, group))
            patch_sums = kernel_call(sum_kernel, [(PATCH_DEV, lanes)], shares)[0]
            earlier, later = kernel_call(
                step_kernel,
                [whole, whole],
                args + [sums[0], later, back],
                scratch=[
                    native, pltpu.VMEM(whole, jnp.float32), pltpu.SemaphoreType.DMA((4,)),
                ],
                unread=(len(args),),
                out_spec=HBM,
                **static,
            )
    return (
        jnp.transpose(earlier, (0, 2, 1, 3)),
        jnp.transpose(later, (0, 2, 1, 3)),
        patch_sums[None],
    )


def solution(mesh):
    return jax.shard_map(
        on_device,
        mesh=mesh,
        in_specs=(
            P(None, "dom", "depth", None),
            P(None, "dom", "depth", None),
            P("dom", "depth", None),
            P("dom", "depth", None),
            P("dom", "depth", None),
            P(None, "depth", "dom", None),
            P("depth", "dom", None),
            P("depth", "dom", None),
            P("depth", "dom"),
        ),
        out_specs=(
            P(None, "dom", "depth", None),
            P(None, "dom", "depth", None),
            P("depth", "dom", None),
        ),
        check_vma=False,
    )
```
